256 devices in a mesh: lat: 32 (over z, x_hi, core), lon: 8 (over x_lo, y).
Axes of the slice: x: 4 (x_hi: 2, x_lo: 2; x = x_hi * 2 + x_lo), y: 4, z: 8, core: 2. Of those that a mesh axis runs over, the one named last changes fastest.
Arguments:
- row_signs: int32 [4, 4, 512], P(None, None, 'lat'), may hold values from 0 to 1
- col_signs: int32 [4, 4, 3600], P(None, None, 'lon'), may hold values from 0 to 1
- spread: float32 [4, 4, 512, 3600], P(None, None, 'lat', 'lon'), may hold values from 0.5 to 2
- east_wind: float32 [4, 512, 3600], P(None, 'lat', 'lon'), may hold values from -4 to 4
- north_wind: float32 [4, 512, 3600], P(None, 'lat', 'lon'), may hold values from -4 to 4
- cutoffs: int32 [512], P('lat'), may hold values from 1 to 256, as said below
Outputs:
- tangent: float32 [4, 4, 512, 3600], P(None, None, 'lat', 'lon')
- probe_diag: float32 [4, 4, 512, 3600], P(None, None, 'lat', 'lon')
The draws below stay inside these ranges and needn't reach their ends.
Inputs may be any that keep to these rules, and one draw needn't show every extreme that they name: Rows within 32 rows of either pole have cutoffs from 1 to 128, the row next to each pole exactly 1; all other rows have 256, where the filter leaves them unchanged.
All inputs are finite; a program needn't handle non-finite values.
Results may differ from the reference program's by a relative error of at most 0.000082.
Values sent between devices are 32-bit elements; how exact they have to be, the bound alone decides.
A program may use at most 128 MiB of HBM per device.

```python
import math
import jax
import jax.numpy as jnp
from jax import lax

NLON = 3600
LEV = 4
KTOP = 256
POLAR = 32
NLAT = 512


def draw_cutoffs(key, part):
    key = jax.random.fold_in(key, 7)
    rows = jnp.arange(NLAT, dtype=jnp.int32)
    nearest = jnp.minimum(rows, NLAT - 1 - rows)
    drawn = jax.random.randint(key, (NLAT,), 1, KTOP // 2 + 1, dtype=jnp.int32)
    values = jnp.where(nearest < POLAR, drawn, KTOP)
    return jnp.where(nearest == 0, 1, values).astype(jnp.int32)


def set_ends(values, own_key, smallest, high):
    shape = values.shape
    index_at = [jax.random.randint(jax.random.fold_in(own_key, axis), (), 0, shape[axis]) for axis in range(len(shape))]
    values = values.at[tuple(index_at)].set(smallest)
    longest = shape.index(max(shape))
    index_at[longest] = (index_at[longest] + 1) % shape[longest]
    return values.at[tuple(index_at)].set(high)


def steps_of(rng, dims, pieces, least, top_value):
    factor_of, own = 1.0, jax.random.fold_in(rng, 6)
    for dim, blocks in pieces:
        heights = jnp.exp(jax.random.uniform(jax.random.fold_in(own, dim), (blocks,), jnp.float32, least / len(pieces), top_value / len(pieces)))
        factor_of = factor_of * jnp.repeat(heights, dims[dim] // blocks).reshape([-1 if axis == dim else 1 for axis in range(len(dims))])
    return factor_of


def normal_values(own_key, dims, scale, limit, split=(), kind=jnp.bfloat16):
    gain = steps_of(own_key, dims, split, -0.22, 0.18) if split else 1.0
    entries = jax.random.normal(own_key, dims, jnp.float32) * scale * gain
    return jnp.minimum(jnp.maximum(entries, -limit), limit).astype(kind)


def setup_inputs(seed: int = 0) -> dict:
    key_of = jax.random.split(jax.random.key(seed), 7)
    row_signs = set_ends(jax.random.randint(key_of[0], (4, LEV, NLAT), 0, 2), jax.random.fold_in(key_of[0], 1), 0, 1).astype(jnp.int32)
    col_signs = set_ends(jax.random.randint(key_of[1], (4, LEV, NLON), 0, 2), jax.random.fold_in(key_of[1], 1), 0, 1).astype(jnp.int32)
    spread = jnp.clip(jnp.exp(math.log(2.0) - 1.3862944 * jax.random.uniform(key_of[2], (4, LEV, NLAT, NLON), jnp.float32) ** steps_of(key_of[2], (4, LEV, NLAT, NLON), ((2, 32), (3, 8)), -0.2, 0.2)), 0.5, 2.0)
    east_wind = normal_values(key_of[3], (LEV, NLAT, NLON), 1.0, 4.0, ((1, 32), (2, 8)), jnp.float32)
    north_wind = normal_values(key_of[4], (LEV, NLAT, NLON), 1.0, 4.0, ((1, 32), (2, 8)), jnp.float32)
    cutoffs = draw_cutoffs(jax.random.fold_in(key_of[6], 71), 0)
    return dict(row_signs=row_signs, col_signs=col_signs, spread=spread, east_wind=east_wind, north_wind=north_wind, cutoffs=cutoffs)


time_step = 0.5
coupling = 0.5
mixing = 0.2
metric_cap = 4.0

def metric_rows(first_row, count, total_rows):
    rows = first_row + jnp.arange(count, dtype=jnp.int32)
    latitude = jnp.pi * ((rows.astype(jnp.float32) + 0.5) / total_rows - 0.5)
    return jnp.minimum(1.0 / jnp.cos(latitude), metric_cap)

def tendency(padded, east_wind, north_wind, metric):
    center = padded[:, :, 1:-1, 1:-1]
    along_x = 0.5 * (padded[:, :, 1:-1, 2:] - padded[:, :, 1:-1, :-2]) * metric[:, None]
    along_y = 0.5 * (padded[:, :, 2:, 1:-1] - padded[:, :, :-2, 1:-1])
    advect = east_wind * along_x + north_wind * along_y
    linked = jnp.stack([along_x[2], along_y[2], along_x[0] + along_y[1], jnp.zeros_like(center[3])])
    above = jnp.concatenate([center[:, :1], center[:, :-1]], axis=1)
    below = jnp.concatenate([center[:, 1:], center[:, -1:]], axis=1)
    return -advect - coupling * linked + mixing * (above - 2.0 * center + below)

def mode_table(first_col, count, total_cols, modes):
    cols = first_col + jnp.arange(count, dtype=jnp.int32)
    waves = jnp.arange(1, modes + 1, dtype=jnp.int32)
    phase = cols[:, None] * waves[None, :] % total_cols
    angle = 2.0 * jnp.pi / total_cols * phase.astype(jnp.float32)
    return jnp.concatenate([jnp.cos(angle), jnp.sin(angle)], axis=1)

def removal_mask(cutoffs, modes):
    waves = jnp.arange(1, modes + 1, dtype=jnp.int32)
    high = (waves[None, :] > cutoffs[:, None]).astype(jnp.float32)
    return jnp.concatenate([high, high], axis=1)

def pad_global(field):
    half = field.shape[-1] // 2
    sign = jnp.array([-1.0, -1.0, 1.0, 1.0], field.dtype)[:, None, None, None]
    north = sign * jnp.roll(field[:, :, :1], half, axis=3)
    south = sign * jnp.roll(field[:, :, -1:], half, axis=3)
    rows = jnp.concatenate([north, field, south], axis=2)
    return jnp.concatenate([rows[..., -1:], rows, rows[..., :1]], axis=3)

def polar_filter(field, cutoffs):
    table = mode_table(0, NLON, NLON, KTOP)
    coef = jnp.einsum('flrj,jk->flrk', field, table, precision=lax.Precision.HIGHEST)
    coef = coef * removal_mask(cutoffs, KTOP) * (2.0 / NLON)
    return field - jnp.einsum('flrk,jk->flrj', coef, table, precision=lax.Precision.HIGHEST)

def forward(field, east_wind, north_wind, cutoffs):
    metric = metric_rows(0, NLAT, NLAT)
    return field + time_step * polar_filter(tendency(pad_global(field), east_wind, north_wind, metric), cutoffs)

def reference(row_signs, col_signs, spread, east_wind, north_wind, cutoffs):
    row_part = (2 * row_signs - 1).astype(jnp.float32)
    col_part = (2 * col_signs - 1).astype(jnp.float32)
    signs = row_part[:, :, :, None] * col_part[:, :, None, :]
    probe = spread * signs
    tangent, pullback = jax.vjp(lambda field: forward(field, east_wind, north_wind, cutoffs), probe)
    back = tangent + (pullback(tangent)[0] - tangent)
    return (tangent, signs * spread * (back - probe))
```

```python
import functools

import jax
import jax.numpy as jnp
import ml_dtypes
import numpy as np
from jax import lax
from jax.experimental import pallas as pl
from jax.experimental.pallas import tpu as pltpu
from jax.sharding import PartitionSpec as P

KTOP = 256
POLAR = 32
RANK = 128
ROWS = 16
COLS = 450
WIDE = 512
LANES = 8
FIELDS = 4
LEV = 4
PAIRS = FIELDS * LEV

time_step = 0.5
coupling = 0.5
mixing = 0.2
metric_cap = 4.0

MESH = pl.DeviceIdType.MESH
F32 = jnp.float32
BF16 = jnp.bfloat16


def split_table(table):
    high = table.astype(ml_dtypes.bfloat16)
    low = (table - high.astype(np.float64)).astype(ml_dtypes.bfloat16)
    return high, low


@functools.lru_cache(None)
def mode_factors():
    total = COLS * LANES
    size = COLS + 2
    place = np.arange(size, dtype=np.float64)
    width = (KTOP + 0.5) / total
    diag = ((size - 1 - 2 * place) / 2) ** 2 * np.cos(2 * np.pi * width)
    side = place[1:] * (size - place[1:]) / 2
    vectors = np.linalg.eigh(np.diag(diag) + np.diag(side, 1) + np.diag(side, -1))[1]
    basis = vectors[:, ::-1][:, :RANK]
    basis = basis * np.where(basis[size // 2] < 0, -1.0, 1.0)
    waves = np.arange(1, KTOP + 1)
    factors = []
    for lane in range(LANES):
        cols = lane * COLS - 1 + np.arange(size)
        angle = 2 * np.pi / total * (cols[:, None] * waves[None, :] % total)
        factors.append(basis.T @ np.concatenate([np.cos(angle), np.sin(angle)], axis=1))
    factors = np.round(np.concatenate(factors, axis=0) * 2.0**22) / 2.0**22
    wide = np.zeros((RANK, WIDE))
    wide[:, : COLS + 1] = basis[1:].T
    wide[:, WIDE - 1] = basis[0]
    wide = np.round(wide * 2.0**26) / 2.0**26
    return split_table(wide) + split_table(factors)


@functools.lru_cache(None)
def half_metric(bands):
    total = bands * ROWS
    rows = np.clip(np.arange(bands)[:, None] * ROWS - 8 + np.arange(32)[None, :], 0, total - 1)
    metric = np.minimum(1.0 / np.cos(np.pi * ((rows + 0.5) / total - 0.5)), metric_cap)
    return np.broadcast_to((0.5 * metric).astype(np.float32)[:, :, None], (bands, 32, 128)).copy()


def dot_rows(a, b):
    return lax.dot_general(a, b, (((1,), (1,)), ((), ())), preferred_element_type=F32)


def dot_cols(a, b):
    return lax.dot_general(a, b, (((1,), (0,)), ((), ())), preferred_element_type=F32)


def dot3(dot, x, high, low):
    xh = x.astype(BF16)
    xl = (x - xh.astype(F32)).astype(BF16)
    return dot(xh, high) + dot(xl, high) + dot(xh, low)


def roll(x, shift, axis):
    return pltpu.roll(x, shift % x.shape[axis], axis)


def roll_blocks(x, shift):
    return roll(x.reshape(x.shape[0] * x.shape[1], x.shape[2]), shift, 1).reshape(x.shape)


def fold(x):
    while x.shape[0] > 1:
        half = x.shape[0] // 2
        x = x[:half] + roll_blocks(x[half:], 2 * half)
    return x


def kernel(
    bands, spread, east, north, rs, cs, cut, metric, qh_in, ql_in, rh_in, rl_in, tan_out, diag_out,
    spread_v, east_v, north_v, rs_v, cs_v, cut_s, hm, qh, ql, rh, rl,
    grid, er, hr, hc, cp, hcol, ybuf, yr, zbuf, zr, bz,
    tend, proj_p, proj_t, edge_t, edge_proj, adj, gy, tan_v, diag_v,
    in_sem, row_send, row_recv, cor_send, cor_recv, col_send, col_recv,
    y_send, y_recv, z_send, z_recv, b_send, b_recv, out_sem,
):
    b = lax.axis_index("lat")
    i = lax.axis_index("lon")
    caps = POLAR // ROWS
    is_north = b == 0
    is_south = b == bands - 1
    polar = jnp.logical_or(b < caps, b >= bands - caps)
    above_polar = jnp.logical_or(b <= caps, is_south)
    below_polar = jnp.logical_or(b >= bands - caps - 1, is_north)
    across = lax.rem(i + LANES // 2, LANES)
    west = lax.rem(i + LANES - 1, LANES)
    east_lane = lax.rem(i + 1, LANES)
    nb = jnp.where(is_north, 0, b - 1)
    nl = jnp.where(is_north, across, i)
    sb = jnp.where(is_south, bands - 1, b + 1)
    sl = jnp.where(is_south, across, i)
    slot_n = jnp.where(is_north, 0, 1)
    slot_s = jnp.where(is_south, 1, 0)
    first, last = 0, LANES - 1

    def plus(lane, d):
        return lax.rem(lane + d, LANES)

    loads = [
        pltpu.make_async_copy(spread, spread_v, in_sem.at[0]),
        pltpu.make_async_copy(rs, rs_v, in_sem.at[1]),
        pltpu.make_async_copy(cs, cs_v, in_sem.at[2]),
        pltpu.make_async_copy(east, east_v, in_sem.at[3]),
        pltpu.make_async_copy(north, north_v, in_sem.at[4]),
        pltpu.make_async_copy(metric.at[b], hm, in_sem.at[5]),
        pltpu.make_async_copy(cut, cut_s, in_sem.at[6]),
        pltpu.make_async_copy(qh_in, qh, in_sem.at[7]),
        pltpu.make_async_copy(ql_in, ql, in_sem.at[8]),
    ]
    table_loads = [
        pltpu.make_async_copy(rh_in, rh, in_sem.at[9]),
        pltpu.make_async_copy(rl_in, rl, in_sem.at[10]),
    ]
    for load in loads:
        load.start()

    @pl.when(polar)
    def _():
        for load in table_loads:
            load.start()

    barrier = pltpu.get_barrier_semaphore()

    def greet(lat, lon):
        pl.semaphore_signal(barrier, inc=1, device_id=(lat, lon), device_id_type=MESH)

    greet(nb, nl)
    greet(sb, sl)
    greet(b, west)
    greet(b, east_lane)
    greet(nb, plus(nl, 1))
    greet(nb, plus(nl, LANES - 1))
    greet(sb, plus(sl, 1))
    greet(sb, plus(sl, LANES - 1))

    @pl.when(polar)
    def _():
        @pl.loop(1, LANES)
        def _(d):
            greet(b, plus(i, d))

    @pl.when(jnp.logical_and(above_polar, jnp.logical_not(is_north)))
    def _():
        greet(nb, last)

    @pl.when(jnp.logical_and(below_polar, jnp.logical_not(is_south)))
    def _():
        greet(sb, first)

    for load in loads[:5]:
        load.wait()
    grid[:, 8:24, 384:512] = jnp.zeros((PAIRS + 2 * LEV, ROWS, 128), F32)
    row_part = jnp.concatenate([rs_v[f] for f in range(FIELDS)], axis=0)
    row_part = (2 * row_part - 1).astype(F32).T
    for f in range(FIELDS):
        col_part = (2 * cs_v[f] - 1).astype(F32)
        for l in range(LEV):
            n = f * LEV + l
            grid[n, 8:24, 0:COLS] = spread_v[f, l] * (row_part[:, n : n + 1] * col_part[l : l + 1, :])
    for l in range(LEV):
        grid[PAIRS + l, 8:24, 0:COLS] = east_v[l]
        grid[PAIRS + LEV + l, 8:24, 0:COLS] = north_v[l]

    for s, (near, far) in enumerate(((8, 9), (23, 22))):
        for f in range(FIELDS + 2):
            er[s, f if f < FIELDS else f + FIELDS] = grid[f * LEV : (f + 1) * LEV, near, :]
        for f in range(FIELDS):
            er[s, FIELDS + f] = grid[f * LEV : (f + 1) * LEV, far, :]
    lane128 = lax.broadcasted_iota(jnp.int32, (1, 1, 128), 2)
    for s, (start, shift) in enumerate(((0, 0), (384, COLS - 2 - 384))):
        tile = grid[:, 8:24, start : start + 128]
        tile = jnp.where(jnp.logical_and(lane128 >= shift, lane128 < shift + 2), tile, 0.0)
        packed = fold(tile[:PAIRS]) + roll_blocks(fold(tile[PAIRS:]), 2 * PAIRS)
        cp[s] = roll_blocks(packed, -shift)[0]

    pl.semaphore_wait(
        barrier,
        8
        + jnp.where(polar, LANES - 1, 0)
        + jnp.where(jnp.logical_and(polar, jnp.logical_and(i == first, jnp.logical_not(is_north))), LANES, 0)
        + jnp.where(jnp.logical_and(polar, jnp.logical_and(i == last, jnp.logical_not(is_south))), LANES, 0),
    )

    def remote(src, dst, send, recv, lat, lon):
        return pltpu.make_async_remote_copy(
            src_ref=src, dst_ref=dst, send_sem=send, recv_sem=recv, device_id=(lat, lon), device_id_type=MESH
        )

    halo_sends = [
        remote(er.at[0], hr.at[slot_n], row_send.at[0], row_recv.at[slot_n], nb, nl),
        remote(er.at[1], hr.at[slot_s], row_send.at[1], row_recv.at[slot_s], sb, sl),
        remote(cp.at[0], hcol.at[1], col_send.at[0], col_recv.at[1], b, west),
        remote(cp.at[1], hcol.at[0], col_send.at[1], col_recv.at[0], b, east_lane),
    ]
    for s, (slot, lat, lon) in enumerate(((slot_n, nb, nl), (slot_s, sb, sl))):
        halo_sends.append(
            remote(
                er.at[s, 0:FIELDS, :, 384:512], hc.at[slot, 0], cor_send.at[s, 0], cor_recv.at[slot, 0],
                lat, plus(lon, 1),
            )
        )
        halo_sends.append(
            remote(
                er.at[s, 0:FIELDS, :, 0:128], hc.at[slot, 1], cor_send.at[s, 1], cor_recv.at[slot, 1],
                lat, plus(lon, LANES - 1),
            )
        )
    for send in halo_sends:
        send.start()

    lane512 = lax.broadcasted_iota(jnp.int32, (1, WIDE), 1)
    own_cols = lane512 < COLS

    def y_copy(q, o):
        return remote(ybuf.at[q, o], yr.at[q, i], y_send.at[q, o], y_recv.at[q, i], b, o)

    def y_arrival(q, j):
        return remote(ybuf.at[q, j], yr.at[q, j], y_send.at[q, j], y_recv.at[q, j], b, j)

    def send_row_values(q, x):
        y = dot3(dot_rows, jnp.where(own_cols, x, 0.0), qh[...], ql[...])
        y = jnp.swapaxes(y.reshape(PAIRS, ROWS, RANK), 0, 1)
        ybuf[q] = y.reshape(LANES, 2 * PAIRS, RANK)

        @pl.loop(1, LANES)
        def _(d):
            y_copy(q, plus(i, d)).start()

        yr[q, i] = ybuf[q, i]

    def z_copy(q, j):
        return remote(zbuf.at[q, j], zr.at[q, i], z_send.at[q, j], z_recv.at[q, i], b, j)

    def z_arrival(q, j):
        return remote(zbuf.at[q, j], zr.at[q, j], z_send.at[q, j], z_recv.at[q, j], b, j)

    def edge_copy(q, j, s):
        slot, lat = ((slot_n, nb), (slot_s, sb))[s]
        over = (is_north, is_south)[s]
        lon = jnp.where(over, plus(j, LANES // 2), j)
        part = zbuf.at[q, j, PAIRS * s : PAIRS * (s + 1)]
        here = jnp.logical_and(over, lon == i)

        def away():
            return remote(part, bz.at[slot, q], b_send.at[q, j], b_recv.at[slot, q], lat, lon)

        def local():
            return pltpu.make_async_copy(part, bz.at[s, q], b_recv.at[s, q])

        return here, away, local

    def edge_sends(q, act):
        for s, owner in ((0, first), (1, last)):
            @pl.when(i == owner)
            def _():
                @pl.loop(0, LANES)
                def _(j):
                    here, away, local = edge_copy(q, j, s)

                    @pl.when(jnp.logical_not(here))
                    def _():
                        act(away())

                    if act is start_copy:
                        @pl.when(here)
                        def _():
                            local().start()

    def start_copy(copy):
        copy.start()

    def end_copy(copy):
        copy.wait_send()

    def own_rows(q):
        @pl.loop(1, LANES)
        def _(d):
            y_arrival(q, plus(i, d)).wait_recv()

        y = jnp.concatenate([yr[q, j] for j in range(LANES)], axis=1)
        coef = dot3(dot_cols, y, rh[...], rl[...])
        wave = lax.rem(lax.broadcasted_iota(jnp.int32, (PAIRS, 2 * KTOP), 1), KTOP) + 1
        keep = jnp.concatenate(
            [jnp.where(wave > cut_s[2 * i + part], 2.0 / (COLS * LANES), 0.0) for part in range(2)], axis=0
        )
        z = dot3(dot_rows, coef * keep, rh[...], rl[...])
        for j in range(LANES):
            zbuf[q, j] = z[:, j * RANK : (j + 1) * RANK]

        @pl.loop(1, LANES)
        def _(d):
            z_copy(q, plus(i, d)).start()

        edge_sends(q, start_copy)
        zr[q, i] = zbuf[q, i]

    def project(q, out):
        @pl.loop(1, LANES)
        def _(d):
            z_arrival(q, plus(i, d)).wait_recv()

        z = jnp.swapaxes(zr[q].reshape(ROWS, PAIRS, RANK), 0, 1).reshape(PAIRS * ROWS, RANK)
        out[...] = dot3(dot_cols, z, qh[...], ql[...]).reshape(PAIRS, ROWS, WIDE)

    for load in loads[5:]:
        load.wait()

    @pl.when(polar)
    def _():
        send_row_values(0, grid[0:PAIRS, 8:24, :].reshape(PAIRS * ROWS, WIDE))

    for s in range(2):
        remote(er.at[s], hr.at[s], row_send.at[s], row_recv.at[s], nb, nl).wait_recv()
        remote(cp.at[s], hcol.at[s], col_send.at[s], col_recv.at[s], b, west).wait_recv()
        for side in range(2):
            remote(
                er.at[s, 0:FIELDS, :, 0:128], hc.at[s, side], cor_send.at[s, side], cor_recv.at[s, side], nb, nl
            ).wait_recv()

    from_west = roll(hcol[0], 126, 1)
    from_east = roll(hcol[1], COLS - 384, 1)
    lane2 = lax.broadcasted_iota(jnp.int32, (1, 128), 1)
    both = jnp.where(jnp.logical_and(lane2 >= 66, lane2 < 114), from_east, from_west)[None]
    for width in (2, 4, 8):
        both = jnp.concatenate([both, roll_blocks(both, -width)], axis=0)
    both = jnp.concatenate([both, roll_blocks(both, -16), roll_blocks(both, -32)], axis=0)
    in_halo = jnp.logical_or(
        jnp.logical_and(lane128 >= 66, lane128 < 68), lane128 >= 126
    )
    grid[:, 8:24, 384:512] = jnp.where(in_halo, both, grid[:, 8:24, 384:512])

    flips = (-1.0, -1.0, 1.0, 1.0)
    over_pole = (is_north, is_south)
    edge_row = (7, 24)
    inward = (1.0, -1.0)

    def edge_center(s, f):
        tile = hr[s, f][:, 384:512]
        tile = jnp.where(lane2 == 66, roll(hc[s, 1, f], 66, 1), tile)
        tile = jnp.where(lane2 == 127, roll(hc[s, 0, f], 62, 1), tile)
        return jnp.concatenate([hr[s, f][:, 0:384], tile], axis=1)

    edge_probe = []
    for s in range(2):
        centers = [edge_center(s, f) for f in range(FIELDS)]
        edge_probe.append(centers)
        half = jnp.concatenate([hm[edge_row[s] : edge_row[s] + 1, :]] * 4, axis=1)
        turn = jnp.where(over_pole[s], -inward[s], inward[s])
        along_x, along_y = [], []
        for f in range(FIELDS):
            flip = jnp.where(over_pole[s], flips[f], 1.0)
            grid[f * LEV : (f + 1) * LEV, edge_row[s], :] = flip * centers[f]
            along_x.append(half * (roll(centers[f], -1, 1) - roll(centers[f], 1, 1)))
            along_y.append((0.5 * turn) * (flip * er[s, f] - hr[s, FIELDS + f]))
        linked = (along_x[2], along_y[2], along_x[0] + along_y[1], None)
        for f in range(FIELDS):
            mid = centers[f]
            up = jnp.concatenate([mid[0:1], mid[0:3]], axis=0)
            down = jnp.concatenate([mid[1:4], mid[3:4]], axis=0)
            t = -(hr[s, 8] * along_x[f] + hr[s, 9] * along_y[f]) + mixing * (up + down - 2.0 * mid)
            if linked[f] is not None:
                t = t - coupling * linked[f]
            edge_t[s, f] = t

    @pl.loop(0, LEV)
    def _(l):
        lo = jnp.maximum(l - 1, 0)
        hi = jnp.minimum(l + 1, LEV - 1)
        for h in (8, 16):
            half = jnp.concatenate([hm[h : h + 8, :]] * 4, axis=1)
            ew = grid[PAIRS + l, h : h + 8, :]
            nw = grid[PAIRS + LEV + l, h : h + 8, :]
            along_x, along_y = [], []
            for f in range(FIELDS):
                mid = grid[f * LEV + l, h : h + 8, :]
                along_x.append(half * (roll(mid, -1, 1) - roll(mid, 1, 1)))
                along_y.append(0.5 * (grid[f * LEV + l, h + 1 : h + 9, :] - grid[f * LEV + l, h - 1 : h + 7, :]))
            linked = (along_x[2], along_y[2], along_x[0] + along_y[1], None)
            for f in range(FIELDS):
                mid = grid[f * LEV + l, h : h + 8, :]
                mixed = grid[f * LEV + lo, h : h + 8, :] + grid[f * LEV + hi, h : h + 8, :] - 2.0 * mid
                t = -(ew * along_x[f] + nw * along_y[f]) + mixing * mixed
                if linked[f] is not None:
                    t = t - coupling * linked[f]
                tend[f * LEV + l, h - 8 : h, :] = t

    @pl.when(polar)
    def _():
        send_row_values(1, tend[...].reshape(PAIRS * ROWS, WIDE))
        for load in table_loads:
            load.wait()
        own_rows(0)
        own_rows(1)
        project(0, proj_p)
        project(1, proj_t)

    @pl.when(jnp.logical_not(polar))
    def _():
        proj_p[...] = jnp.zeros(proj_p.shape, F32)
        proj_t[...] = jnp.zeros(proj_t.shape, F32)

    for s, wanted in enumerate((above_polar, below_polar)):
        @pl.when(wanted)
        def _():
            for q in range(2):
                remote(
                    zbuf.at[q, 0, 0:PAIRS], bz.at[s, q], b_send.at[q, 0], b_recv.at[s, q], nb, nl
                ).wait_recv()
            z = bz[s].reshape(2 * PAIRS, RANK)
            edge_proj[s] = dot3(dot_cols, z, qh[...], ql[...]).reshape(2, PAIRS, WIDE)

        @pl.when(jnp.logical_not(wanted))
        def _():
            edge_proj[s] = jnp.zeros((2, PAIRS, WIDE), F32)

    def row_weights(a, nw):
        return (
            -nw * a[0],
            -nw * a[1] - coupling * a[2],
            -nw * a[2] - coupling * a[1],
            -nw * a[3],
        )

    for s in range(2):
        a = []
        for f in range(FIELDS):
            rows = slice(f * LEV, (f + 1) * LEV)
            a.append(
                edge_probe[s][f]
                + time_step * (edge_t[s, f] - edge_proj[s, 1, rows, :])
                - edge_proj[s, 0, rows, :]
            )
        for f, weight in enumerate(row_weights(a, hr[s, 9])):
            flip = jnp.where(over_pole[s], -flips[f], 1.0)
            gy[f * LEV : (f + 1) * LEV, edge_row[s], :] = flip * weight

    @pl.loop(0, LEV)
    def _(l):
        for h in (8, 16):
            nw = grid[PAIRS + LEV + l, h : h + 8, :]
            a = []
            for f in range(FIELDS):
                n = f * LEV + l
                change = time_step * (tend[n, h - 8 : h, :] - proj_t[n, h - 8 : h, :])
                tend[n, h - 8 : h, :] = change
                tangent = grid[n, h : h + 8, :] + change
                tan_v[f, l, h - 8 : h, :] = tangent[:, :COLS]
                a.append(tangent - proj_p[n, h - 8 : h, :])
                adj[n, h - 8 : h, :] = a[f]
            for f, weight in enumerate(row_weights(a, nw)):
                gy[f * LEV + l, h : h + 8, :] = weight

    tan_copy = pltpu.make_async_copy(tan_v, tan_out, out_sem.at[0])
    tan_copy.start()

    @pl.loop(0, LEV)
    def _(l):
        lo = jnp.maximum(l - 1, 0)
        hi = jnp.minimum(l + 1, LEV - 1)
        for h in (8, 16):
            rows = slice(h - 8, h)
            half = jnp.concatenate([hm[h : h + 8, :]] * 4, axis=1)
            ew = grid[PAIRS + l, h : h + 8, :]
            a = [adj[f * LEV + l, rows, :] for f in range(FIELDS)]
            col_weights = (
                -ew * a[0] - coupling * a[2],
                -ew * a[1],
                -ew * a[2] - coupling * a[0],
                -ew * a[3],
            )
            for f in range(FIELDS):
                n = f * LEV + l
                back = half * (roll(col_weights[f], 1, 1) - roll(col_weights[f], -1, 1))
                back = back + 0.5 * (gy[n, h - 1 : h + 7, :] - gy[n, h + 1 : h + 9, :])
                back = back + mixing * (adj[f * LEV + lo, rows, :] + adj[f * LEV + hi, rows, :] - 2.0 * a[f])
                diag = grid[n, h : h + 8, :] * (tend[n, rows, :] + time_step * back)
                diag_v[f, l, rows, :] = diag[:, :COLS]

    diag_copy = pltpu.make_async_copy(diag_v, diag_out, out_sem.at[1])
    diag_copy.start()

    for send in halo_sends:
        send.wait_send()

    @pl.when(polar)
    def _():
        for q in range(2):
            @pl.loop(1, LANES)
            def _(d):
                y_copy(q, plus(i, d)).wait_send()
                z_copy(q, plus(i, d)).wait_send()

            edge_sends(q, end_copy)

    tan_copy.wait()
    diag_copy.wait()


def per_device(bands, row_signs, col_signs, spread, east_wind, north_wind, cutoffs):
    any_spec = pl.BlockSpec(memory_space=pl.ANY)
    out = jax.ShapeDtypeStruct((FIELDS, LEV, ROWS, COLS), F32)
    tables = [jnp.asarray(table) for table in (half_metric(bands),) + mode_factors()]
    vmem = pltpu.VMEM
    dma = pltpu.SemaphoreType.DMA
    return pl.pallas_call(
        functools.partial(kernel, bands),
        out_shape=(out, out),
        in_specs=[any_spec] * 11,
        out_specs=(any_spec, any_spec),
        scratch_shapes=[
            vmem((FIELDS, LEV, ROWS, COLS), F32),
            vmem((LEV, ROWS, COLS), F32),
            vmem((LEV, ROWS, COLS), F32),
            vmem((FIELDS, LEV, ROWS), jnp.int32),
            vmem((FIELDS, LEV, COLS), jnp.int32),
            pltpu.SMEM((ROWS,), jnp.int32),
            vmem((32, 128), F32),
            vmem((RANK, WIDE), BF16),
            vmem((RANK, WIDE), BF16),
            vmem((LANES * RANK, 2 * KTOP), BF16),
            vmem((LANES * RANK, 2 * KTOP), BF16),
            vmem((PAIRS + 2 * LEV, 32, WIDE), F32),
            vmem((2, 10, LEV, WIDE), F32),
            vmem((2, 10, LEV, WIDE), F32),
            vmem((2, 2, FIELDS, LEV, 128), F32),
            vmem((2, ROWS, 128), F32),
            vmem((2, ROWS, 128), F32),
            vmem((2, LANES, 2 * PAIRS, RANK), F32),
            vmem((2, LANES, 2 * PAIRS, RANK), F32),
            vmem((2, LANES, 2 * PAIRS, RANK), F32),
            vmem((2, LANES, 2 * PAIRS, RANK), F32),
            vmem((2, 2, PAIRS, RANK), F32),
            vmem((PAIRS, ROWS, WIDE), F32),
            vmem((PAIRS, ROWS, WIDE), F32),
            vmem((PAIRS, ROWS, WIDE), F32),
            vmem((2, FIELDS, LEV, WIDE), F32),
            vmem((2, 2, PAIRS, WIDE), F32),
            vmem((PAIRS, ROWS, WIDE), F32),
            vmem((PAIRS, 32, WIDE), F32),
            vmem((FIELDS, LEV, ROWS, COLS), F32),
            vmem((FIELDS, LEV, ROWS, COLS), F32),
            dma((11,)),
            dma((2,)),
            dma((2,)),
            dma((2, 2)),
            dma((2, 2)),
            dma((2,)),
            dma((2,)),
            dma((2, LANES)),
            dma((2, LANES)),
            dma((2, LANES)),
            dma((2, LANES)),
            dma((2, LANES)),
            dma((2, 2)),
            dma((2,)),
        ],
        compiler_params=pltpu.CompilerParams(
            collective_id=0, has_side_effects=True, vmem_limit_bytes=48 * 2**20
        ),
        cost_estimate=pl.CostEstimate(flops=10**9, bytes_accessed=4 * 10**6, transcendentals=0),
    )(spread, east_wind, north_wind, row_signs, col_signs, cutoffs, *tables)


def solution(mesh):
    return jax.shard_map(
        functools.partial(per_device, mesh.shape["lat"]),
        mesh=mesh,
        in_specs=(
            P(None, None, "lat"),
            P(None, None, "lon"),
            P(None, None, "lat", "lon"),
            P(None, "lat", "lon"),
            P(None, "lat", "lon"),
            P("lat"),
        ),
        out_specs=(P(None, None, "lat", "lon"), P(None, None, "lat", "lon")),
        check_vma=False,
    )
```

```python
import functools

import jax
import jax.numpy as jnp
import ml_dtypes
import numpy as np
from jax import lax
from jax.experimental import pallas as pl
from jax.experimental.pallas import tpu as pltpu
from jax.sharding import PartitionSpec as P

KTOP = 256
POLAR = 32
RANK = 128
ROWS = 16
COLS = 450
WIDE = 512
LANES = 8
FIELDS = 4
LEV = 4
PAIRS = FIELDS * LEV

time_step = 0.5
coupling = 0.5
mixing = 0.2
metric_cap = 4.0

MESH = pl.DeviceIdType.MESH
F32 = jnp.float32
BF16 = jnp.bfloat16


def split_table(table):
    high = table.astype(ml_dtypes.bfloat16)
    low = (table - high.astype(np.float64)).astype(ml_dtypes.bfloat16)
    return high, low


def waves_of(group, lane_index):
    place = lane_index % 64
    second = place // 32
    other = (8 - group) if group else 4
    residue = group + second * (other - group)
    return 8 * (place % 32) + residue + (8 * (1 - second) if group == 0 else 0)


@functools.lru_cache(None)
def mode_factors():
    total = COLS * LANES
    size = COLS + 2
    place = np.arange(size, dtype=np.float64)
    width = (KTOP + 0.5) / total
    diag = ((size - 1 - 2 * place) / 2) ** 2 * np.cos(2 * np.pi * width)
    side = place[1:] * (size - place[1:]) / 2
    vectors = np.linalg.eigh(np.diag(diag) + np.diag(side, 1) + np.diag(side, -1))[1]
    basis = vectors[:, ::-1][:, :RANK]
    basis = basis * np.where(basis[size // 2] < 0, -1.0, 1.0)
    weights = []
    for group in range(4):
        waves = waves_of(group, np.arange(64))
        angle = 2 * np.pi / total * ((np.arange(size)[:, None] - 1) * waves[None, :] % total)
        alpha, beta = basis.T @ np.cos(angle), basis.T @ np.sin(angle)
        if group:
            sign = np.where(np.arange(64) < 32, 1.0, -1.0)
            top, low = (alpha, beta), (sign * beta, -sign * alpha)
        else:
            use = np.where(np.arange(64) < 32, 1.0, 0.0)
            top, low = (use * alpha, use * beta), ((1 - use) * alpha, (1 - use) * beta)
        weights.append(np.concatenate([np.concatenate(top, axis=1), np.concatenate(low, axis=1)], axis=0))
    weights = np.round(np.stack(weights) * 2.0**22) / 2.0**22
    wide = np.zeros((RANK, WIDE))
    wide[:, : COLS + 1] = basis[1:].T
    wide[:, WIDE - 1] = basis[0]
    wide = np.round(wide * 2.0**26) / 2.0**26
    return split_table(wide) + split_table(weights)


ROOT = float(np.sqrt(0.5))


def over_lanes(y):
    s = [y[j] + y[j + 4] for j in range(4)]
    d = [y[j] - y[j + 4] for j in range(4)]
    even, odd = s[0] + s[2], s[1] + s[3]
    minus, plus = ROOT * (d[1] - d[3]), ROOT * (d[1] + d[3])
    return [
        (even + odd, even - odd),
        (d[0] + minus, -(d[2] + plus)),
        (s[0] - s[2], s[3] - s[1]),
        (d[0] - minus, d[2] - plus),
    ]


def to_lanes(pairs):
    (y0, y4), (u1, v1), (u2, v2), (u3, v3) = pairs
    even, odd = y0 + y4, y0 - y4
    s = [even + u2, odd - v2, even - u2, odd + v2]
    du, sv = ROOT * (u1 - u3), ROOT * (v1 + v3)
    d = [u1 + u3, du - sv, v3 - v1, -du - sv]
    return [s[j] + d[j] for j in range(4)] + [s[j] - d[j] for j in range(4)]


@functools.lru_cache(None)
def half_metric(bands):
    total = bands * ROWS
    rows = np.clip(np.arange(bands)[:, None] * ROWS - 8 + np.arange(32)[None, :], 0, total - 1)
    metric = np.minimum(1.0 / np.cos(np.pi * ((rows + 0.5) / total - 0.5)), metric_cap)
    return np.broadcast_to((0.5 * metric).astype(np.float32)[:, :, None], (bands, 32, 128)).copy()


def dot_rows(a, b):
    return lax.dot_general(a, b, (((1,), (1,)), ((), ())), preferred_element_type=F32)


def dot_cols(a, b):
    return lax.dot_general(a, b, (((1,), (0,)), ((), ())), preferred_element_type=F32)


def dot3(dot, x, high, low):
    xh = x.astype(BF16)
    xl = (x - xh.astype(F32)).astype(BF16)
    rows = x.shape[0]
    both = dot(jnp.concatenate([xh, xl], axis=0), high)
    return both[:rows] + both[rows:] + dot(xh, low)


def roll(x, shift, axis):
    return pltpu.roll(x, shift % x.shape[axis], axis)


def roll_blocks(x, shift):
    return roll(x.reshape(x.shape[0] * x.shape[1], x.shape[2]), shift, 1).reshape(x.shape)


def fold(x):
    while x.shape[0] > 1:
        half = x.shape[0] // 2
        x = x[:half] + roll_blocks(x[half:], 2 * half)
    return x


def kernel(
    bands, spread, east, north, rs, cs, cut, metric, qh_in, ql_in, wh_in, wl_in, tan_out, diag_out,
    spread_v, east_v, north_v, rs_v, cs_v, cut_s, hm, qh, ql, wh, wl,
    grid, er, hr, hc, cp, hcol, ybuf, yr, zbuf, zr, bz,
    tend, proj_p, proj_t, edge_t, edge_proj, adj, gy, tan_v, diag_v,
    in_sem, row_send, row_recv, cor_send, cor_recv, col_send, col_recv,
    y_send, y_recv, z_send, z_recv, b_send, b_recv, out_sem,
):
    b = lax.axis_index("lat")
    i = lax.axis_index("lon")
    caps = POLAR // ROWS
    is_north = b == 0
    is_south = b == bands - 1
    polar = jnp.logical_or(b < caps, b >= bands - caps)
    above_polar = jnp.logical_or(b <= caps, is_south)
    below_polar = jnp.logical_or(b >= bands - caps - 1, is_north)
    across = lax.rem(i + LANES // 2, LANES)
    west = lax.rem(i + LANES - 1, LANES)
    east_lane = lax.rem(i + 1, LANES)
    nb = jnp.where(is_north, 0, b - 1)
    nl = jnp.where(is_north, across, i)
    sb = jnp.where(is_south, bands - 1, b + 1)
    sl = jnp.where(is_south, across, i)
    slot_n = jnp.where(is_north, 0, 1)
    slot_s = jnp.where(is_south, 1, 0)
    first, last = 0, LANES - 1

    def plus(lane, d):
        return lax.rem(lane + d, LANES)

    loads = [
        pltpu.make_async_copy(spread, spread_v, in_sem.at[0]),
        pltpu.make_async_copy(rs, rs_v, in_sem.at[1]),
        pltpu.make_async_copy(cs, cs_v, in_sem.at[2]),
        pltpu.make_async_copy(east, east_v, in_sem.at[3]),
        pltpu.make_async_copy(north, north_v, in_sem.at[4]),
        pltpu.make_async_copy(metric.at[b], hm, in_sem.at[5]),
        pltpu.make_async_copy(cut, cut_s, in_sem.at[6]),
        pltpu.make_async_copy(qh_in, qh, in_sem.at[7]),
        pltpu.make_async_copy(ql_in, ql, in_sem.at[8]),
    ]
    table_loads = [
        pltpu.make_async_copy(wh_in, wh, in_sem.at[9]),
        pltpu.make_async_copy(wl_in, wl, in_sem.at[10]),
    ]
    for load in loads:
        load.start()

    @pl.when(polar)
    def _():
        for load in table_loads:
            load.start()

    barrier = pltpu.get_barrier_semaphore()

    def greet(lat, lon):
        pl.semaphore_signal(barrier, inc=1, device_id=(lat, lon), device_id_type=MESH)

    greet(nb, nl)
    greet(sb, sl)
    greet(b, west)
    greet(b, east_lane)
    greet(nb, plus(nl, 1))
    greet(nb, plus(nl, LANES - 1))
    greet(sb, plus(sl, 1))
    greet(sb, plus(sl, LANES - 1))

    @pl.when(polar)
    def _():
        @pl.loop(1, LANES)
        def _(d):
            greet(b, plus(i, d))

    @pl.when(jnp.logical_and(above_polar, jnp.logical_not(is_north)))
    def _():
        greet(nb, last)

    @pl.when(jnp.logical_and(below_polar, jnp.logical_not(is_south)))
    def _():
        greet(sb, first)

    for load in loads[:5]:
        load.wait()
    grid[:, 8:24, 384:512] = jnp.zeros((PAIRS + 2 * LEV, ROWS, 128), F32)
    row_part = jnp.concatenate([rs_v[f] for f in range(FIELDS)], axis=0)
    row_part = (2 * row_part - 1).astype(F32).T
    for f in range(FIELDS):
        col_part = (2 * cs_v[f] - 1).astype(F32)
        for l in range(LEV):
            n = f * LEV + l
            grid[n, 8:24, 0:COLS] = spread_v[f, l] * (row_part[:, n : n + 1] * col_part[l : l + 1, :])
    for l in range(LEV):
        grid[PAIRS + l, 8:24, 0:COLS] = east_v[l]
        grid[PAIRS + LEV + l, 8:24, 0:COLS] = north_v[l]

    for s, (near, far) in enumerate(((8, 9), (23, 22))):
        for f in range(FIELDS + 2):
            er[s, f if f < FIELDS else f + FIELDS] = grid[f * LEV : (f + 1) * LEV, near, :]
        for f in range(FIELDS):
            er[s, FIELDS + f] = grid[f * LEV : (f + 1) * LEV, far, :]
    lane128 = lax.broadcasted_iota(jnp.int32, (1, 1, 128), 2)
    for s, (start, shift) in enumerate(((0, 0), (384, COLS - 2 - 384))):
        tile = grid[:, 8:24, start : start + 128]
        tile = jnp.where(jnp.logical_and(lane128 >= shift, lane128 < shift + 2), tile, 0.0)
        packed = fold(tile[:PAIRS]) + roll_blocks(fold(tile[PAIRS:]), 2 * PAIRS)
        cp[s] = roll_blocks(packed, -shift)[0]

    pl.semaphore_wait(
        barrier,
        8
        + jnp.where(polar, LANES - 1, 0)
        + jnp.where(jnp.logical_and(polar, jnp.logical_and(i == first, jnp.logical_not(is_north))), LANES, 0)
        + jnp.where(jnp.logical_and(polar, jnp.logical_and(i == last, jnp.logical_not(is_south))), LANES, 0),
    )

    def remote(src, dst, send, recv, lat, lon):
        return pltpu.make_async_remote_copy(
            src_ref=src, dst_ref=dst, send_sem=send, recv_sem=recv, device_id=(lat, lon), device_id_type=MESH
        )

    halo_sends = [
        remote(er.at[0], hr.at[slot_n], row_send.at[0], row_recv.at[slot_n], nb, nl),
        remote(er.at[1], hr.at[slot_s], row_send.at[1], row_recv.at[slot_s], sb, sl),
        remote(cp.at[0], hcol.at[1], col_send.at[0], col_recv.at[1], b, west),
        remote(cp.at[1], hcol.at[0], col_send.at[1], col_recv.at[0], b, east_lane),
    ]
    for s, (slot, lat, lon) in enumerate(((slot_n, nb, nl), (slot_s, sb, sl))):
        halo_sends.append(
            remote(
                er.at[s, 0:FIELDS, :, 384:512], hc.at[slot, 0], cor_send.at[s, 0], cor_recv.at[slot, 0],
                lat, plus(lon, 1),
            )
        )
        halo_sends.append(
            remote(
                er.at[s, 0:FIELDS, :, 0:128], hc.at[slot, 1], cor_send.at[s, 1], cor_recv.at[slot, 1],
                lat, plus(lon, LANES - 1),
            )
        )
    for send in halo_sends:
        send.start()

    lane512 = lax.broadcasted_iota(jnp.int32, (1, WIDE), 1)
    own_cols = lane512 < COLS

    def y_copy(q, o):
        return remote(ybuf.at[q, o], yr.at[q, i], y_send.at[q, o], y_recv.at[q, i], b, o)

    def y_arrival(q, j):
        return remote(ybuf.at[q, j], yr.at[q, j], y_send.at[q, j], y_recv.at[q, j], b, j)

    def send_row_values(q, x):
        y = dot3(dot_rows, jnp.where(own_cols, x, 0.0), qh[...], ql[...])
        y = jnp.swapaxes(y.reshape(PAIRS, ROWS, RANK), 0, 1)
        ybuf[q] = y.reshape(LANES, 2 * PAIRS, RANK)

        @pl.loop(1, LANES)
        def _(d):
            y_copy(q, plus(i, d)).start()

        yr[q, i] = ybuf[q, i]

    def z_copy(q, j):
        return remote(zbuf.at[q, j], zr.at[q, i], z_send.at[q, j], z_recv.at[q, i], b, j)

    def z_arrival(q, j):
        return remote(zbuf.at[q, j], zr.at[q, j], z_send.at[q, j], z_recv.at[q, j], b, j)

    def edge_copy(q, j, s):
        slot, lat = ((slot_n, nb), (slot_s, sb))[s]
        over = (is_north, is_south)[s]
        lon = jnp.where(over, plus(j, LANES // 2), j)
        part = zbuf.at[q, j, PAIRS * s : PAIRS * (s + 1)]
        here = jnp.logical_and(over, lon == i)

        def away():
            return remote(part, bz.at[slot, q], b_send.at[q, j], b_recv.at[slot, q], lat, lon)

        def local():
            return pltpu.make_async_copy(part, bz.at[s, q], b_recv.at[s, q])

        return here, away, local

    def edge_sends(q, act):
        for s, owner in ((0, first), (1, last)):
            @pl.when(i == owner)
            def _():
                @pl.loop(0, LANES)
                def _(j):
                    here, away, local = edge_copy(q, j, s)

                    @pl.when(jnp.logical_not(here))
                    def _():
                        act(away())

                    if act is start_copy:
                        @pl.when(here)
                        def _():
                            local().start()

    def start_copy(copy):
        copy.start()

    def end_copy(copy):
        copy.wait_send()

    def own_rows(q):
        @pl.loop(1, LANES)
        def _(d):
            y_arrival(q, plus(i, d)).wait_recv()

        pairs = []
        for group, pair in enumerate(over_lanes([yr[q, j] for j in range(LANES)])):
            coef = dot3(dot_cols, jnp.concatenate(pair, axis=1), wh[group], wl[group])
            wave = waves_of(group, lax.broadcasted_iota(jnp.int32, (PAIRS, 2 * 64), 1))
            keep = jnp.concatenate(
                [jnp.where(wave > cut_s[2 * i + part], 2.0 / (COLS * LANES), 0.0) for part in range(2)], axis=0
            )
            back = dot3(dot_rows, coef * keep, wh[group], wl[group])
            pairs.append((back[:, :RANK], back[:, RANK:]))
        for j, z in enumerate(to_lanes(pairs)):
            zbuf[q, j] = z

        @pl.loop(1, LANES)
        def _(d):
            z_copy(q, plus(i, d)).start()

        edge_sends(q, start_copy)
        zr[q, i] = zbuf[q, i]

    def project(q, out):
        @pl.loop(1, LANES)
        def _(d):
            z_arrival(q, plus(i, d)).wait_recv()

        z = jnp.swapaxes(zr[q].reshape(ROWS, PAIRS, RANK), 0, 1).reshape(PAIRS * ROWS, RANK)
        out[...] = dot3(dot_cols, z, qh[...], ql[...]).reshape(PAIRS, ROWS, WIDE)

    for load in loads[5:]:
        load.wait()

    @pl.when(polar)
    def _():
        send_row_values(0, grid[0:PAIRS, 8:24, :].reshape(PAIRS * ROWS, WIDE))

    for s in range(2):
        remote(er.at[s], hr.at[s], row_send.at[s], row_recv.at[s], nb, nl).wait_recv()
        remote(cp.at[s], hcol.at[s], col_send.at[s], col_recv.at[s], b, west).wait_recv()
        for side in range(2):
            remote(
                er.at[s, 0:FIELDS, :, 0:128], hc.at[s, side], cor_send.at[s, side], cor_recv.at[s, side], nb, nl
            ).wait_recv()

    from_west = roll(hcol[0], 126, 1)
    from_east = roll(hcol[1], COLS - 384, 1)
    lane2 = lax.broadcasted_iota(jnp.int32, (1, 128), 1)
    both = jnp.where(jnp.logical_and(lane2 >= 66, lane2 < 114), from_east, from_west)[None]
    for width in (2, 4, 8):
        both = jnp.concatenate([both, roll_blocks(both, -width)], axis=0)
    both = jnp.concatenate([both, roll_blocks(both, -16), roll_blocks(both, -32)], axis=0)
    in_halo = jnp.logical_or(
        jnp.logical_and(lane128 >= 66, lane128 < 68), lane128 >= 126
    )
    grid[:, 8:24, 384:512] = jnp.where(in_halo, both, grid[:, 8:24, 384:512])

    flips = (-1.0, -1.0, 1.0, 1.0)
    over_pole = (is_north, is_south)
    edge_row = (7, 24)
    inward = (1.0, -1.0)

    def edge_center(s, f):
        tile = hr[s, f][:, 384:512]
        tile = jnp.where(lane2 == 66, roll(hc[s, 1, f], 66, 1), tile)
        tile = jnp.where(lane2 == 127, roll(hc[s, 0, f], 62, 1), tile)
        return jnp.concatenate([hr[s, f][:, 0:384], tile], axis=1)

    edge_probe = [[edge_center(s, f) for f in range(FIELDS)] for s in range(2)]
    for s in range(2):
        for f in range(FIELDS):
            flip = jnp.where(over_pole[s], flips[f], 1.0)
            grid[f * LEV : (f + 1) * LEV, edge_row[s], :] = flip * edge_probe[s][f]

    @pl.loop(0, LEV)
    def _(l):
        lo = jnp.maximum(l - 1, 0)
        hi = jnp.minimum(l + 1, LEV - 1)
        for h in (8, 16):
            half = jnp.concatenate([hm[h : h + 8, :]] * 4, axis=1)
            ew = grid[PAIRS + l, h : h + 8, :]
            nw = grid[PAIRS + LEV + l, h : h + 8, :]
            along_x, along_y = [], []
            for f in range(FIELDS):
                mid = grid[f * LEV + l, h : h + 8, :]
                along_x.append(half * (roll(mid, -1, 1) - roll(mid, 1, 1)))
                along_y.append(0.5 * (grid[f * LEV + l, h + 1 : h + 9, :] - grid[f * LEV + l, h - 1 : h + 7, :]))
            linked = (along_x[2], along_y[2], along_x[0] + along_y[1], None)
            for f in range(FIELDS):
                mid = grid[f * LEV + l, h : h + 8, :]
                mixed = grid[f * LEV + lo, h : h + 8, :] + grid[f * LEV + hi, h : h + 8, :] - 2.0 * mid
                t = -(ew * along_x[f] + nw * along_y[f]) + mixing * mixed
                if linked[f] is not None:
                    t = t - coupling * linked[f]
                tend[f * LEV + l, h - 8 : h, :] = t

    @pl.when(polar)
    def _():
        send_row_values(1, tend[...].reshape(PAIRS * ROWS, WIDE))

    for s in range(2):
        centers = edge_probe[s]
        half = jnp.concatenate([hm[edge_row[s] : edge_row[s] + 1, :]] * 4, axis=1)
        turn = jnp.where(over_pole[s], -inward[s], inward[s])
        along_x, along_y = [], []
        for f in range(FIELDS):
            flip = jnp.where(over_pole[s], flips[f], 1.0)
            along_x.append(half * (roll(centers[f], -1, 1) - roll(centers[f], 1, 1)))
            along_y.append((0.5 * turn) * (flip * er[s, f] - hr[s, FIELDS + f]))
        linked = (along_x[2], along_y[2], along_x[0] + along_y[1], None)
        for f in range(FIELDS):
            mid = centers[f]
            up = jnp.concatenate([mid[0:1], mid[0:3]], axis=0)
            down = jnp.concatenate([mid[1:4], mid[3:4]], axis=0)
            t = -(hr[s, 8] * along_x[f] + hr[s, 9] * along_y[f]) + mixing * (up + down - 2.0 * mid)
            if linked[f] is not None:
                t = t - coupling * linked[f]
            edge_t[s, f] = t

    @pl.when(polar)
    def _():
        for load in table_loads:
            load.wait()
        own_rows(0)
        own_rows(1)
        project(0, proj_p)
        project(1, proj_t)

    @pl.when(jnp.logical_not(polar))
    def _():
        proj_p[...] = jnp.zeros(proj_p.shape, F32)
        proj_t[...] = jnp.zeros(proj_t.shape, F32)

    for s, wanted in enumerate((above_polar, below_polar)):
        @pl.when(wanted)
        def _():
            for q in range(2):
                remote(
                    zbuf.at[q, 0, 0:PAIRS], bz.at[s, q], b_send.at[q, 0], b_recv.at[s, q], nb, nl
                ).wait_recv()
            z = bz[s].reshape(2 * PAIRS, RANK)
            edge_proj[s] = dot3(dot_cols, z, qh[...], ql[...]).reshape(2, PAIRS, WIDE)

        @pl.when(jnp.logical_not(wanted))
        def _():
            edge_proj[s] = jnp.zeros((2, PAIRS, WIDE), F32)

    def row_weights(a, nw):
        return (
            -nw * a[0],
            -nw * a[1] - coupling * a[2],
            -nw * a[2] - coupling * a[1],
            -nw * a[3],
        )

    for s in range(2):
        a = []
        for f in range(FIELDS):
            rows = slice(f * LEV, (f + 1) * LEV)
            a.append(
                edge_probe[s][f]
                + time_step * (edge_t[s, f] - edge_proj[s, 1, rows, :])
                - edge_proj[s, 0, rows, :]
            )
        for f, weight in enumerate(row_weights(a, hr[s, 9])):
            flip = jnp.where(over_pole[s], -flips[f], 1.0)
            gy[f * LEV : (f + 1) * LEV, edge_row[s], :] = flip * weight

    @pl.loop(0, LEV)
    def _(l):
        for h in (8, 16):
            nw = grid[PAIRS + LEV + l, h : h + 8, :]
            a = []
            for f in range(FIELDS):
                n = f * LEV + l
                change = time_step * (tend[n, h - 8 : h, :] - proj_t[n, h - 8 : h, :])
                tend[n, h - 8 : h, :] = change
                tangent = grid[n, h : h + 8, :] + change
                tan_v[f, l, h - 8 : h, :] = tangent[:, :COLS]
                a.append(tangent - proj_p[n, h - 8 : h, :])
                adj[n, h - 8 : h, :] = a[f]
            for f, weight in enumerate(row_weights(a, nw)):
                gy[f * LEV + l, h : h + 8, :] = weight

    tan_copy = pltpu.make_async_copy(tan_v, tan_out, out_sem.at[0])
    tan_copy.start()

    @pl.loop(0, LEV)
    def _(l):
        lo = jnp.maximum(l - 1, 0)
        hi = jnp.minimum(l + 1, LEV - 1)
        for h in (8, 16):
            rows = slice(h - 8, h)
            half = jnp.concatenate([hm[h : h + 8, :]] * 4, axis=1)
            ew = grid[PAIRS + l, h : h + 8, :]
            a = [adj[f * LEV + l, rows, :] for f in range(FIELDS)]
            col_weights = (
                -ew * a[0] - coupling * a[2],
                -ew * a[1],
                -ew * a[2] - coupling * a[0],
                -ew * a[3],
            )
            for f in range(FIELDS):
                n = f * LEV + l
                back = half * (roll(col_weights[f], 1, 1) - roll(col_weights[f], -1, 1))
                back = back + 0.5 * (gy[n, h - 1 : h + 7, :] - gy[n, h + 1 : h + 9, :])
                back = back + mixing * (adj[f * LEV + lo, rows, :] + adj[f * LEV + hi, rows, :] - 2.0 * a[f])
                diag = grid[n, h : h + 8, :] * (tend[n, rows, :] + time_step * back)
                diag_v[f, l, rows, :] = diag[:, :COLS]

    diag_copy = pltpu.make_async_copy(diag_v, diag_out, out_sem.at[1])
    diag_copy.start()

    for send in halo_sends:
        send.wait_send()

    @pl.when(polar)
    def _():
        for q in range(2):
            @pl.loop(1, LANES)
            def _(d):
                y_copy(q, plus(i, d)).wait_send()
                z_copy(q, plus(i, d)).wait_send()

            edge_sends(q, end_copy)

    tan_copy.wait()
    diag_copy.wait()


def per_device(bands, row_signs, col_signs, spread, east_wind, north_wind, cutoffs):
    any_spec = pl.BlockSpec(memory_space=pl.ANY)
    out = jax.ShapeDtypeStruct((FIELDS, LEV, ROWS, COLS), F32)
    tables = [jnp.asarray(table) for table in (half_metric(bands),) + mode_factors()]
    vmem = pltpu.VMEM
    dma = pltpu.SemaphoreType.DMA
    return pl.pallas_call(
        functools.partial(kernel, bands),
        out_shape=(out, out),
        in_specs=[any_spec] * 11,
        out_specs=(any_spec, any_spec),
        scratch_shapes=[
            vmem((FIELDS, LEV, ROWS, COLS), F32),
            vmem((LEV, ROWS, COLS), F32),
            vmem((LEV, ROWS, COLS), F32),
            vmem((FIELDS, LEV, ROWS), jnp.int32),
            vmem((FIELDS, LEV, COLS), jnp.int32),
            pltpu.SMEM((ROWS,), jnp.int32),
            vmem((32, 128), F32),
            vmem((RANK, WIDE), BF16),
            vmem((RANK, WIDE), BF16),
            vmem((4, 2 * RANK, 2 * 64), BF16),
            vmem((4, 2 * RANK, 2 * 64), BF16),
            vmem((PAIRS + 2 * LEV, 32, WIDE), F32),
            vmem((2, 10, LEV, WIDE), F32),
            vmem((2, 10, LEV, WIDE), F32),
            vmem((2, 2, FIELDS, LEV, 128), F32),
            vmem((2, ROWS, 128), F32),
            vmem((2, ROWS, 128), F32),
            vmem((2, LANES, 2 * PAIRS, RANK), F32),
            vmem((2, LANES, 2 * PAIRS, RANK), F32),
            vmem((2, LANES, 2 * PAIRS, RANK), F32),
            vmem((2, LANES, 2 * PAIRS, RANK), F32),
            vmem((2, 2, PAIRS, RANK), F32),
            vmem((PAIRS, ROWS, WIDE), F32),
            vmem((PAIRS, ROWS, WIDE), F32),
            vmem((PAIRS, ROWS, WIDE), F32),
            vmem((2, FIELDS, LEV, WIDE), F32),
            vmem((2, 2, PAIRS, WIDE), F32),
            vmem((PAIRS, ROWS, WIDE), F32),
            vmem((PAIRS, 32, WIDE), F32),
            vmem((FIELDS, LEV, ROWS, COLS), F32),
            vmem((FIELDS, LEV, ROWS, COLS), F32),
            dma((11,)),
            dma((2,)),
            dma((2,)),
            dma((2, 2)),
            dma((2, 2)),
            dma((2,)),
            dma((2,)),
            dma((2, LANES)),
            dma((2, LANES)),
            dma((2, LANES)),
            dma((2, LANES)),
            dma((2, LANES)),
            dma((2, 2)),
            dma((2,)),
        ],
        compiler_params=pltpu.CompilerParams(
            collective_id=0, has_side_effects=True, vmem_limit_bytes=64 * 2**20
        ),
        cost_estimate=pl.CostEstimate(flops=10**9, bytes_accessed=4 * 10**6, transcendentals=0),
    )(spread, east_wind, north_wind, row_signs, col_signs, cutoffs, *tables)


def solution(mesh):
    return jax.shard_map(
        functools.partial(per_device, mesh.shape["lat"]),
        mesh=mesh,
        in_specs=(
            P(None, None, "lat"),
            P(None, None, "lon"),
            P(None, None, "lat", "lon"),
            P(None, "lat", "lon"),
            P(None, "lat", "lon"),
            P("lat"),
        ),
        out_specs=(P(None, None, "lat", "lon"), P(None, None, "lat", "lon")),
        check_vma=False,
    )
```

```python
import functools

import jax
import jax.numpy as jnp
import ml_dtypes
import numpy as np
from jax import lax
from jax.experimental import pallas as pl
from jax.experimental.pallas import tpu as pltpu
from jax.sharding import PartitionSpec as P

KTOP = 256
POLAR = 32
RANK = 128
ROWS = 16
COLS = 450
WIDE = 512
LANES = 8
FIELDS = 4
LEV = 4
PAIRS = FIELDS * LEV

time_step = 0.5
coupling = 0.5
mixing = 0.2
metric_cap = 4.0

MESH = pl.DeviceIdType.MESH
F32 = jnp.float32
BF16 = jnp.bfloat16


def split_table(table):
    high = table.astype(ml_dtypes.bfloat16)
    low = (table - high.astype(np.float64)).astype(ml_dtypes.bfloat16)
    return high, low


def waves_of(group, lane_index):
    place = lane_index % 64
    second = place // 32
    other = (8 - group) if group else 4
    residue = group + second * (other - group)
    return 8 * (place % 32) + residue + (8 * (1 - second) if group == 0 else 0)


@functools.lru_cache(None)
def mode_factors():
    total = COLS * LANES
    size = COLS + 2
    place = np.arange(size, dtype=np.float64)
    width = (KTOP + 0.5) / total
    diag = ((size - 1 - 2 * place) / 2) ** 2 * np.cos(2 * np.pi * width)
    side = place[1:] * (size - place[1:]) / 2
    vectors = np.linalg.eigh(np.diag(diag) + np.diag(side, 1) + np.diag(side, -1))[1]
    basis = vectors[:, ::-1][:, :RANK]
    basis = basis * np.where(basis[size // 2] < 0, -1.0, 1.0)
    weights = []
    for group in range(4):
        waves = waves_of(group, np.arange(64))
        angle = 2 * np.pi / total * ((np.arange(size)[:, None] - 1) * waves[None, :] % total)
        alpha, beta = basis.T @ np.cos(angle), basis.T @ np.sin(angle)
        if group:
            sign = np.where(np.arange(64) < 32, 1.0, -1.0)
            top, low = (alpha, beta), (sign * beta, -sign * alpha)
        else:
            use = np.where(np.arange(64) < 32, 1.0, 0.0)
            top, low = (use * alpha, use * beta), ((1 - use) * alpha, (1 - use) * beta)
        weights.append(np.concatenate([np.concatenate(top, axis=1), np.concatenate(low, axis=1)], axis=0))
    weights = np.round(np.stack(weights) * 2.0**22) / 2.0**22
    wide = np.zeros((RANK, WIDE))
    wide[:, : COLS + 1] = basis[1:].T
    wide[:, WIDE - 1] = basis[0]
    wide = np.round(wide * 2.0**26) / 2.0**26
    wide_h, wide_l = split_table(wide)
    return np.concatenate([wide_h, wide_l, wide_h], axis=0), np.concatenate(split_table(weights), axis=2)


ROOT = float(np.sqrt(0.5))


def over_lanes(y):
    s = [y[j] + y[j + 4] for j in range(4)]
    d = [y[j] - y[j + 4] for j in range(4)]
    even, odd = s[0] + s[2], s[1] + s[3]
    minus, plus = ROOT * (d[1] - d[3]), ROOT * (d[1] + d[3])
    return [
        (even + odd, even - odd),
        (d[0] + minus, -(d[2] + plus)),
        (s[0] - s[2], s[3] - s[1]),
        (d[0] - minus, d[2] - plus),
    ]


def to_lanes(pairs):
    (y0, y4), (u1, v1), (u2, v2), (u3, v3) = pairs
    even, odd = y0 + y4, y0 - y4
    s = [even + u2, odd - v2, even - u2, odd + v2]
    du, sv = ROOT * (u1 - u3), ROOT * (v1 + v3)
    d = [u1 + u3, du - sv, v3 - v1, -du - sv]
    return [s[j] + d[j] for j in range(4)] + [s[j] - d[j] for j in range(4)]


@functools.lru_cache(None)
def half_metric(bands):
    total = bands * ROWS
    rows = np.clip(np.arange(bands)[:, None] * ROWS - 8 + np.arange(32)[None, :], 0, total - 1)
    metric = np.minimum(1.0 / np.cos(np.pi * ((rows + 0.5) / total - 0.5)), metric_cap)
    return np.broadcast_to((0.5 * metric).astype(np.float32)[:, :, None], (bands, 32, 128)).copy()


def dot_rows(a, b):
    return lax.dot_general(a, b, (((1,), (1,)), ((), ())), preferred_element_type=F32)


def dot_cols(a, b):
    return lax.dot_general(a, b, (((1,), (0,)), ((), ())), preferred_element_type=F32)


def split(x):
    high = x.astype(BF16)
    return high, (x - high.astype(F32)).astype(BF16)


def to_modes(dot, x, both, high):
    xh, xl = split(x)
    wide = dot(xh, both)
    half = wide.shape[1] // 2
    return wide[:, :half] + wide[:, half:] + dot(xl, high)


def evaluate(z, table):
    zh, zl = split(z)
    return dot_cols(jnp.concatenate([zh, zh, zl], axis=1), table[...])


def roll(x, shift, axis):
    return pltpu.roll(x, shift % x.shape[axis], axis)


def roll_blocks(x, shift):
    return roll(x.reshape(x.shape[0] * x.shape[1], x.shape[2]), shift, 1).reshape(x.shape)


def fold(x):
    while x.shape[0] > 1:
        half = x.shape[0] // 2
        x = x[:half] + roll_blocks(x[half:], 2 * half)
    return x


def kernel(
    bands, spread, east, north, rs, cs, cut, metric, q3_in, w2_in, tan_out, diag_out,
    spread_v, east_v, north_v, rs_v, cs_v, cut_s, hm, q3, w2,
    grid, er, hr, hc, cp, hcol, ybuf, yr, zbuf, zr, bz,
    tend, proj_p, proj_t, edge_t, edge_proj, adj, gy, tan_v, diag_v,
    in_sem, row_send, row_recv, cor_send, cor_recv, col_send, col_recv,
    y_send, y_recv, z_send, z_recv, b_send, b_recv, out_sem,
):
    b = lax.axis_index("lat")
    i = lax.axis_index("lon")
    caps = POLAR // ROWS
    is_north = b == 0
    is_south = b == bands - 1
    polar = jnp.logical_or(b < caps, b >= bands - caps)
    above_polar = jnp.logical_or(b <= caps, is_south)
    below_polar = jnp.logical_or(b >= bands - caps - 1, is_north)
    across = lax.rem(i + LANES // 2, LANES)
    west = lax.rem(i + LANES - 1, LANES)
    east_lane = lax.rem(i + 1, LANES)
    nb = jnp.where(is_north, 0, b - 1)
    nl = jnp.where(is_north, across, i)
    sb = jnp.where(is_south, bands - 1, b + 1)
    sl = jnp.where(is_south, across, i)
    slot_n = jnp.where(is_north, 0, 1)
    slot_s = jnp.where(is_south, 1, 0)
    first, last = 0, LANES - 1

    def plus(lane, d):
        return lax.rem(lane + d, LANES)

    loads = [
        pltpu.make_async_copy(spread, spread_v, in_sem.at[0]),
        pltpu.make_async_copy(rs, rs_v, in_sem.at[1]),
        pltpu.make_async_copy(cs, cs_v, in_sem.at[2]),
        pltpu.make_async_copy(east, east_v, in_sem.at[3]),
        pltpu.make_async_copy(north, north_v, in_sem.at[4]),
        pltpu.make_async_copy(metric.at[b], hm, in_sem.at[5]),
        pltpu.make_async_copy(cut, cut_s, in_sem.at[6]),
        pltpu.make_async_copy(q3_in, q3, in_sem.at[7]),
    ]
    table_load = pltpu.make_async_copy(w2_in, w2, in_sem.at[8])
    for load in loads:
        load.start()

    @pl.when(polar)
    def _():
        table_load.start()

    barrier = pltpu.get_barrier_semaphore()

    def greet(lat, lon):
        pl.semaphore_signal(barrier, inc=1, device_id=(lat, lon), device_id_type=MESH)

    greet(nb, nl)
    greet(sb, sl)
    greet(b, west)
    greet(b, east_lane)
    greet(nb, plus(nl, 1))
    greet(nb, plus(nl, LANES - 1))
    greet(sb, plus(sl, 1))
    greet(sb, plus(sl, LANES - 1))

    @pl.when(polar)
    def _():
        @pl.loop(1, LANES)
        def _(d):
            greet(b, plus(i, d))

    for load in loads[:5]:
        load.wait()
    grid[:, 8:24, 384:512] = jnp.zeros((PAIRS + 2 * LEV, ROWS, 128), F32)
    row_part = jnp.concatenate([rs_v[f] for f in range(FIELDS)], axis=0)
    row_part = (2 * row_part - 1).astype(F32).T
    for f in range(FIELDS):
        col_part = (2 * cs_v[f] - 1).astype(F32)
        for l in range(LEV):
            n = f * LEV + l
            grid[n, 8:24, 0:COLS] = spread_v[f, l] * (row_part[:, n : n + 1] * col_part[l : l + 1, :])
    for l in range(LEV):
        grid[PAIRS + l, 8:24, 0:COLS] = east_v[l]
        grid[PAIRS + LEV + l, 8:24, 0:COLS] = north_v[l]

    for s, (near, far) in enumerate(((8, 9), (23, 22))):
        for f in range(FIELDS + 2):
            er[s, f if f < FIELDS else f + FIELDS] = grid[f * LEV : (f + 1) * LEV, near, :]
        for f in range(FIELDS):
            er[s, FIELDS + f] = grid[f * LEV : (f + 1) * LEV, far, :]
    lane128 = lax.broadcasted_iota(jnp.int32, (1, 1, 128), 2)
    for s, (start, shift) in enumerate(((0, 0), (384, COLS - 2 - 384))):
        tile = grid[:, 8:24, start : start + 128]
        tile = jnp.where(jnp.logical_and(lane128 >= shift, lane128 < shift + 2), tile, 0.0)
        packed = fold(tile[:PAIRS]) + roll_blocks(fold(tile[PAIRS:]), 2 * PAIRS)
        cp[s] = roll_blocks(packed, -shift)[0]

    pl.semaphore_wait(barrier, 8 + jnp.where(polar, LANES - 1, 0))

    def remote(src, dst, send, recv, lat, lon):
        return pltpu.make_async_remote_copy(
            src_ref=src, dst_ref=dst, send_sem=send, recv_sem=recv, device_id=(lat, lon), device_id_type=MESH
        )

    halo_sends = [
        remote(er.at[0], hr.at[slot_n], row_send.at[0], row_recv.at[slot_n], nb, nl),
        remote(er.at[1], hr.at[slot_s], row_send.at[1], row_recv.at[slot_s], sb, sl),
        remote(cp.at[0], hcol.at[1], col_send.at[0], col_recv.at[1], b, west),
        remote(cp.at[1], hcol.at[0], col_send.at[1], col_recv.at[0], b, east_lane),
    ]
    for s, (slot, lat, lon) in enumerate(((slot_n, nb, nl), (slot_s, sb, sl))):
        halo_sends.append(
            remote(
                er.at[s, 0:FIELDS, :, 384:512], hc.at[slot, 0], cor_send.at[s, 0], cor_recv.at[slot, 0],
                lat, plus(lon, 1),
            )
        )
        halo_sends.append(
            remote(
                er.at[s, 0:FIELDS, :, 0:128], hc.at[slot, 1], cor_send.at[s, 1], cor_recv.at[slot, 1],
                lat, plus(lon, LANES - 1),
            )
        )
    for send in halo_sends:
        send.start()

    lane512 = lax.broadcasted_iota(jnp.int32, (1, WIDE), 1)
    own_cols = lane512 < COLS

    def y_copy(q, o):
        return remote(ybuf.at[q, o], yr.at[q, i], y_send.at[q, o], y_recv.at[q, i], b, o)

    def y_arrival(q, j):
        return remote(ybuf.at[q, j], yr.at[q, j], y_send.at[q, j], y_recv.at[q, j], b, j)

    def send_row_values(q, x):
        y = to_modes(dot_rows, jnp.where(own_cols, x, 0.0), q3[0 : 2 * RANK, :], q3[0:RANK, :])
        y = jnp.swapaxes(y.reshape(PAIRS, ROWS, RANK), 0, 1)
        ybuf[q] = y.reshape(LANES, 2 * PAIRS, RANK)

        @pl.loop(1, LANES)
        def _(d):
            y_copy(q, plus(i, d)).start()

        yr[q, i] = ybuf[q, i]

    def z_copy(j):
        return remote(zbuf.at[j], zr.at[i], z_send.at[j], z_recv.at[i], b, j)

    def z_arrival(j):
        return remote(zbuf.at[j], zr.at[j], z_send.at[j], z_recv.at[j], b, j)

    def own_rows():
        for q in range(2):
            @pl.loop(1, LANES)
            def _(d):
                y_arrival(q, plus(i, d)).wait_recv()

        pairs = []
        over = over_lanes([yr[:, j].reshape(4 * PAIRS, RANK) for j in range(LANES)])
        for group, pair in enumerate(over):
            coef = to_modes(dot_cols, jnp.concatenate(pair, axis=1), w2[group], w2[group, :, 0:128])
            wave = waves_of(group, lax.broadcasted_iota(jnp.int32, (PAIRS, 128), 1))
            keep = [jnp.where(wave > cut_s[2 * i + part], 2.0 / (COLS * LANES), 0.0) for part in range(2)]
            high, low = split(coef * jnp.concatenate(keep + keep, axis=0))
            back = dot_rows(jnp.concatenate([high, high], axis=1), w2[group])
            back = back + dot_rows(low, w2[group, :, 0:128])
            pairs.append((back[:, :RANK], back[:, RANK:]))
        for j, z in enumerate(to_lanes(pairs)):
            zbuf[j] = z.reshape(2, 2 * PAIRS, RANK)

        @pl.loop(1, LANES)
        def _(d):
            z_copy(plus(i, d)).start()

        zr[i] = zbuf[i]

    def edge_sends():
        return (
            remote(zr.at[first, :, 0:PAIRS], bz.at[slot_n], b_send.at[0], b_recv.at[slot_n], nb, nl),
            remote(zr.at[last, :, PAIRS : 2 * PAIRS], bz.at[slot_s], b_send.at[1], b_recv.at[slot_s], sb, sl),
        )

    def project():
        for owner, send in zip((first, last), edge_sends()):
            @pl.when(i != owner)
            def _():
                z_arrival(owner).wait_recv()

            send.start()

        @pl.loop(1, LANES)
        def _(d):
            j = plus(i, d)

            @pl.when(jnp.logical_and(j != first, j != last))
            def _():
                z_arrival(j).wait_recv()

        for q, out in enumerate((proj_p, proj_t)):
            z = jnp.swapaxes(zr[:, q].reshape(ROWS, PAIRS, RANK), 0, 1).reshape(PAIRS * ROWS, RANK)
            out[...] = evaluate(z, q3).reshape(PAIRS, ROWS, WIDE)

    for load in loads[5:]:
        load.wait()

    @pl.when(polar)
    def _():
        send_row_values(0, grid[0:PAIRS, 8:24, :].reshape(PAIRS * ROWS, WIDE))

    for s in range(2):
        remote(er.at[s], hr.at[s], row_send.at[s], row_recv.at[s], nb, nl).wait_recv()
        remote(cp.at[s], hcol.at[s], col_send.at[s], col_recv.at[s], b, west).wait_recv()
        for side in range(2):
            remote(
                er.at[s, 0:FIELDS, :, 0:128], hc.at[s, side], cor_send.at[s, side], cor_recv.at[s, side], nb, nl
            ).wait_recv()

    from_west = roll(hcol[0], 126, 1)
    from_east = roll(hcol[1], COLS - 384, 1)
    lane2 = lax.broadcasted_iota(jnp.int32, (1, 128), 1)
    both = jnp.where(jnp.logical_and(lane2 >= 66, lane2 < 114), from_east, from_west)[None]
    for width in (2, 4, 8):
        both = jnp.concatenate([both, roll_blocks(both, -width)], axis=0)
    both = jnp.concatenate([both, roll_blocks(both, -16), roll_blocks(both, -32)], axis=0)
    in_halo = jnp.logical_or(
        jnp.logical_and(lane128 >= 66, lane128 < 68), lane128 >= 126
    )
    grid[:, 8:24, 384:512] = jnp.where(in_halo, both, grid[:, 8:24, 384:512])

    flips = (-1.0, -1.0, 1.0, 1.0)
    over_pole = (is_north, is_south)
    edge_row = (7, 24)
    inward = (1.0, -1.0)

    def edge_center(s, f):
        tile = hr[s, f][:, 384:512]
        tile = jnp.where(lane2 == 66, roll(hc[s, 1, f], 66, 1), tile)
        tile = jnp.where(lane2 == 127, roll(hc[s, 0, f], 62, 1), tile)
        return jnp.concatenate([hr[s, f][:, 0:384], tile], axis=1)

    edge_probe = [[edge_center(s, f) for f in range(FIELDS)] for s in range(2)]
    for s in range(2):
        for f in range(FIELDS):
            flip = jnp.where(over_pole[s], flips[f], 1.0)
            grid[f * LEV : (f + 1) * LEV, edge_row[s], :] = flip * edge_probe[s][f]

    @pl.loop(0, LEV)
    def _(l):
        lo = jnp.maximum(l - 1, 0)
        hi = jnp.minimum(l + 1, LEV - 1)
        for h in (8, 16):
            half = jnp.concatenate([hm[h : h + 8, :]] * 4, axis=1)
            ew = grid[PAIRS + l, h : h + 8, :]
            nw = grid[PAIRS + LEV + l, h : h + 8, :]
            along_x, along_y = [], []
            for f in range(FIELDS):
                mid = grid[f * LEV + l, h : h + 8, :]
                along_x.append(half * (roll(mid, -1, 1) - roll(mid, 1, 1)))
                along_y.append(0.5 * (grid[f * LEV + l, h + 1 : h + 9, :] - grid[f * LEV + l, h - 1 : h + 7, :]))
            linked = (along_x[2], along_y[2], along_x[0] + along_y[1], None)
            for f in range(FIELDS):
                mid = grid[f * LEV + l, h : h + 8, :]
                mixed = grid[f * LEV + lo, h : h + 8, :] + grid[f * LEV + hi, h : h + 8, :] - 2.0 * mid
                t = -(ew * along_x[f] + nw * along_y[f]) + mixing * mixed
                if linked[f] is not None:
                    t = t - coupling * linked[f]
                tend[f * LEV + l, h - 8 : h, :] = t

    @pl.when(polar)
    def _():
        send_row_values(1, tend[...].reshape(PAIRS * ROWS, WIDE))

    for s in range(2):
        centers = edge_probe[s]
        half = jnp.concatenate([hm[edge_row[s] : edge_row[s] + 1, :]] * 4, axis=1)
        turn = jnp.where(over_pole[s], -inward[s], inward[s])
        along_x, along_y = [], []
        for f in range(FIELDS):
            flip = jnp.where(over_pole[s], flips[f], 1.0)
            along_x.append(half * (roll(centers[f], -1, 1) - roll(centers[f], 1, 1)))
            along_y.append((0.5 * turn) * (flip * er[s, f] - hr[s, FIELDS + f]))
        linked = (along_x[2], along_y[2], along_x[0] + along_y[1], None)
        for f in range(FIELDS):
            mid = centers[f]
            up = jnp.concatenate([mid[0:1], mid[0:3]], axis=0)
            down = jnp.concatenate([mid[1:4], mid[3:4]], axis=0)
            t = -(hr[s, 8] * along_x[f] + hr[s, 9] * along_y[f]) + mixing * (up + down - 2.0 * mid)
            if linked[f] is not None:
                t = t - coupling * linked[f]
            edge_t[s, f] = t

    @pl.when(polar)
    def _():
        table_load.wait()
        own_rows()
        project()

    @pl.when(jnp.logical_not(polar))
    def _():
        proj_p[...] = jnp.zeros(proj_p.shape, F32)
        proj_t[...] = jnp.zeros(proj_t.shape, F32)

    def row_weights(a, nw):
        return (
            -nw * a[0],
            -nw * a[1] - coupling * a[2],
            -nw * a[2] - coupling * a[1],
            -nw * a[3],
        )

    @pl.loop(0, LEV)
    def _(l):
        for h in (8, 16):
            nw = grid[PAIRS + LEV + l, h : h + 8, :]
            a = []
            for f in range(FIELDS):
                n = f * LEV + l
                change = time_step * (tend[n, h - 8 : h, :] - proj_t[n, h - 8 : h, :])
                tend[n, h - 8 : h, :] = change
                tangent = grid[n, h : h + 8, :] + change
                tan_v[f, l, h - 8 : h, :] = tangent[:, :COLS]
                a.append(tangent - proj_p[n, h - 8 : h, :])
                adj[n, h - 8 : h, :] = a[f]
            for f, weight in enumerate(row_weights(a, nw)):
                gy[f * LEV + l, h : h + 8, :] = weight

    tan_copy = pltpu.make_async_copy(tan_v, tan_out, out_sem.at[0])
    tan_copy.start()

    for s, wanted in enumerate((above_polar, below_polar)):
        @pl.when(wanted)
        def _():
            remote(zr.at[first, :, 0:PAIRS], bz.at[s], b_send.at[0], b_recv.at[s], nb, nl).wait_recv()
            edge_proj[s] = evaluate(bz[s].reshape(2 * PAIRS, RANK), q3).reshape(2, PAIRS, WIDE)

        @pl.when(jnp.logical_not(wanted))
        def _():
            edge_proj[s] = jnp.zeros((2, PAIRS, WIDE), F32)

    for s in range(2):
        a = []
        for f in range(FIELDS):
            rows = slice(f * LEV, (f + 1) * LEV)
            a.append(
                edge_probe[s][f]
                + time_step * (edge_t[s, f] - edge_proj[s, 1, rows, :])
                - edge_proj[s, 0, rows, :]
            )
        for f, weight in enumerate(row_weights(a, hr[s, 9])):
            flip = jnp.where(over_pole[s], -flips[f], 1.0)
            gy[f * LEV : (f + 1) * LEV, edge_row[s], :] = flip * weight

    @pl.loop(0, LEV)
    def _(l):
        lo = jnp.maximum(l - 1, 0)
        hi = jnp.minimum(l + 1, LEV - 1)
        for h in (8, 16):
            rows = slice(h - 8, h)
            half = jnp.concatenate([hm[h : h + 8, :]] * 4, axis=1)
            ew = grid[PAIRS + l, h : h + 8, :]
            a = [adj[f * LEV + l, rows, :] for f in range(FIELDS)]
            col_weights = (
                -ew * a[0] - coupling * a[2],
                -ew * a[1],
                -ew * a[2] - coupling * a[0],
                -ew * a[3],
            )
            for f in range(FIELDS):
                n = f * LEV + l
                back = half * (roll(col_weights[f], 1, 1) - roll(col_weights[f], -1, 1))
                back = back + 0.5 * (gy[n, h - 1 : h + 7, :] - gy[n, h + 1 : h + 9, :])
                back = back + mixing * (adj[f * LEV + lo, rows, :] + adj[f * LEV + hi, rows, :] - 2.0 * a[f])
                diag = grid[n, h : h + 8, :] * (tend[n, rows, :] + time_step * back)
                diag_v[f, l, rows, :] = diag[:, :COLS]

    diag_copy = pltpu.make_async_copy(diag_v, diag_out, out_sem.at[1])
    diag_copy.start()

    for send in halo_sends:
        send.wait_send()

    @pl.when(polar)
    def _():
        @pl.loop(1, LANES)
        def _(d):
            j = plus(i, d)
            y_copy(0, j).wait_send()
            y_copy(1, j).wait_send()
            z_copy(j).wait_send()

        for send in edge_sends():
            send.wait_send()

    tan_copy.wait()
    diag_copy.wait()


def hand_out(tan_in, diag_in, tan_out, diag_out, sem):
    copies = [
        pltpu.make_async_copy(src.at[f], dst.at[f], sem.at[n, f])
        for n, (src, dst) in enumerate(((tan_in, tan_out), (diag_in, diag_out)))
        for f in range(FIELDS)
    ]
    for copy in copies:
        copy.start()
    for copy in copies:
        copy.wait()


def per_device(bands, row_signs, col_signs, spread, east_wind, north_wind, cutoffs):
    any_spec = pl.BlockSpec(memory_space=pl.ANY)
    out = jax.ShapeDtypeStruct((FIELDS, LEV, ROWS, COLS), F32)
    tables = [jnp.asarray(table) for table in (half_metric(bands),) + mode_factors()]
    vmem = pltpu.VMEM
    dma = pltpu.SemaphoreType.DMA
    results = pl.pallas_call(
        functools.partial(kernel, bands),
        out_shape=(out, out),
        in_specs=[any_spec] * 9,
        out_specs=(any_spec, any_spec),
        scratch_shapes=[
            vmem((FIELDS, LEV, ROWS, COLS), F32),
            vmem((LEV, ROWS, COLS), F32),
            vmem((LEV, ROWS, COLS), F32),
            vmem((FIELDS, LEV, ROWS), jnp.int32),
            vmem((FIELDS, LEV, COLS), jnp.int32),
            pltpu.SMEM((ROWS,), jnp.int32),
            vmem((32, 128), F32),
            vmem((3 * RANK, WIDE), BF16),
            vmem((4, 2 * RANK, 4 * 64), BF16),
            vmem((PAIRS + 2 * LEV, 32, WIDE), F32),
            vmem((2, 10, LEV, WIDE), F32),
            vmem((2, 10, LEV, WIDE), F32),
            vmem((2, 2, FIELDS, LEV, 128), F32),
            vmem((2, ROWS, 128), F32),
            vmem((2, ROWS, 128), F32),
            vmem((2, LANES, 2 * PAIRS, RANK), F32),
            vmem((2, LANES, 2 * PAIRS, RANK), F32),
            vmem((LANES, 2, 2 * PAIRS, RANK), F32),
            vmem((LANES, 2, 2 * PAIRS, RANK), F32),
            vmem((2, 2, PAIRS, RANK), F32),
            vmem((PAIRS, ROWS, WIDE), F32),
            vmem((PAIRS, ROWS, WIDE), F32),
            vmem((PAIRS, ROWS, WIDE), F32),
            vmem((2, FIELDS, LEV, WIDE), F32),
            vmem((2, 2, PAIRS, WIDE), F32),
            vmem((PAIRS, ROWS, WIDE), F32),
            vmem((PAIRS, 32, WIDE), F32),
            vmem((FIELDS, LEV, ROWS, COLS), F32),
            vmem((FIELDS, LEV, ROWS, COLS), F32),
            dma((9,)),
            dma((2,)),
            dma((2,)),
            dma((2, 2)),
            dma((2, 2)),
            dma((2,)),
            dma((2,)),
            dma((2, LANES)),
            dma((2, LANES)),
            dma((LANES,)),
            dma((LANES,)),
            dma((2,)),
            dma((2,)),
            dma((2,)),
        ],
        compiler_params=pltpu.CompilerParams(
            collective_id=0, has_side_effects=True, vmem_limit_bytes=64 * 2**20
        ),
        cost_estimate=pl.CostEstimate(flops=10**9, bytes_accessed=4 * 10**6, transcendentals=0),
    )(spread, east_wind, north_wind, row_signs, col_signs, cutoffs, *tables)
    return pl.pallas_call(
        hand_out,
        out_shape=(out, out),
        in_specs=[any_spec] * 2,
        out_specs=(any_spec, any_spec),
        scratch_shapes=[dma((2, FIELDS))],
        compiler_params=pltpu.CompilerParams(vmem_limit_bytes=64 * 2**20),
    )(*results)


def solution(mesh):
    return jax.shard_map(
        functools.partial(per_device, mesh.shape["lat"]),
        mesh=mesh,
        in_specs=(
            P(None, None, "lat"),
            P(None, None, "lon"),
            P(None, None, "lat", "lon"),
            P(None, "lat", "lon"),
            P(None, "lat", "lon"),
            P("lat"),
        ),
        out_specs=(P(None, None, "lat", "lon"), P(None, None, "lat", "lon")),
        check_vma=False,
    )
```

```python
import functools

import jax
import jax.numpy as jnp
import ml_dtypes
import numpy as np
from jax import lax
from jax.experimental import pallas as pl
from jax.experimental.pallas import tpu as pltpu
from jax.sharding import PartitionSpec as P

KTOP = 256
POLAR = 32
RANK = 128
ROWS = 16
COLS = 450
WIDE = 512
LANES = 8
FIELDS = 4
LEV = 4
PAIRS = FIELDS * LEV

time_step = 0.5
coupling = 0.5
mixing = 0.2
metric_cap = 4.0

MESH = pl.DeviceIdType.MESH
F32 = jnp.float32
BF16 = jnp.bfloat16


def split_table(table):
    high = table.astype(ml_dtypes.bfloat16)
    low = (table - high.astype(np.float64)).astype(ml_dtypes.bfloat16)
    return high, low


def waves_of(group, lane_index):
    place = lane_index % 64
    second = place // 32
    other = (8 - group) if group else 4
    residue = group + second * (other - group)
    return 8 * (place % 32) + residue + (8 * (1 - second) if group == 0 else 0)


@functools.lru_cache(None)
def mode_factors():
    total = COLS * LANES
    size = COLS + 2
    place = np.arange(size, dtype=np.float64)
    width = (KTOP + 0.5) / total
    diag = ((size - 1 - 2 * place) / 2) ** 2 * np.cos(2 * np.pi * width)
    side = place[1:] * (size - place[1:]) / 2
    vectors = np.linalg.eigh(np.diag(diag) + np.diag(side, 1) + np.diag(side, -1))[1]
    basis = vectors[:, ::-1][:, :RANK]
    basis = basis * np.where(basis[size // 2] < 0, -1.0, 1.0)
    weights = []
    for group in range(4):
        waves = waves_of(group, np.arange(64))
        angle = 2 * np.pi / total * ((np.arange(size)[:, None] - 1) * waves[None, :] % total)
        alpha, beta = basis.T @ np.cos(angle), basis.T @ np.sin(angle)
        if group:
            sign = np.where(np.arange(64) < 32, 1.0, -1.0)
            top, low = (alpha, beta), (sign * beta, -sign * alpha)
        else:
            use = np.where(np.arange(64) < 32, 1.0, 0.0)
            top, low = (use * alpha, use * beta), ((1 - use) * alpha, (1 - use) * beta)
        weights.append(np.concatenate([np.concatenate(top, axis=1), np.concatenate(low, axis=1)], axis=0))
    weights = np.round(np.stack(weights) * 2.0**22) / 2.0**22
    wide = np.zeros((RANK, WIDE))
    wide[:, : COLS + 1] = basis[1:].T
    wide[:, WIDE - 1] = basis[0]
    wide = np.round(wide * 2.0**26) / 2.0**26
    wide_h, wide_l = split_table(wide)
    return np.concatenate([wide_h, wide_l, wide_h], axis=0), np.concatenate(split_table(weights), axis=2)


ROOT = float(np.sqrt(0.5))


def over_lanes(y):
    s = [y[j] + y[j + 4] for j in range(4)]
    d = [y[j] - y[j + 4] for j in range(4)]
    even, odd = s[0] + s[2], s[1] + s[3]
    minus, plus = ROOT * (d[1] - d[3]), ROOT * (d[1] + d[3])
    return [
        (even + odd, even - odd),
        (d[0] + minus, -(d[2] + plus)),
        (s[0] - s[2], s[3] - s[1]),
        (d[0] - minus, d[2] - plus),
    ]


def to_lanes(pairs):
    (y0, y4), (u1, v1), (u2, v2), (u3, v3) = pairs
    even, odd = y0 + y4, y0 - y4
    s = [even + u2, odd - v2, even - u2, odd + v2]
    du, sv = ROOT * (u1 - u3), ROOT * (v1 + v3)
    d = [u1 + u3, du - sv, v3 - v1, -du - sv]
    return [s[j] + d[j] for j in range(4)] + [s[j] - d[j] for j in range(4)]


@functools.lru_cache(None)
def half_metric(bands):
    total = bands * ROWS
    rows = np.clip(np.arange(bands)[:, None] * ROWS - 8 + np.arange(32)[None, :], 0, total - 1)
    metric = np.minimum(1.0 / np.cos(np.pi * ((rows + 0.5) / total - 0.5)), metric_cap)
    return np.broadcast_to((0.5 * metric).astype(np.float32)[:, :, None], (bands, 32, 128)).copy()


def dot_rows(a, b):
    return lax.dot_general(a, b, (((1,), (1,)), ((), ())), preferred_element_type=F32)


def dot_cols(a, b):
    return lax.dot_general(a, b, (((1,), (0,)), ((), ())), preferred_element_type=F32)


def split(x):
    high = x.astype(BF16)
    return high, (x - high.astype(F32)).astype(BF16)


def to_modes(dot, x, both, high):
    xh, xl = split(x)
    wide = dot(xh, both)
    half = wide.shape[1] // 2
    return wide[:, :half] + wide[:, half:] + dot(xl, high)


def evaluate(z, table):
    zh, zl = split(z)
    return dot_cols(jnp.concatenate([zh, zh, zl], axis=1), table[...])


def roll(x, shift, axis):
    return pltpu.roll(x, shift % x.shape[axis], axis)


def roll_blocks(x, shift):
    return roll(x.reshape(x.shape[0] * x.shape[1], x.shape[2]), shift, 1).reshape(x.shape)


def fold(x):
    while x.shape[0] > 1:
        half = x.shape[0] // 2
        x = x[:half] + roll_blocks(x[half:], 2 * half)
    return x


def kernel(
    bands, spread, east, north, rs, cs, cut, metric, q3_in, w2_in, tan_out, diag_out,
    spread_v, east_v, north_v, rs_v, cs_v, cut_s, hm, q3, w2,
    grid, er, hr, hc, cp, hcol, ybuf, yr, zbuf, zr, eb, bz,
    tend, proj_p, proj_t, edge_t, edge_proj, adj, gy, tan_v, diag_v,
    in_sem, row_send, row_recv, cor_send, cor_recv, col_send, col_recv,
    y_send, y_recv, z_send, z_recv, b_send, b_recv, out_sem,
):
    b = lax.axis_index("lat")
    i = lax.axis_index("lon")
    caps = POLAR // ROWS
    is_north = b == 0
    is_south = b == bands - 1
    polar = jnp.logical_or(b < caps, b >= bands - caps)
    above_polar = jnp.logical_or(b <= caps, is_south)
    below_polar = jnp.logical_or(b >= bands - caps - 1, is_north)
    across = lax.rem(i + LANES // 2, LANES)
    west = lax.rem(i + LANES - 1, LANES)
    east_lane = lax.rem(i + 1, LANES)
    nb = jnp.where(is_north, 0, b - 1)
    nl = jnp.where(is_north, across, i)
    sb = jnp.where(is_south, bands - 1, b + 1)
    sl = jnp.where(is_south, across, i)
    slot_n = jnp.where(is_north, 0, 1)
    slot_s = jnp.where(is_south, 1, 0)

    def plus(lane, d):
        return lax.rem(lane + d, LANES)

    loads = [
        pltpu.make_async_copy(spread, spread_v, in_sem.at[0]),
        pltpu.make_async_copy(rs, rs_v, in_sem.at[1]),
        pltpu.make_async_copy(cs, cs_v, in_sem.at[2]),
        pltpu.make_async_copy(east, east_v, in_sem.at[3]),
        pltpu.make_async_copy(north, north_v, in_sem.at[4]),
        pltpu.make_async_copy(metric.at[b], hm, in_sem.at[5]),
        pltpu.make_async_copy(cut, cut_s, in_sem.at[6]),
        pltpu.make_async_copy(q3_in, q3, in_sem.at[7]),
    ]
    table_load = pltpu.make_async_copy(w2_in, w2, in_sem.at[8])
    for load in loads:
        load.start()

    @pl.when(polar)
    def _():
        table_load.start()

    barrier = pltpu.get_barrier_semaphore()

    def greet(lat, lon):
        pl.semaphore_signal(barrier, inc=1, device_id=(lat, lon), device_id_type=MESH)

    greet(nb, nl)
    greet(sb, sl)
    greet(b, west)
    greet(b, east_lane)
    greet(nb, plus(nl, 1))
    greet(nb, plus(nl, LANES - 1))
    greet(sb, plus(sl, 1))
    greet(sb, plus(sl, LANES - 1))

    @pl.when(polar)
    def _():
        @pl.loop(1, LANES)
        def _(d):
            greet(b, plus(i, d))

    for load in loads[:5]:
        load.wait()
    grid[:, 8:24, 384:512] = jnp.zeros((PAIRS + 2 * LEV, ROWS, 128), F32)
    row_part = jnp.concatenate([rs_v[f] for f in range(FIELDS)], axis=0)
    row_part = (2 * row_part - 1).astype(F32).T
    for f in range(FIELDS):
        col_part = (2 * cs_v[f] - 1).astype(F32)
        for l in range(LEV):
            n = f * LEV + l
            grid[n, 8:24, 0:COLS] = spread_v[f, l] * (row_part[:, n : n + 1] * col_part[l : l + 1, :])
    for l in range(LEV):
        grid[PAIRS + l, 8:24, 0:COLS] = east_v[l]
        grid[PAIRS + LEV + l, 8:24, 0:COLS] = north_v[l]

    for s, (near, far) in enumerate(((8, 9), (23, 22))):
        for f in range(FIELDS + 2):
            er[s, f if f < FIELDS else f + FIELDS] = grid[f * LEV : (f + 1) * LEV, near, :]
        for f in range(FIELDS):
            er[s, FIELDS + f] = grid[f * LEV : (f + 1) * LEV, far, :]
    lane128 = lax.broadcasted_iota(jnp.int32, (1, 1, 128), 2)
    for s, (start, shift) in enumerate(((0, 0), (384, COLS - 2 - 384))):
        tile = grid[:, 8:24, start : start + 128]
        tile = jnp.where(jnp.logical_and(lane128 >= shift, lane128 < shift + 2), tile, 0.0)
        packed = fold(tile[:PAIRS]) + roll_blocks(fold(tile[PAIRS:]), 2 * PAIRS)
        cp[s] = roll_blocks(packed, -shift)[0]

    pl.semaphore_wait(barrier, 8 + jnp.where(polar, LANES - 1, 0))

    def remote(src, dst, send, recv, lat, lon):
        return pltpu.make_async_remote_copy(
            src_ref=src, dst_ref=dst, send_sem=send, recv_sem=recv, device_id=(lat, lon), device_id_type=MESH
        )

    halo_sends = [
        remote(er.at[0], hr.at[slot_n], row_send.at[0], row_recv.at[slot_n], nb, nl),
        remote(er.at[1], hr.at[slot_s], row_send.at[1], row_recv.at[slot_s], sb, sl),
        remote(cp.at[0], hcol.at[1], col_send.at[0], col_recv.at[1], b, west),
        remote(cp.at[1], hcol.at[0], col_send.at[1], col_recv.at[0], b, east_lane),
    ]
    for s, (slot, lat, lon) in enumerate(((slot_n, nb, nl), (slot_s, sb, sl))):
        halo_sends.append(
            remote(
                er.at[s, 0:FIELDS, :, 384:512], hc.at[slot, 0], cor_send.at[s, 0], cor_recv.at[slot, 0],
                lat, plus(lon, 1),
            )
        )
        halo_sends.append(
            remote(
                er.at[s, 0:FIELDS, :, 0:128], hc.at[slot, 1], cor_send.at[s, 1], cor_recv.at[slot, 1],
                lat, plus(lon, LANES - 1),
            )
        )
    for send in halo_sends:
        send.start()

    lane512 = lax.broadcasted_iota(jnp.int32, (1, WIDE), 1)
    own_cols = lane512 < COLS

    def y_copy(q, o):
        return remote(ybuf.at[q, o], yr.at[q, i], y_send.at[q, o], y_recv.at[q, i], b, o)

    def y_arrival(q, j):
        return remote(ybuf.at[q, j], yr.at[q, j], y_send.at[q, j], y_recv.at[q, j], b, j)

    def row_values(x):
        return to_modes(dot_rows, jnp.where(own_cols, x, 0.0), q3[0 : 2 * RANK, :], q3[0:RANK, :])

    def send_probe_values():
        y = row_values(grid[0:PAIRS, 8:24, :].reshape(PAIRS * ROWS, WIDE)).reshape(FIELDS, LEV, 2, 8, RANK)
        for f in range(FIELDS):
            for h in range(2):
                for l in range(LEV):
                    ybuf[0, 2 * f + h, l] = y[f, l, h]

        @pl.loop(1, LANES)
        def _(d):
            y_copy(0, plus(i, d)).start()

        yr[0, i] = ybuf[0, i]

    def send_tendency_values(h):
        y = row_values(tend[:, 8 * h : 8 * h + 8, :].reshape(PAIRS * 8, WIDE)).reshape(FIELDS, LEV, 8, RANK)
        for f in range(FIELDS):
            ybuf[1, 2 * f + h] = y[f]

        @pl.loop(0, FIELDS)
        def _(d):
            o = 2 * lax.rem(i // 2 + d, FIELDS) + h

            @pl.when(o != i)
            def _():
                y_copy(1, o).start()

            @pl.when(o == i)
            def _():
                yr[1, i] = ybuf[1, i]

    def z_copy(q, j):
        return remote(zbuf.at[q, j], zr.at[q, i], z_send.at[q, j], z_recv.at[q, i], b, j)

    def z_arrival(q, j):
        return remote(zbuf.at[q, j], zr.at[q, j], z_send.at[q, j], z_recv.at[q, j], b, j)

    def own_rows(q):
        row = lax.broadcasted_iota(jnp.int32, (8, 128), 0)
        cutoff = jnp.zeros((8, 128), jnp.int32)
        for r in range(8):
            cutoff = jnp.where(row == r, cut_s[8 * lax.rem(i, 2) + r], cutoff)

        @pl.loop(1, LANES)
        def _(d):
            y_arrival(q, plus(i, d)).wait_recv()

        pairs = []
        over = over_lanes([yr[q, j].reshape(LEV * 8, RANK) for j in range(LANES)])
        for group, pair in enumerate(over):
            coef = to_modes(dot_cols, jnp.concatenate(pair, axis=1), w2[group], w2[group, :, 0:128])
            wave = waves_of(group, lax.broadcasted_iota(jnp.int32, (8, 128), 1))
            keep = jnp.where(wave > cutoff, 2.0 / (COLS * LANES), 0.0)
            high, low = split(coef * jnp.concatenate([keep] * LEV, axis=0))
            back = dot_rows(jnp.concatenate([high, high], axis=1), w2[group])
            back = back + dot_rows(low, w2[group, :, 0:128])
            pairs.append((back[:, :RANK], back[:, RANK:]))
        for j, z in enumerate(to_lanes(pairs)):
            zbuf[q, j] = z.reshape(LEV, 8, RANK)

        @pl.loop(1, LANES)
        def _(d):
            z_copy(q, plus(i, d)).start()

        zr[q, i] = zbuf[q, i]

    def edge_send(q, s):
        slot, lat, lon = ((slot_n, nb, nl), (slot_s, sb, sl))[s]
        return remote(eb.at[s, q], bz.at[slot, q], b_send.at[s, q], b_recv.at[slot, q], lat, lon)

    def project(q, out):
        @pl.loop(1, LANES)
        def _(d):
            z_arrival(q, plus(i, d)).wait_recv()

        for s, row in ((0, 0), (1, 7)):
            for f in range(FIELDS):
                eb[s, q, f * LEV : (f + 1) * LEV, :] = zr[q, 2 * f + s, :, row, :]
            edge_send(q, s).start()
        z = jnp.concatenate(
            [zr[q, 2 * f + h, l] for f in range(FIELDS) for l in range(LEV) for h in range(2)], axis=0
        )
        out[...] = evaluate(z, q3).reshape(PAIRS, ROWS, WIDE)

    for load in loads[5:]:
        load.wait()

    @pl.when(polar)
    def _():
        send_probe_values()

    for s in range(2):
        remote(er.at[s], hr.at[s], row_send.at[s], row_recv.at[s], nb, nl).wait_recv()
        remote(cp.at[s], hcol.at[s], col_send.at[s], col_recv.at[s], b, west).wait_recv()
        for side in range(2):
            remote(
                er.at[s, 0:FIELDS, :, 0:128], hc.at[s, side], cor_send.at[s, side], cor_recv.at[s, side], nb, nl
            ).wait_recv()

    from_west = roll(hcol[0], 126, 1)
    from_east = roll(hcol[1], COLS - 384, 1)
    lane2 = lax.broadcasted_iota(jnp.int32, (1, 128), 1)
    both = jnp.where(jnp.logical_and(lane2 >= 66, lane2 < 114), from_east, from_west)[None]
    for width in (2, 4, 8):
        both = jnp.concatenate([both, roll_blocks(both, -width)], axis=0)
    both = jnp.concatenate([both, roll_blocks(both, -16), roll_blocks(both, -32)], axis=0)
    in_halo = jnp.logical_or(
        jnp.logical_and(lane128 >= 66, lane128 < 68), lane128 >= 126
    )
    grid[:, 8:24, 384:512] = jnp.where(in_halo, both, grid[:, 8:24, 384:512])

    flips = (-1.0, -1.0, 1.0, 1.0)
    over_pole = (is_north, is_south)
    edge_row = (7, 24)
    inward = (1.0, -1.0)

    def edge_center(s, f):
        tile = hr[s, f][:, 384:512]
        tile = jnp.where(lane2 == 66, roll(hc[s, 1, f], 66, 1), tile)
        tile = jnp.where(lane2 == 127, roll(hc[s, 0, f], 62, 1), tile)
        return jnp.concatenate([hr[s, f][:, 0:384], tile], axis=1)

    edge_probe = [[edge_center(s, f) for f in range(FIELDS)] for s in range(2)]
    for s in range(2):
        for f in range(FIELDS):
            flip = jnp.where(over_pole[s], flips[f], 1.0)
            grid[f * LEV : (f + 1) * LEV, edge_row[s], :] = flip * edge_probe[s][f]

    def tendency_rows(h):
        @pl.loop(0, LEV)
        def _(l):
            lo = jnp.maximum(l - 1, 0)
            hi = jnp.minimum(l + 1, LEV - 1)
            half = jnp.concatenate([hm[h : h + 8, :]] * 4, axis=1)
            ew = grid[PAIRS + l, h : h + 8, :]
            nw = grid[PAIRS + LEV + l, h : h + 8, :]
            along_x, along_y = [], []
            for f in range(FIELDS):
                mid = grid[f * LEV + l, h : h + 8, :]
                along_x.append(half * (roll(mid, -1, 1) - roll(mid, 1, 1)))
                along_y.append(0.5 * (grid[f * LEV + l, h + 1 : h + 9, :] - grid[f * LEV + l, h - 1 : h + 7, :]))
            linked = (along_x[2], along_y[2], along_x[0] + along_y[1], None)
            for f in range(FIELDS):
                mid = grid[f * LEV + l, h : h + 8, :]
                mixed = grid[f * LEV + lo, h : h + 8, :] + grid[f * LEV + hi, h : h + 8, :] - 2.0 * mid
                t = -(ew * along_x[f] + nw * along_y[f]) + mixing * mixed
                if linked[f] is not None:
                    t = t - coupling * linked[f]
                tend[f * LEV + l, h - 8 : h, :] = t

    for part in range(2):
        tendency_rows(8 + 8 * part)

        @pl.when(polar)
        def _():
            send_tendency_values(part)

    @pl.when(polar)
    def _():
        table_load.wait()
        own_rows(0)

    for s in range(2):
        centers = edge_probe[s]
        half = jnp.concatenate([hm[edge_row[s] : edge_row[s] + 1, :]] * 4, axis=1)
        turn = jnp.where(over_pole[s], -inward[s], inward[s])
        along_x, along_y = [], []
        for f in range(FIELDS):
            flip = jnp.where(over_pole[s], flips[f], 1.0)
            along_x.append(half * (roll(centers[f], -1, 1) - roll(centers[f], 1, 1)))
            along_y.append((0.5 * turn) * (flip * er[s, f] - hr[s, FIELDS + f]))
        linked = (along_x[2], along_y[2], along_x[0] + along_y[1], None)
        for f in range(FIELDS):
            mid = centers[f]
            up = jnp.concatenate([mid[0:1], mid[0:3]], axis=0)
            down = jnp.concatenate([mid[1:4], mid[3:4]], axis=0)
            t = -(hr[s, 8] * along_x[f] + hr[s, 9] * along_y[f]) + mixing * (up + down - 2.0 * mid)
            if linked[f] is not None:
                t = t - coupling * linked[f]
            edge_t[s, f] = t

    @pl.when(polar)
    def _():
        own_rows(1)
        project(0, proj_p)
        project(1, proj_t)

    @pl.when(jnp.logical_not(polar))
    def _():
        proj_p[...] = jnp.zeros(proj_p.shape, F32)
        proj_t[...] = jnp.zeros(proj_t.shape, F32)

    def row_weights(a, nw):
        return (
            -nw * a[0],
            -nw * a[1] - coupling * a[2],
            -nw * a[2] - coupling * a[1],
            -nw * a[3],
        )

    @pl.loop(0, LEV)
    def _(l):
        for h in (8, 16):
            nw = grid[PAIRS + LEV + l, h : h + 8, :]
            a = []
            for f in range(FIELDS):
                n = f * LEV + l
                change = time_step * (tend[n, h - 8 : h, :] - proj_t[n, h - 8 : h, :])
                tend[n, h - 8 : h, :] = change
                tangent = grid[n, h : h + 8, :] + change
                tan_v[f, l, h - 8 : h, :] = tangent[:, :COLS]
                a.append(tangent - proj_p[n, h - 8 : h, :])
                adj[n, h - 8 : h, :] = a[f]
            for f, weight in enumerate(row_weights(a, nw)):
                gy[f * LEV + l, h : h + 8, :] = weight

    tan_copy = pltpu.make_async_copy(tan_v, tan_out, out_sem.at[0])
    tan_copy.start()

    for s, wanted in enumerate((above_polar, below_polar)):
        @pl.when(wanted)
        def _():
            for q in range(2):
                remote(eb.at[s, q], bz.at[s, q], b_send.at[s, q], b_recv.at[s, q], nb, nl).wait_recv()
            edge_proj[s] = evaluate(bz[s].reshape(2 * PAIRS, RANK), q3).reshape(2, PAIRS, WIDE)

        @pl.when(jnp.logical_not(wanted))
        def _():
            edge_proj[s] = jnp.zeros((2, PAIRS, WIDE), F32)

    for s in range(2):
        a = []
        for f in range(FIELDS):
            rows = slice(f * LEV, (f + 1) * LEV)
            a.append(
                edge_probe[s][f]
                + time_step * (edge_t[s, f] - edge_proj[s, 1, rows, :])
                - edge_proj[s, 0, rows, :]
            )
        for f, weight in enumerate(row_weights(a, hr[s, 9])):
            flip = jnp.where(over_pole[s], -flips[f], 1.0)
            gy[f * LEV : (f + 1) * LEV, edge_row[s], :] = flip * weight

    @pl.loop(0, LEV)
    def _(l):
        lo = jnp.maximum(l - 1, 0)
        hi = jnp.minimum(l + 1, LEV - 1)
        for h in (8, 16):
            rows = slice(h - 8, h)
            half = jnp.concatenate([hm[h : h + 8, :]] * 4, axis=1)
            ew = grid[PAIRS + l, h : h + 8, :]
            a = [adj[f * LEV + l, rows, :] for f in range(FIELDS)]
            col_weights = (
                -ew * a[0] - coupling * a[2],
                -ew * a[1],
                -ew * a[2] - coupling * a[0],
                -ew * a[3],
            )
            for f in range(FIELDS):
                n = f * LEV + l
                back = half * (roll(col_weights[f], 1, 1) - roll(col_weights[f], -1, 1))
                back = back + 0.5 * (gy[n, h - 1 : h + 7, :] - gy[n, h + 1 : h + 9, :])
                back = back + mixing * (adj[f * LEV + lo, rows, :] + adj[f * LEV + hi, rows, :] - 2.0 * a[f])
                diag = grid[n, h : h + 8, :] * (tend[n, rows, :] + time_step * back)
                diag_v[f, l, rows, :] = diag[:, :COLS]

    diag_copy = pltpu.make_async_copy(diag_v, diag_out, out_sem.at[1])
    diag_copy.start()

    for send in halo_sends:
        send.wait_send()

    @pl.when(polar)
    def _():
        @pl.loop(1, LANES)
        def _(d):
            j = plus(i, d)
            for q in range(2):
                y_copy(q, j).wait_send()
                z_copy(q, j).wait_send()

        for q in range(2):
            for s in range(2):
                edge_send(q, s).wait_send()

    tan_copy.wait()
    diag_copy.wait()


def hand_out(tan_in, diag_in, tan_out, diag_out, held, in_sem, out_sem):
    ways = [
        (
            pltpu.make_async_copy(src.at[f], held.at[n, f], in_sem.at[n, f]),
            pltpu.make_async_copy(held.at[n, f], dst.at[f], out_sem.at[n, f]),
        )
        for n, (src, dst) in enumerate(((tan_in, tan_out), (diag_in, diag_out)))
        for f in range(FIELDS)
    ]
    for arrive, leave in ways:
        arrive.start()
    for arrive, leave in ways:
        arrive.wait()
        leave.start()
    for arrive, leave in ways:
        leave.wait()


def per_device(bands, row_signs, col_signs, spread, east_wind, north_wind, cutoffs):
    any_spec = pl.BlockSpec(memory_space=pl.ANY)
    out = jax.ShapeDtypeStruct((FIELDS, LEV, ROWS, COLS), F32)
    tables = [jnp.asarray(table) for table in (half_metric(bands),) + mode_factors()]
    vmem = pltpu.VMEM
    dma = pltpu.SemaphoreType.DMA
    results = pl.pallas_call(
        functools.partial(kernel, bands),
        out_shape=(out, out),
        in_specs=[any_spec] * 9,
        out_specs=(any_spec, any_spec),
        scratch_shapes=[
            vmem((FIELDS, LEV, ROWS, COLS), F32),
            vmem((LEV, ROWS, COLS), F32),
            vmem((LEV, ROWS, COLS), F32),
            vmem((FIELDS, LEV, ROWS), jnp.int32),
            vmem((FIELDS, LEV, COLS), jnp.int32),
            pltpu.SMEM((ROWS,), jnp.int32),
            vmem((32, 128), F32),
            vmem((3 * RANK, WIDE), BF16),
            vmem((4, 2 * RANK, 4 * 64), BF16),
            vmem((PAIRS + 2 * LEV, 32, WIDE), F32),
            vmem((2, 10, LEV, WIDE), F32),
            vmem((2, 10, LEV, WIDE), F32),
            vmem((2, 2, FIELDS, LEV, 128), F32),
            vmem((2, ROWS, 128), F32),
            vmem((2, ROWS, 128), F32),
            vmem((2, LANES, LEV, 8, RANK), F32),
            vmem((2, LANES, LEV, 8, RANK), F32),
            vmem((2, LANES, LEV, 8, RANK), F32),
            vmem((2, LANES, LEV, 8, RANK), F32),
            vmem((2, 2, PAIRS, RANK), F32),
            vmem((2, 2, PAIRS, RANK), F32),
            vmem((PAIRS, ROWS, WIDE), F32),
            vmem((PAIRS, ROWS, WIDE), F32),
            vmem((PAIRS, ROWS, WIDE), F32),
            vmem((2, FIELDS, LEV, WIDE), F32),
            vmem((2, 2, PAIRS, WIDE), F32),
            vmem((PAIRS, ROWS, WIDE), F32),
            vmem((PAIRS, 32, WIDE), F32),
            vmem((FIELDS, LEV, ROWS, COLS), F32),
            vmem((FIELDS, LEV, ROWS, COLS), F32),
            dma((9,)),
            dma((2,)),
            dma((2,)),
            dma((2, 2)),
            dma((2, 2)),
            dma((2,)),
            dma((2,)),
            dma((2, LANES)),
            dma((2, LANES)),
            dma((2, LANES)),
            dma((2, LANES)),
            dma((2, 2)),
            dma((2, 2)),
            dma((2,)),
        ],
        compiler_params=pltpu.CompilerParams(
            collective_id=0, has_side_effects=True, vmem_limit_bytes=64 * 2**20
        ),
        cost_estimate=pl.CostEstimate(flops=10**9, bytes_accessed=4 * 10**6, transcendentals=0),
    )(spread, east_wind, north_wind, row_signs, col_signs, cutoffs, *tables)
    return pl.pallas_call(
        hand_out,
        out_shape=(out, out),
        in_specs=[any_spec] * 2,
        out_specs=(any_spec, any_spec),
        scratch_shapes=[vmem((2, FIELDS, LEV, ROWS, COLS), F32), dma((2, FIELDS)), dma((2, FIELDS))],
        compiler_params=pltpu.CompilerParams(vmem_limit_bytes=64 * 2**20),
    )(*results)


def solution(mesh):
    return jax.shard_map(
        functools.partial(per_device, mesh.shape["lat"]),
        mesh=mesh,
        in_specs=(
            P(None, None, "lat"),
            P(None, None, "lon"),
            P(None, None, "lat", "lon"),
            P(None, "lat", "lon"),
            P(None, "lat", "lon"),
            P("lat"),
        ),
        out_specs=(P(None, None, "lat", "lon"), P(None, None, "lat", "lon")),
        check_vma=False,
    )
```

```python
import functools

import jax
import jax.numpy as jnp
import ml_dtypes
import numpy as np
from jax import lax
from jax.experimental import pallas as pl
from jax.experimental.pallas import tpu as pltpu
from jax.sharding import PartitionSpec as P

KTOP = 256
POLAR = 32
RANK = 128
ROWS = 16
COLS = 450
WIDE = 512
LANES = 8
FIELDS = 4
LEV = 4
PAIRS = FIELDS * LEV

time_step = 0.5
coupling = 0.5
mixing = 0.2
metric_cap = 4.0

MESH = pl.DeviceIdType.MESH
F32 = jnp.float32
BF16 = jnp.bfloat16


def split_table(table):
    high = table.astype(ml_dtypes.bfloat16)
    low = (table - high.astype(np.float64)).astype(ml_dtypes.bfloat16)
    return high, low


def waves_of(group, lane_index):
    place = lane_index % 64
    second = place // 32
    other = (8 - group) if group else 4
    residue = group + second * (other - group)
    return 8 * (place % 32) + residue + (8 * (1 - second) if group == 0 else 0)


@functools.lru_cache(None)
def mode_factors():
    total = COLS * LANES
    size = COLS + 2
    place = np.arange(size, dtype=np.float64)
    width = (KTOP + 0.5) / total
    diag = ((size - 1 - 2 * place) / 2) ** 2 * np.cos(2 * np.pi * width)
    side = place[1:] * (size - place[1:]) / 2
    vectors = np.linalg.eigh(np.diag(diag) + np.diag(side, 1) + np.diag(side, -1))[1]
    basis = vectors[:, ::-1][:, :RANK]
    basis = basis * np.where(basis[size // 2] < 0, -1.0, 1.0)
    weights = []
    for group in range(4):
        waves = waves_of(group, np.arange(64))
        angle = 2 * np.pi / total * ((np.arange(size)[:, None] - 1) * waves[None, :] % total)
        alpha, beta = basis.T @ np.cos(angle), basis.T @ np.sin(angle)
        if group:
            sign = np.where(np.arange(64) < 32, 1.0, -1.0)
            top, low = (alpha, beta), (sign * beta, -sign * alpha)
        else:
            use = np.where(np.arange(64) < 32, 1.0, 0.0)
            top, low = (use * alpha, use * beta), ((1 - use) * alpha, (1 - use) * beta)
        weights.append(np.concatenate([np.concatenate(top, axis=1), np.concatenate(low, axis=1)], axis=0))
    weights = np.round(np.stack(weights) * 2.0**22) / 2.0**22
    wide = np.zeros((RANK, WIDE))
    wide[:, : COLS + 1] = basis[1:].T
    wide[:, WIDE - 1] = basis[0]
    wide = np.round(wide * 2.0**26) / 2.0**26
    wide_h, wide_l = split_table(wide)
    own = np.where(np.arange(WIDE)[:, None] < COLS, 1, 0).astype(ml_dtypes.bfloat16)
    high, low = split_table(weights)
    back = [np.swapaxes(part, 1, 2) for part in (high, low, high)]
    return (
        np.concatenate([wide_h.T * own, wide_l.T * own], axis=1),
        np.concatenate([wide_h, wide_l, wide_h], axis=0),
        np.concatenate([high, low], axis=2),
        np.concatenate(back, axis=1),
    )


ROOT = float(np.sqrt(0.5))


def over_lanes(y):
    s = [y[j] + y[j + 4] for j in range(4)]
    d = [y[j] - y[j + 4] for j in range(4)]
    even, odd = s[0] + s[2], s[1] + s[3]
    minus, plus = ROOT * (d[1] - d[3]), ROOT * (d[1] + d[3])
    return [
        (even + odd, even - odd),
        (d[0] + minus, -(d[2] + plus)),
        (s[0] - s[2], s[3] - s[1]),
        (d[0] - minus, d[2] - plus),
    ]


def to_lanes(pairs):
    (y0, y4), (u1, v1), (u2, v2), (u3, v3) = pairs
    even, odd = y0 + y4, y0 - y4
    s = [even + u2, odd - v2, even - u2, odd + v2]
    du, sv = ROOT * (u1 - u3), ROOT * (v1 + v3)
    d = [u1 + u3, du - sv, v3 - v1, -du - sv]
    return [s[j] + d[j] for j in range(4)] + [s[j] - d[j] for j in range(4)]


@functools.lru_cache(None)
def half_metric(bands):
    total = bands * ROWS
    rows = np.clip(np.arange(bands)[:, None] * ROWS - 8 + np.arange(32)[None, :], 0, total - 1)
    metric = np.minimum(1.0 / np.cos(np.pi * ((rows + 0.5) / total - 0.5)), metric_cap)
    return np.broadcast_to((0.5 * metric).astype(np.float32)[:, :, None], (bands, 32, 128)).copy()


def dot_cols(a, b):
    return lax.dot_general(a, b, (((1,), (0,)), ((), ())), preferred_element_type=F32)


def split(x):
    high = x.astype(BF16)
    return high, (x - high.astype(F32)).astype(BF16)


def to_modes(x, table):
    xh, xl = split(x)
    half = table.shape[1] // 2
    wide = dot_cols(xh, table[...])
    return wide[:, :half] + wide[:, half:] + dot_cols(xl, table[:, 0:half])


def from_modes(z, table):
    zh, zl = split(z)
    return dot_cols(jnp.concatenate([zh, zh, zl], axis=1), table[...])


def roll(x, shift, axis):
    return pltpu.roll(x, shift % x.shape[axis], axis)


def roll_blocks(x, shift):
    return roll(x.reshape(x.shape[0] * x.shape[1], x.shape[2]), shift, 1).reshape(x.shape)


def fold(x):
    while x.shape[0] > 1:
        half = x.shape[0] // 2
        x = x[:half] + roll_blocks(x[half:], 2 * half)
    return x


def kernel(
    bands, spread, east, north, rs, cs, cut, metric, qf_in, qe_in, wf_in, wb_in, tan_out, diag_out,
    spread_v, east_v, north_v, rs_v, cs_v, cut_s, hm, qf, qe, wf, wb,
    grid, er, hr, hc, cp, hcol, ybuf, yr, zbuf, zr, eb, bz,
    tend, proj_p, proj_t, edge_t, edge_proj, adj, gy, tan_v, diag_v,
    in_sem, row_send, row_recv, cor_send, cor_recv, col_send, col_recv,
    y_send, y_recv, z_send, z_recv, b_send, b_recv, out_sem,
):
    b = lax.axis_index("lat")
    i = lax.axis_index("lon")
    caps = POLAR // ROWS
    is_north = b == 0
    is_south = b == bands - 1
    polar = jnp.logical_or(b < caps, b >= bands - caps)
    above_polar = jnp.logical_or(b <= caps, is_south)
    below_polar = jnp.logical_or(b >= bands - caps - 1, is_north)
    across = lax.rem(i + LANES // 2, LANES)
    west = lax.rem(i + LANES - 1, LANES)
    east_lane = lax.rem(i + 1, LANES)
    nb = jnp.where(is_north, 0, b - 1)
    nl = jnp.where(is_north, across, i)
    sb = jnp.where(is_south, bands - 1, b + 1)
    sl = jnp.where(is_south, across, i)
    slot_n = jnp.where(is_north, 0, 1)
    slot_s = jnp.where(is_south, 1, 0)

    def plus(lane, d):
        return lax.rem(lane + d, LANES)

    loads = [
        pltpu.make_async_copy(spread, spread_v, in_sem.at[0]),
        pltpu.make_async_copy(rs, rs_v, in_sem.at[1]),
        pltpu.make_async_copy(cs, cs_v, in_sem.at[2]),
        pltpu.make_async_copy(east, east_v, in_sem.at[3]),
        pltpu.make_async_copy(north, north_v, in_sem.at[4]),
        pltpu.make_async_copy(metric.at[b], hm, in_sem.at[5]),
        pltpu.make_async_copy(cut, cut_s, in_sem.at[6]),
        pltpu.make_async_copy(qe_in, qe, in_sem.at[7]),
    ]
    table_loads = [
        pltpu.make_async_copy(qf_in, qf, in_sem.at[8]),
        pltpu.make_async_copy(wf_in, wf, in_sem.at[9]),
        pltpu.make_async_copy(wb_in, wb, in_sem.at[10]),
    ]
    for load in loads:
        load.start()

    @pl.when(polar)
    def _():
        for load in table_loads:
            load.start()

    barrier = pltpu.get_barrier_semaphore()

    def greet(lat, lon):
        pl.semaphore_signal(barrier, inc=1, device_id=(lat, lon), device_id_type=MESH)

    greet(nb, nl)
    greet(sb, sl)
    greet(b, west)
    greet(b, east_lane)
    greet(nb, plus(nl, 1))
    greet(nb, plus(nl, LANES - 1))
    greet(sb, plus(sl, 1))
    greet(sb, plus(sl, LANES - 1))

    @pl.when(polar)
    def _():
        @pl.loop(1, LANES)
        def _(d):
            greet(b, plus(i, d))

    @pl.when(jnp.logical_and(above_polar, jnp.logical_not(is_north)))
    def _():
        for f in range(FIELDS):
            greet(nb, 2 * f + 1)

    @pl.when(jnp.logical_and(below_polar, jnp.logical_not(is_south)))
    def _():
        for f in range(FIELDS):
            greet(sb, 2 * f)

    for load in loads[:5]:
        load.wait()
    grid[:, 8:24, 384:512] = jnp.zeros((PAIRS + 2 * LEV, ROWS, 128), F32)
    row_part = jnp.concatenate([rs_v[f] for f in range(FIELDS)], axis=0)
    row_part = (2 * row_part - 1).astype(F32).T
    for f in range(FIELDS):
        col_part = (2 * cs_v[f] - 1).astype(F32)
        for l in range(LEV):
            n = f * LEV + l
            grid[n, 8:24, 0:COLS] = spread_v[f, l] * (row_part[:, n : n + 1] * col_part[l : l + 1, :])
    for l in range(LEV):
        grid[PAIRS + l, 8:24, 0:COLS] = east_v[l]
        grid[PAIRS + LEV + l, 8:24, 0:COLS] = north_v[l]

    for s, (near, far) in enumerate(((8, 9), (23, 22))):
        for f in range(FIELDS + 2):
            er[s, f if f < FIELDS else f + FIELDS] = grid[f * LEV : (f + 1) * LEV, near, :]
        for f in range(FIELDS):
            er[s, FIELDS + f] = grid[f * LEV : (f + 1) * LEV, far, :]
    lane128 = lax.broadcasted_iota(jnp.int32, (1, 1, 128), 2)
    for s, (start, shift) in enumerate(((0, 0), (384, COLS - 2 - 384))):
        tile = grid[:, 8:24, start : start + 128]
        tile = jnp.where(jnp.logical_and(lane128 >= shift, lane128 < shift + 2), tile, 0.0)
        packed = fold(tile[:PAIRS]) + roll_blocks(fold(tile[PAIRS:]), 2 * PAIRS)
        cp[s] = roll_blocks(packed, -shift)[0]

    own_half = lax.rem(i, 2)
    edge_over = jnp.where(own_half == 0, is_north, is_south)
    pl.semaphore_wait(
        barrier,
        8
        + jnp.where(polar, LANES - 1, 0)
        + jnp.where(jnp.logical_and(polar, jnp.logical_not(edge_over)), LANES, 0),
    )

    def remote(src, dst, send, recv, lat, lon):
        return pltpu.make_async_remote_copy(
            src_ref=src, dst_ref=dst, send_sem=send, recv_sem=recv, device_id=(lat, lon), device_id_type=MESH
        )

    halo_sends = [
        remote(
            er.at[0, 0:FIELDS], hr.at[slot_n, 0:FIELDS], row_send.at[0, 0], row_recv.at[slot_n, 0], nb, nl
        ),
        remote(
            er.at[1, 0:FIELDS], hr.at[slot_s, 0:FIELDS], row_send.at[1, 0], row_recv.at[slot_s, 0], sb, sl
        ),
        remote(cp.at[0], hcol.at[1], col_send.at[0], col_recv.at[1], b, west),
        remote(cp.at[1], hcol.at[0], col_send.at[1], col_recv.at[0], b, east_lane),
    ]
    for s, (slot, lat, lon) in enumerate(((slot_n, nb, nl), (slot_s, sb, sl))):
        halo_sends.append(
            remote(
                er.at[s, 0:FIELDS, :, 384:512], hc.at[slot, 0], cor_send.at[s, 0], cor_recv.at[slot, 0],
                lat, plus(lon, 1),
            )
        )
        halo_sends.append(
            remote(
                er.at[s, 0:FIELDS, :, 0:128], hc.at[slot, 1], cor_send.at[s, 1], cor_recv.at[slot, 1],
                lat, plus(lon, LANES - 1),
            )
        )
    halo_sends += [
        remote(er.at[0, FIELDS:10], hr.at[slot_n, FIELDS:10], row_send.at[0, 1], row_recv.at[slot_n, 1], nb, nl),
        remote(er.at[1, FIELDS:10], hr.at[slot_s, FIELDS:10], row_send.at[1, 1], row_recv.at[slot_s, 1], sb, sl),
    ]
    for send in halo_sends:
        send.start()

    def y_copy(q, o):
        return remote(ybuf.at[q, o], yr.at[q, i], y_send.at[q, o], y_recv.at[q, i], b, o)

    def y_arrival(q, j):
        return remote(ybuf.at[q, j], yr.at[q, j], y_send.at[q, j], y_recv.at[q, j], b, j)

    def send_probe_values():
        y = to_modes(grid[0:PAIRS, 8:24, :].reshape(PAIRS * ROWS, WIDE), qf).reshape(FIELDS, LEV, 2, 8, RANK)
        for f in range(FIELDS):
            for h in range(2):
                for l in range(LEV):
                    ybuf[0, 2 * f + h, l] = y[f, l, h]

        @pl.loop(1, LANES)
        def _(d):
            y_copy(0, plus(i, d)).start()

        yr[0, i] = ybuf[0, i]

    def send_tendency_values(h):
        y = to_modes(tend[:, 8 * h : 8 * h + 8, :].reshape(PAIRS * 8, WIDE), qf).reshape(FIELDS, LEV, 8, RANK)
        for f in range(FIELDS):
            ybuf[1, 2 * f + h] = y[f]

        @pl.loop(0, FIELDS)
        def _(d):
            o = 2 * lax.rem(i // 2 + d, FIELDS) + h

            @pl.when(o != i)
            def _():
                y_copy(1, o).start()

            @pl.when(o == i)
            def _():
                yr[1, i] = ybuf[1, i]

    def z_copy(q, j):
        return remote(zbuf.at[q, j], zr.at[q, i], z_send.at[q, j], z_recv.at[q, i], b, j)

    def z_arrival(q, j):
        return remote(zbuf.at[q, j], zr.at[q, j], z_send.at[q, j], z_recv.at[q, j], b, j)

    def own_rows(q):
        row = lax.broadcasted_iota(jnp.int32, (8, 128), 0)
        cutoff = jnp.zeros((8, 128), jnp.int32)
        for r in range(8):
            cutoff = jnp.where(row == r, cut_s[8 * own_half + r], cutoff)

        @pl.loop(1, LANES)
        def _(d):
            y_arrival(q, plus(i, d)).wait_recv()

        pairs = []
        over = over_lanes([yr[q, j].reshape(LEV * 8, RANK) for j in range(LANES)])
        for group, pair in enumerate(over):
            coef = to_modes(jnp.concatenate(pair, axis=1), wf.at[group])
            wave = waves_of(group, lax.broadcasted_iota(jnp.int32, (8, 128), 1))
            keep = jnp.where(wave > cutoff, 2.0 / (COLS * LANES), 0.0)
            back = from_modes(coef * jnp.concatenate([keep] * LEV, axis=0), wb.at[group])
            pairs.append((back[:, :RANK], back[:, RANK:]))
        for j, z in enumerate(to_lanes(pairs)):
            z = z.reshape(LEV, 8, RANK)
            zbuf[q, j] = z
            eb[j, LEV * q : LEV * (q + 1), :] = jnp.where(own_half == 0, z[:, 0, :], z[:, 7, :])

        @pl.loop(1, LANES)
        def _(d):
            z_copy(q, plus(i, d)).start()

        zr[q, i] = zbuf[q, i]

    def edge_sends(act):
        slot = jnp.where(own_half == 0, slot_n, slot_s)
        lat = jnp.where(own_half == 0, nb, sb)

        @pl.loop(0, LANES)
        def _(d):
            j = plus(i, d)
            lon = jnp.where(edge_over, plus(j, LANES // 2), j)
            here = jnp.logical_and(edge_over, lon == i)

            @pl.when(jnp.logical_not(here))
            def _():
                act(
                    remote(
                        eb.at[j], bz.at[slot, i // 2], b_send.at[j], b_recv.at[slot, i // 2], lat, lon
                    )
                )

            if act is start_copy:
                @pl.when(here)
                def _():
                    pltpu.make_async_copy(eb.at[j], bz.at[slot, i // 2], b_recv.at[slot, i // 2]).start()

    def start_copy(copy):
        copy.start()

    def end_copy(copy):
        copy.wait_send()

    def project(q, out):
        @pl.loop(1, LANES)
        def _(d):
            z_arrival(q, plus(i, d)).wait_recv()

        z = jnp.concatenate(
            [zr[q, 2 * f + h, l] for f in range(FIELDS) for l in range(LEV) for h in range(2)], axis=0
        )
        out[...] = from_modes(z, qe).reshape(PAIRS, ROWS, WIDE)

    for load in loads[5:]:
        load.wait()

    @pl.when(polar)
    def _():
        for load in table_loads:
            load.wait()
        send_probe_values()

    for s in range(2):
        remote(
            er.at[s, 0:FIELDS], hr.at[s, 0:FIELDS], row_send.at[s, 0], row_recv.at[s, 0], nb, nl
        ).wait_recv()
        remote(cp.at[s], hcol.at[s], col_send.at[s], col_recv.at[s], b, west).wait_recv()
        for side in range(2):
            remote(
                er.at[s, 0:FIELDS, :, 0:128], hc.at[s, side], cor_send.at[s, side], cor_recv.at[s, side], nb, nl
            ).wait_recv()

    from_west = roll(hcol[0], 126, 1)
    from_east = roll(hcol[1], COLS - 384, 1)
    lane2 = lax.broadcasted_iota(jnp.int32, (1, 128), 1)
    both = jnp.where(jnp.logical_and(lane2 >= 66, lane2 < 114), from_east, from_west)[None]
    for width in (2, 4, 8):
        both = jnp.concatenate([both, roll_blocks(both, -width)], axis=0)
    both = jnp.concatenate([both, roll_blocks(both, -16), roll_blocks(both, -32)], axis=0)
    in_halo = jnp.logical_or(
        jnp.logical_and(lane128 >= 66, lane128 < 68), lane128 >= 126
    )
    grid[:, 8:24, 384:512] = jnp.where(in_halo, both, grid[:, 8:24, 384:512])

    flips = (-1.0, -1.0, 1.0, 1.0)
    over_pole = (is_north, is_south)
    edge_row = (7, 24)
    inward = (1.0, -1.0)

    def edge_center(s, f):
        tile = hr[s, f][:, 384:512]
        tile = jnp.where(lane2 == 66, roll(hc[s, 1, f], 66, 1), tile)
        tile = jnp.where(lane2 == 127, roll(hc[s, 0, f], 62, 1), tile)
        return jnp.concatenate([hr[s, f][:, 0:384], tile], axis=1)

    edge_probe = [[edge_center(s, f) for f in range(FIELDS)] for s in range(2)]
    for s in range(2):
        for f in range(FIELDS):
            flip = jnp.where(over_pole[s], flips[f], 1.0)
            grid[f * LEV : (f + 1) * LEV, edge_row[s], :] = flip * edge_probe[s][f]

    def tendency_rows(h):
        @pl.loop(0, LEV)
        def _(l):
            lo = jnp.maximum(l - 1, 0)
            hi = jnp.minimum(l + 1, LEV - 1)
            half = jnp.concatenate([hm[h : h + 8, :]] * 4, axis=1)
            ew = grid[PAIRS + l, h : h + 8, :]
            nw = grid[PAIRS + LEV + l, h : h + 8, :]
            along_x, along_y = [], []
            for f in range(FIELDS):
                mid = grid[f * LEV + l, h : h + 8, :]
                along_x.append(half * (roll(mid, -1, 1) - roll(mid, 1, 1)))
                along_y.append(0.5 * (grid[f * LEV + l, h + 1 : h + 9, :] - grid[f * LEV + l, h - 1 : h + 7, :]))
            linked = (along_x[2], along_y[2], along_x[0] + along_y[1], None)
            for f in range(FIELDS):
                mid = grid[f * LEV + l, h : h + 8, :]
                mixed = grid[f * LEV + lo, h : h + 8, :] + grid[f * LEV + hi, h : h + 8, :] - 2.0 * mid
                t = -(ew * along_x[f] + nw * along_y[f]) + mixing * mixed
                if linked[f] is not None:
                    t = t - coupling * linked[f]
                tend[f * LEV + l, h - 8 : h, :] = t

    for part in range(2):
        tendency_rows(8 + 8 * part)

        @pl.when(polar)
        def _():
            send_tendency_values(part)

    @pl.when(polar)
    def _():
        own_rows(0)

    for s in range(2):
        remote(
            er.at[s, FIELDS:10], hr.at[s, FIELDS:10], row_send.at[s, 1], row_recv.at[s, 1], nb, nl
        ).wait_recv()
        centers = edge_probe[s]
        half = jnp.concatenate([hm[edge_row[s] : edge_row[s] + 1, :]] * 4, axis=1)
        turn = jnp.where(over_pole[s], -inward[s], inward[s])
        along_x, along_y = [], []
        for f in range(FIELDS):
            flip = jnp.where(over_pole[s], flips[f], 1.0)
            along_x.append(half * (roll(centers[f], -1, 1) - roll(centers[f], 1, 1)))
            along_y.append((0.5 * turn) * (flip * er[s, f] - hr[s, FIELDS + f]))
        linked = (along_x[2], along_y[2], along_x[0] + along_y[1], None)
        for f in range(FIELDS):
            mid = centers[f]
            up = jnp.concatenate([mid[0:1], mid[0:3]], axis=0)
            down = jnp.concatenate([mid[1:4], mid[3:4]], axis=0)
            t = -(hr[s, 8] * along_x[f] + hr[s, 9] * along_y[f]) + mixing * (up + down - 2.0 * mid)
            if linked[f] is not None:
                t = t - coupling * linked[f]
            edge_t[s, f] = t

    @pl.when(polar)
    def _():
        own_rows(1)
        edge_sends(start_copy)
        project(0, proj_p)
        project(1, proj_t)

    @pl.when(jnp.logical_not(polar))
    def _():
        proj_p[...] = jnp.zeros(proj_p.shape, F32)
        proj_t[...] = jnp.zeros(proj_t.shape, F32)

    def row_weights(a, nw):
        return (
            -nw * a[0],
            -nw * a[1] - coupling * a[2],
            -nw * a[2] - coupling * a[1],
            -nw * a[3],
        )

    @pl.loop(0, LEV)
    def _(l):
        for h in (8, 16):
            nw = grid[PAIRS + LEV + l, h : h + 8, :]
            a = []
            for f in range(FIELDS):
                n = f * LEV + l
                change = time_step * (tend[n, h - 8 : h, :] - proj_t[n, h - 8 : h, :])
                tend[n, h - 8 : h, :] = change
                tangent = grid[n, h : h + 8, :] + change
                tan_v[f, l, h - 8 : h, :] = tangent[:, :COLS]
                a.append(tangent - proj_p[n, h - 8 : h, :])
                adj[n, h - 8 : h, :] = a[f]
            for f, weight in enumerate(row_weights(a, nw)):
                gy[f * LEV + l, h : h + 8, :] = weight

    tan_copy = pltpu.make_async_copy(tan_v, tan_out, out_sem.at[0])
    tan_copy.start()

    for s, wanted in enumerate((above_polar, below_polar)):
        @pl.when(wanted)
        def _():
            for f in range(FIELDS):
                remote(eb.at[f], bz.at[s, f], b_send.at[f], b_recv.at[s, f], nb, nl).wait_recv()
            edge_proj[s] = from_modes(bz[s].reshape(2 * PAIRS, RANK), qe).reshape(FIELDS, 2 * LEV, WIDE)

        @pl.when(jnp.logical_not(wanted))
        def _():
            edge_proj[s] = jnp.zeros((FIELDS, 2 * LEV, WIDE), F32)

    for s in range(2):
        a = []
        for f in range(FIELDS):
            a.append(
                edge_probe[s][f]
                + time_step * (edge_t[s, f] - edge_proj[s, f, LEV : 2 * LEV, :])
                - edge_proj[s, f, 0:LEV, :]
            )
        for f, weight in enumerate(row_weights(a, hr[s, 9])):
            flip = jnp.where(over_pole[s], -flips[f], 1.0)
            gy[f * LEV : (f + 1) * LEV, edge_row[s], :] = flip * weight

    @pl.loop(0, LEV)
    def _(l):
        lo = jnp.maximum(l - 1, 0)
        hi = jnp.minimum(l + 1, LEV - 1)
        for h in (8, 16):
            rows = slice(h - 8, h)
            half = jnp.concatenate([hm[h : h + 8, :]] * 4, axis=1)
            ew = grid[PAIRS + l, h : h + 8, :]
            a = [adj[f * LEV + l, rows, :] for f in range(FIELDS)]
            col_weights = (
                -ew * a[0] - coupling * a[2],
                -ew * a[1],
                -ew * a[2] - coupling * a[0],
                -ew * a[3],
            )
            for f in range(FIELDS):
                n = f * LEV + l
                back = half * (roll(col_weights[f], 1, 1) - roll(col_weights[f], -1, 1))
                back = back + 0.5 * (gy[n, h - 1 : h + 7, :] - gy[n, h + 1 : h + 9, :])
                back = back + mixing * (adj[f * LEV + lo, rows, :] + adj[f * LEV + hi, rows, :] - 2.0 * a[f])
                diag = grid[n, h : h + 8, :] * (tend[n, rows, :] + time_step * back)
                diag_v[f, l, rows, :] = diag[:, :COLS]

    diag_copy = pltpu.make_async_copy(diag_v, diag_out, out_sem.at[1])
    diag_copy.start()

    for send in halo_sends:
        send.wait_send()

    @pl.when(polar)
    def _():
        @pl.loop(1, LANES)
        def _(d):
            j = plus(i, d)
            for q in range(2):
                y_copy(q, j).wait_send()
                z_copy(q, j).wait_send()

        edge_sends(end_copy)

    tan_copy.wait()
    diag_copy.wait()


def hand_out(tan_in, diag_in, tan_out, diag_out, held, in_sem, out_sem):
    ways = [
        (
            pltpu.make_async_copy(src.at[f], held.at[n, f], in_sem.at[n, f]),
            pltpu.make_async_copy(held.at[n, f], dst.at[f], out_sem.at[n, f]),
        )
        for n, (src, dst) in enumerate(((tan_in, tan_out), (diag_in, diag_out)))
        for f in range(FIELDS)
    ]
    for arrive, leave in ways:
        arrive.start()
    for arrive, leave in ways:
        arrive.wait()
        leave.start()
    for arrive, leave in ways:
        leave.wait()


def per_device(bands, row_signs, col_signs, spread, east_wind, north_wind, cutoffs):
    any_spec = pl.BlockSpec(memory_space=pl.ANY)
    out = jax.ShapeDtypeStruct((FIELDS, LEV, ROWS, COLS), F32)
    tables = [jnp.asarray(table) for table in (half_metric(bands),) + mode_factors()]
    vmem = pltpu.VMEM
    dma = pltpu.SemaphoreType.DMA
    results = pl.pallas_call(
        functools.partial(kernel, bands),
        out_shape=(out, out),
        in_specs=[any_spec] * 11,
        out_specs=(any_spec, any_spec),
        scratch_shapes=[
            vmem((FIELDS, LEV, ROWS, COLS), F32),
            vmem((LEV, ROWS, COLS), F32),
            vmem((LEV, ROWS, COLS), F32),
            vmem((FIELDS, LEV, ROWS), jnp.int32),
            vmem((FIELDS, LEV, COLS), jnp.int32),
            pltpu.SMEM((ROWS,), jnp.int32),
            vmem((32, 128), F32),
            vmem((WIDE, 2 * RANK), BF16),
            vmem((3 * RANK, WIDE), BF16),
            vmem((4, 2 * RANK, 4 * 64), BF16),
            vmem((4, 6 * 64, 2 * RANK), BF16),
            vmem((PAIRS + 2 * LEV, 32, WIDE), F32),
            vmem((2, 10, LEV, WIDE), F32),
            vmem((2, 10, LEV, WIDE), F32),
            vmem((2, 2, FIELDS, LEV, 128), F32),
            vmem((2, ROWS, 128), F32),
            vmem((2, ROWS, 128), F32),
            vmem((2, LANES, LEV, 8, RANK), F32),
            vmem((2, LANES, LEV, 8, RANK), F32),
            vmem((2, LANES, LEV, 8, RANK), F32),
            vmem((2, LANES, LEV, 8, RANK), F32),
            vmem((LANES, 2 * LEV, RANK), F32),
            vmem((2, FIELDS, 2 * LEV, RANK), F32),
            vmem((PAIRS, ROWS, WIDE), F32),
            vmem((PAIRS, ROWS, WIDE), F32),
            vmem((PAIRS, ROWS, WIDE), F32),
            vmem((2, FIELDS, LEV, WIDE), F32),
            vmem((2, FIELDS, 2 * LEV, WIDE), F32),
            vmem((PAIRS, ROWS, WIDE), F32),
            vmem((PAIRS, 32, WIDE), F32),
            vmem((FIELDS, LEV, ROWS, COLS), F32),
            vmem((FIELDS, LEV, ROWS, COLS), F32),
            dma((11,)),
            dma((2, 2)),
            dma((2, 2)),
            dma((2, 2)),
            dma((2, 2)),
            dma((2,)),
            dma((2,)),
            dma((2, LANES)),
            dma((2, LANES)),
            dma((2, LANES)),
            dma((2, LANES)),
            dma((LANES,)),
            dma((2, FIELDS)),
            dma((2,)),
        ],
        compiler_params=pltpu.CompilerParams(
            collective_id=0, has_side_effects=True, vmem_limit_bytes=64 * 2**20
        ),
        cost_estimate=pl.CostEstimate(flops=10**9, bytes_accessed=4 * 10**6, transcendentals=0),
    )(spread, east_wind, north_wind, row_signs, col_signs, cutoffs, *tables)
    return pl.pallas_call(
        hand_out,
        out_shape=(out, out),
        in_specs=[any_spec] * 2,
        out_specs=(any_spec, any_spec),
        scratch_shapes=[vmem((2, FIELDS, LEV, ROWS, COLS), F32), dma((2, FIELDS)), dma((2, FIELDS))],
        compiler_params=pltpu.CompilerParams(vmem_limit_bytes=64 * 2**20),
    )(*results)


def solution(mesh):
    return jax.shard_map(
        functools.partial(per_device, mesh.shape["lat"]),
        mesh=mesh,
        in_specs=(
            P(None, None, "lat"),
            P(None, None, "lon"),
            P(None, None, "lat", "lon"),
            P(None, "lat", "lon"),
            P(None, "lat", "lon"),
            P("lat"),
        ),
        out_specs=(P(None, None, "lat", "lon"), P(None, None, "lat", "lon")),
        check_vma=False,
    )
```

```python
import functools

import jax
import jax.numpy as jnp
import ml_dtypes
import numpy as np
from jax import lax
from jax.experimental import pallas as pl
from jax.experimental.pallas import tpu as pltpu
from jax.sharding import PartitionSpec as P

KTOP = 256
POLAR = 32
RANK = 128
ROWS = 16
COLS = 450
WIDE = 512
LANES = 8
FIELDS = 4
LEV = 4
PAIRS = FIELDS * LEV

time_step = 0.5
coupling = 0.5
mixing = 0.2
metric_cap = 4.0

MESH = pl.DeviceIdType.MESH
F32 = jnp.float32
BF16 = jnp.bfloat16


def split_table(table):
    high = table.astype(ml_dtypes.bfloat16)
    low = (table - high.astype(np.float64)).astype(ml_dtypes.bfloat16)
    return high, low


def waves_of(group, lane_index):
    place = lane_index % 64
    second = place // 32
    other = (8 - group) if group else 4
    residue = group + second * (other - group)
    return 8 * (place % 32) + residue + (8 * (1 - second) if group == 0 else 0)


@functools.lru_cache(None)
def mode_factors():
    total = COLS * LANES
    size = COLS + 2
    place = np.arange(size, dtype=np.float64)
    width = (KTOP + 0.5) / total
    diag = ((size - 1 - 2 * place) / 2) ** 2 * np.cos(2 * np.pi * width)
    side = place[1:] * (size - place[1:]) / 2
    vectors = np.linalg.eigh(np.diag(diag) + np.diag(side, 1) + np.diag(side, -1))[1]
    basis = vectors[:, ::-1][:, :RANK]
    basis = basis * np.where(basis[size // 2] < 0, -1.0, 1.0)
    weights = []
    for group in range(4):
        waves = waves_of(group, np.arange(64))
        angle = 2 * np.pi / total * ((np.arange(size)[:, None] - 1) * waves[None, :] % total)
        alpha, beta = basis.T @ np.cos(angle), basis.T @ np.sin(angle)
        if group:
            sign = np.where(np.arange(64) < 32, 1.0, -1.0)
            top, low = (alpha, beta), (sign * beta, -sign * alpha)
        else:
            use = np.where(np.arange(64) < 32, 1.0, 0.0)
            top, low = (use * alpha, use * beta), ((1 - use) * alpha, (1 - use) * beta)
        weights.append(np.concatenate([np.concatenate(top, axis=1), np.concatenate(low, axis=1)], axis=0))
    weights = np.round(np.stack(weights) * 2.0**22) / 2.0**22
    wide = np.zeros((RANK, WIDE))
    wide[:, : COLS + 1] = basis[1:].T
    wide[:, WIDE - 1] = basis[0]
    wide = np.round(wide * 2.0**26) / 2.0**26
    wide_h, wide_l = split_table(wide)
    own = np.where(np.arange(WIDE)[:, None] < COLS, 1, 0).astype(ml_dtypes.bfloat16)
    high, low = split_table(weights)
    back = [np.swapaxes(part, 1, 2) for part in (high, low, high)]
    return (
        np.concatenate([wide_h.T * own, wide_l.T * own], axis=1),
        np.concatenate([wide_h, wide_l, wide_h], axis=0),
        np.concatenate([high, low], axis=2),
        np.concatenate(back, axis=1),
    )


ROOT = float(np.sqrt(0.5))


def over_lanes(y):
    s = [y[j] + y[j + 4] for j in range(4)]
    d = [y[j] - y[j + 4] for j in range(4)]
    even, odd = s[0] + s[2], s[1] + s[3]
    minus, plus = ROOT * (d[1] - d[3]), ROOT * (d[1] + d[3])
    return [
        (even + odd, even - odd),
        (d[0] + minus, -(d[2] + plus)),
        (s[0] - s[2], s[3] - s[1]),
        (d[0] - minus, d[2] - plus),
    ]


def to_lanes(pairs):
    (y0, y4), (u1, v1), (u2, v2), (u3, v3) = pairs
    even, odd = y0 + y4, y0 - y4
    s = [even + u2, odd - v2, even - u2, odd + v2]
    du, sv = ROOT * (u1 - u3), ROOT * (v1 + v3)
    d = [u1 + u3, du - sv, v3 - v1, -du - sv]
    return [s[j] + d[j] for j in range(4)] + [s[j] - d[j] for j in range(4)]


@functools.lru_cache(None)
def half_metric(bands):
    total = bands * ROWS
    rows = np.clip(np.arange(bands)[:, None] * ROWS - 8 + np.arange(32)[None, :], 0, total - 1)
    metric = np.minimum(1.0 / np.cos(np.pi * ((rows + 0.5) / total - 0.5)), metric_cap)
    table = np.broadcast_to((0.5 * metric).astype(np.float32)[:, :, None], (bands, 32, 128)).copy()
    forward = mode_factors()[0].astype(np.float32)
    for row, col in enumerate((0, COLS - 1)):
        table[:, row] = forward[col, :RANK] + forward[col, RANK:]
    return table


def dot_cols(a, b):
    return lax.dot_general(a, b, (((1,), (0,)), ((), ())), preferred_element_type=F32)


def split(x):
    high = x.astype(BF16)
    return high, (x - high.astype(F32)).astype(BF16)


def to_modes(x, table):
    xh, xl = split(x)
    half = table.shape[1] // 2
    wide = dot_cols(xh, table[...])
    return wide[:, :half] + wide[:, half:] + dot_cols(xl, table[:, 0:half])


def from_modes(z, table):
    zh, zl = split(z)
    return dot_cols(jnp.concatenate([zh, zh, zl], axis=1), table[...])


def roll(x, shift, axis):
    return pltpu.roll(x, shift % x.shape[axis], axis)


def roll_blocks(x, shift):
    return roll(x.reshape(x.shape[0] * x.shape[1], x.shape[2]), shift, 1).reshape(x.shape)


def fold(x):
    while x.shape[0] > 1:
        half = x.shape[0] // 2
        x = x[:half] + roll_blocks(x[half:], 2 * half)
    return x


def kernel(
    bands, spread, east, north, rs, cs, cut, metric, qf_in, qe_in, wf_in, wb_in, tan_out, diag_out,
    spread_v, east_v, north_v, rs_v, cs_v, cut_s, hm, qf, qe, wf, wb,
    grid, er, hr, hc, cp, hcol, ybuf, yr, zbuf, zr, xb, cb, yc, eb, bz,
    tend, proj_p, proj_t, edge_t, edge_proj, adj, gy, tan_v, diag_v,
    in_sem, row_send, row_recv, cor_send, cor_recv, col_send, col_recv,
    y_send, y_recv, c_send, c_recv, z_send, z_recv, b_send, b_recv, out_sem,
):
    b = lax.axis_index("lat")
    i = lax.axis_index("lon")
    caps = POLAR // ROWS
    is_north = b == 0
    is_south = b == bands - 1
    polar = jnp.logical_or(b < caps, b >= bands - caps)
    above_polar = jnp.logical_or(b <= caps, is_south)
    below_polar = jnp.logical_or(b >= bands - caps - 1, is_north)
    across = lax.rem(i + LANES // 2, LANES)
    west = lax.rem(i + LANES - 1, LANES)
    east_lane = lax.rem(i + 1, LANES)
    nb = jnp.where(is_north, 0, b - 1)
    nl = jnp.where(is_north, across, i)
    sb = jnp.where(is_south, bands - 1, b + 1)
    sl = jnp.where(is_south, across, i)
    slot_n = jnp.where(is_north, 0, 1)
    slot_s = jnp.where(is_south, 1, 0)

    def plus(lane, d):
        return lax.rem(lane + d, LANES)

    loads = [
        pltpu.make_async_copy(spread, spread_v, in_sem.at[0]),
        pltpu.make_async_copy(rs, rs_v, in_sem.at[1]),
        pltpu.make_async_copy(cs, cs_v, in_sem.at[2]),
        pltpu.make_async_copy(east, east_v, in_sem.at[3]),
        pltpu.make_async_copy(north, north_v, in_sem.at[4]),
        pltpu.make_async_copy(metric.at[b], hm, in_sem.at[5]),
        pltpu.make_async_copy(cut, cut_s, in_sem.at[6]),
        pltpu.make_async_copy(qe_in, qe, in_sem.at[7]),
    ]
    table_loads = [
        pltpu.make_async_copy(qf_in, qf, in_sem.at[8]),
        pltpu.make_async_copy(wf_in, wf, in_sem.at[9]),
        pltpu.make_async_copy(wb_in, wb, in_sem.at[10]),
    ]
    for load in loads:
        load.start()

    @pl.when(polar)
    def _():
        for load in table_loads:
            load.start()

    def values(q, x):
        y = to_modes(x.reshape(PAIRS * ROWS, WIDE), qf).reshape(FIELDS, LEV, 2, 8, RANK)
        for f in range(FIELDS):
            for h in range(2):
                for l in range(LEV):
                    ybuf[q, 2 * f + h, l] = y[f, l, h]

    def probe_values():
        values(0, grid[0:PAIRS, 8:24, :])

    barrier = pltpu.get_barrier_semaphore()

    def greet(lat, lon):
        pl.semaphore_signal(barrier, inc=1, device_id=(lat, lon), device_id_type=MESH)

    greet(nb, nl)
    greet(sb, sl)
    greet(b, west)
    greet(b, east_lane)

    @pl.when(polar)
    def _():
        @pl.loop(2, LANES - 1)
        def _(d):
            greet(b, plus(i, d))

    for load in loads[:5]:
        load.wait()
    grid[:, 8:24, 384:512] = jnp.zeros((PAIRS + 2 * LEV, ROWS, 128), F32)
    row_part = jnp.concatenate([rs_v[f] for f in range(FIELDS)], axis=0)
    row_part = (2 * row_part - 1).astype(F32).T
    for f in range(FIELDS):
        col_part = (2 * cs_v[f] - 1).astype(F32)
        for l in range(LEV):
            n = f * LEV + l
            grid[n, 8:24, 0:COLS] = spread_v[f, l] * (row_part[:, n : n + 1] * col_part[l : l + 1, :])
    for l in range(LEV):
        grid[PAIRS + l, 8:24, 0:COLS] = east_v[l]
        grid[PAIRS + LEV + l, 8:24, 0:COLS] = north_v[l]

    for s, (near, far) in enumerate(((8, 9), (23, 22))):
        for f in range(FIELDS + 2):
            er[s, f if f < FIELDS else f + FIELDS] = grid[f * LEV : (f + 1) * LEV, near, :]
        for f in range(FIELDS):
            er[s, FIELDS + f] = grid[f * LEV : (f + 1) * LEV, far, :]
    lane128 = lax.broadcasted_iota(jnp.int32, (1, 1, 128), 2)
    for s, (start, shift) in enumerate(((0, 0), (384, COLS - 2 - 384))):
        tile = grid[:, 8:24, start : start + 128]
        tile = jnp.where(jnp.logical_and(lane128 >= shift, lane128 < shift + 2), tile, 0.0)
        packed = fold(tile[:PAIRS]) + roll_blocks(fold(tile[PAIRS:]), 2 * PAIRS)
        cp[s] = roll_blocks(packed, -shift)[0]

    own_half = lax.rem(i, 2)
    edge_over = jnp.where(own_half == 0, is_north, is_south)

    @pl.when(polar)
    def _():
        for load in table_loads:
            load.wait()
        probe_values()

    pl.semaphore_wait(barrier, 4 + jnp.where(polar, LANES - 3, 0))

    def remote(src, dst, send, recv, lat, lon):
        return pltpu.make_async_remote_copy(
            src_ref=src, dst_ref=dst, send_sem=send, recv_sem=recv, device_id=(lat, lon), device_id_type=MESH
        )

    halo_sends = [
        remote(
            er.at[0, 0:FIELDS], hr.at[slot_n, 0:FIELDS], row_send.at[0, 0], row_recv.at[slot_n, 0], nb, nl
        ),
        remote(
            er.at[1, 0:FIELDS], hr.at[slot_s, 0:FIELDS], row_send.at[1, 0], row_recv.at[slot_s, 0], sb, sl
        ),
        remote(cp.at[0], hcol.at[1], col_send.at[0], col_recv.at[1], b, west),
        remote(cp.at[1], hcol.at[0], col_send.at[1], col_recv.at[0], b, east_lane),
    ]
    halo_sends += [
        remote(er.at[0, FIELDS:10], hr.at[slot_n, FIELDS:10], row_send.at[0, 1], row_recv.at[slot_n, 1], nb, nl),
        remote(er.at[1, FIELDS:10], hr.at[slot_s, FIELDS:10], row_send.at[1, 1], row_recv.at[slot_s, 1], sb, sl),
    ]
    for send in halo_sends:
        send.start()

    corner_sends = [
        remote(
            hr.at[s, 0:FIELDS, :, start : start + 128], hc.at[s, side], cor_send.at[s, side], cor_recv.at[s, side],
            b, lon,
        )
        for s in range(2)
        for side, start, lon in ((0, 384, east_lane), (1, 0, west))
    ]

    def y_copy(q, o):
        return remote(ybuf.at[q, o], yr.at[q, i], y_send.at[q, o], y_recv.at[q, i], b, o)

    def y_arrival(q, j):
        return remote(ybuf.at[q, j], yr.at[q, j], y_send.at[q, j], y_recv.at[q, j], b, j)

    def send_values(q):
        @pl.loop(1, LANES)
        def _(d):
            y_copy(q, plus(i, d)).start()

        yr[q, i] = ybuf[q, i]

    def c_copy(o):
        return remote(cb.at[o], yc.at[i], c_send.at[o], c_recv.at[i], b, o)

    def c_arrival(j):
        return remote(cb.at[j], yc.at[j], c_send.at[j], c_recv.at[j], b, j)

    def z_copy(q, j):
        return remote(zbuf.at[q, j], zr.at[q, i], z_send.at[q, j], z_recv.at[q, i], b, j)

    def z_arrival(q, j):
        return remote(zbuf.at[q, j], zr.at[q, j], z_send.at[q, j], z_recv.at[q, j], b, j)

    def own_rows(q):
        row = lax.broadcasted_iota(jnp.int32, (8, 128), 0)
        cutoff = jnp.zeros((8, 128), jnp.int32)
        for r in range(8):
            cutoff = jnp.where(row == r, cut_s[8 * own_half + r], cutoff)

        @pl.loop(1, LANES)
        def _(d):
            y_arrival(q, plus(i, d)).wait_recv()

        if q == 1:
            @pl.loop(1, LANES)
            def _(d):
                c_arrival(plus(i, d)).wait_recv()

        lanes = []
        for j in range(LANES):
            y = yr[q, j]
            if q == 1:
                ends = pltpu.roll(yc[j, 8:16, :], lax.rem(128 - 2 * LEV * (i // 2), 128), 1)
                edge = jnp.where(row == 7 * own_half, 1.0, 0.0)
                y = jnp.concatenate(
                    [
                        y[l]
                        + ends[:, 2 * l : 2 * l + 1] * hm[0:1, :]
                        + ends[:, 2 * l + 1 : 2 * l + 2] * hm[1:2, :]
                        + edge * yc[j, l : l + 1, :]
                        for l in range(LEV)
                    ],
                    axis=0,
                )
            lanes.append(y.reshape(LEV * 8, RANK))
        pairs = []
        over = over_lanes(lanes)
        for group, pair in enumerate(over):
            coef = to_modes(jnp.concatenate(pair, axis=1), wf.at[group])
            wave = waves_of(group, lax.broadcasted_iota(jnp.int32, (8, 128), 1))
            keep = jnp.where(wave > cutoff, 2.0 / (COLS * LANES), 0.0)
            back = from_modes(coef * jnp.concatenate([keep] * LEV, axis=0), wb.at[group])
            pairs.append((back[:, :RANK], back[:, RANK:]))
        for j, z in enumerate(to_lanes(pairs)):
            z = z.reshape(LEV, 8, RANK)
            zbuf[q, j] = z
            eb[j, LEV * q : LEV * (q + 1), :] = jnp.where(own_half == 0, z[:, 0, :], z[:, 7, :])

        @pl.loop(1, LANES)
        def _(d):
            z_copy(q, plus(i, d)).start()

        zr[q, i] = zbuf[q, i]

    def edge_sends(act):
        slot = jnp.where(own_half == 0, slot_n, slot_s)
        lat = jnp.where(own_half == 0, nb, sb)

        @pl.loop(0, LANES)
        def _(d):
            j = plus(i, d)
            lon = jnp.where(edge_over, plus(j, LANES // 2), j)
            here = jnp.logical_and(edge_over, lon == i)

            @pl.when(jnp.logical_not(here))
            def _():
                act(
                    remote(
                        eb.at[j], bz.at[slot, i // 2], b_send.at[j], b_recv.at[slot, i // 2], lat, lon
                    )
                )

            if act is start_copy:
                @pl.when(here)
                def _():
                    pltpu.make_async_copy(eb.at[j], bz.at[slot, i // 2], b_recv.at[slot, i // 2]).start()

    def start_copy(copy):
        copy.start()

    def end_copy(copy):
        copy.wait_send()

    def project(q, out):
        @pl.loop(1, LANES)
        def _(d):
            z_arrival(q, plus(i, d)).wait_recv()

        z = jnp.concatenate(
            [zr[q, 2 * f + h, l] for f in range(FIELDS) for l in range(LEV) for h in range(2)], axis=0
        )
        out[...] = from_modes(z, qe).reshape(PAIRS, ROWS, WIDE)

    def tendency_rows(h):
        @pl.loop(0, LEV)
        def _(l):
            lo = jnp.maximum(l - 1, 0)
            hi = jnp.minimum(l + 1, LEV - 1)
            half = jnp.concatenate([hm[h : h + 8, :]] * 4, axis=1)
            ew = grid[PAIRS + l, h : h + 8, :]
            nw = grid[PAIRS + LEV + l, h : h + 8, :]
            along_x, along_y = [], []
            for f in range(FIELDS):
                mid = grid[f * LEV + l, h : h + 8, :]
                along_x.append(half * (roll(mid, -1, 1) - roll(mid, 1, 1)))
                along_y.append(0.5 * (grid[f * LEV + l, h + 1 : h + 9, :] - grid[f * LEV + l, h - 1 : h + 7, :]))
            linked = (along_x[2], along_y[2], along_x[0] + along_y[1], None)
            for f in range(FIELDS):
                mid = grid[f * LEV + l, h : h + 8, :]
                mixed = grid[f * LEV + lo, h : h + 8, :] + grid[f * LEV + hi, h : h + 8, :] - 2.0 * mid
                t = -(ew * along_x[f] + nw * along_y[f]) + mixing * mixed
                if linked[f] is not None:
                    t = t - coupling * linked[f]
                tend[f * LEV + l, h - 8 : h, :] = t

    for load in loads[5:]:
        load.wait()

    @pl.when(polar)
    def _():
        send_values(0)
        grid[0:PAIRS, 7:8, :] = jnp.zeros((PAIRS, 1, WIDE), F32)
        grid[0:PAIRS, 24:25, :] = jnp.zeros((PAIRS, 1, WIDE), F32)
        for part in range(2):
            tendency_rows(8 + 8 * part)
        values(1, tend[...])
        send_values(1)

    for s in range(2):
        remote(
            er.at[s, 0:FIELDS], hr.at[s, 0:FIELDS], row_send.at[s, 0], row_recv.at[s, 0], nb, nl
        ).wait_recv()
        remote(cp.at[s], hcol.at[s], col_send.at[s], col_recv.at[s], b, west).wait_recv()
    for send in corner_sends:
        send.start()

    flips = (-1.0, -1.0, 1.0, 1.0)
    over_pole = (is_north, is_south)
    lane2 = lax.broadcasted_iota(jnp.int32, (1, 128), 1)

    @pl.when(polar)
    def _():
        for s, sign in ((0, 1.0), (1, -1.0)):
            ghosts = [jnp.where(over_pole[s], flips[f], 1.0) * hr[s, f] for f in range(FIELDS)]
            for f, other in enumerate((None, 2, 1, None)):
                added = (0.5 * sign) * (er[s, 9] * ghosts[f])
                if other is not None:
                    added = added + (0.5 * sign * coupling) * ghosts[other]
                xb[(s * FIELDS + f) * LEV : (s * FIELDS + f + 1) * LEV, :] = added
        y = to_modes(xb[...], qf)
        for s in range(2):
            for f in range(FIELDS):
                cb[2 * f + s, 0:LEV, :] = y[(s * FIELDS + f) * LEV : (s * FIELDS + f + 1) * LEV, :]
        ends = []
        for side, sign in ((0, -1.0), (1, 1.0)):
            along_x = (sign * hm[8:24, :]) * (roll(hcol[0], -1, 1) if side == 0 else hcol[1])
            mine = jnp.where(
                jnp.logical_and(lane2 >= 2 * PAIRS, lane2 < 2 * (PAIRS + LEV)), cp[side], 0.0
            )
            ew = sum(roll(mine, 2 * LEV * f - 2 * PAIRS - side, 1) for f in range(FIELDS))
            linked = jnp.where(
                lane2 < 2 * LEV,
                roll(along_x, -4 * LEV, 1),
                jnp.where(
                    jnp.logical_and(lane2 >= 4 * LEV, lane2 < 6 * LEV), roll(along_x, 4 * LEV, 1), 0.0
                ),
            )
            ends.append(-ew * along_x - coupling * linked)
        ends = jnp.where(lax.rem(lane2, 2) == 0, ends[0], roll(ends[1], 1, 1))
        for f in range(FIELDS):
            for h in range(2):
                cb[2 * f + h, 8:16, :] = ends[8 * h : 8 * h + 8, :]

        @pl.loop(1, LANES)
        def _(d):
            c_copy(plus(i, d)).start()

        yc[i] = cb[i]

    @pl.when(polar)
    def _():
        own_rows(0)

    from_west = roll(hcol[0], 126, 1)
    from_east = roll(hcol[1], COLS - 384, 1)
    both = jnp.where(jnp.logical_and(lane2 >= 66, lane2 < 114), from_east, from_west)[None]
    for width in (2, 4, 8):
        both = jnp.concatenate([both, roll_blocks(both, -width)], axis=0)
    both = jnp.concatenate([both, roll_blocks(both, -16), roll_blocks(both, -32)], axis=0)
    in_halo = jnp.logical_or(
        jnp.logical_and(lane128 >= 66, lane128 < 68), lane128 >= 126
    )
    grid[:, 8:24, 384:512] = jnp.where(in_halo, both, grid[:, 8:24, 384:512])

    edge_row = (7, 24)
    inward = (1.0, -1.0)

    def edge_center(s, f):
        tile = hr[s, f][:, 384:512]
        tile = jnp.where(lane2 == 66, roll(hc[s, 1, f], 66, 1), tile)
        tile = jnp.where(lane2 == 127, roll(hc[s, 0, f], 62, 1), tile)
        return jnp.concatenate([hr[s, f][:, 0:384], tile], axis=1)

    for s in range(2):
        for side in range(2):
            remote(
                hr.at[s, 0:FIELDS, :, 0:128], hc.at[s, side], cor_send.at[s, side], cor_recv.at[s, side], b, west
            ).wait_recv()
    edge_probe = [[edge_center(s, f) for f in range(FIELDS)] for s in range(2)]
    for s in range(2):
        for f in range(FIELDS):
            flip = jnp.where(over_pole[s], flips[f], 1.0)
            grid[f * LEV : (f + 1) * LEV, edge_row[s], :] = flip * edge_probe[s][f]

    for part in range(2):
        tendency_rows(8 + 8 * part)

    for s in range(2):
        remote(
            er.at[s, FIELDS:10], hr.at[s, FIELDS:10], row_send.at[s, 1], row_recv.at[s, 1], nb, nl
        ).wait_recv()
        centers = edge_probe[s]
        half = jnp.concatenate([hm[edge_row[s] : edge_row[s] + 1, :]] * 4, axis=1)
        turn = jnp.where(over_pole[s], -inward[s], inward[s])
        along_x, along_y = [], []
        for f in range(FIELDS):
            flip = jnp.where(over_pole[s], flips[f], 1.0)
            along_x.append(half * (roll(centers[f], -1, 1) - roll(centers[f], 1, 1)))
            along_y.append((0.5 * turn) * (flip * er[s, f] - hr[s, FIELDS + f]))
        linked = (along_x[2], along_y[2], along_x[0] + along_y[1], None)
        for f in range(FIELDS):
            mid = centers[f]
            up = jnp.concatenate([mid[0:1], mid[0:3]], axis=0)
            down = jnp.concatenate([mid[1:4], mid[3:4]], axis=0)
            t = -(hr[s, 8] * along_x[f] + hr[s, 9] * along_y[f]) + mixing * (up + down - 2.0 * mid)
            if linked[f] is not None:
                t = t - coupling * linked[f]
            edge_t[s, f] = t

    @pl.when(polar)
    def _():
        own_rows(1)
        edge_sends(start_copy)
        project(0, proj_p)
        project(1, proj_t)

    @pl.when(jnp.logical_not(polar))
    def _():
        proj_p[...] = jnp.zeros(proj_p.shape, F32)
        proj_t[...] = jnp.zeros(proj_t.shape, F32)

    def row_weights(a, nw):
        return (
            -nw * a[0],
            -nw * a[1] - coupling * a[2],
            -nw * a[2] - coupling * a[1],
            -nw * a[3],
        )

    @pl.loop(0, LEV)
    def _(l):
        for h in (8, 16):
            nw = grid[PAIRS + LEV + l, h : h + 8, :]
            a = []
            for f in range(FIELDS):
                n = f * LEV + l
                change = time_step * (tend[n, h - 8 : h, :] - proj_t[n, h - 8 : h, :])
                tend[n, h - 8 : h, :] = change
                tangent = grid[n, h : h + 8, :] + change
                tan_v[f, l, h - 8 : h, :] = tangent[:, :COLS]
                a.append(tangent - proj_p[n, h - 8 : h, :])
                adj[n, h - 8 : h, :] = a[f]
            for f, weight in enumerate(row_weights(a, nw)):
                gy[f * LEV + l, h : h + 8, :] = weight

    tan_copy = pltpu.make_async_copy(tan_v, tan_out, out_sem.at[0])
    tan_copy.start()

    for s, wanted in enumerate((above_polar, below_polar)):
        @pl.when(wanted)
        def _():
            for f in range(FIELDS):
                remote(eb.at[f], bz.at[s, f], b_send.at[f], b_recv.at[s, f], nb, nl).wait_recv()
            edge_proj[s] = from_modes(bz[s].reshape(2 * PAIRS, RANK), qe).reshape(FIELDS, 2 * LEV, WIDE)

        @pl.when(jnp.logical_not(wanted))
        def _():
            edge_proj[s] = jnp.zeros((FIELDS, 2 * LEV, WIDE), F32)

    for s in range(2):
        a = []
        for f in range(FIELDS):
            a.append(
                edge_probe[s][f]
                + time_step * (edge_t[s, f] - edge_proj[s, f, LEV : 2 * LEV, :])
                - edge_proj[s, f, 0:LEV, :]
            )
        for f, weight in enumerate(row_weights(a, hr[s, 9])):
            flip = jnp.where(over_pole[s], -flips[f], 1.0)
            gy[f * LEV : (f + 1) * LEV, edge_row[s], :] = flip * weight

    @pl.loop(0, LEV)
    def _(l):
        lo = jnp.maximum(l - 1, 0)
        hi = jnp.minimum(l + 1, LEV - 1)
        for h in (8, 16):
            rows = slice(h - 8, h)
            half = jnp.concatenate([hm[h : h + 8, :]] * 4, axis=1)
            ew = grid[PAIRS + l, h : h + 8, :]
            a = [adj[f * LEV + l, rows, :] for f in range(FIELDS)]
            col_weights = (
                -ew * a[0] - coupling * a[2],
                -ew * a[1],
                -ew * a[2] - coupling * a[0],
                -ew * a[3],
            )
            for f in range(FIELDS):
                n = f * LEV + l
                back = half * (roll(col_weights[f], 1, 1) - roll(col_weights[f], -1, 1))
                back = back + 0.5 * (gy[n, h - 1 : h + 7, :] - gy[n, h + 1 : h + 9, :])
                back = back + mixing * (adj[f * LEV + lo, rows, :] + adj[f * LEV + hi, rows, :] - 2.0 * a[f])
                diag = grid[n, h : h + 8, :] * (tend[n, rows, :] + time_step * back)
                diag_v[f, l, rows, :] = diag[:, :COLS]

    diag_copy = pltpu.make_async_copy(diag_v, diag_out, out_sem.at[1])
    diag_copy.start()

    for send in halo_sends + corner_sends:
        send.wait_send()

    @pl.when(polar)
    def _():
        @pl.loop(1, LANES)
        def _(d):
            j = plus(i, d)
            for q in range(2):
                y_copy(q, j).wait_send()
                z_copy(q, j).wait_send()
            c_copy(j).wait_send()

        edge_sends(end_copy)

    tan_copy.wait()
    diag_copy.wait()


def hand_out(tan_in, diag_in, tan_out, diag_out, held, in_sem, out_sem):
    ways = [
        (
            pltpu.make_async_copy(src.at[f], held.at[n, f], in_sem.at[n, f]),
            pltpu.make_async_copy(held.at[n, f], dst.at[f], out_sem.at[n, f]),
        )
        for n, (src, dst) in enumerate(((tan_in, tan_out), (diag_in, diag_out)))
        for f in range(FIELDS)
    ]
    for arrive, leave in ways:
        arrive.start()
    for arrive, leave in ways:
        arrive.wait()
        leave.start()
    for arrive, leave in ways:
        leave.wait()


def per_device(bands, row_signs, col_signs, spread, east_wind, north_wind, cutoffs):
    any_spec = pl.BlockSpec(memory_space=pl.ANY)
    out = jax.ShapeDtypeStruct((FIELDS, LEV, ROWS, COLS), F32)
    tables = [jnp.asarray(table) for table in (half_metric(bands),) + mode_factors()]
    vmem = pltpu.VMEM
    dma = pltpu.SemaphoreType.DMA
    results = pl.pallas_call(
        functools.partial(kernel, bands),
        out_shape=(out, out),
        in_specs=[any_spec] * 11,
        out_specs=(any_spec, any_spec),
        scratch_shapes=[
            vmem((FIELDS, LEV, ROWS, COLS), F32),
            vmem((LEV, ROWS, COLS), F32),
            vmem((LEV, ROWS, COLS), F32),
            vmem((FIELDS, LEV, ROWS), jnp.int32),
            vmem((FIELDS, LEV, COLS), jnp.int32),
            pltpu.SMEM((ROWS,), jnp.int32),
            vmem((32, 128), F32),
            vmem((WIDE, 2 * RANK), BF16),
            vmem((3 * RANK, WIDE), BF16),
            vmem((4, 2 * RANK, 4 * 64), BF16),
            vmem((4, 6 * 64, 2 * RANK), BF16),
            vmem((PAIRS + 2 * LEV, 32, WIDE), F32),
            vmem((2, 10, LEV, WIDE), F32),
            vmem((2, 10, LEV, WIDE), F32),
            vmem((2, 2, FIELDS, LEV, 128), F32),
            vmem((2, ROWS, 128), F32),
            vmem((2, ROWS, 128), F32),
            vmem((2, LANES, LEV, 8, RANK), F32),
            vmem((2, LANES, LEV, 8, RANK), F32),
            vmem((2, LANES, LEV, 8, RANK), F32),
            vmem((2, LANES, LEV, 8, RANK), F32),
            vmem((2 * PAIRS, WIDE), F32),
            vmem((LANES, 16, RANK), F32),
            vmem((LANES, 16, RANK), F32),
            vmem((LANES, 2 * LEV, RANK), F32),
            vmem((2, FIELDS, 2 * LEV, RANK), F32),
            vmem((PAIRS, ROWS, WIDE), F32),
            vmem((PAIRS, ROWS, WIDE), F32),
            vmem((PAIRS, ROWS, WIDE), F32),
            vmem((2, FIELDS, LEV, WIDE), F32),
            vmem((2, FIELDS, 2 * LEV, WIDE), F32),
            vmem((PAIRS, ROWS, WIDE), F32),
            vmem((PAIRS, 32, WIDE), F32),
            vmem((FIELDS, LEV, ROWS, COLS), F32),
            vmem((FIELDS, LEV, ROWS, COLS), F32),
            dma((11,)),
            dma((2, 2)),
            dma((2, 2)),
            dma((2, 2)),
            dma((2, 2)),
            dma((2,)),
            dma((2,)),
            dma((2, LANES)),
            dma((2, LANES)),
            dma((LANES,)),
            dma((LANES,)),
            dma((2, LANES)),
            dma((2, LANES)),
            dma((LANES,)),
            dma((2, FIELDS)),
            dma((2,)),
        ],
        compiler_params=pltpu.CompilerParams(
            collective_id=0, has_side_effects=True, vmem_limit_bytes=64 * 2**20
        ),
        cost_estimate=pl.CostEstimate(flops=10**9, bytes_accessed=4 * 10**6, transcendentals=0),
    )(spread, east_wind, north_wind, row_signs, col_signs, cutoffs, *tables)
    return pl.pallas_call(
        hand_out,
        out_shape=(out, out),
        in_specs=[any_spec] * 2,
        out_specs=(any_spec, any_spec),
        scratch_shapes=[vmem((2, FIELDS, LEV, ROWS, COLS), F32), dma((2, FIELDS)), dma((2, FIELDS))],
        compiler_params=pltpu.CompilerParams(vmem_limit_bytes=64 * 2**20),
    )(*results)


def solution(mesh):
    return jax.shard_map(
        functools.partial(per_device, mesh.shape["lat"]),
        mesh=mesh,
        in_specs=(
            P(None, None, "lat"),
            P(None, None, "lon"),
            P(None, None, "lat", "lon"),
            P(None, "lat", "lon"),
            P(None, "lat", "lon"),
            P("lat"),
        ),
        out_specs=(P(None, None, "lat", "lon"), P(None, None, "lat", "lon")),
        check_vma=False,
    )
```

```python
import functools

import jax
import jax.numpy as jnp
import ml_dtypes
import numpy as np
from jax import lax
from jax.experimental import pallas as pl
from jax.experimental.pallas import tpu as pltpu
from jax.sharding import PartitionSpec as P

KTOP = 256
POLAR = 32
RANK = 128
ROWS = 16
COLS = 450
WIDE = 512
LANES = 8
FIELDS = 4
LEV = 4
PAIRS = FIELDS * LEV

time_step = 0.5
coupling = 0.5
mixing = 0.2
metric_cap = 4.0

MESH = pl.DeviceIdType.MESH
F32 = jnp.float32
BF16 = jnp.bfloat16


def split_table(table):
    high = table.astype(ml_dtypes.bfloat16)
    low = (table - high.astype(np.float64)).astype(ml_dtypes.bfloat16)
    return high, low


def waves_of(group, lane_index):
    place = lane_index % 64
    second = place // 32
    other = (8 - group) if group else 4
    residue = group + second * (other - group)
    return 8 * (place % 32) + residue + (8 * (1 - second) if group == 0 else 0)


@functools.lru_cache(None)
def mode_factors():
    total = COLS * LANES
    size = COLS + 2
    place = np.arange(size, dtype=np.float64)
    width = (KTOP + 0.5) / total
    diag = ((size - 1 - 2 * place) / 2) ** 2 * np.cos(2 * np.pi * width)
    side = place[1:] * (size - place[1:]) / 2
    vectors = np.linalg.eigh(np.diag(diag) + np.diag(side, 1) + np.diag(side, -1))[1]
    basis = vectors[:, ::-1][:, :RANK]
    basis = basis * np.where(basis[size // 2] < 0, -1.0, 1.0)
    weights = []
    for group in range(4):
        waves = waves_of(group, np.arange(64))
        angle = 2 * np.pi / total * ((np.arange(size)[:, None] - 1) * waves[None, :] % total)
        alpha, beta = basis.T @ np.cos(angle), basis.T @ np.sin(angle)
        if group:
            sign = np.where(np.arange(64) < 32, 1.0, -1.0)
            top, low = (alpha, beta), (sign * beta, -sign * alpha)
        else:
            use = np.where(np.arange(64) < 32, 1.0, 0.0)
            top, low = (use * alpha, use * beta), ((1 - use) * alpha, (1 - use) * beta)
        weights.append(np.concatenate([np.concatenate(top, axis=1), np.concatenate(low, axis=1)], axis=0))
    weights = np.round(np.stack(weights) * 2.0**22) / 2.0**22
    wide = np.zeros((RANK, WIDE))
    wide[:, : COLS + 1] = basis[1:].T
    wide[:, WIDE - 1] = basis[0]
    wide = np.round(wide * 2.0**26) / 2.0**26
    wide_h, wide_l = split_table(wide)
    own = np.where(np.arange(WIDE)[:, None] < COLS, 1, 0).astype(ml_dtypes.bfloat16)
    high, low = split_table(weights)
    back = [np.swapaxes(part, 1, 2) for part in (high, low, high)]
    return (
        np.concatenate([wide_h.T * own, wide_l.T * own], axis=1),
        np.concatenate([wide_h, wide_l, wide_h], axis=0),
        np.concatenate([high, low], axis=2),
        np.concatenate(back, axis=1),
    )


ROOT = float(np.sqrt(0.5))


def over_lanes(y):
    s = [y[j] + y[j + 4] for j in range(4)]
    d = [y[j] - y[j + 4] for j in range(4)]
    even, odd = s[0] + s[2], s[1] + s[3]
    minus, plus = ROOT * (d[1] - d[3]), ROOT * (d[1] + d[3])
    return [
        (even + odd, even - odd),
        (d[0] + minus, -(d[2] + plus)),
        (s[0] - s[2], s[3] - s[1]),
        (d[0] - minus, d[2] - plus),
    ]


def to_lanes(pairs):
    (y0, y4), (u1, v1), (u2, v2), (u3, v3) = pairs
    even, odd = y0 + y4, y0 - y4
    s = [even + u2, odd - v2, even - u2, odd + v2]
    du, sv = ROOT * (u1 - u3), ROOT * (v1 + v3)
    d = [u1 + u3, du - sv, v3 - v1, -du - sv]
    return [s[j] + d[j] for j in range(4)] + [s[j] - d[j] for j in range(4)]


@functools.lru_cache(None)
def half_metric(bands):
    total = bands * ROWS
    rows = np.clip(np.arange(bands)[:, None] * ROWS - 8 + np.arange(32)[None, :], 0, total - 1)
    metric = np.minimum(1.0 / np.cos(np.pi * ((rows + 0.5) / total - 0.5)), metric_cap)
    table = np.broadcast_to((0.5 * metric).astype(np.float32)[:, :, None], (bands, 32, 128)).copy()
    forward = mode_factors()[0].astype(np.float32)
    for row, col in enumerate((0, COLS - 1)):
        table[:, row] = forward[col, :RANK] + forward[col, RANK:]
    return table


def dot_cols(a, b):
    return lax.dot_general(a, b, (((1,), (0,)), ((), ())), preferred_element_type=F32)


def split(x):
    high = x.astype(BF16)
    return high, (x - high.astype(F32)).astype(BF16)


def to_modes(x, table):
    xh, xl = split(x)
    half = table.shape[1] // 2
    wide = dot_cols(xh, table[...])
    return wide[:, :half] + wide[:, half:] + dot_cols(xl, table[:, 0:half])


def from_modes(z, table):
    zh, zl = split(z)
    return dot_cols(jnp.concatenate([zh, zh, zl], axis=1), table[...])


def roll(x, shift, axis):
    return pltpu.roll(x, shift % x.shape[axis], axis)


def roll_blocks(x, shift):
    return roll(x.reshape(x.shape[0] * x.shape[1], x.shape[2]), shift, 1).reshape(x.shape)


def fold(x):
    while x.shape[0] > 1:
        half = x.shape[0] // 2
        x = x[:half] + roll_blocks(x[half:], 2 * half)
    return x


def kernel(
    bands, spread, east, north, rs, cs, cut, metric, qf_in, qe_in, wf_in, wb_in, tan_out, diag_out,
    spread_v, east_v, north_v, rs_v, cs_v, cut_s, hm, qf, qe, wf, wb,
    grid, er, hr, hc, cp, hcol, ybuf, yr, zbuf, zr, xb, cb, yc, eb, bz,
    tend, proj_p, proj_t, edge_t, edge_proj, adj, gy, tan_v, diag_v,
    in_sem, row_send, row_recv, cor_send, cor_recv, col_send, col_recv,
    y_send, y_recv, c_send, c_recv, z_send, z_recv, b_send, b_recv, out_sem,
):
    b = lax.axis_index("lat")
    i = lax.axis_index("lon")
    caps = POLAR // ROWS
    is_north = b == 0
    is_south = b == bands - 1
    polar = jnp.logical_or(b < caps, b >= bands - caps)
    above_polar = jnp.logical_or(b <= caps, is_south)
    below_polar = jnp.logical_or(b >= bands - caps - 1, is_north)
    across = lax.rem(i + LANES // 2, LANES)
    west = lax.rem(i + LANES - 1, LANES)
    east_lane = lax.rem(i + 1, LANES)
    nb = jnp.where(is_north, 0, b - 1)
    nl = jnp.where(is_north, across, i)
    sb = jnp.where(is_south, bands - 1, b + 1)
    sl = jnp.where(is_south, across, i)
    slot_n = jnp.where(is_north, 0, 1)
    slot_s = jnp.where(is_south, 1, 0)

    def plus(lane, d):
        return lax.rem(lane + d, LANES)

    loads = [
        pltpu.make_async_copy(spread, spread_v, in_sem.at[0]),
        pltpu.make_async_copy(rs, rs_v, in_sem.at[1]),
        pltpu.make_async_copy(cs, cs_v, in_sem.at[2]),
        pltpu.make_async_copy(east, east_v, in_sem.at[3]),
        pltpu.make_async_copy(north, north_v, in_sem.at[4]),
        pltpu.make_async_copy(metric.at[b], hm, in_sem.at[5]),
        pltpu.make_async_copy(cut, cut_s, in_sem.at[6]),
        pltpu.make_async_copy(qe_in, qe, in_sem.at[7]),
    ]
    table_loads = [
        pltpu.make_async_copy(qf_in, qf, in_sem.at[8]),
        pltpu.make_async_copy(wf_in, wf, in_sem.at[9]),
        pltpu.make_async_copy(wb_in, wb, in_sem.at[10]),
    ]
    for load in loads:
        load.start()

    @pl.when(polar)
    def _():
        for load in table_loads:
            load.start()

    def values(q, x):
        y = to_modes(x.reshape(PAIRS * ROWS, WIDE), qf).reshape(FIELDS, LEV, 2, 8, RANK)
        for f in range(FIELDS):
            for h in range(2):
                for l in range(LEV):
                    ybuf[2 * f + h, q, l] = y[f, l, h]

    def probe_values():
        values(0, grid[0:PAIRS, 8:24, :])

    barrier = pltpu.get_barrier_semaphore()

    def greet(lat, lon):
        pl.semaphore_signal(barrier, inc=1, device_id=(lat, lon), device_id_type=MESH)

    greet(nb, nl)
    greet(sb, sl)
    greet(b, west)
    greet(b, east_lane)

    @pl.when(polar)
    def _():
        @pl.loop(2, LANES - 1)
        def _(d):
            greet(b, plus(i, d))

    for load in loads[:5]:
        load.wait()
    grid[:, 8:24, 384:512] = jnp.zeros((PAIRS + 2 * LEV, ROWS, 128), F32)
    row_part = jnp.concatenate([rs_v[f] for f in range(FIELDS)], axis=0)
    row_part = (2 * row_part - 1).astype(F32).T
    for f in range(FIELDS):
        col_part = (2 * cs_v[f] - 1).astype(F32)
        for l in range(LEV):
            n = f * LEV + l
            grid[n, 8:24, 0:COLS] = spread_v[f, l] * (row_part[:, n : n + 1] * col_part[l : l + 1, :])
    for l in range(LEV):
        grid[PAIRS + l, 8:24, 0:COLS] = east_v[l]
        grid[PAIRS + LEV + l, 8:24, 0:COLS] = north_v[l]

    for s, (near, far) in enumerate(((8, 9), (23, 22))):
        for f in range(FIELDS + 2):
            er[s, f if f < FIELDS else f + FIELDS] = grid[f * LEV : (f + 1) * LEV, near, :]
        for f in range(FIELDS):
            er[s, FIELDS + f] = grid[f * LEV : (f + 1) * LEV, far, :]
    lane128 = lax.broadcasted_iota(jnp.int32, (1, 1, 128), 2)
    for s, (start, shift) in enumerate(((0, 0), (384, COLS - 2 - 384))):
        tile = grid[:, 8:24, start : start + 128]
        tile = jnp.where(jnp.logical_and(lane128 >= shift, lane128 < shift + 2), tile, 0.0)
        packed = fold(tile[:PAIRS]) + roll_blocks(fold(tile[PAIRS:]), 2 * PAIRS)
        cp[s] = roll_blocks(packed, -shift)[0]

    own_half = lax.rem(i, 2)
    edge_over = jnp.where(own_half == 0, is_north, is_south)

    @pl.when(polar)
    def _():
        for load in table_loads:
            load.wait()
        probe_values()

    pl.semaphore_wait(barrier, 4 + jnp.where(polar, LANES - 3, 0))

    def remote(src, dst, send, recv, lat, lon):
        return pltpu.make_async_remote_copy(
            src_ref=src, dst_ref=dst, send_sem=send, recv_sem=recv, device_id=(lat, lon), device_id_type=MESH
        )

    halo_sends = [
        remote(
            er.at[0, 0:FIELDS], hr.at[slot_n, 0:FIELDS], row_send.at[0, 0], row_recv.at[slot_n, 0], nb, nl
        ),
        remote(
            er.at[1, 0:FIELDS], hr.at[slot_s, 0:FIELDS], row_send.at[1, 0], row_recv.at[slot_s, 0], sb, sl
        ),
        remote(cp.at[0], hcol.at[1], col_send.at[0], col_recv.at[1], b, west),
        remote(cp.at[1], hcol.at[0], col_send.at[1], col_recv.at[0], b, east_lane),
    ]
    halo_sends += [
        remote(er.at[0, FIELDS:10], hr.at[slot_n, FIELDS:10], row_send.at[0, 1], row_recv.at[slot_n, 1], nb, nl),
        remote(er.at[1, FIELDS:10], hr.at[slot_s, FIELDS:10], row_send.at[1, 1], row_recv.at[slot_s, 1], sb, sl),
    ]
    for send in halo_sends:
        send.start()

    corner_sends = [
        remote(
            hr.at[s, 0:FIELDS, :, start : start + 128], hc.at[s, side], cor_send, cor_recv, b, lon,
        )
        for s in range(2)
        for side, start, lon in ((0, 384, east_lane), (1, 0, west))
    ]

    def y_copy(o):
        return remote(ybuf.at[o], yr.at[i], y_send, y_recv, b, o)

    others = pl.ds(0, LANES - 1)

    def all_y():
        return remote(ybuf.at[others], yr.at[others], y_send, y_recv, b, west)

    def send_values():
        @pl.loop(1, LANES)
        def _(d):
            y_copy(plus(i, d)).start()

        yr[i] = ybuf[i]

    def c_copy(o):
        return remote(cb.at[o], yc.at[i], c_send, c_recv, b, o)

    def all_c():
        return remote(cb.at[others], yc.at[others], c_send, c_recv, b, west)

    def z_copy(q, j):
        return remote(zbuf.at[q, j], zr.at[q, i], z_send.at[q], z_recv.at[q], b, j)

    def all_z(q):
        return remote(zbuf.at[q, others], zr.at[q, others], z_send.at[q], z_recv.at[q], b, west)

    def own_rows(q):
        row = lax.broadcasted_iota(jnp.int32, (8, 128), 0)
        cutoff = jnp.zeros((8, 128), jnp.int32)
        for r in range(8):
            cutoff = jnp.where(row == r, cut_s[8 * own_half + r], cutoff)

        if q == 0:
            all_y().wait_recv()
        else:
            all_c().wait_recv()

        lanes = []
        for j in range(LANES):
            y = yr[j, q]
            if q == 1:
                ends = pltpu.roll(yc[j, 8:16, :], lax.rem(128 - 2 * LEV * (i // 2), 128), 1)
                edge = jnp.where(row == 7 * own_half, 1.0, 0.0)
                y = jnp.concatenate(
                    [
                        y[l]
                        + ends[:, 2 * l : 2 * l + 1] * hm[0:1, :]
                        + ends[:, 2 * l + 1 : 2 * l + 2] * hm[1:2, :]
                        + edge * yc[j, l : l + 1, :]
                        for l in range(LEV)
                    ],
                    axis=0,
                )
            lanes.append(y.reshape(LEV * 8, RANK))
        pairs = []
        over = over_lanes(lanes)
        for group, pair in enumerate(over):
            coef = to_modes(jnp.concatenate(pair, axis=1), wf.at[group])
            wave = waves_of(group, lax.broadcasted_iota(jnp.int32, (8, 128), 1))
            keep = jnp.where(wave > cutoff, 2.0 / (COLS * LANES), 0.0)
            back = from_modes(coef * jnp.concatenate([keep] * LEV, axis=0), wb.at[group])
            pairs.append((back[:, :RANK], back[:, RANK:]))
        for j, z in enumerate(to_lanes(pairs)):
            z = z.reshape(LEV, 8, RANK)
            zbuf[q, j] = z
            eb[j, LEV * q : LEV * (q + 1), :] = jnp.where(own_half == 0, z[:, 0, :], z[:, 7, :])

        @pl.loop(1, LANES)
        def _(d):
            z_copy(q, plus(i, d)).start()

        zr[q, i] = zbuf[q, i]

    def edge_sends():
        slot = jnp.where(own_half == 0, slot_n, slot_s)
        lat = jnp.where(own_half == 0, nb, sb)

        @pl.loop(0, LANES)
        def _(d):
            j = plus(i, d)
            lon = jnp.where(edge_over, plus(j, LANES // 2), j)
            here = jnp.logical_and(edge_over, lon == i)

            @pl.when(jnp.logical_not(here))
            def _():
                remote(eb.at[j], bz.at[slot, i // 2], b_send, b_recv.at[slot], lat, lon).start()

            @pl.when(here)
            def _():
                pltpu.make_async_copy(eb.at[j], bz.at[slot, i // 2], b_recv.at[slot]).start()

    def project(q, out):
        all_z(q).wait_recv()
        z = jnp.concatenate(
            [zr[q, 2 * f + h, l] for f in range(FIELDS) for l in range(LEV) for h in range(2)], axis=0
        )
        out[...] = from_modes(z, qe).reshape(PAIRS, ROWS, WIDE)

    def tendency_rows(h):
        @pl.loop(0, LEV)
        def _(l):
            lo = jnp.maximum(l - 1, 0)
            hi = jnp.minimum(l + 1, LEV - 1)
            half = jnp.concatenate([hm[h : h + 8, :]] * 4, axis=1)
            ew = grid[PAIRS + l, h : h + 8, :]
            nw = grid[PAIRS + LEV + l, h : h + 8, :]
            along_x, along_y = [], []
            for f in range(FIELDS):
                mid = grid[f * LEV + l, h : h + 8, :]
                along_x.append(half * (roll(mid, -1, 1) - roll(mid, 1, 1)))
                along_y.append(0.5 * (grid[f * LEV + l, h + 1 : h + 9, :] - grid[f * LEV + l, h - 1 : h + 7, :]))
            linked = (along_x[2], along_y[2], along_x[0] + along_y[1], None)
            for f in range(FIELDS):
                mid = grid[f * LEV + l, h : h + 8, :]
                mixed = grid[f * LEV + lo, h : h + 8, :] + grid[f * LEV + hi, h : h + 8, :] - 2.0 * mid
                t = -(ew * along_x[f] + nw * along_y[f]) + mixing * mixed
                if linked[f] is not None:
                    t = t - coupling * linked[f]
                tend[f * LEV + l, h - 8 : h, :] = t

    for load in loads[5:]:
        load.wait()

    @pl.when(polar)
    def _():
        grid[0:PAIRS, 7:8, :] = jnp.zeros((PAIRS, 1, WIDE), F32)
        grid[0:PAIRS, 24:25, :] = jnp.zeros((PAIRS, 1, WIDE), F32)
        for part in range(2):
            tendency_rows(8 + 8 * part)
        values(1, tend[...])
        send_values()

    for s in range(2):
        remote(
            er.at[s, 0:FIELDS], hr.at[s, 0:FIELDS], row_send.at[s, 0], row_recv.at[s, 0], nb, nl
        ).wait_recv()
        remote(cp.at[s], hcol.at[s], col_send.at[s], col_recv.at[s], b, west).wait_recv()
    for send in corner_sends:
        send.start()

    flips = (-1.0, -1.0, 1.0, 1.0)
    over_pole = (is_north, is_south)
    lane2 = lax.broadcasted_iota(jnp.int32, (1, 128), 1)

    @pl.when(polar)
    def _():
        for s, sign in ((0, 1.0), (1, -1.0)):
            ghosts = [jnp.where(over_pole[s], flips[f], 1.0) * hr[s, f] for f in range(FIELDS)]
            for f, other in enumerate((None, 2, 1, None)):
                added = (0.5 * sign) * (er[s, 9] * ghosts[f])
                if other is not None:
                    added = added + (0.5 * sign * coupling) * ghosts[other]
                xb[(s * FIELDS + f) * LEV : (s * FIELDS + f + 1) * LEV, :] = added
        y = to_modes(xb[...], qf)
        for s in range(2):
            for f in range(FIELDS):
                cb[2 * f + s, 0:LEV, :] = y[(s * FIELDS + f) * LEV : (s * FIELDS + f + 1) * LEV, :]
        ends = []
        for side, sign in ((0, -1.0), (1, 1.0)):
            along_x = (sign * hm[8:24, :]) * (roll(hcol[0], -1, 1) if side == 0 else hcol[1])
            mine = jnp.where(
                jnp.logical_and(lane2 >= 2 * PAIRS, lane2 < 2 * (PAIRS + LEV)), cp[side], 0.0
            )
            ew = sum(roll(mine, 2 * LEV * f - 2 * PAIRS - side, 1) for f in range(FIELDS))
            linked = jnp.where(
                lane2 < 2 * LEV,
                roll(along_x, -4 * LEV, 1),
                jnp.where(
                    jnp.logical_and(lane2 >= 4 * LEV, lane2 < 6 * LEV), roll(along_x, 4 * LEV, 1), 0.0
                ),
            )
            ends.append(-ew * along_x - coupling * linked)
        ends = jnp.where(lax.rem(lane2, 2) == 0, ends[0], roll(ends[1], 1, 1))
        for f in range(FIELDS):
            for h in range(2):
                cb[2 * f + h, 8:16, :] = ends[8 * h : 8 * h + 8, :]

        @pl.loop(1, LANES)
        def _(d):
            c_copy(plus(i, d)).start()

        yc[i] = cb[i]

    @pl.when(polar)
    def _():
        own_rows(0)
        own_rows(1)
        edge_sends()

    from_west = roll(hcol[0], 126, 1)
    from_east = roll(hcol[1], COLS - 384, 1)
    both = jnp.where(jnp.logical_and(lane2 >= 66, lane2 < 114), from_east, from_west)[None]
    for width in (2, 4, 8):
        both = jnp.concatenate([both, roll_blocks(both, -width)], axis=0)
    both = jnp.concatenate([both, roll_blocks(both, -16), roll_blocks(both, -32)], axis=0)
    in_halo = jnp.logical_or(
        jnp.logical_and(lane128 >= 66, lane128 < 68), lane128 >= 126
    )
    grid[:, 8:24, 384:512] = jnp.where(in_halo, both, grid[:, 8:24, 384:512])

    edge_row = (7, 24)
    inward = (1.0, -1.0)

    def edge_center(s, f):
        tile = hr[s, f][:, 384:512]
        tile = jnp.where(lane2 == 66, roll(hc[s, 1, f], 66, 1), tile)
        tile = jnp.where(lane2 == 127, roll(hc[s, 0, f], 62, 1), tile)
        return jnp.concatenate([hr[s, f][:, 0:384], tile], axis=1)

    remote(hc, hc, cor_send, cor_recv, b, west).wait_recv()
    edge_probe = [[edge_center(s, f) for f in range(FIELDS)] for s in range(2)]
    for s in range(2):
        for f in range(FIELDS):
            flip = jnp.where(over_pole[s], flips[f], 1.0)
            grid[f * LEV : (f + 1) * LEV, edge_row[s], :] = flip * edge_probe[s][f]

    for part in range(2):
        tendency_rows(8 + 8 * part)

    for s in range(2):
        remote(
            er.at[s, FIELDS:10], hr.at[s, FIELDS:10], row_send.at[s, 1], row_recv.at[s, 1], nb, nl
        ).wait_recv()
        centers = edge_probe[s]
        half = jnp.concatenate([hm[edge_row[s] : edge_row[s] + 1, :]] * 4, axis=1)
        turn = jnp.where(over_pole[s], -inward[s], inward[s])
        along_x, along_y = [], []
        for f in range(FIELDS):
            flip = jnp.where(over_pole[s], flips[f], 1.0)
            along_x.append(half * (roll(centers[f], -1, 1) - roll(centers[f], 1, 1)))
            along_y.append((0.5 * turn) * (flip * er[s, f] - hr[s, FIELDS + f]))
        linked = (along_x[2], along_y[2], along_x[0] + along_y[1], None)
        for f in range(FIELDS):
            mid = centers[f]
            up = jnp.concatenate([mid[0:1], mid[0:3]], axis=0)
            down = jnp.concatenate([mid[1:4], mid[3:4]], axis=0)
            t = -(hr[s, 8] * along_x[f] + hr[s, 9] * along_y[f]) + mixing * (up + down - 2.0 * mid)
            if linked[f] is not None:
                t = t - coupling * linked[f]
            edge_t[s, f] = t

    @pl.when(polar)
    def _():
        project(0, proj_p)
        project(1, proj_t)

    @pl.when(jnp.logical_not(polar))
    def _():
        proj_p[...] = jnp.zeros(proj_p.shape, F32)
        proj_t[...] = jnp.zeros(proj_t.shape, F32)

    def row_weights(a, nw):
        return (
            -nw * a[0],
            -nw * a[1] - coupling * a[2],
            -nw * a[2] - coupling * a[1],
            -nw * a[3],
        )

    @pl.loop(0, LEV)
    def _(l):
        for h in (8, 16):
            nw = grid[PAIRS + LEV + l, h : h + 8, :]
            a = []
            for f in range(FIELDS):
                n = f * LEV + l
                change = time_step * (tend[n, h - 8 : h, :] - proj_t[n, h - 8 : h, :])
                tend[n, h - 8 : h, :] = change
                tangent = grid[n, h : h + 8, :] + change
                tan_v[f, l, h - 8 : h, :] = tangent[:, :COLS]
                a.append(tangent - proj_p[n, h - 8 : h, :])
                adj[n, h - 8 : h, :] = a[f]
            for f, weight in enumerate(row_weights(a, nw)):
                gy[f * LEV + l, h : h + 8, :] = weight

    tan_copy = pltpu.make_async_copy(tan_v, tan_out, out_sem.at[0])
    tan_copy.start()

    for s, wanted in enumerate((above_polar, below_polar)):
        @pl.when(wanted)
        def _():
            remote(bz.at[s], bz.at[s], b_send, b_recv.at[s], nb, nl).wait_recv()
            edge_proj[s] = from_modes(bz[s].reshape(2 * PAIRS, RANK), qe).reshape(FIELDS, 2 * LEV, WIDE)

        @pl.when(jnp.logical_not(wanted))
        def _():
            edge_proj[s] = jnp.zeros((FIELDS, 2 * LEV, WIDE), F32)

    for s in range(2):
        a = []
        for f in range(FIELDS):
            a.append(
                edge_probe[s][f]
                + time_step * (edge_t[s, f] - edge_proj[s, f, LEV : 2 * LEV, :])
                - edge_proj[s, f, 0:LEV, :]
            )
        for f, weight in enumerate(row_weights(a, hr[s, 9])):
            flip = jnp.where(over_pole[s], -flips[f], 1.0)
            gy[f * LEV : (f + 1) * LEV, edge_row[s], :] = flip * weight

    @pl.loop(0, LEV)
    def _(l):
        lo = jnp.maximum(l - 1, 0)
        hi = jnp.minimum(l + 1, LEV - 1)
        for h in (8, 16):
            rows = slice(h - 8, h)
            half = jnp.concatenate([hm[h : h + 8, :]] * 4, axis=1)
            ew = grid[PAIRS + l, h : h + 8, :]
            a = [adj[f * LEV + l, rows, :] for f in range(FIELDS)]
            col_weights = (
                -ew * a[0] - coupling * a[2],
                -ew * a[1],
                -ew * a[2] - coupling * a[0],
                -ew * a[3],
            )
            for f in range(FIELDS):
                n = f * LEV + l
                back = half * (roll(col_weights[f], 1, 1) - roll(col_weights[f], -1, 1))
                back = back + 0.5 * (gy[n, h - 1 : h + 7, :] - gy[n, h + 1 : h + 9, :])
                back = back + mixing * (adj[f * LEV + lo, rows, :] + adj[f * LEV + hi, rows, :] - 2.0 * a[f])
                diag = grid[n, h : h + 8, :] * (tend[n, rows, :] + time_step * back)
                diag_v[f, l, rows, :] = diag[:, :COLS]

    diag_copy = pltpu.make_async_copy(diag_v, diag_out, out_sem.at[1])
    diag_copy.start()

    for send in halo_sends:
        send.wait_send()
    remote(hc, hc, cor_send, cor_recv, b, west).wait_send()

    @pl.when(polar)
    def _():
        all_y().wait_send()
        all_c().wait_send()
        for q in range(2):
            all_z(q).wait_send()

        @pl.when(edge_over)
        def _():
            remote(eb.at[others], eb.at[others], b_send, b_recv.at[0], b, west).wait_send()

        @pl.when(jnp.logical_not(edge_over))
        def _():
            remote(eb, eb, b_send, b_recv.at[0], b, west).wait_send()

    tan_copy.wait()
    diag_copy.wait()


def hand_out(tan_in, diag_in, tan_out, diag_out, held, in_sem, out_sem):
    ways = [
        (
            pltpu.make_async_copy(src.at[f], held.at[n, f], in_sem.at[n, f]),
            pltpu.make_async_copy(held.at[n, f], dst.at[f], out_sem.at[n, f]),
        )
        for n, (src, dst) in enumerate(((tan_in, tan_out), (diag_in, diag_out)))
        for f in range(FIELDS)
    ]
    for arrive, leave in ways:
        arrive.start()
    for arrive, leave in ways:
        arrive.wait()
        leave.start()
    for arrive, leave in ways:
        leave.wait()


def per_device(bands, row_signs, col_signs, spread, east_wind, north_wind, cutoffs):
    any_spec = pl.BlockSpec(memory_space=pl.ANY)
    out = jax.ShapeDtypeStruct((FIELDS, LEV, ROWS, COLS), F32)
    tables = [jnp.asarray(table) for table in (half_metric(bands),) + mode_factors()]
    vmem = pltpu.VMEM
    dma = pltpu.SemaphoreType.DMA
    results = pl.pallas_call(
        functools.partial(kernel, bands),
        out_shape=(out, out),
        in_specs=[any_spec] * 11,
        out_specs=(any_spec, any_spec),
        scratch_shapes=[
            vmem((FIELDS, LEV, ROWS, COLS), F32),
            vmem((LEV, ROWS, COLS), F32),
            vmem((LEV, ROWS, COLS), F32),
            vmem((FIELDS, LEV, ROWS), jnp.int32),
            vmem((FIELDS, LEV, COLS), jnp.int32),
            pltpu.SMEM((ROWS,), jnp.int32),
            vmem((32, 128), F32),
            vmem((WIDE, 2 * RANK), BF16),
            vmem((3 * RANK, WIDE), BF16),
            vmem((4, 2 * RANK, 4 * 64), BF16),
            vmem((4, 6 * 64, 2 * RANK), BF16),
            vmem((PAIRS + 2 * LEV, 32, WIDE), F32),
            vmem((2, 10, LEV, WIDE), F32),
            vmem((2, 10, LEV, WIDE), F32),
            vmem((2, 2, FIELDS, LEV, 128), F32),
            vmem((2, ROWS, 128), F32),
            vmem((2, ROWS, 128), F32),
            vmem((LANES, 2, LEV, 8, RANK), F32),
            vmem((LANES, 2, LEV, 8, RANK), F32),
            vmem((2, LANES, LEV, 8, RANK), F32),
            vmem((2, LANES, LEV, 8, RANK), F32),
            vmem((2 * PAIRS, WIDE), F32),
            vmem((LANES, 16, RANK), F32),
            vmem((LANES, 16, RANK), F32),
            vmem((LANES, 2 * LEV, RANK), F32),
            vmem((2, FIELDS, 2 * LEV, RANK), F32),
            vmem((PAIRS, ROWS, WIDE), F32),
            vmem((PAIRS, ROWS, WIDE), F32),
            vmem((PAIRS, ROWS, WIDE), F32),
            vmem((2, FIELDS, LEV, WIDE), F32),
            vmem((2, FIELDS, 2 * LEV, WIDE), F32),
            vmem((PAIRS, ROWS, WIDE), F32),
            vmem((PAIRS, 32, WIDE), F32),
            vmem((FIELDS, LEV, ROWS, COLS), F32),
            vmem((FIELDS, LEV, ROWS, COLS), F32),
            dma((11,)),
            dma((2, 2)),
            dma((2, 2)),
            dma,
            dma,
            dma((2,)),
            dma((2,)),
            dma,
            dma,
            dma,
            dma,
            dma((2,)),
            dma((2,)),
            dma,
            dma((2,)),
            dma((2,)),
        ],
        compiler_params=pltpu.CompilerParams(
            collective_id=0, has_side_effects=True, vmem_limit_bytes=64 * 2**20
        ),
        cost_estimate=pl.CostEstimate(flops=10**9, bytes_accessed=4 * 10**6, transcendentals=0),
    )(spread, east_wind, north_wind, row_signs, col_signs, cutoffs, *tables)
    return pl.pallas_call(
        hand_out,
        out_shape=(out, out),
        in_specs=[any_spec] * 2,
        out_specs=(any_spec, any_spec),
        scratch_shapes=[vmem((2, FIELDS, LEV, ROWS, COLS), F32), dma((2, FIELDS)), dma((2, FIELDS))],
        compiler_params=pltpu.CompilerParams(vmem_limit_bytes=64 * 2**20),
    )(*results)


def solution(mesh):
    return jax.shard_map(
        functools.partial(per_device, mesh.shape["lat"]),
        mesh=mesh,
        in_specs=(
            P(None, None, "lat"),
            P(None, None, "lon"),
            P(None, None, "lat", "lon"),
            P(None, "lat", "lon"),
            P(None, "lat", "lon"),
            P("lat"),
        ),
        out_specs=(P(None, None, "lat", "lon"), P(None, None, "lat", "lon")),
        check_vma=False,
    )
```

```python
import functools

import jax
import jax.numpy as jnp
import ml_dtypes
import numpy as np
from jax import lax
from jax.experimental import pallas as pl
from jax.experimental.pallas import tpu as pltpu
from jax.sharding import PartitionSpec as P

KTOP = 256
POLAR = 32
RANK = 128
ROWS = 16
COLS = 450
WIDE = 512
LANES = 8
FIELDS = 4
LEV = 4
PAIRS = FIELDS * LEV

time_step = 0.5
coupling = 0.5
mixing = 0.2
metric_cap = 4.0

EVALUATE, FORWARD, TO_COEFS, FROM_COEFS, TABLE_ROWS = 0, 768, 1280, 2304, 3840
NEAR, SIDES, REST, BLOCKS = 0, 8, 10, 24

MESH = pl.DeviceIdType.MESH
F32 = jnp.float32
BF16 = jnp.bfloat16


def split_table(table):
    high = table.astype(ml_dtypes.bfloat16)
    low = (table - high.astype(np.float64)).astype(ml_dtypes.bfloat16)
    return high, low


def waves_of(group, lane_index):
    place = lane_index % 64
    second = place // 32
    other = (8 - group) if group else 4
    residue = group + second * (other - group)
    return 8 * (place % 32) + residue + (8 * (1 - second) if group == 0 else 0)


@functools.lru_cache(None)
def mode_factors():
    total = COLS * LANES
    size = COLS + 2
    place = np.arange(size, dtype=np.float64)
    width = (KTOP + 0.5) / total
    diag = ((size - 1 - 2 * place) / 2) ** 2 * np.cos(2 * np.pi * width)
    side = place[1:] * (size - place[1:]) / 2
    vectors = np.linalg.eigh(np.diag(diag) + np.diag(side, 1) + np.diag(side, -1))[1]
    basis = vectors[:, ::-1][:, :RANK]
    basis = basis * np.where(basis[size // 2] < 0, -1.0, 1.0)
    weights = []
    for group in range(4):
        waves = waves_of(group, np.arange(64))
        angle = 2 * np.pi / total * ((np.arange(size)[:, None] - 1) * waves[None, :] % total)
        alpha, beta = basis.T @ np.cos(angle), basis.T @ np.sin(angle)
        if group:
            sign = np.where(np.arange(64) < 32, 1.0, -1.0)
            top, low = (alpha, beta), (sign * beta, -sign * alpha)
        else:
            use = np.where(np.arange(64) < 32, 1.0, 0.0)
            top, low = (use * alpha, use * beta), ((1 - use) * alpha, (1 - use) * beta)
        weights.append(np.concatenate([np.concatenate(top, axis=1), np.concatenate(low, axis=1)], axis=0))
    weights = np.round(np.stack(weights) * 2.0**22) / 2.0**22
    wide = np.zeros((RANK, WIDE))
    wide[:, : COLS + 1] = basis[1:].T
    wide[:, WIDE - 1] = basis[0]
    wide = np.round(wide * 2.0**26) / 2.0**26
    wide_h, wide_l = split_table(wide)
    own = np.where(np.arange(WIDE)[:, None] < COLS, 1, 0).astype(ml_dtypes.bfloat16)
    high, low = split_table(weights)
    back = np.concatenate([np.swapaxes(part, 1, 2) for part in (high, low, high)], axis=1)
    evaluate = np.concatenate([wide_h, wide_l, wide_h], axis=0)
    return np.concatenate(
        [
            evaluate[:, : WIDE // 2],
            evaluate[:, WIDE // 2 :],
            np.concatenate([wide_h.T * own, wide_l.T * own], axis=1),
            np.concatenate([high, low], axis=2).reshape(-1, 2 * RANK),
            back.reshape(-1, 2 * RANK),
        ],
        axis=0,
    )


ROOT = float(np.sqrt(0.5))


def over_lanes(y):
    s = [y[j] + y[j + 4] for j in range(4)]
    d = [y[j] - y[j + 4] for j in range(4)]
    even, odd = s[0] + s[2], s[1] + s[3]
    minus, plus = ROOT * (d[1] - d[3]), ROOT * (d[1] + d[3])
    return [
        (even + odd, even - odd),
        (d[0] + minus, -(d[2] + plus)),
        (s[0] - s[2], s[3] - s[1]),
        (d[0] - minus, d[2] - plus),
    ]


def to_lanes(pairs):
    (y0, y4), (u1, v1), (u2, v2), (u3, v3) = pairs
    even, odd = y0 + y4, y0 - y4
    s = [even + u2, odd - v2, even - u2, odd + v2]
    du, sv = ROOT * (u1 - u3), ROOT * (v1 + v3)
    d = [u1 + u3, du - sv, v3 - v1, -du - sv]
    return [s[j] + d[j] for j in range(4)] + [s[j] - d[j] for j in range(4)]


@functools.lru_cache(None)
def half_metric(bands):
    total = bands * ROWS
    rows = np.clip(np.arange(bands)[:, None] * ROWS - 8 + np.arange(32)[None, :], 0, total - 1)
    metric = np.minimum(1.0 / np.cos(np.pi * ((rows + 0.5) / total - 0.5)), metric_cap)
    table = np.broadcast_to((0.5 * metric).astype(np.float32)[:, :, None], (bands, 32, 128)).copy()
    forward = mode_factors()[FORWARD : FORWARD + WIDE].astype(np.float32)
    for row, col in enumerate((0, COLS - 1)):
        table[:, row] = forward[col, :RANK] + forward[col, RANK:]
    return table


def dot_cols(a, b):
    return lax.dot_general(a, b, (((1,), (0,)), ((), ())), preferred_element_type=F32)


def split(x):
    high = x.astype(BF16)
    return high, (x - high.astype(F32)).astype(BF16)


def to_modes(x, table):
    xh, xl = split(x)
    half = table.shape[1] // 2
    wide = dot_cols(xh, table[...])
    return wide[:, :half] + wide[:, half:] + dot_cols(xl, table[:, 0:half])


def from_modes(z, *tables):
    zh, zl = split(z)
    three = jnp.concatenate([zh, zh, zl], axis=1)
    return jnp.concatenate([dot_cols(three, table[...]) for table in tables], axis=1)


def roll(x, shift, axis):
    return pltpu.roll(x, shift % x.shape[axis], axis)


def roll_blocks(x, shift):
    return roll(x.reshape(x.shape[0] * x.shape[1], x.shape[2]), shift, 1).reshape(x.shape)


def fold(x):
    while x.shape[0] > 1:
        half = x.shape[0] // 2
        x = x[:half] + roll_blocks(x[half:], 2 * half)
    return x


def kernel(
    bands, spread, east, north, rs, cs, cut, metric, table_in, tan_out, diag_out,
    spread_v, winds_v, rs_v, cs_v, cut_s, hm, table,
    grid, halo_out, halo_in, ybuf, yr, cb, yc, zbuf, zr, eb, bz,
    tend, proj_p, proj_t, edge_t, edge_proj, adj, gy, tan_v, diag_v,
    in_sem, halo_send, halo_recv, y_send, y_recv, c_send, c_recv, z_send, z_recv, b_send, b_recv, out_sem,
):
    b = lax.axis_index("lat")
    i = lax.axis_index("lon")
    caps = POLAR // ROWS
    is_north = b == 0
    is_south = b == bands - 1
    polar = jnp.logical_or(b < caps, b >= bands - caps)
    above_polar = jnp.logical_or(b <= caps, is_south)
    below_polar = jnp.logical_or(b >= bands - caps - 1, is_north)
    near_polar = jnp.logical_or(above_polar, below_polar)
    across = lax.rem(i + LANES // 2, LANES)
    west = lax.rem(i + LANES - 1, LANES)
    east_lane = lax.rem(i + 1, LANES)
    nb = jnp.where(is_north, 0, b - 1)
    nl = jnp.where(is_north, across, i)
    sb = jnp.where(is_south, bands - 1, b + 1)
    sl = jnp.where(is_south, across, i)
    slot_n = jnp.where(is_north, 0, 1)
    slot_s = jnp.where(is_south, 1, 0)
    own_half = lax.rem(i, 2)
    edge_over = jnp.where(own_half == 0, is_north, is_south)
    over_pole = (is_north, is_south)

    def plus(lane, d):
        return lax.rem(lane + d, LANES)

    load_spread = pltpu.make_async_copy(spread, spread_v, in_sem.at[0])
    load_rows = pltpu.make_async_copy(rs, rs_v, in_sem.at[1])
    load_cols = pltpu.make_async_copy(cs, cs_v, in_sem.at[2])
    load_metric = pltpu.make_async_copy(metric.at[b], hm, in_sem.at[4])
    load_cut = pltpu.make_async_copy(cut, cut_s, in_sem.at[5])
    load_table = pltpu.make_async_copy(table_in, table, in_sem.at[6])
    load_part = pltpu.make_async_copy(
        table_in.at[EVALUATE:FORWARD], table.at[EVALUATE:FORWARD], in_sem.at[6]
    )
    load_spread.start()
    load_rows.start()
    load_cols.start()
    pltpu.make_async_copy(east, winds_v.at[0], in_sem.at[3]).start()
    pltpu.make_async_copy(north, winds_v.at[1], in_sem.at[3]).start()
    load_metric.start()

    barrier = pltpu.get_barrier_semaphore()

    def greet(lat, lon):
        pl.semaphore_signal(barrier, inc=1, device_id=(lat, lon), device_id_type=MESH)

    greet(nb, nl)
    greet(sb, sl)
    greet(b, west)
    greet(b, east_lane)

    @pl.when(polar)
    def _():
        @pl.loop(2, LANES - 1)
        def _(d):
            greet(b, plus(i, d))

        load_table.start()
        load_cut.start()

    @pl.when(jnp.logical_and(near_polar, jnp.logical_not(polar)))
    def _():
        load_part.start()

    load_rows.wait()
    load_cols.wait()
    load_spread.wait()
    grid[:, 8:24, 384:512] = jnp.zeros((PAIRS + 2 * LEV, ROWS, 128), F32)
    row_part = jnp.concatenate([rs_v[f] for f in range(FIELDS)], axis=0)
    row_part = (2 * row_part - 1).astype(F32).T
    for f in range(FIELDS):
        col_part = (2 * cs_v[f] - 1).astype(F32)
        for l in range(LEV):
            n = f * LEV + l
            grid[n, 8:24, 0:COLS] = spread_v[f, l] * (row_part[:, n : n + 1] * col_part[l : l + 1, :])
    pltpu.make_async_copy(winds_v, winds_v, in_sem.at[3]).wait()
    for w in range(2):
        for l in range(LEV):
            grid[PAIRS + w * LEV + l, 8:24, 0:COLS] = winds_v[w, l]

    for s, (near, far) in enumerate(((8, 9), (23, 22))):
        for t in range(4):
            lanes = slice(128 * t, 128 * t + 128)
            halo_out[NEAR + 4 * s + t] = grid[0:PAIRS, near, lanes]
            halo_out[REST + 7 * s + t] = grid[0:PAIRS, far, lanes]
            halo_out[REST + 7 * s + 4 + t // 2, 8 * (t % 2) : 8 * (t % 2) + 8, :] = grid[
                PAIRS : PAIRS + 2 * LEV, near, lanes
            ]
    lane128 = lax.broadcasted_iota(jnp.int32, (1, 1, 128), 2)
    for s, (start, shift) in enumerate(((0, 0), (384, COLS - 2 - 384))):
        tile = grid[:, 8:24, start : start + 128]
        tile = jnp.where(jnp.logical_and(lane128 >= shift, lane128 < shift + 2), tile, 0.0)
        packed = fold(tile[:PAIRS]) + roll_blocks(fold(tile[PAIRS:]), 2 * PAIRS)
        halo_out[SIDES + s] = roll_blocks(packed, -shift)[0]

    def values(q, x):
        y = to_modes(x.reshape(PAIRS * ROWS, WIDE), table.at[FORWARD:TO_COEFS])
        y = y.reshape(FIELDS, LEV, 2, 8, RANK)
        for f in range(FIELDS):
            for h in range(2):
                for l in range(LEV):
                    ybuf[2 * f + h, q, l] = y[f, l, h]

    @pl.when(polar)
    def _():
        load_table.wait()
        values(0, grid[0:PAIRS, 8:24, :])

    pl.semaphore_wait(barrier, 4 + jnp.where(polar, LANES - 3, 0))

    def remote(src, dst, send, recv, lat, lon):
        return pltpu.make_async_remote_copy(
            src_ref=src, dst_ref=dst, send_sem=send, recv_sem=recv, device_id=(lat, lon), device_id_type=MESH
        )

    def halo_copy(start, count, to, which, lat, lon):
        return remote(
            halo_out.at[start : start + count], halo_in.at[pl.ds(to, count)], halo_send, halo_recv.at[which], lat, lon
        )

    def halo_arrival(start, stop, which):
        return remote(
            halo_out.at[start:stop], halo_in.at[start:stop], halo_send, halo_recv.at[which], b, west
        )

    halo_copy(NEAR, 4, NEAR + 4 * slot_n, 0, nb, nl).start()
    halo_copy(NEAR + 4, 4, NEAR + 4 * slot_s, 0, sb, sl).start()
    halo_copy(SIDES, 1, SIDES + 1, 0, b, west).start()
    halo_copy(SIDES + 1, 1, SIDES, 0, b, east_lane).start()

    def y_copy(o):
        return remote(ybuf.at[o], yr.at[i], y_send, y_recv, b, o)

    others = pl.ds(0, LANES - 1)

    def all_y():
        return remote(ybuf.at[others], yr.at[others], y_send, y_recv, b, west)

    def send_values():
        @pl.loop(1, LANES)
        def _(d):
            y_copy(plus(i, d)).start()

        yr[i] = ybuf[i]

    def c_copy(o):
        return remote(cb.at[o], yc.at[i], c_send, c_recv, b, o)

    def all_c():
        return remote(cb.at[others], yc.at[others], c_send, c_recv, b, west)

    def z_copy(q, j):
        return remote(zbuf.at[q, j], zr.at[q, i], z_send.at[q], z_recv.at[q], b, j)

    def all_z(q):
        return remote(zbuf.at[q, others], zr.at[q, others], z_send.at[q], z_recv.at[q], b, west)

    def own_rows(q):
        row = lax.broadcasted_iota(jnp.int32, (8, 128), 0)
        cutoff = jnp.zeros((8, 128), jnp.int32)
        for r in range(8):
            cutoff = jnp.where(row == r, cut_s[8 * own_half + r], cutoff)

        if q == 0:
            all_y().wait_recv()
        else:
            all_c().wait_recv()

        lanes = []
        for j in range(LANES):
            y = yr[j, q]
            if q == 1:
                ends = pltpu.roll(yc[j, 8:16, :], lax.rem(128 - 2 * LEV * (i // 2), 128), 1)
                edge = jnp.where(row == 7 * own_half, 1.0, 0.0)
                y = jnp.concatenate(
                    [
                        y[l]
                        + ends[:, 2 * l : 2 * l + 1] * hm[0:1, :]
                        + ends[:, 2 * l + 1 : 2 * l + 2] * hm[1:2, :]
                        + edge * yc[j, l : l + 1, :]
                        for l in range(LEV)
                    ],
                    axis=0,
                )
            lanes.append(y.reshape(LEV * 8, RANK))
        pairs = []
        over = over_lanes(lanes)
        for group, pair in enumerate(over):
            coef = to_modes(
                jnp.concatenate(pair, axis=1), table.at[TO_COEFS + 256 * group : TO_COEFS + 256 * (group + 1)]
            )
            wave = waves_of(group, lax.broadcasted_iota(jnp.int32, (8, 128), 1))
            keep = jnp.where(wave > cutoff, 2.0 / (COLS * LANES), 0.0)
            back = from_modes(
                coef * jnp.concatenate([keep] * LEV, axis=0),
                table.at[FROM_COEFS + 384 * group : FROM_COEFS + 384 * (group + 1)],
            )
            pairs.append((back[:, :RANK], back[:, RANK:]))
        for j, z in enumerate(to_lanes(pairs)):
            z = z.reshape(LEV, 8, RANK)
            zbuf[q, j] = z
            eb[j, LEV * q : LEV * (q + 1), :] = jnp.where(own_half == 0, z[:, 0, :], z[:, 7, :])

        @pl.loop(1, LANES)
        def _(d):
            z_copy(q, plus(i, d)).start()

        zr[q, i] = zbuf[q, i]

    def edge_sends():
        slot = jnp.where(own_half == 0, slot_n, slot_s)
        lat = jnp.where(own_half == 0, nb, sb)

        @pl.loop(0, LANES)
        def _(d):
            j = plus(i, d)
            lon = jnp.where(edge_over, plus(j, LANES // 2), j)
            here = jnp.logical_and(edge_over, lon == i)

            @pl.when(jnp.logical_not(here))
            def _():
                remote(eb.at[j], bz.at[slot, i // 2], b_send, b_recv.at[slot], lat, lon).start()

            @pl.when(here)
            def _():
                pltpu.make_async_copy(eb.at[j], bz.at[slot, i // 2], b_recv.at[slot]).start()

    def evaluate(z):
        return from_modes(z, table.at[0:384], table.at[384:768])

    def project(q, out):
        all_z(q).wait_recv()
        z = jnp.concatenate(
            [zr[q, 2 * f + h, l] for f in range(FIELDS) for l in range(LEV) for h in range(2)], axis=0
        )
        out[...] = evaluate(z).reshape(PAIRS, ROWS, WIDE)

    def tendency_rows(h):
        @pl.loop(0, LEV)
        def _(l):
            lo = jnp.maximum(l - 1, 0)
            hi = jnp.minimum(l + 1, LEV - 1)
            half = jnp.concatenate([hm[h : h + 8, :]] * 4, axis=1)
            ew = grid[PAIRS + l, h : h + 8, :]
            nw = grid[PAIRS + LEV + l, h : h + 8, :]
            along_x, along_y = [], []
            for f in range(FIELDS):
                mid = grid[f * LEV + l, h : h + 8, :]
                along_x.append(half * (roll(mid, -1, 1) - roll(mid, 1, 1)))
                along_y.append(0.5 * (grid[f * LEV + l, h + 1 : h + 9, :] - grid[f * LEV + l, h - 1 : h + 7, :]))
            linked = (along_x[2], along_y[2], along_x[0] + along_y[1], None)
            for f in range(FIELDS):
                mid = grid[f * LEV + l, h : h + 8, :]
                mixed = grid[f * LEV + lo, h : h + 8, :] + grid[f * LEV + hi, h : h + 8, :] - 2.0 * mid
                t = -(ew * along_x[f] + nw * along_y[f]) + mixing * mixed
                if linked[f] is not None:
                    t = t - coupling * linked[f]
                tend[f * LEV + l, h - 8 : h, :] = t

    load_metric.wait()

    @pl.when(polar)
    def _():
        grid[0:PAIRS, 7:8, :] = jnp.zeros((PAIRS, 1, WIDE), F32)
        grid[0:PAIRS, 24:25, :] = jnp.zeros((PAIRS, 1, WIDE), F32)
        for part in range(2):
            tendency_rows(8 + 8 * part)
        values(1, tend[...])
        send_values()

    halo_arrival(NEAR, REST, 0).wait_recv()
    lane2 = lax.broadcasted_iota(jnp.int32, (1, 128), 1)
    row16 = lax.broadcasted_iota(jnp.int32, (PAIRS, 1), 0)
    is_v = jnp.logical_and(row16 >= LEV, row16 < 2 * LEV)
    is_temp = jnp.logical_and(row16 >= 2 * LEV, row16 < 3 * LEV)

    def flip(s, minus):
        sign = jnp.where(row16 < 2 * LEV, -1.0, 1.0) * minus
        return jnp.where(over_pole[s], sign, 1.0)

    def row_link(x):
        return jnp.where(is_v, roll(x, -LEV, 0), jnp.where(is_temp, roll(x, LEV, 0), 0.0))

    def wind(buffer, s, w):
        base = REST + 7 * s + 4
        rows = [buffer[base + t // 2, 8 * (t % 2) + LEV * w : 8 * (t % 2) + LEV * (w + 1), :] for t in range(4)]
        return jnp.concatenate([jnp.concatenate(rows, axis=1)] * FIELDS, axis=0)

    def row_of(buffer, start):
        return jnp.concatenate([buffer[start + t] for t in range(4)], axis=1)

    @pl.when(polar)
    def _():
        added = []
        for s, sign in ((0, 0.5), (1, -0.5)):
            ghost = flip(s, 1.0) * row_of(halo_in, NEAR + 4 * s)
            added.append(sign * (wind(halo_out, s, 1) * ghost + coupling * row_link(ghost)))
        y = to_modes(jnp.concatenate(added, axis=0), table.at[FORWARD:TO_COEFS])
        for s in range(2):
            for f in range(FIELDS):
                cb[2 * f + s, 0:LEV, :] = y[(s * FIELDS + f) * LEV : (s * FIELDS + f + 1) * LEV, :]
        ends = []
        for side, sign in ((0, -1.0), (1, 1.0)):
            came = halo_in[SIDES + side]
            along_x = (sign * hm[8:24, :]) * (roll(came, -1, 1) if side == 0 else came)
            mine = jnp.where(
                jnp.logical_and(lane2 >= 2 * PAIRS, lane2 < 2 * (PAIRS + LEV)), halo_out[SIDES + side], 0.0
            )
            ew = sum(roll(mine, 2 * LEV * f - 2 * PAIRS - side, 1) for f in range(FIELDS))
            linked = jnp.where(
                lane2 < 2 * LEV,
                roll(along_x, -4 * LEV, 1),
                jnp.where(
                    jnp.logical_and(lane2 >= 4 * LEV, lane2 < 6 * LEV), roll(along_x, 4 * LEV, 1), 0.0
                ),
            )
            ends.append(-ew * along_x - coupling * linked)
        ends = jnp.where(lax.rem(lane2, 2) == 0, ends[0], roll(ends[1], 1, 1))
        for f in range(FIELDS):
            for h in range(2):
                cb[2 * f + h, 8:16, :] = ends[8 * h : 8 * h + 8, :]

        @pl.loop(1, LANES)
        def _(d):
            c_copy(plus(i, d)).start()

        yc[i] = cb[i]

    from_west = roll(halo_in[SIDES], 126, 1)
    from_east = roll(halo_in[SIDES + 1], COLS - 384, 1)
    both = jnp.where(jnp.logical_and(lane2 >= 66, lane2 < 114), from_east, from_west)[None]
    for width in (2, 4, 8):
        both = jnp.concatenate([both, roll_blocks(both, -width)], axis=0)
    both = jnp.concatenate([both, roll_blocks(both, -16), roll_blocks(both, -32)], axis=0)
    in_halo = jnp.logical_or(jnp.logical_and(lane128 >= 66, lane128 < 68), lane128 >= 126)
    grid[:, 8:24, 384:512] = jnp.where(in_halo, both, grid[:, 8:24, 384:512])
    for s, near in enumerate((8, 23)):
        halo_out[REST + 7 * s + 6] = grid[0:PAIRS, near, 384:512]
    halo_copy(REST, 7, REST + 7 * slot_n, 1, nb, nl).start()
    halo_copy(REST + 7, 7, REST + 7 * slot_s, 1, sb, sl).start()

    @pl.when(polar)
    def _():
        load_cut.wait()
        own_rows(0)
        own_rows(1)
        edge_sends()

    halo_arrival(REST, BLOCKS, 1).wait_recv()
    edge_row = (7, 24)
    edge_probe = []
    for s in range(2):
        edge_probe.append(
            jnp.concatenate([halo_in[NEAR + 4 * s + t] for t in range(3)] + [halo_in[REST + 7 * s + 6]], axis=1)
        )
        grid[0:PAIRS, edge_row[s], :] = flip(s, 1.0) * edge_probe[s]

    for part in range(2):
        tendency_rows(8 + 8 * part)

    for s, inward in ((0, 1.0), (1, -1.0)):
        mid = edge_probe[s]
        half = jnp.concatenate([hm[edge_row[s] : edge_row[s] + 1, :]] * 4, axis=1)
        along_x = half * (roll(mid, -1, 1) - roll(mid, 1, 1))
        turn = jnp.where(over_pole[s], -0.5 * inward, 0.5 * inward)
        along_y = turn * (flip(s, 1.0) * row_of(halo_out, NEAR + 4 * s) - row_of(halo_in, REST + 7 * s))
        linked = jnp.where(row16 < LEV, roll(along_x, -2 * LEV, 0), row_link(along_y))
        linked = linked + jnp.where(is_temp, roll(along_x, 2 * LEV, 0), 0.0)
        up = jnp.where(lax.rem(row16, LEV) == 0, mid, roll(mid, 1, 0))
        down = jnp.where(lax.rem(row16, LEV) == LEV - 1, mid, roll(mid, -1, 0))
        t = -(wind(halo_in, s, 0) * along_x + wind(halo_in, s, 1) * along_y) - coupling * linked
        edge_t[s] = t + mixing * (up + down - 2.0 * mid)

    @pl.when(polar)
    def _():
        project(0, proj_p)
        project(1, proj_t)

    @pl.when(jnp.logical_not(polar))
    def _():
        proj_p[...] = jnp.zeros(proj_p.shape, F32)
        proj_t[...] = jnp.zeros(proj_t.shape, F32)

    def row_weights(a, nw):
        return (
            -nw * a[0],
            -nw * a[1] - coupling * a[2],
            -nw * a[2] - coupling * a[1],
            -nw * a[3],
        )

    @pl.loop(0, LEV)
    def _(l):
        for h in (8, 16):
            nw = grid[PAIRS + LEV + l, h : h + 8, :]
            a = []
            for f in range(FIELDS):
                n = f * LEV + l
                change = time_step * (tend[n, h - 8 : h, :] - proj_t[n, h - 8 : h, :])
                tend[n, h - 8 : h, :] = change
                tangent = grid[n, h : h + 8, :] + change
                tan_v[f, l, h - 8 : h, :] = tangent[:, :COLS]
                a.append(tangent - proj_p[n, h - 8 : h, :])
                adj[n, h - 8 : h, :] = a[f]
            for f, weight in enumerate(row_weights(a, nw)):
                gy[f * LEV + l, h : h + 8, :] = weight

    tan_copy = pltpu.make_async_copy(tan_v, tan_out, out_sem.at[0])
    tan_copy.start()

    for s, wanted in enumerate((above_polar, below_polar)):
        @pl.when(wanted)
        def _():
            remote(bz.at[s], bz.at[s], b_send, b_recv.at[s], nb, nl).wait_recv()

        @pl.when(jnp.logical_not(wanted))
        def _():
            bz[s] = jnp.zeros((FIELDS, 2 * LEV, RANK), F32)

    @pl.when(jnp.logical_and(near_polar, jnp.logical_not(polar)))
    def _():
        load_part.wait()

    @pl.when(near_polar)
    def _():
        parts = [
            bz[s, f, LEV * q : LEV * (q + 1), :] for s in range(2) for q in range(2) for f in range(FIELDS)
        ]
        edge_proj[...] = evaluate(jnp.concatenate(parts, axis=0))

    @pl.when(jnp.logical_not(near_polar))
    def _():
        edge_proj[...] = jnp.zeros(edge_proj.shape, F32)

    for s in range(2):
        base = 2 * PAIRS * s
        a = (
            edge_probe[s]
            + time_step * (edge_t[s] - edge_proj[base + PAIRS : base + 2 * PAIRS, :])
            - edge_proj[base : base + PAIRS, :]
        )
        weight = -wind(halo_in, s, 1) * a - coupling * row_link(a)
        gy[0:PAIRS, edge_row[s], :] = flip(s, -1.0) * weight

    @pl.loop(0, LEV)
    def _(l):
        lo = jnp.maximum(l - 1, 0)
        hi = jnp.minimum(l + 1, LEV - 1)
        for h in (8, 16):
            rows = slice(h - 8, h)
            half = jnp.concatenate([hm[h : h + 8, :]] * 4, axis=1)
            ew = grid[PAIRS + l, h : h + 8, :]
            a = [adj[f * LEV + l, rows, :] for f in range(FIELDS)]
            col_weights = (
                -ew * a[0] - coupling * a[2],
                -ew * a[1],
                -ew * a[2] - coupling * a[0],
                -ew * a[3],
            )
            for f in range(FIELDS):
                n = f * LEV + l
                back = half * (roll(col_weights[f], 1, 1) - roll(col_weights[f], -1, 1))
                back = back + 0.5 * (gy[n, h - 1 : h + 7, :] - gy[n, h + 1 : h + 9, :])
                back = back + mixing * (adj[f * LEV + lo, rows, :] + adj[f * LEV + hi, rows, :] - 2.0 * a[f])
                diag = grid[n, h : h + 8, :] * (tend[n, rows, :] + time_step * back)
                diag_v[f, l, rows, :] = diag[:, :COLS]

    diag_copy = pltpu.make_async_copy(diag_v, diag_out, out_sem.at[1])
    diag_copy.start()

    halo_arrival(0, BLOCKS, 0).wait_send()

    @pl.when(polar)
    def _():
        all_y().wait_send()
        all_c().wait_send()
        for q in range(2):
            all_z(q).wait_send()

        @pl.when(edge_over)
        def _():
            remote(eb.at[others], eb.at[others], b_send, b_recv.at[0], b, west).wait_send()

        @pl.when(jnp.logical_not(edge_over))
        def _():
            remote(eb, eb, b_send, b_recv.at[0], b, west).wait_send()

    tan_copy.wait()
    diag_copy.wait()


def hand_out(tan_in, diag_in, tan_out, diag_out, held, in_sem, out_sem):
    arrive = [pltpu.make_async_copy(src, held.at[n], in_sem.at[n]) for n, src in enumerate((tan_in, diag_in))]
    leave = [pltpu.make_async_copy(held.at[n], dst, out_sem.at[n]) for n, dst in enumerate((tan_out, diag_out))]
    for copy in arrive:
        copy.start()
    for copy, onward in zip(arrive, leave):
        copy.wait()
        onward.start()
    for onward in leave:
        onward.wait()


def per_device(bands, row_signs, col_signs, spread, east_wind, north_wind, cutoffs):
    any_spec = pl.BlockSpec(memory_space=pl.ANY)
    out = jax.ShapeDtypeStruct((FIELDS, LEV, ROWS, COLS), F32)
    tables = [jnp.asarray(half_metric(bands)), jnp.asarray(mode_factors())]
    vmem = pltpu.VMEM
    dma = pltpu.SemaphoreType.DMA
    results = pl.pallas_call(
        functools.partial(kernel, bands),
        out_shape=(out, out),
        in_specs=[any_spec] * 8,
        out_specs=(any_spec, any_spec),
        scratch_shapes=[
            vmem((FIELDS, LEV, ROWS, COLS), F32),
            vmem((2, LEV, ROWS, COLS), F32),
            vmem((FIELDS, LEV, ROWS), jnp.int32),
            vmem((FIELDS, LEV, COLS), jnp.int32),
            pltpu.SMEM((ROWS,), jnp.int32),
            vmem((32, 128), F32),
            vmem((TABLE_ROWS, 2 * RANK), BF16),
            vmem((PAIRS + 2 * LEV, 32, WIDE), F32),
            vmem((BLOCKS, 16, 128), F32),
            vmem((BLOCKS, 16, 128), F32),
            vmem((LANES, 2, LEV, 8, RANK), F32),
            vmem((LANES, 2, LEV, 8, RANK), F32),
            vmem((LANES, 16, RANK), F32),
            vmem((LANES, 16, RANK), F32),
            vmem((2, LANES, LEV, 8, RANK), F32),
            vmem((2, LANES, LEV, 8, RANK), F32),
            vmem((LANES, 2 * LEV, RANK), F32),
            vmem((2, FIELDS, 2 * LEV, RANK), F32),
            vmem((PAIRS, ROWS, WIDE), F32),
            vmem((PAIRS, ROWS, WIDE), F32),
            vmem((PAIRS, ROWS, WIDE), F32),
            vmem((2, PAIRS, WIDE), F32),
            vmem((4 * PAIRS, WIDE), F32),
            vmem((PAIRS, ROWS, WIDE), F32),
            vmem((PAIRS, 32, WIDE), F32),
            vmem((FIELDS, LEV, ROWS, COLS), F32),
            vmem((FIELDS, LEV, ROWS, COLS), F32),
            dma((7,)),
            dma,
            dma((2,)),
            dma,
            dma,
            dma,
            dma,
            dma((2,)),
            dma((2,)),
            dma,
            dma((2,)),
            dma((2,)),
        ],
        compiler_params=pltpu.CompilerParams(
            collective_id=0, has_side_effects=True, vmem_limit_bytes=64 * 2**20
        ),
        cost_estimate=pl.CostEstimate(flops=10**9, bytes_accessed=4 * 10**6, transcendentals=0),
    )(spread, east_wind, north_wind, row_signs, col_signs, cutoffs, *tables)
    return pl.pallas_call(
        hand_out,
        out_shape=(out, out),
        in_specs=[any_spec] * 2,
        out_specs=(any_spec, any_spec),
        scratch_shapes=[vmem((2, FIELDS, LEV, ROWS, COLS), F32), dma((2,)), dma((2,))],
        compiler_params=pltpu.CompilerParams(vmem_limit_bytes=64 * 2**20),
    )(*results)


def solution(mesh):
    return jax.shard_map(
        functools.partial(per_device, mesh.shape["lat"]),
        mesh=mesh,
        in_specs=(
            P(None, None, "lat"),
            P(None, None, "lon"),
            P(None, None, "lat", "lon"),
            P(None, "lat", "lon"),
            P(None, "lat", "lon"),
            P("lat"),
        ),
        out_specs=(P(None, None, "lat", "lon"), P(None, None, "lat", "lon")),
        check_vma=False,
    )
```

```python
import functools

import jax
import jax.numpy as jnp
import ml_dtypes
import numpy as np
from jax import lax
from jax.experimental import pallas as pl
from jax.experimental.pallas import tpu as pltpu
from jax.sharding import PartitionSpec as P

KTOP = 256
POLAR = 32
RANK = 128
ROWS = 16
COLS = 450
WIDE = 512
LANES = 8
FIELDS = 4
LEV = 4
PAIRS = FIELDS * LEV

time_step = 0.5
coupling = 0.5
mixing = 0.2
metric_cap = 4.0

FORWARD, EVALUATE, TO_COEFS, FROM_COEFS, TABLE_ROWS = 0, 512, 1280, 2304, 3840
NEAR, SIDES, REST, BLOCKS = 0, 8, 10, 24

MESH = pl.DeviceIdType.MESH
F32 = jnp.float32
BF16 = jnp.bfloat16


def split_table(table):
    high = table.astype(ml_dtypes.bfloat16)
    low = (table - high.astype(np.float64)).astype(ml_dtypes.bfloat16)
    return high, low


def waves_of(group, lane_index):
    place = lane_index % 64
    second = place // 32
    other = (8 - group) if group else 4
    residue = group + second * (other - group)
    return 8 * (place % 32) + residue + (8 * (1 - second) if group == 0 else 0)


@functools.lru_cache(None)
def mode_factors():
    total = COLS * LANES
    size = COLS + 2
    place = np.arange(size, dtype=np.float64)
    width = (KTOP + 0.5) / total
    diag = ((size - 1 - 2 * place) / 2) ** 2 * np.cos(2 * np.pi * width)
    side = place[1:] * (size - place[1:]) / 2
    vectors = np.linalg.eigh(np.diag(diag) + np.diag(side, 1) + np.diag(side, -1))[1]
    basis = vectors[:, ::-1][:, :RANK]
    basis = basis * np.where(basis[size // 2] < 0, -1.0, 1.0)
    weights = []
    for group in range(4):
        waves = waves_of(group, np.arange(64))
        angle = 2 * np.pi / total * ((np.arange(size)[:, None] - 1) * waves[None, :] % total)
        alpha, beta = basis.T @ np.cos(angle), basis.T @ np.sin(angle)
        if group:
            sign = np.where(np.arange(64) < 32, 1.0, -1.0)
            top, low = (alpha, beta), (sign * beta, -sign * alpha)
        else:
            use = np.where(np.arange(64) < 32, 1.0, 0.0)
            top, low = (use * alpha, use * beta), ((1 - use) * alpha, (1 - use) * beta)
        weights.append(np.concatenate([np.concatenate(top, axis=1), np.concatenate(low, axis=1)], axis=0))
    weights = np.round(np.stack(weights) * 2.0**22) / 2.0**22
    wide = np.zeros((RANK, WIDE))
    wide[:, : COLS + 1] = basis[1:].T
    wide[:, WIDE - 1] = basis[0]
    wide = np.round(wide * 2.0**26) / 2.0**26
    wide_h, wide_l = split_table(wide)
    own = np.where(np.arange(WIDE)[:, None] < COLS, 1, 0).astype(ml_dtypes.bfloat16)
    high, low = split_table(weights)
    back = np.concatenate([np.swapaxes(part, 1, 2) for part in (high, low, high)], axis=1)
    evaluate = np.concatenate([wide_h, wide_l, wide_h], axis=0)
    return np.concatenate(
        [
            np.concatenate([wide_h.T * own, wide_l.T * own], axis=1),
            evaluate[:, : WIDE // 2],
            evaluate[:, WIDE // 2 :],
            np.concatenate([high, low], axis=2).reshape(-1, 2 * RANK),
            back.reshape(-1, 2 * RANK),
        ],
        axis=0,
    )


ROOT = float(np.sqrt(0.5))


def over_lanes(y):
    s = [y[j] + y[j + 4] for j in range(4)]
    d = [y[j] - y[j + 4] for j in range(4)]
    even, odd = s[0] + s[2], s[1] + s[3]
    minus, plus = ROOT * (d[1] - d[3]), ROOT * (d[1] + d[3])
    return [
        (even + odd, even - odd),
        (d[0] + minus, -(d[2] + plus)),
        (s[0] - s[2], s[3] - s[1]),
        (d[0] - minus, d[2] - plus),
    ]


def to_lanes(pairs):
    (y0, y4), (u1, v1), (u2, v2), (u3, v3) = pairs
    even, odd = y0 + y4, y0 - y4
    s = [even + u2, odd - v2, even - u2, odd + v2]
    du, sv = ROOT * (u1 - u3), ROOT * (v1 + v3)
    d = [u1 + u3, du - sv, v3 - v1, -du - sv]
    return [s[j] + d[j] for j in range(4)] + [s[j] - d[j] for j in range(4)]


@functools.lru_cache(None)
def half_metric(bands):
    total = bands * ROWS
    rows = np.clip(np.arange(bands)[:, None] * ROWS - 8 + np.arange(32)[None, :], 0, total - 1)
    metric = np.minimum(1.0 / np.cos(np.pi * ((rows + 0.5) / total - 0.5)), metric_cap)
    table = np.broadcast_to((0.5 * metric).astype(np.float32)[:, :, None], (bands, 32, 128)).copy()
    forward = mode_factors()[FORWARD : FORWARD + WIDE].astype(np.float32)
    for row, col in enumerate((0, COLS - 1)):
        table[:, row] = forward[col, :RANK] + forward[col, RANK:]
    return table


def dot_cols(a, b):
    return lax.dot_general(a, b, (((1,), (0,)), ((), ())), preferred_element_type=F32)


def split(x):
    high = x.astype(BF16)
    return high, (x - high.astype(F32)).astype(BF16)


def to_modes(x, table):
    xh, xl = split(x)
    half = table.shape[1] // 2
    wide = dot_cols(xh, table[...])
    return wide[:, :half] + wide[:, half:] + dot_cols(xl, table[:, 0:half])


def from_modes(z, *tables):
    zh, zl = split(z)
    three = jnp.concatenate([zh, zh, zl], axis=1)
    return jnp.concatenate([dot_cols(three, table[...]) for table in tables], axis=1)


def roll(x, shift, axis):
    return pltpu.roll(x, shift % x.shape[axis], axis)


def roll_blocks(x, shift):
    return roll(x.reshape(x.shape[0] * x.shape[1], x.shape[2]), shift, 1).reshape(x.shape)


def fold(x):
    while x.shape[0] > 1:
        half = x.shape[0] // 2
        x = x[:half] + roll_blocks(x[half:], 2 * half)
    return x


def kernel(
    bands, spread, east, north, rs, cs, cut, metric, table_in, tan_out, diag_out,
    spread_v, winds_v, rs_v, cs_v, cut_s, hm, table,
    grid, halo_out, halo_in, ybuf, yr, cb, yc, zbuf, zr, eb, bz,
    tend, proj_p, proj_t, edge_t, edge_proj, adj, gy,
    in_sem, halo_send, halo_recv, y_send, y_recv, c_send, c_recv, z_send, z_recv, b_send, b_recv,
):
    b = lax.axis_index("lat")
    i = lax.axis_index("lon")
    caps = POLAR // ROWS
    is_north = b == 0
    is_south = b == bands - 1
    polar = jnp.logical_or(b < caps, b >= bands - caps)
    above_polar = jnp.logical_or(b <= caps, is_south)
    below_polar = jnp.logical_or(b >= bands - caps - 1, is_north)
    near_polar = jnp.logical_or(above_polar, below_polar)
    across = lax.rem(i + LANES // 2, LANES)
    west = lax.rem(i + LANES - 1, LANES)
    east_lane = lax.rem(i + 1, LANES)
    nb = jnp.where(is_north, 0, b - 1)
    nl = jnp.where(is_north, across, i)
    sb = jnp.where(is_south, bands - 1, b + 1)
    sl = jnp.where(is_south, across, i)
    slot_n = jnp.where(is_north, 0, 1)
    slot_s = jnp.where(is_south, 1, 0)
    own_half = lax.rem(i, 2)
    edge_over = jnp.where(own_half == 0, is_north, is_south)
    over_pole = (is_north, is_south)

    def plus(lane, d):
        return lax.rem(lane + d, LANES)

    load_spread = pltpu.make_async_copy(spread, spread_v, in_sem.at[0])
    load_rows = pltpu.make_async_copy(rs, rs_v, in_sem.at[1])
    load_cols = pltpu.make_async_copy(cs, cs_v, in_sem.at[2])
    load_metric = pltpu.make_async_copy(metric.at[b], hm, in_sem.at[4])
    load_cut = pltpu.make_async_copy(cut, cut_s, in_sem.at[5])

    def load_table(start, stop, sem):
        return pltpu.make_async_copy(table_in.at[start:stop], table.at[start:stop], in_sem.at[sem])

    load_forward = load_table(FORWARD, EVALUATE, 6)
    load_others = load_table(EVALUATE, TABLE_ROWS, 7)
    load_part = load_table(EVALUATE, TO_COEFS, 7)
    load_spread.start()
    load_rows.start()
    load_cols.start()
    pltpu.make_async_copy(east, winds_v.at[0], in_sem.at[3]).start()
    pltpu.make_async_copy(north, winds_v.at[1], in_sem.at[3]).start()
    load_metric.start()

    barrier = pltpu.get_barrier_semaphore()

    def greet(lat, lon):
        pl.semaphore_signal(barrier, inc=1, device_id=(lat, lon), device_id_type=MESH)

    greet(nb, nl)
    greet(sb, sl)
    greet(b, west)
    greet(b, east_lane)

    @pl.when(polar)
    def _():
        @pl.loop(2, LANES - 1)
        def _(d):
            greet(b, plus(i, d))

        load_forward.start()
        load_cut.start()
        load_others.start()

    @pl.when(jnp.logical_and(near_polar, jnp.logical_not(polar)))
    def _():
        load_part.start()

    load_rows.wait()
    load_cols.wait()
    load_spread.wait()
    grid[:, 8:24, 384:512] = jnp.zeros((PAIRS + 2 * LEV, ROWS, 128), F32)
    row_part = jnp.concatenate([rs_v[f] for f in range(FIELDS)], axis=0)
    row_part = (2 * row_part - 1).astype(F32).T
    for f in range(FIELDS):
        col_part = (2 * cs_v[f] - 1).astype(F32)
        for l in range(LEV):
            n = f * LEV + l
            grid[n, 8:24, 0:COLS] = spread_v[f, l] * (row_part[:, n : n + 1] * col_part[l : l + 1, :])
    pltpu.make_async_copy(winds_v, winds_v, in_sem.at[3]).wait()
    for w in range(2):
        for l in range(LEV):
            grid[PAIRS + w * LEV + l, 8:24, 0:COLS] = winds_v[w, l]

    for s, (near, far) in enumerate(((8, 9), (23, 22))):
        for t in range(4):
            lanes = slice(128 * t, 128 * t + 128)
            halo_out[NEAR + 4 * s + t] = grid[0:PAIRS, near, lanes]
            halo_out[REST + 7 * s + t] = grid[0:PAIRS, far, lanes]
            halo_out[REST + 7 * s + 4 + t // 2, 8 * (t % 2) : 8 * (t % 2) + 8, :] = grid[
                PAIRS : PAIRS + 2 * LEV, near, lanes
            ]
    lane128 = lax.broadcasted_iota(jnp.int32, (1, 1, 128), 2)
    for s, (start, shift) in enumerate(((0, 0), (384, COLS - 2 - 384))):
        tile = grid[:, 8:24, start : start + 128]
        tile = jnp.where(jnp.logical_and(lane128 >= shift, lane128 < shift + 2), tile, 0.0)
        packed = fold(tile[:PAIRS]) + roll_blocks(fold(tile[PAIRS:]), 2 * PAIRS)
        halo_out[SIDES + s] = roll_blocks(packed, -shift)[0]

    def values(q, x):
        y = to_modes(x.reshape(PAIRS * ROWS, WIDE), table.at[FORWARD:EVALUATE])
        y = y.reshape(FIELDS, LEV, 2, 8, RANK)
        for f in range(FIELDS):
            for h in range(2):
                for l in range(LEV):
                    ybuf[2 * f + h, q, l] = y[f, l, h]

    @pl.when(polar)
    def _():
        load_forward.wait()
        values(0, grid[0:PAIRS, 8:24, :])

    pl.semaphore_wait(barrier, 4 + jnp.where(polar, LANES - 3, 0))

    def remote(src, dst, send, recv, lat, lon):
        return pltpu.make_async_remote_copy(
            src_ref=src, dst_ref=dst, send_sem=send, recv_sem=recv, device_id=(lat, lon), device_id_type=MESH
        )

    def halo_copy(start, count, to, which, lat, lon):
        return remote(
            halo_out.at[start : start + count], halo_in.at[pl.ds(to, count)], halo_send, halo_recv.at[which], lat, lon
        )

    def halo_arrival(start, stop, which):
        return remote(
            halo_out.at[start:stop], halo_in.at[start:stop], halo_send, halo_recv.at[which], b, west
        )

    halo_copy(NEAR, 4, NEAR + 4 * slot_n, 0, nb, nl).start()
    halo_copy(NEAR + 4, 4, NEAR + 4 * slot_s, 0, sb, sl).start()
    halo_copy(SIDES, 1, SIDES + 1, 0, b, west).start()
    halo_copy(SIDES + 1, 1, SIDES, 0, b, east_lane).start()

    def y_copy(o):
        return remote(ybuf.at[o], yr.at[i], y_send, y_recv, b, o)

    others = pl.ds(0, LANES - 1)

    def all_y():
        return remote(ybuf.at[others], yr.at[others], y_send, y_recv, b, west)

    def send_values():
        @pl.loop(1, LANES)
        def _(d):
            y_copy(plus(i, d)).start()

        yr[i] = ybuf[i]

    def c_copy(o):
        return remote(cb.at[o], yc.at[i], c_send, c_recv, b, o)

    def all_c():
        return remote(cb.at[others], yc.at[others], c_send, c_recv, b, west)

    def z_copy(q, j):
        return remote(zbuf.at[q, j], zr.at[q, i], z_send.at[q], z_recv.at[q], b, j)

    def all_z(q):
        return remote(zbuf.at[q, others], zr.at[q, others], z_send.at[q], z_recv.at[q], b, west)

    def own_rows(q):
        row = lax.broadcasted_iota(jnp.int32, (8, 128), 0)
        cutoff = jnp.zeros((8, 128), jnp.int32)
        for r in range(8):
            cutoff = jnp.where(row == r, cut_s[8 * own_half + r], cutoff)

        if q == 0:
            all_y().wait_recv()
        else:
            all_c().wait_recv()

        lanes = []
        for j in range(LANES):
            y = yr[j, q]
            if q == 1:
                ends = pltpu.roll(yc[j, 8:16, :], lax.rem(128 - 2 * LEV * (i // 2), 128), 1)
                edge = jnp.where(row == 7 * own_half, 1.0, 0.0)
                y = jnp.concatenate(
                    [
                        y[l]
                        + ends[:, 2 * l : 2 * l + 1] * hm[0:1, :]
                        + ends[:, 2 * l + 1 : 2 * l + 2] * hm[1:2, :]
                        + edge * yc[j, l : l + 1, :]
                        for l in range(LEV)
                    ],
                    axis=0,
                )
            lanes.append(y.reshape(LEV * 8, RANK))
        pairs = []
        over = over_lanes(lanes)
        for group, pair in enumerate(over):
            coef = to_modes(
                jnp.concatenate(pair, axis=1), table.at[TO_COEFS + 256 * group : TO_COEFS + 256 * (group + 1)]
            )
            wave = waves_of(group, lax.broadcasted_iota(jnp.int32, (8, 128), 1))
            keep = jnp.where(wave > cutoff, 2.0 / (COLS * LANES), 0.0)
            back = from_modes(
                coef * jnp.concatenate([keep] * LEV, axis=0),
                table.at[FROM_COEFS + 384 * group : FROM_COEFS + 384 * (group + 1)],
            )
            pairs.append((back[:, :RANK], back[:, RANK:]))
        for j, z in enumerate(to_lanes(pairs)):
            z = z.reshape(LEV, 8, RANK)
            zbuf[q, j] = z
            eb[j, LEV * q : LEV * (q + 1), :] = jnp.where(own_half == 0, z[:, 0, :], z[:, 7, :])

        @pl.loop(1, LANES)
        def _(d):
            z_copy(q, plus(i, d)).start()

        zr[q, i] = zbuf[q, i]

    def edge_sends():
        slot = jnp.where(own_half == 0, slot_n, slot_s)
        lat = jnp.where(own_half == 0, nb, sb)

        @pl.loop(0, LANES)
        def _(d):
            j = plus(i, d)
            lon = jnp.where(edge_over, plus(j, LANES // 2), j)
            here = jnp.logical_and(edge_over, lon == i)

            @pl.when(jnp.logical_not(here))
            def _():
                remote(eb.at[j], bz.at[slot, i // 2], b_send, b_recv.at[slot], lat, lon).start()

            @pl.when(here)
            def _():
                pltpu.make_async_copy(eb.at[j], bz.at[slot, i // 2], b_recv.at[slot]).start()

    def evaluate(z):
        return from_modes(z, table.at[EVALUATE : EVALUATE + 384], table.at[EVALUATE + 384 : TO_COEFS])

    def project(q, out):
        all_z(q).wait_recv()
        z = jnp.concatenate(
            [zr[q, 2 * f + h, l] for f in range(FIELDS) for l in range(LEV) for h in range(2)], axis=0
        )
        out[...] = evaluate(z).reshape(PAIRS, ROWS, WIDE)

    def tendency_rows(h):
        @pl.loop(0, LEV)
        def _(l):
            lo = jnp.maximum(l - 1, 0)
            hi = jnp.minimum(l + 1, LEV - 1)
            half = jnp.concatenate([hm[h : h + 8, :]] * 4, axis=1)
            ew = grid[PAIRS + l, h : h + 8, :]
            nw = grid[PAIRS + LEV + l, h : h + 8, :]
            along_x, along_y = [], []
            for f in range(FIELDS):
                mid = grid[f * LEV + l, h : h + 8, :]
                along_x.append(half * (roll(mid, -1, 1) - roll(mid, 1, 1)))
                along_y.append(0.5 * (grid[f * LEV + l, h + 1 : h + 9, :] - grid[f * LEV + l, h - 1 : h + 7, :]))
            linked = (along_x[2], along_y[2], along_x[0] + along_y[1], None)
            for f in range(FIELDS):
                mid = grid[f * LEV + l, h : h + 8, :]
                mixed = grid[f * LEV + lo, h : h + 8, :] + grid[f * LEV + hi, h : h + 8, :] - 2.0 * mid
                t = -(ew * along_x[f] + nw * along_y[f]) + mixing * mixed
                if linked[f] is not None:
                    t = t - coupling * linked[f]
                tend[f * LEV + l, h - 8 : h, :] = t

    load_metric.wait()

    @pl.when(polar)
    def _():
        grid[0:PAIRS, 7:8, :] = jnp.zeros((PAIRS, 1, WIDE), F32)
        grid[0:PAIRS, 24:25, :] = jnp.zeros((PAIRS, 1, WIDE), F32)
        for part in range(2):
            tendency_rows(8 + 8 * part)
        values(1, tend[...])
        send_values()

    halo_arrival(NEAR, REST, 0).wait_recv()
    lane2 = lax.broadcasted_iota(jnp.int32, (1, 128), 1)
    row16 = lax.broadcasted_iota(jnp.int32, (PAIRS, 1), 0)
    is_v = jnp.logical_and(row16 >= LEV, row16 < 2 * LEV)
    is_temp = jnp.logical_and(row16 >= 2 * LEV, row16 < 3 * LEV)

    def flip(s, minus):
        sign = jnp.where(row16 < 2 * LEV, -1.0, 1.0) * minus
        return jnp.where(over_pole[s], sign, 1.0)

    def row_link(x):
        return jnp.where(is_v, roll(x, -LEV, 0), jnp.where(is_temp, roll(x, LEV, 0), 0.0))

    def wind(buffer, s, w):
        base = REST + 7 * s + 4
        rows = [buffer[base + t // 2, 8 * (t % 2) + LEV * w : 8 * (t % 2) + LEV * (w + 1), :] for t in range(4)]
        return jnp.concatenate([jnp.concatenate(rows, axis=1)] * FIELDS, axis=0)

    def row_of(buffer, start):
        return jnp.concatenate([buffer[start + t] for t in range(4)], axis=1)

    @pl.when(polar)
    def _():
        added = []
        for s, sign in ((0, 0.5), (1, -0.5)):
            ghost = flip(s, 1.0) * row_of(halo_in, NEAR + 4 * s)
            added.append(sign * (wind(halo_out, s, 1) * ghost + coupling * row_link(ghost)))
        y = to_modes(jnp.concatenate(added, axis=0), table.at[FORWARD:EVALUATE])
        for s in range(2):
            for f in range(FIELDS):
                cb[2 * f + s, 0:LEV, :] = y[(s * FIELDS + f) * LEV : (s * FIELDS + f + 1) * LEV, :]
        ends = []
        for side, sign in ((0, -1.0), (1, 1.0)):
            came = halo_in[SIDES + side]
            along_x = (sign * hm[8:24, :]) * (roll(came, -1, 1) if side == 0 else came)
            mine = jnp.where(
                jnp.logical_and(lane2 >= 2 * PAIRS, lane2 < 2 * (PAIRS + LEV)), halo_out[SIDES + side], 0.0
            )
            ew = sum(roll(mine, 2 * LEV * f - 2 * PAIRS - side, 1) for f in range(FIELDS))
            linked = jnp.where(
                lane2 < 2 * LEV,
                roll(along_x, -4 * LEV, 1),
                jnp.where(
                    jnp.logical_and(lane2 >= 4 * LEV, lane2 < 6 * LEV), roll(along_x, 4 * LEV, 1), 0.0
                ),
            )
            ends.append(-ew * along_x - coupling * linked)
        ends = jnp.where(lax.rem(lane2, 2) == 0, ends[0], roll(ends[1], 1, 1))
        for f in range(FIELDS):
            for h in range(2):
                cb[2 * f + h, 8:16, :] = ends[8 * h : 8 * h + 8, :]

        @pl.loop(1, LANES)
        def _(d):
            c_copy(plus(i, d)).start()

        yc[i] = cb[i]

    from_west = roll(halo_in[SIDES], 126, 1)
    from_east = roll(halo_in[SIDES + 1], COLS - 384, 1)
    both = jnp.where(jnp.logical_and(lane2 >= 66, lane2 < 114), from_east, from_west)[None]
    for width in (2, 4, 8):
        both = jnp.concatenate([both, roll_blocks(both, -width)], axis=0)
    both = jnp.concatenate([both, roll_blocks(both, -16), roll_blocks(both, -32)], axis=0)
    in_halo = jnp.logical_or(jnp.logical_and(lane128 >= 66, lane128 < 68), lane128 >= 126)
    grid[:, 8:24, 384:512] = jnp.where(in_halo, both, grid[:, 8:24, 384:512])
    for s, near in enumerate((8, 23)):
        halo_out[REST + 7 * s + 6] = grid[0:PAIRS, near, 384:512]
    halo_copy(REST, 7, REST + 7 * slot_n, 1, nb, nl).start()
    halo_copy(REST + 7, 7, REST + 7 * slot_s, 1, sb, sl).start()

    @pl.when(polar)
    def _():
        load_cut.wait()
        load_others.wait()
        own_rows(0)
        own_rows(1)
        edge_sends()

    halo_arrival(REST, BLOCKS, 1).wait_recv()
    edge_row = (7, 24)
    edge_probe = []
    for s in range(2):
        edge_probe.append(
            jnp.concatenate([halo_in[NEAR + 4 * s + t] for t in range(3)] + [halo_in[REST + 7 * s + 6]], axis=1)
        )
        grid[0:PAIRS, edge_row[s], :] = flip(s, 1.0) * edge_probe[s]

    for part in range(2):
        tendency_rows(8 + 8 * part)

    for s, inward in ((0, 1.0), (1, -1.0)):
        mid = edge_probe[s]
        half = jnp.concatenate([hm[edge_row[s] : edge_row[s] + 1, :]] * 4, axis=1)
        along_x = half * (roll(mid, -1, 1) - roll(mid, 1, 1))
        turn = jnp.where(over_pole[s], -0.5 * inward, 0.5 * inward)
        along_y = turn * (flip(s, 1.0) * row_of(halo_out, NEAR + 4 * s) - row_of(halo_in, REST + 7 * s))
        linked = jnp.where(row16 < LEV, roll(along_x, -2 * LEV, 0), row_link(along_y))
        linked = linked + jnp.where(is_temp, roll(along_x, 2 * LEV, 0), 0.0)
        up = jnp.where(lax.rem(row16, LEV) == 0, mid, roll(mid, 1, 0))
        down = jnp.where(lax.rem(row16, LEV) == LEV - 1, mid, roll(mid, -1, 0))
        t = -(wind(halo_in, s, 0) * along_x + wind(halo_in, s, 1) * along_y) - coupling * linked
        edge_t[s] = t + mixing * (up + down - 2.0 * mid)

    @pl.when(polar)
    def _():
        project(0, proj_p)
        project(1, proj_t)

    @pl.when(jnp.logical_not(polar))
    def _():
        proj_p[...] = jnp.zeros(proj_p.shape, F32)
        proj_t[...] = jnp.zeros(proj_t.shape, F32)

    def row_weights(a, nw):
        return (
            -nw * a[0],
            -nw * a[1] - coupling * a[2],
            -nw * a[2] - coupling * a[1],
            -nw * a[3],
        )

    @pl.loop(0, LEV)
    def _(l):
        for h in (8, 16):
            nw = grid[PAIRS + LEV + l, h : h + 8, :]
            a = []
            for f in range(FIELDS):
                n = f * LEV + l
                change = time_step * (tend[n, h - 8 : h, :] - proj_t[n, h - 8 : h, :])
                tend[n, h - 8 : h, :] = change
                tangent = grid[n, h : h + 8, :] + change
                tan_out[f, l, h - 8 : h, :] = tangent[:, :COLS]
                a.append(tangent - proj_p[n, h - 8 : h, :])
                adj[n, h - 8 : h, :] = a[f]
            for f, weight in enumerate(row_weights(a, nw)):
                gy[f * LEV + l, h : h + 8, :] = weight

    for s, wanted in enumerate((above_polar, below_polar)):
        @pl.when(wanted)
        def _():
            remote(bz.at[s], bz.at[s], b_send, b_recv.at[s], nb, nl).wait_recv()

        @pl.when(jnp.logical_not(wanted))
        def _():
            bz[s] = jnp.zeros((FIELDS, 2 * LEV, RANK), F32)

    @pl.when(jnp.logical_and(near_polar, jnp.logical_not(polar)))
    def _():
        load_part.wait()

    @pl.when(near_polar)
    def _():
        parts = [
            bz[s, f, LEV * q : LEV * (q + 1), :] for s in range(2) for q in range(2) for f in range(FIELDS)
        ]
        edge_proj[...] = evaluate(jnp.concatenate(parts, axis=0))

    @pl.when(jnp.logical_not(near_polar))
    def _():
        edge_proj[...] = jnp.zeros(edge_proj.shape, F32)

    for s in range(2):
        base = 2 * PAIRS * s
        a = (
            edge_probe[s]
            + time_step * (edge_t[s] - edge_proj[base + PAIRS : base + 2 * PAIRS, :])
            - edge_proj[base : base + PAIRS, :]
        )
        weight = -wind(halo_in, s, 1) * a - coupling * row_link(a)
        gy[0:PAIRS, edge_row[s], :] = flip(s, -1.0) * weight

    @pl.loop(0, LEV)
    def _(l):
        lo = jnp.maximum(l - 1, 0)
        hi = jnp.minimum(l + 1, LEV - 1)
        for h in (8, 16):
            rows = slice(h - 8, h)
            half = jnp.concatenate([hm[h : h + 8, :]] * 4, axis=1)
            ew = grid[PAIRS + l, h : h + 8, :]
            a = [adj[f * LEV + l, rows, :] for f in range(FIELDS)]
            col_weights = (
                -ew * a[0] - coupling * a[2],
                -ew * a[1],
                -ew * a[2] - coupling * a[0],
                -ew * a[3],
            )
            for f in range(FIELDS):
                n = f * LEV + l
                back = half * (roll(col_weights[f], 1, 1) - roll(col_weights[f], -1, 1))
                back = back + 0.5 * (gy[n, h - 1 : h + 7, :] - gy[n, h + 1 : h + 9, :])
                back = back + mixing * (adj[f * LEV + lo, rows, :] + adj[f * LEV + hi, rows, :] - 2.0 * a[f])
                diag = grid[n, h : h + 8, :] * (tend[n, rows, :] + time_step * back)
                diag_out[f, l, rows, :] = diag[:, :COLS]

    halo_arrival(0, BLOCKS, 0).wait_send()

    @pl.when(polar)
    def _():
        all_y().wait_send()
        all_c().wait_send()
        for q in range(2):
            all_z(q).wait_send()

        @pl.when(edge_over)
        def _():
            remote(eb.at[others], eb.at[others], b_send, b_recv.at[0], b, west).wait_send()

        @pl.when(jnp.logical_not(edge_over))
        def _():
            remote(eb, eb, b_send, b_recv.at[0], b, west).wait_send()


def hand_out(tan_in, diag_in, tan_out, diag_out, sem):
    copies = [
        pltpu.make_async_copy(src, dst, sem.at[n])
        for n, (src, dst) in enumerate(((tan_in, tan_out), (diag_in, diag_out)))
    ]
    for copy in copies:
        copy.start()
    for copy in copies:
        copy.wait()


def per_device(bands, row_signs, col_signs, spread, east_wind, north_wind, cutoffs):
    any_spec = pl.BlockSpec(memory_space=pl.ANY)
    out = jax.ShapeDtypeStruct((FIELDS, LEV, ROWS, COLS), F32)
    tables = [jnp.asarray(half_metric(bands)), jnp.asarray(mode_factors())]
    operands = (spread, east_wind, north_wind, row_signs, col_signs, cutoffs, *tables)
    vmem = pltpu.VMEM
    dma = pltpu.SemaphoreType.DMA
    held = pltpu.VMEM(out.shape, F32)
    results = pl.pallas_call(
        functools.partial(kernel, bands),
        out_shape=(held, held),
        in_specs=[any_spec] * 8,
        out_specs=(pl.BlockSpec(memory_space=pltpu.VMEM),) * 2,
        scratch_shapes=[
            vmem((FIELDS, LEV, ROWS, COLS), F32),
            vmem((2, LEV, ROWS, COLS), F32),
            vmem((FIELDS, LEV, ROWS), jnp.int32),
            vmem((FIELDS, LEV, COLS), jnp.int32),
            pltpu.SMEM((ROWS,), jnp.int32),
            vmem((32, 128), F32),
            vmem((TABLE_ROWS, 2 * RANK), BF16),
            vmem((PAIRS + 2 * LEV, 32, WIDE), F32),
            vmem((BLOCKS, 16, 128), F32),
            vmem((BLOCKS, 16, 128), F32),
            vmem((LANES, 2, LEV, 8, RANK), F32),
            vmem((LANES, 2, LEV, 8, RANK), F32),
            vmem((LANES, 16, RANK), F32),
            vmem((LANES, 16, RANK), F32),
            vmem((2, LANES, LEV, 8, RANK), F32),
            vmem((2, LANES, LEV, 8, RANK), F32),
            vmem((LANES, 2 * LEV, RANK), F32),
            vmem((2, FIELDS, 2 * LEV, RANK), F32),
            vmem((PAIRS, ROWS, WIDE), F32),
            vmem((PAIRS, ROWS, WIDE), F32),
            vmem((PAIRS, ROWS, WIDE), F32),
            vmem((2, PAIRS, WIDE), F32),
            vmem((4 * PAIRS, WIDE), F32),
            vmem((PAIRS, ROWS, WIDE), F32),
            vmem((PAIRS, 32, WIDE), F32),
            dma((8,)),
            dma,
            dma((2,)),
            dma,
            dma,
            dma,
            dma,
            dma((2,)),
            dma((2,)),
            dma,
            dma((2,)),
        ],
        compiler_params=pltpu.CompilerParams(
            collective_id=0, has_side_effects=True, vmem_limit_bytes=32 * 2**20
        ),
        cost_estimate=pl.CostEstimate(flops=10**9, bytes_accessed=4 * 10**6, transcendentals=0),
    )(*(pltpu.with_memory_space_constraint(x, pltpu.HBM) for x in operands))
    return pl.pallas_call(
        hand_out,
        out_shape=(out, out),
        in_specs=[any_spec] * 2,
        out_specs=(any_spec, any_spec),
        scratch_shapes=[dma((2,))],
    )(*results)


def solution(mesh):
    return jax.shard_map(
        functools.partial(per_device, mesh.shape["lat"]),
        mesh=mesh,
        in_specs=(
            P(None, None, "lat"),
            P(None, None, "lon"),
            P(None, None, "lat", "lon"),
            P(None, "lat", "lon"),
            P(None, "lat", "lon"),
            P("lat"),
        ),
        out_specs=(P(None, None, "lat", "lon"), P(None, None, "lat", "lon")),
        check_vma=False,
    )
```

```python
import functools

import jax
import jax.numpy as jnp
import ml_dtypes
import numpy as np
from jax import lax
from jax.experimental import pallas as pl
from jax.experimental.pallas import tpu as pltpu
from jax.sharding import PartitionSpec as P

KTOP = 256
POLAR = 32
RANK = 128
ROWS = 16
COLS = 450
WIDE = 512
LANES = 8
FIELDS = 4
LEV = 4
PAIRS = FIELDS * LEV

time_step = 0.5
coupling = 0.5
mixing = 0.2
metric_cap = 4.0

FORWARD, EVALUATE, TO_COEFS, FROM_COEFS, TABLE_ROWS = 0, 512, 1280, 2304, 3840
NEAR, SIDES, REST, BLOCKS = 0, 8, 10, 24

MESH = pl.DeviceIdType.MESH
F32 = jnp.float32
BF16 = jnp.bfloat16


def split_table(table):
    high = table.astype(ml_dtypes.bfloat16)
    low = (table - high.astype(np.float64)).astype(ml_dtypes.bfloat16)
    return high, low


def waves_of(group, lane_index):
    place = lane_index % 64
    second = place // 32
    other = (8 - group) if group else 4
    residue = group + second * (other - group)
    return 8 * (place % 32) + residue + (8 * (1 - second) if group == 0 else 0)


@functools.lru_cache(None)
def mode_factors():
    total = COLS * LANES
    size = COLS + 2
    place = np.arange(size, dtype=np.float64)
    width = (KTOP + 0.5) / total
    diag = ((size - 1 - 2 * place) / 2) ** 2 * np.cos(2 * np.pi * width)
    side = place[1:] * (size - place[1:]) / 2
    vectors = np.linalg.eigh(np.diag(diag) + np.diag(side, 1) + np.diag(side, -1))[1]
    basis = vectors[:, ::-1][:, :RANK]
    basis = basis * np.where(basis[size // 2] < 0, -1.0, 1.0)
    weights = []
    for group in range(4):
        waves = waves_of(group, np.arange(64))
        angle = 2 * np.pi / total * ((np.arange(size)[:, None] - 1) * waves[None, :] % total)
        alpha, beta = basis.T @ np.cos(angle), basis.T @ np.sin(angle)
        if group:
            sign = np.where(np.arange(64) < 32, 1.0, -1.0)
            top, low = (alpha, beta), (sign * beta, -sign * alpha)
        else:
            use = np.where(np.arange(64) < 32, 1.0, 0.0)
            top, low = (use * alpha, use * beta), ((1 - use) * alpha, (1 - use) * beta)
        weights.append(np.concatenate([np.concatenate(top, axis=1), np.concatenate(low, axis=1)], axis=0))
    weights = np.round(np.stack(weights) * 2.0**22) / 2.0**22
    wide = np.zeros((RANK, WIDE))
    wide[:, : COLS + 1] = basis[1:].T
    wide[:, WIDE - 1] = basis[0]
    wide = np.round(wide * 2.0**26) / 2.0**26
    wide_h, wide_l = split_table(wide)
    own = np.where(np.arange(WIDE)[:, None] < COLS, 1, 0).astype(ml_dtypes.bfloat16)
    high, low = split_table(weights)
    back = np.concatenate([np.swapaxes(part, 1, 2) for part in (high, low, high)], axis=1)
    evaluate = np.concatenate([wide_h, wide_l, wide_h], axis=0)
    return np.concatenate(
        [
            np.concatenate([wide_h.T * own, wide_l.T * own], axis=1),
            evaluate[:, : WIDE // 2],
            evaluate[:, WIDE // 2 :],
            np.concatenate([high, low], axis=2).reshape(-1, 2 * RANK),
            back.reshape(-1, 2 * RANK),
        ],
        axis=0,
    )


ROOT = float(np.sqrt(0.5))


def over_lanes(y):
    s = [y[j] + y[j + 4] for j in range(4)]
    d = [y[j] - y[j + 4] for j in range(4)]
    even, odd = s[0] + s[2], s[1] + s[3]
    minus, plus = ROOT * (d[1] - d[3]), ROOT * (d[1] + d[3])
    return [
        (even + odd, even - odd),
        (d[0] + minus, -(d[2] + plus)),
        (s[0] - s[2], s[3] - s[1]),
        (d[0] - minus, d[2] - plus),
    ]


def to_lanes(pairs):
    (y0, y4), (u1, v1), (u2, v2), (u3, v3) = pairs
    even, odd = y0 + y4, y0 - y4
    s = [even + u2, odd - v2, even - u2, odd + v2]
    du, sv = ROOT * (u1 - u3), ROOT * (v1 + v3)
    d = [u1 + u3, du - sv, v3 - v1, -du - sv]
    return [s[j] + d[j] for j in range(4)] + [s[j] - d[j] for j in range(4)]


@functools.lru_cache(None)
def half_metric(bands):
    total = bands * ROWS
    rows = np.clip(np.arange(bands)[:, None] * ROWS - 8 + np.arange(32)[None, :], 0, total - 1)
    metric = np.minimum(1.0 / np.cos(np.pi * ((rows + 0.5) / total - 0.5)), metric_cap)
    table = np.broadcast_to((0.5 * metric).astype(np.float32)[:, :, None], (bands, 32, 128)).copy()
    forward = mode_factors()[FORWARD : FORWARD + WIDE].astype(np.float32)
    for row, col in enumerate((0, COLS - 1)):
        table[:, row] = forward[col, :RANK] + forward[col, RANK:]
    return table


def dot_cols(a, b):
    return lax.dot_general(a, b, (((1,), (0,)), ((), ())), preferred_element_type=F32)


def split(x):
    high = x.astype(BF16)
    return high, (x - high.astype(F32)).astype(BF16)


def to_modes(x, table):
    xh, xl = split(x)
    half = table.shape[1] // 2
    wide = dot_cols(xh, table[...])
    return wide[:, :half] + wide[:, half:] + dot_cols(xl, table[:, 0:half])


def from_modes(z, *tables):
    zh, zl = split(z)
    three = jnp.concatenate([zh, zh, zl], axis=1)
    return jnp.concatenate([dot_cols(three, table[...]) for table in tables], axis=1)


def roll(x, shift, axis):
    return pltpu.roll(x, shift % x.shape[axis], axis)


def roll_blocks(x, shift):
    return roll(x.reshape(x.shape[0] * x.shape[1], x.shape[2]), shift, 1).reshape(x.shape)


def fold(x):
    while x.shape[0] > 1:
        half = x.shape[0] // 2
        x = x[:half] + roll_blocks(x[half:], 2 * half)
    return x


def kernel(
    bands, spread, east, north, rs, cs, cut, metric, table_in, tan_out, diag_out,
    spread_v, winds_v, rs_v, cs_v, cut_s, hm, table,
    grid, halo_out, halo_in, ybuf, yr, cb, yc, zbuf, zr, eb, bz,
    tend, proj_p, proj_t, edge_t, edge_proj, adj, gy,
    in_sem, halo_send, halo_recv, y_send, y_recv, c_send, c_recv, z_send, z_recv, b_send, b_recv,
):
    b = lax.axis_index("lat")
    i = lax.axis_index("lon")
    caps = POLAR // ROWS
    is_north = b == 0
    is_south = b == bands - 1
    polar = jnp.logical_or(b < caps, b >= bands - caps)
    above_polar = jnp.logical_or(b <= caps, is_south)
    below_polar = jnp.logical_or(b >= bands - caps - 1, is_north)
    near_polar = jnp.logical_or(above_polar, below_polar)
    across = lax.rem(i + LANES // 2, LANES)
    west = lax.rem(i + LANES - 1, LANES)
    east_lane = lax.rem(i + 1, LANES)
    nb = jnp.where(is_north, 0, b - 1)
    nl = jnp.where(is_north, across, i)
    sb = jnp.where(is_south, bands - 1, b + 1)
    sl = jnp.where(is_south, across, i)
    slot_n = jnp.where(is_north, 0, 1)
    slot_s = jnp.where(is_south, 1, 0)
    own_half = lax.rem(i, 2)
    edge_over = jnp.where(own_half == 0, is_north, is_south)
    over_pole = (is_north, is_south)

    def plus(lane, d):
        return lax.rem(lane + d, LANES)

    load_spread = pltpu.make_async_copy(spread, spread_v, in_sem.at[0])
    load_rows = pltpu.make_async_copy(rs, rs_v, in_sem.at[1])
    load_cols = pltpu.make_async_copy(cs, cs_v, in_sem.at[2])
    load_metric = pltpu.make_async_copy(metric.at[b], hm, in_sem.at[4])
    load_cut = pltpu.make_async_copy(cut, cut_s, in_sem.at[5])

    def load_table(start, stop, sem):
        return pltpu.make_async_copy(table_in.at[start:stop], table.at[start:stop], in_sem.at[sem])

    load_forward = load_table(FORWARD, EVALUATE, 6)
    load_others = load_table(EVALUATE, TABLE_ROWS, 7)
    load_part = load_table(EVALUATE, TO_COEFS, 7)
    load_spread.start()
    load_rows.start()
    load_cols.start()
    pltpu.make_async_copy(east, winds_v.at[0], in_sem.at[3]).start()
    pltpu.make_async_copy(north, winds_v.at[1], in_sem.at[3]).start()
    load_metric.start()

    barrier = pltpu.get_barrier_semaphore()

    def greet(lat, lon):
        pl.semaphore_signal(barrier, inc=1, device_id=(lat, lon), device_id_type=MESH)

    greet(nb, nl)
    greet(sb, sl)
    greet(b, west)
    greet(b, east_lane)

    @pl.when(polar)
    def _():
        @pl.loop(2, LANES - 1)
        def _(d):
            greet(b, plus(i, d))

        load_forward.start()
        load_cut.start()
        load_others.start()

    @pl.when(jnp.logical_and(near_polar, jnp.logical_not(polar)))
    def _():
        load_part.start()

    load_rows.wait()
    load_cols.wait()
    load_spread.wait()
    grid[:, 8:24, 384:512] = jnp.zeros((PAIRS + 2 * LEV, ROWS, 128), F32)
    row_part = jnp.concatenate([rs_v[f] for f in range(FIELDS)], axis=0)
    row_part = (2 * row_part - 1).astype(F32).T
    for f in range(FIELDS):
        col_part = (2 * cs_v[f] - 1).astype(F32)
        for l in range(LEV):
            n = f * LEV + l
            grid[n, 8:24, 0:COLS] = spread_v[f, l] * (row_part[:, n : n + 1] * col_part[l : l + 1, :])
    pltpu.make_async_copy(winds_v, winds_v, in_sem.at[3]).wait()
    for w in range(2):
        for l in range(LEV):
            grid[PAIRS + w * LEV + l, 8:24, 0:COLS] = winds_v[w, l]

    for s, (near, far) in enumerate(((8, 9), (23, 22))):
        for t in range(4):
            lanes = slice(128 * t, 128 * t + 128)
            halo_out[NEAR + 4 * s + t] = grid[0:PAIRS, near, lanes]
            halo_out[REST + 7 * s + t] = grid[0:PAIRS, far, lanes]
            halo_out[REST + 7 * s + 4 + t // 2, 8 * (t % 2) : 8 * (t % 2) + 8, :] = grid[
                PAIRS : PAIRS + 2 * LEV, near, lanes
            ]
    lane128 = lax.broadcasted_iota(jnp.int32, (1, 1, 128), 2)
    for s, (start, shift) in enumerate(((0, 0), (384, COLS - 2 - 384))):
        tile = grid[:, 8:24, start : start + 128]
        tile = jnp.where(jnp.logical_and(lane128 >= shift, lane128 < shift + 2), tile, 0.0)
        packed = fold(tile[:PAIRS]) + roll_blocks(fold(tile[PAIRS:]), 2 * PAIRS)
        halo_out[SIDES + s] = roll_blocks(packed, -shift)[0]

    def values(q, x):
        y = to_modes(x.reshape(PAIRS * ROWS, WIDE), table.at[FORWARD:EVALUATE])
        y = y.reshape(FIELDS, LEV, 2, 8, RANK)
        for f in range(FIELDS):
            for h in range(2):
                for l in range(LEV):
                    ybuf[2 * f + h, q, l] = y[f, l, h]

    @pl.when(polar)
    def _():
        load_forward.wait()
        values(0, grid[0:PAIRS, 8:24, :])

    pl.semaphore_wait(barrier, 4 + jnp.where(polar, LANES - 3, 0))

    def remote(src, dst, send, recv, lat, lon):
        return pltpu.make_async_remote_copy(
            src_ref=src, dst_ref=dst, send_sem=send, recv_sem=recv, device_id=(lat, lon), device_id_type=MESH
        )

    def halo_copy(start, count, to, which, lat, lon):
        return remote(
            halo_out.at[start : start + count], halo_in.at[pl.ds(to, count)], halo_send, halo_recv.at[which], lat, lon
        )

    def halo_arrival(start, stop, which):
        return remote(
            halo_out.at[start:stop], halo_in.at[start:stop], halo_send, halo_recv.at[which], b, west
        )

    halo_copy(NEAR, 4, NEAR + 4 * slot_n, 0, nb, nl).start()
    halo_copy(NEAR + 4, 4, NEAR + 4 * slot_s, 0, sb, sl).start()
    halo_copy(SIDES, 1, SIDES + 1, 0, b, west).start()
    halo_copy(SIDES + 1, 1, SIDES, 0, b, east_lane).start()

    def y_copy(o):
        return remote(ybuf.at[o], yr.at[i], y_send, y_recv, b, o)

    others = pl.ds(0, LANES - 1)

    def all_y():
        return remote(ybuf.at[others], yr.at[others], y_send, y_recv, b, west)

    def send_values():
        @pl.loop(1, LANES)
        def _(d):
            y_copy(plus(i, d)).start()

        yr[i] = ybuf[i]

    def c_copy(o):
        return remote(cb.at[o], yc.at[i], c_send, c_recv, b, o)

    def all_c():
        return remote(cb.at[others], yc.at[others], c_send, c_recv, b, west)

    def z_copy(q, j):
        return remote(zbuf.at[q, j], zr.at[q, i], z_send.at[q], z_recv.at[q], b, j)

    def all_z(q):
        return remote(zbuf.at[q, others], zr.at[q, others], z_send.at[q], z_recv.at[q], b, west)

    def own_rows(q):
        row = lax.broadcasted_iota(jnp.int32, (8, 128), 0)
        cutoff = jnp.zeros((8, 128), jnp.int32)
        for r in range(8):
            cutoff = jnp.where(row == r, cut_s[8 * own_half + r], cutoff)

        if q == 0:
            all_y().wait_recv()
        else:
            all_c().wait_recv()

        lanes = []
        for j in range(LANES):
            y = yr[j, q]
            if q == 1:
                ends = pltpu.roll(yc[j, 8:16, :], lax.rem(128 - 2 * LEV * (i // 2), 128), 1)
                edge = jnp.where(row == 7 * own_half, 1.0, 0.0)
                y = jnp.concatenate(
                    [
                        y[l]
                        + ends[:, 2 * l : 2 * l + 1] * hm[0:1, :]
                        + ends[:, 2 * l + 1 : 2 * l + 2] * hm[1:2, :]
                        + edge * yc[j, l : l + 1, :]
                        for l in range(LEV)
                    ],
                    axis=0,
                )
            lanes.append(y.reshape(LEV * 8, RANK))
        pairs = []
        over = over_lanes(lanes)
        for group, pair in enumerate(over):
            coef = to_modes(
                jnp.concatenate(pair, axis=1), table.at[TO_COEFS + 256 * group : TO_COEFS + 256 * (group + 1)]
            )
            wave = waves_of(group, lax.broadcasted_iota(jnp.int32, (8, 128), 1))
            keep = jnp.where(wave > cutoff, 2.0 / (COLS * LANES), 0.0)
            back = from_modes(
                coef * jnp.concatenate([keep] * LEV, axis=0),
                table.at[FROM_COEFS + 384 * group : FROM_COEFS + 384 * (group + 1)],
            )
            pairs.append((back[:, :RANK], back[:, RANK:]))
        for j, z in enumerate(to_lanes(pairs)):
            z = z.reshape(LEV, 8, RANK)
            zbuf[q, j] = z
            eb[j, LEV * q : LEV * (q + 1), :] = jnp.where(own_half == 0, z[:, 0, :], z[:, 7, :])

        @pl.loop(1, LANES)
        def _(d):
            z_copy(q, plus(i, d)).start()

        zr[q, i] = zbuf[q, i]

    def edge_sends():
        slot = jnp.where(own_half == 0, slot_n, slot_s)
        lat = jnp.where(own_half == 0, nb, sb)

        @pl.loop(0, LANES)
        def _(d):
            j = plus(i, d)
            lon = jnp.where(edge_over, plus(j, LANES // 2), j)
            here = jnp.logical_and(edge_over, lon == i)

            @pl.when(jnp.logical_not(here))
            def _():
                remote(eb.at[j], bz.at[slot, i // 2], b_send, b_recv.at[slot], lat, lon).start()

            @pl.when(here)
            def _():
                pltpu.make_async_copy(eb.at[j], bz.at[slot, i // 2], b_recv.at[slot]).start()

    def evaluate(z):
        return from_modes(z, table.at[EVALUATE : EVALUATE + 384], table.at[EVALUATE + 384 : TO_COEFS])

    def project(q, out):
        all_z(q).wait_recv()
        z = jnp.concatenate(
            [zr[q, 2 * f + h, l] for f in range(FIELDS) for l in range(LEV) for h in range(2)], axis=0
        )
        out[...] = evaluate(z).reshape(PAIRS, ROWS, WIDE)

    def tendency_rows(h):
        @pl.loop(0, LEV)
        def _(l):
            lo = jnp.maximum(l - 1, 0)
            hi = jnp.minimum(l + 1, LEV - 1)
            half = jnp.concatenate([hm[h : h + 8, :]] * 4, axis=1)
            ew = grid[PAIRS + l, h : h + 8, :]
            nw = grid[PAIRS + LEV + l, h : h + 8, :]
            along_x, along_y = [], []
            for f in range(FIELDS):
                mid = grid[f * LEV + l, h : h + 8, :]
                along_x.append(half * (roll(mid, -1, 1) - roll(mid, 1, 1)))
                along_y.append(0.5 * (grid[f * LEV + l, h + 1 : h + 9, :] - grid[f * LEV + l, h - 1 : h + 7, :]))
            linked = (along_x[2], along_y[2], along_x[0] + along_y[1], None)
            for f in range(FIELDS):
                mid = grid[f * LEV + l, h : h + 8, :]
                mixed = grid[f * LEV + lo, h : h + 8, :] + grid[f * LEV + hi, h : h + 8, :] - 2.0 * mid
                t = -(ew * along_x[f] + nw * along_y[f]) + mixing * mixed
                if linked[f] is not None:
                    t = t - coupling * linked[f]
                tend[f * LEV + l, h - 8 : h, :] = t

    load_metric.wait()

    @pl.when(polar)
    def _():
        grid[0:PAIRS, 7:8, :] = jnp.zeros((PAIRS, 1, WIDE), F32)
        grid[0:PAIRS, 24:25, :] = jnp.zeros((PAIRS, 1, WIDE), F32)
        for part in range(2):
            tendency_rows(8 + 8 * part)
        values(1, tend[...])
        send_values()

    halo_arrival(NEAR, REST, 0).wait_recv()
    lane2 = lax.broadcasted_iota(jnp.int32, (1, 128), 1)
    row16 = lax.broadcasted_iota(jnp.int32, (PAIRS, 1), 0)
    is_v = jnp.logical_and(row16 >= LEV, row16 < 2 * LEV)
    is_temp = jnp.logical_and(row16 >= 2 * LEV, row16 < 3 * LEV)

    def flip(s, minus):
        sign = jnp.where(row16 < 2 * LEV, -1.0, 1.0) * minus
        return jnp.where(over_pole[s], sign, 1.0)

    def row_link(x):
        return jnp.where(is_v, roll(x, -LEV, 0), jnp.where(is_temp, roll(x, LEV, 0), 0.0))

    def wind(buffer, s, w):
        base = REST + 7 * s + 4
        rows = [buffer[base + t // 2, 8 * (t % 2) + LEV * w : 8 * (t % 2) + LEV * (w + 1), :] for t in range(4)]
        return jnp.concatenate([jnp.concatenate(rows, axis=1)] * FIELDS, axis=0)

    def row_of(buffer, start):
        return jnp.concatenate([buffer[start + t] for t in range(4)], axis=1)

    @pl.when(polar)
    def _():
        added = []
        for s, sign in ((0, 0.5), (1, -0.5)):
            ghost = flip(s, 1.0) * row_of(halo_in, NEAR + 4 * s)
            added.append(sign * (wind(halo_out, s, 1) * ghost + coupling * row_link(ghost)))
        y = to_modes(jnp.concatenate(added, axis=0), table.at[FORWARD:EVALUATE])
        for s in range(2):
            for f in range(FIELDS):
                cb[2 * f + s, 0:LEV, :] = y[(s * FIELDS + f) * LEV : (s * FIELDS + f + 1) * LEV, :]
        ends = []
        for side, sign in ((0, -1.0), (1, 1.0)):
            came = halo_in[SIDES + side]
            along_x = (sign * hm[8:24, :]) * (roll(came, -1, 1) if side == 0 else came)
            mine = jnp.where(
                jnp.logical_and(lane2 >= 2 * PAIRS, lane2 < 2 * (PAIRS + LEV)), halo_out[SIDES + side], 0.0
            )
            ew = sum(roll(mine, 2 * LEV * f - 2 * PAIRS - side, 1) for f in range(FIELDS))
            linked = jnp.where(
                lane2 < 2 * LEV,
                roll(along_x, -4 * LEV, 1),
                jnp.where(
                    jnp.logical_and(lane2 >= 4 * LEV, lane2 < 6 * LEV), roll(along_x, 4 * LEV, 1), 0.0
                ),
            )
            ends.append(-ew * along_x - coupling * linked)
        ends = jnp.where(lax.rem(lane2, 2) == 0, ends[0], roll(ends[1], 1, 1))
        for f in range(FIELDS):
            for h in range(2):
                cb[2 * f + h, 8:16, :] = ends[8 * h : 8 * h + 8, :]

        @pl.loop(1, LANES)
        def _(d):
            c_copy(plus(i, d)).start()

        yc[i] = cb[i]

    from_west = roll(halo_in[SIDES], 126, 1)
    from_east = roll(halo_in[SIDES + 1], COLS - 384, 1)
    both = jnp.where(jnp.logical_and(lane2 >= 66, lane2 < 114), from_east, from_west)[None]
    for width in (2, 4, 8):
        both = jnp.concatenate([both, roll_blocks(both, -width)], axis=0)
    both = jnp.concatenate([both, roll_blocks(both, -16), roll_blocks(both, -32)], axis=0)
    in_halo = jnp.logical_or(jnp.logical_and(lane128 >= 66, lane128 < 68), lane128 >= 126)
    grid[:, 8:24, 384:512] = jnp.where(in_halo, both, grid[:, 8:24, 384:512])
    for s, near in enumerate((8, 23)):
        halo_out[REST + 7 * s + 6] = grid[0:PAIRS, near, 384:512]
    halo_copy(REST, 7, REST + 7 * slot_n, 1, nb, nl).start()
    halo_copy(REST + 7, 7, REST + 7 * slot_s, 1, sb, sl).start()

    @pl.when(polar)
    def _():
        load_cut.wait()
        load_others.wait()
        own_rows(0)
        own_rows(1)
        edge_sends()

    halo_arrival(REST, BLOCKS, 1).wait_recv()
    edge_row = (7, 24)
    edge_probe = []
    for s in range(2):
        edge_probe.append(
            jnp.concatenate([halo_in[NEAR + 4 * s + t] for t in range(3)] + [halo_in[REST + 7 * s + 6]], axis=1)
        )
        grid[0:PAIRS, edge_row[s], :] = flip(s, 1.0) * edge_probe[s]

    for part in range(2):
        tendency_rows(8 + 8 * part)

    for s, inward in ((0, 1.0), (1, -1.0)):
        mid = edge_probe[s]
        half = jnp.concatenate([hm[edge_row[s] : edge_row[s] + 1, :]] * 4, axis=1)
        along_x = half * (roll(mid, -1, 1) - roll(mid, 1, 1))
        turn = jnp.where(over_pole[s], -0.5 * inward, 0.5 * inward)
        along_y = turn * (flip(s, 1.0) * row_of(halo_out, NEAR + 4 * s) - row_of(halo_in, REST + 7 * s))
        linked = jnp.where(row16 < LEV, roll(along_x, -2 * LEV, 0), row_link(along_y))
        linked = linked + jnp.where(is_temp, roll(along_x, 2 * LEV, 0), 0.0)
        up = jnp.where(lax.rem(row16, LEV) == 0, mid, roll(mid, 1, 0))
        down = jnp.where(lax.rem(row16, LEV) == LEV - 1, mid, roll(mid, -1, 0))
        t = -(wind(halo_in, s, 0) * along_x + wind(halo_in, s, 1) * along_y) - coupling * linked
        edge_t[s] = t + mixing * (up + down - 2.0 * mid)

    @pl.when(polar)
    def _():
        project(0, proj_p)
        project(1, proj_t)

    @pl.when(jnp.logical_not(polar))
    def _():
        proj_p[...] = jnp.zeros(proj_p.shape, F32)
        proj_t[...] = jnp.zeros(proj_t.shape, F32)

    def row_weights(a, nw):
        return (
            -nw * a[0],
            -nw * a[1] - coupling * a[2],
            -nw * a[2] - coupling * a[1],
            -nw * a[3],
        )

    @pl.loop(0, LEV)
    def _(l):
        for h in (8, 16):
            nw = grid[PAIRS + LEV + l, h : h + 8, :]
            a = []
            for f in range(FIELDS):
                n = f * LEV + l
                change = time_step * (tend[n, h - 8 : h, :] - proj_t[n, h - 8 : h, :])
                tend[n, h - 8 : h, :] = change
                tangent = grid[n, h : h + 8, :] + change
                tan_out[f, l, h - 8 : h, :] = tangent[:, :COLS]
                a.append(tangent - proj_p[n, h - 8 : h, :])
                adj[n, h - 8 : h, :] = a[f]
            for f, weight in enumerate(row_weights(a, nw)):
                gy[f * LEV + l, h : h + 8, :] = weight

    for s, wanted in enumerate((above_polar, below_polar)):
        @pl.when(wanted)
        def _():
            remote(bz.at[s], bz.at[s], b_send, b_recv.at[s], nb, nl).wait_recv()

        @pl.when(jnp.logical_not(wanted))
        def _():
            bz[s] = jnp.zeros((FIELDS, 2 * LEV, RANK), F32)

    @pl.when(jnp.logical_and(near_polar, jnp.logical_not(polar)))
    def _():
        load_part.wait()

    @pl.when(near_polar)
    def _():
        parts = [
            bz[s, f, LEV * q : LEV * (q + 1), :] for s in range(2) for q in range(2) for f in range(FIELDS)
        ]
        edge_proj[...] = evaluate(jnp.concatenate(parts, axis=0))

    @pl.when(jnp.logical_not(near_polar))
    def _():
        edge_proj[...] = jnp.zeros(edge_proj.shape, F32)

    for s in range(2):
        base = 2 * PAIRS * s
        a = (
            edge_probe[s]
            + time_step * (edge_t[s] - edge_proj[base + PAIRS : base + 2 * PAIRS, :])
            - edge_proj[base : base + PAIRS, :]
        )
        weight = -wind(halo_in, s, 1) * a - coupling * row_link(a)
        gy[0:PAIRS, edge_row[s], :] = flip(s, -1.0) * weight

    @pl.loop(0, LEV)
    def _(l):
        lo = jnp.maximum(l - 1, 0)
        hi = jnp.minimum(l + 1, LEV - 1)
        for h in (8, 16):
            rows = slice(h - 8, h)
            half = jnp.concatenate([hm[h : h + 8, :]] * 4, axis=1)
            ew = grid[PAIRS + l, h : h + 8, :]
            a = [adj[f * LEV + l, rows, :] for f in range(FIELDS)]
            col_weights = (
                -ew * a[0] - coupling * a[2],
                -ew * a[1],
                -ew * a[2] - coupling * a[0],
                -ew * a[3],
            )
            for f in range(FIELDS):
                n = f * LEV + l
                back = half * (roll(col_weights[f], 1, 1) - roll(col_weights[f], -1, 1))
                back = back + 0.5 * (gy[n, h - 1 : h + 7, :] - gy[n, h + 1 : h + 9, :])
                back = back + mixing * (adj[f * LEV + lo, rows, :] + adj[f * LEV + hi, rows, :] - 2.0 * a[f])
                diag = grid[n, h : h + 8, :] * (tend[n, rows, :] + time_step * back)
                diag_out[f, l, rows, :] = diag[:, :COLS]

    halo_arrival(0, BLOCKS, 0).wait_send()

    @pl.when(polar)
    def _():
        all_y().wait_send()
        all_c().wait_send()
        for q in range(2):
            all_z(q).wait_send()

        @pl.when(edge_over)
        def _():
            remote(eb.at[others], eb.at[others], b_send, b_recv.at[0], b, west).wait_send()

        @pl.when(jnp.logical_not(edge_over))
        def _():
            remote(eb, eb, b_send, b_recv.at[0], b, west).wait_send()


def hand_out(tan_in, diag_in, tan_out, diag_out, sem):
    copies = [
        pltpu.make_async_copy(src, dst, sem.at[n])
        for n, (src, dst) in enumerate(((tan_in, tan_out), (diag_in, diag_out)))
    ]
    for copy in copies:
        copy.start()
    for copy in copies:
        copy.wait()


def per_device(bands, row_signs, col_signs, spread, east_wind, north_wind, cutoffs):
    any_spec = pl.BlockSpec(memory_space=pl.ANY)
    out = jax.ShapeDtypeStruct((FIELDS, LEV, ROWS, COLS), F32)
    tables = [jnp.asarray(half_metric(bands)), jnp.asarray(mode_factors())]
    operands = (spread, east_wind, north_wind, row_signs, col_signs, cutoffs, *tables)
    vmem = pltpu.VMEM
    dma = pltpu.SemaphoreType.DMA
    held = pltpu.VMEM(out.shape, F32)
    results = pl.pallas_call(
        functools.partial(kernel, bands),
        out_shape=(held, held),
        in_specs=[any_spec] * 8,
        out_specs=(pl.BlockSpec(memory_space=pltpu.VMEM),) * 2,
        scratch_shapes=[
            vmem((FIELDS, LEV, ROWS, COLS), F32),
            vmem((2, LEV, ROWS, COLS), F32),
            vmem((FIELDS, LEV, ROWS), jnp.int32),
            vmem((FIELDS, LEV, COLS), jnp.int32),
            pltpu.SMEM((ROWS,), jnp.int32),
            vmem((32, 128), F32),
            vmem((TABLE_ROWS, 2 * RANK), BF16),
            vmem((PAIRS + 2 * LEV, 32, WIDE), F32),
            vmem((BLOCKS, 16, 128), F32),
            vmem((BLOCKS, 16, 128), F32),
            vmem((LANES, 2, LEV, 8, RANK), F32),
            vmem((LANES, 2, LEV, 8, RANK), F32),
            vmem((LANES, 16, RANK), F32),
            vmem((LANES, 16, RANK), F32),
            vmem((2, LANES, LEV, 8, RANK), F32),
            vmem((2, LANES, LEV, 8, RANK), F32),
            vmem((LANES, 2 * LEV, RANK), F32),
            vmem((2, FIELDS, 2 * LEV, RANK), F32),
            vmem((PAIRS, ROWS, WIDE), F32),
            vmem((PAIRS, ROWS, WIDE), F32),
            vmem((PAIRS, ROWS, WIDE), F32),
            vmem((2, PAIRS, WIDE), F32),
            vmem((4 * PAIRS, WIDE), F32),
            vmem((PAIRS, ROWS, WIDE), F32),
            vmem((PAIRS, 32, WIDE), F32),
            dma((8,)),
            dma,
            dma((2,)),
            dma,
            dma,
            dma,
            dma,
            dma((2,)),
            dma((2,)),
            dma,
            dma((2,)),
        ],
        compiler_params=pltpu.CompilerParams(
            collective_id=0, has_side_effects=True, vmem_limit_bytes=32 * 2**20
        ),
        cost_estimate=pl.CostEstimate(flops=10**9, bytes_accessed=4 * 10**6, transcendentals=0),
    )(*(pltpu.with_memory_space_constraint(x, pltpu.HBM) for x in operands))
    return pl.pallas_call(
        hand_out,
        out_shape=(out, out),
        in_specs=[any_spec] * 2,
        out_specs=(any_spec, any_spec),
        scratch_shapes=[dma((2,))],
        compiler_params=pltpu.CompilerParams(vmem_limit_bytes=2**20),
    )(*(pltpu.with_memory_space_constraint(x, pltpu.VMEM) for x in results))


def solution(mesh):
    return jax.shard_map(
        functools.partial(per_device, mesh.shape["lat"]),
        mesh=mesh,
        in_specs=(
            P(None, None, "lat"),
            P(None, None, "lon"),
            P(None, None, "lat", "lon"),
            P(None, "lat", "lon"),
            P(None, "lat", "lon"),
            P("lat"),
        ),
        out_specs=(P(None, None, "lat", "lon"), P(None, None, "lat", "lon")),
        check_vma=False,
    )
```

```python
import functools

import jax
import jax.numpy as jnp
import ml_dtypes
import numpy as np
from jax import lax
from jax.experimental import pallas as pl
from jax.experimental.pallas import tpu as pltpu
from jax.sharding import PartitionSpec as P

KTOP = 256
POLAR = 32
RANK = 128
ROWS = 16
COLS = 450
WIDE = 512
LANES = 8
FIELDS = 4
LEV = 4
PAIRS = FIELDS * LEV

time_step = 0.5
coupling = 0.5
mixing = 0.2
metric_cap = 4.0

FORWARD, EVALUATE, TO_COEFS, FROM_COEFS, TABLE_ROWS = 0, 512, 1280, 2304, 3840
NEAR, SIDES, REST, BLOCKS = 0, 8, 10, 24

MESH = pl.DeviceIdType.MESH
F32 = jnp.float32
BF16 = jnp.bfloat16


def split_table(table):
    high = table.astype(ml_dtypes.bfloat16)
    low = (table - high.astype(np.float64)).astype(ml_dtypes.bfloat16)
    return high, low


def waves_of(group, lane_index):
    place = lane_index % 64
    second = place // 32
    other = (8 - group) if group else 4
    residue = group + second * (other - group)
    return 8 * (place % 32) + residue + (8 * (1 - second) if group == 0 else 0)


@functools.lru_cache(None)
def mode_factors():
    total = COLS * LANES
    size = COLS + 2
    place = np.arange(size, dtype=np.float64)
    width = (KTOP + 0.5) / total
    diag = ((size - 1 - 2 * place) / 2) ** 2 * np.cos(2 * np.pi * width)
    side = place[1:] * (size - place[1:]) / 2
    vectors = np.linalg.eigh(np.diag(diag) + np.diag(side, 1) + np.diag(side, -1))[1]
    basis = vectors[:, ::-1][:, :RANK]
    basis = basis * np.where(basis[size // 2] < 0, -1.0, 1.0)
    weights = []
    for group in range(4):
        waves = waves_of(group, np.arange(64))
        angle = 2 * np.pi / total * ((np.arange(size)[:, None] - 1) * waves[None, :] % total)
        alpha, beta = basis.T @ np.cos(angle), basis.T @ np.sin(angle)
        if group:
            sign = np.where(np.arange(64) < 32, 1.0, -1.0)
            top, low = (alpha, beta), (sign * beta, -sign * alpha)
        else:
            use = np.where(np.arange(64) < 32, 1.0, 0.0)
            top, low = (use * alpha, use * beta), ((1 - use) * alpha, (1 - use) * beta)
        weights.append(np.concatenate([np.concatenate(top, axis=1), np.concatenate(low, axis=1)], axis=0))
    weights = np.round(np.stack(weights) * 2.0**22) / 2.0**22
    wide = np.zeros((RANK, WIDE))
    wide[:, : COLS + 1] = basis[1:].T
    wide[:, WIDE - 1] = basis[0]
    wide = np.round(wide * 2.0**26) / 2.0**26
    wide_h, wide_l = split_table(wide)
    own = np.where(np.arange(WIDE)[:, None] < COLS, 1, 0).astype(ml_dtypes.bfloat16)
    high, low = split_table(weights)
    back = np.concatenate([np.swapaxes(part, 1, 2) for part in (high, low, high)], axis=1)
    evaluate = np.concatenate([wide_h, wide_l, wide_h], axis=0)
    return np.concatenate(
        [
            np.concatenate([wide_h.T * own, wide_l.T * own], axis=1),
            evaluate[:, : WIDE // 2],
            evaluate[:, WIDE // 2 :],
            np.concatenate([high, low], axis=2).reshape(-1, 2 * RANK),
            back.reshape(-1, 2 * RANK),
        ],
        axis=0,
    )


ROOT = float(np.sqrt(0.5))


def over_lanes(y):
    s = [y[j] + y[j + 4] for j in range(4)]
    d = [y[j] - y[j + 4] for j in range(4)]
    even, odd = s[0] + s[2], s[1] + s[3]
    minus, plus = ROOT * (d[1] - d[3]), ROOT * (d[1] + d[3])
    return [
        (even + odd, even - odd),
        (d[0] + minus, -(d[2] + plus)),
        (s[0] - s[2], s[3] - s[1]),
        (d[0] - minus, d[2] - plus),
    ]


def to_lanes(pairs):
    (y0, y4), (u1, v1), (u2, v2), (u3, v3) = pairs
    even, odd = y0 + y4, y0 - y4
    s = [even + u2, odd - v2, even - u2, odd + v2]
    du, sv = ROOT * (u1 - u3), ROOT * (v1 + v3)
    d = [u1 + u3, du - sv, v3 - v1, -du - sv]
    return [s[j] + d[j] for j in range(4)] + [s[j] - d[j] for j in range(4)]


@functools.lru_cache(None)
def half_metric(bands):
    total = bands * ROWS
    rows = np.clip(np.arange(bands)[:, None] * ROWS - 8 + np.arange(32)[None, :], 0, total - 1)
    metric = np.minimum(1.0 / np.cos(np.pi * ((rows + 0.5) / total - 0.5)), metric_cap)
    table = np.broadcast_to((0.5 * metric).astype(np.float32)[:, :, None], (bands, 32, 128)).copy()
    forward = mode_factors()[FORWARD : FORWARD + WIDE].astype(np.float32)
    for row, col in enumerate((0, COLS - 1)):
        table[:, row] = forward[col, :RANK] + forward[col, RANK:]
    return table


def dot_cols(a, b):
    return lax.dot_general(a, b, (((1,), (0,)), ((), ())), preferred_element_type=F32)


def split(x):
    high = x.astype(BF16)
    return high, (x - high.astype(F32)).astype(BF16)


def to_modes(x, table):
    xh, xl = split(x)
    half = table.shape[1] // 2
    wide = dot_cols(xh, table[...])
    return wide[:, :half] + wide[:, half:] + dot_cols(xl, table[:, 0:half])


def from_modes(z, *tables):
    zh, zl = split(z)
    three = jnp.concatenate([zh, zh, zl], axis=1)
    return jnp.concatenate([dot_cols(three, table[...]) for table in tables], axis=1)


def roll(x, shift, axis):
    return pltpu.roll(x, shift % x.shape[axis], axis)


def roll_blocks(x, shift):
    return roll(x.reshape(x.shape[0] * x.shape[1], x.shape[2]), shift, 1).reshape(x.shape)


def fold(x):
    while x.shape[0] > 1:
        half = x.shape[0] // 2
        x = x[:half] + roll_blocks(x[half:], 2 * half)
    return x


def kernel(
    bands, spread, east, north, rs, cs, cut, metric, table_in, tan_out, diag_out,
    spread_v, winds_v, rs_v, cs_v, cut_s, hm, table,
    grid, halo_out, halo_in, ybuf, yr, cb, yc, zbuf, zr, eb, bz,
    tend, adj, gy,
    in_sem, halo_send, halo_recv, y_send, y_recv, c_send, c_recv, z_send, z_recv, b_send, b_recv,
):
    b = lax.axis_index("lat")
    i = lax.axis_index("lon")
    caps = POLAR // ROWS
    is_north = b == 0
    is_south = b == bands - 1
    polar = jnp.logical_or(b < caps, b >= bands - caps)
    above_polar = jnp.logical_or(b <= caps, is_south)
    below_polar = jnp.logical_or(b >= bands - caps - 1, is_north)
    near_polar = jnp.logical_or(above_polar, below_polar)
    across = lax.rem(i + LANES // 2, LANES)
    west = lax.rem(i + LANES - 1, LANES)
    east_lane = lax.rem(i + 1, LANES)
    nb = jnp.where(is_north, 0, b - 1)
    nl = jnp.where(is_north, across, i)
    sb = jnp.where(is_south, bands - 1, b + 1)
    sl = jnp.where(is_south, across, i)
    slot_n = jnp.where(is_north, 0, 1)
    slot_s = jnp.where(is_south, 1, 0)
    own_half = lax.rem(i, 2)
    edge_over = jnp.where(own_half == 0, is_north, is_south)
    over_pole = (is_north, is_south)

    def plus(lane, d):
        return lax.rem(lane + d, LANES)

    load_spread = pltpu.make_async_copy(spread, spread_v, in_sem.at[0])
    load_rows = pltpu.make_async_copy(rs, rs_v, in_sem.at[1])
    load_cols = pltpu.make_async_copy(cs, cs_v, in_sem.at[2])
    load_metric = pltpu.make_async_copy(metric.at[b], hm, in_sem.at[4])
    load_cut = pltpu.make_async_copy(cut, cut_s, in_sem.at[5])

    def load_table(start, stop, sem):
        return pltpu.make_async_copy(table_in.at[start:stop], table.at[start:stop], in_sem.at[sem])

    load_forward = load_table(FORWARD, EVALUATE, 6)
    load_others = load_table(EVALUATE, TABLE_ROWS, 7)
    load_part = load_table(EVALUATE, TO_COEFS, 7)
    load_spread.start()
    load_rows.start()
    load_cols.start()
    pltpu.make_async_copy(east, winds_v.at[0], in_sem.at[3]).start()
    pltpu.make_async_copy(north, winds_v.at[1], in_sem.at[3]).start()
    load_metric.start()

    barrier = pltpu.get_barrier_semaphore()

    def greet(lat, lon):
        pl.semaphore_signal(barrier, inc=1, device_id=(lat, lon), device_id_type=MESH)

    greet(nb, nl)
    greet(sb, sl)
    greet(b, west)
    greet(b, east_lane)

    @pl.when(polar)
    def _():
        @pl.loop(2, LANES - 1)
        def _(d):
            greet(b, plus(i, d))

        load_forward.start()
        load_cut.start()
        load_others.start()

    @pl.when(jnp.logical_and(near_polar, jnp.logical_not(polar)))
    def _():
        load_part.start()

    load_rows.wait()
    load_cols.wait()
    load_spread.wait()
    grid[:, 8:24, 384:512] = jnp.zeros((PAIRS + 2 * LEV, ROWS, 128), F32)
    row_part = jnp.concatenate([rs_v[f] for f in range(FIELDS)], axis=0)
    row_part = (2 * row_part - 1).astype(F32).T
    for f in range(FIELDS):
        col_part = (2 * cs_v[f] - 1).astype(F32)
        for l in range(LEV):
            n = f * LEV + l
            grid[n, 8:24, 0:COLS] = spread_v[f, l] * (row_part[:, n : n + 1] * col_part[l : l + 1, :])
    pltpu.make_async_copy(winds_v, winds_v, in_sem.at[3]).wait()
    for w in range(2):
        for l in range(LEV):
            grid[PAIRS + w * LEV + l, 8:24, 0:COLS] = winds_v[w, l]

    for s, (near, far) in enumerate(((8, 9), (23, 22))):
        for t in range(4):
            lanes = slice(128 * t, 128 * t + 128)
            halo_out[NEAR + 4 * s + t] = grid[0:PAIRS, near, lanes]
            halo_out[REST + 7 * s + t] = grid[0:PAIRS, far, lanes]
            halo_out[REST + 7 * s + 4 + t // 2, 8 * (t % 2) : 8 * (t % 2) + 8, :] = grid[
                PAIRS : PAIRS + 2 * LEV, near, lanes
            ]
    lane128 = lax.broadcasted_iota(jnp.int32, (1, 1, 128), 2)
    for s, (start, shift) in enumerate(((0, 0), (384, COLS - 2 - 384))):
        tile = grid[:, 8:24, start : start + 128]
        tile = jnp.where(jnp.logical_and(lane128 >= shift, lane128 < shift + 2), tile, 0.0)
        packed = fold(tile[:PAIRS]) + roll_blocks(fold(tile[PAIRS:]), 2 * PAIRS)
        halo_out[SIDES + s] = roll_blocks(packed, -shift)[0]

    def values(q, x):
        y = to_modes(x.reshape(PAIRS * ROWS, WIDE), table.at[FORWARD:EVALUATE])
        y = y.reshape(FIELDS, LEV, 2, 8, RANK)
        for f in range(FIELDS):
            for h in range(2):
                for l in range(LEV):
                    ybuf[2 * f + h, q, l] = y[f, l, h]

    @pl.when(polar)
    def _():
        load_forward.wait()
        values(0, grid[0:PAIRS, 8:24, :])

    pl.semaphore_wait(barrier, 4 + jnp.where(polar, LANES - 3, 0))

    def remote(src, dst, send, recv, lat, lon):
        return pltpu.make_async_remote_copy(
            src_ref=src, dst_ref=dst, send_sem=send, recv_sem=recv, device_id=(lat, lon), device_id_type=MESH
        )

    def halo_copy(start, count, to, which, lat, lon):
        return remote(
            halo_out.at[start : start + count], halo_in.at[pl.ds(to, count)], halo_send, halo_recv.at[which], lat, lon
        )

    def halo_arrival(start, stop, which):
        return remote(
            halo_out.at[start:stop], halo_in.at[start:stop], halo_send, halo_recv.at[which], b, west
        )

    halo_copy(NEAR, 4, NEAR + 4 * slot_n, 0, nb, nl).start()
    halo_copy(NEAR + 4, 4, NEAR + 4 * slot_s, 0, sb, sl).start()
    halo_copy(SIDES, 1, SIDES + 1, 0, b, west).start()
    halo_copy(SIDES + 1, 1, SIDES, 0, b, east_lane).start()

    def y_copy(o):
        return remote(ybuf.at[o], yr.at[i], y_send, y_recv, b, o)

    others = pl.ds(0, LANES - 1)

    def all_y():
        return remote(ybuf.at[others], yr.at[others], y_send, y_recv, b, west)

    def send_values():
        @pl.loop(1, LANES)
        def _(d):
            y_copy(plus(i, d)).start()

        yr[i] = ybuf[i]

    def c_copy(o):
        return remote(cb.at[o], yc.at[i], c_send, c_recv, b, o)

    def all_c():
        return remote(cb.at[others], yc.at[others], c_send, c_recv, b, west)

    def z_copy(q, j):
        return remote(zbuf.at[q, j], zr.at[q, i], z_send.at[q], z_recv.at[q], b, j)

    def all_z(q):
        return remote(zbuf.at[q, others], zr.at[q, others], z_send.at[q], z_recv.at[q], b, west)

    def own_rows(q):
        row = lax.broadcasted_iota(jnp.int32, (8, 128), 0)
        cutoff = jnp.zeros((8, 128), jnp.int32)
        for r in range(8):
            cutoff = jnp.where(row == r, cut_s[8 * own_half + r], cutoff)

        if q == 0:
            all_y().wait_recv()
        else:
            all_c().wait_recv()

        lanes = []
        for j in range(LANES):
            y = yr[j, q]
            if q == 1:
                ends = pltpu.roll(yc[j, 8:16, :], lax.rem(128 - 2 * LEV * (i // 2), 128), 1)
                edge_rows = jnp.where(row == 7 * own_half, 1.0, 0.0)
                y = jnp.concatenate(
                    [
                        y[l]
                        + ends[:, 2 * l : 2 * l + 1] * hm[0:1, :]
                        + ends[:, 2 * l + 1 : 2 * l + 2] * hm[1:2, :]
                        + edge_rows * yc[j, l : l + 1, :]
                        for l in range(LEV)
                    ],
                    axis=0,
                )
            lanes.append(y.reshape(LEV * 8, RANK))
        pairs = []
        over = over_lanes(lanes)
        for group, pair in enumerate(over):
            coef = to_modes(
                jnp.concatenate(pair, axis=1), table.at[TO_COEFS + 256 * group : TO_COEFS + 256 * (group + 1)]
            )
            wave = waves_of(group, lax.broadcasted_iota(jnp.int32, (8, 128), 1))
            keep = jnp.where(wave > cutoff, 2.0 / (COLS * LANES), 0.0)
            back = from_modes(
                coef * jnp.concatenate([keep] * LEV, axis=0),
                table.at[FROM_COEFS + 384 * group : FROM_COEFS + 384 * (group + 1)],
            )
            pairs.append((back[:, :RANK], back[:, RANK:]))
        for j, z in enumerate(to_lanes(pairs)):
            z = z.reshape(LEV, 8, RANK)
            zbuf[q, j] = z
            edge = jnp.where(own_half == 0, z[:, 0, :], z[:, 7, :])
            eb[j] = edge if q == 0 else eb[j] + edge

        @pl.loop(1, LANES)
        def _(d):
            z_copy(q, plus(i, d)).start()

        zr[q, i] = zbuf[q, i]

    def edge_sends():
        slot = jnp.where(own_half == 0, slot_n, slot_s)
        lat = jnp.where(own_half == 0, nb, sb)

        @pl.loop(0, LANES)
        def _(d):
            j = plus(i, d)
            lon = jnp.where(edge_over, plus(j, LANES // 2), j)
            here = jnp.logical_and(edge_over, lon == i)

            @pl.when(jnp.logical_not(here))
            def _():
                remote(eb.at[j], bz.at[slot, i // 2], b_send, b_recv.at[slot], lat, lon).start()

            @pl.when(here)
            def _():
                pltpu.make_async_copy(eb.at[j], bz.at[slot, i // 2], b_recv.at[slot]).start()

    def evaluate(z):
        return from_modes(z, table.at[EVALUATE : EVALUATE + 384], table.at[EVALUATE + 384 : TO_COEFS])

    def project(q, h):
        z = jnp.concatenate([zr[q, 2 * f + h, l] for f in range(FIELDS) for l in range(LEV)], axis=0)
        out = evaluate(z)
        return [[out[8 * (LEV * f + l) : 8 * (LEV * f + l + 1), :] for l in range(LEV)] for f in range(FIELDS)]

    def tendency_rows(h):
        @pl.loop(0, LEV)
        def _(l):
            lo = jnp.maximum(l - 1, 0)
            hi = jnp.minimum(l + 1, LEV - 1)
            half = jnp.concatenate([hm[h : h + 8, :]] * 4, axis=1)
            ew = grid[PAIRS + l, h : h + 8, :]
            nw = grid[PAIRS + LEV + l, h : h + 8, :]
            along_x, along_y = [], []
            for f in range(FIELDS):
                mid = grid[f * LEV + l, h : h + 8, :]
                along_x.append(half * (roll(mid, -1, 1) - roll(mid, 1, 1)))
                along_y.append(0.5 * (grid[f * LEV + l, h + 1 : h + 9, :] - grid[f * LEV + l, h - 1 : h + 7, :]))
            linked = (along_x[2], along_y[2], along_x[0] + along_y[1], None)
            for f in range(FIELDS):
                mid = grid[f * LEV + l, h : h + 8, :]
                mixed = grid[f * LEV + lo, h : h + 8, :] + grid[f * LEV + hi, h : h + 8, :] - 2.0 * mid
                t = -(ew * along_x[f] + nw * along_y[f]) + mixing * mixed
                if linked[f] is not None:
                    t = t - coupling * linked[f]
                tend[f * LEV + l, h - 8 : h, :] = time_step * t

    load_metric.wait()

    @pl.when(polar)
    def _():
        grid[0:PAIRS, 7:8, :] = jnp.zeros((PAIRS, 1, WIDE), F32)
        grid[0:PAIRS, 24:25, :] = jnp.zeros((PAIRS, 1, WIDE), F32)
        for part in range(2):
            tendency_rows(8 + 8 * part)
        values(1, tend[...])
        send_values()

    halo_arrival(NEAR, REST, 0).wait_recv()
    lane2 = lax.broadcasted_iota(jnp.int32, (1, 128), 1)
    row16 = lax.broadcasted_iota(jnp.int32, (PAIRS, 1), 0)
    is_v = jnp.logical_and(row16 >= LEV, row16 < 2 * LEV)
    is_temp = jnp.logical_and(row16 >= 2 * LEV, row16 < 3 * LEV)

    def flip(s, minus):
        sign = jnp.where(row16 < 2 * LEV, -1.0, 1.0) * minus
        return jnp.where(over_pole[s], sign, 1.0)

    def row_link(x):
        return jnp.where(is_v, roll(x, -LEV, 0), jnp.where(is_temp, roll(x, LEV, 0), 0.0))

    def wind(buffer, s, w):
        base = REST + 7 * s + 4
        rows = [buffer[base + t // 2, 8 * (t % 2) + LEV * w : 8 * (t % 2) + LEV * (w + 1), :] for t in range(4)]
        return jnp.concatenate([jnp.concatenate(rows, axis=1)] * FIELDS, axis=0)

    def row_of(buffer, start):
        return jnp.concatenate([buffer[start + t] for t in range(4)], axis=1)

    @pl.when(polar)
    def _():
        added = []
        for s, sign in ((0, 0.5 * time_step), (1, -0.5 * time_step)):
            ghost = flip(s, 1.0) * row_of(halo_in, NEAR + 4 * s)
            added.append(sign * (wind(halo_out, s, 1) * ghost + coupling * row_link(ghost)))
        y = to_modes(jnp.concatenate(added, axis=0), table.at[FORWARD:EVALUATE])
        for s in range(2):
            for f in range(FIELDS):
                cb[2 * f + s, 0:LEV, :] = y[(s * FIELDS + f) * LEV : (s * FIELDS + f + 1) * LEV, :]
        ends = []
        for side, sign in ((0, -1.0), (1, 1.0)):
            came = halo_in[SIDES + side]
            along_x = (sign * hm[8:24, :]) * (roll(came, -1, 1) if side == 0 else came)
            mine = jnp.where(
                jnp.logical_and(lane2 >= 2 * PAIRS, lane2 < 2 * (PAIRS + LEV)), halo_out[SIDES + side], 0.0
            )
            ew = sum(roll(mine, 2 * LEV * f - 2 * PAIRS - side, 1) for f in range(FIELDS))
            linked = jnp.where(
                lane2 < 2 * LEV,
                roll(along_x, -4 * LEV, 1),
                jnp.where(
                    jnp.logical_and(lane2 >= 4 * LEV, lane2 < 6 * LEV), roll(along_x, 4 * LEV, 1), 0.0
                ),
            )
            ends.append(time_step * (-ew * along_x - coupling * linked))
        ends = jnp.where(lax.rem(lane2, 2) == 0, ends[0], roll(ends[1], 1, 1))
        for f in range(FIELDS):
            for h in range(2):
                cb[2 * f + h, 8:16, :] = ends[8 * h : 8 * h + 8, :]

        @pl.loop(1, LANES)
        def _(d):
            c_copy(plus(i, d)).start()

        yc[i] = cb[i]

    @pl.when(polar)
    def _():
        load_cut.wait()
        load_others.wait()
        own_rows(0)

    from_west = roll(halo_in[SIDES], 126, 1)
    from_east = roll(halo_in[SIDES + 1], COLS - 384, 1)
    both = jnp.where(jnp.logical_and(lane2 >= 66, lane2 < 114), from_east, from_west)[None]
    for width in (2, 4, 8):
        both = jnp.concatenate([both, roll_blocks(both, -width)], axis=0)
    both = jnp.concatenate([both, roll_blocks(both, -16), roll_blocks(both, -32)], axis=0)
    in_halo = jnp.logical_or(jnp.logical_and(lane128 >= 66, lane128 < 68), lane128 >= 126)
    grid[:, 8:24, 384:512] = jnp.where(in_halo, both, grid[:, 8:24, 384:512])
    for s, near in enumerate((8, 23)):
        halo_out[REST + 7 * s + 6] = grid[0:PAIRS, near, 384:512]
    halo_copy(REST, 7, REST + 7 * slot_n, 1, nb, nl).start()
    halo_copy(REST + 7, 7, REST + 7 * slot_s, 1, sb, sl).start()

    @pl.when(polar)
    def _():
        own_rows(1)
        edge_sends()

    halo_arrival(REST, BLOCKS, 1).wait_recv()
    edge_row = (7, 24)
    edge_probe = []
    for s in range(2):
        edge_probe.append(
            jnp.concatenate([halo_in[NEAR + 4 * s + t] for t in range(3)] + [halo_in[REST + 7 * s + 6]], axis=1)
        )
        grid[0:PAIRS, edge_row[s], :] = flip(s, 1.0) * edge_probe[s]

    for part in range(2):
        tendency_rows(8 + 8 * part)

    def edge_weights(s, a):
        return -wind(halo_in, s, 1) * a - coupling * row_link(a)

    for s, inward in ((0, 1.0), (1, -1.0)):
        mid = edge_probe[s]
        half = jnp.concatenate([hm[edge_row[s] : edge_row[s] + 1, :]] * 4, axis=1)
        along_x = half * (roll(mid, -1, 1) - roll(mid, 1, 1))
        turn = jnp.where(over_pole[s], -0.5 * inward, 0.5 * inward)
        along_y = turn * (flip(s, 1.0) * row_of(halo_out, NEAR + 4 * s) - row_of(halo_in, REST + 7 * s))
        linked = jnp.where(row16 < LEV, roll(along_x, -2 * LEV, 0), row_link(along_y))
        linked = linked + jnp.where(is_temp, roll(along_x, 2 * LEV, 0), 0.0)
        up = jnp.where(lax.rem(row16, LEV) == 0, mid, roll(mid, 1, 0))
        down = jnp.where(lax.rem(row16, LEV) == LEV - 1, mid, roll(mid, -1, 0))
        t = -(wind(halo_in, s, 0) * along_x + wind(halo_in, s, 1) * along_y) - coupling * linked
        a = mid + time_step * (t + mixing * (up + down - 2.0 * mid))
        gy[0:PAIRS, edge_row[s], :] = flip(s, -1.0) * edge_weights(s, a)

    def row_weights(a, nw):
        return (
            -nw * a[0],
            -nw * a[1] - coupling * a[2],
            -nw * a[2] - coupling * a[1],
            -nw * a[3],
        )

    def put_weights(l, h, a):
        for f, weight in enumerate(row_weights(a, grid[PAIRS + LEV + l, h : h + 8, :])):
            gy[f * LEV + l, h : h + 8, :] = weight

    @pl.when(polar)
    def _():
        all_z(0).wait_recv()
        for h in (8, 16):
            taken = project(0, h // 8 - 1)
            for l in range(LEV):
                for f in range(FIELDS):
                    n, rows = f * LEV + l, slice(h - 8, h)
                    adj[n, rows, :] = grid[n, h : h + 8, :] + tend[n, rows, :] - taken[f][l]
        all_z(1).wait_recv()
        for h in (8, 16):
            taken = project(1, h // 8 - 1)
            for l in range(LEV):
                a = []
                for f in range(FIELDS):
                    n, rows = f * LEV + l, slice(h - 8, h)
                    change = tend[n, rows, :] - taken[f][l]
                    tend[n, rows, :] = change
                    tan_out[f, l, rows, :] = (grid[n, h : h + 8, :] + change)[:, :COLS]
                    a.append(adj[n, rows, :] - taken[f][l])
                    adj[n, rows, :] = a[f]
                put_weights(l, h, a)

    @pl.when(jnp.logical_not(polar))
    def _():
        @pl.loop(0, LEV)
        def _(l):
            for h in (8, 16):
                a = []
                for f in range(FIELDS):
                    n, rows = f * LEV + l, slice(h - 8, h)
                    a.append(grid[n, h : h + 8, :] + tend[n, rows, :])
                    tan_out[f, l, rows, :] = a[f][:, :COLS]
                    adj[n, rows, :] = a[f]
                put_weights(l, h, a)

    @pl.loop(0, LEV)
    def _(l):
        lo = jnp.maximum(l - 1, 0)
        hi = jnp.minimum(l + 1, LEV - 1)
        for h in (8, 16):
            rows = slice(h - 8, h)
            half = jnp.concatenate([hm[h : h + 8, :]] * 4, axis=1)
            ew = grid[PAIRS + l, h : h + 8, :]
            a = [adj[f * LEV + l, rows, :] for f in range(FIELDS)]
            col_weights = (
                -ew * a[0] - coupling * a[2],
                -ew * a[1],
                -ew * a[2] - coupling * a[0],
                -ew * a[3],
            )
            for f in range(FIELDS):
                n = f * LEV + l
                back = half * (roll(col_weights[f], 1, 1) - roll(col_weights[f], -1, 1))
                back = back + 0.5 * (gy[n, h - 1 : h + 7, :] - gy[n, h + 1 : h + 9, :])
                back = back + mixing * (adj[f * LEV + lo, rows, :] + adj[f * LEV + hi, rows, :] - 2.0 * a[f])
                diag = grid[n, h : h + 8, :] * (tend[n, rows, :] + time_step * back)
                diag_out[f, l, rows, :] = diag[:, :COLS]

    @pl.when(jnp.logical_and(near_polar, jnp.logical_not(polar)))
    def _():
        load_part.wait()

    for s, wanted in enumerate((above_polar, below_polar)):
        @pl.when(wanted)
        def _():
            remote(bz.at[s], bz.at[s], b_send, b_recv.at[s], nb, nl).wait_recv()
            taken = evaluate(jnp.concatenate([bz[s, f] for f in range(FIELDS)], axis=0))
            weight = flip(s, -1.0) * edge_weights(s, taken)
            row = 15 * s
            less = ((0.5, -0.5)[s] * time_step) * grid[0:PAIRS, 8 + row, :] * weight
            for f in range(FIELDS):
                diag_out[f, :, row, :] = diag_out[f, :, row, :] - less[f * LEV : (f + 1) * LEV, :COLS]

    halo_arrival(0, BLOCKS, 0).wait_send()

    @pl.when(polar)
    def _():
        all_y().wait_send()
        all_c().wait_send()
        for q in range(2):
            all_z(q).wait_send()

        @pl.when(edge_over)
        def _():
            remote(eb.at[others], eb.at[others], b_send, b_recv.at[0], b, west).wait_send()

        @pl.when(jnp.logical_not(edge_over))
        def _():
            remote(eb, eb, b_send, b_recv.at[0], b, west).wait_send()


def hand_out(tan_in, diag_in, tan_out, diag_out, sem):
    copies = [
        pltpu.make_async_copy(src, dst, sem.at[n])
        for n, (src, dst) in enumerate(((tan_in, tan_out), (diag_in, diag_out)))
    ]
    for copy in copies:
        copy.start()
    for copy in copies:
        copy.wait()


def per_device(bands, row_signs, col_signs, spread, east_wind, north_wind, cutoffs):
    any_spec = pl.BlockSpec(memory_space=pl.ANY)
    out = jax.ShapeDtypeStruct((FIELDS, LEV, ROWS, COLS), F32)
    tables = [jnp.asarray(half_metric(bands)), jnp.asarray(mode_factors())]
    operands = (spread, east_wind, north_wind, row_signs, col_signs, cutoffs, *tables)
    vmem = pltpu.VMEM
    dma = pltpu.SemaphoreType.DMA
    held = pltpu.VMEM(out.shape, F32)
    results = pl.pallas_call(
        functools.partial(kernel, bands),
        out_shape=(held, held),
        in_specs=[any_spec] * 8,
        out_specs=(pl.BlockSpec(memory_space=pltpu.VMEM),) * 2,
        scratch_shapes=[
            vmem((FIELDS, LEV, ROWS, COLS), F32),
            vmem((2, LEV, ROWS, COLS), F32),
            vmem((FIELDS, LEV, ROWS), jnp.int32),
            vmem((FIELDS, LEV, COLS), jnp.int32),
            pltpu.SMEM((ROWS,), jnp.int32),
            vmem((32, 128), F32),
            vmem((TABLE_ROWS, 2 * RANK), BF16),
            vmem((PAIRS + 2 * LEV, 32, WIDE), F32),
            vmem((BLOCKS, 16, 128), F32),
            vmem((BLOCKS, 16, 128), F32),
            vmem((LANES, 2, LEV, 8, RANK), F32),
            vmem((LANES, 2, LEV, 8, RANK), F32),
            vmem((LANES, 16, RANK), F32),
            vmem((LANES, 16, RANK), F32),
            vmem((2, LANES, LEV, 8, RANK), F32),
            vmem((2, LANES, LEV, 8, RANK), F32),
            vmem((LANES, LEV, RANK), F32),
            vmem((2, FIELDS, LEV, RANK), F32),
            vmem((PAIRS, ROWS, WIDE), F32),
            vmem((PAIRS, ROWS, WIDE), F32),
            vmem((PAIRS, 32, WIDE), F32),
            dma((8,)),
            dma,
            dma((2,)),
            dma,
            dma,
            dma,
            dma,
            dma((2,)),
            dma((2,)),
            dma,
            dma((2,)),
        ],
        compiler_params=pltpu.CompilerParams(
            collective_id=0, has_side_effects=True, vmem_limit_bytes=32 * 2**20
        ),
        cost_estimate=pl.CostEstimate(flops=10**9, bytes_accessed=4 * 10**6, transcendentals=0),
    )(*(pltpu.with_memory_space_constraint(x, pltpu.HBM) for x in operands))
    return pl.pallas_call(
        hand_out,
        out_shape=(out, out),
        in_specs=[any_spec] * 2,
        out_specs=(any_spec, any_spec),
        scratch_shapes=[dma((2,))],
        compiler_params=pltpu.CompilerParams(vmem_limit_bytes=2**20),
    )(*(pltpu.with_memory_space_constraint(x, pltpu.VMEM) for x in results))


def solution(mesh):
    return jax.shard_map(
        functools.partial(per_device, mesh.shape["lat"]),
        mesh=mesh,
        in_specs=(
            P(None, None, "lat"),
            P(None, None, "lon"),
            P(None, None, "lat", "lon"),
            P(None, "lat", "lon"),
            P(None, "lat", "lon"),
            P("lat"),
        ),
        out_specs=(P(None, None, "lat", "lon"), P(None, None, "lat", "lon")),
        check_vma=False,
    )
```

```python
import functools

import jax
import jax.numpy as jnp
import ml_dtypes
import numpy as np
from jax import lax
from jax.experimental import pallas as pl
from jax.experimental.pallas import tpu as pltpu
from jax.sharding import PartitionSpec as P

KTOP = 256
POLAR = 32
RANK = 128
ROWS = 16
COLS = 450
WIDE = 512
LANES = 8
FIELDS = 4
LEV = 4
PAIRS = FIELDS * LEV

time_step = 0.5
coupling = 0.5
mixing = 0.2
metric_cap = 4.0

FORWARD, EVALUATE, TO_COEFS, FROM_COEFS, TABLE_ROWS = 0, 512, 1280, 2304, 3840
NEAR, SIDES, REST, BLOCKS = 0, 8, 10, 24

MESH = pl.DeviceIdType.MESH
F32 = jnp.float32
BF16 = jnp.bfloat16


def split_table(table):
    high = table.astype(ml_dtypes.bfloat16)
    low = (table - high.astype(np.float64)).astype(ml_dtypes.bfloat16)
    return high, low


def waves_of(group, lane_index):
    place = lane_index % 64
    second = place // 32
    other = (8 - group) if group else 4
    residue = group + second * (other - group)
    return 8 * (place % 32) + residue + (8 * (1 - second) if group == 0 else 0)


@functools.lru_cache(None)
def mode_factors():
    total = COLS * LANES
    size = COLS + 2
    place = np.arange(size, dtype=np.float64)
    width = (KTOP + 0.5) / total
    diag = ((size - 1 - 2 * place) / 2) ** 2 * np.cos(2 * np.pi * width)
    side = place[1:] * (size - place[1:]) / 2
    vectors = np.linalg.eigh(np.diag(diag) + np.diag(side, 1) + np.diag(side, -1))[1]
    basis = vectors[:, ::-1][:, :RANK]
    basis = basis * np.where(basis[size // 2] < 0, -1.0, 1.0)
    weights = []
    for group in range(4):
        waves = waves_of(group, np.arange(64))
        angle = 2 * np.pi / total * ((np.arange(size)[:, None] - 1) * waves[None, :] % total)
        alpha, beta = basis.T @ np.cos(angle), basis.T @ np.sin(angle)
        if group:
            sign = np.where(np.arange(64) < 32, 1.0, -1.0)
            top, low = (alpha, beta), (sign * beta, -sign * alpha)
        else:
            use = np.where(np.arange(64) < 32, 1.0, 0.0)
            top, low = (use * alpha, use * beta), ((1 - use) * alpha, (1 - use) * beta)
        weights.append(np.concatenate([np.concatenate(top, axis=1), np.concatenate(low, axis=1)], axis=0))
    weights = np.round(np.stack(weights) * 2.0**22) / 2.0**22
    wide = np.zeros((RANK, WIDE))
    wide[:, : COLS + 1] = basis[1:].T
    wide[:, WIDE - 1] = basis[0]
    wide = np.round(wide * 2.0**26) / 2.0**26
    wide_h, wide_l = split_table(wide)
    own = np.where(np.arange(WIDE)[:, None] < COLS, 1, 0).astype(ml_dtypes.bfloat16)
    high, low = split_table(weights)
    back = np.concatenate([np.swapaxes(part, 1, 2) for part in (high, low, high)], axis=1)
    evaluate = np.concatenate([wide_h, wide_l, wide_h], axis=0)
    return np.concatenate(
        [
            np.concatenate([wide_h.T * own, wide_l.T * own], axis=1),
            evaluate[:, : WIDE // 2],
            evaluate[:, WIDE // 2 :],
            np.concatenate([high, low], axis=2).reshape(-1, 2 * RANK),
            back.reshape(-1, 2 * RANK),
        ],
        axis=0,
    )


ROOT = float(np.sqrt(0.5))


def over_lanes(y):
    s = [y[j] + y[j + 4] for j in range(4)]
    d = [y[j] - y[j + 4] for j in range(4)]
    even, odd = s[0] + s[2], s[1] + s[3]
    minus, plus = ROOT * (d[1] - d[3]), ROOT * (d[1] + d[3])
    return [
        (even + odd, even - odd),
        (d[0] + minus, -(d[2] + plus)),
        (s[0] - s[2], s[3] - s[1]),
        (d[0] - minus, d[2] - plus),
    ]


def to_lanes(pairs):
    (y0, y4), (u1, v1), (u2, v2), (u3, v3) = pairs
    even, odd = y0 + y4, y0 - y4
    s = [even + u2, odd - v2, even - u2, odd + v2]
    du, sv = ROOT * (u1 - u3), ROOT * (v1 + v3)
    d = [u1 + u3, du - sv, v3 - v1, -du - sv]
    return [s[j] + d[j] for j in range(4)] + [s[j] - d[j] for j in range(4)]


@functools.lru_cache(None)
def half_metric(bands):
    total = bands * ROWS
    rows = np.clip(np.arange(bands)[:, None] * ROWS - 8 + np.arange(32)[None, :], 0, total - 1)
    metric = np.minimum(1.0 / np.cos(np.pi * ((rows + 0.5) / total - 0.5)), metric_cap)
    table = np.broadcast_to((0.5 * metric).astype(np.float32)[:, :, None], (bands, 32, 128)).copy()
    forward = mode_factors()[FORWARD : FORWARD + WIDE].astype(np.float32)
    for row, col in enumerate((0, COLS - 1)):
        table[:, row] = forward[col, :RANK] + forward[col, RANK:]
    return table


def dot_cols(a, b):
    return lax.dot_general(a, b, (((1,), (0,)), ((), ())), preferred_element_type=F32)


def split(x):
    high = x.astype(BF16)
    return high, (x - high.astype(F32)).astype(BF16)


def to_modes(x, table):
    xh, xl = split(x)
    half = table.shape[1] // 2
    wide = dot_cols(xh, table[...])
    return wide[:, :half] + wide[:, half:] + dot_cols(xl, table[:, 0:half])


def from_modes(z, *tables):
    zh, zl = split(z)
    three = jnp.concatenate([zh, zh, zl], axis=1)
    return jnp.concatenate([dot_cols(three, table[...]) for table in tables], axis=1)


def roll(x, shift, axis):
    return pltpu.roll(x, shift % x.shape[axis], axis)


def roll_blocks(x, shift):
    return roll(x.reshape(x.shape[0] * x.shape[1], x.shape[2]), shift, 1).reshape(x.shape)


def fold(x):
    while x.shape[0] > 1:
        half = x.shape[0] // 2
        x = x[:half] + roll_blocks(x[half:], 2 * half)
    return x


def kernel(
    bands, spread, east, north, rs, cs, cut, metric, table_in, tan_out, diag_out,
    spread_v, winds_v, rs_v, cs_v, cut_s, hm, table,
    grid, halo_out, halo_in, ybuf, yr, cb, yc, zbuf, zr, eb, bz,
    tend, adj, gy,
    in_sem, halo_send, halo_recv, y_send, y_recv, c_send, c_recv, z_send, z_recv, b_send, b_recv,
):
    b = lax.axis_index("lat")
    i = lax.axis_index("lon")
    caps = POLAR // ROWS
    is_north = b == 0
    is_south = b == bands - 1
    polar = jnp.logical_or(b < caps, b >= bands - caps)
    above_polar = jnp.logical_or(b <= caps, is_south)
    below_polar = jnp.logical_or(b >= bands - caps - 1, is_north)
    near_polar = jnp.logical_or(above_polar, below_polar)
    across = lax.rem(i + LANES // 2, LANES)
    west = lax.rem(i + LANES - 1, LANES)
    east_lane = lax.rem(i + 1, LANES)
    nb = jnp.where(is_north, 0, b - 1)
    nl = jnp.where(is_north, across, i)
    sb = jnp.where(is_south, bands - 1, b + 1)
    sl = jnp.where(is_south, across, i)
    slot_n = jnp.where(is_north, 0, 1)
    slot_s = jnp.where(is_south, 1, 0)
    own_half = lax.rem(i, 2)
    edge_over = jnp.where(own_half == 0, is_north, is_south)
    over_pole = (is_north, is_south)

    def plus(lane, d):
        return lax.rem(lane + d, LANES)

    load_spread = [
        pltpu.make_async_copy(spread.at[f], spread_v.at[f], in_sem.at[8 + f]) for f in range(FIELDS)
    ]
    load_rows = pltpu.make_async_copy(rs, rs_v, in_sem.at[1])
    load_cols = pltpu.make_async_copy(cs, cs_v, in_sem.at[2])
    load_metric = pltpu.make_async_copy(metric.at[b], hm, in_sem.at[4])
    load_cut = pltpu.make_async_copy(cut, cut_s, in_sem.at[5])

    def load_table(start, stop, sem):
        return pltpu.make_async_copy(table_in.at[start:stop], table.at[start:stop], in_sem.at[sem])

    load_forward = load_table(FORWARD, EVALUATE, 6)
    load_others = load_table(EVALUATE, TABLE_ROWS, 7)
    load_part = load_table(EVALUATE, TO_COEFS, 7)
    load_rows.start()
    load_cols.start()
    for load in load_spread:
        load.start()
    pltpu.make_async_copy(east, winds_v.at[0], in_sem.at[3]).start()
    pltpu.make_async_copy(north, winds_v.at[1], in_sem.at[3]).start()
    load_metric.start()

    barrier = pltpu.get_barrier_semaphore()

    def greet(lat, lon):
        pl.semaphore_signal(barrier, inc=1, device_id=(lat, lon), device_id_type=MESH)

    greet(nb, nl)
    greet(sb, sl)
    greet(b, west)
    greet(b, east_lane)

    @pl.when(polar)
    def _():
        @pl.loop(2, LANES - 1)
        def _(d):
            greet(b, plus(i, d))

        load_forward.start()
        load_cut.start()

    @pl.when(jnp.logical_and(near_polar, jnp.logical_not(polar)))
    def _():
        load_part.start()

    load_rows.wait()
    load_cols.wait()
    grid[:, 8:24, 384:512] = jnp.zeros((PAIRS + 2 * LEV, ROWS, 128), F32)
    row_part = jnp.concatenate([rs_v[f] for f in range(FIELDS)], axis=0)
    row_part = (2 * row_part - 1).astype(F32).T
    for f in range(FIELDS):
        col_part = (2 * cs_v[f] - 1).astype(F32)
        load_spread[f].wait()
        for l in range(LEV):
            n = f * LEV + l
            grid[n, 8:24, 0:COLS] = spread_v[f, l] * (row_part[:, n : n + 1] * col_part[l : l + 1, :])

    @pl.when(polar)
    def _():
        load_others.start()

    pltpu.make_async_copy(winds_v, winds_v, in_sem.at[3]).wait()
    for w in range(2):
        for l in range(LEV):
            grid[PAIRS + w * LEV + l, 8:24, 0:COLS] = winds_v[w, l]

    for s, (near, far) in enumerate(((8, 9), (23, 22))):
        for t in range(4):
            lanes = slice(128 * t, 128 * t + 128)
            halo_out[NEAR + 4 * s + t] = grid[0:PAIRS, near, lanes]
            halo_out[REST + 7 * s + t] = grid[0:PAIRS, far, lanes]
            halo_out[REST + 7 * s + 4 + t // 2, 8 * (t % 2) : 8 * (t % 2) + 8, :] = grid[
                PAIRS : PAIRS + 2 * LEV, near, lanes
            ]
    lane128 = lax.broadcasted_iota(jnp.int32, (1, 1, 128), 2)
    for s, (start, shift) in enumerate(((0, 0), (384, COLS - 2 - 384))):
        tile = grid[:, 8:24, start : start + 128]
        tile = jnp.where(jnp.logical_and(lane128 >= shift, lane128 < shift + 2), tile, 0.0)
        packed = fold(tile[:PAIRS]) + roll_blocks(fold(tile[PAIRS:]), 2 * PAIRS)
        halo_out[SIDES + s] = roll_blocks(packed, -shift)[0]

    pl.semaphore_wait(barrier, 4 + jnp.where(polar, LANES - 3, 0))

    def remote(src, dst, send, recv, lat, lon):
        return pltpu.make_async_remote_copy(
            src_ref=src, dst_ref=dst, send_sem=send, recv_sem=recv, device_id=(lat, lon), device_id_type=MESH
        )

    def halo_copy(start, count, to, which, lat, lon):
        return remote(
            halo_out.at[start : start + count], halo_in.at[pl.ds(to, count)], halo_send, halo_recv.at[which], lat, lon
        )

    def halo_arrival(start, stop, which):
        return remote(
            halo_out.at[start:stop], halo_in.at[start:stop], halo_send, halo_recv.at[which], b, west
        )

    halo_copy(NEAR, 4, NEAR + 4 * slot_n, 0, nb, nl).start()
    halo_copy(NEAR + 4, 4, NEAR + 4 * slot_s, 0, sb, sl).start()
    halo_copy(SIDES, 1, SIDES + 1, 0, b, west).start()
    halo_copy(SIDES + 1, 1, SIDES, 0, b, east_lane).start()

    def y_copy(o):
        return remote(ybuf.at[o], yr.at[i], y_send, y_recv, b, o)

    others = pl.ds(0, LANES - 1)

    def all_y():
        return remote(ybuf.at[others], yr.at[others], y_send, y_recv, b, west)

    def send_values():
        @pl.loop(1, LANES)
        def _(d):
            y_copy(plus(i, d)).start()

        yr[i] = ybuf[i]

    def c_copy(o):
        return remote(cb.at[o], yc.at[i], c_send, c_recv, b, o)

    def all_c():
        return remote(cb.at[others], yc.at[others], c_send, c_recv, b, west)

    def z_copy(q, j):
        return remote(zbuf.at[q, j], zr.at[q, i], z_send.at[q], z_recv.at[q], b, j)

    def all_z(q):
        return remote(zbuf.at[q, others], zr.at[q, others], z_send.at[q], z_recv.at[q], b, west)

    def own_rows(q):
        row = lax.broadcasted_iota(jnp.int32, (8, 128), 0)
        cutoff = jnp.zeros((8, 128), jnp.int32)
        for r in range(8):
            cutoff = jnp.where(row == r, cut_s[8 * own_half + r], cutoff)

        if q == 0:
            all_y().wait_recv()
        else:
            all_c().wait_recv()

        lanes = []
        for j in range(LANES):
            y = yr[j, q]
            if q == 1:
                ends = pltpu.roll(yc[j, 8:16, :], lax.rem(128 - 2 * LEV * (i // 2), 128), 1)
                edge_rows = jnp.where(row == 7 * own_half, 1.0, 0.0)
                y = jnp.concatenate(
                    [
                        y[l]
                        + ends[:, 2 * l : 2 * l + 1] * hm[0:1, :]
                        + ends[:, 2 * l + 1 : 2 * l + 2] * hm[1:2, :]
                        + edge_rows * yc[j, l : l + 1, :]
                        for l in range(LEV)
                    ],
                    axis=0,
                )
            lanes.append(y.reshape(LEV * 8, RANK))
        coefs = [
            to_modes(jnp.concatenate(pair, axis=1), table.at[TO_COEFS + 256 * group : TO_COEFS + 256 * (group + 1)])
            for group, pair in enumerate(over_lanes(lanes))
        ]
        kept = []
        for group, coef in enumerate(coefs):
            wave = waves_of(group, lax.broadcasted_iota(jnp.int32, (8, 128), 1))
            keep = jnp.where(wave > cutoff, 2.0 / (COLS * LANES), 0.0)
            kept.append(coef * jnp.concatenate([keep] * LEV, axis=0))
        backs = [
            from_modes(coef, table.at[FROM_COEFS + 384 * group : FROM_COEFS + 384 * (group + 1)])
            for group, coef in enumerate(kept)
        ]
        pairs = [(back[:, :RANK], back[:, RANK:]) for back in backs]
        for j, z in enumerate(to_lanes(pairs)):
            z = z.reshape(LEV, 8, RANK)
            zbuf[q, j] = z
            edge = jnp.where(own_half == 0, z[:, 0, :], z[:, 7, :])
            eb[j] = edge if q == 0 else eb[j] + edge

        @pl.loop(1, LANES)
        def _(d):
            z_copy(q, plus(i, d)).start()

        zr[q, i] = zbuf[q, i]

    def edge_sends():
        slot = jnp.where(own_half == 0, slot_n, slot_s)
        lat = jnp.where(own_half == 0, nb, sb)

        @pl.loop(0, LANES)
        def _(d):
            j = plus(i, d)
            lon = jnp.where(edge_over, plus(j, LANES // 2), j)
            here = jnp.logical_and(edge_over, lon == i)

            @pl.when(jnp.logical_not(here))
            def _():
                remote(eb.at[j], bz.at[slot, i // 2], b_send, b_recv.at[slot], lat, lon).start()

            @pl.when(here)
            def _():
                pltpu.make_async_copy(eb.at[j], bz.at[slot, i // 2], b_recv.at[slot]).start()

    def evaluate(z):
        return from_modes(z, table.at[EVALUATE : EVALUATE + 384], table.at[EVALUATE + 384 : TO_COEFS])

    def project(q, h):
        z = jnp.concatenate([zr[q, 2 * f + h, l] for f in range(FIELDS) for l in range(LEV)], axis=0)
        out = evaluate(z)
        return [[out[8 * (LEV * f + l) : 8 * (LEV * f + l + 1), :] for l in range(LEV)] for f in range(FIELDS)]

    def tendency_rows(h):
        @pl.loop(0, LEV)
        def _(l):
            lo = jnp.maximum(l - 1, 0)
            hi = jnp.minimum(l + 1, LEV - 1)
            half = jnp.concatenate([hm[h : h + 8, :]] * 4, axis=1)
            ew = grid[PAIRS + l, h : h + 8, :]
            nw = grid[PAIRS + LEV + l, h : h + 8, :]
            along_x, along_y = [], []
            for f in range(FIELDS):
                mid = grid[f * LEV + l, h : h + 8, :]
                along_x.append(half * (roll(mid, -1, 1) - roll(mid, 1, 1)))
                along_y.append(0.5 * (grid[f * LEV + l, h + 1 : h + 9, :] - grid[f * LEV + l, h - 1 : h + 7, :]))
            linked = (along_x[2], along_y[2], along_x[0] + along_y[1], None)
            for f in range(FIELDS):
                mid = grid[f * LEV + l, h : h + 8, :]
                mixed = grid[f * LEV + lo, h : h + 8, :] + grid[f * LEV + hi, h : h + 8, :] - 2.0 * mid
                t = -(ew * along_x[f] + nw * along_y[f]) + mixing * mixed
                if linked[f] is not None:
                    t = t - coupling * linked[f]
                tend[f * LEV + l, h - 8 : h, :] = time_step * t

    load_metric.wait()

    @pl.when(polar)
    def _():
        grid[0:PAIRS, 7:8, :] = jnp.zeros((PAIRS, 1, WIDE), F32)
        grid[0:PAIRS, 24:25, :] = jnp.zeros((PAIRS, 1, WIDE), F32)
        for part in range(2):
            tendency_rows(8 + 8 * part)
        load_forward.wait()
        probe = grid[0:PAIRS, 8:24, :].reshape(PAIRS * ROWS, WIDE)
        change = tend[...].reshape(PAIRS * ROWS, WIDE)
        y = to_modes(jnp.concatenate([probe, change], axis=0), table.at[FORWARD:EVALUATE])
        y = y.reshape(2, FIELDS, LEV, 2, 8, RANK)
        for q in range(2):
            for f in range(FIELDS):
                for h in range(2):
                    for l in range(LEV):
                        ybuf[2 * f + h, q, l] = y[q, f, l, h]
        send_values()

    halo_arrival(NEAR, REST, 0).wait_recv()
    lane2 = lax.broadcasted_iota(jnp.int32, (1, 128), 1)
    row16 = lax.broadcasted_iota(jnp.int32, (PAIRS, 1), 0)
    is_v = jnp.logical_and(row16 >= LEV, row16 < 2 * LEV)
    is_temp = jnp.logical_and(row16 >= 2 * LEV, row16 < 3 * LEV)

    def flip(s, minus):
        sign = jnp.where(row16 < 2 * LEV, -1.0, 1.0) * minus
        return jnp.where(over_pole[s], sign, 1.0)

    def row_link(x):
        return jnp.where(is_v, roll(x, -LEV, 0), jnp.where(is_temp, roll(x, LEV, 0), 0.0))

    def wind(buffer, s, w):
        base = REST + 7 * s + 4
        rows = [buffer[base + t // 2, 8 * (t % 2) + LEV * w : 8 * (t % 2) + LEV * (w + 1), :] for t in range(4)]
        return jnp.concatenate([jnp.concatenate(rows, axis=1)] * FIELDS, axis=0)

    def row_of(buffer, start):
        return jnp.concatenate([buffer[start + t] for t in range(4)], axis=1)

    @pl.when(polar)
    def _():
        added = []
        for s, sign in ((0, 0.5 * time_step), (1, -0.5 * time_step)):
            ghost = flip(s, 1.0) * row_of(halo_in, NEAR + 4 * s)
            added.append(sign * (wind(halo_out, s, 1) * ghost + coupling * row_link(ghost)))
        y = to_modes(jnp.concatenate(added, axis=0), table.at[FORWARD:EVALUATE])
        for s in range(2):
            for f in range(FIELDS):
                cb[2 * f + s, 0:LEV, :] = y[(s * FIELDS + f) * LEV : (s * FIELDS + f + 1) * LEV, :]
        ends = []
        for side, sign in ((0, -1.0), (1, 1.0)):
            came = halo_in[SIDES + side]
            along_x = (sign * hm[8:24, :]) * (roll(came, -1, 1) if side == 0 else came)
            mine = jnp.where(
                jnp.logical_and(lane2 >= 2 * PAIRS, lane2 < 2 * (PAIRS + LEV)), halo_out[SIDES + side], 0.0
            )
            ew = sum(roll(mine, 2 * LEV * f - 2 * PAIRS - side, 1) for f in range(FIELDS))
            linked = jnp.where(
                lane2 < 2 * LEV,
                roll(along_x, -4 * LEV, 1),
                jnp.where(
                    jnp.logical_and(lane2 >= 4 * LEV, lane2 < 6 * LEV), roll(along_x, 4 * LEV, 1), 0.0
                ),
            )
            ends.append(time_step * (-ew * along_x - coupling * linked))
        ends = jnp.where(lax.rem(lane2, 2) == 0, ends[0], roll(ends[1], 1, 1))
        for f in range(FIELDS):
            for h in range(2):
                cb[2 * f + h, 8:16, :] = ends[8 * h : 8 * h + 8, :]

        @pl.loop(1, LANES)
        def _(d):
            c_copy(plus(i, d)).start()

        yc[i] = cb[i]

    @pl.when(polar)
    def _():
        load_cut.wait()
        load_others.wait()
        own_rows(0)

    from_west = roll(halo_in[SIDES], 126, 1)
    from_east = roll(halo_in[SIDES + 1], COLS - 384, 1)
    both = jnp.where(jnp.logical_and(lane2 >= 66, lane2 < 114), from_east, from_west)[None]
    for width in (2, 4, 8):
        both = jnp.concatenate([both, roll_blocks(both, -width)], axis=0)
    both = jnp.concatenate([both, roll_blocks(both, -16), roll_blocks(both, -32)], axis=0)
    in_halo = jnp.logical_or(jnp.logical_and(lane128 >= 66, lane128 < 68), lane128 >= 126)
    grid[:, 8:24, 384:512] = jnp.where(in_halo, both, grid[:, 8:24, 384:512])
    for s, near in enumerate((8, 23)):
        halo_out[REST + 7 * s + 6] = grid[0:PAIRS, near, 384:512]
    halo_copy(REST, 7, REST + 7 * slot_n, 1, nb, nl).start()
    halo_copy(REST + 7, 7, REST + 7 * slot_s, 1, sb, sl).start()

    @pl.when(polar)
    def _():
        own_rows(1)
        edge_sends()

    halo_arrival(REST, BLOCKS, 1).wait_recv()
    edge_row = (7, 24)
    edge_probe = []
    for s in range(2):
        edge_probe.append(
            jnp.concatenate([halo_in[NEAR + 4 * s + t] for t in range(3)] + [halo_in[REST + 7 * s + 6]], axis=1)
        )
        grid[0:PAIRS, edge_row[s], :] = flip(s, 1.0) * edge_probe[s]

    for part in range(2):
        tendency_rows(8 + 8 * part)

    def edge_weights(s, a):
        return -wind(halo_in, s, 1) * a - coupling * row_link(a)

    for s, inward in ((0, 1.0), (1, -1.0)):
        mid = edge_probe[s]
        half = jnp.concatenate([hm[edge_row[s] : edge_row[s] + 1, :]] * 4, axis=1)
        along_x = half * (roll(mid, -1, 1) - roll(mid, 1, 1))
        turn = jnp.where(over_pole[s], -0.5 * inward, 0.5 * inward)
        along_y = turn * (flip(s, 1.0) * row_of(halo_out, NEAR + 4 * s) - row_of(halo_in, REST + 7 * s))
        linked = jnp.where(row16 < LEV, roll(along_x, -2 * LEV, 0), row_link(along_y))
        linked = linked + jnp.where(is_temp, roll(along_x, 2 * LEV, 0), 0.0)
        up = jnp.where(lax.rem(row16, LEV) == 0, mid, roll(mid, 1, 0))
        down = jnp.where(lax.rem(row16, LEV) == LEV - 1, mid, roll(mid, -1, 0))
        t = -(wind(halo_in, s, 0) * along_x + wind(halo_in, s, 1) * along_y) - coupling * linked
        a = mid + time_step * (t + mixing * (up + down - 2.0 * mid))
        gy[0:PAIRS, edge_row[s], :] = flip(s, -1.0) * edge_weights(s, a)

    def row_weights(a, nw):
        return (
            -nw * a[0],
            -nw * a[1] - coupling * a[2],
            -nw * a[2] - coupling * a[1],
            -nw * a[3],
        )

    def put_weights(l, h, a):
        for f, weight in enumerate(row_weights(a, grid[PAIRS + LEV + l, h : h + 8, :])):
            gy[f * LEV + l, h : h + 8, :] = weight

    @pl.when(polar)
    def _():
        all_z(0).wait_recv()
        for h in (8, 16):
            taken = project(0, h // 8 - 1)
            for l in range(LEV):
                for f in range(FIELDS):
                    n, rows = f * LEV + l, slice(h - 8, h)
                    adj[n, rows, :] = grid[n, h : h + 8, :] + tend[n, rows, :] - taken[f][l]
        all_z(1).wait_recv()
        for h in (8, 16):
            taken = project(1, h // 8 - 1)
            for l in range(LEV):
                a = []
                for f in range(FIELDS):
                    n, rows = f * LEV + l, slice(h - 8, h)
                    change = tend[n, rows, :] - taken[f][l]
                    tend[n, rows, :] = change
                    tan_out[f, l, rows, :] = (grid[n, h : h + 8, :] + change)[:, :COLS]
                    a.append(adj[n, rows, :] - taken[f][l])
                    adj[n, rows, :] = a[f]
                put_weights(l, h, a)

    @pl.when(jnp.logical_not(polar))
    def _():
        @pl.loop(0, LEV)
        def _(l):
            for h in (8, 16):
                a = []
                for f in range(FIELDS):
                    n, rows = f * LEV + l, slice(h - 8, h)
                    a.append(grid[n, h : h + 8, :] + tend[n, rows, :])
                    tan_out[f, l, rows, :] = a[f][:, :COLS]
                    adj[n, rows, :] = a[f]
                put_weights(l, h, a)

    @pl.loop(0, LEV)
    def _(l):
        lo = jnp.maximum(l - 1, 0)
        hi = jnp.minimum(l + 1, LEV - 1)
        for h in (8, 16):
            rows = slice(h - 8, h)
            half = jnp.concatenate([hm[h : h + 8, :]] * 4, axis=1)
            ew = grid[PAIRS + l, h : h + 8, :]
            a = [adj[f * LEV + l, rows, :] for f in range(FIELDS)]
            col_weights = (
                -ew * a[0] - coupling * a[2],
                -ew * a[1],
                -ew * a[2] - coupling * a[0],
                -ew * a[3],
            )
            for f in range(FIELDS):
                n = f * LEV + l
                back = half * (roll(col_weights[f], 1, 1) - roll(col_weights[f], -1, 1))
                back = back + 0.5 * (gy[n, h - 1 : h + 7, :] - gy[n, h + 1 : h + 9, :])
                back = back + mixing * (adj[f * LEV + lo, rows, :] + adj[f * LEV + hi, rows, :] - 2.0 * a[f])
                diag = grid[n, h : h + 8, :] * (tend[n, rows, :] + time_step * back)
                diag_out[f, l, rows, :] = diag[:, :COLS]

    @pl.when(jnp.logical_and(near_polar, jnp.logical_not(polar)))
    def _():
        load_part.wait()

    for s, wanted in enumerate((above_polar, below_polar)):
        @pl.when(wanted)
        def _():
            remote(bz.at[s], bz.at[s], b_send, b_recv.at[s], nb, nl).wait_recv()

        @pl.when(jnp.logical_not(wanted))
        def _():
            bz[s] = jnp.zeros((FIELDS, LEV, RANK), F32)

    @pl.when(near_polar)
    def _():
        taken = evaluate(jnp.concatenate([bz[s, f] for s in range(2) for f in range(FIELDS)], axis=0))
        for s, row in ((0, 0), (1, 15)):
            weight = flip(s, -1.0) * edge_weights(s, taken[PAIRS * s : PAIRS * (s + 1), :])
            less = ((0.5, -0.5)[s] * time_step) * grid[0:PAIRS, 8 + row, :] * weight
            for f in range(FIELDS):
                diag_out[f, :, row, :] = diag_out[f, :, row, :] - less[f * LEV : (f + 1) * LEV, :COLS]

    halo_arrival(0, BLOCKS, 0).wait_send()

    @pl.when(polar)
    def _():
        all_y().wait_send()
        all_c().wait_send()
        for q in range(2):
            all_z(q).wait_send()

        @pl.when(edge_over)
        def _():
            remote(eb.at[others], eb.at[others], b_send, b_recv.at[0], b, west).wait_send()

        @pl.when(jnp.logical_not(edge_over))
        def _():
            remote(eb, eb, b_send, b_recv.at[0], b, west).wait_send()


def hand_out(tan_in, diag_in, tan_out, diag_out, sem):
    copies = [
        pltpu.make_async_copy(src, dst, sem.at[n])
        for n, (src, dst) in enumerate(((tan_in, tan_out), (diag_in, diag_out)))
    ]
    for copy in copies:
        copy.start()
    for copy in copies:
        copy.wait()


def per_device(bands, row_signs, col_signs, spread, east_wind, north_wind, cutoffs):
    any_spec = pl.BlockSpec(memory_space=pl.ANY)
    out = jax.ShapeDtypeStruct((FIELDS, LEV, ROWS, COLS), F32)
    tables = [jnp.asarray(half_metric(bands)), jnp.asarray(mode_factors())]
    operands = (spread, east_wind, north_wind, row_signs, col_signs, cutoffs, *tables)
    vmem = pltpu.VMEM
    dma = pltpu.SemaphoreType.DMA
    held = pltpu.VMEM(out.shape, F32)
    results = pl.pallas_call(
        functools.partial(kernel, bands),
        out_shape=(held, held),
        in_specs=[any_spec] * 8,
        out_specs=(pl.BlockSpec(memory_space=pltpu.VMEM),) * 2,
        scratch_shapes=[
            vmem((FIELDS, LEV, ROWS, COLS), F32),
            vmem((2, LEV, ROWS, COLS), F32),
            vmem((FIELDS, LEV, ROWS), jnp.int32),
            vmem((FIELDS, LEV, COLS), jnp.int32),
            pltpu.SMEM((ROWS,), jnp.int32),
            vmem((32, 128), F32),
            vmem((TABLE_ROWS, 2 * RANK), BF16),
            vmem((PAIRS + 2 * LEV, 32, WIDE), F32),
            vmem((BLOCKS, 16, 128), F32),
            vmem((BLOCKS, 16, 128), F32),
            vmem((LANES, 2, LEV, 8, RANK), F32),
            vmem((LANES, 2, LEV, 8, RANK), F32),
            vmem((LANES, 16, RANK), F32),
            vmem((LANES, 16, RANK), F32),
            vmem((2, LANES, LEV, 8, RANK), F32),
            vmem((2, LANES, LEV, 8, RANK), F32),
            vmem((LANES, LEV, RANK), F32),
            vmem((2, FIELDS, LEV, RANK), F32),
            vmem((PAIRS, ROWS, WIDE), F32),
            vmem((PAIRS, ROWS, WIDE), F32),
            vmem((PAIRS, 32, WIDE), F32),
            dma((12,)),
            dma,
            dma((2,)),
            dma,
            dma,
            dma,
            dma,
            dma((2,)),
            dma((2,)),
            dma,
            dma((2,)),
        ],
        compiler_params=pltpu.CompilerParams(
            collective_id=0, has_side_effects=True, vmem_limit_bytes=32 * 2**20
        ),
        cost_estimate=pl.CostEstimate(flops=10**9, bytes_accessed=4 * 10**6, transcendentals=0),
    )(*(pltpu.with_memory_space_constraint(x, pltpu.HBM) for x in operands))
    return pl.pallas_call(
        hand_out,
        out_shape=(out, out),
        in_specs=[any_spec] * 2,
        out_specs=(any_spec, any_spec),
        scratch_shapes=[dma((2,))],
        compiler_params=pltpu.CompilerParams(vmem_limit_bytes=2**20),
    )(*(pltpu.with_memory_space_constraint(x, pltpu.VMEM) for x in results))


def solution(mesh):
    return jax.shard_map(
        functools.partial(per_device, mesh.shape["lat"]),
        mesh=mesh,
        in_specs=(
            P(None, None, "lat"),
            P(None, None, "lon"),
            P(None, None, "lat", "lon"),
            P(None, "lat", "lon"),
            P(None, "lat", "lon"),
            P("lat"),
        ),
        out_specs=(P(None, None, "lat", "lon"), P(None, None, "lat", "lon")),
        check_vma=False,
    )
```

```python
import functools

import jax
import jax.numpy as jnp
import ml_dtypes
import numpy as np
from jax import lax
from jax.experimental import pallas as pl
from jax.experimental.pallas import tpu as pltpu
from jax.sharding import PartitionSpec as P

KTOP = 256
POLAR = 32
RANK = 128
USED = 96
ROWS = 16
COLS = 450
WIDE = 512
LANES = 8
FIELDS = 4
LEV = 4
PAIRS = FIELDS * LEV

time_step = 0.5
coupling = 0.5
mixing = 0.2
metric_cap = 4.0

FORWARD, EVALUATE, TO_COEFS, FROM_COEFS, TABLE_ROWS = 0, 512, 1280, 2304, 3328
NEAR, SIDES, REST, BLOCKS = 0, 8, 10, 24

MESH = pl.DeviceIdType.MESH
F32 = jnp.float32
BF16 = jnp.bfloat16


def split_table(table):
    high = table.astype(ml_dtypes.bfloat16)
    low = (table - high.astype(np.float64)).astype(ml_dtypes.bfloat16)
    return high, low


def waves_of(group, lane_index):
    place = lane_index % 64
    second = place // 32
    other = (8 - group) if group else 4
    residue = group + second * (other - group)
    return 8 * (place % 32) + residue + (8 * (1 - second) if group == 0 else 0)


@functools.lru_cache(None)
def mode_factors():
    total = COLS * LANES
    size = COLS + 2
    place = np.arange(size, dtype=np.float64)
    width = (KTOP + 0.5) / total
    diag = ((size - 1 - 2 * place) / 2) ** 2 * np.cos(2 * np.pi * width)
    side = place[1:] * (size - place[1:]) / 2
    vectors = np.linalg.eigh(np.diag(diag) + np.diag(side, 1) + np.diag(side, -1))[1]
    basis = np.concatenate([vectors[:, ::-1][:, :USED], np.zeros((size, RANK - USED))], axis=1)
    basis = basis * np.where(basis[size // 2] < 0, -1.0, 1.0)
    weights = []
    for group in range(4):
        waves = waves_of(group, np.arange(64))
        angle = 2 * np.pi / total * ((np.arange(size)[:, None] - 1) * waves[None, :] % total)
        alpha, beta = basis.T @ np.cos(angle), basis.T @ np.sin(angle)
        if group:
            sign = np.where(np.arange(64) < 32, 1.0, -1.0)
            top, low = (alpha, beta), (sign * beta, -sign * alpha)
        else:
            use = np.where(np.arange(64) < 32, 1.0, 0.0)
            top, low = (use * alpha, use * beta), ((1 - use) * alpha, (1 - use) * beta)
        weights.append(np.concatenate([np.concatenate(top, axis=1), np.concatenate(low, axis=1)], axis=0))
    weights = np.round(np.stack(weights) * 2.0**22) / 2.0**22
    wide = np.zeros((RANK, WIDE))
    wide[:, : COLS + 1] = basis[1:].T
    wide[:, WIDE - 1] = basis[0]
    wide = np.round(wide * 2.0**26) / 2.0**26
    wide_h, wide_l = split_table(wide)
    own = np.where(np.arange(WIDE)[:, None] < COLS, 1, 0).astype(ml_dtypes.bfloat16)
    high, low = split_table(weights)
    back = np.concatenate([np.swapaxes(part, 1, 2) for part in (high, low)], axis=1)
    evaluate = np.concatenate([wide_h, wide_l, wide_h], axis=0)
    return np.concatenate(
        [
            np.concatenate([wide_h.T * own, wide_l.T * own], axis=1),
            evaluate[:, : WIDE // 2],
            evaluate[:, WIDE // 2 :],
            np.concatenate([high, low], axis=2).reshape(-1, 2 * RANK),
            back.reshape(-1, 2 * RANK),
        ],
        axis=0,
    )


ROOT = float(np.sqrt(0.5))


def over_lanes(y):
    s = [y[j] + y[j + 4] for j in range(4)]
    d = [y[j] - y[j + 4] for j in range(4)]
    even, odd = s[0] + s[2], s[1] + s[3]
    minus, plus = ROOT * (d[1] - d[3]), ROOT * (d[1] + d[3])
    return [
        (even + odd, even - odd),
        (d[0] + minus, -(d[2] + plus)),
        (s[0] - s[2], s[3] - s[1]),
        (d[0] - minus, d[2] - plus),
    ]


def to_lanes(pairs):
    (y0, y4), (u1, v1), (u2, v2), (u3, v3) = pairs
    even, odd = y0 + y4, y0 - y4
    s = [even + u2, odd - v2, even - u2, odd + v2]
    du, sv = ROOT * (u1 - u3), ROOT * (v1 + v3)
    d = [u1 + u3, du - sv, v3 - v1, -du - sv]
    return [s[j] + d[j] for j in range(4)] + [s[j] - d[j] for j in range(4)]


@functools.lru_cache(None)
def half_metric(bands):
    total = bands * ROWS
    rows = np.clip(np.arange(bands)[:, None] * ROWS - 8 + np.arange(32)[None, :], 0, total - 1)
    metric = np.minimum(1.0 / np.cos(np.pi * ((rows + 0.5) / total - 0.5)), metric_cap)
    table = np.broadcast_to((0.5 * metric).astype(np.float32)[:, :, None], (bands, 32, 128)).copy()
    forward = mode_factors()[FORWARD : FORWARD + WIDE].astype(np.float32)
    for row, col in enumerate((0, COLS - 1)):
        table[:, row] = forward[col, :RANK] + forward[col, RANK:]
    return table


def dot_cols(a, b):
    return lax.dot_general(a, b, (((1,), (0,)), ((), ())), preferred_element_type=F32)


def split(x):
    high = x.astype(BF16)
    return high, (x - high.astype(F32)).astype(BF16)


def to_modes(x, table):
    xh, xl = split(x)
    half = table.shape[1] // 2
    wide = dot_cols(xh, table[...])
    return wide[:, :half] + wide[:, half:] + dot_cols(xl, table[:, 0:half])


def from_modes(z, *tables):
    zh, zl = split(z)
    three = jnp.concatenate([zh, zh, zl], axis=1)
    return jnp.concatenate([dot_cols(three, table[...]) for table in tables], axis=1)


def to_coefs(x, table):
    rows = x.shape[0]
    wide = dot_cols(jnp.concatenate(split(x), axis=0), table[...])
    half = wide.shape[1] // 2
    return wide[:rows, :half] + wide[:rows, half:] + wide[rows:, :half]


def from_coefs(z, table):
    zh, zl = split(z)
    rows = jnp.concatenate([jnp.concatenate([zh, zh], axis=1), jnp.concatenate([zl, jnp.zeros_like(zl)], axis=1)], axis=0)
    wide = dot_cols(rows, table[...])
    return wide[: z.shape[0]] + wide[z.shape[0] :]


def pack(levels):
    lane = lax.broadcasted_iota(jnp.int32, (1, RANK), 1)
    return [jnp.where(lane < USED, levels[l], roll(levels[3], 96 - 32 * l, 1)) for l in range(3)]


def unpack(parts):
    lane = lax.broadcasted_iota(jnp.int32, (1, RANK), 1)
    last = jnp.where(lane < 64, roll(parts[1], 64, 1), roll(parts[2], 96, 1))
    return parts + [jnp.where(lane < 32, roll(parts[0], 32, 1), last)]


def roll(x, shift, axis):
    return pltpu.roll(x, shift % x.shape[axis], axis)


def roll_blocks(x, shift):
    return roll(x.reshape(x.shape[0] * x.shape[1], x.shape[2]), shift, 1).reshape(x.shape)


def fold(x):
    while x.shape[0] > 1:
        half = x.shape[0] // 2
        x = x[:half] + roll_blocks(x[half:], 2 * half)
    return x


def kernel(
    bands, spread, east, north, rs, cs, cut, metric, table_in, tan_out, diag_out,
    spread_v, winds_v, rs_v, cs_v, cut_s, hm, table,
    grid, halo_out, halo_in, ybuf, yr, xb, cb, yc, zbuf, zr, eb, bz,
    tend, adj, gy,
    in_sem, halo_send, halo_recv, y_send, y_recv, c_send, c_recv, z_send, z_recv, b_send, b_recv,
):
    b = lax.axis_index("lat")
    i = lax.axis_index("lon")
    caps = POLAR // ROWS
    is_north = b == 0
    is_south = b == bands - 1
    polar = jnp.logical_or(b < caps, b >= bands - caps)
    above_polar = jnp.logical_or(b <= caps, is_south)
    below_polar = jnp.logical_or(b >= bands - caps - 1, is_north)
    near_polar = jnp.logical_or(above_polar, below_polar)
    across = lax.rem(i + LANES // 2, LANES)
    west = lax.rem(i + LANES - 1, LANES)
    east_lane = lax.rem(i + 1, LANES)
    nb = jnp.where(is_north, 0, b - 1)
    nl = jnp.where(is_north, across, i)
    sb = jnp.where(is_south, bands - 1, b + 1)
    sl = jnp.where(is_south, across, i)
    slot_n = jnp.where(is_north, 0, 1)
    slot_s = jnp.where(is_south, 1, 0)
    own_half = lax.rem(i, 2)
    edge_over = jnp.where(own_half == 0, is_north, is_south)
    over_pole = (is_north, is_south)

    def plus(lane, d):
        return lax.rem(lane + d, LANES)

    load_spread = [
        pltpu.make_async_copy(spread.at[f], spread_v.at[f], in_sem.at[8 + f]) for f in range(FIELDS)
    ]
    load_rows = pltpu.make_async_copy(rs, rs_v, in_sem.at[1])
    load_cols = pltpu.make_async_copy(cs, cs_v, in_sem.at[2])
    load_metric = pltpu.make_async_copy(metric.at[b], hm, in_sem.at[4])
    load_cut = pltpu.make_async_copy(cut, cut_s, in_sem.at[5])

    def load_table(start, stop, sem):
        return pltpu.make_async_copy(table_in.at[start:stop], table.at[start:stop], in_sem.at[sem])

    load_forward = load_table(FORWARD, EVALUATE, 6)
    load_others = load_table(EVALUATE, TABLE_ROWS, 7)
    load_part = load_table(EVALUATE, TO_COEFS, 7)
    load_rows.start()
    load_cols.start()
    for load in load_spread:
        load.start()
    pltpu.make_async_copy(east, winds_v.at[0], in_sem.at[3]).start()
    pltpu.make_async_copy(north, winds_v.at[1], in_sem.at[3]).start()
    load_metric.start()

    barrier = pltpu.get_barrier_semaphore()

    def greet(lat, lon):
        pl.semaphore_signal(barrier, inc=1, device_id=(lat, lon), device_id_type=MESH)

    greet(nb, nl)
    greet(sb, sl)
    greet(b, west)
    greet(b, east_lane)

    @pl.when(polar)
    def _():
        @pl.loop(2, LANES - 1)
        def _(d):
            greet(b, plus(i, d))

        load_forward.start()
        load_cut.start()

    @pl.when(jnp.logical_and(near_polar, jnp.logical_not(polar)))
    def _():
        load_part.start()

    load_rows.wait()
    load_cols.wait()
    grid[:, 8:24, 384:512] = jnp.zeros((PAIRS + 2 * LEV, ROWS, 128), F32)
    row_part = jnp.concatenate([rs_v[f] for f in range(FIELDS)], axis=0)
    row_part = (2 * row_part - 1).astype(F32).T
    for f in range(FIELDS):
        col_part = (2 * cs_v[f] - 1).astype(F32)
        load_spread[f].wait()
        for l in range(LEV):
            n = f * LEV + l
            grid[n, 8:24, 0:COLS] = spread_v[f, l] * (row_part[:, n : n + 1] * col_part[l : l + 1, :])

    @pl.when(polar)
    def _():
        load_others.start()

    pltpu.make_async_copy(winds_v, winds_v, in_sem.at[3]).wait()
    for w in range(2):
        for l in range(LEV):
            grid[PAIRS + w * LEV + l, 8:24, 0:COLS] = winds_v[w, l]

    for s, (near, far) in enumerate(((8, 9), (23, 22))):
        for t in range(4):
            lanes = slice(128 * t, 128 * t + 128)
            halo_out[NEAR + 4 * s + t] = grid[0:PAIRS, near, lanes]
            halo_out[REST + 7 * s + t] = grid[0:PAIRS, far, lanes]
            halo_out[REST + 7 * s + 4 + t // 2, 8 * (t % 2) : 8 * (t % 2) + 8, :] = grid[
                PAIRS : PAIRS + 2 * LEV, near, lanes
            ]
    lane128 = lax.broadcasted_iota(jnp.int32, (1, 1, 128), 2)
    for s, (start, shift) in enumerate(((0, 0), (384, COLS - 2 - 384))):
        tile = grid[:, 8:24, start : start + 128]
        tile = jnp.where(jnp.logical_and(lane128 >= shift, lane128 < shift + 2), tile, 0.0)
        packed = fold(tile[:PAIRS]) + roll_blocks(fold(tile[PAIRS:]), 2 * PAIRS)
        halo_out[SIDES + s] = roll_blocks(packed, -shift)[0]

    pl.semaphore_wait(barrier, 4 + jnp.where(polar, LANES - 3, 0))

    def remote(src, dst, send, recv, lat, lon):
        return pltpu.make_async_remote_copy(
            src_ref=src, dst_ref=dst, send_sem=send, recv_sem=recv, device_id=(lat, lon), device_id_type=MESH
        )

    def halo_copy(start, count, to, which, lat, lon):
        return remote(
            halo_out.at[start : start + count], halo_in.at[pl.ds(to, count)], halo_send, halo_recv.at[which], lat, lon
        )

    def halo_arrival(start, stop, which):
        return remote(
            halo_out.at[start:stop], halo_in.at[start:stop], halo_send, halo_recv.at[which], b, west
        )

    halo_copy(NEAR, 4, NEAR + 4 * slot_n, 0, nb, nl).start()
    halo_copy(NEAR + 4, 4, NEAR + 4 * slot_s, 0, sb, sl).start()
    halo_copy(SIDES, 1, SIDES + 1, 0, b, west).start()
    halo_copy(SIDES + 1, 1, SIDES, 0, b, east_lane).start()

    def y_copy(o):
        return remote(ybuf.at[o], yr.at[i], y_send, y_recv, b, o)

    others = pl.ds(0, LANES - 1)

    def all_y():
        return remote(ybuf.at[others], yr.at[others], y_send, y_recv, b, west)

    def send_values():
        @pl.loop(1, LANES)
        def _(d):
            y_copy(plus(i, d)).start()

        yr[i] = ybuf[i]

    def c_copy(o):
        return remote(cb.at[o], yc.at[i], c_send, c_recv, b, o)

    def all_c():
        return remote(cb.at[others], yc.at[others], c_send, c_recv, b, west)

    def z_copy(q, j):
        return remote(zbuf.at[q, j], zr.at[q, i], z_send.at[q], z_recv.at[q], b, j)

    def all_z(q):
        return remote(zbuf.at[q, others], zr.at[q, others], z_send.at[q], z_recv.at[q], b, west)

    def own_rows(q):
        row = lax.broadcasted_iota(jnp.int32, (8, 128), 0)
        cutoff = jnp.zeros((8, 128), jnp.int32)
        for r in range(8):
            cutoff = jnp.where(row == r, cut_s[8 * own_half + r], cutoff)

        if q == 0:
            all_y().wait_recv()
        else:
            all_c().wait_recv()

        levels = unpack([yr[:, q, l].reshape(LANES * 8, RANK) for l in range(LEV - 1)])
        lanes = []
        for j in range(LANES):
            y = [levels[l][8 * j : 8 * j + 8, :] for l in range(LEV)]
            if q == 1:
                ends = pltpu.roll(yc[j, 8:16, :], lax.rem(128 - 2 * LEV * (i // 2), 128), 1)
                edge_rows = jnp.where(row == 7 * own_half, 1.0, 0.0)
                y = [
                    y[l]
                    + ends[:, 2 * l : 2 * l + 1] * hm[0:1, :]
                    + ends[:, 2 * l + 1 : 2 * l + 2] * hm[1:2, :]
                    + edge_rows * yc[j, l : l + 1, :]
                    for l in range(LEV)
                ]
            lanes.append(jnp.concatenate(y, axis=0))
        coefs = [
            to_coefs(jnp.concatenate(pair, axis=1), table.at[TO_COEFS + 256 * group : TO_COEFS + 256 * (group + 1)])
            for group, pair in enumerate(over_lanes(lanes))
        ]
        kept = []
        for group, coef in enumerate(coefs):
            wave = waves_of(group, lax.broadcasted_iota(jnp.int32, (8, 128), 1))
            keep = jnp.where(wave > cutoff, 2.0 / (COLS * LANES), 0.0)
            kept.append(coef * jnp.concatenate([keep] * LEV, axis=0))
        backs = [
            from_coefs(coef, table.at[FROM_COEFS + 256 * group : FROM_COEFS + 256 * (group + 1)])
            for group, coef in enumerate(kept)
        ]
        pairs = [(back[:, :RANK], back[:, RANK:]) for back in backs]
        zs = [z.reshape(LEV, 8, RANK) for z in to_lanes(pairs)]
        for l, part in enumerate(pack([jnp.concatenate([z[l] for z in zs], axis=0) for l in range(LEV)])):
            zbuf[q, :, l] = part.reshape(LANES, 8, RANK)
        for j, z in enumerate(zs):
            edge = jnp.where(own_half == 0, z[:, 0, :], z[:, 7, :])
            eb[j] = edge if q == 0 else eb[j] + edge

        @pl.loop(1, LANES)
        def _(d):
            z_copy(q, plus(i, d)).start()

        zr[q, i] = zbuf[q, i]

    def edge_sends():
        slot = jnp.where(own_half == 0, slot_n, slot_s)
        lat = jnp.where(own_half == 0, nb, sb)

        @pl.loop(0, LANES)
        def _(d):
            j = plus(i, d)
            lon = jnp.where(edge_over, plus(j, LANES // 2), j)
            here = jnp.logical_and(edge_over, lon == i)

            @pl.when(jnp.logical_not(here))
            def _():
                remote(eb.at[j], bz.at[slot, i // 2], b_send, b_recv.at[slot], lat, lon).start()

            @pl.when(here)
            def _():
                pltpu.make_async_copy(eb.at[j], bz.at[slot, i // 2], b_recv.at[slot]).start()

    def evaluate(z):
        return from_modes(z, table.at[EVALUATE : EVALUATE + 384], table.at[EVALUATE + 384 : TO_COEFS])

    def project(q, h):
        levels = unpack(
            [jnp.concatenate([zr[q, 2 * f + h, l] for f in range(FIELDS)], axis=0) for l in range(LEV - 1)]
        )
        z = jnp.concatenate(
            [levels[l][8 * f : 8 * f + 8, :] for f in range(FIELDS) for l in range(LEV)], axis=0
        )
        out = evaluate(z)
        return [[out[8 * (LEV * f + l) : 8 * (LEV * f + l + 1), :] for l in range(LEV)] for f in range(FIELDS)]

    def tendency_rows(h, l, at, half):
        lo = jnp.maximum(l - 1, 0)
        hi = jnp.minimum(l + 1, LEV - 1)
        ew = at(PAIRS + l, h)
        nw = at(PAIRS + LEV + l, h)
        mids, along_x, along_y = [], [], []
        for f in range(FIELDS):
            mid = at(f * LEV + l, h)
            mids.append(mid)
            along_x.append(half * (roll(mid, -1, 1) - roll(mid, 1, 1)))
            along_y.append(0.5 * (at(f * LEV + l, h + 1) - at(f * LEV + l, h - 1)))
        linked = (along_x[2], along_y[2], along_x[0] + along_y[1], None)
        out = []
        for f in range(FIELDS):
            mixed = at(f * LEV + lo, h) + at(f * LEV + hi, h) - 2.0 * mids[f]
            t = -(ew * along_x[f] + nw * along_y[f]) + mixing * mixed
            if linked[f] is not None:
                t = t - coupling * linked[f]
            out.append(time_step * t)
        return out

    def full_tendency():
        @pl.loop(0, LEV)
        def _(l):
            for h in (8, 16):
                half = jnp.concatenate([hm[h : h + 8, :]] * 4, axis=1)
                for f, t in enumerate(tendency_rows(h, l, lambda n, r: grid[n, r : r + 8, :], half)):
                    tend[f * LEV + l, h - 8 : h, :] = t

    def side_tendency():
        lane = lax.broadcasted_iota(jnp.int32, (1, 128), 1)
        late = jnp.logical_or(jnp.logical_or(lane == 65, lane == 66), lane == 127)

        def at(n, r):
            return jnp.where(lane < 2, grid[n, r : r + 8, 0:128], grid[n, r : r + 8, 384:512])

        @pl.loop(0, LEV)
        def _(l):
            for h in (8, 16):
                for f, t in enumerate(tendency_rows(h, l, at, hm[h : h + 8, :])):
                    n, rows = f * LEV + l, slice(h - 8, h)
                    tend[n, rows, 0:128] = jnp.where(lane == 0, t, tend[n, rows, 0:128])
                    tend[n, rows, 384:512] = jnp.where(late, t, tend[n, rows, 384:512])

    load_metric.wait()

    @pl.when(polar)
    def _():
        grid[0:PAIRS, 7:8, :] = jnp.zeros((PAIRS, 1, WIDE), F32)
        grid[0:PAIRS, 24:25, :] = jnp.zeros((PAIRS, 1, WIDE), F32)
        full_tendency()
        load_forward.wait()
        probe = grid[0:PAIRS, 8:24, :].reshape(PAIRS * ROWS, WIDE)
        change = tend[...].reshape(PAIRS * ROWS, WIDE)
        y = to_modes(jnp.concatenate([probe, change], axis=0), table.at[FORWARD:EVALUATE])
        y = y.reshape(2, FIELDS, LEV, 2, 8, RANK)
        for q in range(2):
            blocks = [
                jnp.concatenate([y[q, f, l, h] for f in range(FIELDS) for h in range(2)], axis=0)
                for l in range(LEV)
            ]
            for l, part in enumerate(pack(blocks)):
                ybuf[:, q, l] = part.reshape(LANES, 8, RANK)
        send_values()

    halo_arrival(NEAR, REST, 0).wait_recv()
    lane2 = lax.broadcasted_iota(jnp.int32, (1, 128), 1)
    row16 = lax.broadcasted_iota(jnp.int32, (PAIRS, 1), 0)
    is_v = jnp.logical_and(row16 >= LEV, row16 < 2 * LEV)
    is_temp = jnp.logical_and(row16 >= 2 * LEV, row16 < 3 * LEV)

    def flip(s, minus):
        sign = jnp.where(row16 < 2 * LEV, -1.0, 1.0) * minus
        return jnp.where(over_pole[s], sign, 1.0)

    def row_link(x):
        return jnp.where(is_v, roll(x, -LEV, 0), jnp.where(is_temp, roll(x, LEV, 0), 0.0))

    def wind(buffer, s, w):
        base = REST + 7 * s + 4
        rows = [buffer[base + t // 2, 8 * (t % 2) + LEV * w : 8 * (t % 2) + LEV * (w + 1), :] for t in range(4)]
        return jnp.concatenate([jnp.concatenate(rows, axis=1)] * FIELDS, axis=0)

    def row_of(buffer, start):
        return jnp.concatenate([buffer[start + t] for t in range(4)], axis=1)

    @pl.when(polar)
    def _():
        added = []
        for s, sign in ((0, 0.5 * time_step), (1, -0.5 * time_step)):
            ghost = flip(s, 1.0) * row_of(halo_in, NEAR + 4 * s)
            added.append(sign * (wind(halo_out, s, 1) * ghost + coupling * row_link(ghost)))
            xb[s] = added[s]
        y = to_modes(jnp.concatenate(added, axis=0), table.at[FORWARD:EVALUATE])
        for s in range(2):
            for f in range(FIELDS):
                cb[2 * f + s, 0:LEV, :] = y[(s * FIELDS + f) * LEV : (s * FIELDS + f + 1) * LEV, :]
        ends = []
        for side, sign in ((0, -1.0), (1, 1.0)):
            came = halo_in[SIDES + side]
            along_x = (sign * hm[8:24, :]) * (roll(came, -1, 1) if side == 0 else came)
            mine = jnp.where(
                jnp.logical_and(lane2 >= 2 * PAIRS, lane2 < 2 * (PAIRS + LEV)), halo_out[SIDES + side], 0.0
            )
            ew = sum(roll(mine, 2 * LEV * f - 2 * PAIRS - side, 1) for f in range(FIELDS))
            linked = jnp.where(
                lane2 < 2 * LEV,
                roll(along_x, -4 * LEV, 1),
                jnp.where(
                    jnp.logical_and(lane2 >= 4 * LEV, lane2 < 6 * LEV), roll(along_x, 4 * LEV, 1), 0.0
                ),
            )
            ends.append(time_step * (-ew * along_x - coupling * linked))
        ends = jnp.where(lax.rem(lane2, 2) == 0, ends[0], roll(ends[1], 1, 1))
        for f in range(FIELDS):
            for h in range(2):
                cb[2 * f + h, 8:16, :] = ends[8 * h : 8 * h + 8, :]

        @pl.loop(1, LANES)
        def _(d):
            c_copy(plus(i, d)).start()

        yc[i] = cb[i]

    @pl.when(polar)
    def _():
        load_cut.wait()
        load_others.wait()
        own_rows(0)

    from_west = roll(halo_in[SIDES], 126, 1)
    from_east = roll(halo_in[SIDES + 1], COLS - 384, 1)
    both = jnp.where(jnp.logical_and(lane2 >= 66, lane2 < 114), from_east, from_west)[None]
    for width in (2, 4, 8):
        both = jnp.concatenate([both, roll_blocks(both, -width)], axis=0)
    both = jnp.concatenate([both, roll_blocks(both, -16), roll_blocks(both, -32)], axis=0)
    in_halo = jnp.logical_or(jnp.logical_and(lane128 >= 66, lane128 < 68), lane128 >= 126)
    grid[:, 8:24, 384:512] = jnp.where(in_halo, both, grid[:, 8:24, 384:512])
    for s, near in enumerate((8, 23)):
        halo_out[REST + 7 * s + 6] = grid[0:PAIRS, near, 384:512]
    halo_copy(REST, 7, REST + 7 * slot_n, 1, nb, nl).start()
    halo_copy(REST + 7, 7, REST + 7 * slot_s, 1, sb, sl).start()

    @pl.when(polar)
    def _():
        own_rows(1)
        edge_sends()

    halo_arrival(REST, BLOCKS, 1).wait_recv()
    edge_row = (7, 24)
    edge_probe = []
    for s in range(2):
        edge_probe.append(
            jnp.concatenate([halo_in[NEAR + 4 * s + t] for t in range(3)] + [halo_in[REST + 7 * s + 6]], axis=1)
        )
        grid[0:PAIRS, edge_row[s], :] = flip(s, 1.0) * edge_probe[s]

    @pl.when(polar)
    def _():
        for s, row in ((0, 0), (1, 15)):
            tend[:, row, :] = tend[:, row, :] + xb[s]
        side_tendency()

    @pl.when(jnp.logical_not(polar))
    def _():
        full_tendency()

    def edge_weights(s, a):
        return -wind(halo_in, s, 1) * a - coupling * row_link(a)

    for s, inward in ((0, 1.0), (1, -1.0)):
        mid = edge_probe[s]
        half = jnp.concatenate([hm[edge_row[s] : edge_row[s] + 1, :]] * 4, axis=1)
        along_x = half * (roll(mid, -1, 1) - roll(mid, 1, 1))
        turn = jnp.where(over_pole[s], -0.5 * inward, 0.5 * inward)
        along_y = turn * (flip(s, 1.0) * row_of(halo_out, NEAR + 4 * s) - row_of(halo_in, REST + 7 * s))
        linked = jnp.where(row16 < LEV, roll(along_x, -2 * LEV, 0), row_link(along_y))
        linked = linked + jnp.where(is_temp, roll(along_x, 2 * LEV, 0), 0.0)
        up = jnp.where(lax.rem(row16, LEV) == 0, mid, roll(mid, 1, 0))
        down = jnp.where(lax.rem(row16, LEV) == LEV - 1, mid, roll(mid, -1, 0))
        t = -(wind(halo_in, s, 0) * along_x + wind(halo_in, s, 1) * along_y) - coupling * linked
        a = mid + time_step * (t + mixing * (up + down - 2.0 * mid))
        gy[0:PAIRS, edge_row[s], :] = flip(s, -1.0) * edge_weights(s, a)

    def row_weights(a, nw):
        return (
            -nw * a[0],
            -nw * a[1] - coupling * a[2],
            -nw * a[2] - coupling * a[1],
            -nw * a[3],
        )

    def put_weights(l, h, a):
        for f, weight in enumerate(row_weights(a, grid[PAIRS + LEV + l, h : h + 8, :])):
            gy[f * LEV + l, h : h + 8, :] = weight

    @pl.when(polar)
    def _():
        all_z(0).wait_recv()
        for h in (8, 16):
            taken = project(0, h // 8 - 1)
            for l in range(LEV):
                for f in range(FIELDS):
                    n, rows = f * LEV + l, slice(h - 8, h)
                    adj[n, rows, :] = grid[n, h : h + 8, :] + tend[n, rows, :] - taken[f][l]
        all_z(1).wait_recv()
        for h in (8, 16):
            taken = project(1, h // 8 - 1)
            for l in range(LEV):
                a = []
                for f in range(FIELDS):
                    n, rows = f * LEV + l, slice(h - 8, h)
                    change = tend[n, rows, :] - taken[f][l]
                    tend[n, rows, :] = change
                    tan_out[f, l, rows, :] = (grid[n, h : h + 8, :] + change)[:, :COLS]
                    a.append(adj[n, rows, :] - taken[f][l])
                    adj[n, rows, :] = a[f]
                put_weights(l, h, a)

    @pl.when(jnp.logical_not(polar))
    def _():
        @pl.loop(0, LEV)
        def _(l):
            for h in (8, 16):
                a = []
                for f in range(FIELDS):
                    n, rows = f * LEV + l, slice(h - 8, h)
                    a.append(grid[n, h : h + 8, :] + tend[n, rows, :])
                    tan_out[f, l, rows, :] = a[f][:, :COLS]
                    adj[n, rows, :] = a[f]
                put_weights(l, h, a)

    @pl.loop(0, LEV)
    def _(l):
        lo = jnp.maximum(l - 1, 0)
        hi = jnp.minimum(l + 1, LEV - 1)
        for h in (8, 16):
            rows = slice(h - 8, h)
            half = jnp.concatenate([hm[h : h + 8, :]] * 4, axis=1)
            ew = grid[PAIRS + l, h : h + 8, :]
            a = [adj[f * LEV + l, rows, :] for f in range(FIELDS)]
            col_weights = (
                -ew * a[0] - coupling * a[2],
                -ew * a[1],
                -ew * a[2] - coupling * a[0],
                -ew * a[3],
            )
            for f in range(FIELDS):
                n = f * LEV + l
                back = half * (roll(col_weights[f], 1, 1) - roll(col_weights[f], -1, 1))
                back = back + 0.5 * (gy[n, h - 1 : h + 7, :] - gy[n, h + 1 : h + 9, :])
                back = back + mixing * (adj[f * LEV + lo, rows, :] + adj[f * LEV + hi, rows, :] - 2.0 * a[f])
                diag = grid[n, h : h + 8, :] * (tend[n, rows, :] + time_step * back)
                diag_out[f, l, rows, :] = diag[:, :COLS]

    @pl.when(jnp.logical_and(near_polar, jnp.logical_not(polar)))
    def _():
        load_part.wait()

    for s, wanted in enumerate((above_polar, below_polar)):
        @pl.when(wanted)
        def _():
            remote(bz.at[s], bz.at[s], b_send, b_recv.at[s], nb, nl).wait_recv()

        @pl.when(jnp.logical_not(wanted))
        def _():
            bz[s] = jnp.zeros((FIELDS, LEV, RANK), F32)

    @pl.when(near_polar)
    def _():
        taken = evaluate(jnp.concatenate([bz[s, f] for s in range(2) for f in range(FIELDS)], axis=0))
        for s, row in ((0, 0), (1, 15)):
            weight = flip(s, -1.0) * edge_weights(s, taken[PAIRS * s : PAIRS * (s + 1), :])
            less = ((0.5, -0.5)[s] * time_step) * grid[0:PAIRS, 8 + row, :] * weight
            for f in range(FIELDS):
                diag_out[f, :, row, :] = diag_out[f, :, row, :] - less[f * LEV : (f + 1) * LEV, :COLS]

    halo_arrival(0, BLOCKS, 0).wait_send()

    @pl.when(polar)
    def _():
        all_y().wait_send()
        all_c().wait_send()
        for q in range(2):
            all_z(q).wait_send()

        @pl.when(edge_over)
        def _():
            remote(eb.at[others], eb.at[others], b_send, b_recv.at[0], b, west).wait_send()

        @pl.when(jnp.logical_not(edge_over))
        def _():
            remote(eb, eb, b_send, b_recv.at[0], b, west).wait_send()


def hand_out(tan_in, diag_in, tan_out, diag_out, sem):
    copies = [
        pltpu.make_async_copy(src, dst, sem.at[n])
        for n, (src, dst) in enumerate(((tan_in, tan_out), (diag_in, diag_out)))
    ]
    for copy in copies:
        copy.start()
    for copy in copies:
        copy.wait()


def per_device(bands, row_signs, col_signs, spread, east_wind, north_wind, cutoffs):
    any_spec = pl.BlockSpec(memory_space=pl.ANY)
    out = jax.ShapeDtypeStruct((FIELDS, LEV, ROWS, COLS), F32)
    tables = [jnp.asarray(half_metric(bands)), jnp.asarray(mode_factors())]
    operands = (spread, east_wind, north_wind, row_signs, col_signs, cutoffs, *tables)
    vmem = pltpu.VMEM
    dma = pltpu.SemaphoreType.DMA
    held = pltpu.VMEM(out.shape, F32)
    results = pl.pallas_call(
        functools.partial(kernel, bands),
        out_shape=(held, held),
        in_specs=[any_spec] * 8,
        out_specs=(pl.BlockSpec(memory_space=pltpu.VMEM),) * 2,
        scratch_shapes=[
            vmem((FIELDS, LEV, ROWS, COLS), F32),
            vmem((2, LEV, ROWS, COLS), F32),
            vmem((FIELDS, LEV, ROWS), jnp.int32),
            vmem((FIELDS, LEV, COLS), jnp.int32),
            pltpu.SMEM((ROWS,), jnp.int32),
            vmem((32, 128), F32),
            vmem((TABLE_ROWS, 2 * RANK), BF16),
            vmem((PAIRS + 2 * LEV, 32, WIDE), F32),
            vmem((BLOCKS, 16, 128), F32),
            vmem((BLOCKS, 16, 128), F32),
            vmem((LANES, 2, LEV - 1, 8, RANK), F32),
            vmem((LANES, 2, LEV - 1, 8, RANK), F32),
            vmem((2, PAIRS, WIDE), F32),
            vmem((LANES, 16, RANK), F32),
            vmem((LANES, 16, RANK), F32),
            vmem((2, LANES, LEV - 1, 8, RANK), F32),
            vmem((2, LANES, LEV - 1, 8, RANK), F32),
            vmem((LANES, LEV, RANK), F32),
            vmem((2, FIELDS, LEV, RANK), F32),
            vmem((PAIRS, ROWS, WIDE), F32),
            vmem((PAIRS, ROWS, WIDE), F32),
            vmem((PAIRS, 32, WIDE), F32),
            dma((12,)),
            dma,
            dma((2,)),
            dma,
            dma,
            dma,
            dma,
            dma((2,)),
            dma((2,)),
            dma,
            dma((2,)),
        ],
        compiler_params=pltpu.CompilerParams(
            collective_id=0, has_side_effects=True, vmem_limit_bytes=32 * 2**20
        ),
        cost_estimate=pl.CostEstimate(flops=10**9, bytes_accessed=4 * 10**6, transcendentals=0),
    )(*(pltpu.with_memory_space_constraint(x, pltpu.HBM) for x in operands))
    return pl.pallas_call(
        hand_out,
        out_shape=(out, out),
        in_specs=[any_spec] * 2,
        out_specs=(any_spec, any_spec),
        scratch_shapes=[dma((2,))],
        compiler_params=pltpu.CompilerParams(vmem_limit_bytes=2**20),
    )(*(pltpu.with_memory_space_constraint(x, pltpu.VMEM) for x in results))


def solution(mesh):
    return jax.shard_map(
        functools.partial(per_device, mesh.shape["lat"]),
        mesh=mesh,
        in_specs=(
            P(None, None, "lat"),
            P(None, None, "lon"),
            P(None, None, "lat", "lon"),
            P(None, "lat", "lon"),
            P(None, "lat", "lon"),
            P("lat"),
        ),
        out_specs=(P(None, None, "lat", "lon"), P(None, None, "lat", "lon")),
        check_vma=False,
    )
```

```python
import functools

import jax
import jax.numpy as jnp
import ml_dtypes
import numpy as np
from jax import lax
from jax.experimental import pallas as pl
from jax.experimental.pallas import tpu as pltpu
from jax.sharding import PartitionSpec as P

KTOP = 256
POLAR = 32
RANK = 128
USED = 96
ROWS = 16
COLS = 450
WIDE = 512
LANES = 8
FIELDS = 4
LEV = 4
PAIRS = FIELDS * LEV

time_step = 0.5
coupling = 0.5
mixing = 0.2
metric_cap = 4.0

FORWARD, EVALUATE, TO_COEFS, FROM_COEFS, TABLE_ROWS = 0, 512, 1280, 2304, 3328
NEAR, SIDES, REST, BLOCKS = 0, 8, 10, 24

MESH = pl.DeviceIdType.MESH
F32 = jnp.float32
BF16 = jnp.bfloat16


def split_table(table):
    high = table.astype(ml_dtypes.bfloat16)
    low = (table - high.astype(np.float64)).astype(ml_dtypes.bfloat16)
    return high, low


def waves_of(group, lane_index):
    place = lane_index % 64
    second = place // 32
    other = (8 - group) if group else 4
    residue = group + second * (other - group)
    return 8 * (place % 32) + residue + (8 * (1 - second) if group == 0 else 0)


@functools.lru_cache(None)
def mode_factors():
    total = COLS * LANES
    size = COLS + 2
    place = np.arange(size, dtype=np.float64)
    width = (KTOP + 0.5) / total
    diag = ((size - 1 - 2 * place) / 2) ** 2 * np.cos(2 * np.pi * width)
    side = place[1:] * (size - place[1:]) / 2
    vectors = np.linalg.eigh(np.diag(diag) + np.diag(side, 1) + np.diag(side, -1))[1]
    basis = np.concatenate([vectors[:, ::-1][:, :USED], np.zeros((size, RANK - USED))], axis=1)
    basis = basis * np.where(basis[size // 2] < 0, -1.0, 1.0)
    weights = []
    for group in range(4):
        waves = waves_of(group, np.arange(64))
        angle = 2 * np.pi / total * ((np.arange(size)[:, None] - 1) * waves[None, :] % total)
        alpha, beta = basis.T @ np.cos(angle), basis.T @ np.sin(angle)
        if group:
            sign = np.where(np.arange(64) < 32, 1.0, -1.0)
            top, low = (alpha, beta), (sign * beta, -sign * alpha)
        else:
            use = np.where(np.arange(64) < 32, 1.0, 0.0)
            top, low = (use * alpha, use * beta), ((1 - use) * alpha, (1 - use) * beta)
        weights.append(np.concatenate([np.concatenate(top, axis=1), np.concatenate(low, axis=1)], axis=0))
    weights = np.round(np.stack(weights) * 2.0**22) / 2.0**22
    wide = np.zeros((RANK, WIDE))
    wide[:, : COLS + 1] = basis[1:].T
    wide[:, WIDE - 1] = basis[0]
    wide = np.round(wide * 2.0**26) / 2.0**26
    wide_h, wide_l = split_table(wide)
    own = np.where(np.arange(WIDE)[:, None] < COLS, 1, 0).astype(ml_dtypes.bfloat16)
    high, low = split_table(weights)
    back = np.concatenate([np.swapaxes(part, 1, 2) for part in (high, low)], axis=1)
    evaluate = np.concatenate([wide_h, wide_l, wide_h], axis=0)
    return np.concatenate(
        [
            np.concatenate([wide_h.T * own, wide_l.T * own], axis=1),
            evaluate[:, : WIDE // 2],
            evaluate[:, WIDE // 2 :],
            np.concatenate([high, low], axis=2).reshape(-1, 2 * RANK),
            back.reshape(-1, 2 * RANK),
        ],
        axis=0,
    )


ROOT = float(np.sqrt(0.5))


def over_lanes(y):
    s = [y[j] + y[j + 4] for j in range(4)]
    d = [y[j] - y[j + 4] for j in range(4)]
    even, odd = s[0] + s[2], s[1] + s[3]
    minus, plus = ROOT * (d[1] - d[3]), ROOT * (d[1] + d[3])
    return [
        (even + odd, even - odd),
        (d[0] + minus, -(d[2] + plus)),
        (s[0] - s[2], s[3] - s[1]),
        (d[0] - minus, d[2] - plus),
    ]


def to_lanes(pairs):
    (y0, y4), (u1, v1), (u2, v2), (u3, v3) = pairs
    even, odd = y0 + y4, y0 - y4
    s = [even + u2, odd - v2, even - u2, odd + v2]
    du, sv = ROOT * (u1 - u3), ROOT * (v1 + v3)
    d = [u1 + u3, du - sv, v3 - v1, -du - sv]
    return [s[j] + d[j] for j in range(4)] + [s[j] - d[j] for j in range(4)]


@functools.lru_cache(None)
def half_metric(bands):
    total = bands * ROWS
    rows = np.clip(np.arange(bands)[:, None] * ROWS - 8 + np.arange(32)[None, :], 0, total - 1)
    metric = np.minimum(1.0 / np.cos(np.pi * ((rows + 0.5) / total - 0.5)), metric_cap)
    table = np.broadcast_to((0.5 * metric).astype(np.float32)[:, :, None], (bands, 32, 128)).copy()
    forward = mode_factors()[FORWARD : FORWARD + WIDE].astype(np.float32)
    for row, col in enumerate((0, COLS - 1)):
        table[:, row] = forward[col, :RANK] + forward[col, RANK:]
    return table


def dot_cols(a, b):
    return lax.dot_general(a, b, (((1,), (0,)), ((), ())), preferred_element_type=F32)


def split(x):
    high = x.astype(BF16)
    return high, (x - high.astype(F32)).astype(BF16)


def to_modes(x, table):
    xh, xl = split(x)
    half = table.shape[1] // 2
    wide = dot_cols(xh, table[...])
    return wide[:, :half] + wide[:, half:] + dot_cols(xl, table[:, 0:half])


def from_modes(z, *tables):
    zh, zl = split(z)
    three = jnp.concatenate([zh, zh, zl], axis=1)
    return jnp.concatenate([dot_cols(three, table[...]) for table in tables], axis=1)


def to_coefs(x, table):
    rows = x.shape[0]
    wide = dot_cols(jnp.concatenate(split(x), axis=0), table[...])
    half = wide.shape[1] // 2
    return wide[:rows, :half] + wide[:rows, half:] + wide[rows:, :half]


def from_coefs(z, table):
    zh, zl = split(z)
    rows = jnp.concatenate([jnp.concatenate([zh, zh], axis=1), jnp.concatenate([zl, jnp.zeros_like(zl)], axis=1)], axis=0)
    wide = dot_cols(rows, table[...])
    return wide[: z.shape[0]] + wide[z.shape[0] :]


def pack(levels):
    lane = lax.broadcasted_iota(jnp.int32, (1, RANK), 1)
    return [jnp.where(lane < USED, levels[l], roll(levels[3], 96 - 32 * l, 1)) for l in range(3)]


def unpack(parts):
    lane = lax.broadcasted_iota(jnp.int32, (1, RANK), 1)
    last = jnp.where(lane < 64, roll(parts[1], 64, 1), roll(parts[2], 96, 1))
    return parts + [jnp.where(lane < 32, roll(parts[0], 32, 1), last)]


def roll(x, shift, axis):
    return pltpu.roll(x, shift % x.shape[axis], axis)


def roll_blocks(x, shift):
    return roll(x.reshape(x.shape[0] * x.shape[1], x.shape[2]), shift, 1).reshape(x.shape)


def fold(x):
    while x.shape[0] > 1:
        half = x.shape[0] // 2
        x = x[:half] + roll_blocks(x[half:], 2 * half)
    return x


def kernel(
    bands, spread, east, north, rs, cs, cut, metric, table_in, tan_out, diag_out,
    spread_v, winds_v, rs_v, cs_v, cut_s, hm, table,
    grid, halo_out, halo_in, ybuf, yr, xb, cb, yc, zbuf, zr, eb, bz,
    tend, adj, gy,
    in_sem, halo_send, halo_recv, y_send, y_recv, c_send, c_recv, z_send, z_recv, b_send, b_recv,
):
    b = lax.axis_index("lat")
    i = lax.axis_index("lon")
    caps = POLAR // ROWS
    is_north = b == 0
    is_south = b == bands - 1
    polar = jnp.logical_or(b < caps, b >= bands - caps)
    above_polar = jnp.logical_or(b <= caps, is_south)
    below_polar = jnp.logical_or(b >= bands - caps - 1, is_north)
    near_polar = jnp.logical_or(above_polar, below_polar)
    across = lax.rem(i + LANES // 2, LANES)
    west = lax.rem(i + LANES - 1, LANES)
    east_lane = lax.rem(i + 1, LANES)
    nb = jnp.where(is_north, 0, b - 1)
    nl = jnp.where(is_north, across, i)
    sb = jnp.where(is_south, bands - 1, b + 1)
    sl = jnp.where(is_south, across, i)
    slot_n = jnp.where(is_north, 0, 1)
    slot_s = jnp.where(is_south, 1, 0)
    own_half = lax.rem(i, 2)
    edge_over = jnp.where(own_half == 0, is_north, is_south)
    over_pole = (is_north, is_south)
    outward = jnp.logical_or(
        jnp.logical_and(b == caps - 1, own_half == 1), jnp.logical_and(b == bands - caps, own_half == 0)
    )

    def plus(lane, d):
        return lax.rem(lane + d, LANES)

    load_spread = pltpu.make_async_copy(spread, spread_v, in_sem.at[0])
    load_rows = pltpu.make_async_copy(rs, rs_v, in_sem.at[1])
    load_cols = pltpu.make_async_copy(cs, cs_v, in_sem.at[2])
    load_metric = pltpu.make_async_copy(metric.at[b], hm, in_sem.at[4])
    load_cut = pltpu.make_async_copy(cut, cut_s, in_sem.at[5])

    def load_table(start, stop, sem):
        return pltpu.make_async_copy(table_in.at[start:stop], table.at[start:stop], in_sem.at[sem])

    load_forward = load_table(FORWARD, EVALUATE, 6)
    load_others = load_table(EVALUATE, TABLE_ROWS, 7)
    load_part = load_table(EVALUATE, TO_COEFS, 7)
    load_spread.start()
    load_rows.start()
    load_cols.start()

    barrier = pltpu.get_barrier_semaphore()

    def greet(lat, lon):
        pl.semaphore_signal(barrier, inc=1, device_id=(lat, lon), device_id_type=MESH)

    greet(nb, nl)
    greet(sb, sl)
    greet(b, west)
    greet(b, east_lane)
    pltpu.make_async_copy(east, winds_v.at[0], in_sem.at[3]).start()
    pltpu.make_async_copy(north, winds_v.at[1], in_sem.at[3]).start()
    load_metric.start()

    @pl.when(polar)
    def _():
        @pl.loop(2, LANES - 1)
        def _(d):
            greet(b, plus(i, d))

        load_forward.start()
        load_cut.start()

    @pl.when(jnp.logical_and(near_polar, jnp.logical_not(polar)))
    def _():
        load_part.start()

    load_rows.wait()
    load_cols.wait()
    load_spread.wait()
    grid[:, 8:24, 384:512] = jnp.zeros((PAIRS + 2 * LEV, ROWS, 128), F32)
    row_part = jnp.concatenate([rs_v[f] for f in range(FIELDS)], axis=0)
    row_part = (2 * row_part - 1).astype(F32).T
    for f in range(FIELDS):
        col_part = (2 * cs_v[f] - 1).astype(F32)
        for l in range(LEV):
            n = f * LEV + l
            grid[n, 8:24, 0:COLS] = spread_v[f, l] * (row_part[:, n : n + 1] * col_part[l : l + 1, :])

    @pl.when(polar)
    def _():
        load_others.start()

    pltpu.make_async_copy(winds_v, winds_v, in_sem.at[3]).wait()
    for w in range(2):
        for l in range(LEV):
            grid[PAIRS + w * LEV + l, 8:24, 0:COLS] = winds_v[w, l]

    def edge_rows(start, entries, rows):
        for s, row in enumerate(rows):
            for t in range(4):
                values = grid[entries, row, 128 * t : 128 * t + 128]
                if entries == slice(0, PAIRS):
                    halo_out[start[s] + t] = values
                else:
                    halo_out[start[s] + t // 2, 8 * (t % 2) : 8 * (t % 2) + 8, :] = values

    edge_rows((NEAR, NEAR + 4), slice(0, PAIRS), (8, 23))
    lane128 = lax.broadcasted_iota(jnp.int32, (1, 1, 128), 2)
    for s, (start, shift) in enumerate(((0, 0), (384, COLS - 2 - 384))):
        tile = grid[:, 8:24, start : start + 128]
        tile = jnp.where(jnp.logical_and(lane128 >= shift, lane128 < shift + 2), tile, 0.0)
        packed = fold(tile[:PAIRS]) + roll_blocks(fold(tile[PAIRS:]), 2 * PAIRS)
        halo_out[SIDES + s] = roll_blocks(packed, -shift)[0]

    pl.semaphore_wait(barrier, 4 + jnp.where(polar, LANES - 3, 0))

    def remote(src, dst, send, recv, lat, lon):
        return pltpu.make_async_remote_copy(
            src_ref=src, dst_ref=dst, send_sem=send, recv_sem=recv, device_id=(lat, lon), device_id_type=MESH
        )

    def halo_copy(start, count, to, which, lat, lon):
        return remote(
            halo_out.at[start : start + count], halo_in.at[pl.ds(to, count)], halo_send, halo_recv.at[which], lat, lon
        )

    def halo_arrival(start, stop, which):
        return remote(
            halo_out.at[start:stop], halo_in.at[start:stop], halo_send, halo_recv.at[which], b, west
        )

    halo_copy(NEAR, 4, NEAR + 4 * slot_n, 0, nb, nl).start()
    halo_copy(NEAR + 4, 4, NEAR + 4 * slot_s, 0, sb, sl).start()
    halo_copy(SIDES, 1, SIDES + 1, 0, b, west).start()
    halo_copy(SIDES + 1, 1, SIDES, 0, b, east_lane).start()

    others = pl.ds(0, LANES - 1)

    def all_y(q):
        return remote(ybuf.at[q, others], yr.at[q, others], y_send.at[q], y_recv.at[q], b, west)

    def send_values(q, x):
        y = to_modes(x.reshape(PAIRS * ROWS, WIDE), table.at[FORWARD:EVALUATE])
        y = y.reshape(FIELDS, LEV, 2, 8, RANK)
        blocks = [
            jnp.concatenate([y[f, l, h] for f in range(FIELDS) for h in range(2)], axis=0) for l in range(LEV)
        ]
        for l, part in enumerate(pack(blocks)):
            ybuf[q, :, l] = part.reshape(LANES, 8, RANK)

        @pl.loop(1, LANES)
        def _(d):
            o = plus(i, d)
            remote(ybuf.at[q, o], yr.at[q, i], y_send.at[q], y_recv.at[q], b, o).start()

        yr[q, i] = ybuf[q, i]

    def c_copy(o):
        return remote(cb.at[o], yc.at[i], c_send, c_recv, b, o)

    def all_c():
        return remote(cb.at[others], yc.at[others], c_send, c_recv, b, west)

    def z_copy(q, j):
        return remote(zbuf.at[q, j], zr.at[q, i], z_send.at[q], z_recv.at[q], b, j)

    def all_z(q):
        return remote(zbuf.at[q, others], zr.at[q, others], z_send.at[q], z_recv.at[q], b, west)

    def edge_sends():
        slot = jnp.where(own_half == 0, slot_n, slot_s)
        lat = jnp.where(own_half == 0, nb, sb)

        @pl.loop(0, LANES)
        def _(d):
            j = plus(i, d)
            lon = jnp.where(edge_over, plus(j, LANES // 2), j)
            here = jnp.logical_and(edge_over, lon == i)

            @pl.when(jnp.logical_not(here))
            def _():
                remote(eb.at[j], bz.at[slot, i // 2], b_send, b_recv.at[slot], lat, lon).start()

            @pl.when(here)
            def _():
                pltpu.make_async_copy(eb.at[j], bz.at[slot, i // 2], b_recv.at[slot]).start()

    def own_rows(q):
        row = lax.broadcasted_iota(jnp.int32, (8, 128), 0)
        cutoff = jnp.zeros((8, 128), jnp.int32)
        for r in range(8):
            cutoff = jnp.where(row == r, cut_s[8 * own_half + r], cutoff)

        all_y(q).wait_recv()
        if q == 1:
            all_c().wait_recv()

        levels = unpack([yr[q, :, l].reshape(LANES * 8, RANK) for l in range(LEV - 1)])
        lanes = []
        for j in range(LANES):
            y = [levels[l][8 * j : 8 * j + 8, :] for l in range(LEV)]
            if q == 1:
                ends = pltpu.roll(yc[j, 8:16, :], lax.rem(128 - 2 * LEV * (i // 2), 128), 1)
                edge_rows = jnp.where(row == 7 * own_half, 1.0, 0.0)
                y = [
                    y[l]
                    + ends[:, 2 * l : 2 * l + 1] * hm[0:1, :]
                    + ends[:, 2 * l + 1 : 2 * l + 2] * hm[1:2, :]
                    + edge_rows * yc[j, l : l + 1, :]
                    for l in range(LEV)
                ]
            lanes.append(jnp.concatenate(y, axis=0))
        coefs = [
            to_coefs(jnp.concatenate(pair, axis=1), table.at[TO_COEFS + 256 * group : TO_COEFS + 256 * (group + 1)])
            for group, pair in enumerate(over_lanes(lanes))
        ]
        kept = []
        for group, coef in enumerate(coefs):
            wave = waves_of(group, lax.broadcasted_iota(jnp.int32, (8, 128), 1))
            keep = jnp.where(wave > cutoff, 2.0 / (COLS * LANES), 0.0)
            kept.append(coef * jnp.concatenate([keep] * LEV, axis=0))
        backs = [
            from_coefs(coef, table.at[FROM_COEFS + 256 * group : FROM_COEFS + 256 * (group + 1)])
            for group, coef in enumerate(kept)
        ]
        pairs = [(back[:, :RANK], back[:, RANK:]) for back in backs]
        zs = [z.reshape(LEV, 8, RANK) for z in to_lanes(pairs)]
        for l, part in enumerate(pack([jnp.concatenate([z[l] for z in zs], axis=0) for l in range(LEV)])):
            zbuf[q, :, l] = part.reshape(LANES, 8, RANK)
        for j, z in enumerate(zs):
            edge = jnp.where(own_half == 0, z[:, 0, :], z[:, 7, :])
            eb[j] = edge if q == 0 else eb[j] + edge

        if q == 1:
            pl.when(outward)(edge_sends)

        @pl.loop(1, LANES)
        def _(d):
            z_copy(q, plus(i, d)).start()

        zr[q, i] = zbuf[q, i]
        if q == 1:
            pl.when(jnp.logical_not(outward))(edge_sends)

    def evaluate(z):
        return from_modes(z, table.at[EVALUATE : EVALUATE + 384], table.at[EVALUATE + 384 : TO_COEFS])

    def project(q, h):
        levels = unpack(
            [jnp.concatenate([zr[q, 2 * f + h, l] for f in range(FIELDS)], axis=0) for l in range(LEV - 1)]
        )
        z = jnp.concatenate(
            [levels[l][8 * f : 8 * f + 8, :] for f in range(FIELDS) for l in range(LEV)], axis=0
        )
        out = evaluate(z)
        return [[out[8 * (LEV * f + l) : 8 * (LEV * f + l + 1), :] for l in range(LEV)] for f in range(FIELDS)]

    def tendency_rows(h, l, at, half):
        lo = jnp.maximum(l - 1, 0)
        hi = jnp.minimum(l + 1, LEV - 1)
        ew = at(PAIRS + l, h)
        nw = at(PAIRS + LEV + l, h)
        mids, along_x, along_y = [], [], []
        for f in range(FIELDS):
            mid = at(f * LEV + l, h)
            mids.append(mid)
            along_x.append(half * (roll(mid, -1, 1) - roll(mid, 1, 1)))
            along_y.append(0.5 * (at(f * LEV + l, h + 1) - at(f * LEV + l, h - 1)))
        linked = (along_x[2], along_y[2], along_x[0] + along_y[1], None)
        out = []
        for f in range(FIELDS):
            mixed = at(f * LEV + lo, h) + at(f * LEV + hi, h) - 2.0 * mids[f]
            t = -(ew * along_x[f] + nw * along_y[f]) + mixing * mixed
            if linked[f] is not None:
                t = t - coupling * linked[f]
            out.append(time_step * t)
        return out

    def full_tendency():
        @pl.loop(0, LEV)
        def _(l):
            for h in (8, 16):
                half = jnp.concatenate([hm[h : h + 8, :]] * 4, axis=1)
                for f, t in enumerate(tendency_rows(h, l, lambda n, r: grid[n, r : r + 8, :], half)):
                    tend[f * LEV + l, h - 8 : h, :] = t

    def side_tendency():
        lane = lax.broadcasted_iota(jnp.int32, (1, 128), 1)
        late = jnp.logical_or(jnp.logical_or(lane == 65, lane == 66), lane == 127)

        def at(n, r):
            return jnp.where(lane < 2, grid[n, r : r + 8, 0:128], grid[n, r : r + 8, 384:512])

        @pl.loop(0, LEV)
        def _(l):
            for h in (8, 16):
                for f, t in enumerate(tendency_rows(h, l, at, hm[h : h + 8, :])):
                    n, rows = f * LEV + l, slice(h - 8, h)
                    tend[n, rows, 0:128] = jnp.where(lane == 0, t, tend[n, rows, 0:128])
                    tend[n, rows, 384:512] = jnp.where(late, t, tend[n, rows, 384:512])

    load_metric.wait()

    @pl.when(polar)
    def _():
        load_forward.wait()
        send_values(0, grid[0:PAIRS, 8:24, :])
        grid[0:PAIRS, 7:8, :] = jnp.zeros((PAIRS, 1, WIDE), F32)
        grid[0:PAIRS, 24:25, :] = jnp.zeros((PAIRS, 1, WIDE), F32)
        full_tendency()
        send_values(1, tend[...])

    edge_rows((REST + 4, REST + 11), slice(PAIRS, PAIRS + 2 * LEV), (8, 23))

    halo_arrival(NEAR, REST, 0).wait_recv()
    lane2 = lax.broadcasted_iota(jnp.int32, (1, 128), 1)
    row16 = lax.broadcasted_iota(jnp.int32, (PAIRS, 1), 0)
    is_v = jnp.logical_and(row16 >= LEV, row16 < 2 * LEV)
    is_temp = jnp.logical_and(row16 >= 2 * LEV, row16 < 3 * LEV)

    def flip(s, minus):
        sign = jnp.where(row16 < 2 * LEV, -1.0, 1.0) * minus
        return jnp.where(over_pole[s], sign, 1.0)

    def row_link(x):
        return jnp.where(is_v, roll(x, -LEV, 0), jnp.where(is_temp, roll(x, LEV, 0), 0.0))

    def wind(buffer, s, w):
        base = REST + 7 * s + 4
        rows = [buffer[base + t // 2, 8 * (t % 2) + LEV * w : 8 * (t % 2) + LEV * (w + 1), :] for t in range(4)]
        return jnp.concatenate([jnp.concatenate(rows, axis=1)] * FIELDS, axis=0)

    def row_of(buffer, start):
        return jnp.concatenate([buffer[start + t] for t in range(4)], axis=1)

    @pl.when(polar)
    def _():
        added = []
        for s, sign in ((0, 0.5 * time_step), (1, -0.5 * time_step)):
            ghost = flip(s, 1.0) * row_of(halo_in, NEAR + 4 * s)
            added.append(sign * (wind(halo_out, s, 1) * ghost + coupling * row_link(ghost)))
            xb[s] = added[s]
        y = to_modes(jnp.concatenate(added, axis=0), table.at[FORWARD:EVALUATE])
        for s in range(2):
            for f in range(FIELDS):
                cb[2 * f + s, 0:LEV, :] = y[(s * FIELDS + f) * LEV : (s * FIELDS + f + 1) * LEV, :]
        ends = []
        for side, sign in ((0, -1.0), (1, 1.0)):
            came = halo_in[SIDES + side]
            along_x = (sign * hm[8:24, :]) * (roll(came, -1, 1) if side == 0 else came)
            mine = jnp.where(
                jnp.logical_and(lane2 >= 2 * PAIRS, lane2 < 2 * (PAIRS + LEV)), halo_out[SIDES + side], 0.0
            )
            ew = sum(roll(mine, 2 * LEV * f - 2 * PAIRS - side, 1) for f in range(FIELDS))
            linked = jnp.where(
                lane2 < 2 * LEV,
                roll(along_x, -4 * LEV, 1),
                jnp.where(
                    jnp.logical_and(lane2 >= 4 * LEV, lane2 < 6 * LEV), roll(along_x, 4 * LEV, 1), 0.0
                ),
            )
            ends.append(time_step * (-ew * along_x - coupling * linked))
        ends = jnp.where(lax.rem(lane2, 2) == 0, ends[0], roll(ends[1], 1, 1))
        for f in range(FIELDS):
            for h in range(2):
                cb[2 * f + h, 8:16, :] = ends[8 * h : 8 * h + 8, :]

        @pl.loop(1, LANES)
        def _(d):
            c_copy(plus(i, d)).start()

        yc[i] = cb[i]

    @pl.when(polar)
    def _():
        load_cut.wait()
        load_others.wait()
        own_rows(0)

    from_west = roll(halo_in[SIDES], 126, 1)
    from_east = roll(halo_in[SIDES + 1], COLS - 384, 1)
    both = jnp.where(jnp.logical_and(lane2 >= 66, lane2 < 114), from_east, from_west)[None]
    for width in (2, 4, 8):
        both = jnp.concatenate([both, roll_blocks(both, -width)], axis=0)
    both = jnp.concatenate([both, roll_blocks(both, -16), roll_blocks(both, -32)], axis=0)
    in_halo = jnp.logical_or(jnp.logical_and(lane128 >= 66, lane128 < 68), lane128 >= 126)
    grid[:, 8:24, 384:512] = jnp.where(in_halo, both, grid[:, 8:24, 384:512])
    edge_rows((REST, REST + 7), slice(0, PAIRS), (9, 22))
    for s, near in enumerate((8, 23)):
        halo_out[REST + 7 * s + 6] = grid[0:PAIRS, near, 384:512]
    halo_copy(REST, 7, REST + 7 * slot_n, 1, nb, nl).start()
    halo_copy(REST + 7, 7, REST + 7 * slot_s, 1, sb, sl).start()

    @pl.when(polar)
    def _():
        own_rows(1)

    halo_arrival(REST, BLOCKS, 1).wait_recv()
    edge_row = (7, 24)
    edge_probe = []
    for s in range(2):
        edge_probe.append(
            jnp.concatenate([halo_in[NEAR + 4 * s + t] for t in range(3)] + [halo_in[REST + 7 * s + 6]], axis=1)
        )
        grid[0:PAIRS, edge_row[s], :] = flip(s, 1.0) * edge_probe[s]

    @pl.when(polar)
    def _():
        for s, row in ((0, 0), (1, 15)):
            tend[:, row, :] = tend[:, row, :] + xb[s]
        side_tendency()

    @pl.when(jnp.logical_not(polar))
    def _():
        full_tendency()

    def edge_weights(s, a):
        return -wind(halo_in, s, 1) * a - coupling * row_link(a)

    for s, inward in ((0, 1.0), (1, -1.0)):
        mid = edge_probe[s]
        half = jnp.concatenate([hm[edge_row[s] : edge_row[s] + 1, :]] * 4, axis=1)
        along_x = half * (roll(mid, -1, 1) - roll(mid, 1, 1))
        turn = jnp.where(over_pole[s], -0.5 * inward, 0.5 * inward)
        along_y = turn * (flip(s, 1.0) * row_of(halo_out, NEAR + 4 * s) - row_of(halo_in, REST + 7 * s))
        linked = jnp.where(row16 < LEV, roll(along_x, -2 * LEV, 0), row_link(along_y))
        linked = linked + jnp.where(is_temp, roll(along_x, 2 * LEV, 0), 0.0)
        up = jnp.where(lax.rem(row16, LEV) == 0, mid, roll(mid, 1, 0))
        down = jnp.where(lax.rem(row16, LEV) == LEV - 1, mid, roll(mid, -1, 0))
        t = -(wind(halo_in, s, 0) * along_x + wind(halo_in, s, 1) * along_y) - coupling * linked
        a = mid + time_step * (t + mixing * (up + down - 2.0 * mid))
        gy[0:PAIRS, edge_row[s], :] = flip(s, -1.0) * edge_weights(s, a)

    def row_weights(a, nw):
        return (
            -nw * a[0],
            -nw * a[1] - coupling * a[2],
            -nw * a[2] - coupling * a[1],
            -nw * a[3],
        )

    def put_weights(l, h, a):
        for f, weight in enumerate(row_weights(a, grid[PAIRS + LEV + l, h : h + 8, :])):
            gy[f * LEV + l, h : h + 8, :] = weight

    @pl.when(polar)
    def _():
        all_z(0).wait_recv()
        for h in (8, 16):
            taken = project(0, h // 8 - 1)
            for l in range(LEV):
                for f in range(FIELDS):
                    n, rows = f * LEV + l, slice(h - 8, h)
                    adj[n, rows, :] = grid[n, h : h + 8, :] + tend[n, rows, :] - taken[f][l]
        all_z(1).wait_recv()
        for h in (8, 16):
            taken = project(1, h // 8 - 1)
            for l in range(LEV):
                a = []
                for f in range(FIELDS):
                    n, rows = f * LEV + l, slice(h - 8, h)
                    change = tend[n, rows, :] - taken[f][l]
                    tend[n, rows, :] = change
                    tan_out[f, l, rows, :] = (grid[n, h : h + 8, :] + change)[:, :COLS]
                    a.append(adj[n, rows, :] - taken[f][l])
                    adj[n, rows, :] = a[f]
                put_weights(l, h, a)

    @pl.when(jnp.logical_not(polar))
    def _():
        @pl.loop(0, LEV)
        def _(l):
            for h in (8, 16):
                a = []
                for f in range(FIELDS):
                    n, rows = f * LEV + l, slice(h - 8, h)
                    a.append(grid[n, h : h + 8, :] + tend[n, rows, :])
                    tan_out[f, l, rows, :] = a[f][:, :COLS]
                    adj[n, rows, :] = a[f]
                put_weights(l, h, a)

    @pl.loop(0, LEV)
    def _(l):
        lo = jnp.maximum(l - 1, 0)
        hi = jnp.minimum(l + 1, LEV - 1)
        for h in (8, 16):
            rows = slice(h - 8, h)
            half = jnp.concatenate([hm[h : h + 8, :]] * 4, axis=1)
            ew = grid[PAIRS + l, h : h + 8, :]
            a = [adj[f * LEV + l, rows, :] for f in range(FIELDS)]
            col_weights = (
                -ew * a[0] - coupling * a[2],
                -ew * a[1],
                -ew * a[2] - coupling * a[0],
                -ew * a[3],
            )
            for f in range(FIELDS):
                n = f * LEV + l
                back = half * (roll(col_weights[f], 1, 1) - roll(col_weights[f], -1, 1))
                back = back + 0.5 * (gy[n, h - 1 : h + 7, :] - gy[n, h + 1 : h + 9, :])
                back = back + mixing * (adj[f * LEV + lo, rows, :] + adj[f * LEV + hi, rows, :] - 2.0 * a[f])
                diag = grid[n, h : h + 8, :] * (tend[n, rows, :] + time_step * back)
                diag_out[f, l, rows, :] = diag[:, :COLS]

    @pl.when(jnp.logical_and(near_polar, jnp.logical_not(polar)))
    def _():
        load_part.wait()

    for s, wanted in enumerate((above_polar, below_polar)):
        @pl.when(wanted)
        def _():
            remote(bz.at[s], bz.at[s], b_send, b_recv.at[s], nb, nl).wait_recv()

        @pl.when(jnp.logical_not(wanted))
        def _():
            bz[s] = jnp.zeros((FIELDS, LEV, RANK), F32)

    @pl.when(near_polar)
    def _():
        taken = evaluate(jnp.concatenate([bz[s, f] for s in range(2) for f in range(FIELDS)], axis=0))
        for s, wanted in enumerate((above_polar, below_polar)):
            @pl.when(wanted)
            def _():
                row = 15 * s
                weight = flip(s, -1.0) * edge_weights(s, taken[PAIRS * s : PAIRS * (s + 1), :])
                less = ((0.5, -0.5)[s] * time_step) * grid[0:PAIRS, 8 + row, :] * weight
                for f in range(FIELDS):
                    diag_out[f, :, row, :] = diag_out[f, :, row, :] - less[f * LEV : (f + 1) * LEV, :COLS]

    halo_arrival(0, BLOCKS, 0).wait_send()

    @pl.when(polar)
    def _():
        all_c().wait_send()
        for q in range(2):
            all_y(q).wait_send()
            all_z(q).wait_send()

        @pl.when(edge_over)
        def _():
            remote(eb.at[others], eb.at[others], b_send, b_recv.at[0], b, west).wait_send()

        @pl.when(jnp.logical_not(edge_over))
        def _():
            remote(eb, eb, b_send, b_recv.at[0], b, west).wait_send()


def hand_out(tan_in, diag_in, tan_out, diag_out, sem):
    copies = [
        pltpu.make_async_copy(src.at[f], dst.at[f], sem.at[n, f])
        for n, (src, dst) in enumerate(((tan_in, tan_out), (diag_in, diag_out)))
        for f in range(FIELDS)
    ]
    for copy in copies:
        copy.start()
    for copy in copies:
        copy.wait()


def per_device(bands, row_signs, col_signs, spread, east_wind, north_wind, cutoffs):
    any_spec = pl.BlockSpec(memory_space=pl.ANY)
    out = jax.ShapeDtypeStruct((FIELDS, LEV, ROWS, COLS), F32)
    tables = [jnp.asarray(half_metric(bands)), jnp.asarray(mode_factors())]
    operands = (spread, east_wind, north_wind, row_signs, col_signs, cutoffs, *tables)
    vmem = pltpu.VMEM
    dma = pltpu.SemaphoreType.DMA
    held = pltpu.VMEM(out.shape, F32)
    results = pl.pallas_call(
        functools.partial(kernel, bands),
        out_shape=(held, held),
        in_specs=[any_spec] * 8,
        out_specs=(pl.BlockSpec(memory_space=pltpu.VMEM),) * 2,
        scratch_shapes=[
            vmem((FIELDS, LEV, ROWS, COLS), F32),
            vmem((2, LEV, ROWS, COLS), F32),
            vmem((FIELDS, LEV, ROWS), jnp.int32),
            vmem((FIELDS, LEV, COLS), jnp.int32),
            pltpu.SMEM((ROWS,), jnp.int32),
            vmem((32, 128), F32),
            vmem((TABLE_ROWS, 2 * RANK), BF16),
            vmem((PAIRS + 2 * LEV, 32, WIDE), F32),
            vmem((BLOCKS, 16, 128), F32),
            vmem((BLOCKS, 16, 128), F32),
            vmem((2, LANES, LEV - 1, 8, RANK), F32),
            vmem((2, LANES, LEV - 1, 8, RANK), F32),
            vmem((2, PAIRS, WIDE), F32),
            vmem((LANES, 16, RANK), F32),
            vmem((LANES, 16, RANK), F32),
            vmem((2, LANES, LEV - 1, 8, RANK), F32),
            vmem((2, LANES, LEV - 1, 8, RANK), F32),
            vmem((LANES, LEV, RANK), F32),
            vmem((2, FIELDS, LEV, RANK), F32),
            vmem((PAIRS, ROWS, WIDE), F32),
            vmem((PAIRS, ROWS, WIDE), F32),
            vmem((PAIRS, 32, WIDE), F32),
            dma((8,)),
            dma,
            dma((2,)),
            dma((2,)),
            dma((2,)),
            dma,
            dma,
            dma((2,)),
            dma((2,)),
            dma,
            dma((2,)),
        ],
        compiler_params=pltpu.CompilerParams(
            collective_id=0, has_side_effects=True, vmem_limit_bytes=32 * 2**20
        ),
        cost_estimate=pl.CostEstimate(flops=10**9, bytes_accessed=4 * 10**6, transcendentals=0),
    )(*(pltpu.with_memory_space_constraint(x, pltpu.HBM) for x in operands))
    return pl.pallas_call(
        hand_out,
        out_shape=(out, out),
        in_specs=[any_spec] * 2,
        out_specs=(any_spec, any_spec),
        scratch_shapes=[dma((2, FIELDS))],
        compiler_params=pltpu.CompilerParams(vmem_limit_bytes=2**20),
    )(*(pltpu.with_memory_space_constraint(x, pltpu.VMEM) for x in results))


def solution(mesh):
    return jax.shard_map(
        functools.partial(per_device, mesh.shape["lat"]),
        mesh=mesh,
        in_specs=(
            P(None, None, "lat"),
            P(None, None, "lon"),
            P(None, None, "lat", "lon"),
            P(None, "lat", "lon"),
            P(None, "lat", "lon"),
            P("lat"),
        ),
        out_specs=(P(None, None, "lat", "lon"), P(None, None, "lat", "lon")),
        check_vma=False,
    )
```

```python
import functools

import jax
import jax.numpy as jnp
import ml_dtypes
import numpy as np
from jax import lax
from jax.experimental import pallas as pl
from jax.experimental.pallas import tpu as pltpu
from jax.sharding import PartitionSpec as P

KTOP = 256
POLAR = 32
RANK = 128
USED = 96
ROWS = 16
COLS = 450
WIDE = 512
LANES = 8
FIELDS = 4
LEV = 4
PAIRS = FIELDS * LEV

time_step = 0.5
coupling = 0.5
mixing = 0.2
metric_cap = 4.0

FORWARD, EVALUATE, TO_COEFS, FROM_COEFS, TABLE_ROWS = 0, 512, 1280, 2304, 3328
NEAR, SIDES, REST, BLOCKS = 0, 8, 10, 24

FAR_FIRST = (6, 2, 5, 3, 7, 1, 4)

MESH = pl.DeviceIdType.MESH
F32 = jnp.float32
BF16 = jnp.bfloat16


def split_table(table):
    high = table.astype(ml_dtypes.bfloat16)
    low = (table - high.astype(np.float64)).astype(ml_dtypes.bfloat16)
    return high, low


def waves_of(group, lane_index):
    place = lane_index % 64
    second = place // 32
    other = (8 - group) if group else 4
    residue = group + second * (other - group)
    return 8 * (place % 32) + residue + (8 * (1 - second) if group == 0 else 0)


@functools.lru_cache(None)
def mode_factors():
    total = COLS * LANES
    size = COLS + 2
    place = np.arange(size, dtype=np.float64)
    width = (KTOP + 0.5) / total
    diag = ((size - 1 - 2 * place) / 2) ** 2 * np.cos(2 * np.pi * width)
    side = place[1:] * (size - place[1:]) / 2
    vectors = np.linalg.eigh(np.diag(diag) + np.diag(side, 1) + np.diag(side, -1))[1]
    basis = np.concatenate([vectors[:, ::-1][:, :USED], np.zeros((size, RANK - USED))], axis=1)
    basis = basis * np.where(basis[size // 2] < 0, -1.0, 1.0)
    weights = []
    for group in range(4):
        waves = waves_of(group, np.arange(64))
        angle = 2 * np.pi / total * ((np.arange(size)[:, None] - 1) * waves[None, :] % total)
        alpha, beta = basis.T @ np.cos(angle), basis.T @ np.sin(angle)
        if group:
            sign = np.where(np.arange(64) < 32, 1.0, -1.0)
            top, low = (alpha, beta), (sign * beta, -sign * alpha)
        else:
            use = np.where(np.arange(64) < 32, 1.0, 0.0)
            top, low = (use * alpha, use * beta), ((1 - use) * alpha, (1 - use) * beta)
        weights.append(np.concatenate([np.concatenate(top, axis=1), np.concatenate(low, axis=1)], axis=0))
    weights = np.round(np.stack(weights) * 2.0**22) / 2.0**22
    wide = np.zeros((RANK, WIDE))
    wide[:, : COLS + 1] = basis[1:].T
    wide[:, WIDE - 1] = basis[0]
    wide = np.round(wide * 2.0**26) / 2.0**26
    wide_h, wide_l = split_table(wide)
    own = np.where(np.arange(WIDE)[:, None] < COLS, 1, 0).astype(ml_dtypes.bfloat16)
    high, low = split_table(weights)
    back = np.concatenate([np.swapaxes(part, 1, 2) for part in (high, low)], axis=1)
    evaluate = np.concatenate([wide_h, wide_l, wide_h], axis=0)
    return np.concatenate(
        [
            np.concatenate([wide_h.T * own, wide_l.T * own], axis=1),
            evaluate[:, : WIDE // 2],
            evaluate[:, WIDE // 2 :],
            np.concatenate([high, low], axis=2).reshape(-1, 2 * RANK),
            back.reshape(-1, 2 * RANK),
        ],
        axis=0,
    )


ROOT = float(np.sqrt(0.5))


def over_lanes(y):
    s = [y[j] + y[j + 4] for j in range(4)]
    d = [y[j] - y[j + 4] for j in range(4)]
    even, odd = s[0] + s[2], s[1] + s[3]
    minus, plus = ROOT * (d[1] - d[3]), ROOT * (d[1] + d[3])
    return [
        (even + odd, even - odd),
        (d[0] + minus, -(d[2] + plus)),
        (s[0] - s[2], s[3] - s[1]),
        (d[0] - minus, d[2] - plus),
    ]


def to_lanes(pairs):
    (y0, y4), (u1, v1), (u2, v2), (u3, v3) = pairs
    even, odd = y0 + y4, y0 - y4
    s = [even + u2, odd - v2, even - u2, odd + v2]
    du, sv = ROOT * (u1 - u3), ROOT * (v1 + v3)
    d = [u1 + u3, du - sv, v3 - v1, -du - sv]
    return [s[j] + d[j] for j in range(4)] + [s[j] - d[j] for j in range(4)]


@functools.lru_cache(None)
def half_metric(bands):
    total = bands * ROWS
    rows = np.clip(np.arange(bands)[:, None] * ROWS - 8 + np.arange(32)[None, :], 0, total - 1)
    metric = np.minimum(1.0 / np.cos(np.pi * ((rows + 0.5) / total - 0.5)), metric_cap)
    table = np.broadcast_to((0.5 * metric).astype(np.float32)[:, :, None], (bands, 32, 128)).copy()
    forward = mode_factors()[FORWARD : FORWARD + WIDE].astype(np.float32)
    for row, col in enumerate((0, COLS - 1)):
        table[:, row] = forward[col, :RANK] + forward[col, RANK:]
    return table


def dot_cols(a, b):
    return lax.dot_general(a, b, (((1,), (0,)), ((), ())), preferred_element_type=F32)


def split(x):
    high = x.astype(BF16)
    return high, (x - high.astype(F32)).astype(BF16)


def to_modes(x, table):
    xh, xl = split(x)
    half = table.shape[1] // 2
    wide = dot_cols(xh, table[...])
    return wide[:, :half] + wide[:, half:] + dot_cols(xl, table[:, 0:half])


def from_modes(z, *tables):
    zh, zl = split(z)
    three = jnp.concatenate([zh, zh, zl], axis=1)
    return jnp.concatenate([dot_cols(three, table[...]) for table in tables], axis=1)


def to_coefs(x, table):
    rows = x.shape[0]
    wide = dot_cols(jnp.concatenate(split(x), axis=0), table[...])
    half = wide.shape[1] // 2
    return wide[:rows, :half] + wide[:rows, half:] + wide[rows:, :half]


def from_coefs(z, table):
    zh, zl = split(z)
    rows = jnp.concatenate([jnp.concatenate([zh, zh], axis=1), jnp.concatenate([zl, jnp.zeros_like(zl)], axis=1)], axis=0)
    wide = dot_cols(rows, table[...])
    return wide[: z.shape[0]] + wide[z.shape[0] :]


def pack(levels):
    lane = lax.broadcasted_iota(jnp.int32, (1, RANK), 1)
    return [jnp.where(lane < USED, levels[l], roll(levels[3], 96 - 32 * l, 1)) for l in range(3)]


def unpack(parts):
    lane = lax.broadcasted_iota(jnp.int32, (1, RANK), 1)
    last = jnp.where(lane < 64, roll(parts[1], 64, 1), roll(parts[2], 96, 1))
    return parts + [jnp.where(lane < 32, roll(parts[0], 32, 1), last)]


def roll(x, shift, axis):
    return pltpu.roll(x, shift % x.shape[axis], axis)


def roll_blocks(x, shift):
    return roll(x.reshape(x.shape[0] * x.shape[1], x.shape[2]), shift, 1).reshape(x.shape)


def fold(x):
    while x.shape[0] > 1:
        half = x.shape[0] // 2
        x = x[:half] + roll_blocks(x[half:], 2 * half)
    return x


def kernel(
    bands, spread, east, north, rs, cs, cut, metric, table_in, tan_out, diag_out,
    spread_v, winds_v, rs_v, cs_v, cut_s, hm, table,
    grid, halo_out, halo_in, ybuf, yr, xb, cb, yc, zbuf, zr, eb, bz,
    tend, adj, gy,
    in_sem, halo_send, halo_recv, y_send, y_recv, c_send, c_recv, z_send, z_recv, b_send, b_recv,
):
    b = lax.axis_index("lat")
    i = lax.axis_index("lon")
    caps = POLAR // ROWS
    is_north = b == 0
    is_south = b == bands - 1
    polar = jnp.logical_or(b < caps, b >= bands - caps)
    above_polar = jnp.logical_or(b <= caps, is_south)
    below_polar = jnp.logical_or(b >= bands - caps - 1, is_north)
    near_polar = jnp.logical_or(above_polar, below_polar)
    across = lax.rem(i + LANES // 2, LANES)
    west = lax.rem(i + LANES - 1, LANES)
    east_lane = lax.rem(i + 1, LANES)
    nb = jnp.where(is_north, 0, b - 1)
    nl = jnp.where(is_north, across, i)
    sb = jnp.where(is_south, bands - 1, b + 1)
    sl = jnp.where(is_south, across, i)
    slot_n = jnp.where(is_north, 0, 1)
    slot_s = jnp.where(is_south, 1, 0)
    own_half = lax.rem(i, 2)
    edge_over = jnp.where(own_half == 0, is_north, is_south)
    over_pole = (is_north, is_south)
    outward = jnp.logical_or(
        jnp.logical_and(b == caps - 1, own_half == 1), jnp.logical_and(b == bands - caps, own_half == 0)
    )

    def plus(lane, d):
        return lax.rem(lane + d, LANES)

    load_spread = pltpu.make_async_copy(spread, spread_v, in_sem.at[0])
    load_rows = pltpu.make_async_copy(rs, rs_v, in_sem.at[1])
    load_cols = pltpu.make_async_copy(cs, cs_v, in_sem.at[2])
    load_metric = pltpu.make_async_copy(metric.at[b], hm, in_sem.at[4])
    load_cut = pltpu.make_async_copy(cut, cut_s, in_sem.at[5])

    def load_table(start, stop, sem):
        return pltpu.make_async_copy(table_in.at[start:stop], table.at[start:stop], in_sem.at[sem])

    load_forward = load_table(FORWARD, EVALUATE, 6)
    load_others = load_table(EVALUATE, TABLE_ROWS, 7)
    load_part = load_table(EVALUATE, TO_COEFS, 7)
    barrier = pltpu.get_barrier_semaphore()

    def greet(lat, lon):
        pl.semaphore_signal(barrier, inc=1, device_id=(lat, lon), device_id_type=MESH)

    @pl.when(polar)
    def _():
        for d in FAR_FIRST[:4]:
            greet(b, plus(i, d))

    greet(nb, nl)
    greet(sb, sl)
    greet(b, west)
    greet(b, east_lane)
    load_spread.start()
    load_rows.start()
    load_cols.start()
    pltpu.make_async_copy(east, winds_v.at[0], in_sem.at[3]).start()
    pltpu.make_async_copy(north, winds_v.at[1], in_sem.at[3]).start()
    load_metric.start()

    @pl.when(polar)
    def _():
        greet(b, across)
        load_forward.start()
        load_cut.start()

    @pl.when(jnp.logical_and(near_polar, jnp.logical_not(polar)))
    def _():
        load_part.start()

    load_rows.wait()
    load_cols.wait()
    load_spread.wait()
    grid[:, 8:24, 384:512] = jnp.zeros((PAIRS + 2 * LEV, ROWS, 128), F32)
    row_part = jnp.concatenate([rs_v[f] for f in range(FIELDS)], axis=0)
    row_part = (2 * row_part - 1).astype(F32).T
    for f in range(FIELDS):
        col_part = (2 * cs_v[f] - 1).astype(F32)
        for l in range(LEV):
            n = f * LEV + l
            grid[n, 8:24, 0:COLS] = spread_v[f, l] * (row_part[:, n : n + 1] * col_part[l : l + 1, :])

    @pl.when(polar)
    def _():
        load_others.start()

    pltpu.make_async_copy(winds_v, winds_v, in_sem.at[3]).wait()
    for w in range(2):
        for l in range(LEV):
            grid[PAIRS + w * LEV + l, 8:24, 0:COLS] = winds_v[w, l]

    def edge_rows(start, entries, rows):
        for s, row in enumerate(rows):
            for t in range(4):
                values = grid[entries, row, 128 * t : 128 * t + 128]
                if entries == slice(0, PAIRS):
                    halo_out[start[s] + t] = values
                else:
                    halo_out[start[s] + t // 2, 8 * (t % 2) : 8 * (t % 2) + 8, :] = values

    edge_rows((NEAR, NEAR + 4), slice(0, PAIRS), (8, 23))
    lane128 = lax.broadcasted_iota(jnp.int32, (1, 1, 128), 2)
    for s, (start, shift) in enumerate(((0, 0), (384, COLS - 2 - 384))):
        tile = grid[:, 8:24, start : start + 128]
        tile = jnp.where(jnp.logical_and(lane128 >= shift, lane128 < shift + 2), tile, 0.0)
        packed = fold(tile[:PAIRS]) + roll_blocks(fold(tile[PAIRS:]), 2 * PAIRS)
        halo_out[SIDES + s] = roll_blocks(packed, -shift)[0]

    pl.semaphore_wait(barrier, 4 + jnp.where(polar, LANES - 3, 0))

    def remote(src, dst, send, recv, lat, lon):
        return pltpu.make_async_remote_copy(
            src_ref=src, dst_ref=dst, send_sem=send, recv_sem=recv, device_id=(lat, lon), device_id_type=MESH
        )

    def halo_copy(start, count, to, which, lat, lon):
        return remote(
            halo_out.at[start : start + count], halo_in.at[pl.ds(to, count)], halo_send, halo_recv.at[which], lat, lon
        )

    def halo_arrival(start, stop, which):
        return remote(
            halo_out.at[start:stop], halo_in.at[start:stop], halo_send, halo_recv.at[which], b, west
        )

    halo_copy(NEAR, 4, NEAR + 4 * slot_n, 0, nb, nl).start()
    halo_copy(NEAR + 4, 4, NEAR + 4 * slot_s, 0, sb, sl).start()
    halo_copy(SIDES, 1, SIDES + 1, 0, b, west).start()
    halo_copy(SIDES + 1, 1, SIDES, 0, b, east_lane).start()

    others = pl.ds(0, LANES - 1)

    def all_y(q):
        return remote(ybuf.at[q, others], yr.at[q, others], y_send.at[q], y_recv.at[q], b, west)

    def send_values(q, x):
        y = to_modes(x.reshape(PAIRS * ROWS, WIDE), table.at[FORWARD:EVALUATE])
        y = y.reshape(FIELDS, LEV, 2, 8, RANK)
        blocks = [
            jnp.concatenate([y[f, l, h] for f in range(FIELDS) for h in range(2)], axis=0) for l in range(LEV)
        ]
        for l, part in enumerate(pack(blocks)):
            ybuf[q, :, l] = part.reshape(LANES, 8, RANK)

        for d in FAR_FIRST:
            o = plus(i, d)
            remote(ybuf.at[q, o], yr.at[q, i], y_send.at[q], y_recv.at[q], b, o).start()

        yr[q, i] = ybuf[q, i]

    def c_copy(o):
        return remote(cb.at[o], yc.at[i], c_send, c_recv, b, o)

    def all_c():
        return remote(cb.at[others], yc.at[others], c_send, c_recv, b, west)

    def z_copy(q, j):
        return remote(zbuf.at[q, j], zr.at[q, i], z_send.at[q], z_recv.at[q], b, j)

    def all_z(q):
        return remote(zbuf.at[q, others], zr.at[q, others], z_send.at[q], z_recv.at[q], b, west)

    def edge_sends():
        slot = jnp.where(own_half == 0, slot_n, slot_s)
        lat = jnp.where(own_half == 0, nb, sb)

        @pl.loop(0, LANES)
        def _(d):
            j = plus(i, d)
            lon = jnp.where(edge_over, plus(j, LANES // 2), j)
            here = jnp.logical_and(edge_over, lon == i)

            @pl.when(jnp.logical_not(here))
            def _():
                remote(eb.at[j], bz.at[slot, i // 2], b_send, b_recv.at[slot], lat, lon).start()

            @pl.when(here)
            def _():
                pltpu.make_async_copy(eb.at[j], bz.at[slot, i // 2], b_recv.at[slot]).start()

    def own_rows(q):
        row = lax.broadcasted_iota(jnp.int32, (8, 128), 0)
        cutoff = jnp.zeros((8, 128), jnp.int32)
        for r in range(8):
            cutoff = jnp.where(row == r, cut_s[8 * own_half + r], cutoff)

        all_y(q).wait_recv()
        if q == 1:
            all_c().wait_recv()

        levels = unpack([yr[q, :, l].reshape(LANES * 8, RANK) for l in range(LEV - 1)])
        lanes = []
        for j in range(LANES):
            y = [levels[l][8 * j : 8 * j + 8, :] for l in range(LEV)]
            if q == 1:
                ends = pltpu.roll(yc[j, 8:16, :], lax.rem(128 - 2 * LEV * (i // 2), 128), 1)
                edge_rows = jnp.where(row == 7 * own_half, 1.0, 0.0)
                y = [
                    y[l]
                    + ends[:, 2 * l : 2 * l + 1] * hm[0:1, :]
                    + ends[:, 2 * l + 1 : 2 * l + 2] * hm[1:2, :]
                    + edge_rows * yc[j, l : l + 1, :]
                    for l in range(LEV)
                ]
            lanes.append(jnp.concatenate(y, axis=0))
        coefs = [
            to_coefs(jnp.concatenate(pair, axis=1), table.at[TO_COEFS + 256 * group : TO_COEFS + 256 * (group + 1)])
            for group, pair in enumerate(over_lanes(lanes))
        ]
        kept = []
        for group, coef in enumerate(coefs):
            wave = waves_of(group, lax.broadcasted_iota(jnp.int32, (8, 128), 1))
            keep = jnp.where(wave > cutoff, 2.0 / (COLS * LANES), 0.0)
            kept.append(coef * jnp.concatenate([keep] * LEV, axis=0))
        backs = [
            from_coefs(coef, table.at[FROM_COEFS + 256 * group : FROM_COEFS + 256 * (group + 1)])
            for group, coef in enumerate(kept)
        ]
        pairs = [(back[:, :RANK], back[:, RANK:]) for back in backs]
        zs = [z.reshape(LEV, 8, RANK) for z in to_lanes(pairs)]
        for l, part in enumerate(pack([jnp.concatenate([z[l] for z in zs], axis=0) for l in range(LEV)])):
            zbuf[q, :, l] = part.reshape(LANES, 8, RANK)
        for j, z in enumerate(zs):
            edge = jnp.where(own_half == 0, z[:, 0, :], z[:, 7, :])
            eb[j] = edge if q == 0 else eb[j] + edge

        if q == 1:
            pl.when(outward)(edge_sends)

        for d in FAR_FIRST:
            z_copy(q, plus(i, d)).start()

        zr[q, i] = zbuf[q, i]
        if q == 1:
            pl.when(jnp.logical_not(outward))(edge_sends)

    def evaluate(z):
        return from_modes(z, table.at[EVALUATE : EVALUATE + 384], table.at[EVALUATE + 384 : TO_COEFS])

    def project(q, h):
        levels = unpack(
            [jnp.concatenate([zr[q, 2 * f + h, l] for f in range(FIELDS)], axis=0) for l in range(LEV - 1)]
        )
        z = jnp.concatenate(
            [levels[l][8 * f : 8 * f + 8, :] for f in range(FIELDS) for l in range(LEV)], axis=0
        )
        out = evaluate(z)
        return [[out[8 * (LEV * f + l) : 8 * (LEV * f + l + 1), :] for l in range(LEV)] for f in range(FIELDS)]

    def tendency_rows(h, l, at, half):
        lo = jnp.maximum(l - 1, 0)
        hi = jnp.minimum(l + 1, LEV - 1)
        ew = at(PAIRS + l, h)
        nw = at(PAIRS + LEV + l, h)
        mids, along_x, along_y = [], [], []
        for f in range(FIELDS):
            mid = at(f * LEV + l, h)
            mids.append(mid)
            along_x.append(half * (roll(mid, -1, 1) - roll(mid, 1, 1)))
            along_y.append(0.5 * (at(f * LEV + l, h + 1) - at(f * LEV + l, h - 1)))
        linked = (along_x[2], along_y[2], along_x[0] + along_y[1], None)
        out = []
        for f in range(FIELDS):
            mixed = at(f * LEV + lo, h) + at(f * LEV + hi, h) - 2.0 * mids[f]
            t = -(ew * along_x[f] + nw * along_y[f]) + mixing * mixed
            if linked[f] is not None:
                t = t - coupling * linked[f]
            out.append(time_step * t)
        return out

    def full_tendency():
        @pl.loop(0, LEV)
        def _(l):
            for h in (8, 16):
                half = jnp.concatenate([hm[h : h + 8, :]] * 4, axis=1)
                for f, t in enumerate(tendency_rows(h, l, lambda n, r: grid[n, r : r + 8, :], half)):
                    tend[f * LEV + l, h - 8 : h, :] = t

    def side_tendency():
        lane = lax.broadcasted_iota(jnp.int32, (1, 128), 1)
        late = jnp.logical_or(jnp.logical_or(lane == 65, lane == 66), lane == 127)

        def at(n, r):
            return jnp.where(lane < 2, grid[n, r : r + 8, 0:128], grid[n, r : r + 8, 384:512])

        @pl.loop(0, LEV)
        def _(l):
            for h in (8, 16):
                for f, t in enumerate(tendency_rows(h, l, at, hm[h : h + 8, :])):
                    n, rows = f * LEV + l, slice(h - 8, h)
                    tend[n, rows, 0:128] = jnp.where(lane == 0, t, tend[n, rows, 0:128])
                    tend[n, rows, 384:512] = jnp.where(late, t, tend[n, rows, 384:512])

    load_metric.wait()

    @pl.when(polar)
    def _():
        load_forward.wait()
        send_values(0, grid[0:PAIRS, 8:24, :])
        grid[0:PAIRS, 7:8, :] = jnp.zeros((PAIRS, 1, WIDE), F32)
        grid[0:PAIRS, 24:25, :] = jnp.zeros((PAIRS, 1, WIDE), F32)
        full_tendency()
        send_values(1, tend[...])

    edge_rows((REST + 4, REST + 11), slice(PAIRS, PAIRS + 2 * LEV), (8, 23))

    halo_arrival(NEAR, REST, 0).wait_recv()
    lane2 = lax.broadcasted_iota(jnp.int32, (1, 128), 1)
    row16 = lax.broadcasted_iota(jnp.int32, (PAIRS, 1), 0)
    is_v = jnp.logical_and(row16 >= LEV, row16 < 2 * LEV)
    is_temp = jnp.logical_and(row16 >= 2 * LEV, row16 < 3 * LEV)

    def flip(s, minus):
        sign = jnp.where(row16 < 2 * LEV, -1.0, 1.0) * minus
        return jnp.where(over_pole[s], sign, 1.0)

    def row_link(x):
        return jnp.where(is_v, roll(x, -LEV, 0), jnp.where(is_temp, roll(x, LEV, 0), 0.0))

    def wind(buffer, s, w):
        base = REST + 7 * s + 4
        rows = [buffer[base + t // 2, 8 * (t % 2) + LEV * w : 8 * (t % 2) + LEV * (w + 1), :] for t in range(4)]
        return jnp.concatenate([jnp.concatenate(rows, axis=1)] * FIELDS, axis=0)

    def row_of(buffer, start):
        return jnp.concatenate([buffer[start + t] for t in range(4)], axis=1)

    @pl.when(polar)
    def _():
        added = []
        for s, sign in ((0, 0.5 * time_step), (1, -0.5 * time_step)):
            ghost = flip(s, 1.0) * row_of(halo_in, NEAR + 4 * s)
            added.append(sign * (wind(halo_out, s, 1) * ghost + coupling * row_link(ghost)))
            xb[s] = added[s]
        y = to_modes(jnp.concatenate(added, axis=0), table.at[FORWARD:EVALUATE])
        for s in range(2):
            for f in range(FIELDS):
                cb[2 * f + s, 0:LEV, :] = y[(s * FIELDS + f) * LEV : (s * FIELDS + f + 1) * LEV, :]
        ends = []
        for side, sign in ((0, -1.0), (1, 1.0)):
            came = halo_in[SIDES + side]
            along_x = (sign * hm[8:24, :]) * (roll(came, -1, 1) if side == 0 else came)
            mine = jnp.where(
                jnp.logical_and(lane2 >= 2 * PAIRS, lane2 < 2 * (PAIRS + LEV)), halo_out[SIDES + side], 0.0
            )
            ew = sum(roll(mine, 2 * LEV * f - 2 * PAIRS - side, 1) for f in range(FIELDS))
            linked = jnp.where(
                lane2 < 2 * LEV,
                roll(along_x, -4 * LEV, 1),
                jnp.where(
                    jnp.logical_and(lane2 >= 4 * LEV, lane2 < 6 * LEV), roll(along_x, 4 * LEV, 1), 0.0
                ),
            )
            ends.append(time_step * (-ew * along_x - coupling * linked))
        ends = jnp.where(lax.rem(lane2, 2) == 0, ends[0], roll(ends[1], 1, 1))
        for f in range(FIELDS):
            for h in range(2):
                cb[2 * f + h, 8:16, :] = ends[8 * h : 8 * h + 8, :]

        for d in FAR_FIRST:
            c_copy(plus(i, d)).start()

        yc[i] = cb[i]

    @pl.when(polar)
    def _():
        load_cut.wait()
        load_others.wait()
        own_rows(0)

    from_west = roll(halo_in[SIDES], 126, 1)
    from_east = roll(halo_in[SIDES + 1], COLS - 384, 1)
    both = jnp.where(jnp.logical_and(lane2 >= 66, lane2 < 114), from_east, from_west)[None]
    for width in (2, 4, 8):
        both = jnp.concatenate([both, roll_blocks(both, -width)], axis=0)
    both = jnp.concatenate([both, roll_blocks(both, -16), roll_blocks(both, -32)], axis=0)
    in_halo = jnp.logical_or(jnp.logical_and(lane128 >= 66, lane128 < 68), lane128 >= 126)
    grid[:, 8:24, 384:512] = jnp.where(in_halo, both, grid[:, 8:24, 384:512])
    edge_rows((REST, REST + 7), slice(0, PAIRS), (9, 22))
    for s, near in enumerate((8, 23)):
        halo_out[REST + 7 * s + 6] = grid[0:PAIRS, near, 384:512]
    halo_copy(REST, 7, REST + 7 * slot_n, 1, nb, nl).start()
    halo_copy(REST + 7, 7, REST + 7 * slot_s, 1, sb, sl).start()

    @pl.when(polar)
    def _():
        own_rows(1)

    halo_arrival(REST, BLOCKS, 1).wait_recv()
    edge_row = (7, 24)
    edge_probe = []
    for s in range(2):
        edge_probe.append(
            jnp.concatenate([halo_in[NEAR + 4 * s + t] for t in range(3)] + [halo_in[REST + 7 * s + 6]], axis=1)
        )
        grid[0:PAIRS, edge_row[s], :] = flip(s, 1.0) * edge_probe[s]

    @pl.when(polar)
    def _():
        for s, row in ((0, 0), (1, 15)):
            tend[:, row, :] = tend[:, row, :] + xb[s]
        side_tendency()

    @pl.when(jnp.logical_not(polar))
    def _():
        full_tendency()

    def edge_weights(s, a):
        return -wind(halo_in, s, 1) * a - coupling * row_link(a)

    for s, inward in ((0, 1.0), (1, -1.0)):
        mid = edge_probe[s]
        half = jnp.concatenate([hm[edge_row[s] : edge_row[s] + 1, :]] * 4, axis=1)
        along_x = half * (roll(mid, -1, 1) - roll(mid, 1, 1))
        turn = jnp.where(over_pole[s], -0.5 * inward, 0.5 * inward)
        along_y = turn * (flip(s, 1.0) * row_of(halo_out, NEAR + 4 * s) - row_of(halo_in, REST + 7 * s))
        linked = jnp.where(row16 < LEV, roll(along_x, -2 * LEV, 0), row_link(along_y))
        linked = linked + jnp.where(is_temp, roll(along_x, 2 * LEV, 0), 0.0)
        up = jnp.where(lax.rem(row16, LEV) == 0, mid, roll(mid, 1, 0))
        down = jnp.where(lax.rem(row16, LEV) == LEV - 1, mid, roll(mid, -1, 0))
        t = -(wind(halo_in, s, 0) * along_x + wind(halo_in, s, 1) * along_y) - coupling * linked
        a = mid + time_step * (t + mixing * (up + down - 2.0 * mid))
        gy[0:PAIRS, edge_row[s], :] = flip(s, -1.0) * edge_weights(s, a)

    def row_weights(a, nw):
        return (
            -nw * a[0],
            -nw * a[1] - coupling * a[2],
            -nw * a[2] - coupling * a[1],
            -nw * a[3],
        )

    def put_weights(l, h, a):
        for f, weight in enumerate(row_weights(a, grid[PAIRS + LEV + l, h : h + 8, :])):
            gy[f * LEV + l, h : h + 8, :] = weight

    @pl.when(polar)
    def _():
        all_z(0).wait_recv()
        for h in (8, 16):
            taken = project(0, h // 8 - 1)
            for l in range(LEV):
                for f in range(FIELDS):
                    n, rows = f * LEV + l, slice(h - 8, h)
                    adj[n, rows, :] = grid[n, h : h + 8, :] + tend[n, rows, :] - taken[f][l]
        all_z(1).wait_recv()
        for h in (8, 16):
            taken = project(1, h // 8 - 1)
            for l in range(LEV):
                a = []
                for f in range(FIELDS):
                    n, rows = f * LEV + l, slice(h - 8, h)
                    change = tend[n, rows, :] - taken[f][l]
                    tend[n, rows, :] = change
                    tan_out[f, l, rows, :] = (grid[n, h : h + 8, :] + change)[:, :COLS]
                    a.append(adj[n, rows, :] - taken[f][l])
                    adj[n, rows, :] = a[f]
                put_weights(l, h, a)

    @pl.when(jnp.logical_not(polar))
    def _():
        @pl.loop(0, LEV)
        def _(l):
            for h in (8, 16):
                a = []
                for f in range(FIELDS):
                    n, rows = f * LEV + l, slice(h - 8, h)
                    a.append(grid[n, h : h + 8, :] + tend[n, rows, :])
                    tan_out[f, l, rows, :] = a[f][:, :COLS]
                    adj[n, rows, :] = a[f]
                put_weights(l, h, a)

    @pl.loop(0, LEV)
    def _(l):
        lo = jnp.maximum(l - 1, 0)
        hi = jnp.minimum(l + 1, LEV - 1)
        for h in (8, 16):
            rows = slice(h - 8, h)
            half = jnp.concatenate([hm[h : h + 8, :]] * 4, axis=1)
            ew = grid[PAIRS + l, h : h + 8, :]
            a = [adj[f * LEV + l, rows, :] for f in range(FIELDS)]
            col_weights = (
                -ew * a[0] - coupling * a[2],
                -ew * a[1],
                -ew * a[2] - coupling * a[0],
                -ew * a[3],
            )
            for f in range(FIELDS):
                n = f * LEV + l
                back = half * (roll(col_weights[f], 1, 1) - roll(col_weights[f], -1, 1))
                back = back + 0.5 * (gy[n, h - 1 : h + 7, :] - gy[n, h + 1 : h + 9, :])
                back = back + mixing * (adj[f * LEV + lo, rows, :] + adj[f * LEV + hi, rows, :] - 2.0 * a[f])
                diag = grid[n, h : h + 8, :] * (tend[n, rows, :] + time_step * back)
                diag_out[f, l, rows, :] = diag[:, :COLS]

    @pl.when(jnp.logical_and(near_polar, jnp.logical_not(polar)))
    def _():
        load_part.wait()

    for s, wanted in enumerate((above_polar, below_polar)):
        @pl.when(wanted)
        def _():
            remote(bz.at[s], bz.at[s], b_send, b_recv.at[s], nb, nl).wait_recv()

        @pl.when(jnp.logical_not(wanted))
        def _():
            bz[s] = jnp.zeros((FIELDS, LEV, RANK), F32)

    @pl.when(near_polar)
    def _():
        taken = evaluate(jnp.concatenate([bz[s, f] for s in range(2) for f in range(FIELDS)], axis=0))
        for s, wanted in enumerate((above_polar, below_polar)):
            @pl.when(wanted)
            def _():
                row = 15 * s
                weight = flip(s, -1.0) * edge_weights(s, taken[PAIRS * s : PAIRS * (s + 1), :])
                less = ((0.5, -0.5)[s] * time_step) * grid[0:PAIRS, 8 + row, :] * weight
                for f in range(FIELDS):
                    diag_out[f, :, row, :] = diag_out[f, :, row, :] - less[f * LEV : (f + 1) * LEV, :COLS]

    halo_arrival(0, BLOCKS, 0).wait_send()

    @pl.when(polar)
    def _():
        all_c().wait_send()
        for q in range(2):
            all_y(q).wait_send()
            all_z(q).wait_send()

        @pl.when(edge_over)
        def _():
            remote(eb.at[others], eb.at[others], b_send, b_recv.at[0], b, west).wait_send()

        @pl.when(jnp.logical_not(edge_over))
        def _():
            remote(eb, eb, b_send, b_recv.at[0], b, west).wait_send()


def hand_out(tan_in, diag_in, tan_out, diag_out, sem):
    copies = [
        pltpu.make_async_copy(src, dst, sem.at[n])
        for n, (src, dst) in enumerate(((tan_in, tan_out), (diag_in, diag_out)))
    ]
    for copy in copies:
        copy.start()
    for copy in copies:
        copy.wait()


def per_device(bands, row_signs, col_signs, spread, east_wind, north_wind, cutoffs):
    any_spec = pl.BlockSpec(memory_space=pl.ANY)
    out = jax.ShapeDtypeStruct((FIELDS, LEV, ROWS, COLS), F32)
    tables = [jnp.asarray(half_metric(bands)), jnp.asarray(mode_factors())]
    operands = (spread, east_wind, north_wind, row_signs, col_signs, cutoffs, *tables)
    vmem = pltpu.VMEM
    dma = pltpu.SemaphoreType.DMA
    held = pltpu.VMEM(out.shape, F32)
    results = pl.pallas_call(
        functools.partial(kernel, bands),
        out_shape=(held, held),
        in_specs=[any_spec] * 8,
        out_specs=(pl.BlockSpec(memory_space=pltpu.VMEM),) * 2,
        scratch_shapes=[
            vmem((FIELDS, LEV, ROWS, COLS), F32),
            vmem((2, LEV, ROWS, COLS), F32),
            vmem((FIELDS, LEV, ROWS), jnp.int32),
            vmem((FIELDS, LEV, COLS), jnp.int32),
            pltpu.SMEM((ROWS,), jnp.int32),
            vmem((32, 128), F32),
            vmem((TABLE_ROWS, 2 * RANK), BF16),
            vmem((PAIRS + 2 * LEV, 32, WIDE), F32),
            vmem((BLOCKS, 16, 128), F32),
            vmem((BLOCKS, 16, 128), F32),
            vmem((2, LANES, LEV - 1, 8, RANK), F32),
            vmem((2, LANES, LEV - 1, 8, RANK), F32),
            vmem((2, PAIRS, WIDE), F32),
            vmem((LANES, 16, RANK), F32),
            vmem((LANES, 16, RANK), F32),
            vmem((2, LANES, LEV - 1, 8, RANK), F32),
            vmem((2, LANES, LEV - 1, 8, RANK), F32),
            vmem((LANES, LEV, RANK), F32),
            vmem((2, FIELDS, LEV, RANK), F32),
            vmem((PAIRS, ROWS, WIDE), F32),
            vmem((PAIRS, ROWS, WIDE), F32),
            vmem((PAIRS, 32, WIDE), F32),
            dma((8,)),
            dma,
            dma((2,)),
            dma((2,)),
            dma((2,)),
            dma,
            dma,
            dma((2,)),
            dma((2,)),
            dma,
            dma((2,)),
        ],
        compiler_params=pltpu.CompilerParams(
            collective_id=0, has_side_effects=True, vmem_limit_bytes=32 * 2**20
        ),
        cost_estimate=pl.CostEstimate(flops=10**9, bytes_accessed=4 * 10**6, transcendentals=0),
    )(*(pltpu.with_memory_space_constraint(x, pltpu.HBM) for x in operands))
    return pl.pallas_call(
        hand_out,
        out_shape=(out, out),
        in_specs=[any_spec] * 2,
        out_specs=(any_spec, any_spec),
        scratch_shapes=[dma((2,))],
        compiler_params=pltpu.CompilerParams(vmem_limit_bytes=2**20),
    )(*(pltpu.with_memory_space_constraint(x, pltpu.VMEM) for x in results))


def solution(mesh):
    return jax.shard_map(
        functools.partial(per_device, mesh.shape["lat"]),
        mesh=mesh,
        in_specs=(
            P(None, None, "lat"),
            P(None, None, "lon"),
            P(None, None, "lat", "lon"),
            P(None, "lat", "lon"),
            P(None, "lat", "lon"),
            P("lat"),
        ),
        out_specs=(P(None, None, "lat", "lon"), P(None, None, "lat", "lon")),
        check_vma=False,
    )
```

```python
import functools

import jax
import jax.numpy as jnp
import ml_dtypes
import numpy as np
from jax import lax
from jax.experimental import pallas as pl
from jax.experimental.pallas import tpu as pltpu
from jax.sharding import PartitionSpec as P

KTOP = 256
POLAR = 32
RANK = 128
USED = 96
ROWS = 16
COLS = 450
WIDE = 512
LANES = 8
FIELDS = 4
LEV = 4
PAIRS = FIELDS * LEV

time_step = 0.5
coupling = 0.5
mixing = 0.2
metric_cap = 4.0

FORWARD, EVALUATE, TO_COEFS, FROM_COEFS, TABLE_ROWS = 0, 512, 1280, 2304, 3328
NEAR, SIDES, REST, BLOCKS = 0, 8, 10, 24

FAR_FIRST = (6, 2, 5, 3, 7, 1, 4)

MESH = pl.DeviceIdType.MESH
F32 = jnp.float32
BF16 = jnp.bfloat16


def split_table(table):
    high = table.astype(ml_dtypes.bfloat16)
    low = (table - high.astype(np.float64)).astype(ml_dtypes.bfloat16)
    return high, low


def waves_of(group, lane_index):
    place = lane_index % 64
    second = place // 32
    other = (8 - group) if group else 4
    residue = group + second * (other - group)
    return 8 * (place % 32) + residue + (8 * (1 - second) if group == 0 else 0)


@functools.lru_cache(None)
def mode_factors():
    total = COLS * LANES
    size = COLS + 2
    place = np.arange(size, dtype=np.float64)
    width = (KTOP + 0.5) / total
    diag = ((size - 1 - 2 * place) / 2) ** 2 * np.cos(2 * np.pi * width)
    side = place[1:] * (size - place[1:]) / 2
    vectors = np.linalg.eigh(np.diag(diag) + np.diag(side, 1) + np.diag(side, -1))[1]
    basis = np.concatenate([vectors[:, ::-1][:, :USED], np.zeros((size, RANK - USED))], axis=1)
    basis = basis * np.where(basis[size // 2] < 0, -1.0, 1.0)
    weights = []
    for group in range(4):
        waves = waves_of(group, np.arange(64))
        angle = 2 * np.pi / total * ((np.arange(size)[:, None] - 1) * waves[None, :] % total)
        alpha, beta = basis.T @ np.cos(angle), basis.T @ np.sin(angle)
        if group:
            sign = np.where(np.arange(64) < 32, 1.0, -1.0)
            top, low = (alpha, beta), (sign * beta, -sign * alpha)
        else:
            use = np.where(np.arange(64) < 32, 1.0, 0.0)
            top, low = (use * alpha, use * beta), ((1 - use) * alpha, (1 - use) * beta)
        weights.append(np.concatenate([np.concatenate(top, axis=1), np.concatenate(low, axis=1)], axis=0))
    weights = np.round(np.stack(weights) * 2.0**22) / 2.0**22
    wide = np.zeros((RANK, WIDE))
    wide[:, : COLS + 1] = basis[1:].T
    wide[:, WIDE - 1] = basis[0]
    wide = np.round(wide * 2.0**26) / 2.0**26
    wide_h, wide_l = split_table(wide)
    own = np.where(np.arange(WIDE)[:, None] < COLS, 1, 0).astype(ml_dtypes.bfloat16)
    high, low = split_table(weights)
    back = np.concatenate([np.swapaxes(part, 1, 2) for part in (high, low)], axis=1)
    evaluate = np.concatenate([wide_h, wide_l, wide_h], axis=0)
    return np.concatenate(
        [
            np.concatenate([wide_h.T * own, wide_l.T * own], axis=1),
            evaluate[:, : WIDE // 2],
            evaluate[:, WIDE // 2 :],
            np.concatenate([high, low], axis=2).reshape(-1, 2 * RANK),
            back.reshape(-1, 2 * RANK),
        ],
        axis=0,
    )


ROOT = float(np.sqrt(0.5))


def over_lanes(y):
    s = [y[j] + y[j + 4] for j in range(4)]
    d = [y[j] - y[j + 4] for j in range(4)]
    even, odd = s[0] + s[2], s[1] + s[3]
    minus, plus = ROOT * (d[1] - d[3]), ROOT * (d[1] + d[3])
    return [
        (even + odd, even - odd),
        (d[0] + minus, -(d[2] + plus)),
        (s[0] - s[2], s[3] - s[1]),
        (d[0] - minus, d[2] - plus),
    ]


def to_lanes(pairs):
    (y0, y4), (u1, v1), (u2, v2), (u3, v3) = pairs
    even, odd = y0 + y4, y0 - y4
    s = [even + u2, odd - v2, even - u2, odd + v2]
    du, sv = ROOT * (u1 - u3), ROOT * (v1 + v3)
    d = [u1 + u3, du - sv, v3 - v1, -du - sv]
    return [s[j] + d[j] for j in range(4)] + [s[j] - d[j] for j in range(4)]


@functools.lru_cache(None)
def half_metric(bands):
    total = bands * ROWS
    rows = np.clip(np.arange(bands)[:, None] * ROWS - 8 + np.arange(32)[None, :], 0, total - 1)
    metric = np.minimum(1.0 / np.cos(np.pi * ((rows + 0.5) / total - 0.5)), metric_cap)
    table = np.broadcast_to((0.5 * metric).astype(np.float32)[:, :, None], (bands, 32, 128)).copy()
    forward = mode_factors()[FORWARD : FORWARD + WIDE].astype(np.float32)
    for row, col in enumerate((0, COLS - 1)):
        table[:, row] = forward[col, :RANK] + forward[col, RANK:]
    return table


def dot_cols(a, b):
    return lax.dot_general(a, b, (((1,), (0,)), ((), ())), preferred_element_type=F32)


def split(x):
    high = x.astype(BF16)
    return high, (x - high.astype(F32)).astype(BF16)


def to_modes(x, table):
    xh, xl = split(x)
    half = table.shape[1] // 2
    wide = dot_cols(xh, table[...])
    return wide[:, :half] + wide[:, half:] + dot_cols(xl, table[:, 0:half])


def from_modes(z, *tables):
    zh, zl = split(z)
    three = jnp.concatenate([zh, zh, zl], axis=1)
    return jnp.concatenate([dot_cols(three, table[...]) for table in tables], axis=1)


def to_coefs(x, table):
    rows = x.shape[0]
    wide = dot_cols(jnp.concatenate(split(x), axis=0), table[...])
    half = wide.shape[1] // 2
    return wide[:rows, :half] + wide[:rows, half:] + wide[rows:, :half]


def from_coefs(z, table):
    zh, zl = split(z)
    rows = jnp.concatenate([jnp.concatenate([zh, zh], axis=1), jnp.concatenate([zl, jnp.zeros_like(zl)], axis=1)], axis=0)
    wide = dot_cols(rows, table[...])
    return wide[: z.shape[0]] + wide[z.shape[0] :]


def pack(levels):
    lane = lax.broadcasted_iota(jnp.int32, (1, RANK), 1)
    return [jnp.where(lane < USED, levels[l], roll(levels[3], 96 - 32 * l, 1)) for l in range(3)]


def unpack(parts):
    lane = lax.broadcasted_iota(jnp.int32, (1, RANK), 1)
    last = jnp.where(lane < 64, roll(parts[1], 64, 1), roll(parts[2], 96, 1))
    return parts + [jnp.where(lane < 32, roll(parts[0], 32, 1), last)]


def roll(x, shift, axis):
    return pltpu.roll(x, shift % x.shape[axis], axis)


def roll_blocks(x, shift):
    return roll(x.reshape(x.shape[0] * x.shape[1], x.shape[2]), shift, 1).reshape(x.shape)


def fold(x):
    while x.shape[0] > 1:
        half = x.shape[0] // 2
        x = x[:half] + roll_blocks(x[half:], 2 * half)
    return x


def kernel(
    bands, spread, east, north, rs, cs, cut, metric, table_in, tan_out, diag_out,
    spread_v, winds_v, rs_v, cs_v, cut_s, hm, table,
    grid, halo_out, halo_in, ybuf, yr, xb, cb, yc, zbuf, zr, eb, bz,
    tend, adj, gy,
    in_sem, halo_send, halo_recv, y_send, y_recv, c_send, c_recv, z_send, z_recv, b_send, b_recv,
):
    b = lax.axis_index("lat")
    i = lax.axis_index("lon")
    caps = POLAR // ROWS
    is_north = b == 0
    is_south = b == bands - 1
    polar = jnp.logical_or(b < caps, b >= bands - caps)
    above_polar = jnp.logical_or(b <= caps, is_south)
    below_polar = jnp.logical_or(b >= bands - caps - 1, is_north)
    near_polar = jnp.logical_or(above_polar, below_polar)
    across = lax.rem(i + LANES // 2, LANES)
    west = lax.rem(i + LANES - 1, LANES)
    east_lane = lax.rem(i + 1, LANES)
    nb = jnp.where(is_north, 0, b - 1)
    nl = jnp.where(is_north, across, i)
    sb = jnp.where(is_south, bands - 1, b + 1)
    sl = jnp.where(is_south, across, i)
    slot_n = jnp.where(is_north, 0, 1)
    slot_s = jnp.where(is_south, 1, 0)
    own_half = lax.rem(i, 2)
    edge_over = jnp.where(own_half == 0, is_north, is_south)
    over_pole = (is_north, is_south)
    outward = jnp.logical_or(
        jnp.logical_and(b == caps - 1, own_half == 1), jnp.logical_and(b == bands - caps, own_half == 0)
    )

    def plus(lane, d):
        return lax.rem(lane + d, LANES)

    load_spread = pltpu.make_async_copy(spread, spread_v, in_sem.at[0])
    load_rows = pltpu.make_async_copy(rs, rs_v, in_sem.at[1])
    load_cols = pltpu.make_async_copy(cs, cs_v, in_sem.at[2])
    load_metric = pltpu.make_async_copy(metric.at[b], hm, in_sem.at[4])
    load_cut = pltpu.make_async_copy(cut, cut_s, in_sem.at[5])

    def load_table(start, stop, sem):
        return pltpu.make_async_copy(table_in.at[start:stop], table.at[start:stop], in_sem.at[sem])

    load_forward = load_table(FORWARD, EVALUATE, 6)
    load_others = load_table(EVALUATE, TABLE_ROWS, 7)
    load_part = load_table(EVALUATE, TO_COEFS, 7)
    barrier = pltpu.get_barrier_semaphore()

    def greet(lat, lon):
        pl.semaphore_signal(barrier, inc=1, device_id=(lat, lon), device_id_type=MESH)

    @pl.when(polar)
    def _():
        for d in FAR_FIRST[:4]:
            greet(b, plus(i, d))

    greet(nb, nl)
    greet(sb, sl)
    greet(b, west)
    greet(b, east_lane)
    load_spread.start()
    load_rows.start()
    load_cols.start()
    pltpu.make_async_copy(east, winds_v.at[0], in_sem.at[3]).start()
    pltpu.make_async_copy(north, winds_v.at[1], in_sem.at[3]).start()
    load_metric.start()

    @pl.when(polar)
    def _():
        greet(b, across)
        load_forward.start()
        load_cut.start()

    @pl.when(jnp.logical_and(near_polar, jnp.logical_not(polar)))
    def _():
        load_part.start()

    load_rows.wait()
    load_cols.wait()
    load_spread.wait()
    grid[:, 8:24, 384:512] = jnp.zeros((PAIRS + 2 * LEV, ROWS, 128), F32)
    row_part = jnp.concatenate([rs_v[f] for f in range(FIELDS)], axis=0)
    row_part = (2 * row_part - 1).astype(F32).T
    for f in range(FIELDS):
        col_part = (2 * cs_v[f] - 1).astype(F32)
        for l in range(LEV):
            n = f * LEV + l
            grid[n, 8:24, 0:COLS] = spread_v[f, l] * (row_part[:, n : n + 1] * col_part[l : l + 1, :])

    @pl.when(polar)
    def _():
        load_others.start()

    pltpu.make_async_copy(winds_v, winds_v, in_sem.at[3]).wait()
    for w in range(2):
        for l in range(LEV):
            grid[PAIRS + w * LEV + l, 8:24, 0:COLS] = winds_v[w, l]

    def edge_rows(start, entries, rows):
        for s, row in enumerate(rows):
            for t in range(4):
                values = grid[entries, row, 128 * t : 128 * t + 128]
                if entries == slice(0, PAIRS):
                    halo_out[start[s] + t] = values
                else:
                    halo_out[start[s] + t // 2, 8 * (t % 2) : 8 * (t % 2) + 8, :] = values

    edge_rows((NEAR, NEAR + 4), slice(0, PAIRS), (8, 23))
    lane128 = lax.broadcasted_iota(jnp.int32, (1, 1, 128), 2)
    for s, (start, shift) in enumerate(((0, 0), (384, COLS - 2 - 384))):
        tile = grid[:, 8:24, start : start + 128]
        tile = jnp.where(jnp.logical_and(lane128 >= shift, lane128 < shift + 2), tile, 0.0)
        packed = fold(tile[:PAIRS]) + roll_blocks(fold(tile[PAIRS:]), 2 * PAIRS)
        halo_out[SIDES + s] = roll_blocks(packed, -shift)[0]

    pl.semaphore_wait(barrier, 4 + jnp.where(polar, LANES - 3, 0))

    def remote(src, dst, send, recv, lat, lon):
        return pltpu.make_async_remote_copy(
            src_ref=src, dst_ref=dst, send_sem=send, recv_sem=recv, device_id=(lat, lon), device_id_type=MESH
        )

    def halo_copy(start, count, to, which, lat, lon):
        return remote(
            halo_out.at[start : start + count], halo_in.at[pl.ds(to, count)], halo_send, halo_recv.at[which], lat, lon
        )

    def halo_arrival(start, stop, which):
        return remote(
            halo_out.at[start:stop], halo_in.at[start:stop], halo_send, halo_recv.at[which], b, west
        )

    halo_copy(NEAR, 4, NEAR + 4 * slot_n, 0, nb, nl).start()
    halo_copy(NEAR + 4, 4, NEAR + 4 * slot_s, 0, sb, sl).start()
    halo_copy(SIDES, 1, SIDES + 1, 0, b, west).start()
    halo_copy(SIDES + 1, 1, SIDES, 0, b, east_lane).start()

    others = pl.ds(0, LANES - 1)

    def all_y(q):
        return remote(ybuf.at[q, others], yr.at[q, others], y_send.at[q], y_recv.at[q], b, west)

    def send_values(q, x):
        y = to_modes(x.reshape(PAIRS * ROWS, WIDE), table.at[FORWARD:EVALUATE])
        y = y.reshape(FIELDS, LEV, 2, 8, RANK)
        blocks = [
            jnp.concatenate([y[f, l, h] for f in range(FIELDS) for h in range(2)], axis=0) for l in range(LEV)
        ]
        for l, part in enumerate(pack(blocks)):
            ybuf[q, :, l] = part.reshape(LANES, 8, RANK)

        for d in FAR_FIRST:
            o = plus(i, d)
            remote(ybuf.at[q, o], yr.at[q, i], y_send.at[q], y_recv.at[q], b, o).start()

        yr[q, i] = ybuf[q, i]

    def c_copy(o):
        return remote(cb.at[o], yc.at[i], c_send, c_recv, b, o)

    def all_c():
        return remote(cb.at[others], yc.at[others], c_send, c_recv, b, west)

    def z_copy(q, j):
        return remote(zbuf.at[q, j], zr.at[q, i], z_send.at[q], z_recv.at[q], b, j)

    def all_z(q):
        return remote(zbuf.at[q, others], zr.at[q, others], z_send.at[q], z_recv.at[q], b, west)

    def edge_sends():
        slot = jnp.where(own_half == 0, slot_n, slot_s)
        lat = jnp.where(own_half == 0, nb, sb)

        @pl.loop(0, LANES)
        def _(d):
            j = plus(i, d)
            lon = jnp.where(edge_over, plus(j, LANES // 2), j)
            here = jnp.logical_and(edge_over, lon == i)

            @pl.when(jnp.logical_not(here))
            def _():
                remote(eb.at[j], bz.at[slot, i // 2], b_send, b_recv.at[slot], lat, lon).start()

            @pl.when(here)
            def _():
                pltpu.make_async_copy(eb.at[j], bz.at[slot, i // 2], b_recv.at[slot]).start()

    def own_rows(q):
        row = lax.broadcasted_iota(jnp.int32, (8, 128), 0)
        cutoff = jnp.zeros((8, 128), jnp.int32)
        for r in range(8):
            cutoff = jnp.where(row == r, cut_s[8 * own_half + r], cutoff)
        keeps = []
        for group in range(4):
            wave = waves_of(group, lax.broadcasted_iota(jnp.int32, (8, 128), 1))
            keep = jnp.where(wave > cutoff, 2.0 / (COLS * LANES), 0.0)
            keeps.append(jnp.concatenate([keep] * LEV, axis=0))
        all_y(q).wait_recv()
        levels = unpack([yr[q, :, l].reshape(LANES * 8, RANK) for l in range(LEV - 1)])
        if q == 1:
            edge_row = jnp.where(row == 7 * own_half, 1.0, 0.0)
            all_c().wait_recv()
            ends = jnp.concatenate([yc[j, 8:16, :] for j in range(LANES)], axis=0)
            ends = pltpu.roll(ends, lax.rem(128 - 2 * LEV * (i // 2), 128), 1)
            levels = [
                levels[l]
                + ends[:, 2 * l : 2 * l + 1] * hm[0:1, :]
                + ends[:, 2 * l + 1 : 2 * l + 2] * hm[1:2, :]
                + jnp.concatenate([edge_row * yc[j, l : l + 1, :] for j in range(LANES)], axis=0)
                for l in range(LEV)
            ]
        lanes = [
            jnp.concatenate([levels[l][8 * j : 8 * j + 8, :] for l in range(LEV)], axis=0) for j in range(LANES)
        ]
        coefs = [
            to_coefs(jnp.concatenate(pair, axis=1), table.at[TO_COEFS + 256 * group : TO_COEFS + 256 * (group + 1)])
            for group, pair in enumerate(over_lanes(lanes))
        ]
        kept = [coef * keep for coef, keep in zip(coefs, keeps)]
        backs = [
            from_coefs(coef, table.at[FROM_COEFS + 256 * group : FROM_COEFS + 256 * (group + 1)])
            for group, coef in enumerate(kept)
        ]
        pairs = [(back[:, :RANK], back[:, RANK:]) for back in backs]
        zs = [z.reshape(LEV, 8, RANK) for z in to_lanes(pairs)]
        for l, part in enumerate(pack([jnp.concatenate([z[l] for z in zs], axis=0) for l in range(LEV)])):
            zbuf[q, :, l] = part.reshape(LANES, 8, RANK)

        def edges():
            for j, z in enumerate(zs):
                edge = jnp.where(own_half == 0, z[:, 0, :], z[:, 7, :])
                eb[j] = edge if q == 0 else eb[j] + edge
            if q == 1:
                edge_sends()

        if q == 1:
            pl.when(outward)(edges)
        for d in FAR_FIRST:
            z_copy(q, plus(i, d)).start()
        if q == 1:
            pl.when(jnp.logical_not(outward))(edges)
        else:
            edges()
        zr[q, i] = zbuf[q, i]

    def evaluate(z):
        return from_modes(z, table.at[EVALUATE : EVALUATE + 384], table.at[EVALUATE + 384 : TO_COEFS])

    def project(q, h):
        levels = unpack(
            [jnp.concatenate([zr[q, 2 * f + h, l] for f in range(FIELDS)], axis=0) for l in range(LEV - 1)]
        )
        z = jnp.concatenate(
            [levels[l][8 * f : 8 * f + 8, :] for f in range(FIELDS) for l in range(LEV)], axis=0
        )
        out = evaluate(z)
        return [[out[8 * (LEV * f + l) : 8 * (LEV * f + l + 1), :] for l in range(LEV)] for f in range(FIELDS)]

    def tendency_rows(h, l, at, half):
        lo = jnp.maximum(l - 1, 0)
        hi = jnp.minimum(l + 1, LEV - 1)
        ew = at(PAIRS + l, h)
        nw = at(PAIRS + LEV + l, h)
        mids, along_x, along_y = [], [], []
        for f in range(FIELDS):
            mid = at(f * LEV + l, h)
            mids.append(mid)
            along_x.append(half * (roll(mid, -1, 1) - roll(mid, 1, 1)))
            along_y.append(0.5 * (at(f * LEV + l, h + 1) - at(f * LEV + l, h - 1)))
        linked = (along_x[2], along_y[2], along_x[0] + along_y[1], None)
        out = []
        for f in range(FIELDS):
            mixed = at(f * LEV + lo, h) + at(f * LEV + hi, h) - 2.0 * mids[f]
            t = -(ew * along_x[f] + nw * along_y[f]) + mixing * mixed
            if linked[f] is not None:
                t = t - coupling * linked[f]
            out.append(time_step * t)
        return out

    def full_tendency():
        @pl.loop(0, LEV)
        def _(l):
            for h in (8, 16):
                half = jnp.concatenate([hm[h : h + 8, :]] * 4, axis=1)
                for f, t in enumerate(tendency_rows(h, l, lambda n, r: grid[n, r : r + 8, :], half)):
                    tend[f * LEV + l, h - 8 : h, :] = t

    def side_tendency():
        lane = lax.broadcasted_iota(jnp.int32, (1, 128), 1)
        late = jnp.logical_or(jnp.logical_or(lane == 65, lane == 66), lane == 127)

        def at(n, r):
            return jnp.where(lane < 2, grid[n, r : r + 8, 0:128], grid[n, r : r + 8, 384:512])

        @pl.loop(0, LEV)
        def _(l):
            for h in (8, 16):
                for f, t in enumerate(tendency_rows(h, l, at, hm[h : h + 8, :])):
                    n, rows = f * LEV + l, slice(h - 8, h)
                    tend[n, rows, 0:128] = jnp.where(lane == 0, t, tend[n, rows, 0:128])
                    tend[n, rows, 384:512] = jnp.where(late, t, tend[n, rows, 384:512])

    load_metric.wait()

    @pl.when(polar)
    def _():
        load_forward.wait()
        send_values(0, grid[0:PAIRS, 8:24, :])
        grid[0:PAIRS, 7:8, :] = jnp.zeros((PAIRS, 1, WIDE), F32)
        grid[0:PAIRS, 24:25, :] = jnp.zeros((PAIRS, 1, WIDE), F32)
        full_tendency()
        send_values(1, tend[...])

    edge_rows((REST + 4, REST + 11), slice(PAIRS, PAIRS + 2 * LEV), (8, 23))

    halo_arrival(NEAR, REST, 0).wait_recv()
    lane2 = lax.broadcasted_iota(jnp.int32, (1, 128), 1)
    row16 = lax.broadcasted_iota(jnp.int32, (PAIRS, 1), 0)
    is_v = jnp.logical_and(row16 >= LEV, row16 < 2 * LEV)
    is_temp = jnp.logical_and(row16 >= 2 * LEV, row16 < 3 * LEV)

    def flip(s, minus):
        sign = jnp.where(row16 < 2 * LEV, -1.0, 1.0) * minus
        return jnp.where(over_pole[s], sign, 1.0)

    def row_link(x):
        return jnp.where(is_v, roll(x, -LEV, 0), jnp.where(is_temp, roll(x, LEV, 0), 0.0))

    def wind(buffer, s, w):
        base = REST + 7 * s + 4
        rows = [buffer[base + t // 2, 8 * (t % 2) + LEV * w : 8 * (t % 2) + LEV * (w + 1), :] for t in range(4)]
        return jnp.concatenate([jnp.concatenate(rows, axis=1)] * FIELDS, axis=0)

    def row_of(buffer, start):
        return jnp.concatenate([buffer[start + t] for t in range(4)], axis=1)

    @pl.when(polar)
    def _():
        added = []
        for s, sign in ((0, 0.5 * time_step), (1, -0.5 * time_step)):
            ghost = flip(s, 1.0) * row_of(halo_in, NEAR + 4 * s)
            added.append(sign * (wind(halo_out, s, 1) * ghost + coupling * row_link(ghost)))
            xb[s] = added[s]
        y = to_modes(jnp.concatenate(added, axis=0), table.at[FORWARD:EVALUATE])
        for s in range(2):
            for f in range(FIELDS):
                cb[2 * f + s, 0:LEV, :] = y[(s * FIELDS + f) * LEV : (s * FIELDS + f + 1) * LEV, :]
        ends = []
        for side, sign in ((0, -1.0), (1, 1.0)):
            came = halo_in[SIDES + side]
            along_x = (sign * hm[8:24, :]) * (roll(came, -1, 1) if side == 0 else came)
            mine = jnp.where(
                jnp.logical_and(lane2 >= 2 * PAIRS, lane2 < 2 * (PAIRS + LEV)), halo_out[SIDES + side], 0.0
            )
            ew = sum(roll(mine, 2 * LEV * f - 2 * PAIRS - side, 1) for f in range(FIELDS))
            linked = jnp.where(
                lane2 < 2 * LEV,
                roll(along_x, -4 * LEV, 1),
                jnp.where(
                    jnp.logical_and(lane2 >= 4 * LEV, lane2 < 6 * LEV), roll(along_x, 4 * LEV, 1), 0.0
                ),
            )
            ends.append(time_step * (-ew * along_x - coupling * linked))
        ends = jnp.where(lax.rem(lane2, 2) == 0, ends[0], roll(ends[1], 1, 1))
        for f in range(FIELDS):
            for h in range(2):
                cb[2 * f + h, 8:16, :] = ends[8 * h : 8 * h + 8, :]

        for d in FAR_FIRST:
            c_copy(plus(i, d)).start()

        yc[i] = cb[i]

    from_west = roll(halo_in[SIDES], 126, 1)
    from_east = roll(halo_in[SIDES + 1], COLS - 384, 1)
    both = jnp.where(jnp.logical_and(lane2 >= 66, lane2 < 114), from_east, from_west)[None]
    for width in (2, 4, 8):
        both = jnp.concatenate([both, roll_blocks(both, -width)], axis=0)
    both = jnp.concatenate([both, roll_blocks(both, -16), roll_blocks(both, -32)], axis=0)
    in_halo = jnp.logical_or(jnp.logical_and(lane128 >= 66, lane128 < 68), lane128 >= 126)
    grid[:, 8:24, 384:512] = jnp.where(in_halo, both, grid[:, 8:24, 384:512])
    edge_rows((REST, REST + 7), slice(0, PAIRS), (9, 22))
    for s, near in enumerate((8, 23)):
        halo_out[REST + 7 * s + 6] = grid[0:PAIRS, near, 384:512]
    halo_copy(REST, 7, REST + 7 * slot_n, 1, nb, nl).start()
    halo_copy(REST + 7, 7, REST + 7 * slot_s, 1, sb, sl).start()

    @pl.when(polar)
    def _():
        load_cut.wait()
        load_others.wait()
        own_rows(0)

    halo_arrival(REST, BLOCKS, 1).wait_recv()
    edge_row = (7, 24)
    edge_probe = []
    for s in range(2):
        edge_probe.append(
            jnp.concatenate([halo_in[NEAR + 4 * s + t] for t in range(3)] + [halo_in[REST + 7 * s + 6]], axis=1)
        )
        grid[0:PAIRS, edge_row[s], :] = flip(s, 1.0) * edge_probe[s]

    @pl.when(polar)
    def _():
        for s, row in ((0, 0), (1, 15)):
            tend[:, row, :] = tend[:, row, :] + xb[s]
        side_tendency()

    @pl.when(jnp.logical_not(polar))
    def _():
        full_tendency()

    def edge_weights(s, a):
        return -wind(halo_in, s, 1) * a - coupling * row_link(a)

    for s, inward in ((0, 1.0), (1, -1.0)):
        mid = edge_probe[s]
        half = jnp.concatenate([hm[edge_row[s] : edge_row[s] + 1, :]] * 4, axis=1)
        along_x = half * (roll(mid, -1, 1) - roll(mid, 1, 1))
        turn = jnp.where(over_pole[s], -0.5 * inward, 0.5 * inward)
        along_y = turn * (flip(s, 1.0) * row_of(halo_out, NEAR + 4 * s) - row_of(halo_in, REST + 7 * s))
        linked = jnp.where(row16 < LEV, roll(along_x, -2 * LEV, 0), row_link(along_y))
        linked = linked + jnp.where(is_temp, roll(along_x, 2 * LEV, 0), 0.0)
        up = jnp.where(lax.rem(row16, LEV) == 0, mid, roll(mid, 1, 0))
        down = jnp.where(lax.rem(row16, LEV) == LEV - 1, mid, roll(mid, -1, 0))
        t = -(wind(halo_in, s, 0) * along_x + wind(halo_in, s, 1) * along_y) - coupling * linked
        a = mid + time_step * (t + mixing * (up + down - 2.0 * mid))
        gy[0:PAIRS, edge_row[s], :] = flip(s, -1.0) * edge_weights(s, a)

    @pl.when(polar)
    def _():
        own_rows(1)

    def row_weights(a, nw):
        return (
            -nw * a[0],
            -nw * a[1] - coupling * a[2],
            -nw * a[2] - coupling * a[1],
            -nw * a[3],
        )

    def put_weights(l, h, a):
        for f, weight in enumerate(row_weights(a, grid[PAIRS + LEV + l, h : h + 8, :])):
            gy[f * LEV + l, h : h + 8, :] = weight

    @pl.when(polar)
    def _():
        all_z(0).wait_recv()
        for h in (8, 16):
            taken = project(0, h // 8 - 1)
            for l in range(LEV):
                for f in range(FIELDS):
                    n, rows = f * LEV + l, slice(h - 8, h)
                    adj[n, rows, :] = grid[n, h : h + 8, :] + tend[n, rows, :] - taken[f][l]
        all_z(1).wait_recv()
        for h in (8, 16):
            taken = project(1, h // 8 - 1)
            for l in range(LEV):
                a = []
                for f in range(FIELDS):
                    n, rows = f * LEV + l, slice(h - 8, h)
                    change = tend[n, rows, :] - taken[f][l]
                    tend[n, rows, :] = change
                    tan_out[f, l, rows, :] = (grid[n, h : h + 8, :] + change)[:, :COLS]
                    a.append(adj[n, rows, :] - taken[f][l])
                    adj[n, rows, :] = a[f]
                put_weights(l, h, a)

    @pl.when(jnp.logical_not(polar))
    def _():
        @pl.loop(0, LEV)
        def _(l):
            for h in (8, 16):
                a = []
                for f in range(FIELDS):
                    n, rows = f * LEV + l, slice(h - 8, h)
                    a.append(grid[n, h : h + 8, :] + tend[n, rows, :])
                    tan_out[f, l, rows, :] = a[f][:, :COLS]
                    adj[n, rows, :] = a[f]
                put_weights(l, h, a)

    @pl.loop(0, LEV)
    def _(l):
        lo = jnp.maximum(l - 1, 0)
        hi = jnp.minimum(l + 1, LEV - 1)
        for h in (8, 16):
            rows = slice(h - 8, h)
            half = jnp.concatenate([hm[h : h + 8, :]] * 4, axis=1)
            ew = grid[PAIRS + l, h : h + 8, :]
            a = [adj[f * LEV + l, rows, :] for f in range(FIELDS)]
            col_weights = (
                -ew * a[0] - coupling * a[2],
                -ew * a[1],
                -ew * a[2] - coupling * a[0],
                -ew * a[3],
            )
            for f in range(FIELDS):
                n = f * LEV + l
                back = half * (roll(col_weights[f], 1, 1) - roll(col_weights[f], -1, 1))
                back = back + 0.5 * (gy[n, h - 1 : h + 7, :] - gy[n, h + 1 : h + 9, :])
                back = back + mixing * (adj[f * LEV + lo, rows, :] + adj[f * LEV + hi, rows, :] - 2.0 * a[f])
                diag = grid[n, h : h + 8, :] * (tend[n, rows, :] + time_step * back)
                diag_out[f, l, rows, :] = diag[:, :COLS]

    @pl.when(jnp.logical_and(near_polar, jnp.logical_not(polar)))
    def _():
        load_part.wait()

    for s, wanted in enumerate((above_polar, below_polar)):
        @pl.when(wanted)
        def _():
            remote(bz.at[s], bz.at[s], b_send, b_recv.at[s], nb, nl).wait_recv()

        @pl.when(jnp.logical_not(wanted))
        def _():
            bz[s] = jnp.zeros((FIELDS, LEV, RANK), F32)

    @pl.when(near_polar)
    def _():
        taken = evaluate(jnp.concatenate([bz[s, f] for s in range(2) for f in range(FIELDS)], axis=0))
        for s, wanted in enumerate((above_polar, below_polar)):
            @pl.when(wanted)
            def _():
                row = 15 * s
                weight = flip(s, -1.0) * edge_weights(s, taken[PAIRS * s : PAIRS * (s + 1), :])
                less = ((0.5, -0.5)[s] * time_step) * grid[0:PAIRS, 8 + row, :] * weight
                for f in range(FIELDS):
                    diag_out[f, :, row, :] = diag_out[f, :, row, :] - less[f * LEV : (f + 1) * LEV, :COLS]

    halo_arrival(0, BLOCKS, 0).wait_send()

    @pl.when(polar)
    def _():
        all_c().wait_send()
        for q in range(2):
            all_y(q).wait_send()
            all_z(q).wait_send()

        @pl.when(edge_over)
        def _():
            remote(eb.at[others], eb.at[others], b_send, b_recv.at[0], b, west).wait_send()

        @pl.when(jnp.logical_not(edge_over))
        def _():
            remote(eb, eb, b_send, b_recv.at[0], b, west).wait_send()


def hand_out(tan_in, diag_in, tan_out, diag_out, sem):
    copies = [
        pltpu.make_async_copy(src, dst, sem.at[n])
        for n, (src, dst) in enumerate(((tan_in, tan_out), (diag_in, diag_out)))
    ]
    for copy in copies:
        copy.start()
    for copy in copies:
        copy.wait()


def per_device(bands, row_signs, col_signs, spread, east_wind, north_wind, cutoffs):
    any_spec = pl.BlockSpec(memory_space=pl.ANY)
    out = jax.ShapeDtypeStruct((FIELDS, LEV, ROWS, COLS), F32)
    tables = [jnp.asarray(half_metric(bands)), jnp.asarray(mode_factors())]
    operands = (spread, east_wind, north_wind, row_signs, col_signs, cutoffs, *tables)
    vmem = pltpu.VMEM
    dma = pltpu.SemaphoreType.DMA
    held = pltpu.VMEM(out.shape, F32)
    results = pl.pallas_call(
        functools.partial(kernel, bands),
        out_shape=(held, held),
        in_specs=[any_spec] * 8,
        out_specs=(pl.BlockSpec(memory_space=pltpu.VMEM),) * 2,
        scratch_shapes=[
            vmem((FIELDS, LEV, ROWS, COLS), F32),
            vmem((2, LEV, ROWS, COLS), F32),
            vmem((FIELDS, LEV, ROWS), jnp.int32),
            vmem((FIELDS, LEV, COLS), jnp.int32),
            pltpu.SMEM((ROWS,), jnp.int32),
            vmem((32, 128), F32),
            vmem((TABLE_ROWS, 2 * RANK), BF16),
            vmem((PAIRS + 2 * LEV, 32, WIDE), F32),
            vmem((BLOCKS, 16, 128), F32),
            vmem((BLOCKS, 16, 128), F32),
            vmem((2, LANES, LEV - 1, 8, RANK), F32),
            vmem((2, LANES, LEV - 1, 8, RANK), F32),
            vmem((2, PAIRS, WIDE), F32),
            vmem((LANES, 16, RANK), F32),
            vmem((LANES, 16, RANK), F32),
            vmem((2, LANES, LEV - 1, 8, RANK), F32),
            vmem((2, LANES, LEV - 1, 8, RANK), F32),
            vmem((LANES, LEV, RANK), F32),
            vmem((2, FIELDS, LEV, RANK), F32),
            vmem((PAIRS, ROWS, WIDE), F32),
            vmem((PAIRS, ROWS, WIDE), F32),
            vmem((PAIRS, 32, WIDE), F32),
            dma((8,)),
            dma,
            dma((2,)),
            dma((2,)),
            dma((2,)),
            dma,
            dma,
            dma((2,)),
            dma((2,)),
            dma,
            dma((2,)),
        ],
        compiler_params=pltpu.CompilerParams(
            collective_id=0, has_side_effects=True, vmem_limit_bytes=32 * 2**20
        ),
        cost_estimate=pl.CostEstimate(flops=10**9, bytes_accessed=4 * 10**6, transcendentals=0),
    )(*(pltpu.with_memory_space_constraint(x, pltpu.HBM) for x in operands))
    return pl.pallas_call(
        hand_out,
        out_shape=(out, out),
        in_specs=[any_spec] * 2,
        out_specs=(any_spec, any_spec),
        scratch_shapes=[dma((2,))],
        compiler_params=pltpu.CompilerParams(vmem_limit_bytes=2**20),
    )(*(pltpu.with_memory_space_constraint(x, pltpu.VMEM) for x in results))


def solution(mesh):
    return jax.shard_map(
        functools.partial(per_device, mesh.shape["lat"]),
        mesh=mesh,
        in_specs=(
            P(None, None, "lat"),
            P(None, None, "lon"),
            P(None, None, "lat", "lon"),
            P(None, "lat", "lon"),
            P(None, "lat", "lon"),
            P("lat"),
        ),
        out_specs=(P(None, None, "lat", "lon"), P(None, None, "lat", "lon")),
        check_vma=False,
    )
```

```python
import functools

import jax
import jax.numpy as jnp
import ml_dtypes
import numpy as np
from jax import lax
from jax.experimental import pallas as pl
from jax.experimental.pallas import tpu as pltpu
from jax.sharding import PartitionSpec as P

KTOP = 256
POLAR = 32
RANK = 128
USED = 96
ROWS = 16
COLS = 450
WIDE = 512
LANES = 8
FIELDS = 4
LEV = 4
PAIRS = FIELDS * LEV

time_step = 0.5
coupling = 0.5
mixing = 0.2
metric_cap = 4.0

FORWARD, EVALUATE, TO_COEFS, FROM_COEFS, TABLE_ROWS = 0, 512, 1280, 2304, 3328
NEAR, SIDES, REST, BLOCKS = 0, 8, 10, 24

FAR_FIRST = (6, 2, 5, 3, 7, 1, 4)

MESH = pl.DeviceIdType.MESH
F32 = jnp.float32
BF16 = jnp.bfloat16


def split_table(table):
    high = table.astype(ml_dtypes.bfloat16)
    low = (table - high.astype(np.float64)).astype(ml_dtypes.bfloat16)
    return high, low


def waves_of(group, lane_index):
    place = lane_index % 64
    second = place // 32
    other = (8 - group) if group else 4
    residue = group + second * (other - group)
    return 8 * (place % 32) + residue + (8 * (1 - second) if group == 0 else 0)


@functools.lru_cache(None)
def mode_factors():
    total = COLS * LANES
    size = COLS + 2
    place = np.arange(size, dtype=np.float64)
    width = (KTOP + 0.5) / total
    diag = ((size - 1 - 2 * place) / 2) ** 2 * np.cos(2 * np.pi * width)
    side = place[1:] * (size - place[1:]) / 2
    vectors = np.linalg.eigh(np.diag(diag) + np.diag(side, 1) + np.diag(side, -1))[1]
    basis = np.concatenate([vectors[:, ::-1][:, :USED], np.zeros((size, RANK - USED))], axis=1)
    basis = basis * np.where(basis[size // 2] < 0, -1.0, 1.0)
    weights = []
    for group in range(4):
        waves = waves_of(group, np.arange(64))
        angle = 2 * np.pi / total * ((np.arange(size)[:, None] - 1) * waves[None, :] % total)
        alpha, beta = basis.T @ np.cos(angle), basis.T @ np.sin(angle)
        if group:
            sign = np.where(np.arange(64) < 32, 1.0, -1.0)
            top, low = (alpha, beta), (sign * beta, -sign * alpha)
        else:
            use = np.where(np.arange(64) < 32, 1.0, 0.0)
            top, low = (use * alpha, use * beta), ((1 - use) * alpha, (1 - use) * beta)
        weights.append(np.concatenate([np.concatenate(top, axis=1), np.concatenate(low, axis=1)], axis=0))
    weights = np.round(np.stack(weights) * 2.0**22) / 2.0**22
    wide = np.zeros((RANK, WIDE))
    wide[:, : COLS + 1] = basis[1:].T
    wide[:, WIDE - 1] = basis[0]
    wide = np.round(wide * 2.0**26) / 2.0**26
    wide_h, wide_l = split_table(wide)
    own = np.where(np.arange(WIDE)[:, None] < COLS, 1, 0).astype(ml_dtypes.bfloat16)
    high, low = split_table(weights)
    back = np.concatenate([np.swapaxes(part, 1, 2) for part in (high, low)], axis=1)
    evaluate = np.concatenate([wide_h, wide_l, wide_h], axis=0)
    return np.concatenate(
        [
            np.concatenate([wide_h.T * own, wide_l.T * own], axis=1),
            evaluate[:, : WIDE // 2],
            evaluate[:, WIDE // 2 :],
            np.concatenate([high, low], axis=2).reshape(-1, 2 * RANK),
            back.reshape(-1, 2 * RANK),
        ],
        axis=0,
    )


ROOT = float(np.sqrt(0.5))


def over_lanes(y):
    s = [y[j] + y[j + 4] for j in range(4)]
    d = [y[j] - y[j + 4] for j in range(4)]
    even, odd = s[0] + s[2], s[1] + s[3]
    minus, plus = ROOT * (d[1] - d[3]), ROOT * (d[1] + d[3])
    return [
        (even + odd, even - odd),
        (d[0] + minus, -(d[2] + plus)),
        (s[0] - s[2], s[3] - s[1]),
        (d[0] - minus, d[2] - plus),
    ]


def to_lanes(pairs):
    (y0, y4), (u1, v1), (u2, v2), (u3, v3) = pairs
    even, odd = y0 + y4, y0 - y4
    s = [even + u2, odd - v2, even - u2, odd + v2]
    du, sv = ROOT * (u1 - u3), ROOT * (v1 + v3)
    d = [u1 + u3, du - sv, v3 - v1, -du - sv]
    return [s[j] + d[j] for j in range(4)] + [s[j] - d[j] for j in range(4)]


@functools.lru_cache(None)
def half_metric(bands):
    total = bands * ROWS
    rows = np.clip(np.arange(bands)[:, None] * ROWS - 8 + np.arange(32)[None, :], 0, total - 1)
    metric = np.minimum(1.0 / np.cos(np.pi * ((rows + 0.5) / total - 0.5)), metric_cap)
    table = np.broadcast_to((0.5 * metric).astype(np.float32)[:, :, None], (bands, 32, 128)).copy()
    forward = mode_factors()[FORWARD : FORWARD + WIDE].astype(np.float32)
    for row, col in enumerate((0, COLS - 1)):
        table[:, row] = forward[col, :RANK] + forward[col, RANK:]
    return table


def dot_cols(a, b):
    return lax.dot_general(a, b, (((1,), (0,)), ((), ())), preferred_element_type=F32)


def split(x):
    high = x.astype(BF16)
    return high, (x - high.astype(F32)).astype(BF16)


def to_modes(x, table):
    xh, xl = split(x)
    half = table.shape[1] // 2
    wide = dot_cols(xh, table[...])
    return wide[:, :half] + wide[:, half:] + dot_cols(xl, table[:, 0:half])


def from_modes(z, *tables):
    zh, zl = split(z)
    three = jnp.concatenate([zh, zh, zl], axis=1)
    return jnp.concatenate([dot_cols(three, table[...]) for table in tables], axis=1)


def to_coefs(x, table):
    rows = x.shape[0]
    wide = dot_cols(jnp.concatenate(split(x), axis=0), table[...])
    half = wide.shape[1] // 2
    return wide[:rows, :half] + wide[:rows, half:] + wide[rows:, :half]


def from_coefs(z, table):
    zh, zl = split(z)
    rows = jnp.concatenate([jnp.concatenate([zh, zh], axis=1), jnp.concatenate([zl, jnp.zeros_like(zl)], axis=1)], axis=0)
    wide = dot_cols(rows, table[...])
    return wide[: z.shape[0]] + wide[z.shape[0] :]


def pack(levels):
    lane = lax.broadcasted_iota(jnp.int32, (1, RANK), 1)
    return [jnp.where(lane < USED, levels[l], roll(levels[3], 96 - 32 * l, 1)) for l in range(3)]


def unpack(parts):
    lane = lax.broadcasted_iota(jnp.int32, (1, RANK), 1)
    last = jnp.where(lane < 64, roll(parts[1], 64, 1), roll(parts[2], 96, 1))
    return parts + [jnp.where(lane < 32, roll(parts[0], 32, 1), last)]


def roll(x, shift, axis):
    return pltpu.roll(x, shift % x.shape[axis], axis)


def roll_blocks(x, shift):
    return roll(x.reshape(x.shape[0] * x.shape[1], x.shape[2]), shift, 1).reshape(x.shape)


def fold(x):
    while x.shape[0] > 1:
        half = x.shape[0] // 2
        x = x[:half] + roll_blocks(x[half:], 2 * half)
    return x


def kernel(
    bands, spread, east, north, rs, cs, cut, metric, table_in, tan_out, diag_out,
    spread_v, winds_v, rs_v, cs_v, cut_s, hm, table,
    grid, halo_out, halo_in, ybuf, yr, xb, cb, yc, zbuf, zr, eb, bz,
    tend, adj, gy,
    in_sem, halo_send, halo_recv, y_send, y_recv, c_send, c_recv, z_send, z_recv, b_send, b_recv,
):
    b = lax.axis_index("lat")
    i = lax.axis_index("lon")
    caps = POLAR // ROWS
    is_north = b == 0
    is_south = b == bands - 1
    polar = jnp.logical_or(b < caps, b >= bands - caps)
    above_polar = jnp.logical_or(b <= caps, is_south)
    below_polar = jnp.logical_or(b >= bands - caps - 1, is_north)
    near_polar = jnp.logical_or(above_polar, below_polar)
    across = lax.rem(i + LANES // 2, LANES)
    west = lax.rem(i + LANES - 1, LANES)
    east_lane = lax.rem(i + 1, LANES)
    nb = jnp.where(is_north, 0, b - 1)
    nl = jnp.where(is_north, across, i)
    sb = jnp.where(is_south, bands - 1, b + 1)
    sl = jnp.where(is_south, across, i)
    slot_n = jnp.where(is_north, 0, 1)
    slot_s = jnp.where(is_south, 1, 0)
    own_half = lax.rem(i, 2)
    edge_over = jnp.where(own_half == 0, is_north, is_south)
    over_pole = (is_north, is_south)
    outward = jnp.logical_or(
        jnp.logical_and(b == caps - 1, own_half == 1), jnp.logical_and(b == bands - caps, own_half == 0)
    )

    def plus(lane, d):
        return lax.rem(lane + d, LANES)

    load_spread = pltpu.make_async_copy(spread, spread_v, in_sem.at[0])
    load_rows = pltpu.make_async_copy(rs, rs_v, in_sem.at[1])
    load_cols = pltpu.make_async_copy(cs, cs_v, in_sem.at[2])
    load_metric = pltpu.make_async_copy(metric.at[b], hm, in_sem.at[4])
    load_cut = pltpu.make_async_copy(cut, cut_s, in_sem.at[5])

    def load_table(start, stop, sem):
        return pltpu.make_async_copy(table_in.at[start:stop], table.at[start:stop], in_sem.at[sem])

    load_forward = load_table(FORWARD, EVALUATE, 6)
    load_others = load_table(EVALUATE, TABLE_ROWS, 7)
    load_part = load_table(EVALUATE, TO_COEFS, 7)
    barrier = pltpu.get_barrier_semaphore()

    def greet(lat, lon):
        pl.semaphore_signal(barrier, inc=1, device_id=(lat, lon), device_id_type=MESH)

    @pl.when(polar)
    def _():
        for d in FAR_FIRST[:4]:
            greet(b, plus(i, d))

    greet(nb, nl)
    greet(sb, sl)
    greet(b, west)
    greet(b, east_lane)
    load_spread.start()
    load_rows.start()
    load_cols.start()
    pltpu.make_async_copy(east, winds_v.at[0], in_sem.at[3]).start()
    pltpu.make_async_copy(north, winds_v.at[1], in_sem.at[3]).start()
    load_metric.start()

    @pl.when(polar)
    def _():
        greet(b, across)
        load_forward.start()
        load_cut.start()

    @pl.when(jnp.logical_and(near_polar, jnp.logical_not(polar)))
    def _():
        load_part.start()

    load_rows.wait()
    load_cols.wait()
    load_spread.wait()
    grid[:, 8:24, 384:512] = jnp.zeros((PAIRS + 2 * LEV, ROWS, 128), F32)
    row_part = jnp.concatenate([rs_v[f] for f in range(FIELDS)], axis=0)
    row_part = (2 * row_part - 1).astype(F32).T
    for f in range(FIELDS):
        col_part = (2 * cs_v[f] - 1).astype(F32)
        for l in range(LEV):
            n = f * LEV + l
            grid[n, 8:24, 0:COLS] = spread_v[f, l] * (row_part[:, n : n + 1] * col_part[l : l + 1, :])

    @pl.when(polar)
    def _():
        load_others.start()

    pltpu.make_async_copy(winds_v, winds_v, in_sem.at[3]).wait()
    for w in range(2):
        for l in range(LEV):
            grid[PAIRS + w * LEV + l, 8:24, 0:COLS] = winds_v[w, l]

    def edge_rows(start, entries, rows):
        for s, row in enumerate(rows):
            for t in range(4):
                values = grid[entries, row, 128 * t : 128 * t + 128]
                if entries == slice(0, PAIRS):
                    halo_out[start[s] + t] = values
                else:
                    halo_out[start[s] + t // 2, 8 * (t % 2) : 8 * (t % 2) + 8, :] = values

    edge_rows((NEAR, NEAR + 4), slice(0, PAIRS), (8, 23))
    lane128 = lax.broadcasted_iota(jnp.int32, (1, 1, 128), 2)
    for s, (start, shift) in enumerate(((0, 0), (384, COLS - 2 - 384))):
        tile = grid[:, 8:24, start : start + 128]
        tile = jnp.where(jnp.logical_and(lane128 >= shift, lane128 < shift + 2), tile, 0.0)
        packed = fold(tile[:PAIRS]) + roll_blocks(fold(tile[PAIRS:]), 2 * PAIRS)
        halo_out[SIDES + s] = roll_blocks(packed, -shift)[0]

    pl.semaphore_wait(barrier, 4 + jnp.where(polar, LANES - 3, 0))

    def remote(src, dst, send, recv, lat, lon):
        return pltpu.make_async_remote_copy(
            src_ref=src, dst_ref=dst, send_sem=send, recv_sem=recv, device_id=(lat, lon), device_id_type=MESH
        )

    def halo_copy(start, count, to, which, lat, lon):
        return remote(
            halo_out.at[start : start + count], halo_in.at[pl.ds(to, count)], halo_send, halo_recv.at[which], lat, lon
        )

    def halo_arrival(start, stop, which):
        return remote(
            halo_out.at[start:stop], halo_in.at[start:stop], halo_send, halo_recv.at[which], b, west
        )

    halo_copy(NEAR, 4, NEAR + 4 * slot_n, 0, nb, nl).start()
    halo_copy(NEAR + 4, 4, NEAR + 4 * slot_s, 0, sb, sl).start()
    halo_copy(SIDES, 1, SIDES + 1, 0, b, west).start()
    halo_copy(SIDES + 1, 1, SIDES, 0, b, east_lane).start()

    others = pl.ds(0, LANES - 1)

    def all_y(q):
        return remote(ybuf.at[q, others], yr.at[q, others], y_send.at[q], y_recv.at[q], b, west)

    def send_values(q, x):
        y = to_modes(x.reshape(PAIRS * ROWS, WIDE), table.at[FORWARD:EVALUATE])
        y = y.reshape(FIELDS, LEV, 2, 8, RANK)
        blocks = [
            jnp.concatenate([y[f, l, h] for f in range(FIELDS) for h in range(2)], axis=0) for l in range(LEV)
        ]
        for l, part in enumerate(pack(blocks)):
            ybuf[q, :, l] = part.reshape(LANES, 8, RANK)

        for d in FAR_FIRST:
            o = plus(i, d)
            remote(ybuf.at[q, o], yr.at[q, i], y_send.at[q], y_recv.at[q], b, o).start()

        yr[q, i] = ybuf[q, i]

    def c_copy(o):
        return remote(cb.at[o], yc.at[i], c_send, c_recv, b, o)

    def all_c():
        return remote(cb.at[others], yc.at[others], c_send, c_recv, b, west)

    def z_copy(q, j):
        return remote(zbuf.at[q, j], zr.at[q, i], z_send.at[q], z_recv.at[q], b, j)

    def all_z(q):
        return remote(zbuf.at[q, others], zr.at[q, others], z_send.at[q], z_recv.at[q], b, west)

    def edge_sends():
        slot = jnp.where(own_half == 0, slot_n, slot_s)
        lat = jnp.where(own_half == 0, nb, sb)

        @pl.loop(0, LANES)
        def _(d):
            j = plus(i, d)
            lon = jnp.where(edge_over, plus(j, LANES // 2), j)
            here = jnp.logical_and(edge_over, lon == i)

            @pl.when(jnp.logical_not(here))
            def _():
                remote(eb.at[j], bz.at[slot, i // 2], b_send, b_recv.at[slot], lat, lon).start()

            @pl.when(here)
            def _():
                pltpu.make_async_copy(eb.at[j], bz.at[slot, i // 2], b_recv.at[slot]).start()

    def own_rows(q):
        row = lax.broadcasted_iota(jnp.int32, (8, 128), 0)
        cutoff = jnp.zeros((8, 128), jnp.int32)
        for r in range(8):
            cutoff = jnp.where(row == r, cut_s[8 * own_half + r], cutoff)
        keeps = []
        for group in range(4):
            wave = waves_of(group, lax.broadcasted_iota(jnp.int32, (8, 128), 1))
            keep = jnp.where(wave > cutoff, 2.0 / (COLS * LANES), 0.0)
            keeps.append(jnp.concatenate([keep] * LEV, axis=0))
        all_y(q).wait_recv()
        levels = unpack([yr[q, :, l].reshape(LANES * 8, RANK) for l in range(LEV - 1)])
        if q == 1:
            edge_row = jnp.where(row == 7 * own_half, 1.0, 0.0)
            all_c().wait_recv()
            ends = jnp.concatenate([yc[j, 8:16, :] for j in range(LANES)], axis=0)
            ends = pltpu.roll(ends, lax.rem(128 - 2 * LEV * (i // 2), 128), 1)
            levels = [
                levels[l]
                + ends[:, 2 * l : 2 * l + 1] * hm[0:1, :]
                + ends[:, 2 * l + 1 : 2 * l + 2] * hm[1:2, :]
                + jnp.concatenate([edge_row * yc[j, l : l + 1, :] for j in range(LANES)], axis=0)
                for l in range(LEV)
            ]
        lanes = [
            jnp.concatenate([levels[l][8 * j : 8 * j + 8, :] for l in range(LEV)], axis=0) for j in range(LANES)
        ]
        coefs = [
            to_coefs(jnp.concatenate(pair, axis=1), table.at[TO_COEFS + 256 * group : TO_COEFS + 256 * (group + 1)])
            for group, pair in enumerate(over_lanes(lanes))
        ]
        kept = [coef * keep for coef, keep in zip(coefs, keeps)]
        backs = [
            from_coefs(coef, table.at[FROM_COEFS + 256 * group : FROM_COEFS + 256 * (group + 1)])
            for group, coef in enumerate(kept)
        ]
        pairs = [(back[:, :RANK], back[:, RANK:]) for back in backs]
        zs = [z.reshape(LEV, 8, RANK) for z in to_lanes(pairs)]
        for l, part in enumerate(pack([jnp.concatenate([z[l] for z in zs], axis=0) for l in range(LEV)])):
            zbuf[q, :, l] = part.reshape(LANES, 8, RANK)

        def edges():
            for j, z in enumerate(zs):
                edge = jnp.where(own_half == 0, z[:, 0, :], z[:, 7, :])
                eb[j] = edge if q == 0 else eb[j] + edge
            if q == 1:
                edge_sends()

        if q == 1:
            pl.when(outward)(edges)
        for d in FAR_FIRST:
            z_copy(q, plus(i, d)).start()
        if q == 1:
            pl.when(jnp.logical_not(outward))(edges)
        else:
            edges()
        zr[q, i] = zbuf[q, i]

    def evaluate(z):
        return from_modes(z, table.at[EVALUATE : EVALUATE + 384], table.at[EVALUATE + 384 : TO_COEFS])

    def project(q, h):
        levels = unpack(
            [jnp.concatenate([zr[q, 2 * f + h, l] for f in range(FIELDS)], axis=0) for l in range(LEV - 1)]
        )
        z = jnp.concatenate(
            [levels[l][8 * f : 8 * f + 8, :] for f in range(FIELDS) for l in range(LEV)], axis=0
        )
        out = evaluate(z)
        return [[out[8 * (LEV * f + l) : 8 * (LEV * f + l + 1), :] for l in range(LEV)] for f in range(FIELDS)]

    def tendency_rows(h, l, at, half):
        lo = jnp.maximum(l - 1, 0)
        hi = jnp.minimum(l + 1, LEV - 1)
        ew = at(PAIRS + l, h)
        nw = at(PAIRS + LEV + l, h)
        mids, along_x, along_y = [], [], []
        for f in range(FIELDS):
            mid = at(f * LEV + l, h)
            mids.append(mid)
            along_x.append(half * (roll(mid, -1, 1) - roll(mid, 1, 1)))
            along_y.append(0.5 * (at(f * LEV + l, h + 1) - at(f * LEV + l, h - 1)))
        linked = (along_x[2], along_y[2], along_x[0] + along_y[1], None)
        out = []
        for f in range(FIELDS):
            mixed = at(f * LEV + lo, h) + at(f * LEV + hi, h) - 2.0 * mids[f]
            t = -(ew * along_x[f] + nw * along_y[f]) + mixing * mixed
            if linked[f] is not None:
                t = t - coupling * linked[f]
            out.append(time_step * t)
        return out

    def full_tendency():
        @pl.loop(0, LEV)
        def _(l):
            for h in (8, 16):
                half = jnp.concatenate([hm[h : h + 8, :]] * 4, axis=1)
                for f, t in enumerate(tendency_rows(h, l, lambda n, r: grid[n, r : r + 8, :], half)):
                    tend[f * LEV + l, h - 8 : h, :] = t

    def side_tendency():
        lane = lax.broadcasted_iota(jnp.int32, (1, 128), 1)
        late = jnp.logical_or(jnp.logical_or(lane == 65, lane == 66), lane == 127)

        def at(n, r):
            return jnp.where(lane < 2, grid[n, r : r + 8, 0:128], grid[n, r : r + 8, 384:512])

        @pl.loop(0, LEV)
        def _(l):
            for h in (8, 16):
                for f, t in enumerate(tendency_rows(h, l, at, hm[h : h + 8, :])):
                    n, rows = f * LEV + l, slice(h - 8, h)
                    tend[n, rows, 0:128] = jnp.where(lane == 0, t, tend[n, rows, 0:128])
                    tend[n, rows, 384:512] = jnp.where(late, t, tend[n, rows, 384:512])

    load_metric.wait()

    @pl.when(polar)
    def _():
        load_forward.wait()
        send_values(0, grid[0:PAIRS, 8:24, :])
        grid[0:PAIRS, 7:8, :] = jnp.zeros((PAIRS, 1, WIDE), F32)
        grid[0:PAIRS, 24:25, :] = jnp.zeros((PAIRS, 1, WIDE), F32)
        full_tendency()
        send_values(1, tend[...])

    edge_rows((REST + 4, REST + 11), slice(PAIRS, PAIRS + 2 * LEV), (8, 23))

    halo_arrival(NEAR, REST, 0).wait_recv()
    lane2 = lax.broadcasted_iota(jnp.int32, (1, 128), 1)
    row16 = lax.broadcasted_iota(jnp.int32, (PAIRS, 1), 0)
    is_v = jnp.logical_and(row16 >= LEV, row16 < 2 * LEV)
    is_temp = jnp.logical_and(row16 >= 2 * LEV, row16 < 3 * LEV)

    def flip(s, minus):
        sign = jnp.where(row16 < 2 * LEV, -1.0, 1.0) * minus
        return jnp.where(over_pole[s], sign, 1.0)

    def row_link(x):
        return jnp.where(is_v, roll(x, -LEV, 0), jnp.where(is_temp, roll(x, LEV, 0), 0.0))

    def wind(buffer, s, w):
        base = REST + 7 * s + 4
        rows = [buffer[base + t // 2, 8 * (t % 2) + LEV * w : 8 * (t % 2) + LEV * (w + 1), :] for t in range(4)]
        return jnp.concatenate([jnp.concatenate(rows, axis=1)] * FIELDS, axis=0)

    def row_of(buffer, start):
        return jnp.concatenate([buffer[start + t] for t in range(4)], axis=1)

    @pl.when(polar)
    def _():
        added = []
        for s, sign in ((0, 0.5 * time_step), (1, -0.5 * time_step)):
            ghost = flip(s, 1.0) * row_of(halo_in, NEAR + 4 * s)
            added.append(sign * (wind(halo_out, s, 1) * ghost + coupling * row_link(ghost)))
            xb[s] = added[s]
        y = to_modes(jnp.concatenate(added, axis=0), table.at[FORWARD:EVALUATE])
        for s in range(2):
            for f in range(FIELDS):
                cb[2 * f + s, 0:LEV, :] = y[(s * FIELDS + f) * LEV : (s * FIELDS + f + 1) * LEV, :]
        ends = []
        for side, sign in ((0, -1.0), (1, 1.0)):
            came = halo_in[SIDES + side]
            along_x = (sign * hm[8:24, :]) * (roll(came, -1, 1) if side == 0 else came)
            mine = jnp.where(
                jnp.logical_and(lane2 >= 2 * PAIRS, lane2 < 2 * (PAIRS + LEV)), halo_out[SIDES + side], 0.0
            )
            ew = sum(roll(mine, 2 * LEV * f - 2 * PAIRS - side, 1) for f in range(FIELDS))
            linked = jnp.where(
                lane2 < 2 * LEV,
                roll(along_x, -4 * LEV, 1),
                jnp.where(
                    jnp.logical_and(lane2 >= 4 * LEV, lane2 < 6 * LEV), roll(along_x, 4 * LEV, 1), 0.0
                ),
            )
            ends.append(time_step * (-ew * along_x - coupling * linked))
        ends = jnp.where(lax.rem(lane2, 2) == 0, ends[0], roll(ends[1], 1, 1))
        for f in range(FIELDS):
            for h in range(2):
                cb[2 * f + h, 8:16, :] = ends[8 * h : 8 * h + 8, :]

        for d in FAR_FIRST:
            c_copy(plus(i, d)).start()

        yc[i] = cb[i]

    from_west = roll(halo_in[SIDES], 126, 1)
    from_east = roll(halo_in[SIDES + 1], COLS - 384, 1)
    both = jnp.where(jnp.logical_and(lane2 >= 66, lane2 < 114), from_east, from_west)[None]
    for width in (2, 4, 8):
        both = jnp.concatenate([both, roll_blocks(both, -width)], axis=0)
    both = jnp.concatenate([both, roll_blocks(both, -16), roll_blocks(both, -32)], axis=0)
    in_halo = jnp.logical_or(jnp.logical_and(lane128 >= 66, lane128 < 68), lane128 >= 126)
    grid[:, 8:24, 384:512] = jnp.where(in_halo, both, grid[:, 8:24, 384:512])
    edge_rows((REST, REST + 7), slice(0, PAIRS), (9, 22))
    for s, near in enumerate((8, 23)):
        halo_out[REST + 7 * s + 6] = grid[0:PAIRS, near, 384:512]
    halo_copy(REST, 7, REST + 7 * slot_n, 1, nb, nl).start()
    halo_copy(REST + 7, 7, REST + 7 * slot_s, 1, sb, sl).start()

    @pl.when(polar)
    def _():
        load_cut.wait()
        load_others.wait()
        own_rows(0)

    @pl.when(jnp.logical_and(polar, b < bands // 2))
    def _():
        own_rows(1)

    halo_arrival(REST, BLOCKS, 1).wait_recv()
    edge_row = (7, 24)
    edge_probe = []
    for s in range(2):
        edge_probe.append(
            jnp.concatenate([halo_in[NEAR + 4 * s + t] for t in range(3)] + [halo_in[REST + 7 * s + 6]], axis=1)
        )
        grid[0:PAIRS, edge_row[s], :] = flip(s, 1.0) * edge_probe[s]

    @pl.when(polar)
    def _():
        for s, row in ((0, 0), (1, 15)):
            tend[:, row, :] = tend[:, row, :] + xb[s]
        side_tendency()

    @pl.when(jnp.logical_not(polar))
    def _():
        full_tendency()

    def edge_weights(s, a):
        return -wind(halo_in, s, 1) * a - coupling * row_link(a)

    for s, inward in ((0, 1.0), (1, -1.0)):
        mid = edge_probe[s]
        half = jnp.concatenate([hm[edge_row[s] : edge_row[s] + 1, :]] * 4, axis=1)
        along_x = half * (roll(mid, -1, 1) - roll(mid, 1, 1))
        turn = jnp.where(over_pole[s], -0.5 * inward, 0.5 * inward)
        along_y = turn * (flip(s, 1.0) * row_of(halo_out, NEAR + 4 * s) - row_of(halo_in, REST + 7 * s))
        linked = jnp.where(row16 < LEV, roll(along_x, -2 * LEV, 0), row_link(along_y))
        linked = linked + jnp.where(is_temp, roll(along_x, 2 * LEV, 0), 0.0)
        up = jnp.where(lax.rem(row16, LEV) == 0, mid, roll(mid, 1, 0))
        down = jnp.where(lax.rem(row16, LEV) == LEV - 1, mid, roll(mid, -1, 0))
        t = -(wind(halo_in, s, 0) * along_x + wind(halo_in, s, 1) * along_y) - coupling * linked
        a = mid + time_step * (t + mixing * (up + down - 2.0 * mid))
        gy[0:PAIRS, edge_row[s], :] = flip(s, -1.0) * edge_weights(s, a)

    @pl.when(jnp.logical_and(polar, b >= bands // 2))
    def _():
        own_rows(1)

    def row_weights(a, nw):
        return (
            -nw * a[0],
            -nw * a[1] - coupling * a[2],
            -nw * a[2] - coupling * a[1],
            -nw * a[3],
        )

    def put_weights(l, h, a):
        for f, weight in enumerate(row_weights(a, grid[PAIRS + LEV + l, h : h + 8, :])):
            gy[f * LEV + l, h : h + 8, :] = weight

    @pl.when(polar)
    def _():
        all_z(0).wait_recv()
        for h in (8, 16):
            taken = project(0, h // 8 - 1)
            for l in range(LEV):
                for f in range(FIELDS):
                    n, rows = f * LEV + l, slice(h - 8, h)
                    adj[n, rows, :] = grid[n, h : h + 8, :] + tend[n, rows, :] - taken[f][l]
        all_z(1).wait_recv()
        for h in (8, 16):
            taken = project(1, h // 8 - 1)
            for l in range(LEV):
                a = []
                for f in range(FIELDS):
                    n, rows = f * LEV + l, slice(h - 8, h)
                    change = tend[n, rows, :] - taken[f][l]
                    tend[n, rows, :] = change
                    tan_out[f, l, rows, :] = (grid[n, h : h + 8, :] + change)[:, :COLS]
                    a.append(adj[n, rows, :] - taken[f][l])
                    adj[n, rows, :] = a[f]
                put_weights(l, h, a)

    @pl.when(jnp.logical_not(polar))
    def _():
        @pl.loop(0, LEV)
        def _(l):
            for h in (8, 16):
                a = []
                for f in range(FIELDS):
                    n, rows = f * LEV + l, slice(h - 8, h)
                    a.append(grid[n, h : h + 8, :] + tend[n, rows, :])
                    tan_out[f, l, rows, :] = a[f][:, :COLS]
                    adj[n, rows, :] = a[f]
                put_weights(l, h, a)

    @pl.loop(0, LEV)
    def _(l):
        lo = jnp.maximum(l - 1, 0)
        hi = jnp.minimum(l + 1, LEV - 1)
        for h in (8, 16):
            rows = slice(h - 8, h)
            half = jnp.concatenate([hm[h : h + 8, :]] * 4, axis=1)
            ew = grid[PAIRS + l, h : h + 8, :]
            a = [adj[f * LEV + l, rows, :] for f in range(FIELDS)]
            col_weights = (
                -ew * a[0] - coupling * a[2],
                -ew * a[1],
                -ew * a[2] - coupling * a[0],
                -ew * a[3],
            )
            for f in range(FIELDS):
                n = f * LEV + l
                back = half * (roll(col_weights[f], 1, 1) - roll(col_weights[f], -1, 1))
                back = back + 0.5 * (gy[n, h - 1 : h + 7, :] - gy[n, h + 1 : h + 9, :])
                back = back + mixing * (adj[f * LEV + lo, rows, :] + adj[f * LEV + hi, rows, :] - 2.0 * a[f])
                diag = grid[n, h : h + 8, :] * (tend[n, rows, :] + time_step * back)
                diag_out[f, l, rows, :] = diag[:, :COLS]

    @pl.when(jnp.logical_and(near_polar, jnp.logical_not(polar)))
    def _():
        load_part.wait()

    for s, wanted in enumerate((above_polar, below_polar)):
        @pl.when(wanted)
        def _():
            remote(bz.at[s], bz.at[s], b_send, b_recv.at[s], nb, nl).wait_recv()

        @pl.when(jnp.logical_not(wanted))
        def _():
            bz[s] = jnp.zeros((FIELDS, LEV, RANK), F32)

    @pl.when(near_polar)
    def _():
        taken = evaluate(jnp.concatenate([bz[s, f] for s in range(2) for f in range(FIELDS)], axis=0))
        for s, wanted in enumerate((above_polar, below_polar)):
            @pl.when(wanted)
            def _():
                row = 15 * s
                weight = flip(s, -1.0) * edge_weights(s, taken[PAIRS * s : PAIRS * (s + 1), :])
                less = ((0.5, -0.5)[s] * time_step) * grid[0:PAIRS, 8 + row, :] * weight
                for f in range(FIELDS):
                    diag_out[f, :, row, :] = diag_out[f, :, row, :] - less[f * LEV : (f + 1) * LEV, :COLS]

    halo_arrival(0, BLOCKS, 0).wait_send()

    @pl.when(polar)
    def _():
        all_c().wait_send()
        for q in range(2):
            all_y(q).wait_send()
            all_z(q).wait_send()

        @pl.when(edge_over)
        def _():
            remote(eb.at[others], eb.at[others], b_send, b_recv.at[0], b, west).wait_send()

        @pl.when(jnp.logical_not(edge_over))
        def _():
            remote(eb, eb, b_send, b_recv.at[0], b, west).wait_send()


def hand_out(tan_in, diag_in, tan_out, diag_out, sem):
    copies = [
        pltpu.make_async_copy(src, dst, sem.at[n])
        for n, (src, dst) in enumerate(((tan_in, tan_out), (diag_in, diag_out)))
    ]
    for copy in copies:
        copy.start()
    for copy in copies:
        copy.wait()


def per_device(bands, row_signs, col_signs, spread, east_wind, north_wind, cutoffs):
    any_spec = pl.BlockSpec(memory_space=pl.ANY)
    out = jax.ShapeDtypeStruct((FIELDS, LEV, ROWS, COLS), F32)
    tables = [jnp.asarray(half_metric(bands)), jnp.asarray(mode_factors())]
    operands = (spread, east_wind, north_wind, row_signs, col_signs, cutoffs, *tables)
    vmem = pltpu.VMEM
    dma = pltpu.SemaphoreType.DMA
    held = pltpu.VMEM(out.shape, F32)
    results = pl.pallas_call(
        functools.partial(kernel, bands),
        out_shape=(held, held),
        in_specs=[any_spec] * 8,
        out_specs=(pl.BlockSpec(memory_space=pltpu.VMEM),) * 2,
        scratch_shapes=[
            vmem((FIELDS, LEV, ROWS, COLS), F32),
            vmem((2, LEV, ROWS, COLS), F32),
            vmem((FIELDS, LEV, ROWS), jnp.int32),
            vmem((FIELDS, LEV, COLS), jnp.int32),
            pltpu.SMEM((ROWS,), jnp.int32),
            vmem((32, 128), F32),
            vmem((TABLE_ROWS, 2 * RANK), BF16),
            vmem((PAIRS + 2 * LEV, 32, WIDE), F32),
            vmem((BLOCKS, 16, 128), F32),
            vmem((BLOCKS, 16, 128), F32),
            vmem((2, LANES, LEV - 1, 8, RANK), F32),
            vmem((2, LANES, LEV - 1, 8, RANK), F32),
            vmem((2, PAIRS, WIDE), F32),
            vmem((LANES, 16, RANK), F32),
            vmem((LANES, 16, RANK), F32),
            vmem((2, LANES, LEV - 1, 8, RANK), F32),
            vmem((2, LANES, LEV - 1, 8, RANK), F32),
            vmem((LANES, LEV, RANK), F32),
            vmem((2, FIELDS, LEV, RANK), F32),
            vmem((PAIRS, ROWS, WIDE), F32),
            vmem((PAIRS, ROWS, WIDE), F32),
            vmem((PAIRS, 32, WIDE), F32),
            dma((8,)),
            dma,
            dma((2,)),
            dma((2,)),
            dma((2,)),
            dma,
            dma,
            dma((2,)),
            dma((2,)),
            dma,
            dma((2,)),
        ],
        compiler_params=pltpu.CompilerParams(
            collective_id=0, has_side_effects=True, vmem_limit_bytes=32 * 2**20
        ),
        cost_estimate=pl.CostEstimate(flops=10**9, bytes_accessed=4 * 10**6, transcendentals=0),
    )(*(pltpu.with_memory_space_constraint(x, pltpu.HBM) for x in operands))
    return pl.pallas_call(
        hand_out,
        out_shape=(out, out),
        in_specs=[any_spec] * 2,
        out_specs=(any_spec, any_spec),
        scratch_shapes=[dma((2,))],
        compiler_params=pltpu.CompilerParams(vmem_limit_bytes=2**20),
    )(*(pltpu.with_memory_space_constraint(x, pltpu.VMEM) for x in results))


def solution(mesh):
    return jax.shard_map(
        functools.partial(per_device, mesh.shape["lat"]),
        mesh=mesh,
        in_specs=(
            P(None, None, "lat"),
            P(None, None, "lon"),
            P(None, None, "lat", "lon"),
            P(None, "lat", "lon"),
            P(None, "lat", "lon"),
            P("lat"),
        ),
        out_specs=(P(None, None, "lat", "lon"), P(None, None, "lat", "lon")),
        check_vma=False,
    )
```

```python
import functools

import jax
import jax.numpy as jnp
import ml_dtypes
import numpy as np
from jax import lax
from jax.experimental import pallas as pl
from jax.experimental.pallas import tpu as pltpu
from jax.sharding import PartitionSpec as P

KTOP = 256
POLAR = 32
RANK = 128
USED = 96
ROWS = 16
COLS = 450
WIDE = 512
LANES = 8
FIELDS = 4
LEV = 4
PAIRS = FIELDS * LEV

time_step = 0.5
coupling = 0.5
mixing = 0.2
metric_cap = 4.0

FORWARD, EVALUATE, TO_COEFS, FROM_COEFS, TABLE_ROWS = 0, 512, 1280, 2304, 3328
NEAR, SIDES, REST, BLOCKS = 0, 8, 10, 24

FAR_FIRST = (6, 2, 5, 3, 7, 1, 4)

MESH = pl.DeviceIdType.MESH
F32 = jnp.float32
BF16 = jnp.bfloat16


def split_table(table):
    high = table.astype(ml_dtypes.bfloat16)
    low = (table - high.astype(np.float64)).astype(ml_dtypes.bfloat16)
    return high, low


def waves_of(group, lane_index):
    place = lane_index % 64
    second = place // 32
    other = (8 - group) if group else 4
    residue = group + second * (other - group)
    return 8 * (place % 32) + residue + (8 * (1 - second) if group == 0 else 0)


@functools.lru_cache(None)
def mode_factors():
    total = COLS * LANES
    size = COLS + 2
    place = np.arange(size, dtype=np.float64)
    width = (KTOP + 0.5) / total
    diag = ((size - 1 - 2 * place) / 2) ** 2 * np.cos(2 * np.pi * width)
    side = place[1:] * (size - place[1:]) / 2
    vectors = np.linalg.eigh(np.diag(diag) + np.diag(side, 1) + np.diag(side, -1))[1]
    basis = np.concatenate([vectors[:, ::-1][:, :USED], np.zeros((size, RANK - USED))], axis=1)
    basis = basis * np.where(basis[size // 2] < 0, -1.0, 1.0)
    weights = []
    for group in range(4):
        waves = waves_of(group, np.arange(64))
        angle = 2 * np.pi / total * ((np.arange(size)[:, None] - 1) * waves[None, :] % total)
        alpha, beta = basis.T @ np.cos(angle), basis.T @ np.sin(angle)
        if group:
            sign = np.where(np.arange(64) < 32, 1.0, -1.0)
            top, low = (alpha, beta), (sign * beta, -sign * alpha)
        else:
            use = np.where(np.arange(64) < 32, 1.0, 0.0)
            top, low = (use * alpha, use * beta), ((1 - use) * alpha, (1 - use) * beta)
        weights.append(np.concatenate([np.concatenate(top, axis=1), np.concatenate(low, axis=1)], axis=0))
    weights = np.round(np.stack(weights) * 2.0**22) / 2.0**22
    wide = np.zeros((RANK, WIDE))
    wide[:, : COLS + 1] = basis[1:].T
    wide[:, WIDE - 1] = basis[0]
    wide = np.round(wide * 2.0**26) / 2.0**26
    wide_h, wide_l = split_table(wide)
    own = np.where(np.arange(WIDE)[:, None] < COLS, 1, 0).astype(ml_dtypes.bfloat16)
    high, low = split_table(weights)
    back = np.concatenate([np.swapaxes(part, 1, 2) for part in (high, low)], axis=1)
    evaluate = np.concatenate([wide_h, wide_l, wide_h], axis=0)
    return np.concatenate(
        [
            np.concatenate([wide_h.T * own, wide_l.T * own], axis=1),
            evaluate[:, : WIDE // 2],
            evaluate[:, WIDE // 2 :],
            np.concatenate([high, low], axis=2).reshape(-1, 2 * RANK),
            back.reshape(-1, 2 * RANK),
        ],
        axis=0,
    )


ROOT = float(np.sqrt(0.5))


def over_lanes(y):
    s = [y[j] + y[j + 4] for j in range(4)]
    d = [y[j] - y[j + 4] for j in range(4)]
    even, odd = s[0] + s[2], s[1] + s[3]
    minus, plus = ROOT * (d[1] - d[3]), ROOT * (d[1] + d[3])
    return [
        (even + odd, even - odd),
        (d[0] + minus, -(d[2] + plus)),
        (s[0] - s[2], s[3] - s[1]),
        (d[0] - minus, d[2] - plus),
    ]


def to_lanes(pairs):
    (y0, y4), (u1, v1), (u2, v2), (u3, v3) = pairs
    even, odd = y0 + y4, y0 - y4
    s = [even + u2, odd - v2, even - u2, odd + v2]
    du, sv = ROOT * (u1 - u3), ROOT * (v1 + v3)
    d = [u1 + u3, du - sv, v3 - v1, -du - sv]
    return [s[j] + d[j] for j in range(4)] + [s[j] - d[j] for j in range(4)]


@functools.lru_cache(None)
def half_metric(bands):
    total = bands * ROWS
    rows = np.clip(np.arange(bands)[:, None] * ROWS - 8 + np.arange(32)[None, :], 0, total - 1)
    metric = np.minimum(1.0 / np.cos(np.pi * ((rows + 0.5) / total - 0.5)), metric_cap)
    table = np.broadcast_to((0.5 * metric).astype(np.float32)[:, :, None], (bands, 32, 128)).copy()
    forward = mode_factors()[FORWARD : FORWARD + WIDE].astype(np.float32)
    for row, col in enumerate((0, COLS - 1)):
        table[:, row] = forward[col, :RANK] + forward[col, RANK:]
    return table


def dot_cols(a, b):
    return lax.dot_general(a, b, (((1,), (0,)), ((), ())), preferred_element_type=F32)


def split(x):
    high = x.astype(BF16)
    return high, (x - high.astype(F32)).astype(BF16)


def to_modes(x, table):
    xh, xl = split(x)
    half = table.shape[1] // 2
    wide = dot_cols(xh, table[...])
    return wide[:, :half] + wide[:, half:] + dot_cols(xl, table[:, 0:half])


def from_modes(z, *tables):
    zh, zl = split(z)
    three = jnp.concatenate([zh, zh, zl], axis=1)
    return jnp.concatenate([dot_cols(three, table[...]) for table in tables], axis=1)


def to_coefs(x, table):
    rows = x.shape[0]
    wide = dot_cols(jnp.concatenate(split(x), axis=0), table[...])
    half = wide.shape[1] // 2
    return wide[:rows, :half] + wide[:rows, half:] + wide[rows:, :half]


def from_coefs(z, table):
    zh, zl = split(z)
    rows = jnp.concatenate([jnp.concatenate([zh, zh], axis=1), jnp.concatenate([zl, jnp.zeros_like(zl)], axis=1)], axis=0)
    wide = dot_cols(rows, table[...])
    return wide[: z.shape[0]] + wide[z.shape[0] :]


def pack(levels):
    lane = lax.broadcasted_iota(jnp.int32, (1, RANK), 1)
    return [jnp.where(lane < USED, levels[l], roll(levels[3], 96 - 32 * l, 1)) for l in range(3)]


def unpack(parts):
    lane = lax.broadcasted_iota(jnp.int32, (1, RANK), 1)
    last = jnp.where(lane < 64, roll(parts[1], 64, 1), roll(parts[2], 96, 1))
    return parts + [jnp.where(lane < 32, roll(parts[0], 32, 1), last)]


def roll(x, shift, axis):
    return pltpu.roll(x, shift % x.shape[axis], axis)


def roll_blocks(x, shift):
    return roll(x.reshape(x.shape[0] * x.shape[1], x.shape[2]), shift, 1).reshape(x.shape)


def fold(x):
    while x.shape[0] > 1:
        half = x.shape[0] // 2
        x = x[:half] + roll_blocks(x[half:], 2 * half)
    return x


def kernel(
    bands, spread, east, north, rs, cs, cut, metric, table_in, tan_out, diag_out,
    spread_v, winds_v, rs_v, cs_v, cut_s, hm, table,
    grid, halo_out, halo_in, ybuf, yr, xb, cb, yc, zbuf, zr, eb, bz,
    tend, adj, gy,
    in_sem, halo_send, halo_recv, y_send, y_recv, c_send, c_recv, z_send, z_recv, b_send, b_recv,
):
    b = lax.axis_index("lat")
    i = lax.axis_index("lon")
    caps = POLAR // ROWS
    is_north = b == 0
    is_south = b == bands - 1
    polar = jnp.logical_or(b < caps, b >= bands - caps)
    above_polar = jnp.logical_or(b <= caps, is_south)
    below_polar = jnp.logical_or(b >= bands - caps - 1, is_north)
    near_polar = jnp.logical_or(above_polar, below_polar)
    across = lax.rem(i + LANES // 2, LANES)
    west = lax.rem(i + LANES - 1, LANES)
    east_lane = lax.rem(i + 1, LANES)
    nb = jnp.where(is_north, 0, b - 1)
    nl = jnp.where(is_north, across, i)
    sb = jnp.where(is_south, bands - 1, b + 1)
    sl = jnp.where(is_south, across, i)
    slot_n = jnp.where(is_north, 0, 1)
    slot_s = jnp.where(is_south, 1, 0)
    own_half = lax.rem(i, 2)
    edge_over = jnp.where(own_half == 0, is_north, is_south)
    over_pole = (is_north, is_south)
    outward = jnp.logical_or(
        jnp.logical_and(b == caps - 1, own_half == 1), jnp.logical_and(b == bands - caps, own_half == 0)
    )

    def plus(lane, d):
        return lax.rem(lane + d, LANES)

    load_spread = pltpu.make_async_copy(spread, spread_v, in_sem.at[0])
    load_rows = pltpu.make_async_copy(rs, rs_v, in_sem.at[1])
    load_cols = pltpu.make_async_copy(cs, cs_v, in_sem.at[2])
    load_metric = pltpu.make_async_copy(metric.at[b], hm, in_sem.at[4])
    load_cut = pltpu.make_async_copy(cut, cut_s, in_sem.at[5])

    def load_table(start, stop, sem):
        return pltpu.make_async_copy(table_in.at[start:stop], table.at[start:stop], in_sem.at[sem])

    load_forward = load_table(FORWARD, EVALUATE, 6)
    load_others = load_table(EVALUATE, TABLE_ROWS, 7)
    load_part = load_table(EVALUATE, TO_COEFS, 7)
    barrier = pltpu.get_barrier_semaphore()

    def greet(lat, lon):
        pl.semaphore_signal(barrier, inc=1, device_id=(lat, lon), device_id_type=MESH)

    greet(nb, nl)
    greet(sb, sl)

    @pl.when(polar)
    def _():
        for d in FAR_FIRST[:4]:
            greet(b, plus(i, d))

    greet(b, west)
    greet(b, east_lane)
    load_spread.start()
    load_rows.start()
    load_cols.start()
    pltpu.make_async_copy(east, winds_v.at[0], in_sem.at[3]).start()
    pltpu.make_async_copy(north, winds_v.at[1], in_sem.at[3]).start()
    load_metric.start()

    @pl.when(polar)
    def _():
        greet(b, across)
        load_forward.start()
        load_cut.start()

    @pl.when(jnp.logical_and(near_polar, jnp.logical_not(polar)))
    def _():
        load_part.start()

    load_rows.wait()
    load_cols.wait()
    load_spread.wait()
    grid[:, 8:24, 384:512] = jnp.zeros((PAIRS + 2 * LEV, ROWS, 128), F32)
    row_part = jnp.concatenate([rs_v[f] for f in range(FIELDS)], axis=0)
    row_part = (2 * row_part - 1).astype(F32).T
    for f in range(FIELDS):
        col_part = (2 * cs_v[f] - 1).astype(F32)
        for l in range(LEV):
            n = f * LEV + l
            grid[n, 8:24, 0:COLS] = spread_v[f, l] * (row_part[:, n : n + 1] * col_part[l : l + 1, :])

    @pl.when(polar)
    def _():
        load_others.start()

    pltpu.make_async_copy(winds_v, winds_v, in_sem.at[3]).wait()
    for w in range(2):
        for l in range(LEV):
            grid[PAIRS + w * LEV + l, 8:24, 0:COLS] = winds_v[w, l]

    def edge_rows(start, entries, rows):
        for s, row in enumerate(rows):
            for t in range(4):
                values = grid[entries, row, 128 * t : 128 * t + 128]
                if entries == slice(0, PAIRS):
                    halo_out[start[s] + t] = values
                else:
                    halo_out[start[s] + t // 2, 8 * (t % 2) : 8 * (t % 2) + 8, :] = values

    edge_rows((NEAR, NEAR + 4), slice(0, PAIRS), (8, 23))
    lane128 = lax.broadcasted_iota(jnp.int32, (1, 1, 128), 2)
    for s, (start, shift) in enumerate(((0, 0), (384, COLS - 2 - 384))):
        tile = grid[:, 8:24, start : start + 128]
        tile = jnp.where(jnp.logical_and(lane128 >= shift, lane128 < shift + 2), tile, 0.0)
        packed = fold(tile[:PAIRS]) + roll_blocks(fold(tile[PAIRS:]), 2 * PAIRS)
        halo_out[SIDES + s] = roll_blocks(packed, -shift)[0]

    pl.semaphore_wait(barrier, 4 + jnp.where(polar, LANES - 3, 0))

    def remote(src, dst, send, recv, lat, lon):
        return pltpu.make_async_remote_copy(
            src_ref=src, dst_ref=dst, send_sem=send, recv_sem=recv, device_id=(lat, lon), device_id_type=MESH
        )

    def halo_copy(start, count, to, which, lat, lon):
        return remote(
            halo_out.at[start : start + count], halo_in.at[pl.ds(to, count)], halo_send, halo_recv.at[which], lat, lon
        )

    def halo_arrival(start, stop, which):
        return remote(
            halo_out.at[start:stop], halo_in.at[start:stop], halo_send, halo_recv.at[which], b, west
        )

    @pl.when(b < bands // 2)
    def _():
        halo_copy(NEAR, 4, NEAR + 4 * slot_n, 0, nb, nl).start()

    halo_copy(NEAR + 4, 4, NEAR + 4 * slot_s, 0, sb, sl).start()

    @pl.when(b >= bands // 2)
    def _():
        halo_copy(NEAR, 4, NEAR + 4 * slot_n, 0, nb, nl).start()

    halo_copy(SIDES, 1, SIDES + 1, 0, b, west).start()
    halo_copy(SIDES + 1, 1, SIDES, 0, b, east_lane).start()

    others = pl.ds(0, LANES - 1)

    def all_y(q):
        return remote(ybuf.at[q, others], yr.at[q, others], y_send.at[q], y_recv.at[q], b, west)

    def send_values(q, x):
        y = to_modes(x.reshape(PAIRS * ROWS, WIDE), table.at[FORWARD:EVALUATE])
        y = y.reshape(FIELDS, LEV, 2, 8, RANK)
        blocks = [
            jnp.concatenate([y[f, l, h] for f in range(FIELDS) for h in range(2)], axis=0) for l in range(LEV)
        ]
        for l, part in enumerate(pack(blocks)):
            ybuf[q, :, l] = part.reshape(LANES, 8, RANK)

        for d in FAR_FIRST:
            o = plus(i, d)
            remote(ybuf.at[q, o], yr.at[q, i], y_send.at[q], y_recv.at[q], b, o).start()

        yr[q, i] = ybuf[q, i]

    def c_copy(o):
        return remote(cb.at[o], yc.at[i], c_send, c_recv, b, o)

    def all_c():
        return remote(cb.at[others], yc.at[others], c_send, c_recv, b, west)

    def z_copy(q, j):
        return remote(zbuf.at[q, j], zr.at[q, i], z_send.at[q], z_recv.at[q], b, j)

    def all_z(q):
        return remote(zbuf.at[q, others], zr.at[q, others], z_send.at[q], z_recv.at[q], b, west)

    def edge_sends():
        slot = jnp.where(own_half == 0, slot_n, slot_s)
        lat = jnp.where(own_half == 0, nb, sb)

        @pl.loop(0, LANES)
        def _(d):
            j = plus(i, d)
            lon = jnp.where(edge_over, plus(j, LANES // 2), j)
            here = jnp.logical_and(edge_over, lon == i)

            @pl.when(jnp.logical_not(here))
            def _():
                remote(eb.at[j], bz.at[slot, i // 2], b_send, b_recv.at[slot], lat, lon).start()

            @pl.when(here)
            def _():
                pltpu.make_async_copy(eb.at[j], bz.at[slot, i // 2], b_recv.at[slot]).start()

    def own_rows(q):
        row = lax.broadcasted_iota(jnp.int32, (8, 128), 0)
        cutoff = jnp.zeros((8, 128), jnp.int32)
        for r in range(8):
            cutoff = jnp.where(row == r, cut_s[8 * own_half + r], cutoff)
        keeps = []
        for group in range(4):
            wave = waves_of(group, lax.broadcasted_iota(jnp.int32, (8, 128), 1))
            keep = jnp.where(wave > cutoff, 2.0 / (COLS * LANES), 0.0)
            keeps.append(jnp.concatenate([keep] * LEV, axis=0))
        all_y(q).wait_recv()
        levels = unpack([yr[q, :, l].reshape(LANES * 8, RANK) for l in range(LEV - 1)])
        if q == 1:
            edge_row = jnp.where(row == 7 * own_half, 1.0, 0.0)
            all_c().wait_recv()
            ends = jnp.concatenate([yc[j, 8:16, :] for j in range(LANES)], axis=0)
            ends = pltpu.roll(ends, lax.rem(128 - 2 * LEV * (i // 2), 128), 1)
            levels = [
                levels[l]
                + ends[:, 2 * l : 2 * l + 1] * hm[0:1, :]
                + ends[:, 2 * l + 1 : 2 * l + 2] * hm[1:2, :]
                + jnp.concatenate([edge_row * yc[j, l : l + 1, :] for j in range(LANES)], axis=0)
                for l in range(LEV)
            ]
        lanes = [
            jnp.concatenate([levels[l][8 * j : 8 * j + 8, :] for l in range(LEV)], axis=0) for j in range(LANES)
        ]
        coefs = [
            to_coefs(jnp.concatenate(pair, axis=1), table.at[TO_COEFS + 256 * group : TO_COEFS + 256 * (group + 1)])
            for group, pair in enumerate(over_lanes(lanes))
        ]
        kept = [coef * keep for coef, keep in zip(coefs, keeps)]
        backs = [
            from_coefs(coef, table.at[FROM_COEFS + 256 * group : FROM_COEFS + 256 * (group + 1)])
            for group, coef in enumerate(kept)
        ]
        pairs = [(back[:, :RANK], back[:, RANK:]) for back in backs]
        zs = [z.reshape(LEV, 8, RANK) for z in to_lanes(pairs)]
        for l, part in enumerate(pack([jnp.concatenate([z[l] for z in zs], axis=0) for l in range(LEV)])):
            zbuf[q, :, l] = part.reshape(LANES, 8, RANK)

        def edges():
            for j, z in enumerate(zs):
                edge = jnp.where(own_half == 0, z[:, 0, :], z[:, 7, :])
                eb[j] = edge if q == 0 else eb[j] + edge
            if q == 1:
                edge_sends()

        if q == 1:
            pl.when(outward)(edges)
        for d in FAR_FIRST:
            z_copy(q, plus(i, d)).start()
        if q == 1:
            pl.when(jnp.logical_not(outward))(edges)
        else:
            edges()
        zr[q, i] = zbuf[q, i]

    def evaluate(z):
        return from_modes(z, table.at[EVALUATE : EVALUATE + 384], table.at[EVALUATE + 384 : TO_COEFS])

    def project(q, h):
        levels = unpack(
            [jnp.concatenate([zr[q, 2 * f + h, l] for f in range(FIELDS)], axis=0) for l in range(LEV - 1)]
        )
        z = jnp.concatenate(
            [levels[l][8 * f : 8 * f + 8, :] for f in range(FIELDS) for l in range(LEV)], axis=0
        )
        out = evaluate(z)
        return [[out[8 * (LEV * f + l) : 8 * (LEV * f + l + 1), :] for l in range(LEV)] for f in range(FIELDS)]

    def tendency_rows(h, l, at, half):
        lo = jnp.maximum(l - 1, 0)
        hi = jnp.minimum(l + 1, LEV - 1)
        ew = at(PAIRS + l, h)
        nw = at(PAIRS + LEV + l, h)
        mids, along_x, along_y = [], [], []
        for f in range(FIELDS):
            mid = at(f * LEV + l, h)
            mids.append(mid)
            along_x.append(half * (roll(mid, -1, 1) - roll(mid, 1, 1)))
            along_y.append(0.5 * (at(f * LEV + l, h + 1) - at(f * LEV + l, h - 1)))
        linked = (along_x[2], along_y[2], along_x[0] + along_y[1], None)
        out = []
        for f in range(FIELDS):
            mixed = at(f * LEV + lo, h) + at(f * LEV + hi, h) - 2.0 * mids[f]
            t = -(ew * along_x[f] + nw * along_y[f]) + mixing * mixed
            if linked[f] is not None:
                t = t - coupling * linked[f]
            out.append(time_step * t)
        return out

    def full_tendency():
        @pl.loop(0, LEV)
        def _(l):
            for h in (8, 16):
                half = jnp.concatenate([hm[h : h + 8, :]] * 4, axis=1)
                for f, t in enumerate(tendency_rows(h, l, lambda n, r: grid[n, r : r + 8, :], half)):
                    tend[f * LEV + l, h - 8 : h, :] = t

    def side_tendency():
        lane = lax.broadcasted_iota(jnp.int32, (1, 128), 1)
        late = jnp.logical_or(jnp.logical_or(lane == 65, lane == 66), lane == 127)

        def at(n, r):
            return jnp.where(lane < 2, grid[n, r : r + 8, 0:128], grid[n, r : r + 8, 384:512])

        @pl.loop(0, LEV)
        def _(l):
            for h in (8, 16):
                for f, t in enumerate(tendency_rows(h, l, at, hm[h : h + 8, :])):
                    n, rows = f * LEV + l, slice(h - 8, h)
                    tend[n, rows, 0:128] = jnp.where(lane == 0, t, tend[n, rows, 0:128])
                    tend[n, rows, 384:512] = jnp.where(late, t, tend[n, rows, 384:512])

    load_metric.wait()

    @pl.when(polar)
    def _():
        load_forward.wait()
        send_values(0, grid[0:PAIRS, 8:24, :])
        grid[0:PAIRS, 7:8, :] = jnp.zeros((PAIRS, 1, WIDE), F32)
        grid[0:PAIRS, 24:25, :] = jnp.zeros((PAIRS, 1, WIDE), F32)
        full_tendency()
        send_values(1, tend[...])

    edge_rows((REST + 4, REST + 11), slice(PAIRS, PAIRS + 2 * LEV), (8, 23))

    halo_arrival(NEAR, REST, 0).wait_recv()
    lane2 = lax.broadcasted_iota(jnp.int32, (1, 128), 1)
    row16 = lax.broadcasted_iota(jnp.int32, (PAIRS, 1), 0)
    is_v = jnp.logical_and(row16 >= LEV, row16 < 2 * LEV)
    is_temp = jnp.logical_and(row16 >= 2 * LEV, row16 < 3 * LEV)

    def flip(s, minus):
        sign = jnp.where(row16 < 2 * LEV, -1.0, 1.0) * minus
        return jnp.where(over_pole[s], sign, 1.0)

    def row_link(x):
        return jnp.where(is_v, roll(x, -LEV, 0), jnp.where(is_temp, roll(x, LEV, 0), 0.0))

    def wind(buffer, s, w):
        base = REST + 7 * s + 4
        rows = [buffer[base + t // 2, 8 * (t % 2) + LEV * w : 8 * (t % 2) + LEV * (w + 1), :] for t in range(4)]
        return jnp.concatenate([jnp.concatenate(rows, axis=1)] * FIELDS, axis=0)

    def row_of(buffer, start):
        return jnp.concatenate([buffer[start + t] for t in range(4)], axis=1)

    @pl.when(polar)
    def _():
        added = []
        for s, sign in ((0, 0.5 * time_step), (1, -0.5 * time_step)):
            ghost = flip(s, 1.0) * row_of(halo_in, NEAR + 4 * s)
            added.append(sign * (wind(halo_out, s, 1) * ghost + coupling * row_link(ghost)))
            xb[s] = added[s]
        y = to_modes(jnp.concatenate(added, axis=0), table.at[FORWARD:EVALUATE])
        for s in range(2):
            for f in range(FIELDS):
                cb[2 * f + s, 0:LEV, :] = y[(s * FIELDS + f) * LEV : (s * FIELDS + f + 1) * LEV, :]
        ends = []
        for side, sign in ((0, -1.0), (1, 1.0)):
            came = halo_in[SIDES + side]
            along_x = (sign * hm[8:24, :]) * (roll(came, -1, 1) if side == 0 else came)
            mine = jnp.where(
                jnp.logical_and(lane2 >= 2 * PAIRS, lane2 < 2 * (PAIRS + LEV)), halo_out[SIDES + side], 0.0
            )
            ew = sum(roll(mine, 2 * LEV * f - 2 * PAIRS - side, 1) for f in range(FIELDS))
            linked = jnp.where(
                lane2 < 2 * LEV,
                roll(along_x, -4 * LEV, 1),
                jnp.where(
                    jnp.logical_and(lane2 >= 4 * LEV, lane2 < 6 * LEV), roll(along_x, 4 * LEV, 1), 0.0
                ),
            )
            ends.append(time_step * (-ew * along_x - coupling * linked))
        ends = jnp.where(lax.rem(lane2, 2) == 0, ends[0], roll(ends[1], 1, 1))
        for f in range(FIELDS):
            for h in range(2):
                cb[2 * f + h, 8:16, :] = ends[8 * h : 8 * h + 8, :]

        for d in FAR_FIRST:
            c_copy(plus(i, d)).start()

        yc[i] = cb[i]

    from_west = roll(halo_in[SIDES], 126, 1)
    from_east = roll(halo_in[SIDES + 1], COLS - 384, 1)
    both = jnp.where(jnp.logical_and(lane2 >= 66, lane2 < 114), from_east, from_west)[None]
    for width in (2, 4, 8):
        both = jnp.concatenate([both, roll_blocks(both, -width)], axis=0)
    both = jnp.concatenate([both, roll_blocks(both, -16), roll_blocks(both, -32)], axis=0)
    in_halo = jnp.logical_or(jnp.logical_and(lane128 >= 66, lane128 < 68), lane128 >= 126)
    grid[:, 8:24, 384:512] = jnp.where(in_halo, both, grid[:, 8:24, 384:512])
    edge_rows((REST, REST + 7), slice(0, PAIRS), (9, 22))
    for s, near in enumerate((8, 23)):
        halo_out[REST + 7 * s + 6] = grid[0:PAIRS, near, 384:512]
    halo_copy(REST, 7, REST + 7 * slot_n, 1, nb, nl).start()
    halo_copy(REST + 7, 7, REST + 7 * slot_s, 1, sb, sl).start()

    @pl.when(polar)
    def _():
        load_cut.wait()
        load_others.wait()
        own_rows(0)

    @pl.when(jnp.logical_and(polar, b < bands // 2))
    def _():
        own_rows(1)

    halo_arrival(REST, BLOCKS, 1).wait_recv()
    edge_row = (7, 24)
    edge_probe = []
    for s in range(2):
        edge_probe.append(
            jnp.concatenate([halo_in[NEAR + 4 * s + t] for t in range(3)] + [halo_in[REST + 7 * s + 6]], axis=1)
        )
        grid[0:PAIRS, edge_row[s], :] = flip(s, 1.0) * edge_probe[s]

    @pl.when(polar)
    def _():
        for s, row in ((0, 0), (1, 15)):
            tend[:, row, :] = tend[:, row, :] + xb[s]
        side_tendency()

    @pl.when(jnp.logical_not(polar))
    def _():
        full_tendency()

    def edge_weights(s, a):
        return -wind(halo_in, s, 1) * a - coupling * row_link(a)

    for s, inward in ((0, 1.0), (1, -1.0)):
        mid = edge_probe[s]
        half = jnp.concatenate([hm[edge_row[s] : edge_row[s] + 1, :]] * 4, axis=1)
        along_x = half * (roll(mid, -1, 1) - roll(mid, 1, 1))
        turn = jnp.where(over_pole[s], -0.5 * inward, 0.5 * inward)
        along_y = turn * (flip(s, 1.0) * row_of(halo_out, NEAR + 4 * s) - row_of(halo_in, REST + 7 * s))
        linked = jnp.where(row16 < LEV, roll(along_x, -2 * LEV, 0), row_link(along_y))
        linked = linked + jnp.where(is_temp, roll(along_x, 2 * LEV, 0), 0.0)
        up = jnp.where(lax.rem(row16, LEV) == 0, mid, roll(mid, 1, 0))
        down = jnp.where(lax.rem(row16, LEV) == LEV - 1, mid, roll(mid, -1, 0))
        t = -(wind(halo_in, s, 0) * along_x + wind(halo_in, s, 1) * along_y) - coupling * linked
        a = mid + time_step * (t + mixing * (up + down - 2.0 * mid))
        gy[0:PAIRS, edge_row[s], :] = flip(s, -1.0) * edge_weights(s, a)

    @pl.when(jnp.logical_and(polar, b >= bands // 2))
    def _():
        own_rows(1)

    def row_weights(a, nw):
        return (
            -nw * a[0],
            -nw * a[1] - coupling * a[2],
            -nw * a[2] - coupling * a[1],
            -nw * a[3],
        )

    def put_weights(l, h, a):
        for f, weight in enumerate(row_weights(a, grid[PAIRS + LEV + l, h : h + 8, :])):
            gy[f * LEV + l, h : h + 8, :] = weight

    @pl.when(polar)
    def _():
        all_z(0).wait_recv()
        for h in (8, 16):
            taken = project(0, h // 8 - 1)
            for l in range(LEV):
                for f in range(FIELDS):
                    n, rows = f * LEV + l, slice(h - 8, h)
                    adj[n, rows, :] = grid[n, h : h + 8, :] + tend[n, rows, :] - taken[f][l]
        all_z(1).wait_recv()
        for h in (8, 16):
            taken = project(1, h // 8 - 1)
            for l in range(LEV):
                a = []
                for f in range(FIELDS):
                    n, rows = f * LEV + l, slice(h - 8, h)
                    change = tend[n, rows, :] - taken[f][l]
                    tend[n, rows, :] = change
                    tan_out[f, l, rows, :] = (grid[n, h : h + 8, :] + change)[:, :COLS]
                    a.append(adj[n, rows, :] - taken[f][l])
                    adj[n, rows, :] = a[f]
                put_weights(l, h, a)

    @pl.when(jnp.logical_not(polar))
    def _():
        @pl.loop(0, LEV)
        def _(l):
            for h in (8, 16):
                a = []
                for f in range(FIELDS):
                    n, rows = f * LEV + l, slice(h - 8, h)
                    a.append(grid[n, h : h + 8, :] + tend[n, rows, :])
                    tan_out[f, l, rows, :] = a[f][:, :COLS]
                    adj[n, rows, :] = a[f]
                put_weights(l, h, a)

    @pl.loop(0, LEV)
    def _(l):
        lo = jnp.maximum(l - 1, 0)
        hi = jnp.minimum(l + 1, LEV - 1)
        for h in (8, 16):
            rows = slice(h - 8, h)
            half = jnp.concatenate([hm[h : h + 8, :]] * 4, axis=1)
            ew = grid[PAIRS + l, h : h + 8, :]
            a = [adj[f * LEV + l, rows, :] for f in range(FIELDS)]
            col_weights = (
                -ew * a[0] - coupling * a[2],
                -ew * a[1],
                -ew * a[2] - coupling * a[0],
                -ew * a[3],
            )
            for f in range(FIELDS):
                n = f * LEV + l
                back = half * (roll(col_weights[f], 1, 1) - roll(col_weights[f], -1, 1))
                back = back + 0.5 * (gy[n, h - 1 : h + 7, :] - gy[n, h + 1 : h + 9, :])
                back = back + mixing * (adj[f * LEV + lo, rows, :] + adj[f * LEV + hi, rows, :] - 2.0 * a[f])
                diag = grid[n, h : h + 8, :] * (tend[n, rows, :] + time_step * back)
                diag_out[f, l, rows, :] = diag[:, :COLS]

    @pl.when(jnp.logical_and(near_polar, jnp.logical_not(polar)))
    def _():
        load_part.wait()

    for s, wanted in enumerate((above_polar, below_polar)):
        @pl.when(wanted)
        def _():
            row = 15 * s
            north_wind = wind(halo_in, s, 1)
            factor = ((0.5, -0.5)[s] * time_step) * grid[0:PAIRS, 8 + row, :] * flip(s, -1.0)
            before = [diag_out[f, :, row, :] for f in range(FIELDS)]
            remote(bz.at[s], bz.at[s], b_send, b_recv.at[s], nb, nl).wait_recv()
            taken = evaluate(jnp.concatenate([bz[s, f] for f in range(FIELDS)], axis=0))
            more = factor * (north_wind * taken + coupling * row_link(taken))
            for f in range(FIELDS):
                diag_out[f, :, row, :] = before[f] + more[f * LEV : (f + 1) * LEV, :COLS]

    halo_arrival(0, BLOCKS, 0).wait_send()

    @pl.when(polar)
    def _():
        all_c().wait_send()
        for q in range(2):
            all_y(q).wait_send()
            all_z(q).wait_send()

        @pl.when(edge_over)
        def _():
            remote(eb.at[others], eb.at[others], b_send, b_recv.at[0], b, west).wait_send()

        @pl.when(jnp.logical_not(edge_over))
        def _():
            remote(eb, eb, b_send, b_recv.at[0], b, west).wait_send()


def hand_out(tan_in, diag_in, tan_out, diag_out, sem):
    copies = [
        pltpu.make_async_copy(src, dst, sem.at[n])
        for n, (src, dst) in enumerate(((tan_in, tan_out), (diag_in, diag_out)))
    ]
    for copy in copies:
        copy.start()
    for copy in copies:
        copy.wait()


def per_device(bands, row_signs, col_signs, spread, east_wind, north_wind, cutoffs):
    any_spec = pl.BlockSpec(memory_space=pl.ANY)
    out = jax.ShapeDtypeStruct((FIELDS, LEV, ROWS, COLS), F32)
    tables = [jnp.asarray(half_metric(bands)), jnp.asarray(mode_factors())]
    operands = (spread, east_wind, north_wind, row_signs, col_signs, cutoffs, *tables)
    vmem = pltpu.VMEM
    dma = pltpu.SemaphoreType.DMA
    held = pltpu.VMEM(out.shape, F32)
    results = pl.pallas_call(
        functools.partial(kernel, bands),
        out_shape=(held, held),
        in_specs=[any_spec] * 8,
        out_specs=(pl.BlockSpec(memory_space=pltpu.VMEM),) * 2,
        scratch_shapes=[
            vmem((FIELDS, LEV, ROWS, COLS), F32),
            vmem((2, LEV, ROWS, COLS), F32),
            vmem((FIELDS, LEV, ROWS), jnp.int32),
            vmem((FIELDS, LEV, COLS), jnp.int32),
            pltpu.SMEM((ROWS,), jnp.int32),
            vmem((32, 128), F32),
            vmem((TABLE_ROWS, 2 * RANK), BF16),
            vmem((PAIRS + 2 * LEV, 32, WIDE), F32),
            vmem((BLOCKS, 16, 128), F32),
            vmem((BLOCKS, 16, 128), F32),
            vmem((2, LANES, LEV - 1, 8, RANK), F32),
            vmem((2, LANES, LEV - 1, 8, RANK), F32),
            vmem((2, PAIRS, WIDE), F32),
            vmem((LANES, 16, RANK), F32),
            vmem((LANES, 16, RANK), F32),
            vmem((2, LANES, LEV - 1, 8, RANK), F32),
            vmem((2, LANES, LEV - 1, 8, RANK), F32),
            vmem((LANES, LEV, RANK), F32),
            vmem((2, FIELDS, LEV, RANK), F32),
            vmem((PAIRS, ROWS, WIDE), F32),
            vmem((PAIRS, ROWS, WIDE), F32),
            vmem((PAIRS, 32, WIDE), F32),
            dma((8,)),
            dma,
            dma((2,)),
            dma((2,)),
            dma((2,)),
            dma,
            dma,
            dma((2,)),
            dma((2,)),
            dma,
            dma((2,)),
        ],
        compiler_params=pltpu.CompilerParams(
            collective_id=0, has_side_effects=True, vmem_limit_bytes=32 * 2**20
        ),
        cost_estimate=pl.CostEstimate(flops=10**9, bytes_accessed=4 * 10**6, transcendentals=0),
    )(*(pltpu.with_memory_space_constraint(x, pltpu.HBM) for x in operands))
    return pl.pallas_call(
        hand_out,
        out_shape=(out, out),
        in_specs=[any_spec] * 2,
        out_specs=(any_spec, any_spec),
        scratch_shapes=[dma((2,))],
        compiler_params=pltpu.CompilerParams(vmem_limit_bytes=2**20),
    )(*(pltpu.with_memory_space_constraint(x, pltpu.VMEM) for x in results))


def solution(mesh):
    return jax.shard_map(
        functools.partial(per_device, mesh.shape["lat"]),
        mesh=mesh,
        in_specs=(
            P(None, None, "lat"),
            P(None, None, "lon"),
            P(None, None, "lat", "lon"),
            P(None, "lat", "lon"),
            P(None, "lat", "lon"),
            P("lat"),
        ),
        out_specs=(P(None, None, "lat", "lon"), P(None, None, "lat", "lon")),
        check_vma=False,
    )
```

```python
import functools

import jax
import jax.numpy as jnp
import ml_dtypes
import numpy as np
from jax import lax
from jax.experimental import pallas as pl
from jax.experimental.pallas import tpu as pltpu
from jax.sharding import PartitionSpec as P

KTOP = 256
POLAR = 32
RANK = 128
USED = 96
ROWS = 16
COLS = 450
WIDE = 512
LANES = 8
FIELDS = 4
LEV = 4
PAIRS = FIELDS * LEV

time_step = 0.5
coupling = 0.5
mixing = 0.2
metric_cap = 4.0

FORWARD, EVALUATE, TO_COEFS, FROM_COEFS, TABLE_ROWS = 0, 512, 1280, 2304, 3328
NEAR, SIDES, REST, BLOCKS = 0, 8, 10, 24

FAR_FIRST = (6, 2, 5, 3, 7, 1, 4)

MESH = pl.DeviceIdType.MESH
F32 = jnp.float32
BF16 = jnp.bfloat16


def split_table(table):
    high = table.astype(ml_dtypes.bfloat16)
    low = (table - high.astype(np.float64)).astype(ml_dtypes.bfloat16)
    return high, low


def waves_of(group, lane_index):
    place = lane_index % 64
    second = place // 32
    other = (8 - group) if group else 4
    residue = group + second * (other - group)
    return 8 * (place % 32) + residue + (8 * (1 - second) if group == 0 else 0)


@functools.lru_cache(None)
def mode_factors():
    total = COLS * LANES
    size = COLS + 2
    place = np.arange(size, dtype=np.float64)
    width = (KTOP + 0.5) / total
    diag = ((size - 1 - 2 * place) / 2) ** 2 * np.cos(2 * np.pi * width)
    side = place[1:] * (size - place[1:]) / 2
    vectors = np.linalg.eigh(np.diag(diag) + np.diag(side, 1) + np.diag(side, -1))[1]
    basis = np.concatenate([vectors[:, ::-1][:, :USED], np.zeros((size, RANK - USED))], axis=1)
    basis = basis * np.where(basis[size // 2] < 0, -1.0, 1.0)
    weights = []
    for group in range(4):
        waves = waves_of(group, np.arange(64))
        angle = 2 * np.pi / total * ((np.arange(size)[:, None] - 1) * waves[None, :] % total)
        alpha, beta = basis.T @ np.cos(angle), basis.T @ np.sin(angle)
        if group:
            sign = np.where(np.arange(64) < 32, 1.0, -1.0)
            top, low = (alpha, beta), (sign * beta, -sign * alpha)
        else:
            use = np.where(np.arange(64) < 32, 1.0, 0.0)
            top, low = (use * alpha, use * beta), ((1 - use) * alpha, (1 - use) * beta)
        weights.append(np.concatenate([np.concatenate(top, axis=1), np.concatenate(low, axis=1)], axis=0))
    weights = np.round(np.stack(weights) * 2.0**22) / 2.0**22
    wide = np.zeros((RANK, WIDE))
    wide[:, : COLS + 1] = basis[1:].T
    wide[:, WIDE - 1] = basis[0]
    wide = np.round(wide * 2.0**26) / 2.0**26
    wide_h, wide_l = split_table(wide)
    own = np.where(np.arange(WIDE)[:, None] < COLS, 1, 0).astype(ml_dtypes.bfloat16)
    high, low = split_table(weights)
    back = np.concatenate([np.swapaxes(part, 1, 2) for part in (high, low)], axis=1)
    evaluate = np.concatenate([wide_h, wide_l, wide_h], axis=0)
    return np.concatenate(
        [
            np.concatenate([wide_h.T * own, wide_l.T * own], axis=1),
            evaluate[:, : WIDE // 2],
            evaluate[:, WIDE // 2 :],
            np.concatenate([high, low], axis=2).reshape(-1, 2 * RANK),
            back.reshape(-1, 2 * RANK),
        ],
        axis=0,
    )


ROOT = float(np.sqrt(0.5))


def over_lanes(y):
    s = [y[j] + y[j + 4] for j in range(4)]
    d = [y[j] - y[j + 4] for j in range(4)]
    even, odd = s[0] + s[2], s[1] + s[3]
    minus, plus = ROOT * (d[1] - d[3]), ROOT * (d[1] + d[3])
    return [
        (even + odd, even - odd),
        (d[0] + minus, -(d[2] + plus)),
        (s[0] - s[2], s[3] - s[1]),
        (d[0] - minus, d[2] - plus),
    ]


def to_lanes(pairs):
    (y0, y4), (u1, v1), (u2, v2), (u3, v3) = pairs
    even, odd = y0 + y4, y0 - y4
    s = [even + u2, odd - v2, even - u2, odd + v2]
    du, sv = ROOT * (u1 - u3), ROOT * (v1 + v3)
    d = [u1 + u3, du - sv, v3 - v1, -du - sv]
    return [s[j] + d[j] for j in range(4)] + [s[j] - d[j] for j in range(4)]


@functools.lru_cache(None)
def half_metric(bands):
    total = bands * ROWS
    rows = np.clip(np.arange(bands)[:, None] * ROWS - 8 + np.arange(32)[None, :], 0, total - 1)
    metric = np.minimum(1.0 / np.cos(np.pi * ((rows + 0.5) / total - 0.5)), metric_cap)
    table = np.broadcast_to((0.5 * metric).astype(np.float32)[:, :, None], (bands, 32, 128)).copy()
    forward = mode_factors()[FORWARD : FORWARD + WIDE].astype(np.float32)
    for row, col in enumerate((0, COLS - 1)):
        table[:, row] = forward[col, :RANK] + forward[col, RANK:]
    return table


def dot_cols(a, b):
    return lax.dot_general(a, b, (((1,), (0,)), ((), ())), preferred_element_type=F32)


def split(x):
    high = x.astype(BF16)
    return high, (x - high.astype(F32)).astype(BF16)


def to_modes(x, table):
    xh, xl = split(x)
    half = table.shape[1] // 2
    wide = dot_cols(xh, table[...])
    return wide[:, :half] + wide[:, half:] + dot_cols(xl, table[:, 0:half])


def from_modes(z, *tables):
    zh, zl = split(z)
    three = jnp.concatenate([zh, zh, zl], axis=1)
    return jnp.concatenate([dot_cols(three, table[...]) for table in tables], axis=1)


def to_coefs(x, table):
    rows = x.shape[0]
    wide = dot_cols(jnp.concatenate(split(x), axis=0), table[...])
    half = wide.shape[1] // 2
    return wide[:rows, :half] + wide[:rows, half:] + wide[rows:, :half]


def from_coefs(z, table):
    zh, zl = split(z)
    rows = jnp.concatenate([jnp.concatenate([zh, zh], axis=1), jnp.concatenate([zl, jnp.zeros_like(zl)], axis=1)], axis=0)
    wide = dot_cols(rows, table[...])
    return wide[: z.shape[0]] + wide[z.shape[0] :]


def pack(levels):
    lane = lax.broadcasted_iota(jnp.int32, (1, RANK), 1)
    return [jnp.where(lane < USED, levels[l], roll(levels[3], 96 - 32 * l, 1)) for l in range(3)]


def unpack(parts):
    lane = lax.broadcasted_iota(jnp.int32, (1, RANK), 1)
    last = jnp.where(lane < 64, roll(parts[1], 64, 1), roll(parts[2], 96, 1))
    return parts + [jnp.where(lane < 32, roll(parts[0], 32, 1), last)]


def roll(x, shift, axis):
    return pltpu.roll(x, shift % x.shape[axis], axis)


def roll_blocks(x, shift):
    return roll(x.reshape(x.shape[0] * x.shape[1], x.shape[2]), shift, 1).reshape(x.shape)


def fold(x):
    while x.shape[0] > 1:
        half = x.shape[0] // 2
        x = x[:half] + roll_blocks(x[half:], 2 * half)
    return x


def kernel(
    bands, spread, east, north, rs, cs, cut, metric, table_in, tan_out, diag_out,
    spread_v, winds_v, rs_v, cs_v, cut_s, hm, table,
    grid, halo_out, halo_in, ybuf, yr, xb, cb, yc, zbuf, zr, eb, bz,
    tend, adj, gy,
    in_sem, halo_send, halo_recv, y_send, y_recv, c_send, c_recv, z_send, z_recv, b_send, b_recv,
):
    b = lax.axis_index("lat")
    i = lax.axis_index("lon")
    caps = POLAR // ROWS
    is_north = b == 0
    is_south = b == bands - 1
    polar = jnp.logical_or(b < caps, b >= bands - caps)
    above_polar = jnp.logical_or(b <= caps, is_south)
    below_polar = jnp.logical_or(b >= bands - caps - 1, is_north)
    near_polar = jnp.logical_or(above_polar, below_polar)
    across = lax.rem(i + LANES // 2, LANES)
    west = lax.rem(i + LANES - 1, LANES)
    east_lane = lax.rem(i + 1, LANES)
    nb = jnp.where(is_north, 0, b - 1)
    nl = jnp.where(is_north, across, i)
    sb = jnp.where(is_south, bands - 1, b + 1)
    sl = jnp.where(is_south, across, i)
    slot_n = jnp.where(is_north, 0, 1)
    slot_s = jnp.where(is_south, 1, 0)
    own_half = lax.rem(i, 2)
    edge_over = jnp.where(own_half == 0, is_north, is_south)
    over_pole = (is_north, is_south)
    outward = jnp.logical_or(
        jnp.logical_and(b == caps - 1, own_half == 1), jnp.logical_and(b == bands - caps, own_half == 0)
    )

    def plus(lane, d):
        return lax.rem(lane + d, LANES)

    load_spread = pltpu.make_async_copy(spread, spread_v, in_sem.at[0])
    load_rows = pltpu.make_async_copy(rs, rs_v, in_sem.at[1])
    load_cols = pltpu.make_async_copy(cs, cs_v, in_sem.at[2])
    load_metric = pltpu.make_async_copy(metric.at[b], hm, in_sem.at[4])
    load_cut = pltpu.make_async_copy(cut, cut_s, in_sem.at[5])

    def load_table(start, stop, sem):
        return pltpu.make_async_copy(table_in.at[start:stop], table.at[start:stop], in_sem.at[sem])

    load_forward = load_table(FORWARD, EVALUATE, 6)
    load_others = load_table(EVALUATE, TABLE_ROWS, 7)
    load_part = load_table(EVALUATE, TO_COEFS, 7)
    barrier = pltpu.get_barrier_semaphore()

    def greet(lat, lon):
        pl.semaphore_signal(barrier, inc=1, device_id=(lat, lon), device_id_type=MESH)

    greet(nb, nl)
    greet(sb, sl)

    @pl.when(polar)
    def _():
        for d in FAR_FIRST[:4]:
            greet(b, plus(i, d))

    greet(b, west)
    greet(b, east_lane)
    load_spread.start()
    load_rows.start()
    load_cols.start()
    pltpu.make_async_copy(east, winds_v.at[0], in_sem.at[3]).start()
    pltpu.make_async_copy(north, winds_v.at[1], in_sem.at[3]).start()
    load_metric.start()

    @pl.when(polar)
    def _():
        greet(b, across)
        load_forward.start()
        load_cut.start()

    @pl.when(jnp.logical_and(near_polar, jnp.logical_not(polar)))
    def _():
        load_part.start()

    load_rows.wait()
    load_cols.wait()
    load_spread.wait()
    grid[:, 8:24, 384:512] = jnp.zeros((PAIRS + 2 * LEV, ROWS, 128), F32)
    row_part = jnp.concatenate([rs_v[f] for f in range(FIELDS)], axis=0)
    row_part = (2 * row_part - 1).astype(F32).T
    for f in range(FIELDS):
        col_part = (2 * cs_v[f] - 1).astype(F32)
        for l in range(LEV):
            n = f * LEV + l
            grid[n, 8:24, 0:COLS] = spread_v[f, l] * (row_part[:, n : n + 1] * col_part[l : l + 1, :])

    @pl.when(polar)
    def _():
        load_others.start()

    pltpu.make_async_copy(winds_v, winds_v, in_sem.at[3]).wait()
    for w in range(2):
        for l in range(LEV):
            grid[PAIRS + w * LEV + l, 8:24, 0:COLS] = winds_v[w, l]

    def edge_rows(start, entries, rows):
        for s, row in enumerate(rows):
            for t in range(4):
                values = grid[entries, row, 128 * t : 128 * t + 128]
                if entries == slice(0, PAIRS):
                    halo_out[start[s] + t] = values
                else:
                    halo_out[start[s] + t // 2, 8 * (t % 2) : 8 * (t % 2) + 8, :] = values

    edge_rows((NEAR, NEAR + 4), slice(0, PAIRS), (8, 23))
    lane128 = lax.broadcasted_iota(jnp.int32, (1, 1, 128), 2)
    for s, (start, shift) in enumerate(((0, 0), (384, COLS - 2 - 384))):
        tile = grid[:, 8:24, start : start + 128]
        tile = jnp.where(jnp.logical_and(lane128 >= shift, lane128 < shift + 2), tile, 0.0)
        packed = fold(tile[:PAIRS]) + roll_blocks(fold(tile[PAIRS:]), 2 * PAIRS)
        halo_out[SIDES + s] = roll_blocks(packed, -shift)[0]

    pl.semaphore_wait(barrier, 4 + jnp.where(polar, LANES - 3, 0))

    def remote(src, dst, send, recv, lat, lon):
        return pltpu.make_async_remote_copy(
            src_ref=src, dst_ref=dst, send_sem=send, recv_sem=recv, device_id=(lat, lon), device_id_type=MESH
        )

    def halo_copy(start, count, to, which, lat, lon):
        return remote(
            halo_out.at[start : start + count], halo_in.at[pl.ds(to, count)], halo_send, halo_recv.at[which], lat, lon
        )

    def halo_arrival(start, stop, which):
        return remote(
            halo_out.at[start:stop], halo_in.at[start:stop], halo_send, halo_recv.at[which], b, west
        )

    @pl.when(b < bands // 2)
    def _():
        halo_copy(NEAR, 4, NEAR + 4 * slot_n, 0, nb, nl).start()

    halo_copy(NEAR + 4, 4, NEAR + 4 * slot_s, 0, sb, sl).start()

    @pl.when(b >= bands // 2)
    def _():
        halo_copy(NEAR, 4, NEAR + 4 * slot_n, 0, nb, nl).start()

    halo_copy(SIDES, 1, SIDES + 1, 0, b, west).start()
    halo_copy(SIDES + 1, 1, SIDES, 0, b, east_lane).start()

    others = pl.ds(0, LANES - 1)

    def all_y(q):
        return remote(ybuf.at[q, others], yr.at[q, others], y_send.at[q], y_recv.at[q], b, west)

    def send_values(q, x):
        y = to_modes(x.reshape(PAIRS * ROWS, WIDE), table.at[FORWARD:EVALUATE])
        y = y.reshape(FIELDS, LEV, 2, 8, RANK)
        blocks = [
            jnp.concatenate([y[f, l, h] for f in range(FIELDS) for h in range(2)], axis=0) for l in range(LEV)
        ]
        for l, part in enumerate(pack(blocks)):
            ybuf[q, :, l] = part.reshape(LANES, 8, RANK)

        for d in FAR_FIRST:
            o = plus(i, d)
            remote(ybuf.at[q, o], yr.at[q, i], y_send.at[q], y_recv.at[q], b, o).start()

        yr[q, i] = ybuf[q, i]

    def c_copy(o):
        return remote(cb.at[o], yc.at[i], c_send, c_recv, b, o)

    def all_c():
        return remote(cb.at[others], yc.at[others], c_send, c_recv, b, west)

    def z_copy(q, j):
        return remote(zbuf.at[q, j], zr.at[q, i], z_send.at[q], z_recv.at[q], b, j)

    def all_z(q):
        return remote(zbuf.at[q, others], zr.at[q, others], z_send.at[q], z_recv.at[q], b, west)

    def edge_sends():
        slot = jnp.where(own_half == 0, slot_n, slot_s)
        lat = jnp.where(own_half == 0, nb, sb)

        @pl.loop(0, LANES)
        def _(d):
            j = plus(i, d)
            lon = jnp.where(edge_over, plus(j, LANES // 2), j)
            here = jnp.logical_and(edge_over, lon == i)

            @pl.when(jnp.logical_not(here))
            def _():
                remote(eb.at[j], bz.at[slot, i // 2], b_send, b_recv.at[slot], lat, lon).start()

            @pl.when(here)
            def _():
                pltpu.make_async_copy(eb.at[j], bz.at[slot, i // 2], b_recv.at[slot]).start()

    def own_rows(q):
        row = lax.broadcasted_iota(jnp.int32, (8, 128), 0)
        cutoff = jnp.zeros((8, 128), jnp.int32)
        for r in range(8):
            cutoff = jnp.where(row == r, cut_s[8 * own_half + r], cutoff)
        keeps = []
        for group in range(4):
            wave = waves_of(group, lax.broadcasted_iota(jnp.int32, (8, 128), 1))
            keep = jnp.where(wave > cutoff, 2.0 / (COLS * LANES), 0.0)
            keeps.append(jnp.concatenate([keep] * LEV, axis=0))
        all_y(q).wait_recv()
        levels = unpack([yr[q, :, l].reshape(LANES * 8, RANK) for l in range(LEV - 1)])
        if q == 1:
            edge_row = jnp.where(row == 7 * own_half, 1.0, 0.0)
            all_c().wait_recv()
            ends = jnp.concatenate([yc[j, 8:16, :] for j in range(LANES)], axis=0)
            ends = pltpu.roll(ends, lax.rem(128 - 2 * LEV * (i // 2), 128), 1)
            levels = [
                levels[l]
                + ends[:, 2 * l : 2 * l + 1] * hm[0:1, :]
                + ends[:, 2 * l + 1 : 2 * l + 2] * hm[1:2, :]
                + jnp.concatenate([edge_row * yc[j, l : l + 1, :] for j in range(LANES)], axis=0)
                for l in range(LEV)
            ]
        lanes = [
            jnp.concatenate([levels[l][8 * j : 8 * j + 8, :] for l in range(LEV)], axis=0) for j in range(LANES)
        ]
        coefs = [
            to_coefs(jnp.concatenate(pair, axis=1), table.at[TO_COEFS + 256 * group : TO_COEFS + 256 * (group + 1)])
            for group, pair in enumerate(over_lanes(lanes))
        ]
        kept = [coef * keep for coef, keep in zip(coefs, keeps)]
        backs = [
            from_coefs(coef, table.at[FROM_COEFS + 256 * group : FROM_COEFS + 256 * (group + 1)])
            for group, coef in enumerate(kept)
        ]
        pairs = [(back[:, :RANK], back[:, RANK:]) for back in backs]
        zs = [z.reshape(LEV, 8, RANK) for z in to_lanes(pairs)]
        for l, part in enumerate(pack([jnp.concatenate([z[l] for z in zs], axis=0) for l in range(LEV)])):
            zbuf[q, :, l] = part.reshape(LANES, 8, RANK)

        def edges():
            for j, z in enumerate(zs):
                edge = jnp.where(own_half == 0, z[:, 0, :], z[:, 7, :])
                eb[j] = edge if q == 0 else eb[j] + edge
            if q == 1:
                edge_sends()

        if q == 1:
            pl.when(outward)(edges)
        for d in FAR_FIRST:
            z_copy(q, plus(i, d)).start()
        if q == 1:
            pl.when(jnp.logical_not(outward))(edges)
        else:
            edges()
        zr[q, i] = zbuf[q, i]

    def evaluate(z):
        return from_modes(z, table.at[EVALUATE : EVALUATE + 384], table.at[EVALUATE + 384 : TO_COEFS])

    def project(q, h):
        levels = unpack(
            [jnp.concatenate([zr[q, 2 * f + h, l] for f in range(FIELDS)], axis=0) for l in range(LEV - 1)]
        )
        z = jnp.concatenate(
            [levels[l][8 * f : 8 * f + 8, :] for f in range(FIELDS) for l in range(LEV)], axis=0
        )
        out = evaluate(z)
        return [[out[8 * (LEV * f + l) : 8 * (LEV * f + l + 1), :] for l in range(LEV)] for f in range(FIELDS)]

    def tendency_rows(h, l, at, half):
        lo = jnp.maximum(l - 1, 0)
        hi = jnp.minimum(l + 1, LEV - 1)
        ew = at(PAIRS + l, h)
        nw = at(PAIRS + LEV + l, h)
        mids, along_x, along_y = [], [], []
        for f in range(FIELDS):
            mid = at(f * LEV + l, h)
            mids.append(mid)
            along_x.append(half * (roll(mid, -1, 1) - roll(mid, 1, 1)))
            along_y.append(0.5 * (at(f * LEV + l, h + 1) - at(f * LEV + l, h - 1)))
        linked = (along_x[2], along_y[2], along_x[0] + along_y[1], None)
        out = []
        for f in range(FIELDS):
            mixed = at(f * LEV + lo, h) + at(f * LEV + hi, h) - 2.0 * mids[f]
            t = -(ew * along_x[f] + nw * along_y[f]) + mixing * mixed
            if linked[f] is not None:
                t = t - coupling * linked[f]
            out.append(time_step * t)
        return out

    def full_tendency():
        @pl.loop(0, LEV, unroll=True)
        def _(l):
            for h in (8, 16):
                half = jnp.concatenate([hm[h : h + 8, :]] * 4, axis=1)
                for f, t in enumerate(tendency_rows(h, l, lambda n, r: grid[n, r : r + 8, :], half)):
                    tend[f * LEV + l, h - 8 : h, :] = t

    def side_tendency():
        lane = lax.broadcasted_iota(jnp.int32, (1, 128), 1)
        late = jnp.logical_or(jnp.logical_or(lane == 65, lane == 66), lane == 127)

        def at(n, r):
            return jnp.where(lane < 2, grid[n, r : r + 8, 0:128], grid[n, r : r + 8, 384:512])

        @pl.loop(0, LEV, unroll=True)
        def _(l):
            for h in (8, 16):
                for f, t in enumerate(tendency_rows(h, l, at, hm[h : h + 8, :])):
                    n, rows = f * LEV + l, slice(h - 8, h)
                    tend[n, rows, 0:128] = jnp.where(lane == 0, t, tend[n, rows, 0:128])
                    tend[n, rows, 384:512] = jnp.where(late, t, tend[n, rows, 384:512])

    load_metric.wait()

    @pl.when(polar)
    def _():
        load_forward.wait()
        send_values(0, grid[0:PAIRS, 8:24, :])
        grid[0:PAIRS, 7:8, :] = jnp.zeros((PAIRS, 1, WIDE), F32)
        grid[0:PAIRS, 24:25, :] = jnp.zeros((PAIRS, 1, WIDE), F32)
        full_tendency()
        send_values(1, tend[...])

    edge_rows((REST + 4, REST + 11), slice(PAIRS, PAIRS + 2 * LEV), (8, 23))

    halo_arrival(NEAR, REST, 0).wait_recv()
    lane2 = lax.broadcasted_iota(jnp.int32, (1, 128), 1)
    row16 = lax.broadcasted_iota(jnp.int32, (PAIRS, 1), 0)
    is_v = jnp.logical_and(row16 >= LEV, row16 < 2 * LEV)
    is_temp = jnp.logical_and(row16 >= 2 * LEV, row16 < 3 * LEV)

    def flip(s, minus):
        sign = jnp.where(row16 < 2 * LEV, -1.0, 1.0) * minus
        return jnp.where(over_pole[s], sign, 1.0)

    def row_link(x):
        return jnp.where(is_v, roll(x, -LEV, 0), jnp.where(is_temp, roll(x, LEV, 0), 0.0))

    def wind(buffer, s, w):
        base = REST + 7 * s + 4
        rows = [buffer[base + t // 2, 8 * (t % 2) + LEV * w : 8 * (t % 2) + LEV * (w + 1), :] for t in range(4)]
        return jnp.concatenate([jnp.concatenate(rows, axis=1)] * FIELDS, axis=0)

    def row_of(buffer, start):
        return jnp.concatenate([buffer[start + t] for t in range(4)], axis=1)

    @pl.when(polar)
    def _():
        added = []
        for s, sign in ((0, 0.5 * time_step), (1, -0.5 * time_step)):
            ghost = flip(s, 1.0) * row_of(halo_in, NEAR + 4 * s)
            added.append(sign * (wind(halo_out, s, 1) * ghost + coupling * row_link(ghost)))
            xb[s] = added[s]
        y = to_modes(jnp.concatenate(added, axis=0), table.at[FORWARD:EVALUATE])
        for s in range(2):
            for f in range(FIELDS):
                cb[2 * f + s, 0:LEV, :] = y[(s * FIELDS + f) * LEV : (s * FIELDS + f + 1) * LEV, :]
        ends = []
        for side, sign in ((0, -1.0), (1, 1.0)):
            came = halo_in[SIDES + side]
            along_x = (sign * hm[8:24, :]) * (roll(came, -1, 1) if side == 0 else came)
            mine = jnp.where(
                jnp.logical_and(lane2 >= 2 * PAIRS, lane2 < 2 * (PAIRS + LEV)), halo_out[SIDES + side], 0.0
            )
            ew = sum(roll(mine, 2 * LEV * f - 2 * PAIRS - side, 1) for f in range(FIELDS))
            linked = jnp.where(
                lane2 < 2 * LEV,
                roll(along_x, -4 * LEV, 1),
                jnp.where(
                    jnp.logical_and(lane2 >= 4 * LEV, lane2 < 6 * LEV), roll(along_x, 4 * LEV, 1), 0.0
                ),
            )
            ends.append(time_step * (-ew * along_x - coupling * linked))
        ends = jnp.where(lax.rem(lane2, 2) == 0, ends[0], roll(ends[1], 1, 1))
        for f in range(FIELDS):
            for h in range(2):
                cb[2 * f + h, 8:16, :] = ends[8 * h : 8 * h + 8, :]

        for d in FAR_FIRST:
            c_copy(plus(i, d)).start()

        yc[i] = cb[i]

    from_west = roll(halo_in[SIDES], 126, 1)
    from_east = roll(halo_in[SIDES + 1], COLS - 384, 1)
    both = jnp.where(jnp.logical_and(lane2 >= 66, lane2 < 114), from_east, from_west)[None]
    for width in (2, 4, 8):
        both = jnp.concatenate([both, roll_blocks(both, -width)], axis=0)
    both = jnp.concatenate([both, roll_blocks(both, -16), roll_blocks(both, -32)], axis=0)
    in_halo = jnp.logical_or(jnp.logical_and(lane128 >= 66, lane128 < 68), lane128 >= 126)
    grid[:, 8:24, 384:512] = jnp.where(in_halo, both, grid[:, 8:24, 384:512])
    edge_rows((REST, REST + 7), slice(0, PAIRS), (9, 22))
    for s, near in enumerate((8, 23)):
        halo_out[REST + 7 * s + 6] = grid[0:PAIRS, near, 384:512]
    halo_copy(REST, 7, REST + 7 * slot_n, 1, nb, nl).start()
    halo_copy(REST + 7, 7, REST + 7 * slot_s, 1, sb, sl).start()

    @pl.when(polar)
    def _():
        load_cut.wait()
        load_others.wait()
        own_rows(0)

    @pl.when(jnp.logical_and(polar, b < bands // 2))
    def _():
        own_rows(1)

    halo_arrival(REST, BLOCKS, 1).wait_recv()
    edge_row = (7, 24)
    edge_probe = []
    for s in range(2):
        edge_probe.append(
            jnp.concatenate([halo_in[NEAR + 4 * s + t] for t in range(3)] + [halo_in[REST + 7 * s + 6]], axis=1)
        )
        grid[0:PAIRS, edge_row[s], :] = flip(s, 1.0) * edge_probe[s]

    @pl.when(polar)
    def _():
        for s, row in ((0, 0), (1, 15)):
            tend[:, row, :] = tend[:, row, :] + xb[s]
        side_tendency()

    @pl.when(jnp.logical_not(polar))
    def _():
        full_tendency()

    def edge_weights(s, a):
        return -wind(halo_in, s, 1) * a - coupling * row_link(a)

    for s, inward in ((0, 1.0), (1, -1.0)):
        mid = edge_probe[s]
        half = jnp.concatenate([hm[edge_row[s] : edge_row[s] + 1, :]] * 4, axis=1)
        along_x = half * (roll(mid, -1, 1) - roll(mid, 1, 1))
        turn = jnp.where(over_pole[s], -0.5 * inward, 0.5 * inward)
        along_y = turn * (flip(s, 1.0) * row_of(halo_out, NEAR + 4 * s) - row_of(halo_in, REST + 7 * s))
        linked = jnp.where(row16 < LEV, roll(along_x, -2 * LEV, 0), row_link(along_y))
        linked = linked + jnp.where(is_temp, roll(along_x, 2 * LEV, 0), 0.0)
        up = jnp.where(lax.rem(row16, LEV) == 0, mid, roll(mid, 1, 0))
        down = jnp.where(lax.rem(row16, LEV) == LEV - 1, mid, roll(mid, -1, 0))
        t = -(wind(halo_in, s, 0) * along_x + wind(halo_in, s, 1) * along_y) - coupling * linked
        a = mid + time_step * (t + mixing * (up + down - 2.0 * mid))
        gy[0:PAIRS, edge_row[s], :] = flip(s, -1.0) * edge_weights(s, a)

    @pl.when(jnp.logical_and(polar, b >= bands // 2))
    def _():
        own_rows(1)

    def row_weights(a, nw):
        return (
            -nw * a[0],
            -nw * a[1] - coupling * a[2],
            -nw * a[2] - coupling * a[1],
            -nw * a[3],
        )

    def put_weights(l, h, a):
        for f, weight in enumerate(row_weights(a, grid[PAIRS + LEV + l, h : h + 8, :])):
            gy[f * LEV + l, h : h + 8, :] = weight

    @pl.when(polar)
    def _():
        all_z(0).wait_recv()
        for h in (8, 16):
            taken = project(0, h // 8 - 1)
            for l in range(LEV):
                for f in range(FIELDS):
                    n, rows = f * LEV + l, slice(h - 8, h)
                    adj[n, rows, :] = grid[n, h : h + 8, :] + tend[n, rows, :] - taken[f][l]
        all_z(1).wait_recv()
        for h in (8, 16):
            taken = project(1, h // 8 - 1)
            for l in range(LEV):
                a = []
                for f in range(FIELDS):
                    n, rows = f * LEV + l, slice(h - 8, h)
                    change = tend[n, rows, :] - taken[f][l]
                    tend[n, rows, :] = change
                    tan_out[f, l, rows, :] = (grid[n, h : h + 8, :] + change)[:, :COLS]
                    a.append(adj[n, rows, :] - taken[f][l])
                    adj[n, rows, :] = a[f]
                put_weights(l, h, a)

    @pl.when(jnp.logical_not(polar))
    def _():
        @pl.loop(0, LEV, unroll=True)
        def _(l):
            for h in (8, 16):
                a = []
                for f in range(FIELDS):
                    n, rows = f * LEV + l, slice(h - 8, h)
                    a.append(grid[n, h : h + 8, :] + tend[n, rows, :])
                    tan_out[f, l, rows, :] = a[f][:, :COLS]
                    adj[n, rows, :] = a[f]
                put_weights(l, h, a)

    @pl.loop(0, LEV, unroll=True)
    def _(l):
        lo = jnp.maximum(l - 1, 0)
        hi = jnp.minimum(l + 1, LEV - 1)
        for h in (8, 16):
            rows = slice(h - 8, h)
            half = jnp.concatenate([hm[h : h + 8, :]] * 4, axis=1)
            ew = grid[PAIRS + l, h : h + 8, :]
            a = [adj[f * LEV + l, rows, :] for f in range(FIELDS)]
            col_weights = (
                -ew * a[0] - coupling * a[2],
                -ew * a[1],
                -ew * a[2] - coupling * a[0],
                -ew * a[3],
            )
            for f in range(FIELDS):
                n = f * LEV + l
                back = half * (roll(col_weights[f], 1, 1) - roll(col_weights[f], -1, 1))
                back = back + 0.5 * (gy[n, h - 1 : h + 7, :] - gy[n, h + 1 : h + 9, :])
                back = back + mixing * (adj[f * LEV + lo, rows, :] + adj[f * LEV + hi, rows, :] - 2.0 * a[f])
                diag = grid[n, h : h + 8, :] * (tend[n, rows, :] + time_step * back)
                diag_out[f, l, rows, :] = diag[:, :COLS]

    @pl.when(jnp.logical_and(near_polar, jnp.logical_not(polar)))
    def _():
        load_part.wait()

    for s, wanted in enumerate((above_polar, below_polar)):
        @pl.when(wanted)
        def _():
            row = 15 * s
            north_wind = wind(halo_in, s, 1)
            factor = ((0.5, -0.5)[s] * time_step) * grid[0:PAIRS, 8 + row, :] * flip(s, -1.0)
            before = [diag_out[f, :, row, :] for f in range(FIELDS)]
            remote(bz.at[s], bz.at[s], b_send, b_recv.at[s], nb, nl).wait_recv()
            taken = evaluate(jnp.concatenate([bz[s, f] for f in range(FIELDS)], axis=0))
            more = factor * (north_wind * taken + coupling * row_link(taken))
            for f in range(FIELDS):
                diag_out[f, :, row, :] = before[f] + more[f * LEV : (f + 1) * LEV, :COLS]

    halo_arrival(0, BLOCKS, 0).wait_send()

    @pl.when(polar)
    def _():
        all_c().wait_send()
        for q in range(2):
            all_y(q).wait_send()
            all_z(q).wait_send()

        @pl.when(edge_over)
        def _():
            remote(eb.at[others], eb.at[others], b_send, b_recv.at[0], b, west).wait_send()

        @pl.when(jnp.logical_not(edge_over))
        def _():
            remote(eb, eb, b_send, b_recv.at[0], b, west).wait_send()


def hand_out(tan_in, diag_in, tan_out, diag_out, sem):
    copies = [
        pltpu.make_async_copy(src, dst, sem.at[n])
        for n, (src, dst) in enumerate(((tan_in, tan_out), (diag_in, diag_out)))
    ]
    for copy in copies:
        copy.start()
    for copy in copies:
        copy.wait()


def per_device(bands, row_signs, col_signs, spread, east_wind, north_wind, cutoffs):
    any_spec = pl.BlockSpec(memory_space=pl.ANY)
    out = jax.ShapeDtypeStruct((FIELDS, LEV, ROWS, COLS), F32)
    tables = [jnp.asarray(half_metric(bands)), jnp.asarray(mode_factors())]
    operands = (spread, east_wind, north_wind, row_signs, col_signs, cutoffs, *tables)
    vmem = pltpu.VMEM
    dma = pltpu.SemaphoreType.DMA
    held = pltpu.VMEM(out.shape, F32)
    results = pl.pallas_call(
        functools.partial(kernel, bands),
        out_shape=(held, held),
        in_specs=[any_spec] * 8,
        out_specs=(pl.BlockSpec(memory_space=pltpu.VMEM),) * 2,
        scratch_shapes=[
            vmem((FIELDS, LEV, ROWS, COLS), F32),
            vmem((2, LEV, ROWS, COLS), F32),
            vmem((FIELDS, LEV, ROWS), jnp.int32),
            vmem((FIELDS, LEV, COLS), jnp.int32),
            pltpu.SMEM((ROWS,), jnp.int32),
            vmem((32, 128), F32),
            vmem((TABLE_ROWS, 2 * RANK), BF16),
            vmem((PAIRS + 2 * LEV, 32, WIDE), F32),
            vmem((BLOCKS, 16, 128), F32),
            vmem((BLOCKS, 16, 128), F32),
            vmem((2, LANES, LEV - 1, 8, RANK), F32),
            vmem((2, LANES, LEV - 1, 8, RANK), F32),
            vmem((2, PAIRS, WIDE), F32),
            vmem((LANES, 16, RANK), F32),
            vmem((LANES, 16, RANK), F32),
            vmem((2, LANES, LEV - 1, 8, RANK), F32),
            vmem((2, LANES, LEV - 1, 8, RANK), F32),
            vmem((LANES, LEV, RANK), F32),
            vmem((2, FIELDS, LEV, RANK), F32),
            vmem((PAIRS, ROWS, WIDE), F32),
            vmem((PAIRS, ROWS, WIDE), F32),
            vmem((PAIRS, 32, WIDE), F32),
            dma((8,)),
            dma,
            dma((2,)),
            dma((2,)),
            dma((2,)),
            dma,
            dma,
            dma((2,)),
            dma((2,)),
            dma,
            dma((2,)),
        ],
        compiler_params=pltpu.CompilerParams(
            collective_id=0, has_side_effects=True, vmem_limit_bytes=32 * 2**20
        ),
        cost_estimate=pl.CostEstimate(flops=10**9, bytes_accessed=4 * 10**6, transcendentals=0),
    )(*(pltpu.with_memory_space_constraint(x, pltpu.HBM) for x in operands))
    return pl.pallas_call(
        hand_out,
        out_shape=(out, out),
        in_specs=[any_spec] * 2,
        out_specs=(any_spec, any_spec),
        scratch_shapes=[dma((2,))],
        compiler_params=pltpu.CompilerParams(vmem_limit_bytes=2**20),
    )(*(pltpu.with_memory_space_constraint(x, pltpu.VMEM) for x in results))


def solution(mesh):
    return jax.shard_map(
        functools.partial(per_device, mesh.shape["lat"]),
        mesh=mesh,
        in_specs=(
            P(None, None, "lat"),
            P(None, None, "lon"),
            P(None, None, "lat", "lon"),
            P(None, "lat", "lon"),
            P(None, "lat", "lon"),
            P("lat"),
        ),
        out_specs=(P(None, None, "lat", "lon"), P(None, None, "lat", "lon")),
        check_vma=False,
    )
```

```python
import functools

import jax
import jax.numpy as jnp
import ml_dtypes
import numpy as np
from jax import lax
from jax.experimental import pallas as pl
from jax.experimental.pallas import tpu as pltpu
from jax.sharding import PartitionSpec as P

KTOP = 256
POLAR = 32
RANK = 128
USED = 96
ROWS = 16
COLS = 450
WIDE = 512
LANES = 8
FIELDS = 4
LEV = 4
PAIRS = FIELDS * LEV

time_step = 0.5
coupling = 0.5
mixing = 0.2
metric_cap = 4.0

FORWARD, EVALUATE, TO_COEFS, FROM_COEFS, TABLE_ROWS = 0, 512, 1280, 2304, 3328
NEAR, SIDES, REST, BLOCKS = 0, 8, 10, 24

FAR_FIRST = (6, 2, 5, 3, 7, 1, 4)
ANSWERS = (0, 4, 1, 3, 2, 7, 5, 6)

MESH = pl.DeviceIdType.MESH
F32 = jnp.float32
BF16 = jnp.bfloat16


def split_table(table):
    high = table.astype(ml_dtypes.bfloat16)
    low = (table - high.astype(np.float64)).astype(ml_dtypes.bfloat16)
    return high, low


def waves_of(group, lane_index):
    place = lane_index % 64
    second = place // 32
    other = (8 - group) if group else 4
    residue = group + second * (other - group)
    return 8 * (place % 32) + residue + (8 * (1 - second) if group == 0 else 0)


@functools.lru_cache(None)
def mode_factors():
    total = COLS * LANES
    size = COLS + 2
    place = np.arange(size, dtype=np.float64)
    width = (KTOP + 0.5) / total
    diag = ((size - 1 - 2 * place) / 2) ** 2 * np.cos(2 * np.pi * width)
    side = place[1:] * (size - place[1:]) / 2
    vectors = np.linalg.eigh(np.diag(diag) + np.diag(side, 1) + np.diag(side, -1))[1]
    basis = np.concatenate([vectors[:, ::-1][:, :USED], np.zeros((size, RANK - USED))], axis=1)
    basis = basis * np.where(basis[size // 2] < 0, -1.0, 1.0)
    weights = []
    for group in range(4):
        waves = waves_of(group, np.arange(64))
        angle = 2 * np.pi / total * ((np.arange(size)[:, None] - 1) * waves[None, :] % total)
        alpha, beta = basis.T @ np.cos(angle), basis.T @ np.sin(angle)
        if group:
            sign = np.where(np.arange(64) < 32, 1.0, -1.0)
            top, low = (alpha, beta), (sign * beta, -sign * alpha)
        else:
            use = np.where(np.arange(64) < 32, 1.0, 0.0)
            top, low = (use * alpha, use * beta), ((1 - use) * alpha, (1 - use) * beta)
        weights.append(np.concatenate([np.concatenate(top, axis=1), np.concatenate(low, axis=1)], axis=0))
    weights = np.round(np.stack(weights) * 2.0**22) / 2.0**22
    wide = np.zeros((RANK, WIDE))
    wide[:, : COLS + 1] = basis[1:].T
    wide[:, WIDE - 1] = basis[0]
    wide = np.round(wide * 2.0**26) / 2.0**26
    wide_h, wide_l = split_table(wide)
    own = np.where(np.arange(WIDE)[:, None] < COLS, 1, 0).astype(ml_dtypes.bfloat16)
    high, low = split_table(weights)
    back = np.concatenate([np.swapaxes(part, 1, 2) for part in (high, low)], axis=1)
    evaluate = np.concatenate([wide_h, wide_l, wide_h], axis=0)
    return np.concatenate(
        [
            np.concatenate([wide_h.T * own, wide_l.T * own], axis=1),
            evaluate[:, : WIDE // 2],
            evaluate[:, WIDE // 2 :],
            np.concatenate([high, low], axis=2).reshape(-1, 2 * RANK),
            back.reshape(-1, 2 * RANK),
        ],
        axis=0,
    )


ROOT = float(np.sqrt(0.5))


def over_lanes(y):
    s = [y[j] + y[j + 4] for j in range(4)]
    d = [y[j] - y[j + 4] for j in range(4)]
    even, odd = s[0] + s[2], s[1] + s[3]
    minus, plus = ROOT * (d[1] - d[3]), ROOT * (d[1] + d[3])
    return [
        (even + odd, even - odd),
        (d[0] + minus, -(d[2] + plus)),
        (s[0] - s[2], s[3] - s[1]),
        (d[0] - minus, d[2] - plus),
    ]


def to_lanes(pairs):
    (y0, y4), (u1, v1), (u2, v2), (u3, v3) = pairs
    even, odd = y0 + y4, y0 - y4
    s = [even + u2, odd - v2, even - u2, odd + v2]
    du, sv = ROOT * (u1 - u3), ROOT * (v1 + v3)
    d = [u1 + u3, du - sv, v3 - v1, -du - sv]
    return [s[j] + d[j] for j in range(4)] + [s[j] - d[j] for j in range(4)]


@functools.lru_cache(None)
def half_metric(bands):
    total = bands * ROWS
    rows = np.clip(np.arange(bands)[:, None] * ROWS - 8 + np.arange(32)[None, :], 0, total - 1)
    metric = np.minimum(1.0 / np.cos(np.pi * ((rows + 0.5) / total - 0.5)), metric_cap)
    table = np.broadcast_to((0.5 * metric).astype(np.float32)[:, :, None], (bands, 32, 128)).copy()
    forward = mode_factors()[FORWARD : FORWARD + WIDE].astype(np.float32)
    for row, col in enumerate((0, COLS - 1)):
        table[:, row] = forward[col, :RANK] + forward[col, RANK:]
    return table


def dot_cols(a, b):
    return lax.dot_general(a, b, (((1,), (0,)), ((), ())), preferred_element_type=F32)


def split(x):
    high = x.astype(BF16)
    return high, (x - high.astype(F32)).astype(BF16)


def to_modes(x, table):
    xh, xl = split(x)
    half = table.shape[1] // 2
    wide = dot_cols(xh, table[...])
    return wide[:, :half] + wide[:, half:] + dot_cols(xl, table[:, 0:half])


def from_modes(z, *tables):
    zh, zl = split(z)
    three = jnp.concatenate([zh, zh, zl], axis=1)
    return jnp.concatenate([dot_cols(three, table[...]) for table in tables], axis=1)


def to_coefs(x, table):
    rows = x.shape[0]
    wide = dot_cols(jnp.concatenate(split(x), axis=0), table[...])
    half = wide.shape[1] // 2
    return wide[:rows, :half] + wide[:rows, half:] + wide[rows:, :half]


def from_coefs(z, table):
    zh, zl = split(z)
    rows = jnp.concatenate([jnp.concatenate([zh, zh], axis=1), jnp.concatenate([zl, jnp.zeros_like(zl)], axis=1)], axis=0)
    wide = dot_cols(rows, table[...])
    return wide[: z.shape[0]] + wide[z.shape[0] :]


def pack(levels):
    lane = lax.broadcasted_iota(jnp.int32, (1, RANK), 1)
    return [jnp.where(lane < USED, levels[l], roll(levels[3], 96 - 32 * l, 1)) for l in range(3)]


def unpack(parts):
    lane = lax.broadcasted_iota(jnp.int32, (1, RANK), 1)
    last = jnp.where(lane < 64, roll(parts[1], 64, 1), roll(parts[2], 96, 1))
    return parts + [jnp.where(lane < 32, roll(parts[0], 32, 1), last)]


def roll(x, shift, axis):
    return pltpu.roll(x, shift % x.shape[axis], axis)


def roll_blocks(x, shift):
    return roll(x.reshape(x.shape[0] * x.shape[1], x.shape[2]), shift, 1).reshape(x.shape)


def fold(x):
    while x.shape[0] > 1:
        half = x.shape[0] // 2
        x = x[:half] + roll_blocks(x[half:], 2 * half)
    return x


def kernel(
    bands, spread, east, north, rs, cs, cut, metric, table_in, tan_out, diag_out,
    spread_v, winds_v, rs_v, cs_v, cut_s, hm, table,
    grid, halo_out, halo_in, ybuf, yr, xb, cb, yc, zbuf, zr, eb, bz,
    tend, adj, gy,
    in_sem, halo_send, halo_recv, y_send, y_recv, c_send, c_recv, z_send, z_recv, b_send, b_recv,
):
    b = lax.axis_index("lat")
    i = lax.axis_index("lon")
    caps = POLAR // ROWS
    is_north = b == 0
    is_south = b == bands - 1
    polar = jnp.logical_or(b < caps, b >= bands - caps)
    above_polar = jnp.logical_or(b <= caps, is_south)
    below_polar = jnp.logical_or(b >= bands - caps - 1, is_north)
    near_polar = jnp.logical_or(above_polar, below_polar)
    across = lax.rem(i + LANES // 2, LANES)
    west = lax.rem(i + LANES - 1, LANES)
    east_lane = lax.rem(i + 1, LANES)
    nb = jnp.where(is_north, 0, b - 1)
    nl = jnp.where(is_north, across, i)
    sb = jnp.where(is_south, bands - 1, b + 1)
    sl = jnp.where(is_south, across, i)
    slot_n = jnp.where(is_north, 0, 1)
    slot_s = jnp.where(is_south, 1, 0)
    own_half = lax.rem(i, 2)
    edge_over = jnp.where(own_half == 0, is_north, is_south)
    over_pole = (is_north, is_south)
    outward = jnp.logical_and(b == bands - caps, own_half == 0)

    def plus(lane, d):
        return lax.rem(lane + d, LANES)

    load_spread = pltpu.make_async_copy(spread, spread_v, in_sem.at[0])
    load_rows = pltpu.make_async_copy(rs, rs_v, in_sem.at[1])
    load_cols = pltpu.make_async_copy(cs, cs_v, in_sem.at[2])
    load_metric = pltpu.make_async_copy(metric.at[b], hm, in_sem.at[4])
    load_cut = pltpu.make_async_copy(cut, cut_s, in_sem.at[5])

    def load_table(start, stop, sem):
        return pltpu.make_async_copy(table_in.at[start:stop], table.at[start:stop], in_sem.at[sem])

    load_forward = load_table(FORWARD, EVALUATE, 6)
    load_others = load_table(EVALUATE, TABLE_ROWS, 7)
    load_part = load_table(EVALUATE, TO_COEFS, 7)
    barrier = pltpu.get_barrier_semaphore()

    def greet(lat, lon):
        pl.semaphore_signal(barrier, inc=1, device_id=(lat, lon), device_id_type=MESH)

    greet(nb, nl)
    greet(sb, sl)

    @pl.when(polar)
    def _():
        for d in FAR_FIRST[:4]:
            greet(b, plus(i, d))

    greet(b, west)
    greet(b, east_lane)
    load_spread.start()
    load_rows.start()
    load_cols.start()
    pltpu.make_async_copy(east, winds_v.at[0], in_sem.at[3]).start()
    pltpu.make_async_copy(north, winds_v.at[1], in_sem.at[3]).start()
    load_metric.start()

    @pl.when(polar)
    def _():
        greet(b, across)
        load_forward.start()
        load_cut.start()

    @pl.when(jnp.logical_and(near_polar, jnp.logical_not(polar)))
    def _():
        load_part.start()

    load_rows.wait()
    load_cols.wait()
    load_spread.wait()
    grid[:, 8:24, 384:512] = jnp.zeros((PAIRS + 2 * LEV, ROWS, 128), F32)
    row_part = jnp.concatenate([rs_v[f] for f in range(FIELDS)], axis=0)
    row_part = (2 * row_part - 1).astype(F32).T
    for f in range(FIELDS):
        col_part = (2 * cs_v[f] - 1).astype(F32)
        for l in range(LEV):
            n = f * LEV + l
            grid[n, 8:24, 0:COLS] = spread_v[f, l] * (row_part[:, n : n + 1] * col_part[l : l + 1, :])

    @pl.when(polar)
    def _():
        load_others.start()

    pltpu.make_async_copy(winds_v, winds_v, in_sem.at[3]).wait()
    for w in range(2):
        for l in range(LEV):
            grid[PAIRS + w * LEV + l, 8:24, 0:COLS] = winds_v[w, l]

    def edge_rows(start, entries, rows):
        for s, row in enumerate(rows):
            for t in range(4):
                values = grid[entries, row, 128 * t : 128 * t + 128]
                if entries == slice(0, PAIRS):
                    halo_out[start[s] + t] = values
                else:
                    halo_out[start[s] + t // 2, 8 * (t % 2) : 8 * (t % 2) + 8, :] = values

    edge_rows((NEAR, NEAR + 4), slice(0, PAIRS), (8, 23))
    lane128 = lax.broadcasted_iota(jnp.int32, (1, 1, 128), 2)
    for s, (start, shift) in enumerate(((0, 0), (384, COLS - 2 - 384))):
        tile = grid[:, 8:24, start : start + 128]
        tile = jnp.where(jnp.logical_and(lane128 >= shift, lane128 < shift + 2), tile, 0.0)
        packed = fold(tile[:PAIRS]) + roll_blocks(fold(tile[PAIRS:]), 2 * PAIRS)
        halo_out[SIDES + s] = roll_blocks(packed, -shift)[0]

    pl.semaphore_wait(barrier, 4 + jnp.where(polar, LANES - 3, 0))

    def remote(src, dst, send, recv, lat, lon):
        return pltpu.make_async_remote_copy(
            src_ref=src, dst_ref=dst, send_sem=send, recv_sem=recv, device_id=(lat, lon), device_id_type=MESH
        )

    def halo_copy(start, count, to, which, lat, lon):
        return remote(
            halo_out.at[start : start + count], halo_in.at[pl.ds(to, count)], halo_send, halo_recv.at[which], lat, lon
        )

    def halo_arrival(start, stop, which):
        return remote(
            halo_out.at[start:stop], halo_in.at[start:stop], halo_send, halo_recv.at[which], b, west
        )

    @pl.when(b < bands // 2)
    def _():
        halo_copy(NEAR, 4, NEAR + 4 * slot_n, 0, nb, nl).start()

    halo_copy(NEAR + 4, 4, NEAR + 4 * slot_s, 0, sb, sl).start()

    @pl.when(b >= bands // 2)
    def _():
        halo_copy(NEAR, 4, NEAR + 4 * slot_n, 0, nb, nl).start()

    halo_copy(SIDES, 1, SIDES + 1, 0, b, west).start()
    halo_copy(SIDES + 1, 1, SIDES, 0, b, east_lane).start()

    others = pl.ds(0, LANES - 1)

    def all_y(q):
        return remote(ybuf.at[q, others], yr.at[q, others], y_send.at[q], y_recv.at[q], b, west)

    def send_values(q, x):
        y = to_modes(x.reshape(PAIRS * ROWS, WIDE), table.at[FORWARD:EVALUATE])
        y = y.reshape(FIELDS, LEV, 2, 8, RANK)
        blocks = [
            jnp.concatenate([y[f, l, h] for f in range(FIELDS) for h in range(2)], axis=0) for l in range(LEV)
        ]
        for l, part in enumerate(pack(blocks)):
            ybuf[q, :, l] = part.reshape(LANES, 8, RANK)

        for d in FAR_FIRST:
            o = plus(i, d)
            remote(ybuf.at[q, o], yr.at[q, i], y_send.at[q], y_recv.at[q], b, o).start()

        yr[q, i] = ybuf[q, i]

    def c_copy(o):
        return remote(cb.at[o], yc.at[i], c_send, c_recv, b, o)

    def all_c():
        return remote(cb.at[others], yc.at[others], c_send, c_recv, b, west)

    def z_copy(q, j):
        return remote(zbuf.at[q, j], zr.at[q, i], z_send.at[q], z_recv.at[q], b, j)

    def all_z(q):
        return remote(zbuf.at[q, others], zr.at[q, others], z_send.at[q], z_recv.at[q], b, west)

    def edge_sends():
        slot = jnp.where(own_half == 0, slot_n, slot_s)
        lat = jnp.where(own_half == 0, nb, sb)

        def away(j, lon):
            remote(eb.at[j], bz.at[slot, i // 2], b_send, b_recv.at[slot], lat, lon).start()

        @pl.when(jnp.logical_not(edge_over))
        def _():
            for j in ANSWERS:
                away(j, j)

        @pl.when(edge_over)
        def _():
            for j in ANSWERS:
                lon = (j + LANES // 2) % LANES

                @pl.when(i != lon)
                def _():
                    away(j, lon)

                @pl.when(i == lon)
                def _():
                    pltpu.make_async_copy(eb.at[j], bz.at[slot, i // 2], b_recv.at[slot]).start()

    def own_rows(q):
        row = lax.broadcasted_iota(jnp.int32, (8, 128), 0)
        cutoff = jnp.zeros((8, 128), jnp.int32)
        for r in range(8):
            cutoff = jnp.where(row == r, cut_s[8 * own_half + r], cutoff)
        keeps = []
        for group in range(4):
            wave = waves_of(group, lax.broadcasted_iota(jnp.int32, (8, 128), 1))
            keep = jnp.where(wave > cutoff, 2.0 / (COLS * LANES), 0.0)
            keeps.append(jnp.concatenate([keep] * LEV, axis=0))
        all_y(q).wait_recv()
        levels = unpack([yr[q, :, l].reshape(LANES * 8, RANK) for l in range(LEV - 1)])
        if q == 1:
            edge_row = jnp.where(row == 7 * own_half, 1.0, 0.0)
            all_c().wait_recv()
            ends = jnp.concatenate([yc[j, 8:16, :] for j in range(LANES)], axis=0)
            ends = pltpu.roll(ends, lax.rem(128 - 2 * LEV * (i // 2), 128), 1)
            levels = [
                levels[l]
                + ends[:, 2 * l : 2 * l + 1] * hm[0:1, :]
                + ends[:, 2 * l + 1 : 2 * l + 2] * hm[1:2, :]
                + jnp.concatenate([edge_row * yc[j, l : l + 1, :] for j in range(LANES)], axis=0)
                for l in range(LEV)
            ]
        lanes = [
            jnp.concatenate([levels[l][8 * j : 8 * j + 8, :] for l in range(LEV)], axis=0) for j in range(LANES)
        ]
        coefs = [
            to_coefs(jnp.concatenate(pair, axis=1), table.at[TO_COEFS + 256 * group : TO_COEFS + 256 * (group + 1)])
            for group, pair in enumerate(over_lanes(lanes))
        ]
        kept = [coef * keep for coef, keep in zip(coefs, keeps)]
        backs = [
            from_coefs(coef, table.at[FROM_COEFS + 256 * group : FROM_COEFS + 256 * (group + 1)])
            for group, coef in enumerate(kept)
        ]
        pairs = [(back[:, :RANK], back[:, RANK:]) for back in backs]
        zs = [z.reshape(LEV, 8, RANK) for z in to_lanes(pairs)]
        for l, part in enumerate(pack([jnp.concatenate([z[l] for z in zs], axis=0) for l in range(LEV)])):
            zbuf[q, :, l] = part.reshape(LANES, 8, RANK)

        def edges():
            for j, z in enumerate(zs):
                edge = jnp.where(own_half == 0, z[:, 0, :], z[:, 7, :])
                eb[j] = edge if q == 0 else eb[j] + edge
            if q == 1:
                edge_sends()

        if q == 1:
            pl.when(outward)(edges)
        for j in ANSWERS:
            @pl.when(i != j)
            def _():
                z_copy(q, j).start()

        if q == 1:
            pl.when(jnp.logical_not(outward))(edges)
        else:
            edges()
        zr[q, i] = zbuf[q, i]

    def evaluate(z):
        return from_modes(z, table.at[EVALUATE : EVALUATE + 384], table.at[EVALUATE + 384 : TO_COEFS])

    def project(q, h):
        levels = unpack(
            [jnp.concatenate([zr[q, 2 * f + h, l] for f in range(FIELDS)], axis=0) for l in range(LEV - 1)]
        )
        z = jnp.concatenate(
            [levels[l][8 * f : 8 * f + 8, :] for f in range(FIELDS) for l in range(LEV)], axis=0
        )
        out = evaluate(z)
        return [[out[8 * (LEV * f + l) : 8 * (LEV * f + l + 1), :] for l in range(LEV)] for f in range(FIELDS)]

    def tendency_rows(h, l, at, half):
        lo = jnp.maximum(l - 1, 0)
        hi = jnp.minimum(l + 1, LEV - 1)
        ew = at(PAIRS + l, h)
        nw = at(PAIRS + LEV + l, h)
        mids, along_x, along_y = [], [], []
        for f in range(FIELDS):
            mid = at(f * LEV + l, h)
            mids.append(mid)
            along_x.append(half * (roll(mid, -1, 1) - roll(mid, 1, 1)))
            along_y.append(0.5 * (at(f * LEV + l, h + 1) - at(f * LEV + l, h - 1)))
        linked = (along_x[2], along_y[2], along_x[0] + along_y[1], None)
        out = []
        for f in range(FIELDS):
            mixed = at(f * LEV + lo, h) + at(f * LEV + hi, h) - 2.0 * mids[f]
            t = -(ew * along_x[f] + nw * along_y[f]) + mixing * mixed
            if linked[f] is not None:
                t = t - coupling * linked[f]
            out.append(time_step * t)
        return out

    def full_tendency():
        @pl.loop(0, LEV, unroll=True)
        def _(l):
            for h in (8, 16):
                half = jnp.concatenate([hm[h : h + 8, :]] * 4, axis=1)
                for f, t in enumerate(tendency_rows(h, l, lambda n, r: grid[n, r : r + 8, :], half)):
                    tend[f * LEV + l, h - 8 : h, :] = t

    def side_tendency():
        lane = lax.broadcasted_iota(jnp.int32, (1, 128), 1)
        late = jnp.logical_or(jnp.logical_or(lane == 65, lane == 66), lane == 127)

        def at(n, r):
            return jnp.where(lane < 2, grid[n, r : r + 8, 0:128], grid[n, r : r + 8, 384:512])

        @pl.loop(0, LEV, unroll=True)
        def _(l):
            for h in (8, 16):
                for f, t in enumerate(tendency_rows(h, l, at, hm[h : h + 8, :])):
                    n, rows = f * LEV + l, slice(h - 8, h)
                    tend[n, rows, 0:128] = jnp.where(lane == 0, t, tend[n, rows, 0:128])
                    tend[n, rows, 384:512] = jnp.where(late, t, tend[n, rows, 384:512])

    load_metric.wait()

    @pl.when(polar)
    def _():
        load_forward.wait()
        send_values(0, grid[0:PAIRS, 8:24, :])
        grid[0:PAIRS, 7:8, :] = jnp.zeros((PAIRS, 1, WIDE), F32)
        grid[0:PAIRS, 24:25, :] = jnp.zeros((PAIRS, 1, WIDE), F32)
        full_tendency()
        send_values(1, tend[...])

    edge_rows((REST + 4, REST + 11), slice(PAIRS, PAIRS + 2 * LEV), (8, 23))

    halo_arrival(NEAR, REST, 0).wait_recv()
    lane2 = lax.broadcasted_iota(jnp.int32, (1, 128), 1)
    row16 = lax.broadcasted_iota(jnp.int32, (PAIRS, 1), 0)
    is_v = jnp.logical_and(row16 >= LEV, row16 < 2 * LEV)
    is_temp = jnp.logical_and(row16 >= 2 * LEV, row16 < 3 * LEV)

    def flip(s, minus):
        sign = jnp.where(row16 < 2 * LEV, -1.0, 1.0) * minus
        return jnp.where(over_pole[s], sign, 1.0)

    def row_link(x):
        return jnp.where(is_v, roll(x, -LEV, 0), jnp.where(is_temp, roll(x, LEV, 0), 0.0))

    def wind(buffer, s, w):
        base = REST + 7 * s + 4
        rows = [buffer[base + t // 2, 8 * (t % 2) + LEV * w : 8 * (t % 2) + LEV * (w + 1), :] for t in range(4)]
        return jnp.concatenate([jnp.concatenate(rows, axis=1)] * FIELDS, axis=0)

    def row_of(buffer, start):
        return jnp.concatenate([buffer[start + t] for t in range(4)], axis=1)

    @pl.when(polar)
    def _():
        added = []
        for s, sign in ((0, 0.5 * time_step), (1, -0.5 * time_step)):
            ghost = flip(s, 1.0) * row_of(halo_in, NEAR + 4 * s)
            added.append(sign * (wind(halo_out, s, 1) * ghost + coupling * row_link(ghost)))
            xb[s] = added[s]
        y = to_modes(jnp.concatenate(added, axis=0), table.at[FORWARD:EVALUATE])
        for s in range(2):
            for f in range(FIELDS):
                cb[2 * f + s, 0:LEV, :] = y[(s * FIELDS + f) * LEV : (s * FIELDS + f + 1) * LEV, :]
        ends = []
        for side, sign in ((0, -1.0), (1, 1.0)):
            came = halo_in[SIDES + side]
            along_x = (sign * hm[8:24, :]) * (roll(came, -1, 1) if side == 0 else came)
            mine = jnp.where(
                jnp.logical_and(lane2 >= 2 * PAIRS, lane2 < 2 * (PAIRS + LEV)), halo_out[SIDES + side], 0.0
            )
            ew = sum(roll(mine, 2 * LEV * f - 2 * PAIRS - side, 1) for f in range(FIELDS))
            linked = jnp.where(
                lane2 < 2 * LEV,
                roll(along_x, -4 * LEV, 1),
                jnp.where(
                    jnp.logical_and(lane2 >= 4 * LEV, lane2 < 6 * LEV), roll(along_x, 4 * LEV, 1), 0.0
                ),
            )
            ends.append(time_step * (-ew * along_x - coupling * linked))
        ends = jnp.where(lax.rem(lane2, 2) == 0, ends[0], roll(ends[1], 1, 1))
        for f in range(FIELDS):
            for h in range(2):
                cb[2 * f + h, 8:16, :] = ends[8 * h : 8 * h + 8, :]

        for d in FAR_FIRST:
            c_copy(plus(i, d)).start()

        yc[i] = cb[i]

    from_west = roll(halo_in[SIDES], 126, 1)
    from_east = roll(halo_in[SIDES + 1], COLS - 384, 1)
    both = jnp.where(jnp.logical_and(lane2 >= 66, lane2 < 114), from_east, from_west)[None]
    for width in (2, 4, 8):
        both = jnp.concatenate([both, roll_blocks(both, -width)], axis=0)
    both = jnp.concatenate([both, roll_blocks(both, -16), roll_blocks(both, -32)], axis=0)
    in_halo = jnp.logical_or(jnp.logical_and(lane128 >= 66, lane128 < 68), lane128 >= 126)
    grid[:, 8:24, 384:512] = jnp.where(in_halo, both, grid[:, 8:24, 384:512])
    edge_rows((REST, REST + 7), slice(0, PAIRS), (9, 22))
    for s, near in enumerate((8, 23)):
        halo_out[REST + 7 * s + 6] = grid[0:PAIRS, near, 384:512]
    halo_copy(REST, 7, REST + 7 * slot_n, 1, nb, nl).start()
    halo_copy(REST + 7, 7, REST + 7 * slot_s, 1, sb, sl).start()

    @pl.when(polar)
    def _():
        load_cut.wait()
        load_others.wait()
        own_rows(0)

    @pl.when(jnp.logical_and(polar, b < bands // 2))
    def _():
        own_rows(1)

    halo_arrival(REST, BLOCKS, 1).wait_recv()
    edge_row = (7, 24)
    edge_probe = []
    for s in range(2):
        edge_probe.append(
            jnp.concatenate([halo_in[NEAR + 4 * s + t] for t in range(3)] + [halo_in[REST + 7 * s + 6]], axis=1)
        )
        grid[0:PAIRS, edge_row[s], :] = flip(s, 1.0) * edge_probe[s]

    @pl.when(polar)
    def _():
        for s, row in ((0, 0), (1, 15)):
            tend[:, row, :] = tend[:, row, :] + xb[s]
        side_tendency()

    @pl.when(jnp.logical_not(polar))
    def _():
        full_tendency()

    def edge_weights(s, a):
        return -wind(halo_in, s, 1) * a - coupling * row_link(a)

    for s, inward in ((0, 1.0), (1, -1.0)):
        mid = edge_probe[s]
        half = jnp.concatenate([hm[edge_row[s] : edge_row[s] + 1, :]] * 4, axis=1)
        along_x = half * (roll(mid, -1, 1) - roll(mid, 1, 1))
        turn = jnp.where(over_pole[s], -0.5 * inward, 0.5 * inward)
        along_y = turn * (flip(s, 1.0) * row_of(halo_out, NEAR + 4 * s) - row_of(halo_in, REST + 7 * s))
        linked = jnp.where(row16 < LEV, roll(along_x, -2 * LEV, 0), row_link(along_y))
        linked = linked + jnp.where(is_temp, roll(along_x, 2 * LEV, 0), 0.0)
        up = jnp.where(lax.rem(row16, LEV) == 0, mid, roll(mid, 1, 0))
        down = jnp.where(lax.rem(row16, LEV) == LEV - 1, mid, roll(mid, -1, 0))
        t = -(wind(halo_in, s, 0) * along_x + wind(halo_in, s, 1) * along_y) - coupling * linked
        a = mid + time_step * (t + mixing * (up + down - 2.0 * mid))
        gy[0:PAIRS, edge_row[s], :] = flip(s, -1.0) * edge_weights(s, a)

    @pl.when(jnp.logical_and(polar, b >= bands // 2))
    def _():
        own_rows(1)

    def row_weights(a, nw):
        return (
            -nw * a[0],
            -nw * a[1] - coupling * a[2],
            -nw * a[2] - coupling * a[1],
            -nw * a[3],
        )

    def put_weights(l, h, a):
        for f, weight in enumerate(row_weights(a, grid[PAIRS + LEV + l, h : h + 8, :])):
            gy[f * LEV + l, h : h + 8, :] = weight

    @pl.when(polar)
    def _():
        all_z(0).wait_recv()
        for h in (8, 16):
            taken = project(0, h // 8 - 1)
            for l in range(LEV):
                for f in range(FIELDS):
                    n, rows = f * LEV + l, slice(h - 8, h)
                    adj[n, rows, :] = grid[n, h : h + 8, :] + tend[n, rows, :] - taken[f][l]
        all_z(1).wait_recv()
        for h in (8, 16):
            taken = project(1, h // 8 - 1)
            for l in range(LEV):
                a = []
                for f in range(FIELDS):
                    n, rows = f * LEV + l, slice(h - 8, h)
                    change = tend[n, rows, :] - taken[f][l]
                    tend[n, rows, :] = change
                    tan_out[f, l, rows, :] = (grid[n, h : h + 8, :] + change)[:, :COLS]
                    a.append(adj[n, rows, :] - taken[f][l])
                    adj[n, rows, :] = a[f]
                put_weights(l, h, a)

    @pl.when(jnp.logical_not(polar))
    def _():
        @pl.loop(0, LEV, unroll=True)
        def _(l):
            for h in (8, 16):
                a = []
                for f in range(FIELDS):
                    n, rows = f * LEV + l, slice(h - 8, h)
                    a.append(grid[n, h : h + 8, :] + tend[n, rows, :])
                    tan_out[f, l, rows, :] = a[f][:, :COLS]
                    adj[n, rows, :] = a[f]
                put_weights(l, h, a)

    @pl.loop(0, LEV, unroll=True)
    def _(l):
        lo = jnp.maximum(l - 1, 0)
        hi = jnp.minimum(l + 1, LEV - 1)
        for h in (8, 16):
            rows = slice(h - 8, h)
            half = jnp.concatenate([hm[h : h + 8, :]] * 4, axis=1)
            ew = grid[PAIRS + l, h : h + 8, :]
            a = [adj[f * LEV + l, rows, :] for f in range(FIELDS)]
            col_weights = (
                -ew * a[0] - coupling * a[2],
                -ew * a[1],
                -ew * a[2] - coupling * a[0],
                -ew * a[3],
            )
            for f in range(FIELDS):
                n = f * LEV + l
                back = half * (roll(col_weights[f], 1, 1) - roll(col_weights[f], -1, 1))
                back = back + 0.5 * (gy[n, h - 1 : h + 7, :] - gy[n, h + 1 : h + 9, :])
                back = back + mixing * (adj[f * LEV + lo, rows, :] + adj[f * LEV + hi, rows, :] - 2.0 * a[f])
                diag = grid[n, h : h + 8, :] * (tend[n, rows, :] + time_step * back)
                diag_out[f, l, rows, :] = diag[:, :COLS]

    @pl.when(jnp.logical_and(near_polar, jnp.logical_not(polar)))
    def _():
        load_part.wait()

    for s, wanted in enumerate((above_polar, below_polar)):
        @pl.when(wanted)
        def _():
            row = 15 * s
            north_wind = wind(halo_in, s, 1)
            factor = ((0.5, -0.5)[s] * time_step) * grid[0:PAIRS, 8 + row, :] * flip(s, -1.0)
            before = [diag_out[f, :, row, :] for f in range(FIELDS)]
            remote(bz.at[s], bz.at[s], b_send, b_recv.at[s], nb, nl).wait_recv()
            taken = evaluate(jnp.concatenate([bz[s, f] for f in range(FIELDS)], axis=0))
            more = factor * (north_wind * taken + coupling * row_link(taken))
            for f in range(FIELDS):
                diag_out[f, :, row, :] = before[f] + more[f * LEV : (f + 1) * LEV, :COLS]

    halo_arrival(0, BLOCKS, 0).wait_send()

    @pl.when(polar)
    def _():
        all_c().wait_send()
        for q in range(2):
            all_y(q).wait_send()
            all_z(q).wait_send()

        @pl.when(edge_over)
        def _():
            remote(eb.at[others], eb.at[others], b_send, b_recv.at[0], b, west).wait_send()

        @pl.when(jnp.logical_not(edge_over))
        def _():
            remote(eb, eb, b_send, b_recv.at[0], b, west).wait_send()


def hand_out(tan_in, diag_in, tan_out, diag_out, sem):
    copies = [
        pltpu.make_async_copy(src, dst, sem.at[n])
        for n, (src, dst) in enumerate(((tan_in, tan_out), (diag_in, diag_out)))
    ]
    for copy in copies:
        copy.start()
    for copy in copies:
        copy.wait()


def per_device(bands, row_signs, col_signs, spread, east_wind, north_wind, cutoffs):
    any_spec = pl.BlockSpec(memory_space=pl.ANY)
    out = jax.ShapeDtypeStruct((FIELDS, LEV, ROWS, COLS), F32)
    tables = [jnp.asarray(half_metric(bands)), jnp.asarray(mode_factors())]
    operands = (spread, east_wind, north_wind, row_signs, col_signs, cutoffs, *tables)
    vmem = pltpu.VMEM
    dma = pltpu.SemaphoreType.DMA
    held = pltpu.VMEM(out.shape, F32)
    results = pl.pallas_call(
        functools.partial(kernel, bands),
        out_shape=(held, held),
        in_specs=[any_spec] * 8,
        out_specs=(pl.BlockSpec(memory_space=pltpu.VMEM),) * 2,
        scratch_shapes=[
            vmem((FIELDS, LEV, ROWS, COLS), F32),
            vmem((2, LEV, ROWS, COLS), F32),
            vmem((FIELDS, LEV, ROWS), jnp.int32),
            vmem((FIELDS, LEV, COLS), jnp.int32),
            pltpu.SMEM((ROWS,), jnp.int32),
            vmem((32, 128), F32),
            vmem((TABLE_ROWS, 2 * RANK), BF16),
            vmem((PAIRS + 2 * LEV, 32, WIDE), F32),
            vmem((BLOCKS, 16, 128), F32),
            vmem((BLOCKS, 16, 128), F32),
            vmem((2, LANES, LEV - 1, 8, RANK), F32),
            vmem((2, LANES, LEV - 1, 8, RANK), F32),
            vmem((2, PAIRS, WIDE), F32),
            vmem((LANES, 16, RANK), F32),
            vmem((LANES, 16, RANK), F32),
            vmem((2, LANES, LEV - 1, 8, RANK), F32),
            vmem((2, LANES, LEV - 1, 8, RANK), F32),
            vmem((LANES, LEV, RANK), F32),
            vmem((2, FIELDS, LEV, RANK), F32),
            vmem((PAIRS, ROWS, WIDE), F32),
            vmem((PAIRS, ROWS, WIDE), F32),
            vmem((PAIRS, 32, WIDE), F32),
            dma((8,)),
            dma,
            dma((2,)),
            dma((2,)),
            dma((2,)),
            dma,
            dma,
            dma((2,)),
            dma((2,)),
            dma,
            dma((2,)),
        ],
        compiler_params=pltpu.CompilerParams(
            collective_id=0, has_side_effects=True, vmem_limit_bytes=32 * 2**20
        ),
        cost_estimate=pl.CostEstimate(flops=10**9, bytes_accessed=4 * 10**6, transcendentals=0),
    )(*(pltpu.with_memory_space_constraint(x, pltpu.HBM) for x in operands))
    return pl.pallas_call(
        hand_out,
        out_shape=(out, out),
        in_specs=[any_spec] * 2,
        out_specs=(any_spec, any_spec),
        scratch_shapes=[dma((2,))],
        compiler_params=pltpu.CompilerParams(vmem_limit_bytes=2**20),
    )(*(pltpu.with_memory_space_constraint(x, pltpu.VMEM) for x in results))


def solution(mesh):
    return jax.shard_map(
        functools.partial(per_device, mesh.shape["lat"]),
        mesh=mesh,
        in_specs=(
            P(None, None, "lat"),
            P(None, None, "lon"),
            P(None, None, "lat", "lon"),
            P(None, "lat", "lon"),
            P(None, "lat", "lon"),
            P("lat"),
        ),
        out_specs=(P(None, None, "lat", "lon"), P(None, None, "lat", "lon")),
        check_vma=False,
    )
```

```python
import functools

import jax
import jax.numpy as jnp
import ml_dtypes
import numpy as np
from jax import lax
from jax.experimental import pallas as pl
from jax.experimental.pallas import tpu as pltpu
from jax.sharding import PartitionSpec as P

KTOP = 256
POLAR = 32
RANK = 128
USED = 96
ROWS = 16
COLS = 450
WIDE = 512
LANES = 8
FIELDS = 4
LEV = 4
PAIRS = FIELDS * LEV

time_step = 0.5
coupling = 0.5
mixing = 0.2
metric_cap = 4.0

FORWARD, EVALUATE, TO_COEFS, FROM_COEFS, TABLE_ROWS = 0, 512, 1280, 2304, 3328
NEAR, SIDES, REST, BLOCKS = 0, 8, 10, 24

FAR_FIRST = (6, 2, 5, 3, 7, 1, 4)
ANSWERS = (0, 4, 1, 3, 2, 7, 5, 6)

MESH = pl.DeviceIdType.MESH
F32 = jnp.float32
BF16 = jnp.bfloat16


def split_table(table):
    high = table.astype(ml_dtypes.bfloat16)
    low = (table - high.astype(np.float64)).astype(ml_dtypes.bfloat16)
    return high, low


def waves_of(group, lane_index):
    place = lane_index % 64
    second = place // 32
    other = (8 - group) if group else 4
    residue = group + second * (other - group)
    return 8 * (place % 32) + residue + (8 * (1 - second) if group == 0 else 0)


@functools.lru_cache(None)
def mode_factors():
    total = COLS * LANES
    size = COLS + 2
    place = np.arange(size, dtype=np.float64)
    width = (KTOP + 0.5) / total
    diag = ((size - 1 - 2 * place) / 2) ** 2 * np.cos(2 * np.pi * width)
    side = place[1:] * (size - place[1:]) / 2
    vectors = np.linalg.eigh(np.diag(diag) + np.diag(side, 1) + np.diag(side, -1))[1]
    basis = np.concatenate([vectors[:, ::-1][:, :USED], np.zeros((size, RANK - USED))], axis=1)
    basis = basis * np.where(basis[size // 2] < 0, -1.0, 1.0)
    weights = []
    for group in range(4):
        waves = waves_of(group, np.arange(64))
        angle = 2 * np.pi / total * ((np.arange(size)[:, None] - 1) * waves[None, :] % total)
        alpha, beta = basis.T @ np.cos(angle), basis.T @ np.sin(angle)
        if group:
            sign = np.where(np.arange(64) < 32, 1.0, -1.0)
            top, low = (alpha, beta), (sign * beta, -sign * alpha)
        else:
            use = np.where(np.arange(64) < 32, 1.0, 0.0)
            top, low = (use * alpha, use * beta), ((1 - use) * alpha, (1 - use) * beta)
        weights.append(np.concatenate([np.concatenate(top, axis=1), np.concatenate(low, axis=1)], axis=0))
    weights = np.round(np.stack(weights) * 2.0**22) / 2.0**22
    wide = np.zeros((RANK, WIDE))
    wide[:, : COLS + 1] = basis[1:].T
    wide[:, WIDE - 1] = basis[0]
    wide = np.round(wide * 2.0**26) / 2.0**26
    wide_h, wide_l = split_table(wide)
    own = np.where(np.arange(WIDE)[:, None] < COLS, 1, 0).astype(ml_dtypes.bfloat16)
    high, low = split_table(weights)
    back = np.concatenate([np.swapaxes(part, 1, 2) for part in (high, low)], axis=1)
    evaluate = np.concatenate([wide_h, wide_l, wide_h], axis=0)
    return np.concatenate(
        [
            np.concatenate([wide_h.T * own, wide_l.T * own], axis=1),
            evaluate[:, : WIDE // 2],
            evaluate[:, WIDE // 2 :],
            np.concatenate([high, low], axis=2).reshape(-1, 2 * RANK),
            back.reshape(-1, 2 * RANK),
        ],
        axis=0,
    )


ROOT = float(np.sqrt(0.5))


def over_lanes(y):
    s = [y[j] + y[j + 4] for j in range(4)]
    d = [y[j] - y[j + 4] for j in range(4)]
    even, odd = s[0] + s[2], s[1] + s[3]
    minus, plus = ROOT * (d[1] - d[3]), ROOT * (d[1] + d[3])
    return [
        (even + odd, even - odd),
        (d[0] + minus, -(d[2] + plus)),
        (s[0] - s[2], s[3] - s[1]),
        (d[0] - minus, d[2] - plus),
    ]


def to_lanes(pairs):
    (y0, y4), (u1, v1), (u2, v2), (u3, v3) = pairs
    even, odd = y0 + y4, y0 - y4
    s = [even + u2, odd - v2, even - u2, odd + v2]
    du, sv = ROOT * (u1 - u3), ROOT * (v1 + v3)
    d = [u1 + u3, du - sv, v3 - v1, -du - sv]
    return [s[j] + d[j] for j in range(4)] + [s[j] - d[j] for j in range(4)]


@functools.lru_cache(None)
def half_metric(bands):
    total = bands * ROWS
    rows = np.clip(np.arange(bands)[:, None] * ROWS - 8 + np.arange(32)[None, :], 0, total - 1)
    metric = np.minimum(1.0 / np.cos(np.pi * ((rows + 0.5) / total - 0.5)), metric_cap)
    table = np.broadcast_to((0.5 * metric).astype(np.float32)[:, :, None], (bands, 32, 128)).copy()
    forward = mode_factors()[FORWARD : FORWARD + WIDE].astype(np.float32)
    for row, col in enumerate((0, COLS - 1)):
        table[:, row] = forward[col, :RANK] + forward[col, RANK:]
    return table


def dot_cols(a, b):
    return lax.dot_general(a, b, (((1,), (0,)), ((), ())), preferred_element_type=F32)


def split(x):
    high = x.astype(BF16)
    return high, (x - high.astype(F32)).astype(BF16)


def to_modes(x, table):
    xh, xl = split(x)
    half = table.shape[1] // 2
    wide = dot_cols(xh, table[...])
    return wide[:, :half] + wide[:, half:] + dot_cols(xl, table[:, 0:half])


def from_modes(z, *tables):
    zh, zl = split(z)
    three = jnp.concatenate([zh, zh, zl], axis=1)
    return jnp.concatenate([dot_cols(three, table[...]) for table in tables], axis=1)


def to_coefs(x, table):
    rows = x.shape[0]
    wide = dot_cols(jnp.concatenate(split(x), axis=0), table[...])
    half = wide.shape[1] // 2
    return wide[:rows, :half] + wide[:rows, half:] + wide[rows:, :half]


def from_coefs(z, table):
    zh, zl = split(z)
    rows = jnp.concatenate([jnp.concatenate([zh, zh], axis=1), jnp.concatenate([zl, jnp.zeros_like(zl)], axis=1)], axis=0)
    wide = dot_cols(rows, table[...])
    return wide[: z.shape[0]] + wide[z.shape[0] :]


def pack(levels):
    lane = lax.broadcasted_iota(jnp.int32, (1, RANK), 1)
    return [jnp.where(lane < USED, levels[l], roll(levels[3], 96 - 32 * l, 1)) for l in range(3)]


def unpack(parts):
    lane = lax.broadcasted_iota(jnp.int32, (1, RANK), 1)
    last = jnp.where(lane < 64, roll(parts[1], 64, 1), roll(parts[2], 96, 1))
    return parts + [jnp.where(lane < 32, roll(parts[0], 32, 1), last)]


def roll(x, shift, axis):
    return pltpu.roll(x, shift % x.shape[axis], axis)


def kernel(
    bands, spread, east, north, rs, cs, cut, metric, table_in, tan_out, diag_out,
    spread_v, winds_v, rs_v, cs_v, cut_s, hm, table,
    grid, halo_out, halo_in, ybuf, yr, xb, cb, yc, zbuf, zr, eb, bz,
    tend, adj, gy,
    in_sem, halo_send, halo_recv, y_send, y_recv, c_send, c_recv, z_send, z_recv, b_send, b_recv,
):
    b = lax.axis_index("lat")
    i = lax.axis_index("lon")
    caps = POLAR // ROWS
    is_north = b == 0
    is_south = b == bands - 1
    polar = jnp.logical_or(b < caps, b >= bands - caps)
    above_polar = jnp.logical_or(b <= caps, is_south)
    below_polar = jnp.logical_or(b >= bands - caps - 1, is_north)
    near_polar = jnp.logical_or(above_polar, below_polar)
    across = lax.rem(i + LANES // 2, LANES)
    west = lax.rem(i + LANES - 1, LANES)
    east_lane = lax.rem(i + 1, LANES)
    nb = jnp.where(is_north, 0, b - 1)
    nl = jnp.where(is_north, across, i)
    sb = jnp.where(is_south, bands - 1, b + 1)
    sl = jnp.where(is_south, across, i)
    slot_n = jnp.where(is_north, 0, 1)
    slot_s = jnp.where(is_south, 1, 0)
    own_half = lax.rem(i, 2)
    edge_over = jnp.where(own_half == 0, is_north, is_south)
    over_pole = (is_north, is_south)
    outward = jnp.logical_and(b == bands - caps, own_half == 0)

    def plus(lane, d):
        return lax.rem(lane + d, LANES)

    load_spread = pltpu.make_async_copy(spread, spread_v, in_sem.at[0])
    load_rows = pltpu.make_async_copy(rs, rs_v, in_sem.at[1])
    load_cols = pltpu.make_async_copy(cs, cs_v, in_sem.at[2])
    load_metric = pltpu.make_async_copy(metric.at[b], hm, in_sem.at[4])
    load_cut = pltpu.make_async_copy(cut, cut_s, in_sem.at[5])

    def load_table(start, stop, sem):
        return pltpu.make_async_copy(table_in.at[start:stop], table.at[start:stop], in_sem.at[sem])

    load_forward = load_table(FORWARD, EVALUATE, 6)
    load_others = load_table(EVALUATE, TABLE_ROWS, 7)
    load_part = load_table(EVALUATE, TO_COEFS, 7)
    barrier = pltpu.get_barrier_semaphore()

    def greet(lat, lon):
        pl.semaphore_signal(barrier, inc=1, device_id=(lat, lon), device_id_type=MESH)

    greet(nb, nl)
    greet(sb, sl)

    @pl.when(polar)
    def _():
        for d in FAR_FIRST[:4]:
            greet(b, plus(i, d))

    greet(b, west)
    greet(b, east_lane)
    load_spread.start()
    load_rows.start()
    load_cols.start()
    pltpu.make_async_copy(east, winds_v.at[0], in_sem.at[3]).start()
    pltpu.make_async_copy(north, winds_v.at[1], in_sem.at[3]).start()
    load_metric.start()

    @pl.when(polar)
    def _():
        greet(b, across)
        load_forward.start()
        load_cut.start()

    @pl.when(jnp.logical_and(near_polar, jnp.logical_not(polar)))
    def _():
        load_part.start()

    load_rows.wait()
    load_cols.wait()
    load_spread.wait()
    grid[:, 8:24, 384:512] = jnp.zeros((PAIRS + 2 * LEV, ROWS, 128), F32)
    row_part = jnp.concatenate([rs_v[f] for f in range(FIELDS)], axis=0)
    row_part = (2 * row_part - 1).astype(F32).T
    for f in range(FIELDS):
        col_part = (2 * cs_v[f] - 1).astype(F32)
        for l in range(LEV):
            n = f * LEV + l
            grid[n, 8:24, 0:COLS] = spread_v[f, l] * (row_part[:, n : n + 1] * col_part[l : l + 1, :])

    @pl.when(polar)
    def _():
        load_others.start()

    pltpu.make_async_copy(winds_v, winds_v, in_sem.at[3]).wait()
    for w in range(2):
        for l in range(LEV):
            grid[PAIRS + w * LEV + l, 8:24, 0:COLS] = winds_v[w, l]

    def edge_rows(start, entries, rows):
        for s, row in enumerate(rows):
            for t in range(4):
                values = grid[entries, row, 128 * t : 128 * t + 128]
                if entries == slice(0, PAIRS):
                    halo_out[start[s] + t] = values
                else:
                    halo_out[start[s] + t // 2, 8 * (t % 2) : 8 * (t % 2) + 8, :] = values

    edge_rows((NEAR, NEAR + 4), slice(0, PAIRS), (8, 23))
    lane2 = lax.broadcasted_iota(jnp.int32, (1, 128), 1)
    for s, (start, shift) in enumerate(((0, 0), (384, COLS - 2 - 384))):
        ends = jnp.logical_and(lane2 >= shift, lane2 < shift + 2)
        parts = [
            roll(jnp.where(ends, grid[e, 8:24, start : start + 128], 0.0), 2 * e - shift, 1)
            for e in range(PAIRS + 2 * LEV)
        ]
        while len(parts) > 1:
            parts = [sum(parts[k : k + 2]) for k in range(0, len(parts), 2)]
        halo_out[SIDES + s] = parts[0]

    pl.semaphore_wait(barrier, 4 + jnp.where(polar, LANES - 3, 0))

    def remote(src, dst, send, recv, lat, lon):
        return pltpu.make_async_remote_copy(
            src_ref=src, dst_ref=dst, send_sem=send, recv_sem=recv, device_id=(lat, lon), device_id_type=MESH
        )

    def halo_copy(start, count, to, which, lat, lon):
        return remote(
            halo_out.at[start : start + count], halo_in.at[pl.ds(to, count)], halo_send, halo_recv.at[which], lat, lon
        )

    def halo_arrival(start, stop, which):
        return remote(
            halo_out.at[start:stop], halo_in.at[start:stop], halo_send, halo_recv.at[which], b, west
        )

    @pl.when(b < bands // 2)
    def _():
        halo_copy(NEAR, 4, NEAR + 4 * slot_n, 0, nb, nl).start()

    halo_copy(NEAR + 4, 4, NEAR + 4 * slot_s, 0, sb, sl).start()

    @pl.when(b >= bands // 2)
    def _():
        halo_copy(NEAR, 4, NEAR + 4 * slot_n, 0, nb, nl).start()

    halo_copy(SIDES, 1, SIDES + 1, 0, b, west).start()
    halo_copy(SIDES + 1, 1, SIDES, 0, b, east_lane).start()

    others = pl.ds(0, LANES - 1)

    def all_y(q):
        return remote(ybuf.at[q, others], yr.at[q, others], y_send.at[q], y_recv.at[q], b, west)

    def send_values(q, x):
        y = to_modes(x.reshape(PAIRS * ROWS, WIDE), table.at[FORWARD:EVALUATE])
        y = y.reshape(FIELDS, LEV, 2, 8, RANK)
        blocks = [
            jnp.concatenate([y[f, l, h] for f in range(FIELDS) for h in range(2)], axis=0) for l in range(LEV)
        ]
        for l, part in enumerate(pack(blocks)):
            ybuf[q, :, l] = part.reshape(LANES, 8, RANK)

        for d in FAR_FIRST:
            o = plus(i, d)
            remote(ybuf.at[q, o], yr.at[q, i], y_send.at[q], y_recv.at[q], b, o).start()

        yr[q, i] = ybuf[q, i]

    def c_copy(o):
        return remote(cb.at[o], yc.at[i], c_send, c_recv, b, o)

    def all_c():
        return remote(cb.at[others], yc.at[others], c_send, c_recv, b, west)

    def z_copy(q, j):
        return remote(zbuf.at[q, j], zr.at[q, i], z_send.at[q], z_recv.at[q], b, j)

    def all_z(q):
        return remote(zbuf.at[q, others], zr.at[q, others], z_send.at[q], z_recv.at[q], b, west)

    def edge_sends():
        slot = jnp.where(own_half == 0, slot_n, slot_s)
        lat = jnp.where(own_half == 0, nb, sb)

        def away(j, lon):
            remote(eb.at[j], bz.at[slot, i // 2], b_send, b_recv.at[slot], lat, lon).start()

        @pl.when(jnp.logical_not(edge_over))
        def _():
            for j in ANSWERS:
                away(j, j)

        @pl.when(edge_over)
        def _():
            for j in ANSWERS:
                lon = (j + LANES // 2) % LANES

                @pl.when(i != lon)
                def _():
                    away(j, lon)

                @pl.when(i == lon)
                def _():
                    pltpu.make_async_copy(eb.at[j], bz.at[slot, i // 2], b_recv.at[slot]).start()

    def own_rows(q):
        row = lax.broadcasted_iota(jnp.int32, (8, 128), 0)
        cutoff = jnp.zeros((8, 128), jnp.int32)
        for r in range(8):
            cutoff = jnp.where(row == r, cut_s[8 * own_half + r], cutoff)
        keeps = []
        for group in range(4):
            wave = waves_of(group, lax.broadcasted_iota(jnp.int32, (8, 128), 1))
            keep = jnp.where(wave > cutoff, 2.0 / (COLS * LANES), 0.0)
            keeps.append(jnp.concatenate([keep] * LEV, axis=0))
        all_y(q).wait_recv()
        levels = unpack([yr[q, :, l].reshape(LANES * 8, RANK) for l in range(LEV - 1)])
        if q == 1:
            edge_row = jnp.where(row == 7 * own_half, 1.0, 0.0)
            all_c().wait_recv()
            ends = jnp.concatenate([yc[j, 8:16, :] for j in range(LANES)], axis=0)
            ends = pltpu.roll(ends, lax.rem(128 - 2 * LEV * (i // 2), 128), 1)
            levels = [
                levels[l]
                + ends[:, 2 * l : 2 * l + 1] * hm[0:1, :]
                + ends[:, 2 * l + 1 : 2 * l + 2] * hm[1:2, :]
                + jnp.concatenate([edge_row * yc[j, l : l + 1, :] for j in range(LANES)], axis=0)
                for l in range(LEV)
            ]
        lanes = [
            jnp.concatenate([levels[l][8 * j : 8 * j + 8, :] for l in range(LEV)], axis=0) for j in range(LANES)
        ]
        coefs = [
            to_coefs(jnp.concatenate(pair, axis=1), table.at[TO_COEFS + 256 * group : TO_COEFS + 256 * (group + 1)])
            for group, pair in enumerate(over_lanes(lanes))
        ]
        kept = [coef * keep for coef, keep in zip(coefs, keeps)]
        backs = [
            from_coefs(coef, table.at[FROM_COEFS + 256 * group : FROM_COEFS + 256 * (group + 1)])
            for group, coef in enumerate(kept)
        ]
        pairs = [(back[:, :RANK], back[:, RANK:]) for back in backs]
        zs = [z.reshape(LEV, 8, RANK) for z in to_lanes(pairs)]
        for l, part in enumerate(pack([jnp.concatenate([z[l] for z in zs], axis=0) for l in range(LEV)])):
            zbuf[q, :, l] = part.reshape(LANES, 8, RANK)

        def edges():
            for j, z in enumerate(zs):
                edge = jnp.where(own_half == 0, z[:, 0, :], z[:, 7, :])
                eb[j] = edge if q == 0 else eb[j] + edge
            if q == 1:
                edge_sends()

        if q == 1:
            pl.when(outward)(edges)
        for j in ANSWERS:
            @pl.when(i != j)
            def _():
                z_copy(q, j).start()

        if q == 1:
            pl.when(jnp.logical_not(outward))(edges)
        else:
            edges()
        zr[q, i] = zbuf[q, i]

    def evaluate(z):
        return from_modes(z, table.at[EVALUATE : EVALUATE + 384], table.at[EVALUATE + 384 : TO_COEFS])

    def project(q, h):
        levels = unpack(
            [jnp.concatenate([zr[q, 2 * f + h, l] for f in range(FIELDS)], axis=0) for l in range(LEV - 1)]
        )
        z = jnp.concatenate(
            [levels[l][8 * f : 8 * f + 8, :] for f in range(FIELDS) for l in range(LEV)], axis=0
        )
        out = evaluate(z)
        return [[out[8 * (LEV * f + l) : 8 * (LEV * f + l + 1), :] for l in range(LEV)] for f in range(FIELDS)]

    def tendency_rows(h, l, at, half):
        lo = jnp.maximum(l - 1, 0)
        hi = jnp.minimum(l + 1, LEV - 1)
        ew = at(PAIRS + l, h)
        nw = at(PAIRS + LEV + l, h)
        mids, along_x, along_y = [], [], []
        for f in range(FIELDS):
            mid = at(f * LEV + l, h)
            mids.append(mid)
            along_x.append(half * (roll(mid, -1, 1) - roll(mid, 1, 1)))
            along_y.append(0.5 * (at(f * LEV + l, h + 1) - at(f * LEV + l, h - 1)))
        linked = (along_x[2], along_y[2], along_x[0] + along_y[1], None)
        out = []
        for f in range(FIELDS):
            mixed = at(f * LEV + lo, h) + at(f * LEV + hi, h) - 2.0 * mids[f]
            t = -(ew * along_x[f] + nw * along_y[f]) + mixing * mixed
            if linked[f] is not None:
                t = t - coupling * linked[f]
            out.append(time_step * t)
        return out

    def full_tendency():
        @pl.loop(0, LEV, unroll=True)
        def _(l):
            for h in (8, 16):
                half = jnp.concatenate([hm[h : h + 8, :]] * 4, axis=1)
                for f, t in enumerate(tendency_rows(h, l, lambda n, r: grid[n, r : r + 8, :], half)):
                    tend[f * LEV + l, h - 8 : h, :] = t

    def side_tendency():
        lane = lax.broadcasted_iota(jnp.int32, (1, 128), 1)
        late = jnp.logical_or(jnp.logical_or(lane == 65, lane == 66), lane == 127)

        def at(n, r):
            return jnp.where(lane < 2, grid[n, r : r + 8, 0:128], grid[n, r : r + 8, 384:512])

        @pl.loop(0, LEV, unroll=True)
        def _(l):
            for h in (8, 16):
                for f, t in enumerate(tendency_rows(h, l, at, hm[h : h + 8, :])):
                    n, rows = f * LEV + l, slice(h - 8, h)
                    tend[n, rows, 0:128] = jnp.where(lane == 0, t, tend[n, rows, 0:128])
                    tend[n, rows, 384:512] = jnp.where(late, t, tend[n, rows, 384:512])

    load_metric.wait()

    @pl.when(polar)
    def _():
        load_forward.wait()
        send_values(0, grid[0:PAIRS, 8:24, :])
        grid[0:PAIRS, 7:8, :] = jnp.zeros((PAIRS, 1, WIDE), F32)
        grid[0:PAIRS, 24:25, :] = jnp.zeros((PAIRS, 1, WIDE), F32)
        full_tendency()
        send_values(1, tend[...])

    edge_rows((REST + 4, REST + 11), slice(PAIRS, PAIRS + 2 * LEV), (8, 23))

    halo_arrival(NEAR, REST, 0).wait_recv()
    row16 = lax.broadcasted_iota(jnp.int32, (PAIRS, 1), 0)
    is_v = jnp.logical_and(row16 >= LEV, row16 < 2 * LEV)
    is_temp = jnp.logical_and(row16 >= 2 * LEV, row16 < 3 * LEV)

    def flip(s, minus):
        sign = jnp.where(row16 < 2 * LEV, -1.0, 1.0) * minus
        return jnp.where(over_pole[s], sign, 1.0)

    def row_link(x):
        return jnp.where(is_v, roll(x, -LEV, 0), jnp.where(is_temp, roll(x, LEV, 0), 0.0))

    def wind(buffer, s, w):
        base = REST + 7 * s + 4
        rows = [buffer[base + t // 2, 8 * (t % 2) + LEV * w : 8 * (t % 2) + LEV * (w + 1), :] for t in range(4)]
        return jnp.concatenate([jnp.concatenate(rows, axis=1)] * FIELDS, axis=0)

    def row_of(buffer, start):
        return jnp.concatenate([buffer[start + t] for t in range(4)], axis=1)

    @pl.when(polar)
    def _():
        added = []
        for s, sign in ((0, 0.5 * time_step), (1, -0.5 * time_step)):
            ghost = flip(s, 1.0) * row_of(halo_in, NEAR + 4 * s)
            added.append(sign * (wind(halo_out, s, 1) * ghost + coupling * row_link(ghost)))
            xb[s] = added[s]
        y = to_modes(jnp.concatenate(added, axis=0), table.at[FORWARD:EVALUATE])
        for s in range(2):
            for f in range(FIELDS):
                cb[2 * f + s, 0:LEV, :] = y[(s * FIELDS + f) * LEV : (s * FIELDS + f + 1) * LEV, :]
        ends = []
        for side, sign in ((0, -1.0), (1, 1.0)):
            came = halo_in[SIDES + side]
            along_x = (sign * hm[8:24, :]) * (roll(came, -1, 1) if side == 0 else came)
            mine = jnp.where(
                jnp.logical_and(lane2 >= 2 * PAIRS, lane2 < 2 * (PAIRS + LEV)), halo_out[SIDES + side], 0.0
            )
            ew = sum(roll(mine, 2 * LEV * f - 2 * PAIRS - side, 1) for f in range(FIELDS))
            linked = jnp.where(
                lane2 < 2 * LEV,
                roll(along_x, -4 * LEV, 1),
                jnp.where(
                    jnp.logical_and(lane2 >= 4 * LEV, lane2 < 6 * LEV), roll(along_x, 4 * LEV, 1), 0.0
                ),
            )
            ends.append(time_step * (-ew * along_x - coupling * linked))
        ends = jnp.where(lax.rem(lane2, 2) == 0, ends[0], roll(ends[1], 1, 1))
        for f in range(FIELDS):
            for h in range(2):
                cb[2 * f + h, 8:16, :] = ends[8 * h : 8 * h + 8, :]

        for d in FAR_FIRST:
            c_copy(plus(i, d)).start()

        yc[i] = cb[i]

    from_west = roll(halo_in[SIDES], 126, 1)
    from_east = roll(halo_in[SIDES + 1], COLS - 384, 1)
    both = jnp.where(jnp.logical_and(lane2 >= 66, lane2 < 114), from_east, from_west)
    in_halo = jnp.logical_or(jnp.logical_and(lane2 >= 66, lane2 < 68), lane2 >= 126)
    for e in range(PAIRS + 2 * LEV):
        grid[e, 8:24, 384:512] = jnp.where(in_halo, roll(both, -2 * e, 1), grid[e, 8:24, 384:512])
    edge_rows((REST, REST + 7), slice(0, PAIRS), (9, 22))
    for s, near in enumerate((8, 23)):
        halo_out[REST + 7 * s + 6] = grid[0:PAIRS, near, 384:512]
    halo_copy(REST, 7, REST + 7 * slot_n, 1, nb, nl).start()
    halo_copy(REST + 7, 7, REST + 7 * slot_s, 1, sb, sl).start()

    @pl.when(polar)
    def _():
        load_cut.wait()
        load_others.wait()
        own_rows(0)

    @pl.when(jnp.logical_and(polar, b < bands // 2))
    def _():
        own_rows(1)

    halo_arrival(REST, BLOCKS, 1).wait_recv()
    edge_row = (7, 24)
    edge_probe = []
    for s in range(2):
        edge_probe.append(
            jnp.concatenate([halo_in[NEAR + 4 * s + t] for t in range(3)] + [halo_in[REST + 7 * s + 6]], axis=1)
        )
        grid[0:PAIRS, edge_row[s], :] = flip(s, 1.0) * edge_probe[s]

    @pl.when(polar)
    def _():
        for s, row in ((0, 0), (1, 15)):
            tend[:, row, :] = tend[:, row, :] + xb[s]
        side_tendency()

    @pl.when(jnp.logical_not(polar))
    def _():
        full_tendency()

    def edge_weights(s, a):
        return -wind(halo_in, s, 1) * a - coupling * row_link(a)

    for s, inward in ((0, 1.0), (1, -1.0)):
        mid = edge_probe[s]
        half = jnp.concatenate([hm[edge_row[s] : edge_row[s] + 1, :]] * 4, axis=1)
        along_x = half * (roll(mid, -1, 1) - roll(mid, 1, 1))
        turn = jnp.where(over_pole[s], -0.5 * inward, 0.5 * inward)
        along_y = turn * (flip(s, 1.0) * row_of(halo_out, NEAR + 4 * s) - row_of(halo_in, REST + 7 * s))
        linked = jnp.where(row16 < LEV, roll(along_x, -2 * LEV, 0), row_link(along_y))
        linked = linked + jnp.where(is_temp, roll(along_x, 2 * LEV, 0), 0.0)
        up = jnp.where(lax.rem(row16, LEV) == 0, mid, roll(mid, 1, 0))
        down = jnp.where(lax.rem(row16, LEV) == LEV - 1, mid, roll(mid, -1, 0))
        t = -(wind(halo_in, s, 0) * along_x + wind(halo_in, s, 1) * along_y) - coupling * linked
        a = mid + time_step * (t + mixing * (up + down - 2.0 * mid))
        gy[0:PAIRS, edge_row[s], :] = flip(s, -1.0) * edge_weights(s, a)

    @pl.when(jnp.logical_and(polar, b >= bands // 2))
    def _():
        own_rows(1)

    def row_weights(a, nw):
        return (
            -nw * a[0],
            -nw * a[1] - coupling * a[2],
            -nw * a[2] - coupling * a[1],
            -nw * a[3],
        )

    def put_weights(l, h, a):
        for f, weight in enumerate(row_weights(a, grid[PAIRS + LEV + l, h : h + 8, :])):
            gy[f * LEV + l, h : h + 8, :] = weight

    @pl.when(polar)
    def _():
        all_z(0).wait_recv()
        for h in (8, 16):
            taken = project(0, h // 8 - 1)
            for l in range(LEV):
                for f in range(FIELDS):
                    n, rows = f * LEV + l, slice(h - 8, h)
                    adj[n, rows, :] = grid[n, h : h + 8, :] + tend[n, rows, :] - taken[f][l]
        all_z(1).wait_recv()
        for h in (8, 16):
            taken = project(1, h // 8 - 1)
            for l in range(LEV):
                a = []
                for f in range(FIELDS):
                    n, rows = f * LEV + l, slice(h - 8, h)
                    change = tend[n, rows, :] - taken[f][l]
                    tend[n, rows, :] = change
                    tan_out[f, l, rows, :] = (grid[n, h : h + 8, :] + change)[:, :COLS]
                    a.append(adj[n, rows, :] - taken[f][l])
                    adj[n, rows, :] = a[f]
                put_weights(l, h, a)

    @pl.when(jnp.logical_not(polar))
    def _():
        @pl.loop(0, LEV, unroll=True)
        def _(l):
            for h in (8, 16):
                a = []
                for f in range(FIELDS):
                    n, rows = f * LEV + l, slice(h - 8, h)
                    a.append(grid[n, h : h + 8, :] + tend[n, rows, :])
                    tan_out[f, l, rows, :] = a[f][:, :COLS]
                    adj[n, rows, :] = a[f]
                put_weights(l, h, a)

    @pl.loop(0, LEV, unroll=True)
    def _(l):
        lo = jnp.maximum(l - 1, 0)
        hi = jnp.minimum(l + 1, LEV - 1)
        for h in (8, 16):
            rows = slice(h - 8, h)
            half = jnp.concatenate([hm[h : h + 8, :]] * 4, axis=1)
            ew = grid[PAIRS + l, h : h + 8, :]
            a = [adj[f * LEV + l, rows, :] for f in range(FIELDS)]
            col_weights = (
                -ew * a[0] - coupling * a[2],
                -ew * a[1],
                -ew * a[2] - coupling * a[0],
                -ew * a[3],
            )
            for f in range(FIELDS):
                n = f * LEV + l
                back = half * (roll(col_weights[f], 1, 1) - roll(col_weights[f], -1, 1))
                back = back + 0.5 * (gy[n, h - 1 : h + 7, :] - gy[n, h + 1 : h + 9, :])
                back = back + mixing * (adj[f * LEV + lo, rows, :] + adj[f * LEV + hi, rows, :] - 2.0 * a[f])
                diag = grid[n, h : h + 8, :] * (tend[n, rows, :] + time_step * back)
                diag_out[f, l, rows, :] = diag[:, :COLS]

    @pl.when(jnp.logical_and(near_polar, jnp.logical_not(polar)))
    def _():
        load_part.wait()

    for s, wanted in enumerate((above_polar, below_polar)):
        @pl.when(wanted)
        def _():
            row = 15 * s
            north_wind = wind(halo_in, s, 1)
            factor = ((0.5, -0.5)[s] * time_step) * grid[0:PAIRS, 8 + row, :] * flip(s, -1.0)
            before = [diag_out[f, :, row, :] for f in range(FIELDS)]
            remote(bz.at[s], bz.at[s], b_send, b_recv.at[s], nb, nl).wait_recv()
            taken = evaluate(jnp.concatenate([bz[s, f] for f in range(FIELDS)], axis=0))
            more = factor * (north_wind * taken + coupling * row_link(taken))
            for f in range(FIELDS):
                diag_out[f, :, row, :] = before[f] + more[f * LEV : (f + 1) * LEV, :COLS]

    halo_arrival(0, BLOCKS, 0).wait_send()

    @pl.when(polar)
    def _():
        all_c().wait_send()
        for q in range(2):
            all_y(q).wait_send()
            all_z(q).wait_send()

        @pl.when(edge_over)
        def _():
            remote(eb.at[others], eb.at[others], b_send, b_recv.at[0], b, west).wait_send()

        @pl.when(jnp.logical_not(edge_over))
        def _():
            remote(eb, eb, b_send, b_recv.at[0], b, west).wait_send()


def hand_out(tan_in, diag_in, tan_out, diag_out, sem):
    copies = [
        pltpu.make_async_copy(src, dst, sem.at[n])
        for n, (src, dst) in enumerate(((tan_in, tan_out), (diag_in, diag_out)))
    ]
    for copy in copies:
        copy.start()
    for copy in copies:
        copy.wait()


def per_device(bands, row_signs, col_signs, spread, east_wind, north_wind, cutoffs):
    any_spec = pl.BlockSpec(memory_space=pl.ANY)
    out = jax.ShapeDtypeStruct((FIELDS, LEV, ROWS, COLS), F32)
    tables = [jnp.asarray(half_metric(bands)), jnp.asarray(mode_factors())]
    operands = (spread, east_wind, north_wind, row_signs, col_signs, cutoffs, *tables)
    vmem = pltpu.VMEM
    dma = pltpu.SemaphoreType.DMA
    held = pltpu.VMEM(out.shape, F32)
    results = pl.pallas_call(
        functools.partial(kernel, bands),
        out_shape=(held, held),
        in_specs=[any_spec] * 8,
        out_specs=(pl.BlockSpec(memory_space=pltpu.VMEM),) * 2,
        scratch_shapes=[
            vmem((FIELDS, LEV, ROWS, COLS), F32),
            vmem((2, LEV, ROWS, COLS), F32),
            vmem((FIELDS, LEV, ROWS), jnp.int32),
            vmem((FIELDS, LEV, COLS), jnp.int32),
            pltpu.SMEM((ROWS,), jnp.int32),
            vmem((32, 128), F32),
            vmem((TABLE_ROWS, 2 * RANK), BF16),
            vmem((PAIRS + 2 * LEV, 32, WIDE), F32),
            vmem((BLOCKS, 16, 128), F32),
            vmem((BLOCKS, 16, 128), F32),
            vmem((2, LANES, LEV - 1, 8, RANK), F32),
            vmem((2, LANES, LEV - 1, 8, RANK), F32),
            vmem((2, PAIRS, WIDE), F32),
            vmem((LANES, 16, RANK), F32),
            vmem((LANES, 16, RANK), F32),
            vmem((2, LANES, LEV - 1, 8, RANK), F32),
            vmem((2, LANES, LEV - 1, 8, RANK), F32),
            vmem((LANES, LEV, RANK), F32),
            vmem((2, FIELDS, LEV, RANK), F32),
            vmem((PAIRS, ROWS, WIDE), F32),
            vmem((PAIRS, ROWS, WIDE), F32),
            vmem((PAIRS, 32, WIDE), F32),
            dma((8,)),
            dma,
            dma((2,)),
            dma((2,)),
            dma((2,)),
            dma,
            dma,
            dma((2,)),
            dma((2,)),
            dma,
            dma((2,)),
        ],
        compiler_params=pltpu.CompilerParams(
            collective_id=0, has_side_effects=True, vmem_limit_bytes=32 * 2**20
        ),
        cost_estimate=pl.CostEstimate(flops=10**9, bytes_accessed=4 * 10**6, transcendentals=0),
    )(*(pltpu.with_memory_space_constraint(x, pltpu.HBM) for x in operands))
    return pl.pallas_call(
        hand_out,
        out_shape=(out, out),
        in_specs=[any_spec] * 2,
        out_specs=(any_spec, any_spec),
        scratch_shapes=[dma((2,))],
        compiler_params=pltpu.CompilerParams(vmem_limit_bytes=2**20),
    )(*(pltpu.with_memory_space_constraint(x, pltpu.VMEM) for x in results))


def solution(mesh):
    return jax.shard_map(
        functools.partial(per_device, mesh.shape["lat"]),
        mesh=mesh,
        in_specs=(
            P(None, None, "lat"),
            P(None, None, "lon"),
            P(None, None, "lat", "lon"),
            P(None, "lat", "lon"),
            P(None, "lat", "lon"),
            P("lat"),
        ),
        out_specs=(P(None, None, "lat", "lon"), P(None, None, "lat", "lon")),
        check_vma=False,
    )
```

```python
import functools

import jax
import jax.numpy as jnp
import ml_dtypes
import numpy as np
from jax import lax
from jax.experimental import pallas as pl
from jax.experimental.pallas import tpu as pltpu
from jax.sharding import PartitionSpec as P

KTOP = 256
POLAR = 32
RANK = 128
USED = 96
ROWS = 16
COLS = 450
WIDE = 512
LANES = 8
FIELDS = 4
LEV = 4
PAIRS = FIELDS * LEV

time_step = 0.5
coupling = 0.5
mixing = 0.2
metric_cap = 4.0

FORWARD, EVALUATE, TO_COEFS, FROM_COEFS, TABLE_ROWS = 0, 512, 1280, 2304, 3328
NEAR, SIDES, REST, BLOCKS = 0, 8, 10, 24

FAR_FIRST = (6, 2, 5, 3, 7, 1, 4)
ANSWERS = (0, 4, 1, 3, 2, 7, 5, 6)

MESH = pl.DeviceIdType.MESH
F32 = jnp.float32
BF16 = jnp.bfloat16


def split_table(table):
    high = table.astype(ml_dtypes.bfloat16)
    low = (table - high.astype(np.float64)).astype(ml_dtypes.bfloat16)
    return high, low


def waves_of(group, lane_index):
    place = lane_index % 64
    second = place // 32
    other = (8 - group) if group else 4
    residue = group + second * (other - group)
    return 8 * (place % 32) + residue + (8 * (1 - second) if group == 0 else 0)


@functools.lru_cache(None)
def mode_factors():
    total = COLS * LANES
    size = COLS + 2
    place = np.arange(size, dtype=np.float64)
    width = (KTOP + 0.5) / total
    diag = ((size - 1 - 2 * place) / 2) ** 2 * np.cos(2 * np.pi * width)
    side = place[1:] * (size - place[1:]) / 2
    vectors = np.linalg.eigh(np.diag(diag) + np.diag(side, 1) + np.diag(side, -1))[1]
    basis = np.concatenate([vectors[:, ::-1][:, :USED], np.zeros((size, RANK - USED))], axis=1)
    basis = basis * np.where(basis[size // 2] < 0, -1.0, 1.0)
    weights = []
    for group in range(4):
        waves = waves_of(group, np.arange(64))
        angle = 2 * np.pi / total * ((np.arange(size)[:, None] - 1) * waves[None, :] % total)
        alpha, beta = basis.T @ np.cos(angle), basis.T @ np.sin(angle)
        if group:
            sign = np.where(np.arange(64) < 32, 1.0, -1.0)
            top, low = (alpha, beta), (sign * beta, -sign * alpha)
        else:
            use = np.where(np.arange(64) < 32, 1.0, 0.0)
            top, low = (use * alpha, use * beta), ((1 - use) * alpha, (1 - use) * beta)
        weights.append(np.concatenate([np.concatenate(top, axis=1), np.concatenate(low, axis=1)], axis=0))
    weights = np.round(np.stack(weights) * 2.0**22) / 2.0**22
    wide = np.zeros((RANK, WIDE))
    wide[:, : COLS + 1] = basis[1:].T
    wide[:, WIDE - 1] = basis[0]
    wide = np.round(wide * 2.0**26) / 2.0**26
    wide_h, wide_l = split_table(wide)
    own = np.where(np.arange(WIDE)[:, None] < COLS, 1, 0).astype(ml_dtypes.bfloat16)
    high, low = split_table(weights)
    back = np.concatenate([np.swapaxes(part, 1, 2) for part in (high, low)], axis=1)
    evaluate = np.concatenate([wide_h, wide_l, wide_h], axis=0)
    return np.concatenate(
        [
            np.concatenate([wide_h.T * own, wide_l.T * own], axis=1),
            evaluate[:, : WIDE // 2],
            evaluate[:, WIDE // 2 :],
            np.concatenate([high, low], axis=2).reshape(-1, 2 * RANK),
            back.reshape(-1, 2 * RANK),
        ],
        axis=0,
    )


ROOT = float(np.sqrt(0.5))


def over_lanes(y):
    s = [y[j] + y[j + 4] for j in range(4)]
    d = [y[j] - y[j + 4] for j in range(4)]
    even, odd = s[0] + s[2], s[1] + s[3]
    minus, plus = ROOT * (d[1] - d[3]), ROOT * (d[1] + d[3])
    return [
        (even + odd, even - odd),
        (d[0] + minus, -(d[2] + plus)),
        (s[0] - s[2], s[3] - s[1]),
        (d[0] - minus, d[2] - plus),
    ]


def to_lanes(pairs):
    (y0, y4), (u1, v1), (u2, v2), (u3, v3) = pairs
    even, odd = y0 + y4, y0 - y4
    s = [even + u2, odd - v2, even - u2, odd + v2]
    du, sv = ROOT * (u1 - u3), ROOT * (v1 + v3)
    d = [u1 + u3, du - sv, v3 - v1, -du - sv]
    return [s[j] + d[j] for j in range(4)] + [s[j] - d[j] for j in range(4)]


@functools.lru_cache(None)
def half_metric(bands):
    total = bands * ROWS
    rows = np.clip(np.arange(bands)[:, None] * ROWS - 8 + np.arange(32)[None, :], 0, total - 1)
    metric = np.minimum(1.0 / np.cos(np.pi * ((rows + 0.5) / total - 0.5)), metric_cap)
    table = np.broadcast_to((0.5 * metric).astype(np.float32)[:, :, None], (bands, 32, 128)).copy()
    forward = mode_factors()[FORWARD : FORWARD + WIDE].astype(np.float32)
    for row, col in enumerate((0, COLS - 1)):
        table[:, row] = forward[col, :RANK] + forward[col, RANK:]
    return table


def dot_cols(a, b):
    return lax.dot_general(a, b, (((1,), (0,)), ((), ())), preferred_element_type=F32)


def split(x):
    high = x.astype(BF16)
    return high, (x - high.astype(F32)).astype(BF16)


def to_modes(x, table):
    xh, xl = split(x)
    half = table.shape[1] // 2
    wide = dot_cols(xh, table[...])
    return wide[:, :half] + wide[:, half:] + dot_cols(xl, table[:, 0:half])


def from_modes(z, *tables):
    zh, zl = split(z)
    three = jnp.concatenate([zh, zh, zl], axis=1)
    return jnp.concatenate([dot_cols(three, table[...]) for table in tables], axis=1)


def to_coefs(x, table):
    rows = x.shape[0]
    wide = dot_cols(jnp.concatenate(split(x), axis=0), table[...])
    half = wide.shape[1] // 2
    return wide[:rows, :half] + wide[:rows, half:] + wide[rows:, :half]


def from_coefs(z, table):
    zh, zl = split(z)
    rows = jnp.concatenate([jnp.concatenate([zh, zh], axis=1), jnp.concatenate([zl, jnp.zeros_like(zl)], axis=1)], axis=0)
    wide = dot_cols(rows, table[...])
    return wide[: z.shape[0]] + wide[z.shape[0] :]


def pack(levels):
    lane = lax.broadcasted_iota(jnp.int32, (1, RANK), 1)
    return [jnp.where(lane < USED, levels[l], roll(levels[3], 96 - 32 * l, 1)) for l in range(3)]


def unpack(parts):
    lane = lax.broadcasted_iota(jnp.int32, (1, RANK), 1)
    last = jnp.where(lane < 64, roll(parts[1], 64, 1), roll(parts[2], 96, 1))
    return parts + [jnp.where(lane < 32, roll(parts[0], 32, 1), last)]


def roll(x, shift, axis):
    return pltpu.roll(x, shift % x.shape[axis], axis)


def kernel(
    bands, spread, east, north, rs, cs, cut, metric, table_in, tan_out, diag_out,
    spread_v, winds_v, rs_v, cs_v, cut_s, hm, table,
    grid, halo_out, halo_in, ybuf, yr, xb, cb, yc, zbuf, zr, eb, bz,
    tend, adj, gy,
    in_sem, halo_send, halo_recv, y_send, y_recv, c_send, c_recv, z_send, z_recv, b_send, b_recv,
):
    b = lax.axis_index("lat")
    i = lax.axis_index("lon")
    caps = POLAR // ROWS
    is_north = b == 0
    is_south = b == bands - 1
    northern = b < bands // 2
    polar = jnp.logical_or(b < caps, b >= bands - caps)
    above_polar = jnp.logical_or(b <= caps, is_south)
    below_polar = jnp.logical_or(b >= bands - caps - 1, is_north)
    near_polar = jnp.logical_or(above_polar, below_polar)
    across = lax.rem(i + LANES // 2, LANES)
    west = lax.rem(i + LANES - 1, LANES)
    east_lane = lax.rem(i + 1, LANES)
    nb = jnp.where(is_north, 0, b - 1)
    nl = jnp.where(is_north, across, i)
    sb = jnp.where(is_south, bands - 1, b + 1)
    sl = jnp.where(is_south, across, i)
    slot_n = jnp.where(is_north, 0, 1)
    slot_s = jnp.where(is_south, 1, 0)
    own_half = lax.rem(i, 2)
    edge_over = jnp.where(own_half == 0, is_north, is_south)
    over_pole = (is_north, is_south)
    outward = jnp.logical_and(b == bands - caps, own_half == 0)

    def plus(lane, d):
        return lax.rem(lane + d, LANES)

    load_spread = pltpu.make_async_copy(spread, spread_v, in_sem.at[0])
    load_rows = pltpu.make_async_copy(rs, rs_v, in_sem.at[1])
    load_cols = pltpu.make_async_copy(cs, cs_v, in_sem.at[2])
    load_metric = pltpu.make_async_copy(metric.at[b], hm, in_sem.at[4])
    load_cut = pltpu.make_async_copy(cut, cut_s, in_sem.at[5])

    def load_table(start, stop, sem):
        return pltpu.make_async_copy(table_in.at[start:stop], table.at[start:stop], in_sem.at[sem])

    load_forward = load_table(FORWARD, EVALUATE, 6)
    load_others = load_table(EVALUATE, TABLE_ROWS, 7)
    load_part = load_table(EVALUATE, TO_COEFS, 7)
    barrier = pltpu.get_barrier_semaphore()

    def greet(lat, lon):
        pl.semaphore_signal(barrier, inc=1, device_id=(lat, lon), device_id_type=MESH)

    greet(nb, nl)
    greet(sb, sl)

    @pl.when(polar)
    def _():
        for d in FAR_FIRST[:4]:
            greet(b, plus(i, d))

    greet(b, west)
    greet(b, east_lane)
    load_spread.start()
    load_rows.start()
    load_cols.start()
    pltpu.make_async_copy(east, winds_v.at[0], in_sem.at[3]).start()
    pltpu.make_async_copy(north, winds_v.at[1], in_sem.at[3]).start()
    load_metric.start()

    @pl.when(polar)
    def _():
        greet(b, across)
        load_forward.start()
        load_cut.start()

    @pl.when(jnp.logical_and(near_polar, jnp.logical_not(polar)))
    def _():
        load_part.start()

    load_rows.wait()
    load_cols.wait()
    load_spread.wait()
    grid[:, 8:24, 384:512] = jnp.zeros((PAIRS + 2 * LEV, ROWS, 128), F32)
    row_part = jnp.concatenate([rs_v[f] for f in range(FIELDS)], axis=0)
    row_part = (2 * row_part - 1).astype(F32).T
    for f in range(FIELDS):
        col_part = (2 * cs_v[f] - 1).astype(F32)
        for l in range(LEV):
            n = f * LEV + l
            grid[n, 8:24, 0:COLS] = spread_v[f, l] * (row_part[:, n : n + 1] * col_part[l : l + 1, :])

    @pl.when(polar)
    def _():
        load_others.start()

    pltpu.make_async_copy(winds_v, winds_v, in_sem.at[3]).wait()
    for w in range(2):
        for l in range(LEV):
            grid[PAIRS + w * LEV + l, 8:24, 0:COLS] = winds_v[w, l]

    def edge_rows(start, entries, rows):
        for s, row in enumerate(rows):
            for t in range(4):
                values = grid[entries, row, 128 * t : 128 * t + 128]
                if entries == slice(0, PAIRS):
                    halo_out[start[s] + t] = values
                else:
                    halo_out[start[s] + t // 2, 8 * (t % 2) : 8 * (t % 2) + 8, :] = values

    edge_rows((NEAR, NEAR + 4), slice(0, PAIRS), (8, 23))
    lane2 = lax.broadcasted_iota(jnp.int32, (1, 128), 1)
    for s, (start, shift) in enumerate(((0, 0), (384, COLS - 2 - 384))):
        ends = jnp.logical_and(lane2 >= shift, lane2 < shift + 2)
        parts = [
            roll(jnp.where(ends, grid[e, 8:24, start : start + 128], 0.0), 2 * e - shift, 1)
            for e in range(PAIRS + 2 * LEV)
        ]
        while len(parts) > 1:
            parts = [sum(parts[k : k + 2]) for k in range(0, len(parts), 2)]
        halo_out[SIDES + s] = parts[0]

    def tendency_rows(h, l, at, half):
        lo = jnp.maximum(l - 1, 0)
        hi = jnp.minimum(l + 1, LEV - 1)
        ew = at(PAIRS + l, h)
        nw = at(PAIRS + LEV + l, h)
        mids, along_x, along_y = [], [], []
        for f in range(FIELDS):
            mid = at(f * LEV + l, h)
            mids.append(mid)
            along_x.append(half * (roll(mid, -1, 1) - roll(mid, 1, 1)))
            along_y.append(0.5 * (at(f * LEV + l, h + 1) - at(f * LEV + l, h - 1)))
        linked = (along_x[2], along_y[2], along_x[0] + along_y[1], None)
        out = []
        for f in range(FIELDS):
            mixed = at(f * LEV + lo, h) + at(f * LEV + hi, h) - 2.0 * mids[f]
            t = -(ew * along_x[f] + nw * along_y[f]) + mixing * mixed
            if linked[f] is not None:
                t = t - coupling * linked[f]
            out.append(time_step * t)
        return out

    def full_tendency():
        @pl.loop(0, LEV, unroll=True)
        def _(l):
            for h in (8, 16):
                half = jnp.concatenate([hm[h : h + 8, :]] * 4, axis=1)
                for f, t in enumerate(tendency_rows(h, l, lambda n, r: grid[n, r : r + 8, :], half)):
                    tend[f * LEV + l, h - 8 : h, :] = t

    def side_tendency():
        lane = lax.broadcasted_iota(jnp.int32, (1, 128), 1)
        late = jnp.logical_or(jnp.logical_or(lane == 65, lane == 66), lane == 127)

        def at(n, r):
            return jnp.where(lane < 2, grid[n, r : r + 8, 0:128], grid[n, r : r + 8, 384:512])

        @pl.loop(0, LEV, unroll=True)
        def _(l):
            for h in (8, 16):
                for f, t in enumerate(tendency_rows(h, l, at, hm[h : h + 8, :])):
                    n, rows = f * LEV + l, slice(h - 8, h)
                    tend[n, rows, 0:128] = jnp.where(lane == 0, t, tend[n, rows, 0:128])
                    tend[n, rows, 384:512] = jnp.where(late, t, tend[n, rows, 384:512])

    def values(q, x):
        y = to_modes(x.reshape(PAIRS * ROWS, WIDE), table.at[FORWARD:EVALUATE])
        y = y.reshape(FIELDS, LEV, 2, 8, RANK)
        blocks = [
            jnp.concatenate([y[f, l, h] for f in range(FIELDS) for h in range(2)], axis=0) for l in range(LEV)
        ]
        for l, part in enumerate(pack(blocks)):
            ybuf[q, :, l] = part.reshape(LANES, 8, RANK)

    def probe_values():
        values(0, grid[0:PAIRS, 8:24, :])

    def local_tendency_values():
        grid[0:PAIRS, 7:8, :] = jnp.zeros((PAIRS, 1, WIDE), F32)
        grid[0:PAIRS, 24:25, :] = jnp.zeros((PAIRS, 1, WIDE), F32)
        full_tendency()
        values(1, tend[...])

    load_metric.wait()

    @pl.when(jnp.logical_and(polar, northern))
    def _():
        load_forward.wait()
        probe_values()
        local_tendency_values()

    pl.semaphore_wait(barrier, 4 + jnp.where(polar, LANES - 3, 0))

    def remote(src, dst, send, recv, lat, lon):
        return pltpu.make_async_remote_copy(
            src_ref=src, dst_ref=dst, send_sem=send, recv_sem=recv, device_id=(lat, lon), device_id_type=MESH
        )

    def halo_copy(start, count, to, which, lat, lon):
        return remote(
            halo_out.at[start : start + count], halo_in.at[pl.ds(to, count)], halo_send, halo_recv.at[which], lat, lon
        )

    def halo_arrival(start, stop, which):
        return remote(
            halo_out.at[start:stop], halo_in.at[start:stop], halo_send, halo_recv.at[which], b, west
        )

    @pl.when(northern)
    def _():
        halo_copy(NEAR, 4, NEAR + 4 * slot_n, 0, nb, nl).start()

    halo_copy(NEAR + 4, 4, NEAR + 4 * slot_s, 0, sb, sl).start()

    @pl.when(jnp.logical_not(northern))
    def _():
        halo_copy(NEAR, 4, NEAR + 4 * slot_n, 0, nb, nl).start()

    halo_copy(SIDES, 1, SIDES + 1, 0, b, west).start()
    halo_copy(SIDES + 1, 1, SIDES, 0, b, east_lane).start()

    others = pl.ds(0, LANES - 1)

    def all_y(q):
        return remote(ybuf.at[q, others], yr.at[q, others], y_send.at[q], y_recv.at[q], b, west)

    def send_values(q):
        for d in FAR_FIRST:
            o = plus(i, d)
            remote(ybuf.at[q, o], yr.at[q, i], y_send.at[q], y_recv.at[q], b, o).start()

        yr[q, i] = ybuf[q, i]

    def c_copy(o):
        return remote(cb.at[o], yc.at[i], c_send, c_recv, b, o)

    def all_c():
        return remote(cb.at[others], yc.at[others], c_send, c_recv, b, west)

    def z_copy(q, j):
        return remote(zbuf.at[q, j], zr.at[q, i], z_send.at[q], z_recv.at[q], b, j)

    def all_z(q):
        return remote(zbuf.at[q, others], zr.at[q, others], z_send.at[q], z_recv.at[q], b, west)

    def edge_sends():
        slot = jnp.where(own_half == 0, slot_n, slot_s)
        lat = jnp.where(own_half == 0, nb, sb)

        def away(j, lon):
            remote(eb.at[j], bz.at[slot, i // 2], b_send, b_recv.at[slot], lat, lon).start()

        @pl.when(jnp.logical_not(edge_over))
        def _():
            for j in ANSWERS:
                away(j, j)

        @pl.when(edge_over)
        def _():
            for j in ANSWERS:
                lon = (j + LANES // 2) % LANES

                @pl.when(i != lon)
                def _():
                    away(j, lon)

                @pl.when(i == lon)
                def _():
                    pltpu.make_async_copy(eb.at[j], bz.at[slot, i // 2], b_recv.at[slot]).start()

    def own_rows(q):
        row = lax.broadcasted_iota(jnp.int32, (8, 128), 0)
        cutoff = jnp.zeros((8, 128), jnp.int32)
        for r in range(8):
            cutoff = jnp.where(row == r, cut_s[8 * own_half + r], cutoff)
        keeps = []
        for group in range(4):
            wave = waves_of(group, lax.broadcasted_iota(jnp.int32, (8, 128), 1))
            keep = jnp.where(wave > cutoff, 2.0 / (COLS * LANES), 0.0)
            keeps.append(jnp.concatenate([keep] * LEV, axis=0))
        all_y(q).wait_recv()
        levels = unpack([yr[q, :, l].reshape(LANES * 8, RANK) for l in range(LEV - 1)])
        if q == 1:
            edge_row = jnp.where(row == 7 * own_half, 1.0, 0.0)
            all_c().wait_recv()
            ends = jnp.concatenate([yc[j, 8:16, :] for j in range(LANES)], axis=0)
            ends = pltpu.roll(ends, lax.rem(128 - 2 * LEV * (i // 2), 128), 1)
            levels = [
                levels[l]
                + ends[:, 2 * l : 2 * l + 1] * hm[0:1, :]
                + ends[:, 2 * l + 1 : 2 * l + 2] * hm[1:2, :]
                + jnp.concatenate([edge_row * yc[j, l : l + 1, :] for j in range(LANES)], axis=0)
                for l in range(LEV)
            ]
        lanes = [
            jnp.concatenate([levels[l][8 * j : 8 * j + 8, :] for l in range(LEV)], axis=0) for j in range(LANES)
        ]
        coefs = [
            to_coefs(jnp.concatenate(pair, axis=1), table.at[TO_COEFS + 256 * group : TO_COEFS + 256 * (group + 1)])
            for group, pair in enumerate(over_lanes(lanes))
        ]
        kept = [coef * keep for coef, keep in zip(coefs, keeps)]
        backs = [
            from_coefs(coef, table.at[FROM_COEFS + 256 * group : FROM_COEFS + 256 * (group + 1)])
            for group, coef in enumerate(kept)
        ]
        pairs = [(back[:, :RANK], back[:, RANK:]) for back in backs]
        zs = [z.reshape(LEV, 8, RANK) for z in to_lanes(pairs)]
        for l, part in enumerate(pack([jnp.concatenate([z[l] for z in zs], axis=0) for l in range(LEV)])):
            zbuf[q, :, l] = part.reshape(LANES, 8, RANK)

        def edges():
            for j, z in enumerate(zs):
                edge = jnp.where(own_half == 0, z[:, 0, :], z[:, 7, :])
                eb[j] = edge if q == 0 else eb[j] + edge
            if q == 1:
                edge_sends()

        if q == 1:
            pl.when(outward)(edges)
        for j in ANSWERS:
            @pl.when(i != j)
            def _():
                z_copy(q, j).start()

        if q == 1:
            pl.when(jnp.logical_not(outward))(edges)
        else:
            edges()
        zr[q, i] = zbuf[q, i]

    def evaluate(z):
        return from_modes(z, table.at[EVALUATE : EVALUATE + 384], table.at[EVALUATE + 384 : TO_COEFS])

    def project(q, h):
        levels = unpack(
            [jnp.concatenate([zr[q, 2 * f + h, l] for f in range(FIELDS)], axis=0) for l in range(LEV - 1)]
        )
        z = jnp.concatenate(
            [levels[l][8 * f : 8 * f + 8, :] for f in range(FIELDS) for l in range(LEV)], axis=0
        )
        out = evaluate(z)
        return [[out[8 * (LEV * f + l) : 8 * (LEV * f + l + 1), :] for l in range(LEV)] for f in range(FIELDS)]


    @pl.when(jnp.logical_and(polar, northern))
    def _():
        send_values(0)
        send_values(1)

    @pl.when(jnp.logical_and(polar, jnp.logical_not(northern)))
    def _():
        load_forward.wait()
        probe_values()
        send_values(0)
        local_tendency_values()
        send_values(1)

    edge_rows((REST + 4, REST + 11), slice(PAIRS, PAIRS + 2 * LEV), (8, 23))

    halo_arrival(NEAR, REST, 0).wait_recv()
    row16 = lax.broadcasted_iota(jnp.int32, (PAIRS, 1), 0)
    is_v = jnp.logical_and(row16 >= LEV, row16 < 2 * LEV)
    is_temp = jnp.logical_and(row16 >= 2 * LEV, row16 < 3 * LEV)

    def flip(s, minus):
        sign = jnp.where(row16 < 2 * LEV, -1.0, 1.0) * minus
        return jnp.where(over_pole[s], sign, 1.0)

    def row_link(x):
        return jnp.where(is_v, roll(x, -LEV, 0), jnp.where(is_temp, roll(x, LEV, 0), 0.0))

    def wind(buffer, s, w):
        base = REST + 7 * s + 4
        rows = [buffer[base + t // 2, 8 * (t % 2) + LEV * w : 8 * (t % 2) + LEV * (w + 1), :] for t in range(4)]
        return jnp.concatenate([jnp.concatenate(rows, axis=1)] * FIELDS, axis=0)

    def row_of(buffer, start):
        return jnp.concatenate([buffer[start + t] for t in range(4)], axis=1)

    @pl.when(polar)
    def _():
        added = []
        for s, sign in ((0, 0.5 * time_step), (1, -0.5 * time_step)):
            ghost = flip(s, 1.0) * row_of(halo_in, NEAR + 4 * s)
            added.append(sign * (wind(halo_out, s, 1) * ghost + coupling * row_link(ghost)))
            xb[s] = added[s]
        y = to_modes(jnp.concatenate(added, axis=0), table.at[FORWARD:EVALUATE])
        for s in range(2):
            for f in range(FIELDS):
                cb[2 * f + s, 0:LEV, :] = y[(s * FIELDS + f) * LEV : (s * FIELDS + f + 1) * LEV, :]
        ends = []
        for side, sign in ((0, -1.0), (1, 1.0)):
            came = halo_in[SIDES + side]
            along_x = (sign * hm[8:24, :]) * (roll(came, -1, 1) if side == 0 else came)
            mine = jnp.where(
                jnp.logical_and(lane2 >= 2 * PAIRS, lane2 < 2 * (PAIRS + LEV)), halo_out[SIDES + side], 0.0
            )
            ew = sum(roll(mine, 2 * LEV * f - 2 * PAIRS - side, 1) for f in range(FIELDS))
            linked = jnp.where(
                lane2 < 2 * LEV,
                roll(along_x, -4 * LEV, 1),
                jnp.where(
                    jnp.logical_and(lane2 >= 4 * LEV, lane2 < 6 * LEV), roll(along_x, 4 * LEV, 1), 0.0
                ),
            )
            ends.append(time_step * (-ew * along_x - coupling * linked))
        ends = jnp.where(lax.rem(lane2, 2) == 0, ends[0], roll(ends[1], 1, 1))
        for f in range(FIELDS):
            for h in range(2):
                cb[2 * f + h, 8:16, :] = ends[8 * h : 8 * h + 8, :]

        for d in FAR_FIRST:
            c_copy(plus(i, d)).start()

        yc[i] = cb[i]

    from_west = roll(halo_in[SIDES], 126, 1)
    from_east = roll(halo_in[SIDES + 1], COLS - 384, 1)
    both = jnp.where(jnp.logical_and(lane2 >= 66, lane2 < 114), from_east, from_west)
    in_halo = jnp.logical_or(jnp.logical_and(lane2 >= 66, lane2 < 68), lane2 >= 126)
    for e in range(PAIRS + 2 * LEV):
        grid[e, 8:24, 384:512] = jnp.where(in_halo, roll(both, -2 * e, 1), grid[e, 8:24, 384:512])
    edge_rows((REST, REST + 7), slice(0, PAIRS), (9, 22))
    for s, near in enumerate((8, 23)):
        halo_out[REST + 7 * s + 6] = grid[0:PAIRS, near, 384:512]
    halo_copy(REST, 7, REST + 7 * slot_n, 1, nb, nl).start()
    halo_copy(REST + 7, 7, REST + 7 * slot_s, 1, sb, sl).start()

    @pl.when(polar)
    def _():
        load_cut.wait()
        load_others.wait()
        own_rows(0)

    @pl.when(jnp.logical_and(polar, northern))
    def _():
        own_rows(1)

    halo_arrival(REST, BLOCKS, 1).wait_recv()
    edge_row = (7, 24)
    edge_probe = []
    for s in range(2):
        edge_probe.append(
            jnp.concatenate([halo_in[NEAR + 4 * s + t] for t in range(3)] + [halo_in[REST + 7 * s + 6]], axis=1)
        )
        grid[0:PAIRS, edge_row[s], :] = flip(s, 1.0) * edge_probe[s]

    @pl.when(polar)
    def _():
        for s, row in ((0, 0), (1, 15)):
            tend[:, row, :] = tend[:, row, :] + xb[s]
        side_tendency()

    @pl.when(jnp.logical_not(polar))
    def _():
        full_tendency()

    def edge_weights(s, a):
        return -wind(halo_in, s, 1) * a - coupling * row_link(a)

    for s, inward in ((0, 1.0), (1, -1.0)):
        mid = edge_probe[s]
        half = jnp.concatenate([hm[edge_row[s] : edge_row[s] + 1, :]] * 4, axis=1)
        along_x = half * (roll(mid, -1, 1) - roll(mid, 1, 1))
        turn = jnp.where(over_pole[s], -0.5 * inward, 0.5 * inward)
        along_y = turn * (flip(s, 1.0) * row_of(halo_out, NEAR + 4 * s) - row_of(halo_in, REST + 7 * s))
        linked = jnp.where(row16 < LEV, roll(along_x, -2 * LEV, 0), row_link(along_y))
        linked = linked + jnp.where(is_temp, roll(along_x, 2 * LEV, 0), 0.0)
        up = jnp.where(lax.rem(row16, LEV) == 0, mid, roll(mid, 1, 0))
        down = jnp.where(lax.rem(row16, LEV) == LEV - 1, mid, roll(mid, -1, 0))
        t = -(wind(halo_in, s, 0) * along_x + wind(halo_in, s, 1) * along_y) - coupling * linked
        a = mid + time_step * (t + mixing * (up + down - 2.0 * mid))
        gy[0:PAIRS, edge_row[s], :] = flip(s, -1.0) * edge_weights(s, a)

    @pl.when(jnp.logical_and(polar, jnp.logical_not(northern)))
    def _():
        own_rows(1)

    def row_weights(a, nw):
        return (
            -nw * a[0],
            -nw * a[1] - coupling * a[2],
            -nw * a[2] - coupling * a[1],
            -nw * a[3],
        )

    def put_weights(l, h, a):
        for f, weight in enumerate(row_weights(a, grid[PAIRS + LEV + l, h : h + 8, :])):
            gy[f * LEV + l, h : h + 8, :] = weight

    @pl.when(polar)
    def _():
        all_z(0).wait_recv()
        for h in (8, 16):
            taken = project(0, h // 8 - 1)
            for l in range(LEV):
                for f in range(FIELDS):
                    n, rows = f * LEV + l, slice(h - 8, h)
                    adj[n, rows, :] = grid[n, h : h + 8, :] + tend[n, rows, :] - taken[f][l]
        all_z(1).wait_recv()
        for h in (8, 16):
            taken = project(1, h // 8 - 1)
            for l in range(LEV):
                a = []
                for f in range(FIELDS):
                    n, rows = f * LEV + l, slice(h - 8, h)
                    change = tend[n, rows, :] - taken[f][l]
                    tend[n, rows, :] = change
                    tan_out[f, l, rows, :] = (grid[n, h : h + 8, :] + change)[:, :COLS]
                    a.append(adj[n, rows, :] - taken[f][l])
                    adj[n, rows, :] = a[f]
                put_weights(l, h, a)

    @pl.when(jnp.logical_not(polar))
    def _():
        @pl.loop(0, LEV, unroll=True)
        def _(l):
            for h in (8, 16):
                a = []
                for f in range(FIELDS):
                    n, rows = f * LEV + l, slice(h - 8, h)
                    a.append(grid[n, h : h + 8, :] + tend[n, rows, :])
                    tan_out[f, l, rows, :] = a[f][:, :COLS]
                    adj[n, rows, :] = a[f]
                put_weights(l, h, a)

    @pl.loop(0, LEV, unroll=True)
    def _(l):
        lo = jnp.maximum(l - 1, 0)
        hi = jnp.minimum(l + 1, LEV - 1)
        for h in (8, 16):
            rows = slice(h - 8, h)
            half = jnp.concatenate([hm[h : h + 8, :]] * 4, axis=1)
            ew = grid[PAIRS + l, h : h + 8, :]
            a = [adj[f * LEV + l, rows, :] for f in range(FIELDS)]
            col_weights = (
                -ew * a[0] - coupling * a[2],
                -ew * a[1],
                -ew * a[2] - coupling * a[0],
                -ew * a[3],
            )
            for f in range(FIELDS):
                n = f * LEV + l
                back = half * (roll(col_weights[f], 1, 1) - roll(col_weights[f], -1, 1))
                back = back + 0.5 * (gy[n, h - 1 : h + 7, :] - gy[n, h + 1 : h + 9, :])
                back = back + mixing * (adj[f * LEV + lo, rows, :] + adj[f * LEV + hi, rows, :] - 2.0 * a[f])
                diag = grid[n, h : h + 8, :] * (tend[n, rows, :] + time_step * back)
                diag_out[f, l, rows, :] = diag[:, :COLS]

    @pl.when(jnp.logical_and(near_polar, jnp.logical_not(polar)))
    def _():
        load_part.wait()

    for s, wanted in enumerate((above_polar, below_polar)):
        @pl.when(wanted)
        def _():
            row = 15 * s
            north_wind = wind(halo_in, s, 1)
            factor = ((0.5, -0.5)[s] * time_step) * grid[0:PAIRS, 8 + row, :] * flip(s, -1.0)
            before = [diag_out[f, :, row, :] for f in range(FIELDS)]
            remote(bz.at[s], bz.at[s], b_send, b_recv.at[s], nb, nl).wait_recv()
            taken = evaluate(jnp.concatenate([bz[s, f] for f in range(FIELDS)], axis=0))
            more = factor * (north_wind * taken + coupling * row_link(taken))
            for f in range(FIELDS):
                diag_out[f, :, row, :] = before[f] + more[f * LEV : (f + 1) * LEV, :COLS]

    halo_arrival(0, BLOCKS, 0).wait_send()

    @pl.when(polar)
    def _():
        all_c().wait_send()
        for q in range(2):
            all_y(q).wait_send()
            all_z(q).wait_send()

        @pl.when(edge_over)
        def _():
            remote(eb.at[others], eb.at[others], b_send, b_recv.at[0], b, west).wait_send()

        @pl.when(jnp.logical_not(edge_over))
        def _():
            remote(eb, eb, b_send, b_recv.at[0], b, west).wait_send()


def hand_out(tan_in, diag_in, tan_out, diag_out, sem):
    copies = [
        pltpu.make_async_copy(src, dst, sem.at[n])
        for n, (src, dst) in enumerate(((tan_in, tan_out), (diag_in, diag_out)))
    ]
    for copy in copies:
        copy.start()
    for copy in copies:
        copy.wait()


def per_device(bands, row_signs, col_signs, spread, east_wind, north_wind, cutoffs):
    any_spec = pl.BlockSpec(memory_space=pl.ANY)
    out = jax.ShapeDtypeStruct((FIELDS, LEV, ROWS, COLS), F32)
    tables = [jnp.asarray(half_metric(bands)), jnp.asarray(mode_factors())]
    operands = (spread, east_wind, north_wind, row_signs, col_signs, cutoffs, *tables)
    vmem = pltpu.VMEM
    dma = pltpu.SemaphoreType.DMA
    held = pltpu.VMEM(out.shape, F32)
    results = pl.pallas_call(
        functools.partial(kernel, bands),
        out_shape=(held, held),
        in_specs=[any_spec] * 8,
        out_specs=(pl.BlockSpec(memory_space=pltpu.VMEM),) * 2,
        scratch_shapes=[
            vmem((FIELDS, LEV, ROWS, COLS), F32),
            vmem((2, LEV, ROWS, COLS), F32),
            vmem((FIELDS, LEV, ROWS), jnp.int32),
            vmem((FIELDS, LEV, COLS), jnp.int32),
            pltpu.SMEM((ROWS,), jnp.int32),
            vmem((32, 128), F32),
            vmem((TABLE_ROWS, 2 * RANK), BF16),
            vmem((PAIRS + 2 * LEV, 32, WIDE), F32),
            vmem((BLOCKS, 16, 128), F32),
            vmem((BLOCKS, 16, 128), F32),
            vmem((2, LANES, LEV - 1, 8, RANK), F32),
            vmem((2, LANES, LEV - 1, 8, RANK), F32),
            vmem((2, PAIRS, WIDE), F32),
            vmem((LANES, 16, RANK), F32),
            vmem((LANES, 16, RANK), F32),
            vmem((2, LANES, LEV - 1, 8, RANK), F32),
            vmem((2, LANES, LEV - 1, 8, RANK), F32),
            vmem((LANES, LEV, RANK), F32),
            vmem((2, FIELDS, LEV, RANK), F32),
            vmem((PAIRS, ROWS, WIDE), F32),
            vmem((PAIRS, ROWS, WIDE), F32),
            vmem((PAIRS, 32, WIDE), F32),
            dma((8,)),
            dma,
            dma((2,)),
            dma((2,)),
            dma((2,)),
            dma,
            dma,
            dma((2,)),
            dma((2,)),
            dma,
            dma((2,)),
        ],
        compiler_params=pltpu.CompilerParams(
            collective_id=0, has_side_effects=True, vmem_limit_bytes=32 * 2**20
        ),
        cost_estimate=pl.CostEstimate(flops=10**9, bytes_accessed=4 * 10**6, transcendentals=0),
    )(*(pltpu.with_memory_space_constraint(x, pltpu.HBM) for x in operands))
    return pl.pallas_call(
        hand_out,
        out_shape=(out, out),
        in_specs=[any_spec] * 2,
        out_specs=(any_spec, any_spec),
        scratch_shapes=[dma((2,))],
        compiler_params=pltpu.CompilerParams(vmem_limit_bytes=2**20),
    )(*(pltpu.with_memory_space_constraint(x, pltpu.VMEM) for x in results))


def solution(mesh):
    return jax.shard_map(
        functools.partial(per_device, mesh.shape["lat"]),
        mesh=mesh,
        in_specs=(
            P(None, None, "lat"),
            P(None, None, "lon"),
            P(None, None, "lat", "lon"),
            P(None, "lat", "lon"),
            P(None, "lat", "lon"),
            P("lat"),
        ),
        out_specs=(P(None, None, "lat", "lon"), P(None, None, "lat", "lon")),
        check_vma=False,
    )
```

```python
import functools

import jax
import jax.numpy as jnp
import ml_dtypes
import numpy as np
from jax import lax
from jax.experimental import pallas as pl
from jax.experimental.pallas import tpu as pltpu
from jax.sharding import PartitionSpec as P

KTOP = 256
POLAR = 32
RANK = 128
USED = 96
ROWS = 16
COLS = 450
WIDE = 512
LANES = 8
FIELDS = 4
LEV = 4
PAIRS = FIELDS * LEV

time_step = 0.5
coupling = 0.5
mixing = 0.2
metric_cap = 4.0

FORWARD, EVALUATE, TO_COEFS, FROM_COEFS, TABLE_ROWS = 0, 512, 1280, 2304, 3328
NEAR, SIDES, REST, BLOCKS = 0, 8, 10, 24

FAR_FIRST = (6, 2, 5, 3, 7, 1, 4)
ANSWERS = (0, 4, 1, 3, 2, 7, 5, 6)

MESH = pl.DeviceIdType.MESH
F32 = jnp.float32
BF16 = jnp.bfloat16


def split_table(table):
    high = table.astype(ml_dtypes.bfloat16)
    low = (table - high.astype(np.float64)).astype(ml_dtypes.bfloat16)
    return high, low


def waves_of(group, lane_index):
    place = lane_index % 64
    second = place // 32
    other = (8 - group) if group else 4
    residue = group + second * (other - group)
    return 8 * (place % 32) + residue + (8 * (1 - second) if group == 0 else 0)


@functools.lru_cache(None)
def mode_factors():
    total = COLS * LANES
    size = COLS + 2
    place = np.arange(size, dtype=np.float64)
    width = (KTOP + 0.5) / total
    diag = ((size - 1 - 2 * place) / 2) ** 2 * np.cos(2 * np.pi * width)
    side = place[1:] * (size - place[1:]) / 2
    vectors = np.linalg.eigh(np.diag(diag) + np.diag(side, 1) + np.diag(side, -1))[1]
    basis = np.concatenate([vectors[:, ::-1][:, :USED], np.zeros((size, RANK - USED))], axis=1)
    basis = basis * np.where(basis[size // 2] < 0, -1.0, 1.0)
    weights = []
    for group in range(4):
        waves = waves_of(group, np.arange(64))
        angle = 2 * np.pi / total * ((np.arange(size)[:, None] - 1) * waves[None, :] % total)
        alpha, beta = basis.T @ np.cos(angle), basis.T @ np.sin(angle)
        if group:
            sign = np.where(np.arange(64) < 32, 1.0, -1.0)
            top, low = (alpha, beta), (sign * beta, -sign * alpha)
        else:
            use = np.where(np.arange(64) < 32, 1.0, 0.0)
            top, low = (use * alpha, use * beta), ((1 - use) * alpha, (1 - use) * beta)
        weights.append(np.concatenate([np.concatenate(top, axis=1), np.concatenate(low, axis=1)], axis=0))
    weights = np.round(np.stack(weights) * 2.0**22) / 2.0**22
    wide = np.zeros((RANK, WIDE))
    wide[:, : COLS + 1] = basis[1:].T
    wide[:, WIDE - 1] = basis[0]
    wide = np.round(wide * 2.0**26) / 2.0**26
    wide_h, wide_l = split_table(wide)
    own = np.where(np.arange(WIDE)[:, None] < COLS, 1, 0).astype(ml_dtypes.bfloat16)
    high, low = split_table(weights)
    back = np.concatenate([np.swapaxes(part, 1, 2) for part in (high, low)], axis=1)
    evaluate = np.concatenate([wide_h, wide_l, wide_h], axis=0)
    return np.concatenate(
        [
            np.concatenate([wide_h.T * own, wide_l.T * own], axis=1),
            evaluate[:, : WIDE // 2],
            evaluate[:, WIDE // 2 :],
            np.concatenate([high, low], axis=2).reshape(-1, 2 * RANK),
            back.reshape(-1, 2 * RANK),
        ],
        axis=0,
    )


ROOT = float(np.sqrt(0.5))


def over_lanes(y):
    s = [y[j] + y[j + 4] for j in range(4)]
    d = [y[j] - y[j + 4] for j in range(4)]
    even, odd = s[0] + s[2], s[1] + s[3]
    minus, plus = ROOT * (d[1] - d[3]), ROOT * (d[1] + d[3])
    return [
        (even + odd, even - odd),
        (d[0] + minus, -(d[2] + plus)),
        (s[0] - s[2], s[3] - s[1]),
        (d[0] - minus, d[2] - plus),
    ]


def to_lanes(pairs):
    (y0, y4), (u1, v1), (u2, v2), (u3, v3) = pairs
    even, odd = y0 + y4, y0 - y4
    s = [even + u2, odd - v2, even - u2, odd + v2]
    du, sv = ROOT * (u1 - u3), ROOT * (v1 + v3)
    d = [u1 + u3, du - sv, v3 - v1, -du - sv]
    return [s[j] + d[j] for j in range(4)] + [s[j] - d[j] for j in range(4)]


@functools.lru_cache(None)
def half_metric(bands):
    total = bands * ROWS
    rows = np.clip(np.arange(bands)[:, None] * ROWS - 8 + np.arange(32)[None, :], 0, total - 1)
    metric = np.minimum(1.0 / np.cos(np.pi * ((rows + 0.5) / total - 0.5)), metric_cap)
    table = np.broadcast_to((0.5 * metric).astype(np.float32)[:, :, None], (bands, 32, 128)).copy()
    forward = mode_factors()[FORWARD : FORWARD + WIDE].astype(np.float32)
    for row, col in enumerate((0, COLS - 1)):
        table[:, row] = forward[col, :RANK] + forward[col, RANK:]
    return table


def dot_cols(a, b):
    return lax.dot_general(a, b, (((1,), (0,)), ((), ())), preferred_element_type=F32)


def split(x):
    high = x.astype(BF16)
    return high, (x - high.astype(F32)).astype(BF16)


def to_modes(x, table):
    xh, xl = split(x)
    half = table.shape[1] // 2
    wide = dot_cols(xh, table[...])
    return wide[:, :half] + wide[:, half:] + dot_cols(xl, table[:, 0:half])


def from_modes(z, *tables):
    zh, zl = split(z)
    three = jnp.concatenate([zh, zh, zl], axis=1)
    return jnp.concatenate([dot_cols(three, table[...]) for table in tables], axis=1)


def to_coefs(x, table):
    rows = x.shape[0]
    wide = dot_cols(jnp.concatenate(split(x), axis=0), table[...])
    half = wide.shape[1] // 2
    return wide[:rows, :half] + wide[:rows, half:] + wide[rows:, :half]


def from_coefs(z, table):
    zh, zl = split(z)
    rows = jnp.concatenate([jnp.concatenate([zh, zh], axis=1), jnp.concatenate([zl, jnp.zeros_like(zl)], axis=1)], axis=0)
    wide = dot_cols(rows, table[...])
    return wide[: z.shape[0]] + wide[z.shape[0] :]


def pack(levels):
    lane = lax.broadcasted_iota(jnp.int32, (1, RANK), 1)
    return [jnp.where(lane < USED, levels[l], roll(levels[3], 96 - 32 * l, 1)) for l in range(3)]


def unpack(parts):
    lane = lax.broadcasted_iota(jnp.int32, (1, RANK), 1)
    last = jnp.where(lane < 64, roll(parts[1], 64, 1), roll(parts[2], 96, 1))
    return parts + [jnp.where(lane < 32, roll(parts[0], 32, 1), last)]


def roll(x, shift, axis):
    return pltpu.roll(x, shift % x.shape[axis], axis)


def kernel(
    bands, spread, east, north, rs, cs, cut, metric, table_in, tan_out, diag_out,
    spread_v, winds_v, rs_v, cs_v, cut_s, hm, table,
    grid, halo_out, halo_in, ybuf, yr, xb, cb, yc, zbuf, zr, eb, bz,
    tend, adj, gy,
    in_sem, halo_send, halo_recv, y_send, y_recv, c_send, c_recv, z_send, z_recv, b_send, b_recv,
):
    b = lax.axis_index("lat")
    i = lax.axis_index("lon")
    caps = POLAR // ROWS
    is_north = b == 0
    is_south = b == bands - 1
    northern = b < bands // 2
    polar = jnp.logical_or(b < caps, b >= bands - caps)
    above_polar = jnp.logical_or(b <= caps, is_south)
    below_polar = jnp.logical_or(b >= bands - caps - 1, is_north)
    near_polar = jnp.logical_or(above_polar, below_polar)
    across = lax.rem(i + LANES // 2, LANES)
    west = lax.rem(i + LANES - 1, LANES)
    east_lane = lax.rem(i + 1, LANES)
    nb = jnp.where(is_north, 0, b - 1)
    nl = jnp.where(is_north, across, i)
    sb = jnp.where(is_south, bands - 1, b + 1)
    sl = jnp.where(is_south, across, i)
    slot_n = jnp.where(is_north, 0, 1)
    slot_s = jnp.where(is_south, 1, 0)
    own_half = lax.rem(i, 2)
    edge_over = jnp.where(own_half == 0, is_north, is_south)
    over_pole = (is_north, is_south)
    outward = jnp.logical_and(b == bands - caps, own_half == 0)

    def plus(lane, d):
        return lax.rem(lane + d, LANES)

    load_spread = pltpu.make_async_copy(spread, spread_v, in_sem.at[0])
    load_rows = pltpu.make_async_copy(rs, rs_v, in_sem.at[1])
    load_cols = pltpu.make_async_copy(cs, cs_v, in_sem.at[2])
    load_metric = pltpu.make_async_copy(metric.at[b], hm, in_sem.at[4])
    load_cut = pltpu.make_async_copy(cut, cut_s, in_sem.at[5])

    def load_table(start, stop, sem):
        return pltpu.make_async_copy(table_in.at[start:stop], table.at[start:stop], in_sem.at[sem])

    load_forward = load_table(FORWARD, EVALUATE, 6)
    load_others = load_table(EVALUATE, TABLE_ROWS, 7)
    load_part = load_table(EVALUATE, TO_COEFS, 7)
    barrier = pltpu.get_barrier_semaphore()

    def greet(lat, lon):
        pl.semaphore_signal(barrier, inc=1, device_id=(lat, lon), device_id_type=MESH)

    greet(nb, nl)
    greet(sb, sl)

    @pl.when(polar)
    def _():
        for d in FAR_FIRST[:4]:
            greet(b, plus(i, d))

    greet(b, west)
    greet(b, east_lane)
    load_spread.start()
    load_rows.start()
    load_cols.start()
    pltpu.make_async_copy(east, winds_v.at[0], in_sem.at[3]).start()
    pltpu.make_async_copy(north, winds_v.at[1], in_sem.at[3]).start()
    load_metric.start()

    @pl.when(polar)
    def _():
        greet(b, across)
        load_forward.start()
        load_cut.start()

    @pl.when(jnp.logical_and(near_polar, jnp.logical_not(polar)))
    def _():
        load_part.start()

    load_rows.wait()
    load_cols.wait()
    load_spread.wait()
    grid[:, 8:24, 384:512] = jnp.zeros((PAIRS + 2 * LEV, ROWS, 128), F32)
    row_part = jnp.concatenate([rs_v[f] for f in range(FIELDS)], axis=0)
    row_part = (2 * row_part - 1).astype(F32).T
    for f in range(FIELDS):
        col_part = (2 * cs_v[f] - 1).astype(F32)
        for l in range(LEV):
            n = f * LEV + l
            grid[n, 8:24, 0:COLS] = spread_v[f, l] * (row_part[:, n : n + 1] * col_part[l : l + 1, :])

    @pl.when(polar)
    def _():
        load_others.start()

    pltpu.make_async_copy(winds_v, winds_v, in_sem.at[3]).wait()
    for w in range(2):
        for l in range(LEV):
            grid[PAIRS + w * LEV + l, 8:24, 0:COLS] = winds_v[w, l]

    def edge_rows(start, entries, rows):
        for s, row in enumerate(rows):
            for t in range(4):
                values = grid[entries, row, 128 * t : 128 * t + 128]
                if entries == slice(0, PAIRS):
                    halo_out[start[s] + t] = values
                else:
                    halo_out[start[s] + t // 2, 8 * (t % 2) : 8 * (t % 2) + 8, :] = values

    edge_rows((NEAR, NEAR + 4), slice(0, PAIRS), (8, 23))
    lane2 = lax.broadcasted_iota(jnp.int32, (1, 128), 1)
    for s, (start, shift) in enumerate(((0, 0), (384, COLS - 2 - 384))):
        ends = jnp.logical_and(lane2 >= shift, lane2 < shift + 2)
        parts = [
            roll(jnp.where(ends, grid[e, 8:24, start : start + 128], 0.0), 2 * e - shift, 1)
            for e in range(PAIRS + 2 * LEV)
        ]
        while len(parts) > 1:
            parts = [sum(parts[k : k + 2]) for k in range(0, len(parts), 2)]
        halo_out[SIDES + s] = parts[0]

    def tendency_rows(h, l, at, half):
        lo = jnp.maximum(l - 1, 0)
        hi = jnp.minimum(l + 1, LEV - 1)
        ew = at(PAIRS + l, h)
        nw = at(PAIRS + LEV + l, h)
        mids, along_x, along_y = [], [], []
        for f in range(FIELDS):
            mid = at(f * LEV + l, h)
            mids.append(mid)
            along_x.append(half * (roll(mid, -1, 1) - roll(mid, 1, 1)))
            along_y.append(0.5 * (at(f * LEV + l, h + 1) - at(f * LEV + l, h - 1)))
        linked = (along_x[2], along_y[2], along_x[0] + along_y[1], None)
        out = []
        for f in range(FIELDS):
            mixed = at(f * LEV + lo, h) + at(f * LEV + hi, h) - 2.0 * mids[f]
            t = -(ew * along_x[f] + nw * along_y[f]) + mixing * mixed
            if linked[f] is not None:
                t = t - coupling * linked[f]
            out.append(time_step * t)
        return out

    def full_tendency():
        @pl.loop(0, LEV, unroll=True)
        def _(l):
            for h in (8, 16):
                half = jnp.concatenate([hm[h : h + 8, :]] * 4, axis=1)
                for f, t in enumerate(tendency_rows(h, l, lambda n, r: grid[n, r : r + 8, :], half)):
                    tend[f * LEV + l, h - 8 : h, :] = t

    def side_tendency():
        lane = lax.broadcasted_iota(jnp.int32, (1, 128), 1)
        late = jnp.logical_or(jnp.logical_or(lane == 65, lane == 66), lane == 127)

        def at(n, r):
            return jnp.where(lane < 2, grid[n, r : r + 8, 0:128], grid[n, r : r + 8, 384:512])

        @pl.loop(0, LEV, unroll=True)
        def _(l):
            for h in (8, 16):
                for f, t in enumerate(tendency_rows(h, l, at, hm[h : h + 8, :])):
                    n, rows = f * LEV + l, slice(h - 8, h)
                    tend[n, rows, 0:128] = jnp.where(lane == 0, t, tend[n, rows, 0:128])
                    tend[n, rows, 384:512] = jnp.where(late, t, tend[n, rows, 384:512])

    def values(q, x):
        y = to_modes(x.reshape(PAIRS * ROWS, WIDE), table.at[FORWARD:EVALUATE])
        y = y.reshape(FIELDS, LEV, 2, 8, RANK)
        blocks = [
            jnp.concatenate([y[f, l, h] for f in range(FIELDS) for h in range(2)], axis=0) for l in range(LEV)
        ]
        for l, part in enumerate(pack(blocks)):
            ybuf[q, :, l] = part.reshape(LANES, 8, RANK)

    def probe_values():
        values(0, grid[0:PAIRS, 8:24, :])

    def local_tendency_values():
        grid[0:PAIRS, 7:8, :] = jnp.zeros((PAIRS, 1, WIDE), F32)
        grid[0:PAIRS, 24:25, :] = jnp.zeros((PAIRS, 1, WIDE), F32)
        full_tendency()
        values(1, tend[...])

    load_metric.wait()

    @pl.when(jnp.logical_and(polar, northern))
    def _():
        load_forward.wait()
        probe_values()
        local_tendency_values()

    pl.semaphore_wait(barrier, 4 + jnp.where(polar, LANES - 3, 0))

    def remote(src, dst, send, recv, lat, lon):
        return pltpu.make_async_remote_copy(
            src_ref=src, dst_ref=dst, send_sem=send, recv_sem=recv, device_id=(lat, lon), device_id_type=MESH
        )

    def halo_copy(start, count, to, which, lat, lon):
        return remote(
            halo_out.at[start : start + count], halo_in.at[pl.ds(to, count)], halo_send, halo_recv.at[which], lat, lon
        )

    def halo_arrival(start, stop, which):
        return remote(
            halo_out.at[start:stop], halo_in.at[start:stop], halo_send, halo_recv.at[which], b, west
        )

    @pl.when(northern)
    def _():
        halo_copy(NEAR, 4, NEAR + 4 * slot_n, 0, nb, nl).start()

    halo_copy(NEAR + 4, 4, NEAR + 4 * slot_s, 0, sb, sl).start()

    @pl.when(jnp.logical_not(northern))
    def _():
        halo_copy(NEAR, 4, NEAR + 4 * slot_n, 0, nb, nl).start()

    halo_copy(SIDES, 1, SIDES + 1, 0, b, west).start()
    halo_copy(SIDES + 1, 1, SIDES, 0, b, east_lane).start()

    others = pl.ds(0, LANES - 1)

    def all_y(q):
        return remote(ybuf.at[q, others], yr.at[q, others], y_send.at[q], y_recv.at[q], b, west)

    def send_values(q):
        for d in FAR_FIRST:
            o = plus(i, d)
            remote(ybuf.at[q, o], yr.at[q, i], y_send.at[q], y_recv.at[q], b, o).start()

        yr[q, i] = ybuf[q, i]

    def c_copy(o):
        return remote(cb.at[o], yc.at[i], c_send, c_recv, b, o)

    def all_c():
        return remote(cb.at[others], yc.at[others], c_send, c_recv, b, west)

    def z_copy(q, j):
        return remote(zbuf.at[q, j], zr.at[q, i], z_send.at[q], z_recv.at[q], b, j)

    def all_z(q):
        return remote(zbuf.at[q, others], zr.at[q, others], z_send.at[q], z_recv.at[q], b, west)

    def edge_sends():
        slot = jnp.where(own_half == 0, slot_n, slot_s)
        lat = jnp.where(own_half == 0, nb, sb)

        def away(j, lon):
            remote(eb.at[j], bz.at[slot, i // 2], b_send, b_recv.at[slot], lat, lon).start()

        @pl.when(jnp.logical_not(edge_over))
        def _():
            for j in ANSWERS:
                away(j, j)

        @pl.when(edge_over)
        def _():
            for j in ANSWERS:
                lon = (j + LANES // 2) % LANES

                @pl.when(i != lon)
                def _():
                    away(j, lon)

                @pl.when(i == lon)
                def _():
                    pltpu.make_async_copy(eb.at[j], bz.at[slot, i // 2], b_recv.at[slot]).start()

    def own_rows(q):
        row = lax.broadcasted_iota(jnp.int32, (8, 128), 0)
        cutoff = jnp.zeros((8, 128), jnp.int32)
        for r in range(8):
            cutoff = jnp.where(row == r, cut_s[8 * own_half + r], cutoff)
        keeps = []
        for group in range(4):
            wave = waves_of(group, lax.broadcasted_iota(jnp.int32, (8, 128), 1))
            keep = jnp.where(wave > cutoff, 2.0 / (COLS * LANES), 0.0)
            keeps.append(jnp.concatenate([keep] * LEV, axis=0))
        all_y(q).wait_recv()
        levels = unpack([yr[q, :, l].reshape(LANES * 8, RANK) for l in range(LEV - 1)])
        if q == 1:
            edge_row = jnp.where(row == 7 * own_half, 1.0, 0.0)
            all_c().wait_recv()
            ends = jnp.concatenate([yc[j, 8:16, :] for j in range(LANES)], axis=0)
            ends = pltpu.roll(ends, lax.rem(128 - 2 * LEV * (i // 2), 128), 1)
            levels = [
                levels[l]
                + ends[:, 2 * l : 2 * l + 1] * hm[0:1, :]
                + ends[:, 2 * l + 1 : 2 * l + 2] * hm[1:2, :]
                + jnp.concatenate([edge_row * yc[j, l : l + 1, :] for j in range(LANES)], axis=0)
                for l in range(LEV)
            ]
        lanes = [
            jnp.concatenate([levels[l][8 * j : 8 * j + 8, :] for l in range(LEV)], axis=0) for j in range(LANES)
        ]
        coefs = [
            to_coefs(jnp.concatenate(pair, axis=1), table.at[TO_COEFS + 256 * group : TO_COEFS + 256 * (group + 1)])
            for group, pair in enumerate(over_lanes(lanes))
        ]
        kept = [coef * keep for coef, keep in zip(coefs, keeps)]
        backs = [
            from_coefs(coef, table.at[FROM_COEFS + 256 * group : FROM_COEFS + 256 * (group + 1)])
            for group, coef in enumerate(kept)
        ]
        pairs = [(back[:, :RANK], back[:, RANK:]) for back in backs]
        zs = [z.reshape(LEV, 8, RANK) for z in to_lanes(pairs)]
        for l, part in enumerate(pack([jnp.concatenate([z[l] for z in zs], axis=0) for l in range(LEV)])):
            zbuf[q, :, l] = part.reshape(LANES, 8, RANK)

        def edges():
            for j, z in enumerate(zs):
                edge = jnp.where(own_half == 0, z[:, 0, :], z[:, 7, :])
                eb[j] = edge if q == 0 else eb[j] + edge
            if q == 1:
                edge_sends()

        if q == 1:
            pl.when(outward)(edges)
        for j in ANSWERS:
            @pl.when(i != j)
            def _():
                z_copy(q, j).start()

        if q == 1:
            pl.when(jnp.logical_not(outward))(edges)
        else:
            edges()
        zr[q, i] = zbuf[q, i]

    def evaluate(z):
        return from_modes(z, table.at[EVALUATE : EVALUATE + 384], table.at[EVALUATE + 384 : TO_COEFS])

    def project(q, h):
        levels = unpack(
            [jnp.concatenate([zr[q, 2 * f + h, l] for f in range(FIELDS)], axis=0) for l in range(LEV - 1)]
        )
        z = jnp.concatenate(
            [levels[l][8 * f : 8 * f + 8, :] for f in range(FIELDS) for l in range(LEV)], axis=0
        )
        out = evaluate(z)
        return [[out[8 * (LEV * f + l) : 8 * (LEV * f + l + 1), :] for l in range(LEV)] for f in range(FIELDS)]


    @pl.when(jnp.logical_and(polar, northern))
    def _():
        send_values(0)

    @pl.when(jnp.logical_and(polar, jnp.logical_not(northern)))
    def _():
        load_forward.wait()
        probe_values()
        send_values(0)
        local_tendency_values()
        send_values(1)

    edge_rows((REST + 4, REST + 11), slice(PAIRS, PAIRS + 2 * LEV), (8, 23))

    halo_arrival(NEAR, REST, 0).wait_recv()
    row16 = lax.broadcasted_iota(jnp.int32, (PAIRS, 1), 0)
    is_v = jnp.logical_and(row16 >= LEV, row16 < 2 * LEV)
    is_temp = jnp.logical_and(row16 >= 2 * LEV, row16 < 3 * LEV)

    def flip(s, minus):
        sign = jnp.where(row16 < 2 * LEV, -1.0, 1.0) * minus
        return jnp.where(over_pole[s], sign, 1.0)

    def row_link(x):
        return jnp.where(is_v, roll(x, -LEV, 0), jnp.where(is_temp, roll(x, LEV, 0), 0.0))

    def wind(buffer, s, w):
        base = REST + 7 * s + 4
        rows = [buffer[base + t // 2, 8 * (t % 2) + LEV * w : 8 * (t % 2) + LEV * (w + 1), :] for t in range(4)]
        return jnp.concatenate([jnp.concatenate(rows, axis=1)] * FIELDS, axis=0)

    def row_of(buffer, start):
        return jnp.concatenate([buffer[start + t] for t in range(4)], axis=1)

    @pl.when(polar)
    def _():
        added = []
        for s, sign in ((0, 0.5 * time_step), (1, -0.5 * time_step)):
            ghost = flip(s, 1.0) * row_of(halo_in, NEAR + 4 * s)
            added.append(sign * (wind(halo_out, s, 1) * ghost + coupling * row_link(ghost)))
            xb[s] = added[s]
        y = to_modes(jnp.concatenate(added, axis=0), table.at[FORWARD:EVALUATE])
        for s in range(2):
            for f in range(FIELDS):
                cb[2 * f + s, 0:LEV, :] = y[(s * FIELDS + f) * LEV : (s * FIELDS + f + 1) * LEV, :]
        ends = []
        for side, sign in ((0, -1.0), (1, 1.0)):
            came = halo_in[SIDES + side]
            along_x = (sign * hm[8:24, :]) * (roll(came, -1, 1) if side == 0 else came)
            mine = jnp.where(
                jnp.logical_and(lane2 >= 2 * PAIRS, lane2 < 2 * (PAIRS + LEV)), halo_out[SIDES + side], 0.0
            )
            ew = sum(roll(mine, 2 * LEV * f - 2 * PAIRS - side, 1) for f in range(FIELDS))
            linked = jnp.where(
                lane2 < 2 * LEV,
                roll(along_x, -4 * LEV, 1),
                jnp.where(
                    jnp.logical_and(lane2 >= 4 * LEV, lane2 < 6 * LEV), roll(along_x, 4 * LEV, 1), 0.0
                ),
            )
            ends.append(time_step * (-ew * along_x - coupling * linked))
        ends = jnp.where(lax.rem(lane2, 2) == 0, ends[0], roll(ends[1], 1, 1))
        for f in range(FIELDS):
            for h in range(2):
                cb[2 * f + h, 8:16, :] = ends[8 * h : 8 * h + 8, :]

        for d in FAR_FIRST:
            c_copy(plus(i, d)).start()

        yc[i] = cb[i]

    @pl.when(jnp.logical_and(polar, northern))
    def _():
        send_values(1)

    from_west = roll(halo_in[SIDES], 126, 1)
    from_east = roll(halo_in[SIDES + 1], COLS - 384, 1)
    both = jnp.where(jnp.logical_and(lane2 >= 66, lane2 < 114), from_east, from_west)
    in_halo = jnp.logical_or(jnp.logical_and(lane2 >= 66, lane2 < 68), lane2 >= 126)
    for e in range(PAIRS + 2 * LEV):
        grid[e, 8:24, 384:512] = jnp.where(in_halo, roll(both, -2 * e, 1), grid[e, 8:24, 384:512])
    edge_rows((REST, REST + 7), slice(0, PAIRS), (9, 22))
    for s, near in enumerate((8, 23)):
        halo_out[REST + 7 * s + 6] = grid[0:PAIRS, near, 384:512]
    halo_copy(REST, 7, REST + 7 * slot_n, 1, nb, nl).start()
    halo_copy(REST + 7, 7, REST + 7 * slot_s, 1, sb, sl).start()

    @pl.when(polar)
    def _():
        load_cut.wait()
        load_others.wait()
        own_rows(0)

    @pl.when(jnp.logical_and(polar, northern))
    def _():
        own_rows(1)

    halo_arrival(REST, BLOCKS, 1).wait_recv()
    edge_row = (7, 24)
    edge_probe = []
    for s in range(2):
        edge_probe.append(
            jnp.concatenate([halo_in[NEAR + 4 * s + t] for t in range(3)] + [halo_in[REST + 7 * s + 6]], axis=1)
        )
        grid[0:PAIRS, edge_row[s], :] = flip(s, 1.0) * edge_probe[s]

    @pl.when(polar)
    def _():
        for s, row in ((0, 0), (1, 15)):
            tend[:, row, :] = tend[:, row, :] + xb[s]
        side_tendency()

    @pl.when(jnp.logical_not(polar))
    def _():
        full_tendency()

    def edge_weights(s, a):
        return -wind(halo_in, s, 1) * a - coupling * row_link(a)

    for s, inward in ((0, 1.0), (1, -1.0)):
        mid = edge_probe[s]
        half = jnp.concatenate([hm[edge_row[s] : edge_row[s] + 1, :]] * 4, axis=1)
        along_x = half * (roll(mid, -1, 1) - roll(mid, 1, 1))
        turn = jnp.where(over_pole[s], -0.5 * inward, 0.5 * inward)
        along_y = turn * (flip(s, 1.0) * row_of(halo_out, NEAR + 4 * s) - row_of(halo_in, REST + 7 * s))
        linked = jnp.where(row16 < LEV, roll(along_x, -2 * LEV, 0), row_link(along_y))
        linked = linked + jnp.where(is_temp, roll(along_x, 2 * LEV, 0), 0.0)
        up = jnp.where(lax.rem(row16, LEV) == 0, mid, roll(mid, 1, 0))
        down = jnp.where(lax.rem(row16, LEV) == LEV - 1, mid, roll(mid, -1, 0))
        t = -(wind(halo_in, s, 0) * along_x + wind(halo_in, s, 1) * along_y) - coupling * linked
        a = mid + time_step * (t + mixing * (up + down - 2.0 * mid))
        gy[0:PAIRS, edge_row[s], :] = flip(s, -1.0) * edge_weights(s, a)

    @pl.when(jnp.logical_and(polar, jnp.logical_not(northern)))
    def _():
        own_rows(1)

    def row_weights(a, nw):
        return (
            -nw * a[0],
            -nw * a[1] - coupling * a[2],
            -nw * a[2] - coupling * a[1],
            -nw * a[3],
        )

    def put_weights(l, h, a):
        for f, weight in enumerate(row_weights(a, grid[PAIRS + LEV + l, h : h + 8, :])):
            gy[f * LEV + l, h : h + 8, :] = weight

    @pl.when(polar)
    def _():
        all_z(0).wait_recv()
        for h in (8, 16):
            taken = project(0, h // 8 - 1)
            for l in range(LEV):
                for f in range(FIELDS):
                    n, rows = f * LEV + l, slice(h - 8, h)
                    adj[n, rows, :] = grid[n, h : h + 8, :] + tend[n, rows, :] - taken[f][l]
        all_z(1).wait_recv()
        for h in (8, 16):
            taken = project(1, h // 8 - 1)
            for l in range(LEV):
                a = []
                for f in range(FIELDS):
                    n, rows = f * LEV + l, slice(h - 8, h)
                    change = tend[n, rows, :] - taken[f][l]
                    tend[n, rows, :] = change
                    tan_out[f, l, rows, :] = (grid[n, h : h + 8, :] + change)[:, :COLS]
                    a.append(adj[n, rows, :] - taken[f][l])
                    adj[n, rows, :] = a[f]
                put_weights(l, h, a)

    @pl.when(jnp.logical_not(polar))
    def _():
        @pl.loop(0, LEV, unroll=True)
        def _(l):
            for h in (8, 16):
                a = []
                for f in range(FIELDS):
                    n, rows = f * LEV + l, slice(h - 8, h)
                    a.append(grid[n, h : h + 8, :] + tend[n, rows, :])
                    tan_out[f, l, rows, :] = a[f][:, :COLS]
                    adj[n, rows, :] = a[f]
                put_weights(l, h, a)

    @pl.loop(0, LEV, unroll=True)
    def _(l):
        lo = jnp.maximum(l - 1, 0)
        hi = jnp.minimum(l + 1, LEV - 1)
        for h in (8, 16):
            rows = slice(h - 8, h)
            half = jnp.concatenate([hm[h : h + 8, :]] * 4, axis=1)
            ew = grid[PAIRS + l, h : h + 8, :]
            a = [adj[f * LEV + l, rows, :] for f in range(FIELDS)]
            col_weights = (
                -ew * a[0] - coupling * a[2],
                -ew * a[1],
                -ew * a[2] - coupling * a[0],
                -ew * a[3],
            )
            for f in range(FIELDS):
                n = f * LEV + l
                back = half * (roll(col_weights[f], 1, 1) - roll(col_weights[f], -1, 1))
                back = back + 0.5 * (gy[n, h - 1 : h + 7, :] - gy[n, h + 1 : h + 9, :])
                back = back + mixing * (adj[f * LEV + lo, rows, :] + adj[f * LEV + hi, rows, :] - 2.0 * a[f])
                diag = grid[n, h : h + 8, :] * (tend[n, rows, :] + time_step * back)
                diag_out[f, l, rows, :] = diag[:, :COLS]

    @pl.when(jnp.logical_and(near_polar, jnp.logical_not(polar)))
    def _():
        load_part.wait()

    for s, wanted in enumerate((above_polar, below_polar)):
        @pl.when(wanted)
        def _():
            row = 15 * s
            north_wind = wind(halo_in, s, 1)
            factor = ((0.5, -0.5)[s] * time_step) * grid[0:PAIRS, 8 + row, :] * flip(s, -1.0)
            before = [diag_out[f, :, row, :] for f in range(FIELDS)]
            remote(bz.at[s], bz.at[s], b_send, b_recv.at[s], nb, nl).wait_recv()
            taken = evaluate(jnp.concatenate([bz[s, f] for f in range(FIELDS)], axis=0))
            more = factor * (north_wind * taken + coupling * row_link(taken))
            for f in range(FIELDS):
                diag_out[f, :, row, :] = before[f] + more[f * LEV : (f + 1) * LEV, :COLS]

    halo_arrival(0, BLOCKS, 0).wait_send()

    @pl.when(polar)
    def _():
        all_c().wait_send()
        for q in range(2):
            all_y(q).wait_send()
            all_z(q).wait_send()

        @pl.when(edge_over)
        def _():
            remote(eb.at[others], eb.at[others], b_send, b_recv.at[0], b, west).wait_send()

        @pl.when(jnp.logical_not(edge_over))
        def _():
            remote(eb, eb, b_send, b_recv.at[0], b, west).wait_send()


def hand_out(tan_in, diag_in, tan_out, diag_out, sem):
    copies = [
        pltpu.make_async_copy(src, dst, sem.at[n])
        for n, (src, dst) in enumerate(((tan_in, tan_out), (diag_in, diag_out)))
    ]
    for copy in copies:
        copy.start()
    for copy in copies:
        copy.wait()


def per_device(bands, row_signs, col_signs, spread, east_wind, north_wind, cutoffs):
    any_spec = pl.BlockSpec(memory_space=pl.ANY)
    out = jax.ShapeDtypeStruct((FIELDS, LEV, ROWS, COLS), F32)
    tables = [jnp.asarray(half_metric(bands)), jnp.asarray(mode_factors())]
    operands = (spread, east_wind, north_wind, row_signs, col_signs, cutoffs, *tables)
    vmem = pltpu.VMEM
    dma = pltpu.SemaphoreType.DMA
    held = pltpu.VMEM(out.shape, F32)
    results = pl.pallas_call(
        functools.partial(kernel, bands),
        out_shape=(held, held),
        in_specs=[any_spec] * 8,
        out_specs=(pl.BlockSpec(memory_space=pltpu.VMEM),) * 2,
        scratch_shapes=[
            vmem((FIELDS, LEV, ROWS, COLS), F32),
            vmem((2, LEV, ROWS, COLS), F32),
            vmem((FIELDS, LEV, ROWS), jnp.int32),
            vmem((FIELDS, LEV, COLS), jnp.int32),
            pltpu.SMEM((ROWS,), jnp.int32),
            vmem((32, 128), F32),
            vmem((TABLE_ROWS, 2 * RANK), BF16),
            vmem((PAIRS + 2 * LEV, 32, WIDE), F32),
            vmem((BLOCKS, 16, 128), F32),
            vmem((BLOCKS, 16, 128), F32),
            vmem((2, LANES, LEV - 1, 8, RANK), F32),
            vmem((2, LANES, LEV - 1, 8, RANK), F32),
            vmem((2, PAIRS, WIDE), F32),
            vmem((LANES, 16, RANK), F32),
            vmem((LANES, 16, RANK), F32),
            vmem((2, LANES, LEV - 1, 8, RANK), F32),
            vmem((2, LANES, LEV - 1, 8, RANK), F32),
            vmem((LANES, LEV, RANK), F32),
            vmem((2, FIELDS, LEV, RANK), F32),
            vmem((PAIRS, ROWS, WIDE), F32),
            vmem((PAIRS, ROWS, WIDE), F32),
            vmem((PAIRS, 32, WIDE), F32),
            dma((8,)),
            dma,
            dma((2,)),
            dma((2,)),
            dma((2,)),
            dma,
            dma,
            dma((2,)),
            dma((2,)),
            dma,
            dma((2,)),
        ],
        compiler_params=pltpu.CompilerParams(
            collective_id=0, has_side_effects=True, vmem_limit_bytes=32 * 2**20
        ),
        cost_estimate=pl.CostEstimate(flops=10**9, bytes_accessed=4 * 10**6, transcendentals=0),
    )(*(pltpu.with_memory_space_constraint(x, pltpu.HBM) for x in operands))
    return pl.pallas_call(
        hand_out,
        out_shape=(out, out),
        in_specs=[any_spec] * 2,
        out_specs=(any_spec, any_spec),
        scratch_shapes=[dma((2,))],
        compiler_params=pltpu.CompilerParams(vmem_limit_bytes=2**20),
    )(*(pltpu.with_memory_space_constraint(x, pltpu.VMEM) for x in results))


def solution(mesh):
    return jax.shard_map(
        functools.partial(per_device, mesh.shape["lat"]),
        mesh=mesh,
        in_specs=(
            P(None, None, "lat"),
            P(None, None, "lon"),
            P(None, None, "lat", "lon"),
            P(None, "lat", "lon"),
            P(None, "lat", "lon"),
            P("lat"),
        ),
        out_specs=(P(None, None, "lat", "lon"), P(None, None, "lat", "lon")),
        check_vma=False,
    )
```

```python
import functools

import jax
import jax.numpy as jnp
import ml_dtypes
import numpy as np
from jax import lax
from jax.experimental import pallas as pl
from jax.experimental.pallas import tpu as pltpu
from jax.sharding import PartitionSpec as P

KTOP = 256
POLAR = 32
RANK = 128
USED = 96
ROWS = 16
COLS = 450
WIDE = 512
LANES = 8
FIELDS = 4
LEV = 4
PAIRS = FIELDS * LEV

time_step = 0.5
coupling = 0.5
mixing = 0.2
metric_cap = 4.0

FORWARD, EVALUATE, TO_COEFS, FROM_COEFS, TABLE_ROWS = 0, 512, 1280, 2304, 3328
NEAR, SIDES, REST, BLOCKS = 0, 8, 10, 24

FAR_FIRST = (6, 2, 5, 3, 7, 1, 4)
ANSWERS = (0, 4, 1, 3, 2, 7, 5, 6)

MESH = pl.DeviceIdType.MESH
F32 = jnp.float32
BF16 = jnp.bfloat16


def split_table(table):
    high = table.astype(ml_dtypes.bfloat16)
    low = (table - high.astype(np.float64)).astype(ml_dtypes.bfloat16)
    return high, low


def waves_of(group, lane_index):
    place = lane_index % 64
    second = place // 32
    other = (8 - group) if group else 4
    residue = group + second * (other - group)
    return 8 * (place % 32) + residue + (8 * (1 - second) if group == 0 else 0)


@functools.lru_cache(None)
def mode_factors():
    total = COLS * LANES
    size = COLS + 2
    place = np.arange(size, dtype=np.float64)
    width = (KTOP + 0.5) / total
    diag = ((size - 1 - 2 * place) / 2) ** 2 * np.cos(2 * np.pi * width)
    side = place[1:] * (size - place[1:]) / 2
    vectors = np.linalg.eigh(np.diag(diag) + np.diag(side, 1) + np.diag(side, -1))[1]
    basis = np.concatenate([vectors[:, ::-1][:, :USED], np.zeros((size, RANK - USED))], axis=1)
    basis = basis * np.where(basis[size // 2] < 0, -1.0, 1.0)
    weights = []
    for group in range(4):
        waves = waves_of(group, np.arange(64))
        angle = 2 * np.pi / total * ((np.arange(size)[:, None] - 1) * waves[None, :] % total)
        alpha, beta = basis.T @ np.cos(angle), basis.T @ np.sin(angle)
        if group:
            sign = np.where(np.arange(64) < 32, 1.0, -1.0)
            top, low = (alpha, beta), (sign * beta, -sign * alpha)
        else:
            use = np.where(np.arange(64) < 32, 1.0, 0.0)
            top, low = (use * alpha, use * beta), ((1 - use) * alpha, (1 - use) * beta)
        weights.append(np.concatenate([np.concatenate(top, axis=1), np.concatenate(low, axis=1)], axis=0))
    weights = np.round(np.stack(weights) * 2.0**22) / 2.0**22
    wide = np.zeros((RANK, WIDE))
    wide[:, : COLS + 1] = basis[1:].T
    wide[:, WIDE - 1] = basis[0]
    wide = np.round(wide * 2.0**26) / 2.0**26
    wide_h, wide_l = split_table(wide)
    own = np.where(np.arange(WIDE)[:, None] < COLS, 1, 0).astype(ml_dtypes.bfloat16)
    high, low = split_table(weights)
    back = np.concatenate([np.swapaxes(part, 1, 2) for part in (high, low)], axis=1)
    evaluate = np.concatenate([wide_h, wide_l, wide_h], axis=0)
    return np.concatenate(
        [
            np.concatenate([wide_h.T * own, wide_l.T * own], axis=1),
            evaluate[:, : WIDE // 2],
            evaluate[:, WIDE // 2 :],
            np.concatenate([high, low], axis=2).reshape(-1, 2 * RANK),
            back.reshape(-1, 2 * RANK),
        ],
        axis=0,
    )


ROOT = float(np.sqrt(0.5))


def over_lanes(y):
    s = [y[j] + y[j + 4] for j in range(4)]
    d = [y[j] - y[j + 4] for j in range(4)]
    even, odd = s[0] + s[2], s[1] + s[3]
    minus, plus = ROOT * (d[1] - d[3]), ROOT * (d[1] + d[3])
    return [
        (even + odd, even - odd),
        (d[0] + minus, -(d[2] + plus)),
        (s[0] - s[2], s[3] - s[1]),
        (d[0] - minus, d[2] - plus),
    ]


def to_lanes(pairs):
    (y0, y4), (u1, v1), (u2, v2), (u3, v3) = pairs
    even, odd = y0 + y4, y0 - y4
    s = [even + u2, odd - v2, even - u2, odd + v2]
    du, sv = ROOT * (u1 - u3), ROOT * (v1 + v3)
    d = [u1 + u3, du - sv, v3 - v1, -du - sv]
    return [s[j] + d[j] for j in range(4)] + [s[j] - d[j] for j in range(4)]


@functools.lru_cache(None)
def half_metric(bands):
    total = bands * ROWS
    rows = np.clip(np.arange(bands)[:, None] * ROWS - 8 + np.arange(32)[None, :], 0, total - 1)
    metric = np.minimum(1.0 / np.cos(np.pi * ((rows + 0.5) / total - 0.5)), metric_cap)
    table = np.broadcast_to((0.5 * metric).astype(np.float32)[:, :, None], (bands, 32, 128)).copy()
    forward = mode_factors()[FORWARD : FORWARD + WIDE].astype(np.float32)
    for row, col in enumerate((0, COLS - 1)):
        table[:, row] = forward[col, :RANK] + forward[col, RANK:]
    return table


def dot_cols(a, b):
    return lax.dot_general(a, b, (((1,), (0,)), ((), ())), preferred_element_type=F32)


def split(x):
    high = x.astype(BF16)
    return high, (x - high.astype(F32)).astype(BF16)


def to_modes(x, table):
    xh, xl = split(x)
    half = table.shape[1] // 2
    wide = dot_cols(xh, table[...])
    return wide[:, :half] + wide[:, half:] + dot_cols(xl, table[:, 0:half])


def from_modes(z, *tables):
    zh, zl = split(z)
    three = jnp.concatenate([zh, zh, zl], axis=1)
    return jnp.concatenate([dot_cols(three, table[...]) for table in tables], axis=1)


def to_coefs(x, table):
    rows = x.shape[0]
    wide = dot_cols(jnp.concatenate(split(x), axis=0), table[...])
    half = wide.shape[1] // 2
    return wide[:rows, :half] + wide[:rows, half:] + wide[rows:, :half]


def from_coefs(z, table):
    zh, zl = split(z)
    rows = jnp.concatenate([jnp.concatenate([zh, zh], axis=1), jnp.concatenate([zl, jnp.zeros_like(zl)], axis=1)], axis=0)
    wide = dot_cols(rows, table[...])
    return wide[: z.shape[0]] + wide[z.shape[0] :]


def pack(levels):
    lane = lax.broadcasted_iota(jnp.int32, (1, RANK), 1)
    return [jnp.where(lane < USED, levels[l], roll(levels[3], 96 - 32 * l, 1)) for l in range(3)]


def unpack(parts):
    lane = lax.broadcasted_iota(jnp.int32, (1, RANK), 1)
    last = jnp.where(lane < 64, roll(parts[1], 64, 1), roll(parts[2], 96, 1))
    return parts + [jnp.where(lane < 32, roll(parts[0], 32, 1), last)]


def roll(x, shift, axis):
    return pltpu.roll(x, shift % x.shape[axis], axis)


def kernel(
    bands, spread, east, north, rs, cs, cut, metric, table_in, tan_out, diag_out,
    spread_v, winds_v, rs_v, cs_v, cut_s, hm, table,
    grid, halo_out, halo_in, ybuf, yr, xb, cb, yc, zbuf, zr, eb, bz,
    tend, adj, gy,
    in_sem, halo_send, halo_recv, y_send, y_recv, c_send, c_recv, z_send, z_recv, b_send, b_recv,
):
    b = lax.axis_index("lat")
    i = lax.axis_index("lon")
    caps = POLAR // ROWS
    is_north = b == 0
    is_south = b == bands - 1
    northern = b < bands // 2
    polar = jnp.logical_or(b < caps, b >= bands - caps)
    above_polar = jnp.logical_or(b <= caps, is_south)
    below_polar = jnp.logical_or(b >= bands - caps - 1, is_north)
    near_polar = jnp.logical_or(above_polar, below_polar)
    across = lax.rem(i + LANES // 2, LANES)
    west = lax.rem(i + LANES - 1, LANES)
    east_lane = lax.rem(i + 1, LANES)
    nb = jnp.where(is_north, 0, b - 1)
    nl = jnp.where(is_north, across, i)
    sb = jnp.where(is_south, bands - 1, b + 1)
    sl = jnp.where(is_south, across, i)
    slot_n = jnp.where(is_north, 0, 1)
    slot_s = jnp.where(is_south, 1, 0)
    own_half = lax.rem(i, 2)
    edge_over = jnp.where(own_half == 0, is_north, is_south)
    over_pole = (is_north, is_south)
    outward = jnp.logical_and(b == bands - caps, own_half == 0)

    def plus(lane, d):
        return lax.rem(lane + d, LANES)

    load_spread = pltpu.make_async_copy(spread, spread_v, in_sem.at[0])
    load_rows = pltpu.make_async_copy(rs, rs_v, in_sem.at[1])
    load_cols = pltpu.make_async_copy(cs, cs_v, in_sem.at[2])
    load_metric = pltpu.make_async_copy(metric.at[b], hm, in_sem.at[4])
    load_cut = pltpu.make_async_copy(cut, cut_s, in_sem.at[5])

    def load_table(start, stop, sem):
        return pltpu.make_async_copy(table_in.at[start:stop], table.at[start:stop], in_sem.at[sem])

    load_forward = load_table(FORWARD, EVALUATE, 6)
    load_others = load_table(EVALUATE, TABLE_ROWS, 7)
    load_part = load_table(EVALUATE, TO_COEFS, 7)
    barrier = pltpu.get_barrier_semaphore()

    def greet(lat, lon):
        pl.semaphore_signal(barrier, inc=1, device_id=(lat, lon), device_id_type=MESH)

    greet(nb, nl)
    greet(sb, sl)

    @pl.when(polar)
    def _():
        for d in FAR_FIRST[:4]:
            greet(b, plus(i, d))

    greet(b, west)
    greet(b, east_lane)
    load_spread.start()
    load_rows.start()
    load_cols.start()
    pltpu.make_async_copy(east, winds_v.at[0], in_sem.at[3]).start()
    pltpu.make_async_copy(north, winds_v.at[1], in_sem.at[3]).start()
    load_metric.start()

    @pl.when(polar)
    def _():
        greet(b, across)
        load_forward.start()
        load_cut.start()

    @pl.when(jnp.logical_and(near_polar, jnp.logical_not(polar)))
    def _():
        load_part.start()

    load_rows.wait()
    load_cols.wait()
    load_spread.wait()
    grid[:, 8:24, 384:512] = jnp.zeros((PAIRS + 2 * LEV, ROWS, 128), F32)
    row_part = jnp.concatenate([rs_v[f] for f in range(FIELDS)], axis=0)
    row_part = (2 * row_part - 1).astype(F32).T
    for f in range(FIELDS):
        col_part = (2 * cs_v[f] - 1).astype(F32)
        for l in range(LEV):
            n = f * LEV + l
            grid[n, 8:24, 0:COLS] = spread_v[f, l] * (row_part[:, n : n + 1] * col_part[l : l + 1, :])

    @pl.when(polar)
    def _():
        load_others.start()

    pltpu.make_async_copy(winds_v, winds_v, in_sem.at[3]).wait()
    for w in range(2):
        for l in range(LEV):
            grid[PAIRS + w * LEV + l, 8:24, 0:COLS] = winds_v[w, l]

    def edge_rows(start, entries, rows):
        for s, row in enumerate(rows):
            for t in range(4):
                values = grid[entries, row, 128 * t : 128 * t + 128]
                if entries == slice(0, PAIRS):
                    halo_out[start[s] + t] = values
                else:
                    halo_out[start[s] + t // 2, 8 * (t % 2) : 8 * (t % 2) + 8, :] = values

    edge_rows((NEAR, NEAR + 4), slice(0, PAIRS), (8, 23))
    lane2 = lax.broadcasted_iota(jnp.int32, (1, 128), 1)
    for s, (start, shift) in enumerate(((0, 0), (384, COLS - 2 - 384))):
        ends = jnp.logical_and(lane2 >= shift, lane2 < shift + 2)
        parts = [
            roll(jnp.where(ends, grid[e, 8:24, start : start + 128], 0.0), 2 * e - shift, 1)
            for e in range(PAIRS + 2 * LEV)
        ]
        while len(parts) > 1:
            parts = [sum(parts[k : k + 2]) for k in range(0, len(parts), 2)]
        halo_out[SIDES + s] = parts[0]

    def tendency_rows(h, l, at, half):
        lo = jnp.maximum(l - 1, 0)
        hi = jnp.minimum(l + 1, LEV - 1)
        ew = at(PAIRS + l, h)
        nw = at(PAIRS + LEV + l, h)
        mids, along_x, along_y = [], [], []
        for f in range(FIELDS):
            mid = at(f * LEV + l, h)
            mids.append(mid)
            along_x.append(half * (roll(mid, -1, 1) - roll(mid, 1, 1)))
            along_y.append(0.5 * (at(f * LEV + l, h + 1) - at(f * LEV + l, h - 1)))
        linked = (along_x[2], along_y[2], along_x[0] + along_y[1], None)
        out = []
        for f in range(FIELDS):
            mixed = at(f * LEV + lo, h) + at(f * LEV + hi, h) - 2.0 * mids[f]
            t = -(ew * along_x[f] + nw * along_y[f]) + mixing * mixed
            if linked[f] is not None:
                t = t - coupling * linked[f]
            out.append(time_step * t)
        return out

    def full_tendency():
        @pl.loop(0, LEV, unroll=True)
        def _(l):
            for h in (8, 16):
                half = jnp.concatenate([hm[h : h + 8, :]] * 4, axis=1)
                for f, t in enumerate(tendency_rows(h, l, lambda n, r: grid[n, r : r + 8, :], half)):
                    tend[f * LEV + l, h - 8 : h, :] = t

    def side_tendency():
        lane = lax.broadcasted_iota(jnp.int32, (1, 128), 1)
        late = jnp.logical_or(jnp.logical_or(lane == 65, lane == 66), lane == 127)

        def at(n, r):
            return jnp.where(lane < 2, grid[n, r : r + 8, 0:128], grid[n, r : r + 8, 384:512])

        @pl.loop(0, LEV, unroll=True)
        def _(l):
            for h in (8, 16):
                for f, t in enumerate(tendency_rows(h, l, at, hm[h : h + 8, :])):
                    n, rows = f * LEV + l, slice(h - 8, h)
                    tend[n, rows, 0:128] = jnp.where(lane == 0, t, tend[n, rows, 0:128])
                    tend[n, rows, 384:512] = jnp.where(late, t, tend[n, rows, 384:512])

    def values(q, x):
        y = to_modes(x.reshape(PAIRS * ROWS, WIDE), table.at[FORWARD:EVALUATE])
        y = y.reshape(FIELDS, LEV, 2, 8, RANK)
        blocks = [
            jnp.concatenate([y[f, l, h] for f in range(FIELDS) for h in range(2)], axis=0) for l in range(LEV)
        ]
        for l, part in enumerate(pack(blocks)):
            ybuf[q, :, l] = part.reshape(LANES, 8, RANK)

    def probe_values():
        values(0, grid[0:PAIRS, 8:24, :])

    def local_tendency_values():
        grid[0:PAIRS, 7:8, :] = jnp.zeros((PAIRS, 1, WIDE), F32)
        grid[0:PAIRS, 24:25, :] = jnp.zeros((PAIRS, 1, WIDE), F32)
        full_tendency()
        values(1, tend[...])

    load_metric.wait()

    @pl.when(jnp.logical_and(polar, northern))
    def _():
        load_forward.wait()
        probe_values()

    pl.semaphore_wait(barrier, 4 + jnp.where(polar, LANES - 3, 0))

    def remote(src, dst, send, recv, lat, lon):
        return pltpu.make_async_remote_copy(
            src_ref=src, dst_ref=dst, send_sem=send, recv_sem=recv, device_id=(lat, lon), device_id_type=MESH
        )

    def halo_copy(start, count, to, which, lat, lon):
        return remote(
            halo_out.at[start : start + count], halo_in.at[pl.ds(to, count)], halo_send, halo_recv.at[which], lat, lon
        )

    def halo_arrival(start, stop, which):
        return remote(
            halo_out.at[start:stop], halo_in.at[start:stop], halo_send, halo_recv.at[which], b, west
        )

    @pl.when(northern)
    def _():
        halo_copy(NEAR, 4, NEAR + 4 * slot_n, 0, nb, nl).start()

    halo_copy(NEAR + 4, 4, NEAR + 4 * slot_s, 0, sb, sl).start()

    @pl.when(jnp.logical_not(northern))
    def _():
        halo_copy(NEAR, 4, NEAR + 4 * slot_n, 0, nb, nl).start()

    halo_copy(SIDES, 1, SIDES + 1, 0, b, west).start()
    halo_copy(SIDES + 1, 1, SIDES, 0, b, east_lane).start()

    others = pl.ds(0, LANES - 1)

    def all_y(q):
        return remote(ybuf.at[q, others], yr.at[q, others], y_send.at[q], y_recv.at[q], b, west)

    def send_values(q):
        for d in FAR_FIRST:
            o = plus(i, d)
            remote(ybuf.at[q, o], yr.at[q, i], y_send.at[q], y_recv.at[q], b, o).start()

        yr[q, i] = ybuf[q, i]

    def c_copy(o):
        return remote(cb.at[o], yc.at[i], c_send, c_recv, b, o)

    def all_c():
        return remote(cb.at[others], yc.at[others], c_send, c_recv, b, west)

    def z_copy(q, j):
        return remote(zbuf.at[q, j], zr.at[q, i], z_send.at[q], z_recv.at[q], b, j)

    def all_z(q):
        return remote(zbuf.at[q, others], zr.at[q, others], z_send.at[q], z_recv.at[q], b, west)

    def edge_sends():
        slot = jnp.where(own_half == 0, slot_n, slot_s)
        lat = jnp.where(own_half == 0, nb, sb)

        def away(j, lon):
            remote(eb.at[j], bz.at[slot, i // 2], b_send, b_recv.at[slot], lat, lon).start()

        @pl.when(jnp.logical_not(edge_over))
        def _():
            for j in ANSWERS:
                away(j, j)

        @pl.when(edge_over)
        def _():
            for j in ANSWERS:
                lon = (j + LANES // 2) % LANES

                @pl.when(i != lon)
                def _():
                    away(j, lon)

                @pl.when(i == lon)
                def _():
                    pltpu.make_async_copy(eb.at[j], bz.at[slot, i // 2], b_recv.at[slot]).start()

    def own_rows(q):
        row = lax.broadcasted_iota(jnp.int32, (8, 128), 0)
        cutoff = jnp.zeros((8, 128), jnp.int32)
        for r in range(8):
            cutoff = jnp.where(row == r, cut_s[8 * own_half + r], cutoff)
        keeps = []
        for group in range(4):
            wave = waves_of(group, lax.broadcasted_iota(jnp.int32, (8, 128), 1))
            keep = jnp.where(wave > cutoff, 2.0 / (COLS * LANES), 0.0)
            keeps.append(jnp.concatenate([keep] * LEV, axis=0))
        all_y(q).wait_recv()
        levels = unpack([yr[q, :, l].reshape(LANES * 8, RANK) for l in range(LEV - 1)])
        if q == 1:
            edge_row = jnp.where(row == 7 * own_half, 1.0, 0.0)
            all_c().wait_recv()
            ends = jnp.concatenate([yc[j, 8:16, :] for j in range(LANES)], axis=0)
            ends = pltpu.roll(ends, lax.rem(128 - 2 * LEV * (i // 2), 128), 1)
            levels = [
                levels[l]
                + ends[:, 2 * l : 2 * l + 1] * hm[0:1, :]
                + ends[:, 2 * l + 1 : 2 * l + 2] * hm[1:2, :]
                + jnp.concatenate([edge_row * yc[j, l : l + 1, :] for j in range(LANES)], axis=0)
                for l in range(LEV)
            ]
        lanes = [
            jnp.concatenate([levels[l][8 * j : 8 * j + 8, :] for l in range(LEV)], axis=0) for j in range(LANES)
        ]
        coefs = [
            to_coefs(jnp.concatenate(pair, axis=1), table.at[TO_COEFS + 256 * group : TO_COEFS + 256 * (group + 1)])
            for group, pair in enumerate(over_lanes(lanes))
        ]
        kept = [coef * keep for coef, keep in zip(coefs, keeps)]
        backs = [
            from_coefs(coef, table.at[FROM_COEFS + 256 * group : FROM_COEFS + 256 * (group + 1)])
            for group, coef in enumerate(kept)
        ]
        pairs = [(back[:, :RANK], back[:, RANK:]) for back in backs]
        zs = [z.reshape(LEV, 8, RANK) for z in to_lanes(pairs)]
        for l, part in enumerate(pack([jnp.concatenate([z[l] for z in zs], axis=0) for l in range(LEV)])):
            zbuf[q, :, l] = part.reshape(LANES, 8, RANK)

        def edges():
            for j, z in enumerate(zs):
                edge = jnp.where(own_half == 0, z[:, 0, :], z[:, 7, :])
                eb[j] = edge if q == 0 else eb[j] + edge
            if q == 1:
                edge_sends()

        if q == 1:
            pl.when(outward)(edges)
        for j in ANSWERS:
            @pl.when(i != j)
            def _():
                z_copy(q, j).start()

        if q == 1:
            pl.when(jnp.logical_not(outward))(edges)
        else:
            edges()
        zr[q, i] = zbuf[q, i]

    def evaluate(z):
        return from_modes(z, table.at[EVALUATE : EVALUATE + 384], table.at[EVALUATE + 384 : TO_COEFS])

    def project(q, h):
        levels = unpack(
            [jnp.concatenate([zr[q, 2 * f + h, l] for f in range(FIELDS)], axis=0) for l in range(LEV - 1)]
        )
        z = jnp.concatenate(
            [levels[l][8 * f : 8 * f + 8, :] for f in range(FIELDS) for l in range(LEV)], axis=0
        )
        out = evaluate(z)
        return [[out[8 * (LEV * f + l) : 8 * (LEV * f + l + 1), :] for l in range(LEV)] for f in range(FIELDS)]


    @pl.when(jnp.logical_and(polar, jnp.logical_not(northern)))
    def _():
        load_forward.wait()
        probe_values()

    @pl.when(polar)
    def _():
        send_values(0)
        local_tendency_values()
        send_values(1)

    edge_rows((REST + 4, REST + 11), slice(PAIRS, PAIRS + 2 * LEV), (8, 23))

    halo_arrival(NEAR, REST, 0).wait_recv()
    row16 = lax.broadcasted_iota(jnp.int32, (PAIRS, 1), 0)
    is_v = jnp.logical_and(row16 >= LEV, row16 < 2 * LEV)
    is_temp = jnp.logical_and(row16 >= 2 * LEV, row16 < 3 * LEV)

    def flip(s, minus):
        sign = jnp.where(row16 < 2 * LEV, -1.0, 1.0) * minus
        return jnp.where(over_pole[s], sign, 1.0)

    def row_link(x):
        return jnp.where(is_v, roll(x, -LEV, 0), jnp.where(is_temp, roll(x, LEV, 0), 0.0))

    def wind(buffer, s, w):
        base = REST + 7 * s + 4
        rows = [buffer[base + t // 2, 8 * (t % 2) + LEV * w : 8 * (t % 2) + LEV * (w + 1), :] for t in range(4)]
        return jnp.concatenate([jnp.concatenate(rows, axis=1)] * FIELDS, axis=0)

    def row_of(buffer, start):
        return jnp.concatenate([buffer[start + t] for t in range(4)], axis=1)

    @pl.when(polar)
    def _():
        added = []
        for s, sign in ((0, 0.5 * time_step), (1, -0.5 * time_step)):
            ghost = flip(s, 1.0) * row_of(halo_in, NEAR + 4 * s)
            added.append(sign * (wind(halo_out, s, 1) * ghost + coupling * row_link(ghost)))
            xb[s] = added[s]
        y = to_modes(jnp.concatenate(added, axis=0), table.at[FORWARD:EVALUATE])
        for s in range(2):
            for f in range(FIELDS):
                cb[2 * f + s, 0:LEV, :] = y[(s * FIELDS + f) * LEV : (s * FIELDS + f + 1) * LEV, :]
        ends = []
        for side, sign in ((0, -1.0), (1, 1.0)):
            came = halo_in[SIDES + side]
            along_x = (sign * hm[8:24, :]) * (roll(came, -1, 1) if side == 0 else came)
            mine = jnp.where(
                jnp.logical_and(lane2 >= 2 * PAIRS, lane2 < 2 * (PAIRS + LEV)), halo_out[SIDES + side], 0.0
            )
            ew = sum(roll(mine, 2 * LEV * f - 2 * PAIRS - side, 1) for f in range(FIELDS))
            linked = jnp.where(
                lane2 < 2 * LEV,
                roll(along_x, -4 * LEV, 1),
                jnp.where(
                    jnp.logical_and(lane2 >= 4 * LEV, lane2 < 6 * LEV), roll(along_x, 4 * LEV, 1), 0.0
                ),
            )
            ends.append(time_step * (-ew * along_x - coupling * linked))
        ends = jnp.where(lax.rem(lane2, 2) == 0, ends[0], roll(ends[1], 1, 1))
        for f in range(FIELDS):
            for h in range(2):
                cb[2 * f + h, 8:16, :] = ends[8 * h : 8 * h + 8, :]

        for d in FAR_FIRST:
            c_copy(plus(i, d)).start()

        yc[i] = cb[i]

    from_west = roll(halo_in[SIDES], 126, 1)
    from_east = roll(halo_in[SIDES + 1], COLS - 384, 1)
    both = jnp.where(jnp.logical_and(lane2 >= 66, lane2 < 114), from_east, from_west)
    in_halo = jnp.logical_or(jnp.logical_and(lane2 >= 66, lane2 < 68), lane2 >= 126)
    for e in range(PAIRS + 2 * LEV):
        grid[e, 8:24, 384:512] = jnp.where(in_halo, roll(both, -2 * e, 1), grid[e, 8:24, 384:512])
    edge_rows((REST, REST + 7), slice(0, PAIRS), (9, 22))
    for s, near in enumerate((8, 23)):
        halo_out[REST + 7 * s + 6] = grid[0:PAIRS, near, 384:512]
    halo_copy(REST, 7, REST + 7 * slot_n, 1, nb, nl).start()
    halo_copy(REST + 7, 7, REST + 7 * slot_s, 1, sb, sl).start()

    @pl.when(polar)
    def _():
        load_cut.wait()
        load_others.wait()
        own_rows(0)

    @pl.when(jnp.logical_and(polar, northern))
    def _():
        own_rows(1)

    halo_arrival(REST, BLOCKS, 1).wait_recv()
    edge_row = (7, 24)
    edge_probe = []
    for s in range(2):
        edge_probe.append(
            jnp.concatenate([halo_in[NEAR + 4 * s + t] for t in range(3)] + [halo_in[REST + 7 * s + 6]], axis=1)
        )
        grid[0:PAIRS, edge_row[s], :] = flip(s, 1.0) * edge_probe[s]

    @pl.when(polar)
    def _():
        for s, row in ((0, 0), (1, 15)):
            tend[:, row, :] = tend[:, row, :] + xb[s]
        side_tendency()

    @pl.when(jnp.logical_not(polar))
    def _():
        full_tendency()

    def edge_weights(s, a):
        return -wind(halo_in, s, 1) * a - coupling * row_link(a)

    for s, inward in ((0, 1.0), (1, -1.0)):
        mid = edge_probe[s]
        half = jnp.concatenate([hm[edge_row[s] : edge_row[s] + 1, :]] * 4, axis=1)
        along_x = half * (roll(mid, -1, 1) - roll(mid, 1, 1))
        turn = jnp.where(over_pole[s], -0.5 * inward, 0.5 * inward)
        along_y = turn * (flip(s, 1.0) * row_of(halo_out, NEAR + 4 * s) - row_of(halo_in, REST + 7 * s))
        linked = jnp.where(row16 < LEV, roll(along_x, -2 * LEV, 0), row_link(along_y))
        linked = linked + jnp.where(is_temp, roll(along_x, 2 * LEV, 0), 0.0)
        up = jnp.where(lax.rem(row16, LEV) == 0, mid, roll(mid, 1, 0))
        down = jnp.where(lax.rem(row16, LEV) == LEV - 1, mid, roll(mid, -1, 0))
        t = -(wind(halo_in, s, 0) * along_x + wind(halo_in, s, 1) * along_y) - coupling * linked
        a = mid + time_step * (t + mixing * (up + down - 2.0 * mid))
        gy[0:PAIRS, edge_row[s], :] = flip(s, -1.0) * edge_weights(s, a)

    @pl.when(jnp.logical_and(polar, jnp.logical_not(northern)))
    def _():
        own_rows(1)

    def row_weights(a, nw):
        return (
            -nw * a[0],
            -nw * a[1] - coupling * a[2],
            -nw * a[2] - coupling * a[1],
            -nw * a[3],
        )

    def put_weights(l, h, a):
        for f, weight in enumerate(row_weights(a, grid[PAIRS + LEV + l, h : h + 8, :])):
            gy[f * LEV + l, h : h + 8, :] = weight

    @pl.when(polar)
    def _():
        all_z(0).wait_recv()
        for h in (8, 16):
            taken = project(0, h // 8 - 1)
            for l in range(LEV):
                for f in range(FIELDS):
                    n, rows = f * LEV + l, slice(h - 8, h)
                    adj[n, rows, :] = grid[n, h : h + 8, :] + tend[n, rows, :] - taken[f][l]
        all_z(1).wait_recv()
        for h in (8, 16):
            taken = project(1, h // 8 - 1)
            for l in range(LEV):
                a = []
                for f in range(FIELDS):
                    n, rows = f * LEV + l, slice(h - 8, h)
                    change = tend[n, rows, :] - taken[f][l]
                    tend[n, rows, :] = change
                    tan_out[f, l, rows, :] = (grid[n, h : h + 8, :] + change)[:, :COLS]
                    a.append(adj[n, rows, :] - taken[f][l])
                    adj[n, rows, :] = a[f]
                put_weights(l, h, a)

    @pl.when(jnp.logical_not(polar))
    def _():
        @pl.loop(0, LEV, unroll=True)
        def _(l):
            for h in (8, 16):
                a = []
                for f in range(FIELDS):
                    n, rows = f * LEV + l, slice(h - 8, h)
                    a.append(grid[n, h : h + 8, :] + tend[n, rows, :])
                    tan_out[f, l, rows, :] = a[f][:, :COLS]
                    adj[n, rows, :] = a[f]
                put_weights(l, h, a)

    @pl.loop(0, LEV, unroll=True)
    def _(l):
        lo = jnp.maximum(l - 1, 0)
        hi = jnp.minimum(l + 1, LEV - 1)
        for h in (8, 16):
            rows = slice(h - 8, h)
            half = jnp.concatenate([hm[h : h + 8, :]] * 4, axis=1)
            ew = grid[PAIRS + l, h : h + 8, :]
            a = [adj[f * LEV + l, rows, :] for f in range(FIELDS)]
            col_weights = (
                -ew * a[0] - coupling * a[2],
                -ew * a[1],
                -ew * a[2] - coupling * a[0],
                -ew * a[3],
            )
            for f in range(FIELDS):
                n = f * LEV + l
                back = half * (roll(col_weights[f], 1, 1) - roll(col_weights[f], -1, 1))
                back = back + 0.5 * (gy[n, h - 1 : h + 7, :] - gy[n, h + 1 : h + 9, :])
                back = back + mixing * (adj[f * LEV + lo, rows, :] + adj[f * LEV + hi, rows, :] - 2.0 * a[f])
                diag = grid[n, h : h + 8, :] * (tend[n, rows, :] + time_step * back)
                diag_out[f, l, rows, :] = diag[:, :COLS]

    @pl.when(jnp.logical_and(near_polar, jnp.logical_not(polar)))
    def _():
        load_part.wait()

    for s, wanted in enumerate((above_polar, below_polar)):
        @pl.when(wanted)
        def _():
            row = 15 * s
            north_wind = wind(halo_in, s, 1)
            factor = ((0.5, -0.5)[s] * time_step) * grid[0:PAIRS, 8 + row, :] * flip(s, -1.0)
            before = [diag_out[f, :, row, :] for f in range(FIELDS)]
            remote(bz.at[s], bz.at[s], b_send, b_recv.at[s], nb, nl).wait_recv()
            taken = evaluate(jnp.concatenate([bz[s, f] for f in range(FIELDS)], axis=0))
            more = factor * (north_wind * taken + coupling * row_link(taken))
            for f in range(FIELDS):
                diag_out[f, :, row, :] = before[f] + more[f * LEV : (f + 1) * LEV, :COLS]

    halo_arrival(0, BLOCKS, 0).wait_send()

    @pl.when(polar)
    def _():
        all_c().wait_send()
        for q in range(2):
            all_y(q).wait_send()
            all_z(q).wait_send()

        @pl.when(edge_over)
        def _():
            remote(eb.at[others], eb.at[others], b_send, b_recv.at[0], b, west).wait_send()

        @pl.when(jnp.logical_not(edge_over))
        def _():
            remote(eb, eb, b_send, b_recv.at[0], b, west).wait_send()


def hand_out(tan_in, diag_in, tan_out, diag_out, sem):
    copies = [
        pltpu.make_async_copy(src, dst, sem.at[n])
        for n, (src, dst) in enumerate(((tan_in, tan_out), (diag_in, diag_out)))
    ]
    for copy in copies:
        copy.start()
    for copy in copies:
        copy.wait()


def per_device(bands, row_signs, col_signs, spread, east_wind, north_wind, cutoffs):
    any_spec = pl.BlockSpec(memory_space=pl.ANY)
    out = jax.ShapeDtypeStruct((FIELDS, LEV, ROWS, COLS), F32)
    tables = [jnp.asarray(half_metric(bands)), jnp.asarray(mode_factors())]
    operands = (spread, east_wind, north_wind, row_signs, col_signs, cutoffs, *tables)
    vmem = pltpu.VMEM
    dma = pltpu.SemaphoreType.DMA
    held = pltpu.VMEM(out.shape, F32)
    results = pl.pallas_call(
        functools.partial(kernel, bands),
        out_shape=(held, held),
        in_specs=[any_spec] * 8,
        out_specs=(pl.BlockSpec(memory_space=pltpu.VMEM),) * 2,
        scratch_shapes=[
            vmem((FIELDS, LEV, ROWS, COLS), F32),
            vmem((2, LEV, ROWS, COLS), F32),
            vmem((FIELDS, LEV, ROWS), jnp.int32),
            vmem((FIELDS, LEV, COLS), jnp.int32),
            pltpu.SMEM((ROWS,), jnp.int32),
            vmem((32, 128), F32),
            vmem((TABLE_ROWS, 2 * RANK), BF16),
            vmem((PAIRS + 2 * LEV, 32, WIDE), F32),
            vmem((BLOCKS, 16, 128), F32),
            vmem((BLOCKS, 16, 128), F32),
            vmem((2, LANES, LEV - 1, 8, RANK), F32),
            vmem((2, LANES, LEV - 1, 8, RANK), F32),
            vmem((2, PAIRS, WIDE), F32),
            vmem((LANES, 16, RANK), F32),
            vmem((LANES, 16, RANK), F32),
            vmem((2, LANES, LEV - 1, 8, RANK), F32),
            vmem((2, LANES, LEV - 1, 8, RANK), F32),
            vmem((LANES, LEV, RANK), F32),
            vmem((2, FIELDS, LEV, RANK), F32),
            vmem((PAIRS, ROWS, WIDE), F32),
            vmem((PAIRS, ROWS, WIDE), F32),
            vmem((PAIRS, 32, WIDE), F32),
            dma((8,)),
            dma,
            dma((2,)),
            dma((2,)),
            dma((2,)),
            dma,
            dma,
            dma((2,)),
            dma((2,)),
            dma,
            dma((2,)),
        ],
        compiler_params=pltpu.CompilerParams(
            collective_id=0, has_side_effects=True, vmem_limit_bytes=32 * 2**20
        ),
        cost_estimate=pl.CostEstimate(flops=10**9, bytes_accessed=4 * 10**6, transcendentals=0),
    )(*(pltpu.with_memory_space_constraint(x, pltpu.HBM) for x in operands))
    return pl.pallas_call(
        hand_out,
        out_shape=(out, out),
        in_specs=[any_spec] * 2,
        out_specs=(any_spec, any_spec),
        scratch_shapes=[dma((2,))],
        compiler_params=pltpu.CompilerParams(vmem_limit_bytes=2**20),
    )(*(pltpu.with_memory_space_constraint(x, pltpu.VMEM) for x in results))


def solution(mesh):
    return jax.shard_map(
        functools.partial(per_device, mesh.shape["lat"]),
        mesh=mesh,
        in_specs=(
            P(None, None, "lat"),
            P(None, None, "lon"),
            P(None, None, "lat", "lon"),
            P(None, "lat", "lon"),
            P(None, "lat", "lon"),
            P("lat"),
        ),
        out_specs=(P(None, None, "lat", "lon"), P(None, None, "lat", "lon")),
        check_vma=False,
    )
```

```python
import functools

import jax
import jax.numpy as jnp
import ml_dtypes
import numpy as np
from jax import lax
from jax.experimental import pallas as pl
from jax.experimental.pallas import tpu as pltpu
from jax.sharding import PartitionSpec as P

KTOP = 256
POLAR = 32
RANK = 128
USED = 96
ROWS = 16
COLS = 450
WIDE = 512
LANES = 8
FIELDS = 4
LEV = 4
PAIRS = FIELDS * LEV

time_step = 0.5
coupling = 0.5
mixing = 0.2
metric_cap = 4.0

FORWARD, EVALUATE, TO_COEFS, FROM_COEFS, TABLE_ROWS = 0, 512, 1280, 2304, 3328
NEAR, SIDES, REST, BLOCKS = 0, 8, 10, 24

FAR_FIRST = (6, 2, 5, 3, 7, 1, 4)
ANSWERS = (0, 4, 1, 3, 2, 7, 5, 6)

MESH = pl.DeviceIdType.MESH
F32 = jnp.float32
BF16 = jnp.bfloat16


def split_table(table):
    high = table.astype(ml_dtypes.bfloat16)
    low = (table - high.astype(np.float64)).astype(ml_dtypes.bfloat16)
    return high, low


def waves_of(group, lane_index):
    place = lane_index % 64
    second = place // 32
    other = (8 - group) if group else 4
    residue = group + second * (other - group)
    return 8 * (place % 32) + residue + (8 * (1 - second) if group == 0 else 0)


@functools.lru_cache(None)
def mode_factors():
    total = COLS * LANES
    size = COLS + 2
    place = np.arange(size, dtype=np.float64)
    width = (KTOP + 0.5) / total
    diag = ((size - 1 - 2 * place) / 2) ** 2 * np.cos(2 * np.pi * width)
    side = place[1:] * (size - place[1:]) / 2
    vectors = np.linalg.eigh(np.diag(diag) + np.diag(side, 1) + np.diag(side, -1))[1]
    basis = np.concatenate([vectors[:, ::-1][:, :USED], np.zeros((size, RANK - USED))], axis=1)
    basis = basis * np.where(basis[size // 2] < 0, -1.0, 1.0)
    weights = []
    for group in range(4):
        waves = waves_of(group, np.arange(64))
        angle = 2 * np.pi / total * ((np.arange(size)[:, None] - 1) * waves[None, :] % total)
        alpha, beta = basis.T @ np.cos(angle), basis.T @ np.sin(angle)
        if group:
            sign = np.where(np.arange(64) < 32, 1.0, -1.0)
            top, low = (alpha, beta), (sign * beta, -sign * alpha)
        else:
            use = np.where(np.arange(64) < 32, 1.0, 0.0)
            top, low = (use * alpha, use * beta), ((1 - use) * alpha, (1 - use) * beta)
        weights.append(np.concatenate([np.concatenate(top, axis=1), np.concatenate(low, axis=1)], axis=0))
    weights = np.round(np.stack(weights) * 2.0**22) / 2.0**22
    wide = np.zeros((RANK, WIDE))
    wide[:, : COLS + 1] = basis[1:].T
    wide[:, WIDE - 1] = basis[0]
    wide = np.round(wide * 2.0**26) / 2.0**26
    wide_h, wide_l = split_table(wide)
    own = np.where(np.arange(WIDE)[:, None] < COLS, 1, 0).astype(ml_dtypes.bfloat16)
    high, low = split_table(weights)
    back = np.concatenate([np.swapaxes(part, 1, 2) for part in (high, low)], axis=1)
    evaluate = np.concatenate([wide_h, wide_l, wide_h], axis=0)
    return np.concatenate(
        [
            np.concatenate([wide_h.T * own, wide_l.T * own], axis=1),
            evaluate[:, : WIDE // 2],
            evaluate[:, WIDE // 2 :],
            np.concatenate([high, low], axis=2).reshape(-1, 2 * RANK),
            back.reshape(-1, 2 * RANK),
        ],
        axis=0,
    )


ROOT = float(np.sqrt(0.5))


def over_lanes(y):
    s = [y[j] + y[j + 4] for j in range(4)]
    d = [y[j] - y[j + 4] for j in range(4)]
    even, odd = s[0] + s[2], s[1] + s[3]
    minus, plus = ROOT * (d[1] - d[3]), ROOT * (d[1] + d[3])
    return [
        (even + odd, even - odd),
        (d[0] + minus, -(d[2] + plus)),
        (s[0] - s[2], s[3] - s[1]),
        (d[0] - minus, d[2] - plus),
    ]


def to_lanes(pairs):
    (y0, y4), (u1, v1), (u2, v2), (u3, v3) = pairs
    even, odd = y0 + y4, y0 - y4
    s = [even + u2, odd - v2, even - u2, odd + v2]
    du, sv = ROOT * (u1 - u3), ROOT * (v1 + v3)
    d = [u1 + u3, du - sv, v3 - v1, -du - sv]
    return [s[j] + d[j] for j in range(4)] + [s[j] - d[j] for j in range(4)]


@functools.lru_cache(None)
def half_metric(bands):
    total = bands * ROWS
    rows = np.clip(np.arange(bands)[:, None] * ROWS - 8 + np.arange(32)[None, :], 0, total - 1)
    metric = np.minimum(1.0 / np.cos(np.pi * ((rows + 0.5) / total - 0.5)), metric_cap)
    table = np.broadcast_to((0.5 * metric).astype(np.float32)[:, :, None], (bands, 32, 128)).copy()
    forward = mode_factors()[FORWARD : FORWARD + WIDE].astype(np.float32)
    for row, col in enumerate((0, COLS - 1)):
        table[:, row] = forward[col, :RANK] + forward[col, RANK:]
    return table


def dot_cols(a, b):
    return lax.dot_general(a, b, (((1,), (0,)), ((), ())), preferred_element_type=F32)


def split(x):
    high = x.astype(BF16)
    return high, (x - high.astype(F32)).astype(BF16)


def to_modes(x, table):
    xh, xl = split(x)
    half = table.shape[1] // 2
    wide = dot_cols(xh, table[...])
    return wide[:, :half] + wide[:, half:] + dot_cols(xl, table[:, 0:half])


def from_modes(z, *tables):
    zh, zl = split(z)
    three = jnp.concatenate([zh, zh, zl], axis=1)
    return jnp.concatenate([dot_cols(three, table[...]) for table in tables], axis=1)


def to_coefs(x, table):
    rows = x.shape[0]
    wide = dot_cols(jnp.concatenate(split(x), axis=0), table[...])
    half = wide.shape[1] // 2
    return wide[:rows, :half] + wide[:rows, half:] + wide[rows:, :half]


def from_coefs(z, table):
    zh, zl = split(z)
    rows = jnp.concatenate([jnp.concatenate([zh, zh], axis=1), jnp.concatenate([zl, jnp.zeros_like(zl)], axis=1)], axis=0)
    wide = dot_cols(rows, table[...])
    return wide[: z.shape[0]] + wide[z.shape[0] :]


def pack(levels):
    lane = lax.broadcasted_iota(jnp.int32, (1, RANK), 1)
    return [jnp.where(lane < USED, levels[l], roll(levels[3], 96 - 32 * l, 1)) for l in range(3)]


def unpack(parts):
    lane = lax.broadcasted_iota(jnp.int32, (1, RANK), 1)
    last = jnp.where(lane < 64, roll(parts[1], 64, 1), roll(parts[2], 96, 1))
    return parts + [jnp.where(lane < 32, roll(parts[0], 32, 1), last)]


def roll(x, shift, axis):
    return pltpu.roll(x, shift % x.shape[axis], axis)


def roll_blocks(x, shift):
    return roll(x.reshape(x.shape[0] * x.shape[1], x.shape[2]), shift, 1).reshape(x.shape)


def fold(x):
    while x.shape[0] > 1:
        half = x.shape[0] // 2
        x = x[:half] + roll_blocks(x[half:], 2 * half)
    return x


def kernel(
    bands, spread, east, north, rs, cs, cut, metric, table_in, tan_out, diag_out,
    spread_v, winds_v, rs_v, cs_v, cut_s, hm, table,
    grid, halo_out, halo_in, ybuf, yr, xb, cb, yc, zbuf, zr, eb, bz,
    tend, adj, gy,
    in_sem, halo_send, halo_recv, y_send, y_recv, c_send, c_recv, z_send, z_recv, b_send, b_recv,
):
    b = lax.axis_index("lat")
    i = lax.axis_index("lon")
    caps = POLAR // ROWS
    is_north = b == 0
    is_south = b == bands - 1
    northern = b < bands // 2
    polar = jnp.logical_or(b < caps, b >= bands - caps)
    above_polar = jnp.logical_or(b <= caps, is_south)
    below_polar = jnp.logical_or(b >= bands - caps - 1, is_north)
    near_polar = jnp.logical_or(above_polar, below_polar)
    across = lax.rem(i + LANES // 2, LANES)
    west = lax.rem(i + LANES - 1, LANES)
    east_lane = lax.rem(i + 1, LANES)
    nb = jnp.where(is_north, 0, b - 1)
    nl = jnp.where(is_north, across, i)
    sb = jnp.where(is_south, bands - 1, b + 1)
    sl = jnp.where(is_south, across, i)
    slot_n = jnp.where(is_north, 0, 1)
    slot_s = jnp.where(is_south, 1, 0)
    own_half = lax.rem(i, 2)
    edge_over = jnp.where(own_half == 0, is_north, is_south)
    over_pole = (is_north, is_south)
    outward = jnp.logical_and(b == bands - caps, own_half == 0)

    def plus(lane, d):
        return lax.rem(lane + d, LANES)

    load_spread = pltpu.make_async_copy(spread, spread_v, in_sem.at[0])
    load_rows = pltpu.make_async_copy(rs, rs_v, in_sem.at[1])
    load_cols = pltpu.make_async_copy(cs, cs_v, in_sem.at[2])
    load_metric = pltpu.make_async_copy(metric.at[b], hm, in_sem.at[4])
    load_cut = pltpu.make_async_copy(cut, cut_s, in_sem.at[5])

    def load_table(start, stop, sem):
        return pltpu.make_async_copy(table_in.at[start:stop], table.at[start:stop], in_sem.at[sem])

    load_forward = load_table(FORWARD, EVALUATE, 6)
    load_others = load_table(EVALUATE, TABLE_ROWS, 7)
    load_part = load_table(EVALUATE, TO_COEFS, 7)
    barrier = pltpu.get_barrier_semaphore()

    def greet(lat, lon):
        pl.semaphore_signal(barrier, inc=1, device_id=(lat, lon), device_id_type=MESH)

    greet(nb, nl)
    greet(sb, sl)

    @pl.when(polar)
    def _():
        for d in FAR_FIRST[:4]:
            greet(b, plus(i, d))

    greet(b, west)
    greet(b, east_lane)
    load_spread.start()
    load_rows.start()
    load_cols.start()
    pltpu.make_async_copy(east, winds_v.at[0], in_sem.at[3]).start()
    pltpu.make_async_copy(north, winds_v.at[1], in_sem.at[3]).start()
    load_metric.start()

    @pl.when(polar)
    def _():
        greet(b, across)
        load_forward.start()
        load_cut.start()

    @pl.when(jnp.logical_and(near_polar, jnp.logical_not(polar)))
    def _():
        load_part.start()

    load_rows.wait()
    load_cols.wait()
    load_spread.wait()
    grid[:, 8:24, 384:512] = jnp.zeros((PAIRS + 2 * LEV, ROWS, 128), F32)
    row_part = jnp.concatenate([rs_v[f] for f in range(FIELDS)], axis=0)
    row_part = (2 * row_part - 1).astype(F32).T
    for f in range(FIELDS):
        col_part = (2 * cs_v[f] - 1).astype(F32)
        for l in range(LEV):
            n = f * LEV + l
            grid[n, 8:24, 0:COLS] = spread_v[f, l] * (row_part[:, n : n + 1] * col_part[l : l + 1, :])

    @pl.when(polar)
    def _():
        load_others.start()

    pltpu.make_async_copy(winds_v, winds_v, in_sem.at[3]).wait()
    for w in range(2):
        for l in range(LEV):
            grid[PAIRS + w * LEV + l, 8:24, 0:COLS] = winds_v[w, l]

    def edge_rows(start, entries, rows):
        for s, row in enumerate(rows):
            for t in range(4):
                values = grid[entries, row, 128 * t : 128 * t + 128]
                if entries == slice(0, PAIRS):
                    halo_out[start[s] + t] = values
                else:
                    halo_out[start[s] + t // 2, 8 * (t % 2) : 8 * (t % 2) + 8, :] = values

    edge_rows((NEAR, NEAR + 4), slice(0, PAIRS), (8, 23))
    lane2 = lax.broadcasted_iota(jnp.int32, (1, 128), 1)
    for s, (start, shift) in enumerate(((0, 0), (384, COLS - 2 - 384))):
        ends = jnp.logical_and(lane2 >= shift, lane2 < shift + 2)
        tile = jnp.where(ends, grid[:, 8:24, start : start + 128], 0.0)
        packed = fold(tile[:PAIRS]) + roll_blocks(fold(tile[PAIRS:]), 2 * PAIRS)
        halo_out[SIDES + s] = roll_blocks(packed, -shift)[0]

    def tendency_rows(h, l, at, half):
        lo = jnp.maximum(l - 1, 0)
        hi = jnp.minimum(l + 1, LEV - 1)
        ew = at(PAIRS + l, h)
        nw = at(PAIRS + LEV + l, h)
        mids, along_x, along_y = [], [], []
        for f in range(FIELDS):
            mid = at(f * LEV + l, h)
            mids.append(mid)
            along_x.append(half * (roll(mid, -1, 1) - roll(mid, 1, 1)))
            along_y.append(0.5 * (at(f * LEV + l, h + 1) - at(f * LEV + l, h - 1)))
        linked = (along_x[2], along_y[2], along_x[0] + along_y[1], None)
        out = []
        for f in range(FIELDS):
            mixed = at(f * LEV + lo, h) + at(f * LEV + hi, h) - 2.0 * mids[f]
            t = -(ew * along_x[f] + nw * along_y[f]) + mixing * mixed
            if linked[f] is not None:
                t = t - coupling * linked[f]
            out.append(time_step * t)
        return out

    def full_tendency():
        @pl.loop(0, LEV, unroll=True)
        def _(l):
            for h in (8, 16):
                half = jnp.concatenate([hm[h : h + 8, :]] * 4, axis=1)
                for f, t in enumerate(tendency_rows(h, l, lambda n, r: grid[n, r : r + 8, :], half)):
                    tend[f * LEV + l, h - 8 : h, :] = t

    def side_tendency():
        lane = lax.broadcasted_iota(jnp.int32, (1, 128), 1)
        late = jnp.logical_or(jnp.logical_or(lane == 65, lane == 66), lane == 127)

        def at(n, r):
            return jnp.where(lane < 2, grid[n, r : r + 8, 0:128], grid[n, r : r + 8, 384:512])

        @pl.loop(0, LEV, unroll=True)
        def _(l):
            for h in (8, 16):
                for f, t in enumerate(tendency_rows(h, l, at, hm[h : h + 8, :])):
                    n, rows = f * LEV + l, slice(h - 8, h)
                    tend[n, rows, 0:128] = jnp.where(lane == 0, t, tend[n, rows, 0:128])
                    tend[n, rows, 384:512] = jnp.where(late, t, tend[n, rows, 384:512])

    def values(q, x):
        y = to_modes(x.reshape(PAIRS * ROWS, WIDE), table.at[FORWARD:EVALUATE])
        y = y.reshape(FIELDS, LEV, 2, 8, RANK)
        blocks = [
            jnp.concatenate([y[f, l, h] for f in range(FIELDS) for h in range(2)], axis=0) for l in range(LEV)
        ]
        for l, part in enumerate(pack(blocks)):
            ybuf[q, :, l] = part.reshape(LANES, 8, RANK)

    def probe_values():
        values(0, grid[0:PAIRS, 8:24, :])

    def local_tendency_values():
        grid[0:PAIRS, 7:8, :] = jnp.zeros((PAIRS, 1, WIDE), F32)
        grid[0:PAIRS, 24:25, :] = jnp.zeros((PAIRS, 1, WIDE), F32)
        full_tendency()
        values(1, tend[...])

    load_metric.wait()

    @pl.when(jnp.logical_and(polar, northern))
    def _():
        load_forward.wait()
        probe_values()

    pl.semaphore_wait(barrier, 4 + jnp.where(polar, LANES - 3, 0))

    def remote(src, dst, send, recv, lat, lon):
        return pltpu.make_async_remote_copy(
            src_ref=src, dst_ref=dst, send_sem=send, recv_sem=recv, device_id=(lat, lon), device_id_type=MESH
        )

    def halo_copy(start, count, to, which, lat, lon):
        return remote(
            halo_out.at[start : start + count], halo_in.at[pl.ds(to, count)], halo_send, halo_recv.at[which], lat, lon
        )

    def halo_arrival(start, stop, which):
        return remote(
            halo_out.at[start:stop], halo_in.at[start:stop], halo_send, halo_recv.at[which], b, west
        )

    @pl.when(northern)
    def _():
        halo_copy(NEAR, 4, NEAR + 4 * slot_n, 0, nb, nl).start()

    halo_copy(NEAR + 4, 4, NEAR + 4 * slot_s, 0, sb, sl).start()

    @pl.when(jnp.logical_not(northern))
    def _():
        halo_copy(NEAR, 4, NEAR + 4 * slot_n, 0, nb, nl).start()

    halo_copy(SIDES, 1, SIDES + 1, 0, b, west).start()
    halo_copy(SIDES + 1, 1, SIDES, 0, b, east_lane).start()

    others = pl.ds(0, LANES - 1)

    def all_y(q):
        return remote(ybuf.at[q, others], yr.at[q, others], y_send.at[q], y_recv.at[q], b, west)

    def send_values(q):
        for d in FAR_FIRST:
            o = plus(i, d)
            remote(ybuf.at[q, o], yr.at[q, i], y_send.at[q], y_recv.at[q], b, o).start()

        yr[q, i] = ybuf[q, i]

    def c_copy(o):
        return remote(cb.at[o], yc.at[i], c_send, c_recv, b, o)

    def all_c():
        return remote(cb.at[others], yc.at[others], c_send, c_recv, b, west)

    def z_copy(q, j):
        return remote(zbuf.at[q, j], zr.at[q, i], z_send.at[q], z_recv.at[q], b, j)

    def all_z(q):
        return remote(zbuf.at[q, others], zr.at[q, others], z_send.at[q], z_recv.at[q], b, west)

    def edge_sends():
        slot = jnp.where(own_half == 0, slot_n, slot_s)
        lat = jnp.where(own_half == 0, nb, sb)

        def away(j, lon):
            remote(eb.at[j], bz.at[slot, i // 2], b_send, b_recv.at[slot], lat, lon).start()

        @pl.when(jnp.logical_not(edge_over))
        def _():
            for j in ANSWERS:
                away(j, j)

        @pl.when(edge_over)
        def _():
            for j in ANSWERS:
                lon = (j + LANES // 2) % LANES

                @pl.when(i != lon)
                def _():
                    away(j, lon)

                @pl.when(i == lon)
                def _():
                    pltpu.make_async_copy(eb.at[j], bz.at[slot, i // 2], b_recv.at[slot]).start()

    def own_rows(q):
        row = lax.broadcasted_iota(jnp.int32, (8, 128), 0)
        cutoff = jnp.zeros((8, 128), jnp.int32)
        for r in range(8):
            cutoff = jnp.where(row == r, cut_s[8 * own_half + r], cutoff)
        keeps = []
        for group in range(4):
            wave = waves_of(group, lax.broadcasted_iota(jnp.int32, (8, 128), 1))
            keep = jnp.where(wave > cutoff, 2.0 / (COLS * LANES), 0.0)
            keeps.append(jnp.concatenate([keep] * LEV, axis=0))
        all_y(q).wait_recv()
        levels = unpack([yr[q, :, l].reshape(LANES * 8, RANK) for l in range(LEV - 1)])
        if q == 1:
            edge_row = jnp.where(row == 7 * own_half, 1.0, 0.0)
            all_c().wait_recv()
            ends = jnp.concatenate([yc[j, 8:16, :] for j in range(LANES)], axis=0)
            ends = pltpu.roll(ends, lax.rem(128 - 2 * LEV * (i // 2), 128), 1)
            levels = [
                levels[l]
                + ends[:, 2 * l : 2 * l + 1] * hm[0:1, :]
                + ends[:, 2 * l + 1 : 2 * l + 2] * hm[1:2, :]
                + jnp.concatenate([edge_row * yc[j, l : l + 1, :] for j in range(LANES)], axis=0)
                for l in range(LEV)
            ]
        lanes = [
            jnp.concatenate([levels[l][8 * j : 8 * j + 8, :] for l in range(LEV)], axis=0) for j in range(LANES)
        ]
        coefs = [
            to_coefs(jnp.concatenate(pair, axis=1), table.at[TO_COEFS + 256 * group : TO_COEFS + 256 * (group + 1)])
            for group, pair in enumerate(over_lanes(lanes))
        ]
        kept = [coef * keep for coef, keep in zip(coefs, keeps)]
        backs = [
            from_coefs(coef, table.at[FROM_COEFS + 256 * group : FROM_COEFS + 256 * (group + 1)])
            for group, coef in enumerate(kept)
        ]
        pairs = [(back[:, :RANK], back[:, RANK:]) for back in backs]
        zs = [z.reshape(LEV, 8, RANK) for z in to_lanes(pairs)]
        for l, part in enumerate(pack([jnp.concatenate([z[l] for z in zs], axis=0) for l in range(LEV)])):
            zbuf[q, :, l] = part.reshape(LANES, 8, RANK)

        def edges():
            for j, z in enumerate(zs):
                edge = jnp.where(own_half == 0, z[:, 0, :], z[:, 7, :])
                eb[j] = edge if q == 0 else eb[j] + edge
            if q == 1:
                edge_sends()

        if q == 1:
            pl.when(outward)(edges)
        for j in ANSWERS:
            @pl.when(i != j)
            def _():
                z_copy(q, j).start()

        if q == 1:
            pl.when(jnp.logical_not(outward))(edges)
        else:
            edges()
        zr[q, i] = zbuf[q, i]

    def evaluate(z):
        return from_modes(z, table.at[EVALUATE : EVALUATE + 384], table.at[EVALUATE + 384 : TO_COEFS])

    def project(q, h):
        levels = unpack(
            [jnp.concatenate([zr[q, 2 * f + h, l] for f in range(FIELDS)], axis=0) for l in range(LEV - 1)]
        )
        z = jnp.concatenate(
            [levels[l][8 * f : 8 * f + 8, :] for f in range(FIELDS) for l in range(LEV)], axis=0
        )
        out = evaluate(z)
        return [[out[8 * (LEV * f + l) : 8 * (LEV * f + l + 1), :] for l in range(LEV)] for f in range(FIELDS)]


    @pl.when(jnp.logical_and(polar, jnp.logical_not(northern)))
    def _():
        load_forward.wait()
        probe_values()

    @pl.when(polar)
    def _():
        send_values(0)
        local_tendency_values()
        send_values(1)

    edge_rows((REST + 4, REST + 11), slice(PAIRS, PAIRS + 2 * LEV), (8, 23))

    halo_arrival(NEAR, REST, 0).wait_recv()
    row16 = lax.broadcasted_iota(jnp.int32, (PAIRS, 1), 0)
    is_v = jnp.logical_and(row16 >= LEV, row16 < 2 * LEV)
    is_temp = jnp.logical_and(row16 >= 2 * LEV, row16 < 3 * LEV)

    def flip(s, minus):
        sign = jnp.where(row16 < 2 * LEV, -1.0, 1.0) * minus
        return jnp.where(over_pole[s], sign, 1.0)

    def row_link(x):
        return jnp.where(is_v, roll(x, -LEV, 0), jnp.where(is_temp, roll(x, LEV, 0), 0.0))

    def wind(buffer, s, w):
        base = REST + 7 * s + 4
        rows = [buffer[base + t // 2, 8 * (t % 2) + LEV * w : 8 * (t % 2) + LEV * (w + 1), :] for t in range(4)]
        return jnp.concatenate([jnp.concatenate(rows, axis=1)] * FIELDS, axis=0)

    def row_of(buffer, start):
        return jnp.concatenate([buffer[start + t] for t in range(4)], axis=1)

    @pl.when(polar)
    def _():
        added = []
        for s, sign in ((0, 0.5 * time_step), (1, -0.5 * time_step)):
            ghost = flip(s, 1.0) * row_of(halo_in, NEAR + 4 * s)
            added.append(sign * (wind(halo_out, s, 1) * ghost + coupling * row_link(ghost)))
            xb[s] = added[s]
        y = to_modes(jnp.concatenate(added, axis=0), table.at[FORWARD:EVALUATE])
        for s in range(2):
            for f in range(FIELDS):
                cb[2 * f + s, 0:LEV, :] = y[(s * FIELDS + f) * LEV : (s * FIELDS + f + 1) * LEV, :]
        ends = []
        for side, sign in ((0, -1.0), (1, 1.0)):
            came = halo_in[SIDES + side]
            along_x = (sign * hm[8:24, :]) * (roll(came, -1, 1) if side == 0 else came)
            mine = jnp.where(
                jnp.logical_and(lane2 >= 2 * PAIRS, lane2 < 2 * (PAIRS + LEV)), halo_out[SIDES + side], 0.0
            )
            ew = sum(roll(mine, 2 * LEV * f - 2 * PAIRS - side, 1) for f in range(FIELDS))
            linked = jnp.where(
                lane2 < 2 * LEV,
                roll(along_x, -4 * LEV, 1),
                jnp.where(
                    jnp.logical_and(lane2 >= 4 * LEV, lane2 < 6 * LEV), roll(along_x, 4 * LEV, 1), 0.0
                ),
            )
            ends.append(time_step * (-ew * along_x - coupling * linked))
        ends = jnp.where(lax.rem(lane2, 2) == 0, ends[0], roll(ends[1], 1, 1))
        for f in range(FIELDS):
            for h in range(2):
                cb[2 * f + h, 8:16, :] = ends[8 * h : 8 * h + 8, :]

        for d in FAR_FIRST:
            c_copy(plus(i, d)).start()

        yc[i] = cb[i]

    from_west = roll(halo_in[SIDES], 126, 1)
    from_east = roll(halo_in[SIDES + 1], COLS - 384, 1)
    both = jnp.where(jnp.logical_and(lane2 >= 66, lane2 < 114), from_east, from_west)
    in_halo = jnp.logical_or(jnp.logical_and(lane2 >= 66, lane2 < 68), lane2 >= 126)
    for e in range(PAIRS + 2 * LEV):
        grid[e, 8:24, 384:512] = jnp.where(in_halo, roll(both, -2 * e, 1), grid[e, 8:24, 384:512])
    edge_rows((REST, REST + 7), slice(0, PAIRS), (9, 22))
    for s, near in enumerate((8, 23)):
        halo_out[REST + 7 * s + 6] = grid[0:PAIRS, near, 384:512]
    halo_copy(REST, 7, REST + 7 * slot_n, 1, nb, nl).start()
    halo_copy(REST + 7, 7, REST + 7 * slot_s, 1, sb, sl).start()

    @pl.when(polar)
    def _():
        load_cut.wait()
        load_others.wait()
        own_rows(0)

    @pl.when(jnp.logical_and(polar, northern))
    def _():
        own_rows(1)

    halo_arrival(REST, BLOCKS, 1).wait_recv()
    edge_row = (7, 24)
    edge_probe = []
    for s in range(2):
        edge_probe.append(
            jnp.concatenate([halo_in[NEAR + 4 * s + t] for t in range(3)] + [halo_in[REST + 7 * s + 6]], axis=1)
        )
        grid[0:PAIRS, edge_row[s], :] = flip(s, 1.0) * edge_probe[s]

    @pl.when(polar)
    def _():
        for s, row in ((0, 0), (1, 15)):
            tend[:, row, :] = tend[:, row, :] + xb[s]
        side_tendency()

    @pl.when(jnp.logical_not(polar))
    def _():
        full_tendency()

    def edge_weights(s, a):
        return -wind(halo_in, s, 1) * a - coupling * row_link(a)

    for s, inward in ((0, 1.0), (1, -1.0)):
        mid = edge_probe[s]
        half = jnp.concatenate([hm[edge_row[s] : edge_row[s] + 1, :]] * 4, axis=1)
        along_x = half * (roll(mid, -1, 1) - roll(mid, 1, 1))
        turn = jnp.where(over_pole[s], -0.5 * inward, 0.5 * inward)
        along_y = turn * (flip(s, 1.0) * row_of(halo_out, NEAR + 4 * s) - row_of(halo_in, REST + 7 * s))
        linked = jnp.where(row16 < LEV, roll(along_x, -2 * LEV, 0), row_link(along_y))
        linked = linked + jnp.where(is_temp, roll(along_x, 2 * LEV, 0), 0.0)
        up = jnp.where(lax.rem(row16, LEV) == 0, mid, roll(mid, 1, 0))
        down = jnp.where(lax.rem(row16, LEV) == LEV - 1, mid, roll(mid, -1, 0))
        t = -(wind(halo_in, s, 0) * along_x + wind(halo_in, s, 1) * along_y) - coupling * linked
        a = mid + time_step * (t + mixing * (up + down - 2.0 * mid))
        gy[0:PAIRS, edge_row[s], :] = flip(s, -1.0) * edge_weights(s, a)

    @pl.when(jnp.logical_and(polar, jnp.logical_not(northern)))
    def _():
        own_rows(1)

    def row_weights(a, nw):
        return (
            -nw * a[0],
            -nw * a[1] - coupling * a[2],
            -nw * a[2] - coupling * a[1],
            -nw * a[3],
        )

    def put_weights(l, h, a):
        for f, weight in enumerate(row_weights(a, grid[PAIRS + LEV + l, h : h + 8, :])):
            gy[f * LEV + l, h : h + 8, :] = weight

    @pl.when(polar)
    def _():
        all_z(0).wait_recv()
        for h in (8, 16):
            taken = project(0, h // 8 - 1)
            for l in range(LEV):
                for f in range(FIELDS):
                    n, rows = f * LEV + l, slice(h - 8, h)
                    adj[n, rows, :] = grid[n, h : h + 8, :] + tend[n, rows, :] - taken[f][l]
        all_z(1).wait_recv()
        for h in (8, 16):
            taken = project(1, h // 8 - 1)
            for l in range(LEV):
                a = []
                for f in range(FIELDS):
                    n, rows = f * LEV + l, slice(h - 8, h)
                    change = tend[n, rows, :] - taken[f][l]
                    tend[n, rows, :] = change
                    tan_out[f, l, rows, :] = (grid[n, h : h + 8, :] + change)[:, :COLS]
                    a.append(adj[n, rows, :] - taken[f][l])
                    adj[n, rows, :] = a[f]
                put_weights(l, h, a)

    @pl.when(jnp.logical_not(polar))
    def _():
        @pl.loop(0, LEV, unroll=True)
        def _(l):
            for h in (8, 16):
                a = []
                for f in range(FIELDS):
                    n, rows = f * LEV + l, slice(h - 8, h)
                    a.append(grid[n, h : h + 8, :] + tend[n, rows, :])
                    tan_out[f, l, rows, :] = a[f][:, :COLS]
                    adj[n, rows, :] = a[f]
                put_weights(l, h, a)

    @pl.loop(0, LEV, unroll=True)
    def _(l):
        lo = jnp.maximum(l - 1, 0)
        hi = jnp.minimum(l + 1, LEV - 1)
        for h in (8, 16):
            rows = slice(h - 8, h)
            half = jnp.concatenate([hm[h : h + 8, :]] * 4, axis=1)
            ew = grid[PAIRS + l, h : h + 8, :]
            a = [adj[f * LEV + l, rows, :] for f in range(FIELDS)]
            col_weights = (
                -ew * a[0] - coupling * a[2],
                -ew * a[1],
                -ew * a[2] - coupling * a[0],
                -ew * a[3],
            )
            for f in range(FIELDS):
                n = f * LEV + l
                back = half * (roll(col_weights[f], 1, 1) - roll(col_weights[f], -1, 1))
                back = back + 0.5 * (gy[n, h - 1 : h + 7, :] - gy[n, h + 1 : h + 9, :])
                back = back + mixing * (adj[f * LEV + lo, rows, :] + adj[f * LEV + hi, rows, :] - 2.0 * a[f])
                diag = grid[n, h : h + 8, :] * (tend[n, rows, :] + time_step * back)
                diag_out[f, l, rows, :] = diag[:, :COLS]

    @pl.when(jnp.logical_and(near_polar, jnp.logical_not(polar)))
    def _():
        load_part.wait()

    for s, wanted in enumerate((above_polar, below_polar)):
        @pl.when(wanted)
        def _():
            row = 15 * s
            north_wind = wind(halo_in, s, 1)
            factor = ((0.5, -0.5)[s] * time_step) * grid[0:PAIRS, 8 + row, :] * flip(s, -1.0)
            before = [diag_out[f, :, row, :] for f in range(FIELDS)]
            remote(bz.at[s], bz.at[s], b_send, b_recv.at[s], nb, nl).wait_recv()
            taken = evaluate(jnp.concatenate([bz[s, f] for f in range(FIELDS)], axis=0))
            more = factor * (north_wind * taken + coupling * row_link(taken))
            for f in range(FIELDS):
                diag_out[f, :, row, :] = before[f] + more[f * LEV : (f + 1) * LEV, :COLS]

    halo_arrival(0, BLOCKS, 0).wait_send()

    @pl.when(polar)
    def _():
        all_c().wait_send()
        for q in range(2):
            all_y(q).wait_send()
            all_z(q).wait_send()

        @pl.when(edge_over)
        def _():
            remote(eb.at[others], eb.at[others], b_send, b_recv.at[0], b, west).wait_send()

        @pl.when(jnp.logical_not(edge_over))
        def _():
            remote(eb, eb, b_send, b_recv.at[0], b, west).wait_send()


def hand_out(tan_in, diag_in, tan_out, diag_out, sem):
    copies = [
        pltpu.make_async_copy(src, dst, sem.at[n])
        for n, (src, dst) in enumerate(((tan_in, tan_out), (diag_in, diag_out)))
    ]
    for copy in copies:
        copy.start()
    for copy in copies:
        copy.wait()


def per_device(bands, row_signs, col_signs, spread, east_wind, north_wind, cutoffs):
    any_spec = pl.BlockSpec(memory_space=pl.ANY)
    out = jax.ShapeDtypeStruct((FIELDS, LEV, ROWS, COLS), F32)
    tables = [jnp.asarray(half_metric(bands)), jnp.asarray(mode_factors())]
    operands = (spread, east_wind, north_wind, row_signs, col_signs, cutoffs, *tables)
    vmem = pltpu.VMEM
    dma = pltpu.SemaphoreType.DMA
    held = pltpu.VMEM(out.shape, F32)
    results = pl.pallas_call(
        functools.partial(kernel, bands),
        out_shape=(held, held),
        in_specs=[any_spec] * 8,
        out_specs=(pl.BlockSpec(memory_space=pltpu.VMEM),) * 2,
        scratch_shapes=[
            vmem((FIELDS, LEV, ROWS, COLS), F32),
            vmem((2, LEV, ROWS, COLS), F32),
            vmem((FIELDS, LEV, ROWS), jnp.int32),
            vmem((FIELDS, LEV, COLS), jnp.int32),
            pltpu.SMEM((ROWS,), jnp.int32),
            vmem((32, 128), F32),
            vmem((TABLE_ROWS, 2 * RANK), BF16),
            vmem((PAIRS + 2 * LEV, 32, WIDE), F32),
            vmem((BLOCKS, 16, 128), F32),
            vmem((BLOCKS, 16, 128), F32),
            vmem((2, LANES, LEV - 1, 8, RANK), F32),
            vmem((2, LANES, LEV - 1, 8, RANK), F32),
            vmem((2, PAIRS, WIDE), F32),
            vmem((LANES, 16, RANK), F32),
            vmem((LANES, 16, RANK), F32),
            vmem((2, LANES, LEV - 1, 8, RANK), F32),
            vmem((2, LANES, LEV - 1, 8, RANK), F32),
            vmem((LANES, LEV, RANK), F32),
            vmem((2, FIELDS, LEV, RANK), F32),
            vmem((PAIRS, ROWS, WIDE), F32),
            vmem((PAIRS, ROWS, WIDE), F32),
            vmem((PAIRS, 32, WIDE), F32),
            dma((8,)),
            dma,
            dma((2,)),
            dma((2,)),
            dma((2,)),
            dma,
            dma,
            dma((2,)),
            dma((2,)),
            dma,
            dma((2,)),
        ],
        compiler_params=pltpu.CompilerParams(
            collective_id=0, has_side_effects=True, vmem_limit_bytes=32 * 2**20
        ),
        cost_estimate=pl.CostEstimate(flops=10**9, bytes_accessed=4 * 10**6, transcendentals=0),
    )(*(pltpu.with_memory_space_constraint(x, pltpu.HBM) for x in operands))
    return pl.pallas_call(
        hand_out,
        out_shape=(out, out),
        in_specs=[any_spec] * 2,
        out_specs=(any_spec, any_spec),
        scratch_shapes=[dma((2,))],
        compiler_params=pltpu.CompilerParams(vmem_limit_bytes=2**20),
    )(*(pltpu.with_memory_space_constraint(x, pltpu.VMEM) for x in results))


def solution(mesh):
    return jax.shard_map(
        functools.partial(per_device, mesh.shape["lat"]),
        mesh=mesh,
        in_specs=(
            P(None, None, "lat"),
            P(None, None, "lon"),
            P(None, None, "lat", "lon"),
            P(None, "lat", "lon"),
            P(None, "lat", "lon"),
            P("lat"),
        ),
        out_specs=(P(None, None, "lat", "lon"), P(None, None, "lat", "lon")),
        check_vma=False,
    )
```

```python
import functools

import jax
import jax.numpy as jnp
import ml_dtypes
import numpy as np
from jax import lax
from jax.experimental import pallas as pl
from jax.experimental.pallas import tpu as pltpu
from jax.sharding import PartitionSpec as P

KTOP = 256
POLAR = 32
RANK = 128
USED = 96
ROWS = 16
COLS = 450
WIDE = 512
LANES = 8
FIELDS = 4
LEV = 4
PAIRS = FIELDS * LEV

time_step = 0.5
coupling = 0.5
mixing = 0.2
metric_cap = 4.0

FORWARD, EVALUATE, TO_COEFS, FROM_COEFS, TABLE_ROWS = 0, 512, 1280, 2304, 3328
NEAR, SIDES, REST, BLOCKS = 0, 8, 10, 24

FAR_FIRST = (6, 2, 5, 3, 7, 1, 4)
ANSWERS = (0, 4, 1, 3, 2, 7, 5, 6)

MESH = pl.DeviceIdType.MESH
F32 = jnp.float32
BF16 = jnp.bfloat16


def split_table(table):
    high = table.astype(ml_dtypes.bfloat16)
    low = (table - high.astype(np.float64)).astype(ml_dtypes.bfloat16)
    return high, low


def waves_of(group, lane_index):
    place = lane_index % 64
    second = place // 32
    other = (8 - group) if group else 4
    residue = group + second * (other - group)
    return 8 * (place % 32) + residue + (8 * (1 - second) if group == 0 else 0)


@functools.lru_cache(None)
def mode_factors():
    total = COLS * LANES
    size = COLS + 2
    place = np.arange(size, dtype=np.float64)
    width = (KTOP + 0.5) / total
    diag = ((size - 1 - 2 * place) / 2) ** 2 * np.cos(2 * np.pi * width)
    side = place[1:] * (size - place[1:]) / 2
    vectors = np.linalg.eigh(np.diag(diag) + np.diag(side, 1) + np.diag(side, -1))[1]
    basis = np.concatenate([vectors[:, ::-1][:, :USED], np.zeros((size, RANK - USED))], axis=1)
    basis = basis * np.where(basis[size // 2] < 0, -1.0, 1.0)
    weights = []
    for group in range(4):
        waves = waves_of(group, np.arange(64))
        angle = 2 * np.pi / total * ((np.arange(size)[:, None] - 1) * waves[None, :] % total)
        alpha, beta = basis.T @ np.cos(angle), basis.T @ np.sin(angle)
        if group:
            sign = np.where(np.arange(64) < 32, 1.0, -1.0)
            top, low = (alpha, beta), (sign * beta, -sign * alpha)
        else:
            use = np.where(np.arange(64) < 32, 1.0, 0.0)
            top, low = (use * alpha, use * beta), ((1 - use) * alpha, (1 - use) * beta)
        weights.append(np.concatenate([np.concatenate(top, axis=1), np.concatenate(low, axis=1)], axis=0))
    weights = np.round(np.stack(weights) * 2.0**22) / 2.0**22
    wide = np.zeros((RANK, WIDE))
    wide[:, : COLS + 1] = basis[1:].T
    wide[:, WIDE - 1] = basis[0]
    wide = np.round(wide * 2.0**26) / 2.0**26
    wide_h, wide_l = split_table(wide)
    own = np.where(np.arange(WIDE)[:, None] < COLS, 1, 0).astype(ml_dtypes.bfloat16)
    high, low = split_table(weights)
    back = np.concatenate([np.swapaxes(part, 1, 2) for part in (high, low)], axis=1)
    evaluate = np.concatenate([wide_h, wide_l, wide_h], axis=0)
    return np.concatenate(
        [
            np.concatenate([wide_h.T * own, wide_l.T * own], axis=1),
            evaluate[:, : WIDE // 2],
            evaluate[:, WIDE // 2 :],
            np.concatenate([high, low], axis=2).reshape(-1, 2 * RANK),
            back.reshape(-1, 2 * RANK),
        ],
        axis=0,
    )


ROOT = float(np.sqrt(0.5))


def over_lanes(y):
    s = [y[j] + y[j + 4] for j in range(4)]
    d = [y[j] - y[j + 4] for j in range(4)]
    even, odd = s[0] + s[2], s[1] + s[3]
    minus, plus = ROOT * (d[1] - d[3]), ROOT * (d[1] + d[3])
    return [
        (even + odd, even - odd),
        (d[0] + minus, -(d[2] + plus)),
        (s[0] - s[2], s[3] - s[1]),
        (d[0] - minus, d[2] - plus),
    ]


def to_lanes(pairs):
    (y0, y4), (u1, v1), (u2, v2), (u3, v3) = pairs
    even, odd = y0 + y4, y0 - y4
    s = [even + u2, odd - v2, even - u2, odd + v2]
    du, sv = ROOT * (u1 - u3), ROOT * (v1 + v3)
    d = [u1 + u3, du - sv, v3 - v1, -du - sv]
    return [s[j] + d[j] for j in range(4)] + [s[j] - d[j] for j in range(4)]


@functools.lru_cache(None)
def half_metric(bands):
    total = bands * ROWS
    rows = np.clip(np.arange(bands)[:, None] * ROWS - 8 + np.arange(32)[None, :], 0, total - 1)
    metric = np.minimum(1.0 / np.cos(np.pi * ((rows + 0.5) / total - 0.5)), metric_cap)
    table = np.broadcast_to((0.5 * metric).astype(np.float32)[:, :, None], (bands, 32, 128)).copy()
    forward = mode_factors()[FORWARD : FORWARD + WIDE].astype(np.float32)
    for row, col in enumerate((0, COLS - 1)):
        table[:, row] = forward[col, :RANK] + forward[col, RANK:]
    return table


def dot_cols(a, b):
    return lax.dot_general(a, b, (((1,), (0,)), ((), ())), preferred_element_type=F32)


def split(x):
    high = x.astype(BF16)
    return high, (x - high.astype(F32)).astype(BF16)


def to_modes(x, table):
    xh, xl = split(x)
    half = table.shape[1] // 2
    wide = dot_cols(xh, table[...])
    return wide[:, :half] + wide[:, half:] + dot_cols(xl, table[:, 0:half])


def from_modes(z, *tables):
    zh, zl = split(z)
    three = jnp.concatenate([zh, zh, zl], axis=1)
    return jnp.concatenate([dot_cols(three, table[...]) for table in tables], axis=1)


def to_coefs(x, table):
    rows = x.shape[0]
    wide = dot_cols(jnp.concatenate(split(x), axis=0), table[...])
    half = wide.shape[1] // 2
    return wide[:rows, :half] + wide[:rows, half:] + wide[rows:, :half]


def from_coefs(z, table):
    zh, zl = split(z)
    rows = jnp.concatenate([jnp.concatenate([zh, zh], axis=1), jnp.concatenate([zl, jnp.zeros_like(zl)], axis=1)], axis=0)
    wide = dot_cols(rows, table[...])
    return wide[: z.shape[0]] + wide[z.shape[0] :]


def pack(levels):
    lane = lax.broadcasted_iota(jnp.int32, (1, RANK), 1)
    return [jnp.where(lane < USED, levels[l], roll(levels[3], 96 - 32 * l, 1)) for l in range(3)]


def unpack(parts):
    lane = lax.broadcasted_iota(jnp.int32, (1, RANK), 1)
    last = jnp.where(lane < 64, roll(parts[1], 64, 1), roll(parts[2], 96, 1))
    return parts + [jnp.where(lane < 32, roll(parts[0], 32, 1), last)]


def roll(x, shift, axis):
    return pltpu.roll(x, shift % x.shape[axis], axis)


def kernel(
    bands, spread, east, north, rs, cs, cut, metric, table_in, tan_out, diag_out,
    spread_v, winds_v, rs_v, cs_v, cut_s, hm, table,
    grid, halo_out, halo_in, ybuf, yr, xb, cb, yc, zbuf, zr, eb, bz,
    tend, adj, gy,
    in_sem, halo_send, halo_recv, y_send, y_recv, c_send, c_recv, z_send, z_recv, b_send, b_recv,
):
    b = lax.axis_index("lat")
    i = lax.axis_index("lon")
    caps = POLAR // ROWS
    is_north = b == 0
    is_south = b == bands - 1
    northern = b < bands // 2
    polar = jnp.logical_or(b < caps, b >= bands - caps)
    above_polar = jnp.logical_or(b <= caps, is_south)
    below_polar = jnp.logical_or(b >= bands - caps - 1, is_north)
    near_polar = jnp.logical_or(above_polar, below_polar)
    across = lax.rem(i + LANES // 2, LANES)
    west = lax.rem(i + LANES - 1, LANES)
    east_lane = lax.rem(i + 1, LANES)
    nb = jnp.where(is_north, 0, b - 1)
    nl = jnp.where(is_north, across, i)
    sb = jnp.where(is_south, bands - 1, b + 1)
    sl = jnp.where(is_south, across, i)
    slot_n = jnp.where(is_north, 0, 1)
    slot_s = jnp.where(is_south, 1, 0)
    own_half = lax.rem(i, 2)
    edge_over = jnp.where(own_half == 0, is_north, is_south)
    over_pole = (is_north, is_south)
    outward = jnp.logical_and(b == bands - caps, own_half == 0)

    def plus(lane, d):
        return lax.rem(lane + d, LANES)

    load_spread = pltpu.make_async_copy(spread, spread_v, in_sem.at[0])
    load_rows = pltpu.make_async_copy(rs, rs_v, in_sem.at[1])
    load_cols = pltpu.make_async_copy(cs, cs_v, in_sem.at[2])
    load_metric = pltpu.make_async_copy(metric.at[b], hm, in_sem.at[4])
    load_cut = pltpu.make_async_copy(cut, cut_s, in_sem.at[5])

    def load_table(start, stop, sem):
        return pltpu.make_async_copy(table_in.at[start:stop], table.at[start:stop], in_sem.at[sem])

    load_forward = load_table(FORWARD, EVALUATE, 6)
    load_others = load_table(EVALUATE, TABLE_ROWS, 7)
    load_part = load_table(EVALUATE, TO_COEFS, 7)
    barrier = pltpu.get_barrier_semaphore()

    def greet(lat, lon):
        pl.semaphore_signal(barrier, inc=1, device_id=(lat, lon), device_id_type=MESH)

    greet(nb, nl)
    greet(sb, sl)

    @pl.when(polar)
    def _():
        for d in FAR_FIRST[:4]:
            greet(b, plus(i, d))

    greet(b, west)
    greet(b, east_lane)
    load_spread.start()
    load_rows.start()
    load_cols.start()
    pltpu.make_async_copy(east, winds_v.at[0], in_sem.at[3]).start()
    pltpu.make_async_copy(north, winds_v.at[1], in_sem.at[3]).start()
    load_metric.start()

    @pl.when(polar)
    def _():
        greet(b, across)
        load_forward.start()
        load_cut.start()

    @pl.when(jnp.logical_and(near_polar, jnp.logical_not(polar)))
    def _():
        load_part.start()

    load_rows.wait()
    load_cols.wait()
    load_spread.wait()
    grid[:, 8:24, 384:512] = jnp.zeros((PAIRS + 2 * LEV, ROWS, 128), F32)
    row_part = jnp.concatenate([rs_v[f] for f in range(FIELDS)], axis=0)
    row_part = (2 * row_part - 1).astype(F32).T
    for f in range(FIELDS):
        col_part = (2 * cs_v[f] - 1).astype(F32)
        for l in range(LEV):
            n = f * LEV + l
            grid[n, 8:24, 0:COLS] = spread_v[f, l] * (row_part[:, n : n + 1] * col_part[l : l + 1, :])

    @pl.when(polar)
    def _():
        load_others.start()

    pltpu.make_async_copy(winds_v, winds_v, in_sem.at[3]).wait()
    for w in range(2):
        for l in range(LEV):
            grid[PAIRS + w * LEV + l, 8:24, 0:COLS] = winds_v[w, l]

    def edge_rows(start, entries, rows):
        for s, row in enumerate(rows):
            for t in range(4):
                values = grid[entries, row, 128 * t : 128 * t + 128]
                if entries == slice(0, PAIRS):
                    halo_out[start[s] + t] = values
                else:
                    halo_out[start[s] + t // 2, 8 * (t % 2) : 8 * (t % 2) + 8, :] = values

    edge_rows((NEAR, NEAR + 4), slice(0, PAIRS), (8, 23))
    lane2 = lax.broadcasted_iota(jnp.int32, (1, 128), 1)
    for s, (start, shift) in enumerate(((0, 0), (384, COLS - 2 - 384))):
        ends = jnp.logical_and(lane2 >= shift, lane2 < shift + 2)
        parts = [
            roll(jnp.where(ends, grid[e, 8:24, start : start + 128], 0.0), 2 * e - shift, 1)
            for e in range(PAIRS + 2 * LEV)
        ]
        while len(parts) > 1:
            parts = [sum(parts[k : k + 2]) for k in range(0, len(parts), 2)]
        halo_out[SIDES + s] = parts[0]

    def tendency_rows(h, l, at, half):
        lo = jnp.maximum(l - 1, 0)
        hi = jnp.minimum(l + 1, LEV - 1)
        ew = at(PAIRS + l, h)
        nw = at(PAIRS + LEV + l, h)
        mids, along_x, along_y = [], [], []
        for f in range(FIELDS):
            mid = at(f * LEV + l, h)
            mids.append(mid)
            along_x.append(half * (roll(mid, -1, 1) - roll(mid, 1, 1)))
            along_y.append(0.5 * (at(f * LEV + l, h + 1) - at(f * LEV + l, h - 1)))
        linked = (along_x[2], along_y[2], along_x[0] + along_y[1], None)
        out = []
        for f in range(FIELDS):
            mixed = at(f * LEV + lo, h) + at(f * LEV + hi, h) - 2.0 * mids[f]
            t = -(ew * along_x[f] + nw * along_y[f]) + mixing * mixed
            if linked[f] is not None:
                t = t - coupling * linked[f]
            out.append(time_step * t)
        return out

    def full_tendency():
        @pl.loop(0, LEV, unroll=True)
        def _(l):
            for h in (8, 16):
                half = jnp.concatenate([hm[h : h + 8, :]] * 4, axis=1)
                for f, t in enumerate(tendency_rows(h, l, lambda n, r: grid[n, r : r + 8, :], half)):
                    tend[f * LEV + l, h - 8 : h, :] = t

    def side_tendency():
        lane = lax.broadcasted_iota(jnp.int32, (1, 128), 1)
        late = jnp.logical_or(jnp.logical_or(lane == 65, lane == 66), lane == 127)

        def at(n, r):
            return jnp.where(lane < 2, grid[n, r : r + 8, 0:128], grid[n, r : r + 8, 384:512])

        @pl.loop(0, LEV, unroll=True)
        def _(l):
            for h in (8, 16):
                for f, t in enumerate(tendency_rows(h, l, at, hm[h : h + 8, :])):
                    n, rows = f * LEV + l, slice(h - 8, h)
                    tend[n, rows, 0:128] = jnp.where(lane == 0, t, tend[n, rows, 0:128])
                    tend[n, rows, 384:512] = jnp.where(late, t, tend[n, rows, 384:512])

    def values(q, x):
        y = to_modes(x.reshape(PAIRS * ROWS, WIDE), table.at[FORWARD:EVALUATE])
        y = y.reshape(FIELDS, LEV, 2, 8, RANK)
        blocks = [
            jnp.concatenate([y[f, l, h] for f in range(FIELDS) for h in range(2)], axis=0) for l in range(LEV)
        ]
        for l, part in enumerate(pack(blocks)):
            ybuf[q, :, l] = part.reshape(LANES, 8, RANK)

    def probe_values():
        values(0, grid[0:PAIRS, 8:24, :])

    def local_tendency_values():
        grid[0:PAIRS, 7:8, :] = jnp.zeros((PAIRS, 1, WIDE), F32)
        grid[0:PAIRS, 24:25, :] = jnp.zeros((PAIRS, 1, WIDE), F32)
        full_tendency()
        values(1, tend[...])

    load_metric.wait()

    @pl.when(jnp.logical_and(polar, northern))
    def _():
        load_forward.wait()
        probe_values()

    pl.semaphore_wait(barrier, 4 + jnp.where(polar, LANES - 3, 0))

    def remote(src, dst, send, recv, lat, lon):
        return pltpu.make_async_remote_copy(
            src_ref=src, dst_ref=dst, send_sem=send, recv_sem=recv, device_id=(lat, lon), device_id_type=MESH
        )

    def halo_copy(start, count, to, which, lat, lon):
        return remote(
            halo_out.at[start : start + count], halo_in.at[pl.ds(to, count)], halo_send, halo_recv.at[which], lat, lon
        )

    def halo_arrival(start, stop, which):
        return remote(
            halo_out.at[start:stop], halo_in.at[start:stop], halo_send, halo_recv.at[which], b, west
        )

    @pl.when(northern)
    def _():
        halo_copy(NEAR, 4, NEAR + 4 * slot_n, 0, nb, nl).start()

    halo_copy(NEAR + 4, 4, NEAR + 4 * slot_s, 0, sb, sl).start()

    @pl.when(jnp.logical_not(northern))
    def _():
        halo_copy(NEAR, 4, NEAR + 4 * slot_n, 0, nb, nl).start()

    halo_copy(SIDES, 1, SIDES + 1, 0, b, west).start()
    halo_copy(SIDES + 1, 1, SIDES, 0, b, east_lane).start()

    others = pl.ds(0, LANES - 1)

    def all_y(q):
        return remote(ybuf.at[q, others], yr.at[q, others], y_send.at[q], y_recv.at[q], b, west)

    def send_values(q):
        for d in FAR_FIRST:
            o = plus(i, d)
            remote(ybuf.at[q, o], yr.at[q, i], y_send.at[q], y_recv.at[q], b, o).start()

        yr[q, i] = ybuf[q, i]

    def c_copy(o):
        return remote(cb.at[o], yc.at[i], c_send, c_recv, b, o)

    def all_c():
        return remote(cb.at[others], yc.at[others], c_send, c_recv, b, west)

    def z_copy(q, j):
        return remote(zbuf.at[q, j], zr.at[q, i], z_send.at[q], z_recv.at[q], b, j)

    def all_z(q):
        return remote(zbuf.at[q, others], zr.at[q, others], z_send.at[q], z_recv.at[q], b, west)

    def edge_sends():
        slot = jnp.where(own_half == 0, slot_n, slot_s)
        lat = jnp.where(own_half == 0, nb, sb)

        def away(j, lon):
            remote(eb.at[j], bz.at[slot, i // 2], b_send, b_recv.at[slot], lat, lon).start()

        @pl.when(jnp.logical_not(edge_over))
        def _():
            for j in ANSWERS:
                away(j, j)

        @pl.when(edge_over)
        def _():
            for j in ANSWERS:
                lon = (j + LANES // 2) % LANES

                @pl.when(i != lon)
                def _():
                    away(j, lon)

                @pl.when(i == lon)
                def _():
                    pltpu.make_async_copy(eb.at[j], bz.at[slot, i // 2], b_recv.at[slot]).start()

    def own_rows(q):
        row = lax.broadcasted_iota(jnp.int32, (8, 128), 0)
        cutoff = jnp.zeros((8, 128), jnp.int32)
        for r in range(8):
            cutoff = jnp.where(row == r, cut_s[8 * own_half + r], cutoff)
        keeps = []
        for group in range(4):
            wave = waves_of(group, lax.broadcasted_iota(jnp.int32, (8, 128), 1))
            keep = jnp.where(wave > cutoff, 2.0 / (COLS * LANES), 0.0)
            keeps.append(jnp.concatenate([keep] * LEV, axis=0))
        all_y(q).wait_recv()
        levels = unpack([yr[q, :, l].reshape(LANES * 8, RANK) for l in range(LEV - 1)])
        if q == 1:
            edge_row = jnp.where(row == 7 * own_half, 1.0, 0.0)
            all_c().wait_recv()
            ends = jnp.concatenate([yc[j, 8:16, :] for j in range(LANES)], axis=0)
            ends = pltpu.roll(ends, lax.rem(128 - 2 * LEV * (i // 2), 128), 1)
            levels = [
                levels[l]
                + ends[:, 2 * l : 2 * l + 1] * hm[0:1, :]
                + ends[:, 2 * l + 1 : 2 * l + 2] * hm[1:2, :]
                + jnp.concatenate([edge_row * yc[j, l : l + 1, :] for j in range(LANES)], axis=0)
                for l in range(LEV)
            ]
        lanes = [
            jnp.concatenate([levels[l][8 * j : 8 * j + 8, :] for l in range(LEV)], axis=0) for j in range(LANES)
        ]
        coefs = [
            to_coefs(jnp.concatenate(pair, axis=1), table.at[TO_COEFS + 256 * group : TO_COEFS + 256 * (group + 1)])
            for group, pair in enumerate(over_lanes(lanes))
        ]
        kept = [coef * keep for coef, keep in zip(coefs, keeps)]
        backs = [
            from_coefs(coef, table.at[FROM_COEFS + 256 * group : FROM_COEFS + 256 * (group + 1)])
            for group, coef in enumerate(kept)
        ]
        pairs = [(back[:, :RANK], back[:, RANK:]) for back in backs]
        zs = [z.reshape(LEV, 8, RANK) for z in to_lanes(pairs)]
        for l, part in enumerate(pack([jnp.concatenate([z[l] for z in zs], axis=0) for l in range(LEV)])):
            zbuf[q, :, l] = part.reshape(LANES, 8, RANK)

        def edges():
            for j, z in enumerate(zs):
                edge = jnp.where(own_half == 0, z[:, 0, :], z[:, 7, :])
                eb[j] = edge if q == 0 else eb[j] + edge
            if q == 1:
                edge_sends()

        if q == 1:
            pl.when(outward)(edges)
        for j in ANSWERS:
            @pl.when(i != j)
            def _():
                z_copy(q, j).start()

        if q == 1:
            pl.when(jnp.logical_not(outward))(edges)
        else:
            edges()
        zr[q, i] = zbuf[q, i]

    def evaluate(z):
        return from_modes(z, table.at[EVALUATE : EVALUATE + 384], table.at[EVALUATE + 384 : TO_COEFS])

    def project(q, h):
        levels = unpack(
            [jnp.concatenate([zr[q, 2 * f + h, l] for f in range(FIELDS)], axis=0) for l in range(LEV - 1)]
        )
        z = jnp.concatenate(
            [levels[l][8 * f : 8 * f + 8, :] for f in range(FIELDS) for l in range(LEV)], axis=0
        )
        out = evaluate(z)
        return [[out[8 * (LEV * f + l) : 8 * (LEV * f + l + 1), :] for l in range(LEV)] for f in range(FIELDS)]


    @pl.when(jnp.logical_and(polar, jnp.logical_not(northern)))
    def _():
        load_forward.wait()
        probe_values()

    @pl.when(polar)
    def _():
        send_values(0)
        local_tendency_values()
        send_values(1)

    edge_rows((REST + 4, REST + 11), slice(PAIRS, PAIRS + 2 * LEV), (8, 23))

    halo_arrival(NEAR, REST, 0).wait_recv()
    row16 = lax.broadcasted_iota(jnp.int32, (PAIRS, 1), 0)
    is_v = jnp.logical_and(row16 >= LEV, row16 < 2 * LEV)
    is_temp = jnp.logical_and(row16 >= 2 * LEV, row16 < 3 * LEV)

    def flip(s, minus):
        sign = jnp.where(row16 < 2 * LEV, -1.0, 1.0) * minus
        return jnp.where(over_pole[s], sign, 1.0)

    def row_link(x):
        return jnp.where(is_v, roll(x, -LEV, 0), jnp.where(is_temp, roll(x, LEV, 0), 0.0))

    def wind(buffer, s, w):
        base = REST + 7 * s + 4
        rows = [buffer[base + t // 2, 8 * (t % 2) + LEV * w : 8 * (t % 2) + LEV * (w + 1), :] for t in range(4)]
        return jnp.concatenate([jnp.concatenate(rows, axis=1)] * FIELDS, axis=0)

    def row_of(buffer, start):
        return jnp.concatenate([buffer[start + t] for t in range(4)], axis=1)

    @pl.when(polar)
    def _():
        added = []
        for s, sign in ((0, 0.5 * time_step), (1, -0.5 * time_step)):
            ghost = flip(s, 1.0) * row_of(halo_in, NEAR + 4 * s)
            added.append(sign * (wind(halo_out, s, 1) * ghost + coupling * row_link(ghost)))
            xb[s] = added[s]
        y = to_modes(jnp.concatenate(added, axis=0), table.at[FORWARD:EVALUATE])
        for s in range(2):
            for f in range(FIELDS):
                cb[2 * f + s, 0:LEV, :] = y[(s * FIELDS + f) * LEV : (s * FIELDS + f + 1) * LEV, :]
        ends = []
        for side, sign in ((0, -1.0), (1, 1.0)):
            came = halo_in[SIDES + side]
            along_x = (sign * hm[8:24, :]) * (roll(came, -1, 1) if side == 0 else came)
            mine = jnp.where(
                jnp.logical_and(lane2 >= 2 * PAIRS, lane2 < 2 * (PAIRS + LEV)), halo_out[SIDES + side], 0.0
            )
            ew = sum(roll(mine, 2 * LEV * f - 2 * PAIRS - side, 1) for f in range(FIELDS))
            linked = jnp.where(
                lane2 < 2 * LEV,
                roll(along_x, -4 * LEV, 1),
                jnp.where(
                    jnp.logical_and(lane2 >= 4 * LEV, lane2 < 6 * LEV), roll(along_x, 4 * LEV, 1), 0.0
                ),
            )
            ends.append(time_step * (-ew * along_x - coupling * linked))
        ends = jnp.where(lax.rem(lane2, 2) == 0, ends[0], roll(ends[1], 1, 1))
        for f in range(FIELDS):
            for h in range(2):
                cb[2 * f + h, 8:16, :] = ends[8 * h : 8 * h + 8, :]

        for d in FAR_FIRST:
            c_copy(plus(i, d)).start()

        yc[i] = cb[i]

    def first_owner_step():
        load_cut.wait()
        load_others.wait()
        own_rows(0)

    pl.when(jnp.logical_and(polar, northern))(first_owner_step)

    from_west = roll(halo_in[SIDES], 126, 1)
    from_east = roll(halo_in[SIDES + 1], COLS - 384, 1)
    both = jnp.where(jnp.logical_and(lane2 >= 66, lane2 < 114), from_east, from_west)
    in_halo = jnp.logical_or(jnp.logical_and(lane2 >= 66, lane2 < 68), lane2 >= 126)
    for e in range(PAIRS + 2 * LEV):
        grid[e, 8:24, 384:512] = jnp.where(in_halo, roll(both, -2 * e, 1), grid[e, 8:24, 384:512])
    edge_rows((REST, REST + 7), slice(0, PAIRS), (9, 22))
    for s, near in enumerate((8, 23)):
        halo_out[REST + 7 * s + 6] = grid[0:PAIRS, near, 384:512]
    halo_copy(REST, 7, REST + 7 * slot_n, 1, nb, nl).start()
    halo_copy(REST + 7, 7, REST + 7 * slot_s, 1, sb, sl).start()

    pl.when(jnp.logical_and(polar, jnp.logical_not(northern)))(first_owner_step)

    @pl.when(jnp.logical_and(polar, northern))
    def _():
        own_rows(1)

    halo_arrival(REST, BLOCKS, 1).wait_recv()
    edge_row = (7, 24)
    edge_probe = []
    for s in range(2):
        edge_probe.append(
            jnp.concatenate([halo_in[NEAR + 4 * s + t] for t in range(3)] + [halo_in[REST + 7 * s + 6]], axis=1)
        )
        grid[0:PAIRS, edge_row[s], :] = flip(s, 1.0) * edge_probe[s]

    @pl.when(polar)
    def _():
        for s, row in ((0, 0), (1, 15)):
            tend[:, row, :] = tend[:, row, :] + xb[s]
        side_tendency()

    @pl.when(jnp.logical_not(polar))
    def _():
        full_tendency()

    def edge_weights(s, a):
        return -wind(halo_in, s, 1) * a - coupling * row_link(a)

    for s, inward in ((0, 1.0), (1, -1.0)):
        mid = edge_probe[s]
        half = jnp.concatenate([hm[edge_row[s] : edge_row[s] + 1, :]] * 4, axis=1)
        along_x = half * (roll(mid, -1, 1) - roll(mid, 1, 1))
        turn = jnp.where(over_pole[s], -0.5 * inward, 0.5 * inward)
        along_y = turn * (flip(s, 1.0) * row_of(halo_out, NEAR + 4 * s) - row_of(halo_in, REST + 7 * s))
        linked = jnp.where(row16 < LEV, roll(along_x, -2 * LEV, 0), row_link(along_y))
        linked = linked + jnp.where(is_temp, roll(along_x, 2 * LEV, 0), 0.0)
        up = jnp.where(lax.rem(row16, LEV) == 0, mid, roll(mid, 1, 0))
        down = jnp.where(lax.rem(row16, LEV) == LEV - 1, mid, roll(mid, -1, 0))
        t = -(wind(halo_in, s, 0) * along_x + wind(halo_in, s, 1) * along_y) - coupling * linked
        a = mid + time_step * (t + mixing * (up + down - 2.0 * mid))
        gy[0:PAIRS, edge_row[s], :] = flip(s, -1.0) * edge_weights(s, a)

    @pl.when(jnp.logical_and(polar, jnp.logical_not(northern)))
    def _():
        own_rows(1)

    def row_weights(a, nw):
        return (
            -nw * a[0],
            -nw * a[1] - coupling * a[2],
            -nw * a[2] - coupling * a[1],
            -nw * a[3],
        )

    def put_weights(l, h, a):
        for f, weight in enumerate(row_weights(a, grid[PAIRS + LEV + l, h : h + 8, :])):
            gy[f * LEV + l, h : h + 8, :] = weight

    @pl.when(polar)
    def _():
        all_z(0).wait_recv()
        for h in (8, 16):
            taken = project(0, h // 8 - 1)
            for l in range(LEV):
                for f in range(FIELDS):
                    n, rows = f * LEV + l, slice(h - 8, h)
                    adj[n, rows, :] = grid[n, h : h + 8, :] + tend[n, rows, :] - taken[f][l]
        all_z(1).wait_recv()
        for h in (8, 16):
            taken = project(1, h // 8 - 1)
            for l in range(LEV):
                a = []
                for f in range(FIELDS):
                    n, rows = f * LEV + l, slice(h - 8, h)
                    change = tend[n, rows, :] - taken[f][l]
                    tend[n, rows, :] = change
                    tan_out[f, l, rows, :] = (grid[n, h : h + 8, :] + change)[:, :COLS]
                    a.append(adj[n, rows, :] - taken[f][l])
                    adj[n, rows, :] = a[f]
                put_weights(l, h, a)

    @pl.when(jnp.logical_not(polar))
    def _():
        @pl.loop(0, LEV, unroll=True)
        def _(l):
            for h in (8, 16):
                a = []
                for f in range(FIELDS):
                    n, rows = f * LEV + l, slice(h - 8, h)
                    a.append(grid[n, h : h + 8, :] + tend[n, rows, :])
                    tan_out[f, l, rows, :] = a[f][:, :COLS]
                    adj[n, rows, :] = a[f]
                put_weights(l, h, a)

    @pl.loop(0, LEV, unroll=True)
    def _(l):
        lo = jnp.maximum(l - 1, 0)
        hi = jnp.minimum(l + 1, LEV - 1)
        for h in (8, 16):
            rows = slice(h - 8, h)
            half = jnp.concatenate([hm[h : h + 8, :]] * 4, axis=1)
            ew = grid[PAIRS + l, h : h + 8, :]
            a = [adj[f * LEV + l, rows, :] for f in range(FIELDS)]
            col_weights = (
                -ew * a[0] - coupling * a[2],
                -ew * a[1],
                -ew * a[2] - coupling * a[0],
                -ew * a[3],
            )
            for f in range(FIELDS):
                n = f * LEV + l
                back = half * (roll(col_weights[f], 1, 1) - roll(col_weights[f], -1, 1))
                back = back + 0.5 * (gy[n, h - 1 : h + 7, :] - gy[n, h + 1 : h + 9, :])
                back = back + mixing * (adj[f * LEV + lo, rows, :] + adj[f * LEV + hi, rows, :] - 2.0 * a[f])
                diag = grid[n, h : h + 8, :] * (tend[n, rows, :] + time_step * back)
                diag_out[f, l, rows, :] = diag[:, :COLS]

    @pl.when(jnp.logical_and(near_polar, jnp.logical_not(polar)))
    def _():
        load_part.wait()

    for s, wanted in enumerate((above_polar, below_polar)):
        @pl.when(wanted)
        def _():
            row = 15 * s
            north_wind = wind(halo_in, s, 1)
            factor = ((0.5, -0.5)[s] * time_step) * grid[0:PAIRS, 8 + row, :] * flip(s, -1.0)
            before = [diag_out[f, :, row, :] for f in range(FIELDS)]
            remote(bz.at[s], bz.at[s], b_send, b_recv.at[s], nb, nl).wait_recv()
            taken = evaluate(jnp.concatenate([bz[s, f] for f in range(FIELDS)], axis=0))
            more = factor * (north_wind * taken + coupling * row_link(taken))
            for f in range(FIELDS):
                diag_out[f, :, row, :] = before[f] + more[f * LEV : (f + 1) * LEV, :COLS]

    halo_arrival(0, BLOCKS, 0).wait_send()

    @pl.when(polar)
    def _():
        all_c().wait_send()
        for q in range(2):
            all_y(q).wait_send()
            all_z(q).wait_send()

        @pl.when(edge_over)
        def _():
            remote(eb.at[others], eb.at[others], b_send, b_recv.at[0], b, west).wait_send()

        @pl.when(jnp.logical_not(edge_over))
        def _():
            remote(eb, eb, b_send, b_recv.at[0], b, west).wait_send()


def hand_out(tan_in, diag_in, tan_out, diag_out, sem):
    copies = [
        pltpu.make_async_copy(src, dst, sem.at[n])
        for n, (src, dst) in enumerate(((tan_in, tan_out), (diag_in, diag_out)))
    ]
    for copy in copies:
        copy.start()
    for copy in copies:
        copy.wait()


def per_device(bands, row_signs, col_signs, spread, east_wind, north_wind, cutoffs):
    any_spec = pl.BlockSpec(memory_space=pl.ANY)
    out = jax.ShapeDtypeStruct((FIELDS, LEV, ROWS, COLS), F32)
    tables = [jnp.asarray(half_metric(bands)), jnp.asarray(mode_factors())]
    operands = (spread, east_wind, north_wind, row_signs, col_signs, cutoffs, *tables)
    vmem = pltpu.VMEM
    dma = pltpu.SemaphoreType.DMA
    held = pltpu.VMEM(out.shape, F32)
    results = pl.pallas_call(
        functools.partial(kernel, bands),
        out_shape=(held, held),
        in_specs=[any_spec] * 8,
        out_specs=(pl.BlockSpec(memory_space=pltpu.VMEM),) * 2,
        scratch_shapes=[
            vmem((FIELDS, LEV, ROWS, COLS), F32),
            vmem((2, LEV, ROWS, COLS), F32),
            vmem((FIELDS, LEV, ROWS), jnp.int32),
            vmem((FIELDS, LEV, COLS), jnp.int32),
            pltpu.SMEM((ROWS,), jnp.int32),
            vmem((32, 128), F32),
            vmem((TABLE_ROWS, 2 * RANK), BF16),
            vmem((PAIRS + 2 * LEV, 32, WIDE), F32),
            vmem((BLOCKS, 16, 128), F32),
            vmem((BLOCKS, 16, 128), F32),
            vmem((2, LANES, LEV - 1, 8, RANK), F32),
            vmem((2, LANES, LEV - 1, 8, RANK), F32),
            vmem((2, PAIRS, WIDE), F32),
            vmem((LANES, 16, RANK), F32),
            vmem((LANES, 16, RANK), F32),
            vmem((2, LANES, LEV - 1, 8, RANK), F32),
            vmem((2, LANES, LEV - 1, 8, RANK), F32),
            vmem((LANES, LEV, RANK), F32),
            vmem((2, FIELDS, LEV, RANK), F32),
            vmem((PAIRS, ROWS, WIDE), F32),
            vmem((PAIRS, ROWS, WIDE), F32),
            vmem((PAIRS, 32, WIDE), F32),
            dma((8,)),
            dma,
            dma((2,)),
            dma((2,)),
            dma((2,)),
            dma,
            dma,
            dma((2,)),
            dma((2,)),
            dma,
            dma((2,)),
        ],
        compiler_params=pltpu.CompilerParams(
            collective_id=0, has_side_effects=True, vmem_limit_bytes=32 * 2**20
        ),
        cost_estimate=pl.CostEstimate(flops=10**9, bytes_accessed=4 * 10**6, transcendentals=0),
    )(*(pltpu.with_memory_space_constraint(x, pltpu.HBM) for x in operands))
    return pl.pallas_call(
        hand_out,
        out_shape=(out, out),
        in_specs=[any_spec] * 2,
        out_specs=(any_spec, any_spec),
        scratch_shapes=[dma((2,))],
        compiler_params=pltpu.CompilerParams(vmem_limit_bytes=2**20),
    )(*(pltpu.with_memory_space_constraint(x, pltpu.VMEM) for x in results))


def solution(mesh):
    return jax.shard_map(
        functools.partial(per_device, mesh.shape["lat"]),
        mesh=mesh,
        in_specs=(
            P(None, None, "lat"),
            P(None, None, "lon"),
            P(None, None, "lat", "lon"),
            P(None, "lat", "lon"),
            P(None, "lat", "lon"),
            P("lat"),
        ),
        out_specs=(P(None, None, "lat", "lon"), P(None, None, "lat", "lon")),
        check_vma=False,
    )
```
